32 devices in a mesh: branch: 4 (over y, x), crops: 8 (over z, core).
Axes of the slice: x: 2, y: 2, z: 4, core: 2. Of those that a mesh axis runs over, the one named last changes fastest.
Arguments:
- features: bfloat16 [4, 6144, 128], P('branch', 'crops'), may hold values from -16 to 16
- weights: bfloat16 [4, 2, 1708032], P('branch'), may hold values from -0.1875 to 0.1875
- gains: float32 [4, 2, 8, 256], P('branch'), may hold values from 0.1 to 1.9
- shifts: float32 [4, 2, 8, 256], P('branch'), may hold values from -3 to 3
- cotangent: bfloat16 [4, 6144, 128], P('branch', 'crops'), may hold values from -16 to 16
- size_group: int32 [8], replicated, may hold values from 0 to 1, as said below
Outputs:
- outputs: bfloat16 [4, 6144, 128], P('branch', 'crops')
- input_grad: float32 [4, 6144, 128], P('branch', 'crops')
- weight_grad: float32 [4, 2, 1708032], P('branch', None, 'crops')
- gain_grad: float32 [4, 2, 8, 256], P('branch', None, None, 'crops')
- shift_grad: float32 [4, 2, 8, 256], P('branch', None, None, 'crops')
The draws below stay inside these ranges and needn't reach their ends.
Inputs may be any that keep to these rules, and one draw needn't show every extreme that they name: `size_group`: exactly 2 entries are 1; those devices hold large crops, the others small ones.
All inputs are finite; a program needn't handle non-finite values.
Results may differ from the reference program's by a relative error of at most 0.014.
Values may be sent and summed in bfloat16 or wider, within the bound.
A program may use at most 320 MiB of HBM per device.

```python
import jax
import jax.numpy as jnp
from jax import lax

C0 = 32
BLOCKS = 1
MODULES = 2
CROPS_DEV = 1
SH = 32
SW = 24
LH = 64
LW = 48
CROP_SHARDS = 8
ROWS = 768
BNSLOTS = 8
WLEN = 1708032


def draw_features(key, part):
    key = jax.random.fold_in(key, 1)
    noise_key, offset_key = jax.random.split(key, 2)
    array_dims = (4, CROP_SHARDS, ROWS, 128)
    device_ramp = 3.0 ** (jnp.arange(CROP_SHARDS, dtype=jnp.float32) / max(CROP_SHARDS - 1, 1))
    device_ramp = device_ramp.reshape(1, CROP_SHARDS, 1, 1)
    offsets = 0.5 * jax.random.normal(offset_key, (4, CROP_SHARDS, 1, 128), jnp.float32)
    noise_draw = jax.random.normal(noise_key, array_dims, jnp.float32)
    values = (noise_draw + offsets) * device_ramp
    return jnp.clip(values, -16.0, 16.0).reshape(4, CROP_SHARDS * ROWS, 128).astype(jnp.bfloat16)


def draw_cotangent(key, part):
    key = jax.random.fold_in(key, 2)
    noise_key, offset_key = jax.random.split(key, 2)
    array_dims = (4, CROP_SHARDS, ROWS, 128)
    device_ramp = 3.0 ** (jnp.arange(CROP_SHARDS, dtype=jnp.float32) / max(CROP_SHARDS - 1, 1))
    device_ramp = device_ramp.reshape(1, CROP_SHARDS, 1, 1)
    offsets = 0.5 * jax.random.normal(offset_key, (4, CROP_SHARDS, 1, 128), jnp.float32)
    noise_draw = jax.random.normal(noise_key, array_dims, jnp.float32)
    values = (noise_draw + offsets) * device_ramp
    return jnp.clip(values, -16.0, 16.0).reshape(4, CROP_SHARDS * ROWS, 128).astype(jnp.bfloat16)


def draw_size_group(key, part):
    key = jax.random.fold_in(key, 3)
    ordering = jax.random.permutation(key, CROP_SHARDS)
    return (ordering < CROP_SHARDS // 4).astype(jnp.int32)


def level_of(rng, shape, cuts, low, top_value):
    loudness = 1.0
    for axis_at, shards_of in cuts:
        steps = jax.random.uniform(jax.random.fold_in(jax.random.fold_in(rng, 6), axis_at), (shards_of,), jnp.float32, low / len(cuts), top_value / len(cuts))
        loudness = loudness * jnp.repeat(jnp.exp(steps), shape[axis_at] // shards_of).reshape((-1,) + (1,) * (len(shape) - 1 - axis_at))
    return loudness


def noise(own_key, shape, deviation, limit, cuts=(), kind=jnp.bfloat16):
    entries = deviation * jax.random.normal(own_key, shape, jnp.float32)
    if cuts:
        entries = entries * level_of(own_key, shape, cuts, -0.22, 0.18)
    return jnp.clip(entries, -limit, limit).astype(kind)


def setup_inputs(seed: int = 0) -> dict:
    arg_keys = jax.random.split(jax.random.key(seed), 7)
    features = draw_features(jax.random.fold_in(arg_keys[6], 71), 0)
    weights = noise(arg_keys[1], (4, MODULES, WLEN), (36 * C0) ** -0.5, 0.1875, ((0, 4),))
    gains = jnp.clip(1.0 + 0.18 * jax.random.normal(arg_keys[2], (4, MODULES, BNSLOTS, 8 * C0), jnp.float32), 0.1, 1.9)
    shifts = noise(arg_keys[3], (4, MODULES, BNSLOTS, 8 * C0), 0.5, 3.0, ((0, 4),), jnp.float32)
    cotangent = draw_cotangent(jax.random.fold_in(arg_keys[6], 71), 0)
    size_group = draw_size_group(jax.random.fold_in(arg_keys[6], 71), 0)
    return {"features": features, "weights": weights, "gains": gains, "shifts": shifts, "cotangent": cotangent, "size_group": size_group}


EPS = 1e-05
HIGHEST = lax.Precision.HIGHEST

@jax.custom_vjp
def low(v):
    return lax.optimization_barrier(v.astype(jnp.bfloat16)).astype(jnp.float32)

@jax.custom_vjp
def low_back(v):
    return v

def low_keep(v):
    return (low(v), None)

def low_pass(kept, grad):
    return (grad,)

def back_keep(v):
    return (v, None)

def back_low(kept, grad):
    return (low(grad),)
low.defvjp(low_keep, low_pass)
low_back.defvjp(back_keep, back_low)

def sender_plan(branch_index, top_channels, blocks):
    channels = top_channels << branch_index
    operations = []
    for block_index in range(blocks):
        operations.append({'phase': 2 * block_index, 'source': ('h', block_index), 'level': branch_index, 'cin': channels, 'cout': channels, 'stride': 1, 'taps': 3, 'act': 'silu', 'output': ('u', block_index), 'skip': None, 'dest': -1})
        operations.append({'phase': 2 * block_index + 1, 'source': ('u', block_index), 'level': branch_index, 'cin': channels, 'cout': channels, 'stride': 1, 'taps': 3, 'act': 'res', 'output': ('h', block_index + 1), 'skip': ('h', block_index), 'dest': -1})
    top_name = ('h', blocks)
    for target in range(branch_index):
        operations.append({'phase': 2 * blocks, 'source': top_name, 'level': branch_index, 'cin': channels, 'cout': top_channels << target, 'stride': 1, 'taps': 1, 'act': 'none', 'output': None, 'skip': None, 'dest': target})
    for target in range(branch_index + 1, 4):
        for depth_step in range(1, target - branch_index + 1):
            is_last = depth_step == target - branch_index
            operations.append({'phase': 2 * blocks + depth_step - 1, 'source': top_name if depth_step == 1 else ('chain', target, depth_step - 1), 'level': branch_index + depth_step, 'cin': channels, 'cout': top_channels << target if is_last else channels, 'stride': 2, 'taps': 3, 'act': 'none' if is_last else 'silu', 'output': None if is_last else ('chain', target, depth_step), 'skip': None, 'dest': target if is_last else -1})
    for position, operation in enumerate(operations):
        operation['slot'] = position
        operation['size'] = operation['taps'] * operation['taps'] * operation['cin'] * operation['cout']
        if operation['taps'] == 1:
            operation['kshape'] = (operation['cin'], operation['cout'])
        else:
            operation['kshape'] = (3, 3, operation['cin'], operation['cout'])
    return operations

def phase_lengths(top_channels, blocks):
    phase_count = 2 * blocks + 3
    lengths = [0] * phase_count
    for branch_index in range(4):
        per_phase = [0] * phase_count
        for operation in sender_plan(branch_index, top_channels, blocks):
            per_phase[operation['phase']] += operation['size']
        lengths = [max(current, candidate) for current, candidate in zip(lengths, per_phase)]
    return lengths

def weighted_plan(branch_index, top_channels, blocks):
    lengths = phase_lengths(top_channels, blocks)
    starts = [sum(lengths[:phase_index]) for phase_index in range(len(lengths))]
    running = [0] * len(lengths)
    operations = sender_plan(branch_index, top_channels, blocks)
    for operation in operations:
        phase_index = operation['phase']
        operation['inner'] = running[phase_index]
        operation['offset'] = starts[phase_index] + running[phase_index]
        operation['position'] = sum((1 for earlier in operations[:operation['slot']] if earlier['phase'] == phase_index))
        running[phase_index] += operation['size']
    return operations

def batch_norm(preact, gain_row, shift_row):
    average = lax.optimization_barrier(jnp.mean(preact, axis=(0, 1, 2)))
    variance = lax.optimization_barrier(jnp.mean(jnp.square(preact - average), axis=(0, 1, 2)))
    return (preact - average) * lax.rsqrt(variance + EPS) * gain_row + shift_row

def apply_conv(operation, source, kernel):
    if operation['taps'] == 1:
        return jnp.einsum('nhwc,cd->nhwd', source, kernel, precision=HIGHEST)
    stride = operation['stride']
    return lax.conv_general_dilated(source, kernel, (stride, stride), ((1, 1), (1, 1)), dimension_numbers=('NHWC', 'HWIO', 'NHWC'), precision=HIGHEST)

def upsample(message, factor):
    crop_count, height, breadth, channels = message.shape
    widened = jnp.broadcast_to(message[:, :, None, :, None, :], (crop_count, height, factor, breadth, factor, channels))
    return widened.reshape(crop_count, height * factor, breadth * factor, channels)

def run_module(branch_maps, module_weights, module_gains, module_shifts):
    messages = {}
    top_maps = []
    for branch_index in range(4):
        named = {('h', 0): branch_maps[branch_index]}
        rounded = {}
        for operation in weighted_plan(branch_index, C0, BLOCKS):
            source = operation['source']
            if source not in rounded:
                rounded[source] = low(named[source])
            start = operation['offset']
            kernel = module_weights[branch_index, start:start + operation['size']].reshape(operation['kshape'])
            preact = low_back(apply_conv(operation, rounded[source], kernel))
            channels = operation['cout']
            normed = batch_norm(preact, module_gains[branch_index, operation['slot'], :channels], module_shifts[branch_index, operation['slot'], :channels])
            if operation['act'] == 'silu':
                named[operation['output']] = jax.nn.silu(normed)
            elif operation['act'] == 'res':
                named[operation['output']] = jax.nn.silu(normed + named[operation['skip']])
            else:
                messages[branch_index, operation['dest']] = low_back(low(normed))
        top_maps.append(named['h', BLOCKS])
    results = []
    for receiver in range(4):
        summed = top_maps[receiver]
        for sender in range(4):
            if sender < receiver:
                summed = summed + messages[sender, receiver]
            elif sender > receiver:
                summed = summed + upsample(messages[sender, receiver], 2 ** (sender - receiver))
        results.append(jax.nn.silu(summed))
    return results

def reference(features, weights, gains, shifts, cotangent, size_group):
    large_count = CROP_SHARDS // 4
    large_rows = jnp.argsort(1 - size_group, stable=True)[:large_count]
    small_rows = jnp.argsort(size_group, stable=True)[:CROP_SHARDS - large_count]
    layouts = ((small_rows, SH, SW), (large_rows, LH, LW))
    block_length = ROWS * 128

    def unpack(packed, rows_picked, branch_index, height, breadth):
        picked = jnp.take(packed[branch_index], rows_picked, axis=0)
        length = CROPS_DEV * (height >> branch_index) * (breadth >> branch_index) * (C0 << branch_index)
        return picked[:, :length].reshape(-1, height >> branch_index, breadth >> branch_index, C0 << branch_index)
    feature_blocks = features.astype(jnp.float32).reshape(4, CROP_SHARDS, block_length)
    cotangent_blocks = cotangent.astype(jnp.float32).reshape(4, CROP_SHARDS, block_length)
    inputs = [[unpack(feature_blocks, rows_picked, branch_index, height, breadth) for branch_index in range(4)] for rows_picked, height, breadth in layouts]
    cotangents = [[unpack(cotangent_blocks, rows_picked, branch_index, height, breadth) for branch_index in range(4)] for rows_picked, height, breadth in layouts]

    def forward(flat_weights, gain_table, shift_table, group_maps):
        results = []
        for branch_maps in group_maps:
            for module in range(MODULES):
                branch_maps = run_module(branch_maps, flat_weights[:, module], gain_table[:, module], shift_table[:, module])
            results.append(branch_maps)
        return results
    results, pullback = jax.vjp(forward, weights.astype(jnp.float32), gains, shifts, inputs)
    weight_grad, gain_grad, shift_grad, input_maps_grad = pullback(cotangents)

    def pack(group_lists):
        packed = jnp.zeros((4, CROP_SHARDS, block_length), jnp.float32)
        for layout, branch_maps in zip(layouts, group_lists):
            rows_picked = layout[0]
            for branch_index in range(4):
                flattened = branch_maps[branch_index].reshape(rows_picked.shape[0], -1)
                flattened = jnp.pad(flattened, ((0, 0), (0, block_length - flattened.shape[1])))
                packed = packed.at[branch_index, rows_picked].set(flattened)
        return packed.reshape(4, CROP_SHARDS * ROWS, 128)
    return (pack(results).astype(jnp.bfloat16), pack(input_maps_grad), weight_grad, gain_grad, shift_grad)
```

```python
from functools import partial
from types import SimpleNamespace
import math

import jax
import jax.numpy as jnp
import numpy as np
from jax import lax
from jax.experimental import pallas as pl
from jax.experimental.pallas import tpu as pltpu
from jax.sharding import PartitionSpec as P

C0 = 32
BLOCKS = 1
MODULES = 2
CROPS_DEV = 1
SH = 32
SW = 24
LH = 64
LW = 48
ROWS = 768
MSG_ROWS = 384


EPS = 1e-05


def as_sent(x):

    def short(part):
        return part.astype(jnp.bfloat16) if part.dtype == jnp.float32 else part

    return jax.tree.map(short, x)


def sender_plan(branch_index, top_channels, blocks):
    channels = top_channels << branch_index
    operations = []
    for block_index in range(blocks):
        operations.append(
            SimpleNamespace(
                phase=2 * block_index,
                source=("h", block_index),
                level=branch_index,
                cin=channels,
                cout=channels,
                stride=1,
                taps=3,
                act="silu",
                output=("u", block_index),
                skip=None,
                dest=-1,
            )
        )
        operations.append(
            SimpleNamespace(
                phase=2 * block_index + 1,
                source=("u", block_index),
                level=branch_index,
                cin=channels,
                cout=channels,
                stride=1,
                taps=3,
                act="res",
                output=("h", block_index + 1),
                skip=("h", block_index),
                dest=-1,
            )
        )
    top_name = ("h", blocks)
    for target in range(branch_index):
        operations.append(
            SimpleNamespace(
                phase=2 * blocks,
                source=top_name,
                level=branch_index,
                cin=channels,
                cout=top_channels << target,
                stride=1,
                taps=1,
                act="none",
                output=None,
                skip=None,
                dest=target,
            )
        )
    for target in range(branch_index + 1, 4):
        for depth_step in range(1, target - branch_index + 1):
            is_last = depth_step == target - branch_index
            operations.append(
                SimpleNamespace(
                    phase=2 * blocks + depth_step - 1,
                    source=top_name if depth_step == 1 else ("chain", target, depth_step - 1),
                    level=branch_index + depth_step,
                    cin=channels,
                    cout=top_channels << target if is_last else channels,
                    stride=2,
                    taps=3,
                    act="none" if is_last else "silu",
                    output=None if is_last else ("chain", target, depth_step),
                    skip=None,
                    dest=target if is_last else -1,
                )
            )
    for position, operation in enumerate(operations):
        operation.slot = position
        operation.size = (
            operation.taps * operation.taps * operation.cin * operation.cout
        )
        if operation.taps == 1:
            operation.kshape = (operation.cin, operation.cout)
        else:
            operation.kshape = (3, 3, operation.cin, operation.cout)
    return operations


def phase_lengths(top_channels, blocks):
    phase_count = 2 * blocks + 3
    lengths = [0] * phase_count
    for branch_index in range(4):
        per_phase = [0] * phase_count
        for operation in sender_plan(branch_index, top_channels, blocks):
            per_phase[operation.phase] += operation.size
        lengths = [max(current, candidate) for current, candidate in zip(lengths, per_phase)]
    return lengths


def weighted_plan(branch_index, top_channels, blocks):
    lengths = phase_lengths(top_channels, blocks)
    starts = [sum(lengths[:phase_index]) for phase_index in range(len(lengths))]
    running = [0] * len(lengths)
    operations = sender_plan(branch_index, top_channels, blocks)
    for operation in operations:
        phase_index = operation.phase
        operation.inner = running[phase_index]
        operation.offset = starts[phase_index] + running[phase_index]
        operation.position = sum(
            (1 for earlier in operations[: operation.slot] if earlier.phase == phase_index)
        )
        running[phase_index] += operation.size
    return operations


def phase_operations(branch_index, phase_index):
    return [
        operation
        for operation in weighted_plan(branch_index, C0, BLOCKS)
        if operation.phase == phase_index
    ]


def input_names(operations):
    source_names = []
    for operation in operations:
        if operation.source not in source_names:
            source_names.append(operation.source)
    return source_names


def silu_slope(value):
    sigmoid = jax.nn.sigmoid(value)
    return sigmoid * (1.0 + value * (1.0 - sigmoid))


def crop_cells(size_kind):
    return (LH, LW) if size_kind else (SH, SW)


def map_dims(size_kind, level, channels):
    height, breadth = crop_cells(size_kind)
    return (CROPS_DEV, height >> level, breadth >> level, channels)


def source_dims(branch_index, size_kind, map_name):
    level = branch_index + map_name[2] if map_name[0] == "chain" else branch_index
    return map_dims(size_kind, level, C0 << branch_index)


def preact_dims(size_kind, operation):
    return map_dims(size_kind, operation.level, operation.cout)


def to_canvas(arrays, value_type):
    if not arrays:
        return jnp.zeros((ROWS, 128), value_type)
    flattened = jnp.concatenate([array.reshape(-1).astype(value_type) for array in arrays])
    return jnp.pad(flattened, (0, ROWS * 128 - flattened.shape[0])).reshape(ROWS, 128)


def from_canvas(canvas, dims_list):
    flattened = canvas.reshape(-1)
    pieces = []
    offset = 0
    for dims_entry in dims_list:
        count_here = math.prod(dims_entry)
        pieces.append(flattened[offset : offset + count_here].reshape(dims_entry))
        offset += count_here
    return pieces


def to_slot(array):
    flattened = array.reshape(-1)
    return jnp.pad(flattened, (0, MSG_ROWS * 128 - flattened.shape[0])).reshape(MSG_ROWS, 128)


def from_slot(slot_rows, dims_entry):
    return slot_rows.reshape(-1)[: math.prod(dims_entry)].reshape(dims_entry)


def upsample(message, factor):
    crop_count, height, breadth, channels = message.shape
    widened = jnp.broadcast_to(
        message[:, :, None, :, None, :], (crop_count, height, factor, breadth, factor, channels)
    )
    return widened.reshape(crop_count, height * factor, breadth * factor, channels)


def block_pool(array, factor):
    crop_count, height, breadth, channels = array.shape
    return array.reshape(
        crop_count, height // factor, factor, breadth // factor, factor, channels
    ).sum(axis=(2, 4))


def kernel_piece(module_weights, operation):
    start = operation.offset
    return module_weights[start : start + operation.size].reshape(operation.kshape)


def conv_forward(operation, source, kernel):
    if operation.taps == 1:
        return jnp.einsum("nhwc,cd->nhwd", source, kernel, preferred_element_type=jnp.float32)
    stride = operation.stride
    return lax.conv_general_dilated(
        source,
        kernel,
        (stride, stride),
        ((1, 1), (1, 1)),
        dimension_numbers=("NHWC", "HWIO", "NHWC"),
        preferred_element_type=jnp.float32,
    )


def conv_backward(operation, source, kernel, upstream):
    if operation.taps == 1:
        source_grad = jnp.einsum(
            "nhwd,cd->nhwc", upstream, kernel, preferred_element_type=jnp.float32
        )
        kernel_grad = jnp.einsum(
            "nhwc,nhwd->cd", source, upstream, preferred_element_type=jnp.float32
        )
        return (source_grad, kernel_grad)
    stride = operation.stride
    flipped = jnp.transpose(kernel[::-1, ::-1], (0, 1, 3, 2))
    high_pad = 2 if stride == 2 else 1
    source_grad = lax.conv_general_dilated(
        upstream,
        flipped,
        (1, 1),
        ((1, high_pad), (1, high_pad)),
        lhs_dilation=(stride, stride),
        dimension_numbers=("NHWC", "HWIO", "NHWC"),
        preferred_element_type=jnp.float32,
    )
    kernel_grad = lax.conv_general_dilated(
        source,
        upstream,
        (1, 1),
        ((1, 2 - stride), (1, 2 - stride)),
        rhs_dilation=(stride, stride),
        dimension_numbers=("CHWN", "IHWO", "NHWC"),
        preferred_element_type=jnp.float32,
    )
    return (source_grad, jnp.transpose(kernel_grad, (1, 2, 0, 3)))


def cell_total(counts, size_kind, level):
    height, breadth = crop_cells(size_kind)
    return counts[size_kind] * float(CROPS_DEV * (height >> level) * (breadth >> level))


def norm_terms(totals, counts, size_kind, operation):
    cells_here = cell_total(counts, size_kind, operation.level)
    channels = operation.cout
    position = operation.position
    average = totals[size_kind, 0, position, :channels] / cells_here
    variance = totals[size_kind, 1, position, :channels] / cells_here - average * average
    return (average, lax.rsqrt(variance + EPS))


def forward_conv(branch_index, size_kind, phase_index, source_canvas, module_weights):
    operations = phase_operations(branch_index, phase_index)
    source_names = input_names(operations)
    pieces = from_canvas(
        source_canvas, [source_dims(branch_index, size_kind, map_name) for map_name in source_names]
    )
    sources = {
        map_name: piece.astype(jnp.bfloat16) for map_name, piece in zip(source_names, pieces)
    }
    preacts = []
    totals = jnp.zeros((2, 2, 3, 8 * C0), jnp.float32)
    for operation in operations:
        preact = conv_forward(
            operation, sources[operation.source], kernel_piece(module_weights, operation)
        )
        preacts.append(preact)
        channels = operation.cout
        position = operation.position
        totals = totals.at[size_kind, 0, position, :channels].set(jnp.sum(preact, axis=(0, 1, 2)))
        totals = totals.at[size_kind, 1, position, :channels].set(
            jnp.sum(preact * preact, axis=(0, 1, 2))
        )
    return (to_canvas(preacts, jnp.float32), totals)


def forward_norm(
    branch_index,
    size_kind,
    phase_index,
    preact_canvas,
    totals,
    counts,
    module_gains,
    module_shifts,
    skip_canvas,
    message_buffer,
):
    operations = phase_operations(branch_index, phase_index)
    preacts = from_canvas(
        preact_canvas, [preact_dims(size_kind, operation) for operation in operations]
    )
    skip_map = from_canvas(skip_canvas, [map_dims(size_kind, branch_index, C0 << branch_index)])[0]
    produced = []
    for operation, preact in zip(operations, preacts):
        average, inverse_std = norm_terms(totals, counts, size_kind, operation)
        norm_slot = operation.slot
        channels = operation.cout
        normed = (preact - average) * inverse_std * module_gains[
            norm_slot, :channels
        ] + module_shifts[norm_slot, :channels]
        if operation.act == "silu":
            produced.append(jax.nn.silu(normed))
        elif operation.act == "res":
            produced.append(jax.nn.silu(normed + skip_map))
        else:
            message_buffer = message_buffer.at[operation.dest].set(
                to_slot(normed.astype(jnp.bfloat16))
            )
    return (to_canvas(produced, jnp.float32), message_buffer)


def receive_forward(branch_index, size_kind, top_canvas, received):
    channels = C0 << branch_index
    summed = from_canvas(top_canvas, [map_dims(size_kind, branch_index, channels)])[0]
    for sender in range(4):
        if sender < branch_index:
            summed = summed + from_slot(
                received[sender], map_dims(size_kind, branch_index, channels)
            ).astype(jnp.float32)
        elif sender > branch_index:
            coarse = from_slot(received[sender], map_dims(size_kind, sender, channels))
            summed = summed + upsample(coarse, 2 ** (sender - branch_index)).astype(jnp.float32)
    return (to_canvas([jax.nn.silu(summed)], jnp.float32), to_canvas([summed], jnp.float32))


def receive_backward(branch_index, size_kind, grad_canvas, summed_canvas):
    dims_here = map_dims(size_kind, branch_index, C0 << branch_index)
    upstream = from_canvas(grad_canvas, [dims_here])[0]
    summed = from_canvas(summed_canvas, [dims_here])[0]
    summed_grad = upstream * silu_slope(summed)
    buffer = jnp.zeros((4, MSG_ROWS, 128), jnp.bfloat16)
    for sender in range(4):
        if sender < branch_index:
            buffer = buffer.at[sender].set(to_slot(summed_grad.astype(jnp.bfloat16)))
        elif sender > branch_index:
            pooled = block_pool(summed_grad, 2 ** (sender - branch_index))
            buffer = buffer.at[sender].set(to_slot(pooled.astype(jnp.bfloat16)))
    return (to_canvas([summed_grad], jnp.float32), buffer)


def backward_stats(
    branch_index,
    size_kind,
    phase_index,
    dout_canvas,
    message_grads,
    preact_canvas,
    totals,
    counts,
    module_gains,
    module_shifts,
    skip_canvas,
):
    operations = phase_operations(branch_index, phase_index)
    preacts = from_canvas(
        preact_canvas, [preact_dims(size_kind, operation) for operation in operations]
    )
    producing = [operation for operation in operations if operation.act != "none"]
    output_grads = from_canvas(
        dout_canvas, [preact_dims(size_kind, operation) for operation in producing]
    )
    grads_by_name = {
        operation.output: piece for operation, piece in zip(producing, output_grads)
    }
    skip_map = from_canvas(skip_canvas, [map_dims(size_kind, branch_index, C0 << branch_index)])[0]
    upstreams = []
    skip_grads = []
    sums_local = jnp.zeros((2, 2, 3, 8 * C0), jnp.float32)
    for operation, preact in zip(operations, preacts):
        average, inverse_std = norm_terms(totals, counts, size_kind, operation)
        norm_slot = operation.slot
        channels = operation.cout
        centered = (preact - average) * inverse_std
        normed = centered * module_gains[norm_slot, :channels] + module_shifts[norm_slot, :channels]
        if operation.act == "silu":
            upstream = grads_by_name[operation.output] * silu_slope(normed)
        elif operation.act == "res":
            upstream = grads_by_name[operation.output] * silu_slope(normed + skip_map)
            skip_grads.append(upstream)
        else:
            upstream = from_slot(
                message_grads[operation.dest], preact_dims(size_kind, operation)
            ).astype(jnp.float32)
        upstreams.append(upstream)
        position = operation.position
        sums_local = sums_local.at[size_kind, 0, position, :channels].set(
            jnp.sum(upstream, axis=(0, 1, 2))
        )
        sums_local = sums_local.at[size_kind, 1, position, :channels].set(
            jnp.sum(upstream * centered, axis=(0, 1, 2))
        )
    return (to_canvas(upstreams, jnp.float32), sums_local, to_canvas(skip_grads, jnp.float32))


def backward_apply(
    branch_index,
    size_kind,
    phase_index,
    upstream_canvas,
    preact_canvas,
    totals,
    grad_totals,
    counts,
    source_canvas,
    module_weights,
    module_gains,
):
    operations = phase_operations(branch_index, phase_index)
    preacts = from_canvas(
        preact_canvas, [preact_dims(size_kind, operation) for operation in operations]
    )
    upstreams = from_canvas(
        upstream_canvas, [preact_dims(size_kind, operation) for operation in operations]
    )
    source_names = input_names(operations)
    source_list = [source_dims(branch_index, size_kind, map_name) for map_name in source_names]
    pieces = from_canvas(source_canvas, source_list)
    sources = {
        map_name: piece.astype(jnp.bfloat16) for map_name, piece in zip(source_names, pieces)
    }
    source_grads = {
        map_name: jnp.zeros(dims_entry, jnp.float32)
        for map_name, dims_entry in zip(source_names, source_list)
    }
    kernel_grads = []
    slot_count = module_gains.shape[0]
    gain_part = jnp.zeros((slot_count, 8 * C0), jnp.float32)
    shift_part = jnp.zeros((slot_count, 8 * C0), jnp.float32)
    for operation, preact, upstream in zip(operations, preacts, upstreams):
        average, inverse_std = norm_terms(totals, counts, size_kind, operation)
        cells_here = cell_total(counts, size_kind, operation.level)
        norm_slot = operation.slot
        channels = operation.cout
        position = operation.position
        centered = (preact - average) * inverse_std
        mean_upstream = grad_totals[size_kind, 0, position, :channels] / cells_here
        mean_cross = grad_totals[size_kind, 1, position, :channels] / cells_here
        preact_grad = (
            module_gains[norm_slot, :channels]
            * inverse_std
            * (upstream - mean_upstream - centered * mean_cross)
        )
        source_grad, kernel_grad = conv_backward(
            operation,
            sources[operation.source],
            kernel_piece(module_weights, operation),
            preact_grad.astype(jnp.bfloat16),
        )
        source_grads[operation.source] = source_grads[operation.source] + source_grad
        kernel_grads.append(kernel_grad.reshape(-1))
        gain_part = gain_part.at[norm_slot, :channels].set(
            grad_totals[0, 1, position, :channels] + grad_totals[1, 1, position, :channels]
        )
        shift_part = shift_part.at[norm_slot, :channels].set(
            grad_totals[0, 0, position, :channels] + grad_totals[1, 0, position, :channels]
        )
    phase_length = phase_lengths(C0, BLOCKS)[phase_index]
    if kernel_grads:
        joined = jnp.concatenate(kernel_grads)
        weight_part = jnp.pad(joined, (0, phase_length - joined.shape[0]))
    else:
        weight_part = jnp.zeros((phase_length,), jnp.float32)
    return (
        to_canvas([source_grads[map_name] for map_name in source_names], jnp.float32),
        weight_part,
        gain_part,
        shift_part,
    )


def on_device(features, weights, gains, shifts, cotangent, size_group):
    crop_shard = lax.axis_index("crops")
    shard_count = lax.axis_size("crops")
    crop_kind = size_group[crop_shard]
    large_count = jnp.sum(size_group).astype(jnp.float32)
    counts = jnp.stack([shard_count - large_count, large_count])
    case_index = lax.axis_index("branch") * 2 + crop_kind
    phase_total = 2 * BLOCKS + 3
    zero_canvas = jnp.zeros((ROWS, 128), jnp.float32)
    empty_buffer = jnp.zeros((4, MSG_ROWS, 128), jnp.bfloat16)

    def run_phase(function, statics, operands):
        branches_list = [
            partial(function, branch_index, size_kind, *statics)
            for branch_index in range(4)
            for size_kind in range(2)
        ]
        return lax.switch(case_index, branches_list, *operands)

    def statistics(local_totals):
        return lax.psum(local_totals, "crops")

    def module_forward(module, start_canvas, kept):
        module_weights = weights[0, module]
        module_gains = gains[0, module]
        module_shifts = shifts[0, module]
        record = SimpleNamespace(sources=[], preacts=[], totals=[])
        h_canvas = start_canvas
        u_canvas = zero_canvas
        chain_canvas = zero_canvas
        buffer = empty_buffer
        for phase_index in range(phase_total):
            if phase_index < 2 * BLOCKS:
                source = h_canvas if phase_index % 2 == 0 else u_canvas
            elif phase_index == 2 * BLOCKS:
                source = h_canvas
            else:
                source = chain_canvas
            preact, local_totals = run_phase(forward_conv, (phase_index,), (source, module_weights))
            global_totals = kept.totals[phase_index] if kept else statistics(local_totals)
            produced, buffer = run_phase(
                forward_norm,
                (phase_index,),
                (preact, global_totals, counts, module_gains, module_shifts, h_canvas, buffer),
            )
            record.sources.append(source)
            record.preacts.append(preact)
            record.totals.append(global_totals)
            if phase_index < 2 * BLOCKS:
                if phase_index % 2 == 0:
                    u_canvas = produced
                else:
                    h_canvas = produced
            else:
                chain_canvas = produced
        received = (
            kept.received
            if kept
            else jax.tree.map(
                lambda part, own: part.astype(own.dtype),
                lax.all_to_all(as_sent(buffer), "branch", split_axis=0, concat_axis=0, tiled=True),
                buffer,
            )
        )
        result, summed = run_phase(receive_forward, (), (h_canvas, received))
        record.summed = summed
        record.received = received
        return (result, record)

    checkpoints = [features[0].astype(jnp.float32)]
    first_records = []
    for module in range(MODULES):
        result, record = module_forward(module, checkpoints[-1], None)
        checkpoints.append(result)
        first_records.append(record)
    outputs = checkpoints[-1].astype(jnp.bfloat16)
    grad_canvas = cotangent[0].astype(jnp.float32)
    module_grads = [None] * MODULES
    gain_grads = [None] * MODULES
    shift_grads = [None] * MODULES
    for module in reversed(range(MODULES)):
        kept = None
        unused_result, record = module_forward(module, checkpoints[module], kept)
        module_module_weights = weights[0, module]
        module_module_gains = gains[0, module]
        module_module_shifts = shifts[0, module]
        summed_grad, back_buffer = run_phase(receive_backward, (), (grad_canvas, record.summed))
        message_grads = jax.tree.map(
            lambda part, own: part.astype(own.dtype),
            lax.all_to_all(as_sent(back_buffer), "branch", split_axis=0, concat_axis=0, tiled=True),
            back_buffer,
        )
        top_grad = summed_grad
        chain_grad = zero_canvas
        u_grad = zero_canvas
        pending_skip = zero_canvas
        weight_parts = [None] * phase_total
        gain_total = jnp.zeros(gains.shape[2:], jnp.float32)
        shift_total = jnp.zeros(gains.shape[2:], jnp.float32)
        for module_phase_index in reversed(range(phase_total)):
            if module_phase_index >= 2 * BLOCKS:
                output_grad = chain_grad
                skip_canvas = zero_canvas
            elif module_phase_index % 2 == 1:
                output_grad = top_grad
                skip_canvas = record.sources[module_phase_index - 1]
            else:
                output_grad = u_grad
                skip_canvas = zero_canvas
            module_preact = record.preacts[module_phase_index]
            totals = record.totals[module_phase_index]
            upstream, module_local_totals, skip_grad = run_phase(
                backward_stats,
                (module_phase_index,),
                (
                    output_grad,
                    message_grads,
                    module_preact,
                    totals,
                    counts,
                    module_module_gains,
                    module_module_shifts,
                    skip_canvas,
                ),
            )
            grad_totals = lax.psum(module_local_totals, "crops")
            source_grad, weight_parts[module_phase_index], gain_part, shift_part = run_phase(
                backward_apply,
                (module_phase_index,),
                (
                    upstream,
                    module_preact,
                    totals,
                    grad_totals,
                    counts,
                    record.sources[module_phase_index],
                    module_module_weights,
                    module_module_gains,
                ),
            )
            gain_total = gain_total + gain_part
            shift_total = shift_total + shift_part
            if module_phase_index > 2 * BLOCKS:
                chain_grad = source_grad
            elif module_phase_index == 2 * BLOCKS:
                top_grad = top_grad + source_grad
            elif module_phase_index % 2 == 1:
                u_grad = source_grad
                pending_skip = skip_grad
            else:
                top_grad = source_grad + pending_skip
        joined = jnp.concatenate(weight_parts)
        weight_grad = jnp.pad(joined, (0, weights.shape[2] - joined.shape[0]))
        grad_canvas, weight_grad, gain_grads[module], shift_grads[module] = (
            top_grad,
            weight_grad,
            gain_total,
            shift_total,
        )
        module_grads[module] = weight_grad
    weight_out = lax.psum_scatter(jnp.stack(module_grads), "crops", scatter_dimension=1, tiled=True)
    share = gains.shape[3] // shard_count
    gain_out = lax.dynamic_slice_in_dim(jnp.stack(gain_grads), crop_shard * share, share, axis=2)
    shift_out = lax.dynamic_slice_in_dim(jnp.stack(shift_grads), crop_shard * share, share, axis=2)
    return (outputs[None], grad_canvas[None], weight_out[None], gain_out[None], shift_out[None])


LANES = 128
SLOTS = 8
MASKS = 7
DOWN = (((1,), (0,)), ((), ()))
ACROSS = (((1,), (1,)), ((), ()))
ALONG = (((0,), (0,)), ((), ()))


def unit_table(k):
    operations = weighted_plan(k, C0, BLOCKS)
    planes = 8 >> k
    channels = C0 << k
    units = {}
    stat = 0

    def add(name, kind, source, lanes_in, planes_in, planes_out, members):
        nonlocal stat
        segs = []
        tile = 0
        for operation, lanes, chain in members:
            cout = operation.cout
            level = operation.level if operation.taps == 3 else operation.dest
            segs.append(
                SimpleNamespace(
                    slot=operation.slot,
                    off=operation.offset // LANES,
                    cin=operation.cin,
                    cout=cout,
                    taps=operation.taps,
                    tile=tile,
                    tiles=lanes // LANES,
                    blocks=max(1, (8 >> level)),
                    dest=operation.dest,
                    act=operation.act,
                    chain=chain,
                    up=k - operation.dest if operation.taps == 1 else 0,
                )
            )
            tile += lanes // LANES
        rows = {"s1": 768 if k == 3 else 512, "s2": lanes_in + LANES, "p1": 256}[kind]
        units[name] = SimpleNamespace(
            name=name,
            kind=kind,
            source=source,
            lanes_in=lanes_in,
            blocks_in=planes_in,
            planes_in=planes_in,
            planes=planes_out,
            segs=segs,
            tiles=tile,
            rows=rows,
            stat=stat,
            depth=1 if kind == "p1" else 3,
        )
        stat += tile

    add("a", "s1", "h", 256, planes, planes, [(operations[0], 256, None)])
    add("b", "s1", "u", 256, planes, planes, [(operations[1], 256, None)])
    ups = [operation for operation in operations if operation.taps == 1]
    if ups:
        add("u", "p1", "t", 256, planes, planes, [(operation, 256, None) for operation in ups])
    firsts, chains = [], {}
    for target in range(k + 1, 4):
        steps = [
            operation
            for operation in operations
            if operation.taps == 3 and operation.stride == 2
        ]
        start = sum(i - k for i in range(k + 1, target))
        chains[target] = steps[start : start + target - k]
        if target == k + 1:
            firsts.append((chains[target][0], 256, None))
        else:
            firsts.append((chains[target][0], LANES, "c1" if target == k + 2 else "c2"))
    if firsts:
        add("d", "s2", "t", 256, planes, planes // 2, firsts)
    if k <= 1:
        add("e", "s2", "c1", LANES, planes // 2, planes // 4, [(chains[k + 2][1], 256, None)])
    if k == 0:
        add("f", "s2", "c2", LANES, planes // 2, planes // 4, [(chains[3][1], LANES, "c3")])
        add("g", "s2", "c3", LANES, planes // 4, planes // 8, [(chains[3][2], 256, None)])
    return units


def links(k, unit, seg):
    cin = seg.cin
    count_in, count_out = unit.blocks_in, seg.blocks
    found = []
    if unit.kind == "p1":
        for plane in range(count_in):
            wide = 1 << seg.up
            found.append((plane * cin, 0, set(range(plane * wide, plane * wide + wide))))
        return found
    if unit.kind == "s1" and k == 3:
        return [(256 * tap, tap, {0}) for tap in range(3)]
    stride = 1 if unit.kind == "s1" else 2
    for plane in range(count_in):
        for tap in range(3):
            at = plane - tap + 1
            if at % stride == 0 and 0 <= at // stride < count_out:
                found.append((plane * cin, tap, {at // stride}))
    if stride == 1:
        found.append((256, 2, {count_out - 1}))
        found.append((512 - cin, 0, {0}))
    else:
        lanes_in = unit.lanes_in
        found.append((lanes_in + (count_in - 1) * cin - (lanes_in - LANES), 0, {0}))
    return found


def log2(value):
    return value.bit_length() - 1


def sigmoid_of(value):
    return 0.5 * jnp.tanh(0.5 * value) + 0.5


def silu_of(value):
    return value * sigmoid_of(value)


def slope_of(value):
    sigmoid = sigmoid_of(value)
    return sigmoid * (1.0 + value * (1.0 - sigmoid))


def planes_loop(count, body):
    if count == 1:
        body(0)
        return

    def step(index, carry):
        body(index)
        return carry

    lax.fori_loop(0, count, step, 0)


def planes_sum(count, body, initial):
    if count == 1:
        return body(0, initial)
    return lax.fori_loop(0, count, body, initial)


def partial_sum(value):
    rows = value.shape[0]
    return jnp.sum(value.reshape(rows // 8, 8, value.shape[1]), axis=0)


class Planes:
    def __init__(self, mode, tiles, planes, masks, rows, main, edge=None, right=None):
        self.mode, self.tiles, self.planes = mode, tiles, planes
        self.masks, self.rows = masks, rows
        self.main, self.edge, self.right = main, edge, right
        self.base = 1 if mode in ("s1", "wide", "s2") else 0
        extra = {"s1": 2, "wide": 2, "s2": 1, "dz2": 1, "p": 0}[mode]
        self.span = planes + extra
        self.unit = tiles * self.span

    def at(self, m, tile, plane):
        return m * self.unit + tile * self.span + plane + self.base

    def edge_at(self, m, tile, plane):
        if self.mode == "s2":
            return m * self.span + plane + self.base
        return self.at(m, tile, plane)

    def from_left(self, value):
        return pltpu.roll(value, 1, 0) * self.masks[1]

    def from_right(self, value):
        return pltpu.roll(value, self.rows - 1, 0) * self.masks[2]

    def store(self, m, tile, plane, value):
        where = self.at(m, tile, plane)
        self.main[where] = value.astype(jnp.bfloat16)
        if self.mode == "s1":
            side = self.from_right(value) if tile == 0 else self.from_left(value)
            self.edge[where] = side.astype(jnp.bfloat16)
        elif self.mode == "wide":
            self.edge[where] = self.from_left(value).astype(jnp.bfloat16)
            self.right[where] = self.from_right(value).astype(jnp.bfloat16)
        elif self.mode == "s2":
            if tile == self.tiles - 1:
                self.edge[self.edge_at(m, tile, plane)] = self.from_left(value).astype(jnp.bfloat16)
        elif self.mode == "dz2":
            self.edge[where] = self.from_right(value).astype(jnp.bfloat16)

    def close(self, m):
        rows = self.rows
        for tile in range(self.tiles):
            if self.mode in ("s1", "wide", "s2"):
                last = self.main[self.at(m, tile, self.planes - 1)].astype(jnp.float32)
                above = pltpu.roll(last, 6, 0) * self.masks[3] + pltpu.roll(last, 3, 0) * self.masks[4]
                self.store(m, tile, -1, above)
            if self.mode in ("s1", "wide", "dz2"):
                first = self.main[self.at(m, tile, 0)].astype(jnp.float32)
                below = (
                    pltpu.roll(first, rows - 6, 0) * self.masks[5]
                    + pltpu.roll(first, rows - 3, 0) * self.masks[6]
                )
                self.store(m, tile, self.planes, below)


class Branch:
    def __init__(self, k, rows, cells, refs, masks, core):
        self.k, self.rows, self.refs, self.masks = k, rows, refs, masks
        self.units = unit_table(k)
        self.planes = 8 >> k
        self.core = core
        self.cells = cells
        r = refs
        make = partial(Planes, masks=masks, rows=rows)
        one = "wide" if k == 3 else "s1"
        self.maps = dict(
            h=make(one, 2, self.planes, main=r.hC, edge=r.hE, right=r.hR),
            u=make(one, 2, self.planes, main=r.uC, edge=r.uE, right=r.uR),
            t=make("p" if k == 3 else "s2", 2, self.planes, main=r.tC, edge=r.tE),
        )
        if k <= 1:
            self.maps["c1"] = make("s2", 1, self.planes // 2, main=r.c1C, edge=r.c1E)
        if k == 0:
            self.maps["c2"] = make("s2", 1, 4, main=r.c2C, edge=r.c2E)
            self.maps["c3"] = make("s2", 1, 2, main=r.c3C, edge=r.c3E)
        self.grads = dict(t=r.gt, u=r.gu, c1=r.gc1, c2=r.gc2, c3=r.gc3)

    def lane_block(self, shape, cout):
        lanes = lax.broadcasted_iota(jnp.int32, shape, 1)
        return lanes >> log2(cout)

    def keep(self, value, cout, which):
        count = LANES // cout
        if len(which) == count:
            return value
        block = self.lane_block(value.shape, cout)
        mask = block == which[0]
        for entry in which[1:]:
            mask = mask | (block == entry)
        return jnp.where(mask, value, 0.0)

    def spread(self, value, cout):
        shift = LANES // 2
        while shift >= cout:
            value = value + pltpu.roll(value, shift, 1)
            shift //= 2
        return value

    def local_blocks(self, seg, tile, wanted):
        count = LANES // seg.cout
        return [q for q in range(count) if (tile * count + q) % seg.blocks in wanted]


    def fetch(self, m):
        r = self.refs
        copies = []
        lengths = [0] * (2 * BLOCKS + 3)
        starts = [sum(phase_lengths(C0, BLOCKS)[:p]) // LANES for p in range(len(lengths))]
        for operation in weighted_plan(self.k, C0, BLOCKS):
            lengths[operation.phase] += operation.size // LANES
        for phase, length in enumerate(lengths):
            if length:
                span = pl.ds(starts[phase], -(-length // 16) * 16)
                copies.append(
                    pltpu.make_async_copy(r.w.at[m, span], r.wv.at[span], r.wsem.at[phase])
                )
        for copy in copies:
            copy.start()
        for copy in copies:
            copy.wait()

    def expand(self, m):
        for unit in self.units.values():
            for seg in unit.segs:
                self.expand_one(m, unit, seg)

    def expand_one(self, m, unit, seg):
        r = self.refs
        target = getattr(r, "T" + unit.name)
        depth, cin, cout = unit.depth, seg.cin, seg.cout
        taps = seg.taps ** 2
        count = taps * cin * cout // LANES
        first = seg.off // 16 * 16
        skip = seg.off - first
        span = -(-(count + skip) // 16) * 16
        wf, rep = r.wf, r.rep
        wf[0:span] = r.wv[first : first + span].astype(jnp.float32)
        if cout < LANES:
            ratio = LANES // cout
            flat = wf[skip : skip + count]
            for part in range(ratio):
                rep[pl.ds(part, count, stride=ratio)] = self.spread(
                    self.keep(flat, cout, [part]), cout
                )

        def tap_rows(tap, tile):
            if cout < LANES:
                return rep[pl.ds(pl.multiple_of(tap * cin, cin), cin)]
            if cout == LANES:
                return wf[pl.ds(pl.multiple_of(skip + tap * cin, 8), cin)]
            return wf[pl.ds(skip + tap * (2 * cin) + tile, cin, stride=2)]

        by_row = {}
        for row, tap, wanted in links(self.k, unit, seg):
            by_row.setdefault(row, []).append((tap, wanted))

        def fill(d):
            width = 3 if taps == 9 else 1
            for tile in range(seg.tiles):
                column = (seg.tile + tile) * LANES
                for row in range(0, unit.rows, cin):
                    total = None
                    for tap, wanted in by_row.get(row, []):
                        if cout <= LANES:
                            local = self.local_blocks(seg, tile, wanted)
                            if not local:
                                continue
                            piece = self.keep(tap_rows(d * width + tap, 0), cout, local)
                        else:
                            piece = tap_rows(d * width + tap, tile)
                        total = piece if total is None else total + piece
                    if total is None:
                        total = jnp.zeros((cin, LANES), jnp.float32)
                    target[m * depth + d, row : row + cin, column : column + LANES] = total.astype(
                        jnp.bfloat16
                    )

        planes_loop(depth, fill)


    def parts(self, unit, source):
        if unit.kind == "p1":
            return [(source.main, range(2), source.at)]
        if source.mode == "wide":
            return [
                (source.edge, range(2), source.at),
                (source.main, range(2), source.at),
                (source.right, range(2), source.at),
            ]
        if unit.kind == "s1":
            return [(source.main, range(2), source.at), (source.edge, range(2), source.at)]
        last = source.tiles - 1
        return [
            (source.main, range(source.tiles), source.at),
            (source.edge, [last], source.edge_at),
        ]

    def rows_of(self, unit, part, m, d, first, count):
        ref, tiles, at = part
        pieces = []
        for tile in tiles:
            if unit.kind == "s2":
                rows = [ref[at(m, tile, 2 * (first + q) + d - 1)] for q in range(count)]
                pieces.append(rows[0] if count == 1 else jnp.concatenate(rows, axis=0))
            else:
                shift = d - 1 if unit.kind == "s1" else 0
                pieces.append(
                    ref[pl.ds(at(m, tile, first + shift), count)].reshape(count * self.rows, LANES)
                )
        return pieces

    def conv(self, m, unit):
        r = self.refs
        source = self.maps[unit.source]
        target = getattr(r, "T" + unit.name)
        z = getattr(r, "z" + unit.name)
        planes, tiles, depth = unit.planes, unit.tiles, unit.depth
        chunk = min(planes, 4 if tiles <= 2 else 2)
        lanes = tiles * LANES

        def body(step, sums):
            first = step * chunk
            pieces = []
            for d in range(depth):
                for part in self.parts(unit, source):
                    pieces += self.rows_of(unit, part, m, d, first, chunk)
            left = jnp.concatenate(pieces, axis=1)
            right = target[pl.ds(m * depth, depth), 0 : unit.rows, 0:lanes]
            right = right.reshape(depth * unit.rows, lanes)
            result = lax.dot_general(left, right, DOWN, preferred_element_type=jnp.float32)
            for tile in range(tiles):
                block = result[:, tile * LANES : (tile + 1) * LANES]
                z[pl.ds(m * tiles * planes + tile * planes + first, chunk)] = block.reshape(
                    chunk, self.rows, LANES
                )
            return (sums[0] + partial_sum(result), sums[1] + partial_sum(result * result))

        zero = jnp.zeros((8, lanes), jnp.float32)
        sums = planes_sum(planes // chunk, body, (zero, zero))
        for seg in unit.segs:
            scale = self.per_cell(unit, seg)
            totals = self.fold(seg, sums)
            self.norm_rows(m, unit, seg, totals, scale)

    def per_cell(self, unit, seg):
        blocks = seg.tiles * LANES // seg.cout
        small, large = self.cells
        count = unit.planes * blocks
        return jnp.where(self.core == 0, 1.0 / (large * count), 1.0 / (small * count)).astype(
            jnp.float32
        )

    def fold(self, seg, sums):
        first = seg.tile
        found = []
        for value in sums:
            tiles = [
                value[:, (first + t) * LANES : (first + t + 1) * LANES] for t in range(seg.tiles)
            ]
            if seg.cout <= LANES:
                total = tiles[0]
                for tile in tiles[1:]:
                    total = total + tile
                total = jnp.sum(self.spread(total, seg.cout), axis=0, keepdims=True)
                found.append([total] * seg.tiles)
            else:
                found.append([jnp.sum(tile, axis=0, keepdims=True) for tile in tiles])
        return found

    def table_row(self, ref, m, seg, tile):
        slot = seg.slot
        if seg.cout > LANES:
            return ref[m, slot : slot + 1, tile * LANES : (tile + 1) * LANES]
        row = jnp.broadcast_to(ref[m, slot : slot + 1, 0:LANES], (8, LANES))
        if seg.cout < LANES:
            row = self.spread(self.keep(row, seg.cout, [0]), seg.cout)
        return row[0:1]

    def norm_rows(self, m, unit, seg, totals, scale):
        st = self.refs.st
        for tile in range(seg.tiles):
            average = totals[0][tile] * scale
            variance = totals[1][tile] * scale - average * average
            inverse = lax.rsqrt(variance + EPS)
            gain = self.table_row(self.refs.gains, m, seg, tile)
            shift = self.table_row(self.refs.shifts, m, seg, tile)
            where = m * STATS + unit.stat + seg.tile + tile
            factor = gain * inverse
            st[where, 0:1] = average
            st[where, 1:2] = inverse
            st[where, 2:3] = factor
            st[where, 3:4] = shift - average * factor

    def normed(self, m, unit, tile, plane):
        st = self.refs.st
        z = getattr(self.refs, "z" + unit.name)
        where = m * STATS + unit.stat + tile
        value = z[m * unit.tiles * unit.planes + tile * unit.planes + plane]
        return value * st[where, 2:3] + st[where, 3:4]

    def apply_a(self, m):
        unit, u = self.units["a"], self.maps["u"]

        def body(plane):
            for tile in range(2):
                value = silu_of(self.normed(m, unit, tile, plane)) * self.masks[0]
                u.store(m, tile, plane, value)

        planes_loop(self.planes, body)
        u.close(m)

    def apply_b(self, m):
        unit, top = self.units["b"], self.maps["t"]
        hf, s = self.refs.hf, self.refs.s

        def body(plane):
            for tile in range(2):
                where = m * 2 * self.planes + tile * self.planes + plane
                value = silu_of(self.normed(m, unit, tile, plane) + hf[where]) * self.masks[0]
                s[where] = value
                top.store(m, tile, plane, value)

        planes_loop(self.planes, body)
        top.close(m)

    def apply_rest(self, m, unit):
        sb = self.refs.sb
        for seg in unit.segs:
            chain = self.maps[seg.chain] if seg.chain else None

            def body(plane):
                for tile in range(seg.tiles):
                    value = self.normed(m, unit, seg.tile + tile, plane)
                    if chain is not None:
                        chain.store(m, tile, plane, silu_of(value) * self.masks[0])
                    else:
                        sb[m * 32 + seg.dest * 8 + tile * unit.planes + plane] = value.astype(
                            jnp.bfloat16
                        )

            planes_loop(unit.planes, body)
            if chain is not None:
                chain.close(m)
            else:
                self.message(m, seg.dest).start()

    def message(self, e, other):
        count = 2 * (8 >> max(self.k, other))
        r = self.refs
        return pltpu.make_async_remote_copy(
            src_ref=r.sb.at[pl.ds(e * 32 + other * 8, count)],
            dst_ref=r.rb.at[pl.ds(e * 32 + self.k * 8, count)],
            send_sem=r.ssem.at[e * 4 + other],
            recv_sem=r.rsem.at[e * 4 + self.k],
            device_id={"branch": other},
            device_id_type=pl.DeviceIdType.MESH,
        )

    def arrived(self, e, other):
        count = 2 * (8 >> max(self.k, other))
        r = self.refs
        return pltpu.make_async_remote_copy(
            src_ref=r.sb.at[pl.ds(e * 32 + other * 8, count)],
            dst_ref=r.rb.at[pl.ds(e * 32 + other * 8, count)],
            send_sem=r.ssem.at[e * 4 + other],
            recv_sem=r.rsem.at[e * 4 + other],
            device_id={"branch": other},
            device_id_type=pl.DeviceIdType.MESH,
        )

    def others(self):
        return [other for other in range(4) if other != self.k]

    def settle(self, e):
        for other in self.others():
            self.message(e, other).wait_send()
        for other in self.others():
            self.arrived(e, other).wait_recv()

    def receive(self, m):
        r = self.refs
        s, rb, hf, out = r.s, r.rb, r.hf, r.out
        h = self.maps["h"]

        def body(plane):
            for tile in range(2):
                where = m * 2 * self.planes + tile * self.planes + plane
                total = s[where]
                for other in self.others():
                    count = 8 >> max(self.k, other)
                    at = plane >> max(0, other - self.k)
                    total = total + rb[m * 32 + other * 8 + tile * count + at].astype(jnp.float32)
                s[where] = total
                value = silu_of(total) * self.masks[0]
                out[tile * self.planes + plane] = value.astype(jnp.bfloat16)

                @pl.when(m + 1 < MODULES)
                def _():
                    hf[2 * self.planes + tile * self.planes + plane] = value
                    h.store(1, tile, plane, value)

        planes_loop(self.planes, body)

        @pl.when(m + 1 < MODULES)
        def _():
            h.close(1)

    def start(self):
        r = self.refs
        h = self.maps["h"]

        def body(plane):
            for tile in range(2):
                value = r.x[tile * self.planes + plane].astype(jnp.float32)
                r.hf[tile * self.planes + plane] = value
                h.store(0, tile, plane, value)
                r.gin[tile * self.planes + plane] = r.cot[tile * self.planes + plane].astype(
                    jnp.float32
                )

        planes_loop(self.planes, body)
        h.close(0)

    def forward(self, m):
        self.fetch(m)
        self.expand(m)
        self.conv(m, self.units["a"])
        self.apply_a(m)
        self.conv(m, self.units["b"])
        self.apply_b(m)
        for name in ("d", "u", "e", "f", "g"):
            if name in self.units:
                self.conv(m, self.units[name])
                self.apply_rest(m, self.units[name])
        self.settle(m)
        self.receive(m)


    def send_back(self, m):
        r = self.refs
        s, gin, gt, sb = r.s, r.gin, r.gt, r.sb
        e = MODULES + m

        def body(plane):
            for tile in range(2):
                at = tile * self.planes + plane
                value = gin[at] * slope_of(s[m * 2 * self.planes + at])
                gt[at] = value
                for other in range(self.k):
                    sb[e * 32 + other * 8 + at] = value.astype(jnp.bfloat16)

        planes_loop(self.planes, body)
        for other in self.others():
            if other > self.k:
                count = 8 >> other
                wide = 1 << (other - self.k)

                def pool(plane):
                    for tile in range(2):
                        total = gt[tile * self.planes + plane * wide]
                        for step in range(1, wide):
                            total = total + gt[tile * self.planes + plane * wide + step]
                        sb[e * 32 + other * 8 + tile * count + plane] = total.astype(jnp.bfloat16)

                planes_loop(count, pool)
            self.message(e, other).start()

    def back_unit(self, m, unit):
        r = self.refs
        st, dyb, z = r.st, r.dyb, getattr(r, "z" + unit.name)
        name, planes, tiles = unit.name, unit.planes, unit.tiles
        e = MODULES + m
        sums = {}

        def upstream(seg, tile, plane, normed):
            at = tile * planes + plane
            if name == "b":
                hf = r.hf[m * 2 * planes + at]
                value = r.gt[at] * slope_of(normed + hf)
                r.gin[at] = value
                return value
            if name == "a":
                return r.gu[at] * slope_of(normed)
            if seg.chain:
                return self.grads[seg.chain][at] * slope_of(normed)
            return r.rb[e * 32 + seg.dest * 8 + at].astype(jnp.float32)

        for seg in unit.segs:

            def body(plane, carry):
                result = []
                for tile in range(seg.tiles):
                    at = (seg.tile + tile) * planes + plane
                    where = m * STATS + unit.stat + seg.tile + tile
                    value = z[m * tiles * planes + at]
                    normed = value * st[where, 2:3] + st[where, 3:4]
                    dy = upstream(seg, tile, plane, normed)
                    dyb[at] = dy
                    zhat = (value - st[where, 0:1]) * st[where, 1:2]
                    result.append(carry[2 * tile] + partial_sum(dy))
                    result.append(carry[2 * tile + 1] + partial_sum(dy * zhat))
                return tuple(result)

            zero = jnp.zeros((8, LANES), jnp.float32)
            found = planes_sum(planes, body, (zero,) * (2 * seg.tiles))
            pair = [
                jnp.concatenate([found[2 * tile + which] for tile in range(seg.tiles)], axis=1)
                for which in range(2)
            ]
            plain = SimpleNamespace(**vars(seg))
            plain.tile = 0
            totals = self.fold(plain, pair)
            self.table_grads(m, seg, totals)
            sums[seg.slot] = totals
        dz = self.dz_planes(unit)
        for seg in unit.segs:
            scale = self.per_cell(unit, seg)
            totals = sums[seg.slot]

            def apply(plane):
                for tile in range(seg.tiles):
                    at = (seg.tile + tile) * planes + plane
                    where = m * STATS + unit.stat + seg.tile + tile
                    zhat = (z[m * tiles * planes + at] - st[where, 0:1]) * st[where, 1:2]
                    inner = dyb[at] - totals[0][tile] * scale - zhat * (totals[1][tile] * scale)
                    dz.store(0, seg.tile + tile, plane, inner * st[where, 2:3] * self.masks[0])

            planes_loop(planes, apply)
        dz.close(0)
        self.back_data(m, unit, dz)
        self.back_kernel(m, unit, dz)

    def dz_planes(self, unit):
        r = self.refs
        mode = {"p1": "p", "s2": "dz2", "s1": "wide" if self.k == 3 else "s1"}[unit.kind]
        return Planes(
            mode,
            unit.tiles,
            unit.planes,
            self.masks,
            self.rows,
            r.dC,
            r.dE,
            r.dR,
        )

    def table_grads(self, m, seg, totals):
        gg = self.refs.gg
        slot = seg.slot
        for which, found in ((0, totals[1]), (1, totals[0])):
            if seg.cout > LANES:
                for tile in range(2):
                    gg[m, which, slot : slot + 1, tile * LANES : (tile + 1) * LANES] = found[tile]
            else:
                row = jnp.broadcast_to(found[0], (8, LANES))
                if seg.cout < LANES:
                    row = self.keep(row, seg.cout, [0])
                gg[m, which, slot : slot + 1, 0:LANES] = row[0:1]

    def wide_rows(self, ref, at, tiles, plane, count):
        pieces = [
            ref[pl.ds(at(0, tile, plane), count)].reshape(count * self.rows, LANES)
            for tile in range(tiles)
        ]
        return pieces[0] if tiles == 1 else jnp.concatenate(pieces, axis=1)

    def back_data(self, m, unit, dz):
        r = self.refs
        kind, tiles = unit.kind, unit.tiles
        target = getattr(r, "T" + unit.name)
        lanes = tiles * LANES
        rows = self.rows

        def kernel_rows(d, first, count):
            return target[m * unit.depth + d, first : first + count, 0:lanes]

        def product(left, right):
            return lax.dot_general(left, right, ACROSS, preferred_element_type=jnp.float32)

        def put(ref, tile, planes, first, count, value, step=1, add=False):
            block = value.reshape(count, rows, LANES)
            for q in range(count):
                at = tile * planes + first + q * step
                ref[at] = ref[at] + block[q] if add else block[q]

        planes = unit.planes
        if kind == "s1":
            goal = r.gu if unit.name == "b" else r.gin
            add = unit.name == "a"
            if self.k == 3:
                pairs = [(dz.right, 0), (dz.main, 256), (dz.edge, 512)]
            else:
                pairs = [(dz.main, 0), (dz.edge, 256)]
            chunk = min(planes, 4)

            def body(step):
                first = step * chunk
                total = None
                for d in range(3):
                    for ref, at in pairs:
                        left = self.wide_rows(ref, dz.at, 2, first + 1 - d, chunk)
                        piece = product(left, kernel_rows(d, at, 256))
                        total = piece if total is None else total + piece
                for tile in range(2):
                    put(
                        goal,
                        tile,
                        planes,
                        first,
                        chunk,
                        total[:, tile * LANES : (tile + 1) * LANES],
                        add=add,
                    )

            planes_loop(planes // chunk, body)
            return
        if kind == "p1":
            left = self.wide_rows(dz.main, dz.at, tiles, 0, planes)
            total = product(left, kernel_rows(0, 0, 256))
            for tile in range(2):
                put(
                    r.gt,
                    tile,
                    planes,
                    0,
                    planes,
                    total[:, tile * LANES : (tile + 1) * LANES],
                    add=True,
                )
            return
        goal = self.grads[unit.source]
        add = unit.source == "t"
        lanes_in = unit.lanes_in
        count_in = unit.planes_in
        for parity, terms in ((0, [(1, 0)]), (1, [(2, 0), (0, 1)])):
            total, side = None, None
            for d, offset in terms:
                left = self.wide_rows(dz.main, dz.at, tiles, offset, planes)
                piece = product(left, kernel_rows(d, 0, lanes_in))
                total = piece if total is None else total + piece
                left = self.wide_rows(dz.edge, dz.at, tiles, offset, planes)
                piece = product(left, kernel_rows(d, lanes_in, LANES))
                side = piece if side is None else side + piece
            for tile in range(lanes_in // LANES):
                value = total[:, tile * LANES : (tile + 1) * LANES]
                if tile == lanes_in // LANES - 1:
                    value = value + side
                put(goal, tile, count_in, parity, planes, value, step=2, add=add)

    def back_kernel(self, m, unit, dz):
        r = self.refs
        G, rep, wgv = r.G, r.rep, r.wgv
        tiles, planes = unit.tiles, unit.planes
        source = self.maps[unit.source]
        right = self.wide_rows(dz.main, dz.at, tiles, 0, planes)

        def gather(d):
            at = 0
            for part in self.parts(unit, source):
                pieces = self.rows_of(unit, part, m, d, 0, planes)
                left = pieces[0] if len(pieces) == 1 else jnp.concatenate(pieces, axis=1)
                count = left.shape[1]
                result = lax.dot_general(left, right, ALONG, preferred_element_type=jnp.float32)
                for tile in range(tiles):
                    G[d * tiles + tile, at : at + count] = result[
                        :, tile * LANES : (tile + 1) * LANES
                    ]
                at += count

        planes_loop(unit.depth, gather)
        for seg in unit.segs:
            self.fold_kernel(m, unit, seg)

    def fold_kernel(self, m, unit, seg):
        r = self.refs
        G, rep, wgv = r.G, r.rep, r.wgv
        cin, cout, tiles = seg.cin, seg.cout, unit.tiles
        width = 3 if seg.taps == 3 else 1
        found = links(self.k, unit, seg)
        off = seg.off

        def fold(d):
            for column in range(width):
                tap = d * width + column
                totals = []
                for tile in range(seg.tiles):
                    total = None
                    for row, which, wanted in found:
                        if which != column:
                            continue
                        piece = G[d * tiles + seg.tile + tile, row : row + cin]
                        if cout <= LANES:
                            local = self.local_blocks(seg, tile, wanted)
                            if not local:
                                continue
                            piece = self.keep(piece, cout, local)
                        total = piece if total is None else total + piece
                    totals.append(total)
                if cout > LANES:
                    for tile in range(2):
                        wgv[m, pl.ds(off + tap * (2 * cin) + tile, cin, stride=2)] = totals[tile]
                    continue
                total = None
                for piece in totals:
                    if piece is not None:
                        total = piece if total is None else total + piece
                if cout == LANES:
                    wgv[m, pl.ds(pl.multiple_of(off + tap * cin, 8), cin)] = total
                else:
                    rep[pl.ds(pl.multiple_of(tap * cin, cin), cin)] = self.spread(total, cout)

        planes_loop(unit.depth, fold)
        if cout < LANES:
            ratio = LANES // cout
            count = width * width * cin // ratio
            total = None
            for part in range(ratio):
                piece = self.keep(rep[pl.ds(part, count, stride=ratio)], cout, [part])
                total = piece if total is None else total + piece
            wgv[m, off : off + count] = total

    def backward(self, m):
        e = MODULES + m
        self.send_back(m)
        self.settle(e)
        for name in ("g", "f", "e", "d", "u"):
            if name in self.units:
                self.back_unit(m, self.units[name])
        self.back_unit(m, self.units["b"])
        self.back_unit(m, self.units["a"])


STATS = 20
NAMES = list(dict(x=0, cot=0, w=0, gains=0, shifts=0, masks=0, out=0, gin=0, wg=0, gg=0))


def scratch_table(rows, weight_rows):
    def half(count):
        return pltpu.VMEM((count, rows, LANES), jnp.bfloat16)

    def full(count):
        return pltpu.VMEM((count, rows, LANES), jnp.float32)

    def expanded(depth, deep, wide):
        return pltpu.VMEM((MODULES * depth, deep, wide), jnp.bfloat16)

    return dict(
        hC=half(2 * 20),
        hE=half(2 * 20),
        hR=half(2 * 6),
        uC=half(2 * 20),
        uE=half(2 * 20),
        uR=half(2 * 6),
        tC=half(2 * 18),
        tE=half(2 * 9),
        c1C=half(2 * 5),
        c1E=half(2 * 5),
        c2C=half(2 * 5),
        c2E=half(2 * 5),
        c3C=half(2 * 3),
        c3E=half(2 * 3),
        dC=half(20),
        dE=half(20),
        dR=half(6),
        hf=full(2 * 16),
        s=full(2 * 16),
        za=full(2 * 16),
        zb=full(2 * 16),
        zd=full(2 * 16),
        zu=full(2 * 8),
        ze=full(2 * 4),
        zf=full(2 * 2),
        zg=full(2 * 2),
        gt=full(16),
        gu=full(16),
        gc1=full(4),
        gc2=full(4),
        gc3=full(2),
        dyb=full(16),
        sb=half(4 * 32),
        rb=half(4 * 32),
        st=pltpu.VMEM((MODULES * STATS, 8, LANES), jnp.float32),
        Ta=expanded(3, 768, 256),
        Tb=expanded(3, 768, 256),
        Td=expanded(3, 384, 512),
        Tu=expanded(1, 256, 768),
        Te=expanded(3, 256, 256),
        Tf=expanded(3, 256, 128),
        Tg=expanded(3, 256, 256),
        wv=pltpu.VMEM((weight_rows, LANES), jnp.bfloat16),
        wf=pltpu.VMEM((4608, LANES), jnp.float32),
        rep=pltpu.VMEM((640, LANES), jnp.float32),
        G=pltpu.VMEM((12, 768, LANES), jnp.float32),
        wgv=pltpu.VMEM((MODULES, weight_rows, LANES), jnp.float32),
        wsem=pltpu.SemaphoreType.DMA((5,)),
        ssem=pltpu.SemaphoreType.DMA((16,)),
        rsem=pltpu.SemaphoreType.DMA((16,)),
        osem=pltpu.SemaphoreType.DMA((2,)),
    )


def whole_kernel(names, rows, cells, *args):
    refs = SimpleNamespace(**dict(zip(names, args)))
    me = lax.axis_index("branch")
    core = lax.axis_index("crops") % 2
    mask_ref = refs.masks

    class Lazy:
        def __getitem__(self, index):
            return mask_ref[index]

    barrier = pltpu.get_barrier_semaphore()
    for step in range(1, 4):
        pl.semaphore_signal(
            barrier,
            inc=1,
            device_id={"branch": lax.rem(me + step, 4)},
            device_id_type=pl.DeviceIdType.MESH,
        )
    pl.semaphore_wait(barrier, 3)
    refs.wgv[...] = jnp.zeros(refs.wgv.shape, jnp.float32)
    refs.gg[...] = jnp.zeros(refs.gg.shape, jnp.float32)
    for k in range(4):

        @pl.when(me == k)
        def _():
            branch = Branch(k, rows, cells, refs, Lazy(), core)
            branch.start()

            def ahead(m, carry):
                branch.forward(m)
                return carry

            def back(step, carry):
                m = MODULES - 1 - step
                branch.backward(m)
                pltpu.make_async_copy(
                    refs.wgv.at[m], refs.wg.at[m], refs.osem.at[m]
                ).start()
                return carry

            lax.fori_loop(0, MODULES, ahead, 0)
            lax.fori_loop(0, MODULES, back, 0)

    for m in range(MODULES):
        pltpu.make_async_copy(refs.wgv.at[m], refs.wg.at[m], refs.osem.at[m]).wait()


def whole_call(rows, cells, weight_rows, x, cot, w, gains, shifts, masks):
    table = scratch_table(rows, weight_rows)
    vmem = pl.BlockSpec(memory_space=pltpu.VMEM)
    hbm = pl.BlockSpec(memory_space=pl.ANY)
    return pl.pallas_call(
        partial(whole_kernel, NAMES + list(table), rows, cells),
        out_shape=(
            jax.ShapeDtypeStruct((16, rows, LANES), jnp.bfloat16),
            jax.ShapeDtypeStruct((16, rows, LANES), jnp.float32),
            jax.ShapeDtypeStruct((MODULES, weight_rows, LANES), jnp.float32),
            jax.ShapeDtypeStruct((MODULES, 2, SLOTS, 256), jnp.float32),
        ),
        in_specs=[vmem, vmem, hbm, vmem, vmem, vmem],
        out_specs=(vmem, vmem, hbm, vmem),
        scratch_shapes=list(table.values()),
        compiler_params=pltpu.CompilerParams(
            collective_id=0, has_side_effects=True, vmem_limit_bytes=62 * 1024 * 1024
        ),
    )(x, cot, w, gains, shifts, masks)


def mask_table(rows, core, small, large):
    tables = []
    for count, high, wide in ((large, LH // 8, LW // 8), (small, SH // 8, SW // 8)):
        row = np.arange(rows)
        valid = row < count * high * wide
        across, along = row % wide, (row // wide) % high
        six = wide == 6
        tables.append(
            np.stack(
                [
                    valid,
                    valid & (across > 0),
                    valid & (across < wide - 1),
                    valid & (along > 0) & six,
                    valid & (along > 0) & (not six),
                    valid & (along < high - 1) & six,
                    valid & (along < high - 1) & (not six),
                ]
            )
        )
    stacked = np.stack(tables).astype(np.float32)[..., None]
    chosen = lax.dynamic_index_in_dim(jnp.asarray(stacked), core, 0, keepdims=False)
    return jnp.broadcast_to(chosen, (MASKS, rows, LANES))


def group_units(k, large, rows, picked):
    planes = 8 >> k
    high, wide = (LH // 8, LW // 8) if large else (SH // 8, SW // 8)
    count = picked.shape[1]
    used = high * planes * wide * 2
    cells = picked[:, :, :used].reshape(2, count, high, planes, wide, 2, LANES)
    cells = cells.transpose(0, 5, 3, 1, 2, 4, 6).reshape(2, 2 * planes, count * high * wide, LANES)
    return jnp.pad(
        cells, ((0, 0), (0, 16 - 2 * planes), (0, rows - count * high * wide), (0, 0))
    )


def crop_canvas(k, large, units, crop):
    planes = 8 >> k
    high, wide = (LH // 8, LW // 8) if large else (SH // 8, SW // 8)
    cells = lax.dynamic_slice_in_dim(units[: 2 * planes], crop * high * wide, high * wide, axis=1)
    cells = cells.reshape(2, planes, high, wide, LANES).transpose(2, 1, 3, 0, 4)
    flat = cells.reshape(high * planes * wide * 2, LANES)
    return jnp.pad(flat, ((0, ROWS - flat.shape[0]), (0, 0)))


def on_device_grouped(features, weights, gains, shifts, cotangent, size_group):
    shard = lax.axis_index("crops")
    count = lax.axis_size("crops")
    core = shard % 2
    large = count // 4
    small = count - large
    rows = group_rows(count)
    weight_rows = weights.shape[2] // LANES
    case = lax.axis_index("branch") * 2 + core

    pair = jnp.stack([features[0], cotangent[0]])
    gathered = lax.all_gather(pair, "crops", axis=1)
    large_list = jnp.argsort(1 - size_group, stable=True)[:large]
    small_list = jnp.argsort(size_group, stable=True)[:small]
    rank = jnp.where(
        size_group == 1, jnp.cumsum(size_group) - 1, jnp.cumsum(1 - size_group) - 1
    )

    def picking(k, is_large):
        def run(blocks):
            chosen = jnp.take(blocks, large_list if is_large else small_list, axis=1)
            return group_units(k, is_large, rows, chosen)

        return run

    units = lax.switch(
        case, [picking(k, not core_at) for k in range(4) for core_at in range(2)], gathered
    )
    out, grad, weight_grad, table_grad = whole_call(
        rows,
        (small * (SH // 8) * (SW // 8), large * (LH // 8) * (LW // 8)),
        weight_rows,
        units[0],
        units[1],
        weights[0].reshape(MODULES, weight_rows, LANES),
        gains[0],
        shifts[0],
        mask_table(rows, core, small, large),
    )

    def packing(k, is_large):
        def run(out, grad, crops):
            return (
                jnp.stack([crop_canvas(k, is_large, out, crops[i]) for i in range(2)]),
                jnp.stack([crop_canvas(k, is_large, grad, crops[i]) for i in range(2)]),
            )

        return run

    partner = shard + 1 - 2 * core
    mine = rank[shard]
    theirs = rank[partner]
    limit = jnp.where(core == 0, large, small) - 1
    crops = jnp.minimum(jnp.stack([mine, theirs]), limit)
    out, grad = lax.switch(
        case,
        [packing(k, not core_at) for k in range(4) for core_at in range(2)],
        out,
        grad,
        crops,
    )
    swap = [(i, i ^ 1) for i in range(count)]
    share = weights.shape[2] // count
    flat = weight_grad.reshape(MODULES, weight_rows * LANES)
    wide = gains.shape[3] // count

    def slices(at):
        return (
            lax.dynamic_slice_in_dim(flat, at * share, share, axis=1),
            lax.dynamic_slice_in_dim(table_grad, at * wide, wide, axis=3),
        )

    sent = (out[1], grad[1], *slices(partner))
    got = lax.ppermute(sent, "crops", swap)
    own = size_group[shard] != core
    out = jnp.where(own, out[0], got[0])
    grad = jnp.where(own, grad[0], got[1])
    kept = slices(shard)
    weight_out = kept[0] + got[2]
    table_out = kept[1] + got[3]
    return (out[None], grad[None], weight_out[None], table_out[None, :, 0], table_out[None, :, 1])


def group_rows(count):
    large = count // 4
    rows = max(large * (LH // 8) * (LW // 8), (count - large) * (SH // 8) * (SW // 8))
    return -(-rows // 16) * 16


def fits(count):
    return count % 8 == 0 and group_rows(count) <= 96


def solution(mesh):
    placed = (
        P("branch", "crops", None),
        P("branch", None, None),
        P("branch", None, None, None),
        P("branch", None, None, None),
        P("branch", "crops", None),
        P(),
    )
    return jax.shard_map(
        on_device_grouped if fits(mesh.shape["crops"]) else on_device,
        mesh=mesh,
        in_specs=placed,
        out_specs=(
            P("branch", "crops", None),
            P("branch", "crops", None),
            P("branch", None, "crops"),
            P("branch", None, None, "crops"),
            P("branch", None, None, "crops"),
        ),
        check_vma=False,
    )
```

```python
from functools import partial
from types import SimpleNamespace
import math

import jax
import jax.numpy as jnp
import numpy as np
from jax import lax
from jax.experimental import pallas as pl
from jax.experimental.pallas import tpu as pltpu
from jax.sharding import PartitionSpec as P

C0 = 32
BLOCKS = 1
MODULES = 2
CROPS_DEV = 1
SH = 32
SW = 24
LH = 64
LW = 48
ROWS = 768
MSG_ROWS = 384


EPS = 1e-05


def as_sent(x):

    def short(part):
        return part.astype(jnp.bfloat16) if part.dtype == jnp.float32 else part

    return jax.tree.map(short, x)


def sender_plan(branch_index, top_channels, blocks):
    channels = top_channels << branch_index
    operations = []
    for block_index in range(blocks):
        operations.append(
            SimpleNamespace(
                phase=2 * block_index,
                source=("h", block_index),
                level=branch_index,
                cin=channels,
                cout=channels,
                stride=1,
                taps=3,
                act="silu",
                output=("u", block_index),
                skip=None,
                dest=-1,
            )
        )
        operations.append(
            SimpleNamespace(
                phase=2 * block_index + 1,
                source=("u", block_index),
                level=branch_index,
                cin=channels,
                cout=channels,
                stride=1,
                taps=3,
                act="res",
                output=("h", block_index + 1),
                skip=("h", block_index),
                dest=-1,
            )
        )
    top_name = ("h", blocks)
    for target in range(branch_index):
        operations.append(
            SimpleNamespace(
                phase=2 * blocks,
                source=top_name,
                level=branch_index,
                cin=channels,
                cout=top_channels << target,
                stride=1,
                taps=1,
                act="none",
                output=None,
                skip=None,
                dest=target,
            )
        )
    for target in range(branch_index + 1, 4):
        for depth_step in range(1, target - branch_index + 1):
            is_last = depth_step == target - branch_index
            operations.append(
                SimpleNamespace(
                    phase=2 * blocks + depth_step - 1,
                    source=top_name if depth_step == 1 else ("chain", target, depth_step - 1),
                    level=branch_index + depth_step,
                    cin=channels,
                    cout=top_channels << target if is_last else channels,
                    stride=2,
                    taps=3,
                    act="none" if is_last else "silu",
                    output=None if is_last else ("chain", target, depth_step),
                    skip=None,
                    dest=target if is_last else -1,
                )
            )
    for position, operation in enumerate(operations):
        operation.slot = position
        operation.size = (
            operation.taps * operation.taps * operation.cin * operation.cout
        )
        if operation.taps == 1:
            operation.kshape = (operation.cin, operation.cout)
        else:
            operation.kshape = (3, 3, operation.cin, operation.cout)
    return operations


def phase_lengths(top_channels, blocks):
    phase_count = 2 * blocks + 3
    lengths = [0] * phase_count
    for branch_index in range(4):
        per_phase = [0] * phase_count
        for operation in sender_plan(branch_index, top_channels, blocks):
            per_phase[operation.phase] += operation.size
        lengths = [max(current, candidate) for current, candidate in zip(lengths, per_phase)]
    return lengths


def weighted_plan(branch_index, top_channels, blocks):
    lengths = phase_lengths(top_channels, blocks)
    starts = [sum(lengths[:phase_index]) for phase_index in range(len(lengths))]
    running = [0] * len(lengths)
    operations = sender_plan(branch_index, top_channels, blocks)
    for operation in operations:
        phase_index = operation.phase
        operation.inner = running[phase_index]
        operation.offset = starts[phase_index] + running[phase_index]
        operation.position = sum(
            (1 for earlier in operations[: operation.slot] if earlier.phase == phase_index)
        )
        running[phase_index] += operation.size
    return operations


def phase_operations(branch_index, phase_index):
    return [
        operation
        for operation in weighted_plan(branch_index, C0, BLOCKS)
        if operation.phase == phase_index
    ]


def input_names(operations):
    source_names = []
    for operation in operations:
        if operation.source not in source_names:
            source_names.append(operation.source)
    return source_names


def silu_slope(value):
    sigmoid = jax.nn.sigmoid(value)
    return sigmoid * (1.0 + value * (1.0 - sigmoid))


def crop_cells(size_kind):
    return (LH, LW) if size_kind else (SH, SW)


def map_dims(size_kind, level, channels):
    height, breadth = crop_cells(size_kind)
    return (CROPS_DEV, height >> level, breadth >> level, channels)


def source_dims(branch_index, size_kind, map_name):
    level = branch_index + map_name[2] if map_name[0] == "chain" else branch_index
    return map_dims(size_kind, level, C0 << branch_index)


def preact_dims(size_kind, operation):
    return map_dims(size_kind, operation.level, operation.cout)


def to_canvas(arrays, value_type):
    if not arrays:
        return jnp.zeros((ROWS, 128), value_type)
    flattened = jnp.concatenate([array.reshape(-1).astype(value_type) for array in arrays])
    return jnp.pad(flattened, (0, ROWS * 128 - flattened.shape[0])).reshape(ROWS, 128)


def from_canvas(canvas, dims_list):
    flattened = canvas.reshape(-1)
    pieces = []
    offset = 0
    for dims_entry in dims_list:
        count_here = math.prod(dims_entry)
        pieces.append(flattened[offset : offset + count_here].reshape(dims_entry))
        offset += count_here
    return pieces


def to_slot(array):
    flattened = array.reshape(-1)
    return jnp.pad(flattened, (0, MSG_ROWS * 128 - flattened.shape[0])).reshape(MSG_ROWS, 128)


def from_slot(slot_rows, dims_entry):
    return slot_rows.reshape(-1)[: math.prod(dims_entry)].reshape(dims_entry)


def upsample(message, factor):
    crop_count, height, breadth, channels = message.shape
    widened = jnp.broadcast_to(
        message[:, :, None, :, None, :], (crop_count, height, factor, breadth, factor, channels)
    )
    return widened.reshape(crop_count, height * factor, breadth * factor, channels)


def block_pool(array, factor):
    crop_count, height, breadth, channels = array.shape
    return array.reshape(
        crop_count, height // factor, factor, breadth // factor, factor, channels
    ).sum(axis=(2, 4))


def kernel_piece(module_weights, operation):
    start = operation.offset
    return module_weights[start : start + operation.size].reshape(operation.kshape)


def conv_forward(operation, source, kernel):
    if operation.taps == 1:
        return jnp.einsum("nhwc,cd->nhwd", source, kernel, preferred_element_type=jnp.float32)
    stride = operation.stride
    return lax.conv_general_dilated(
        source,
        kernel,
        (stride, stride),
        ((1, 1), (1, 1)),
        dimension_numbers=("NHWC", "HWIO", "NHWC"),
        preferred_element_type=jnp.float32,
    )


def conv_backward(operation, source, kernel, upstream):
    if operation.taps == 1:
        source_grad = jnp.einsum(
            "nhwd,cd->nhwc", upstream, kernel, preferred_element_type=jnp.float32
        )
        kernel_grad = jnp.einsum(
            "nhwc,nhwd->cd", source, upstream, preferred_element_type=jnp.float32
        )
        return (source_grad, kernel_grad)
    stride = operation.stride
    flipped = jnp.transpose(kernel[::-1, ::-1], (0, 1, 3, 2))
    high_pad = 2 if stride == 2 else 1
    source_grad = lax.conv_general_dilated(
        upstream,
        flipped,
        (1, 1),
        ((1, high_pad), (1, high_pad)),
        lhs_dilation=(stride, stride),
        dimension_numbers=("NHWC", "HWIO", "NHWC"),
        preferred_element_type=jnp.float32,
    )
    kernel_grad = lax.conv_general_dilated(
        source,
        upstream,
        (1, 1),
        ((1, 2 - stride), (1, 2 - stride)),
        rhs_dilation=(stride, stride),
        dimension_numbers=("CHWN", "IHWO", "NHWC"),
        preferred_element_type=jnp.float32,
    )
    return (source_grad, jnp.transpose(kernel_grad, (1, 2, 0, 3)))


def cell_total(counts, size_kind, level):
    height, breadth = crop_cells(size_kind)
    return counts[size_kind] * float(CROPS_DEV * (height >> level) * (breadth >> level))


def norm_terms(totals, counts, size_kind, operation):
    cells_here = cell_total(counts, size_kind, operation.level)
    channels = operation.cout
    position = operation.position
    average = totals[size_kind, 0, position, :channels] / cells_here
    variance = totals[size_kind, 1, position, :channels] / cells_here - average * average
    return (average, lax.rsqrt(variance + EPS))


def forward_conv(branch_index, size_kind, phase_index, source_canvas, module_weights):
    operations = phase_operations(branch_index, phase_index)
    source_names = input_names(operations)
    pieces = from_canvas(
        source_canvas, [source_dims(branch_index, size_kind, map_name) for map_name in source_names]
    )
    sources = {
        map_name: piece.astype(jnp.bfloat16) for map_name, piece in zip(source_names, pieces)
    }
    preacts = []
    totals = jnp.zeros((2, 2, 3, 8 * C0), jnp.float32)
    for operation in operations:
        preact = conv_forward(
            operation, sources[operation.source], kernel_piece(module_weights, operation)
        )
        preacts.append(preact)
        channels = operation.cout
        position = operation.position
        totals = totals.at[size_kind, 0, position, :channels].set(jnp.sum(preact, axis=(0, 1, 2)))
        totals = totals.at[size_kind, 1, position, :channels].set(
            jnp.sum(preact * preact, axis=(0, 1, 2))
        )
    return (to_canvas(preacts, jnp.float32), totals)


def forward_norm(
    branch_index,
    size_kind,
    phase_index,
    preact_canvas,
    totals,
    counts,
    module_gains,
    module_shifts,
    skip_canvas,
    message_buffer,
):
    operations = phase_operations(branch_index, phase_index)
    preacts = from_canvas(
        preact_canvas, [preact_dims(size_kind, operation) for operation in operations]
    )
    skip_map = from_canvas(skip_canvas, [map_dims(size_kind, branch_index, C0 << branch_index)])[0]
    produced = []
    for operation, preact in zip(operations, preacts):
        average, inverse_std = norm_terms(totals, counts, size_kind, operation)
        norm_slot = operation.slot
        channels = operation.cout
        normed = (preact - average) * inverse_std * module_gains[
            norm_slot, :channels
        ] + module_shifts[norm_slot, :channels]
        if operation.act == "silu":
            produced.append(jax.nn.silu(normed))
        elif operation.act == "res":
            produced.append(jax.nn.silu(normed + skip_map))
        else:
            message_buffer = message_buffer.at[operation.dest].set(
                to_slot(normed.astype(jnp.bfloat16))
            )
    return (to_canvas(produced, jnp.float32), message_buffer)


def receive_forward(branch_index, size_kind, top_canvas, received):
    channels = C0 << branch_index
    summed = from_canvas(top_canvas, [map_dims(size_kind, branch_index, channels)])[0]
    for sender in range(4):
        if sender < branch_index:
            summed = summed + from_slot(
                received[sender], map_dims(size_kind, branch_index, channels)
            ).astype(jnp.float32)
        elif sender > branch_index:
            coarse = from_slot(received[sender], map_dims(size_kind, sender, channels))
            summed = summed + upsample(coarse, 2 ** (sender - branch_index)).astype(jnp.float32)
    return (to_canvas([jax.nn.silu(summed)], jnp.float32), to_canvas([summed], jnp.float32))


def receive_backward(branch_index, size_kind, grad_canvas, summed_canvas):
    dims_here = map_dims(size_kind, branch_index, C0 << branch_index)
    upstream = from_canvas(grad_canvas, [dims_here])[0]
    summed = from_canvas(summed_canvas, [dims_here])[0]
    summed_grad = upstream * silu_slope(summed)
    buffer = jnp.zeros((4, MSG_ROWS, 128), jnp.bfloat16)
    for sender in range(4):
        if sender < branch_index:
            buffer = buffer.at[sender].set(to_slot(summed_grad.astype(jnp.bfloat16)))
        elif sender > branch_index:
            pooled = block_pool(summed_grad, 2 ** (sender - branch_index))
            buffer = buffer.at[sender].set(to_slot(pooled.astype(jnp.bfloat16)))
    return (to_canvas([summed_grad], jnp.float32), buffer)


def backward_stats(
    branch_index,
    size_kind,
    phase_index,
    dout_canvas,
    message_grads,
    preact_canvas,
    totals,
    counts,
    module_gains,
    module_shifts,
    skip_canvas,
):
    operations = phase_operations(branch_index, phase_index)
    preacts = from_canvas(
        preact_canvas, [preact_dims(size_kind, operation) for operation in operations]
    )
    producing = [operation for operation in operations if operation.act != "none"]
    output_grads = from_canvas(
        dout_canvas, [preact_dims(size_kind, operation) for operation in producing]
    )
    grads_by_name = {
        operation.output: piece for operation, piece in zip(producing, output_grads)
    }
    skip_map = from_canvas(skip_canvas, [map_dims(size_kind, branch_index, C0 << branch_index)])[0]
    upstreams = []
    skip_grads = []
    sums_local = jnp.zeros((2, 2, 3, 8 * C0), jnp.float32)
    for operation, preact in zip(operations, preacts):
        average, inverse_std = norm_terms(totals, counts, size_kind, operation)
        norm_slot = operation.slot
        channels = operation.cout
        centered = (preact - average) * inverse_std
        normed = centered * module_gains[norm_slot, :channels] + module_shifts[norm_slot, :channels]
        if operation.act == "silu":
            upstream = grads_by_name[operation.output] * silu_slope(normed)
        elif operation.act == "res":
            upstream = grads_by_name[operation.output] * silu_slope(normed + skip_map)
            skip_grads.append(upstream)
        else:
            upstream = from_slot(
                message_grads[operation.dest], preact_dims(size_kind, operation)
            ).astype(jnp.float32)
        upstreams.append(upstream)
        position = operation.position
        sums_local = sums_local.at[size_kind, 0, position, :channels].set(
            jnp.sum(upstream, axis=(0, 1, 2))
        )
        sums_local = sums_local.at[size_kind, 1, position, :channels].set(
            jnp.sum(upstream * centered, axis=(0, 1, 2))
        )
    return (to_canvas(upstreams, jnp.float32), sums_local, to_canvas(skip_grads, jnp.float32))


def backward_apply(
    branch_index,
    size_kind,
    phase_index,
    upstream_canvas,
    preact_canvas,
    totals,
    grad_totals,
    counts,
    source_canvas,
    module_weights,
    module_gains,
):
    operations = phase_operations(branch_index, phase_index)
    preacts = from_canvas(
        preact_canvas, [preact_dims(size_kind, operation) for operation in operations]
    )
    upstreams = from_canvas(
        upstream_canvas, [preact_dims(size_kind, operation) for operation in operations]
    )
    source_names = input_names(operations)
    source_list = [source_dims(branch_index, size_kind, map_name) for map_name in source_names]
    pieces = from_canvas(source_canvas, source_list)
    sources = {
        map_name: piece.astype(jnp.bfloat16) for map_name, piece in zip(source_names, pieces)
    }
    source_grads = {
        map_name: jnp.zeros(dims_entry, jnp.float32)
        for map_name, dims_entry in zip(source_names, source_list)
    }
    kernel_grads = []
    slot_count = module_gains.shape[0]
    gain_part = jnp.zeros((slot_count, 8 * C0), jnp.float32)
    shift_part = jnp.zeros((slot_count, 8 * C0), jnp.float32)
    for operation, preact, upstream in zip(operations, preacts, upstreams):
        average, inverse_std = norm_terms(totals, counts, size_kind, operation)
        cells_here = cell_total(counts, size_kind, operation.level)
        norm_slot = operation.slot
        channels = operation.cout
        position = operation.position
        centered = (preact - average) * inverse_std
        mean_upstream = grad_totals[size_kind, 0, position, :channels] / cells_here
        mean_cross = grad_totals[size_kind, 1, position, :channels] / cells_here
        preact_grad = (
            module_gains[norm_slot, :channels]
            * inverse_std
            * (upstream - mean_upstream - centered * mean_cross)
        )
        source_grad, kernel_grad = conv_backward(
            operation,
            sources[operation.source],
            kernel_piece(module_weights, operation),
            preact_grad.astype(jnp.bfloat16),
        )
        source_grads[operation.source] = source_grads[operation.source] + source_grad
        kernel_grads.append(kernel_grad.reshape(-1))
        gain_part = gain_part.at[norm_slot, :channels].set(
            grad_totals[0, 1, position, :channels] + grad_totals[1, 1, position, :channels]
        )
        shift_part = shift_part.at[norm_slot, :channels].set(
            grad_totals[0, 0, position, :channels] + grad_totals[1, 0, position, :channels]
        )
    phase_length = phase_lengths(C0, BLOCKS)[phase_index]
    if kernel_grads:
        joined = jnp.concatenate(kernel_grads)
        weight_part = jnp.pad(joined, (0, phase_length - joined.shape[0]))
    else:
        weight_part = jnp.zeros((phase_length,), jnp.float32)
    return (
        to_canvas([source_grads[map_name] for map_name in source_names], jnp.float32),
        weight_part,
        gain_part,
        shift_part,
    )


def on_device(features, weights, gains, shifts, cotangent, size_group):
    crop_shard = lax.axis_index("crops")
    shard_count = lax.axis_size("crops")
    crop_kind = size_group[crop_shard]
    large_count = jnp.sum(size_group).astype(jnp.float32)
    counts = jnp.stack([shard_count - large_count, large_count])
    case_index = lax.axis_index("branch") * 2 + crop_kind
    phase_total = 2 * BLOCKS + 3
    zero_canvas = jnp.zeros((ROWS, 128), jnp.float32)
    empty_buffer = jnp.zeros((4, MSG_ROWS, 128), jnp.bfloat16)

    def run_phase(function, statics, operands):
        branches_list = [
            partial(function, branch_index, size_kind, *statics)
            for branch_index in range(4)
            for size_kind in range(2)
        ]
        return lax.switch(case_index, branches_list, *operands)

    def statistics(local_totals):
        return lax.psum(local_totals, "crops")

    def module_forward(module, start_canvas, kept):
        module_weights = weights[0, module]
        module_gains = gains[0, module]
        module_shifts = shifts[0, module]
        record = SimpleNamespace(sources=[], preacts=[], totals=[])
        h_canvas = start_canvas
        u_canvas = zero_canvas
        chain_canvas = zero_canvas
        buffer = empty_buffer
        for phase_index in range(phase_total):
            if phase_index < 2 * BLOCKS:
                source = h_canvas if phase_index % 2 == 0 else u_canvas
            elif phase_index == 2 * BLOCKS:
                source = h_canvas
            else:
                source = chain_canvas
            preact, local_totals = run_phase(forward_conv, (phase_index,), (source, module_weights))
            global_totals = kept.totals[phase_index] if kept else statistics(local_totals)
            produced, buffer = run_phase(
                forward_norm,
                (phase_index,),
                (preact, global_totals, counts, module_gains, module_shifts, h_canvas, buffer),
            )
            record.sources.append(source)
            record.preacts.append(preact)
            record.totals.append(global_totals)
            if phase_index < 2 * BLOCKS:
                if phase_index % 2 == 0:
                    u_canvas = produced
                else:
                    h_canvas = produced
            else:
                chain_canvas = produced
        received = (
            kept.received
            if kept
            else jax.tree.map(
                lambda part, own: part.astype(own.dtype),
                lax.all_to_all(as_sent(buffer), "branch", split_axis=0, concat_axis=0, tiled=True),
                buffer,
            )
        )
        result, summed = run_phase(receive_forward, (), (h_canvas, received))
        record.summed = summed
        record.received = received
        return (result, record)

    checkpoints = [features[0].astype(jnp.float32)]
    first_records = []
    for module in range(MODULES):
        result, record = module_forward(module, checkpoints[-1], None)
        checkpoints.append(result)
        first_records.append(record)
    outputs = checkpoints[-1].astype(jnp.bfloat16)
    grad_canvas = cotangent[0].astype(jnp.float32)
    module_grads = [None] * MODULES
    gain_grads = [None] * MODULES
    shift_grads = [None] * MODULES
    for module in reversed(range(MODULES)):
        kept = None
        unused_result, record = module_forward(module, checkpoints[module], kept)
        module_module_weights = weights[0, module]
        module_module_gains = gains[0, module]
        module_module_shifts = shifts[0, module]
        summed_grad, back_buffer = run_phase(receive_backward, (), (grad_canvas, record.summed))
        message_grads = jax.tree.map(
            lambda part, own: part.astype(own.dtype),
            lax.all_to_all(as_sent(back_buffer), "branch", split_axis=0, concat_axis=0, tiled=True),
            back_buffer,
        )
        top_grad = summed_grad
        chain_grad = zero_canvas
        u_grad = zero_canvas
        pending_skip = zero_canvas
        weight_parts = [None] * phase_total
        gain_total = jnp.zeros(gains.shape[2:], jnp.float32)
        shift_total = jnp.zeros(gains.shape[2:], jnp.float32)
        for module_phase_index in reversed(range(phase_total)):
            if module_phase_index >= 2 * BLOCKS:
                output_grad = chain_grad
                skip_canvas = zero_canvas
            elif module_phase_index % 2 == 1:
                output_grad = top_grad
                skip_canvas = record.sources[module_phase_index - 1]
            else:
                output_grad = u_grad
                skip_canvas = zero_canvas
            module_preact = record.preacts[module_phase_index]
            totals = record.totals[module_phase_index]
            upstream, module_local_totals, skip_grad = run_phase(
                backward_stats,
                (module_phase_index,),
                (
                    output_grad,
                    message_grads,
                    module_preact,
                    totals,
                    counts,
                    module_module_gains,
                    module_module_shifts,
                    skip_canvas,
                ),
            )
            grad_totals = lax.psum(module_local_totals, "crops")
            source_grad, weight_parts[module_phase_index], gain_part, shift_part = run_phase(
                backward_apply,
                (module_phase_index,),
                (
                    upstream,
                    module_preact,
                    totals,
                    grad_totals,
                    counts,
                    record.sources[module_phase_index],
                    module_module_weights,
                    module_module_gains,
                ),
            )
            gain_total = gain_total + gain_part
            shift_total = shift_total + shift_part
            if module_phase_index > 2 * BLOCKS:
                chain_grad = source_grad
            elif module_phase_index == 2 * BLOCKS:
                top_grad = top_grad + source_grad
            elif module_phase_index % 2 == 1:
                u_grad = source_grad
                pending_skip = skip_grad
            else:
                top_grad = source_grad + pending_skip
        joined = jnp.concatenate(weight_parts)
        weight_grad = jnp.pad(joined, (0, weights.shape[2] - joined.shape[0]))
        grad_canvas, weight_grad, gain_grads[module], shift_grads[module] = (
            top_grad,
            weight_grad,
            gain_total,
            shift_total,
        )
        module_grads[module] = weight_grad
    weight_out = lax.psum_scatter(jnp.stack(module_grads), "crops", scatter_dimension=1, tiled=True)
    share = gains.shape[3] // shard_count
    gain_out = lax.dynamic_slice_in_dim(jnp.stack(gain_grads), crop_shard * share, share, axis=2)
    shift_out = lax.dynamic_slice_in_dim(jnp.stack(shift_grads), crop_shard * share, share, axis=2)
    return (outputs[None], grad_canvas[None], weight_out[None], gain_out[None], shift_out[None])


LANES = 128
SLOTS = 8
MASKS = 7
DOWN = (((1,), (0,)), ((), ()))
ACROSS = (((1,), (1,)), ((), ()))
ALONG = (((0,), (0,)), ((), ()))


def unit_table(k):
    operations = weighted_plan(k, C0, BLOCKS)
    planes = 8 >> k
    channels = C0 << k
    units = {}
    stat = 0

    def add(name, kind, source, lanes_in, planes_in, planes_out, members):
        nonlocal stat
        segs = []
        tile = 0
        for operation, lanes, chain in members:
            cout = operation.cout
            level = operation.level if operation.taps == 3 else operation.dest
            segs.append(
                SimpleNamespace(
                    slot=operation.slot,
                    off=operation.offset // LANES,
                    cin=operation.cin,
                    cout=cout,
                    taps=operation.taps,
                    tile=tile,
                    tiles=lanes // LANES,
                    blocks=max(1, (8 >> level)),
                    dest=operation.dest,
                    act=operation.act,
                    chain=chain,
                    up=k - operation.dest if operation.taps == 1 else 0,
                )
            )
            tile += lanes // LANES
        rows = {"s1": 768 if k == 3 else 512, "s2": lanes_in + LANES, "p1": 256}[kind]
        units[name] = SimpleNamespace(
            name=name,
            kind=kind,
            source=source,
            lanes_in=lanes_in,
            blocks_in=planes_in,
            planes_in=planes_in,
            planes=planes_out,
            segs=segs,
            tiles=tile,
            rows=rows,
            stat=stat,
            depth=1 if kind == "p1" else 3,
        )
        stat += tile

    add("a", "s1", "h", 256, planes, planes, [(operations[0], 256, None)])
    add("b", "s1", "u", 256, planes, planes, [(operations[1], 256, None)])
    ups = [operation for operation in operations if operation.taps == 1]
    if ups:
        add("u", "p1", "t", 256, planes, planes, [(operation, 256, None) for operation in ups])
    firsts, chains = [], {}
    for target in range(k + 1, 4):
        steps = [
            operation
            for operation in operations
            if operation.taps == 3 and operation.stride == 2
        ]
        start = sum(i - k for i in range(k + 1, target))
        chains[target] = steps[start : start + target - k]
        if target == k + 1:
            firsts.append((chains[target][0], 256, None))
        else:
            firsts.append((chains[target][0], LANES, "c1" if target == k + 2 else "c2"))
    if firsts:
        add("d", "s2", "t", 256, planes, planes // 2, firsts)
    if k <= 1:
        add("e", "s2", "c1", LANES, planes // 2, planes // 4, [(chains[k + 2][1], 256, None)])
    if k == 0:
        add("f", "s2", "c2", LANES, planes // 2, planes // 4, [(chains[3][1], LANES, "c3")])
        add("g", "s2", "c3", LANES, planes // 4, planes // 8, [(chains[3][2], 256, None)])
    return units


def links(k, unit, seg):
    cin = seg.cin
    count_in, count_out = unit.blocks_in, seg.blocks
    found = []
    if unit.kind == "p1":
        for plane in range(count_in):
            wide = 1 << seg.up
            found.append((plane * cin, 0, set(range(plane * wide, plane * wide + wide))))
        return found
    if unit.kind == "s1" and k == 3:
        return [(256 * tap, tap, {0}) for tap in range(3)]
    stride = 1 if unit.kind == "s1" else 2
    for plane in range(count_in):
        for tap in range(3):
            at = plane - tap + 1
            if at % stride == 0 and 0 <= at // stride < count_out:
                found.append((plane * cin, tap, {at // stride}))
    if stride == 1:
        found.append((256, 2, {count_out - 1}))
        found.append((512 - cin, 0, {0}))
    else:
        lanes_in = unit.lanes_in
        found.append((lanes_in + (count_in - 1) * cin - (lanes_in - LANES), 0, {0}))
    return found


def log2(value):
    return value.bit_length() - 1


def sigmoid_of(value):
    return 0.5 * jnp.tanh(0.5 * value) + 0.5


def silu_of(value):
    return value * sigmoid_of(value)


def slope_of(value):
    sigmoid = sigmoid_of(value)
    return sigmoid * (1.0 + value * (1.0 - sigmoid))


def planes_loop(count, body):
    if count == 1:
        body(0)
        return

    def step(index, carry):
        body(index)
        return carry

    lax.fori_loop(0, count, step, 0)


def planes_sum(count, body, initial):
    if count == 1:
        return body(0, initial)
    return lax.fori_loop(0, count, body, initial)


def partial_sum(value):
    rows = value.shape[0]
    return jnp.sum(value.reshape(rows // 8, 8, value.shape[1]), axis=0)


class Planes:
    def __init__(self, mode, tiles, planes, masks, rows, main, edge=None, right=None):
        self.mode, self.tiles, self.planes = mode, tiles, planes
        self.masks, self.rows = masks, rows
        self.main, self.edge, self.right = main, edge, right
        self.base = 1 if mode in ("s1", "wide", "s2") else 0
        extra = {"s1": 2, "wide": 2, "s2": 1, "dz2": 1, "p": 0}[mode]
        self.span = planes + extra
        self.unit = tiles * self.span

    def at(self, m, tile, plane):
        return m * self.unit + tile * self.span + plane + self.base

    def edge_at(self, m, tile, plane):
        if self.mode == "s2":
            return m * self.span + plane + self.base
        return self.at(m, tile, plane)

    def from_left(self, value):
        return pltpu.roll(value, 1, 0) * self.masks[1]

    def from_right(self, value):
        return pltpu.roll(value, self.rows - 1, 0) * self.masks[2]

    def store(self, m, tile, plane, value):
        where = self.at(m, tile, plane)
        self.main[where] = value.astype(jnp.bfloat16)
        if self.mode == "s1":
            side = self.from_right(value) if tile == 0 else self.from_left(value)
            self.edge[where] = side.astype(jnp.bfloat16)
        elif self.mode == "wide":
            self.edge[where] = self.from_left(value).astype(jnp.bfloat16)
            self.right[where] = self.from_right(value).astype(jnp.bfloat16)
        elif self.mode == "s2":
            if tile == self.tiles - 1:
                self.edge[self.edge_at(m, tile, plane)] = self.from_left(value).astype(jnp.bfloat16)
        elif self.mode == "dz2":
            self.edge[where] = self.from_right(value).astype(jnp.bfloat16)

    def close(self, m):
        rows = self.rows
        for tile in range(self.tiles):
            if self.mode in ("s1", "wide", "s2"):
                last = self.main[self.at(m, tile, self.planes - 1)].astype(jnp.float32)
                above = pltpu.roll(last, 6, 0) * self.masks[3] + pltpu.roll(last, 3, 0) * self.masks[4]
                self.store(m, tile, -1, above)
            if self.mode in ("s1", "wide", "dz2"):
                first = self.main[self.at(m, tile, 0)].astype(jnp.float32)
                below = (
                    pltpu.roll(first, rows - 6, 0) * self.masks[5]
                    + pltpu.roll(first, rows - 3, 0) * self.masks[6]
                )
                self.store(m, tile, self.planes, below)


class Branch:
    def __init__(self, k, rows, cells, share, refs, masks, core):
        self.k, self.rows, self.refs, self.masks = k, rows, refs, masks
        self.units = unit_table(k)
        self.planes = 8 >> k
        self.core = core
        self.cells = cells
        self.quarter = lax.axis_index("crops") // 2
        self.share = share
        r = refs
        make = partial(Planes, masks=masks, rows=rows)
        one = "wide" if k == 3 else "s1"
        self.maps = dict(
            h=make(one, 2, self.planes, main=r.hC, edge=r.hE, right=r.hR),
            u=make(one, 2, self.planes, main=r.uC, edge=r.uE, right=r.uR),
            t=make("p" if k == 3 else "s2", 2, self.planes, main=r.tC, edge=r.tE),
        )
        if k <= 1:
            self.maps["c1"] = make("s2", 1, self.planes // 2, main=r.c1C, edge=r.c1E)
        if k == 0:
            self.maps["c2"] = make("s2", 1, 4, main=r.c2C, edge=r.c2E)
            self.maps["c3"] = make("s2", 1, 2, main=r.c3C, edge=r.c3E)
        self.grads = dict(t=r.gt, u=r.gu, c1=r.gc1, c2=r.gc2, c3=r.gc3)

    def lane_block(self, shape, cout):
        lanes = lax.broadcasted_iota(jnp.int32, shape, 1)
        return lanes >> log2(cout)

    def keep(self, value, cout, which):
        count = LANES // cout
        if len(which) == count:
            return value
        block = self.lane_block(value.shape, cout)
        mask = block == which[0]
        for entry in which[1:]:
            mask = mask | (block == entry)
        return jnp.where(mask, value, 0.0)

    def spread(self, value, cout):
        shift = LANES // 2
        while shift >= cout:
            value = value + pltpu.roll(value, shift, 1)
            shift //= 2
        return value

    def local_blocks(self, seg, tile, wanted):
        count = LANES // seg.cout
        return [q for q in range(count) if (tile * count + q) % seg.blocks in wanted]


    def fetch(self, m):
        r = self.refs
        copies = []
        lengths = [0] * (2 * BLOCKS + 3)
        starts = [sum(phase_lengths(C0, BLOCKS)[:p]) // LANES for p in range(len(lengths))]
        for operation in weighted_plan(self.k, C0, BLOCKS):
            lengths[operation.phase] += operation.size // LANES
        for phase, length in enumerate(lengths):
            if length:
                span = pl.ds(starts[phase], -(-length // 16) * 16)
                copies.append(
                    pltpu.make_async_copy(r.w.at[m, span], r.wv.at[span], r.wsem.at[phase])
                )
        for copy in copies:
            copy.start()
        for copy in copies:
            copy.wait()

    def expand(self, m):
        for unit in self.units.values():
            for seg in unit.segs:
                self.expand_one(m, unit, seg)

    def expand_one(self, m, unit, seg):
        r = self.refs
        target = getattr(r, "T" + unit.name)
        depth, cin, cout = unit.depth, seg.cin, seg.cout
        taps = seg.taps ** 2
        count = taps * cin * cout // LANES
        first = seg.off // 16 * 16
        skip = seg.off - first
        span = -(-(count + skip) // 16) * 16
        wf, rep = r.wf, r.rep
        wf[0:span] = r.wv[first : first + span].astype(jnp.float32)
        if cout < LANES:
            ratio = LANES // cout
            flat = wf[skip : skip + count]
            for part in range(ratio):
                rep[pl.ds(part, count, stride=ratio)] = self.spread(
                    self.keep(flat, cout, [part]), cout
                )

        def tap_rows(tap, tile):
            if cout < LANES:
                return rep[pl.ds(pl.multiple_of(tap * cin, cin), cin)]
            if cout == LANES:
                return wf[pl.ds(pl.multiple_of(skip + tap * cin, 8), cin)]
            return wf[pl.ds(skip + tap * (2 * cin) + tile, cin, stride=2)]

        by_row = {}
        for row, tap, wanted in links(self.k, unit, seg):
            by_row.setdefault(row, []).append((tap, wanted))

        def fill(d):
            width = 3 if taps == 9 else 1
            for tile in range(seg.tiles):
                column = (seg.tile + tile) * LANES
                for row in range(0, unit.rows, cin):
                    total = None
                    for tap, wanted in by_row.get(row, []):
                        if cout <= LANES:
                            local = self.local_blocks(seg, tile, wanted)
                            if not local:
                                continue
                            piece = self.keep(tap_rows(d * width + tap, 0), cout, local)
                        else:
                            piece = tap_rows(d * width + tap, tile)
                        total = piece if total is None else total + piece
                    if total is None:
                        total = jnp.zeros((cin, LANES), jnp.float32)
                    target[m * depth + d, row : row + cin, column : column + LANES] = total.astype(
                        jnp.bfloat16
                    )

        planes_loop(depth, fill)


    def parts(self, unit, source):
        if unit.kind == "p1":
            return [(source.main, range(2), source.at)]
        if source.mode == "wide":
            return [
                (source.edge, range(2), source.at),
                (source.main, range(2), source.at),
                (source.right, range(2), source.at),
            ]
        if unit.kind == "s1":
            return [(source.main, range(2), source.at), (source.edge, range(2), source.at)]
        last = source.tiles - 1
        return [
            (source.main, range(source.tiles), source.at),
            (source.edge, [last], source.edge_at),
        ]

    def rows_of(self, unit, part, m, d, first, count):
        ref, tiles, at = part
        pieces = []
        for tile in tiles:
            if unit.kind == "s2":
                rows = [ref[at(m, tile, 2 * (first + q) + d - 1)] for q in range(count)]
                pieces.append(rows[0] if count == 1 else jnp.concatenate(rows, axis=0))
            else:
                shift = d - 1 if unit.kind == "s1" else 0
                pieces.append(
                    ref[pl.ds(at(m, tile, first + shift), count)].reshape(count * self.rows, LANES)
                )
        return pieces

    def conv(self, m, unit):
        r = self.refs
        source = self.maps[unit.source]
        target = getattr(r, "T" + unit.name)
        z = getattr(r, "z" + unit.name)
        planes, tiles, depth = unit.planes, unit.tiles, unit.depth
        chunk = min(planes, 4 if tiles <= 2 else 2)
        lanes = tiles * LANES

        def body(step, sums):
            first = step * chunk
            pieces = []
            for d in range(depth):
                for part in self.parts(unit, source):
                    pieces += self.rows_of(unit, part, m, d, first, chunk)
            left = jnp.concatenate(pieces, axis=1)
            right = target[pl.ds(m * depth, depth), 0 : unit.rows, 0:lanes]
            right = right.reshape(depth * unit.rows, lanes)
            result = lax.dot_general(left, right, DOWN, preferred_element_type=jnp.float32)
            for tile in range(tiles):
                block = result[:, tile * LANES : (tile + 1) * LANES]
                z[pl.ds(m * tiles * planes + tile * planes + first, chunk)] = block.reshape(
                    chunk, self.rows, LANES
                )
            return (sums[0] + partial_sum(result), sums[1] + partial_sum(result * result))

        zero = jnp.zeros((8, lanes), jnp.float32)
        sums = planes_sum(planes // chunk, body, (zero, zero))
        for seg in unit.segs:
            scale = self.per_cell(unit, seg)
            totals = self.fold(seg, sums)
            self.norm_rows(m, unit, seg, totals, scale)

    def per_cell(self, unit, seg):
        blocks = seg.tiles * LANES // seg.cout
        small, large = self.cells
        count = unit.planes * blocks
        return jnp.where(self.core == 0, 1.0 / (large * count), 1.0 / (small * count)).astype(
            jnp.float32
        )

    def fold(self, seg, sums):
        first = seg.tile
        found = []
        for value in sums:
            tiles = [
                value[:, (first + t) * LANES : (first + t + 1) * LANES] for t in range(seg.tiles)
            ]
            if seg.cout <= LANES:
                total = tiles[0]
                for tile in tiles[1:]:
                    total = total + tile
                total = jnp.sum(self.spread(total, seg.cout), axis=0, keepdims=True)
                found.append([total] * seg.tiles)
            else:
                found.append([jnp.sum(tile, axis=0, keepdims=True) for tile in tiles])
        return found

    def table_row(self, ref, m, seg, tile):
        slot = seg.slot
        if seg.cout > LANES:
            return ref[m, slot : slot + 1, tile * LANES : (tile + 1) * LANES]
        row = jnp.broadcast_to(ref[m, slot : slot + 1, 0:LANES], (8, LANES))
        if seg.cout < LANES:
            row = self.spread(self.keep(row, seg.cout, [0]), seg.cout)
        return row[0:1]

    def norm_rows(self, m, unit, seg, totals, scale):
        st = self.refs.st
        for tile in range(seg.tiles):
            average = totals[0][tile] * scale
            variance = totals[1][tile] * scale - average * average
            inverse = lax.rsqrt(variance + EPS)
            gain = self.table_row(self.refs.gains, m, seg, tile)
            shift = self.table_row(self.refs.shifts, m, seg, tile)
            where = m * STATS + unit.stat + seg.tile + tile
            factor = gain * inverse
            st[where, 0:1] = average
            st[where, 1:2] = inverse
            st[where, 2:3] = factor
            st[where, 3:4] = shift - average * factor

    def normed(self, m, unit, tile, plane):
        st = self.refs.st
        z = getattr(self.refs, "z" + unit.name)
        where = m * STATS + unit.stat + tile
        value = z[m * unit.tiles * unit.planes + tile * unit.planes + plane]
        return value * st[where, 2:3] + st[where, 3:4]

    def apply_a(self, m):
        unit, u = self.units["a"], self.maps["u"]

        def body(plane):
            for tile in range(2):
                value = silu_of(self.normed(m, unit, tile, plane)) * self.masks[0]
                u.store(m, tile, plane, value)

        planes_loop(self.planes, body)
        u.close(m)

    def apply_b(self, m):
        unit, top = self.units["b"], self.maps["t"]
        hf, s = self.refs.hf, self.refs.s

        def body(plane):
            for tile in range(2):
                where = m * 2 * self.planes + tile * self.planes + plane
                value = silu_of(self.normed(m, unit, tile, plane) + hf[where]) * self.masks[0]
                s[where] = value
                top.store(m, tile, plane, value)

        planes_loop(self.planes, body)
        top.close(m)

    def apply_rest(self, m, unit):
        sb = self.refs.sb
        for seg in unit.segs:
            chain = self.maps[seg.chain] if seg.chain else None

            def body(plane):
                for tile in range(seg.tiles):
                    value = self.normed(m, unit, seg.tile + tile, plane)
                    if chain is not None:
                        chain.store(m, tile, plane, silu_of(value) * self.masks[0])
                    else:
                        sb[m * 32 + seg.dest * 8 + tile * unit.planes + plane] = value.astype(
                            jnp.bfloat16
                        )

            planes_loop(unit.planes, body)
            if chain is not None:
                chain.close(m)
            else:
                self.message(m, seg.dest).start()

    def message(self, e, other):
        count = 2 * (8 >> max(self.k, other))
        r = self.refs
        return pltpu.make_async_remote_copy(
            src_ref=r.sb.at[pl.ds(e * 32 + other * 8, count)],
            dst_ref=r.rb.at[pl.ds(e * 32 + self.k * 8, count)],
            send_sem=r.ssem.at[e * 4 + other],
            recv_sem=r.rsem.at[e * 4 + self.k],
            device_id={"branch": other},
            device_id_type=pl.DeviceIdType.MESH,
        )

    def arrived(self, e, other):
        count = 2 * (8 >> max(self.k, other))
        r = self.refs
        return pltpu.make_async_remote_copy(
            src_ref=r.sb.at[pl.ds(e * 32 + other * 8, count)],
            dst_ref=r.rb.at[pl.ds(e * 32 + other * 8, count)],
            send_sem=r.ssem.at[e * 4 + other],
            recv_sem=r.rsem.at[e * 4 + other],
            device_id={"branch": other},
            device_id_type=pl.DeviceIdType.MESH,
        )

    def others(self):
        return [other for other in range(4) if other != self.k]

    def settle(self, e):
        for other in self.others():
            self.message(e, other).wait_send()
        for other in self.others():
            self.arrived(e, other).wait_recv()

    def receive(self, m):
        r = self.refs
        s, rb, hf, out = r.s, r.rb, r.hf, r.out
        h = self.maps["h"]

        def body(plane):
            for tile in range(2):
                where = m * 2 * self.planes + tile * self.planes + plane
                total = s[where]
                for other in self.others():
                    count = 8 >> max(self.k, other)
                    at = plane >> max(0, other - self.k)
                    total = total + rb[m * 32 + other * 8 + tile * count + at].astype(jnp.float32)
                s[where] = total
                value = silu_of(total) * self.masks[0]
                out[tile * self.planes + plane] = value.astype(jnp.bfloat16)

                @pl.when(m + 1 < MODULES)
                def _():
                    hf[2 * self.planes + tile * self.planes + plane] = value
                    h.store(1, tile, plane, value)

        planes_loop(self.planes, body)

        @pl.when(m + 1 < MODULES)
        def _():
            h.close(1)

    def start(self):
        r = self.refs
        h = self.maps["h"]

        def body(plane):
            for tile in range(2):
                value = r.x[tile * self.planes + plane].astype(jnp.float32)
                r.hf[tile * self.planes + plane] = value
                h.store(0, tile, plane, value)
                r.gin[tile * self.planes + plane] = r.cot[tile * self.planes + plane].astype(
                    jnp.float32
                )

        planes_loop(self.planes, body)
        h.close(0)

    def forward(self, m):
        self.fetch(m)
        self.expand(m)
        self.conv(m, self.units["a"])
        self.apply_a(m)
        self.conv(m, self.units["b"])
        self.apply_b(m)
        for name in ("d", "u", "e", "f", "g"):
            if name in self.units:
                self.conv(m, self.units[name])
                self.apply_rest(m, self.units[name])
        self.settle(m)
        self.receive(m)


    def send_back(self, m):
        r = self.refs
        s, gin, gt, sb = r.s, r.gin, r.gt, r.sb
        e = MODULES + m

        def body(plane):
            for tile in range(2):
                at = tile * self.planes + plane
                value = gin[at] * slope_of(s[m * 2 * self.planes + at])
                gt[at] = value
                for other in range(self.k):
                    sb[e * 32 + other * 8 + at] = value.astype(jnp.bfloat16)

        planes_loop(self.planes, body)
        for other in reversed(self.others()):
            if other > self.k:
                count = 8 >> other
                wide = 1 << (other - self.k)

                def pool(plane):
                    for tile in range(2):
                        total = gt[tile * self.planes + plane * wide]
                        for step in range(1, wide):
                            total = total + gt[tile * self.planes + plane * wide + step]
                        sb[e * 32 + other * 8 + tile * count + plane] = total.astype(jnp.bfloat16)

                planes_loop(count, pool)
            self.message(e, other).start()

    def back_unit(self, m, unit):
        r = self.refs
        st, dyb, z = r.st, r.dyb, getattr(r, "z" + unit.name)
        name, planes, tiles = unit.name, unit.planes, unit.tiles
        e = MODULES + m
        sums = {}

        def upstream(seg, tile, plane, normed):
            at = tile * planes + plane
            if name == "b":
                hf = r.hf[m * 2 * planes + at]
                value = r.gt[at] * slope_of(normed + hf)
                r.gin[at] = value
                return value
            if name == "a":
                return r.gu[at] * slope_of(normed)
            if seg.chain:
                return self.grads[seg.chain][at] * slope_of(normed)
            return r.rb[e * 32 + seg.dest * 8 + at].astype(jnp.float32)

        for seg in unit.segs:

            def body(plane, carry):
                result = []
                for tile in range(seg.tiles):
                    at = (seg.tile + tile) * planes + plane
                    where = m * STATS + unit.stat + seg.tile + tile
                    value = z[m * tiles * planes + at]
                    normed = value * st[where, 2:3] + st[where, 3:4]
                    dy = upstream(seg, tile, plane, normed)
                    dyb[at] = dy
                    zhat = (value - st[where, 0:1]) * st[where, 1:2]
                    result.append(carry[2 * tile] + partial_sum(dy))
                    result.append(carry[2 * tile + 1] + partial_sum(dy * zhat))
                return tuple(result)

            zero = jnp.zeros((8, LANES), jnp.float32)
            found = planes_sum(planes, body, (zero,) * (2 * seg.tiles))
            pair = [
                jnp.concatenate([found[2 * tile + which] for tile in range(seg.tiles)], axis=1)
                for which in range(2)
            ]
            plain = SimpleNamespace(**vars(seg))
            plain.tile = 0
            totals = self.fold(plain, pair)
            self.table_grads(m, seg, totals)
            sums[seg.slot] = totals
        dz = self.dz_planes(unit)
        for seg in unit.segs:
            scale = self.per_cell(unit, seg)
            totals = sums[seg.slot]

            def apply(plane):
                for tile in range(seg.tiles):
                    at = (seg.tile + tile) * planes + plane
                    where = m * STATS + unit.stat + seg.tile + tile
                    zhat = (z[m * tiles * planes + at] - st[where, 0:1]) * st[where, 1:2]
                    inner = dyb[at] - totals[0][tile] * scale - zhat * (totals[1][tile] * scale)
                    dz.store(0, seg.tile + tile, plane, inner * st[where, 2:3] * self.masks[0])

            planes_loop(planes, apply)
        dz.close(0)
        self.back_data(m, unit, dz)
        first = min(seg.off for seg in unit.segs)
        last = max(seg.off + seg.taps**2 * seg.cin * seg.cout // LANES for seg in unit.segs)
        wanted = (self.quarter * self.share < last) & ((self.quarter + 1) * self.share > first)

        @pl.when(wanted)
        def _():
            self.back_kernel(m, unit, dz)

    def dz_planes(self, unit):
        r = self.refs
        mode = {"p1": "p", "s2": "dz2", "s1": "wide" if self.k == 3 else "s1"}[unit.kind]
        return Planes(
            mode,
            unit.tiles,
            unit.planes,
            self.masks,
            self.rows,
            r.dC,
            r.dE,
            r.dR,
        )

    def table_grads(self, m, seg, totals):
        gg = self.refs.gg
        slot = seg.slot
        for which, found in ((0, totals[1]), (1, totals[0])):
            if seg.cout > LANES:
                for tile in range(2):
                    gg[m, which, slot : slot + 1, tile * LANES : (tile + 1) * LANES] = found[tile]
            else:
                row = jnp.broadcast_to(found[0], (8, LANES))
                if seg.cout < LANES:
                    row = self.keep(row, seg.cout, [0])
                gg[m, which, slot : slot + 1, 0:LANES] = row[0:1]

    def wide_rows(self, ref, at, tiles, plane, count):
        pieces = [
            ref[pl.ds(at(0, tile, plane), count)].reshape(count * self.rows, LANES)
            for tile in range(tiles)
        ]
        return pieces[0] if tiles == 1 else jnp.concatenate(pieces, axis=1)

    def back_data(self, m, unit, dz):
        r = self.refs
        kind, tiles = unit.kind, unit.tiles
        target = getattr(r, "T" + unit.name)
        lanes = tiles * LANES
        rows = self.rows

        def kernel_rows(d, first, count):
            return target[m * unit.depth + d, first : first + count, 0:lanes]

        def product(left, right):
            return lax.dot_general(left, right, ACROSS, preferred_element_type=jnp.float32)

        def put(ref, tile, planes, first, count, value, step=1, add=False):
            block = value.reshape(count, rows, LANES)
            for q in range(count):
                at = tile * planes + first + q * step
                ref[at] = ref[at] + block[q] if add else block[q]

        planes = unit.planes
        if kind == "s1":
            goal = r.gu if unit.name == "b" else r.gin
            add = unit.name == "a"
            if self.k == 3:
                pairs = [(dz.right, 0), (dz.main, 256), (dz.edge, 512)]
            else:
                pairs = [(dz.main, 0), (dz.edge, 256)]
            chunk = min(planes, 4)

            def body(step):
                first = step * chunk
                total = None
                for d in range(3):
                    for ref, at in pairs:
                        left = self.wide_rows(ref, dz.at, 2, first + 1 - d, chunk)
                        piece = product(left, kernel_rows(d, at, 256))
                        total = piece if total is None else total + piece
                for tile in range(2):
                    put(
                        goal,
                        tile,
                        planes,
                        first,
                        chunk,
                        total[:, tile * LANES : (tile + 1) * LANES],
                        add=add,
                    )

            planes_loop(planes // chunk, body)
            return
        if kind == "p1":
            left = self.wide_rows(dz.main, dz.at, tiles, 0, planes)
            total = product(left, kernel_rows(0, 0, 256))
            for tile in range(2):
                put(
                    r.gt,
                    tile,
                    planes,
                    0,
                    planes,
                    total[:, tile * LANES : (tile + 1) * LANES],
                    add=True,
                )
            return
        goal = self.grads[unit.source]
        add = unit.source == "t"
        lanes_in = unit.lanes_in
        count_in = unit.planes_in
        for parity, terms in ((0, [(1, 0)]), (1, [(2, 0), (0, 1)])):
            total, side = None, None
            for d, offset in terms:
                left = self.wide_rows(dz.main, dz.at, tiles, offset, planes)
                piece = product(left, kernel_rows(d, 0, lanes_in))
                total = piece if total is None else total + piece
                left = self.wide_rows(dz.edge, dz.at, tiles, offset, planes)
                piece = product(left, kernel_rows(d, lanes_in, LANES))
                side = piece if side is None else side + piece
            for tile in range(lanes_in // LANES):
                value = total[:, tile * LANES : (tile + 1) * LANES]
                if tile == lanes_in // LANES - 1:
                    value = value + side
                put(goal, tile, count_in, parity, planes, value, step=2, add=add)

    def back_kernel(self, m, unit, dz):
        r = self.refs
        G, rep, wgv = r.G, r.rep, r.wgv
        tiles, planes = unit.tiles, unit.planes
        source = self.maps[unit.source]
        right = self.wide_rows(dz.main, dz.at, tiles, 0, planes)

        def gather(d):
            at = 0
            for part in self.parts(unit, source):
                pieces = self.rows_of(unit, part, m, d, 0, planes)
                left = pieces[0] if len(pieces) == 1 else jnp.concatenate(pieces, axis=1)
                count = left.shape[1]
                result = lax.dot_general(left, right, ALONG, preferred_element_type=jnp.float32)
                for tile in range(tiles):
                    G[d * tiles + tile, at : at + count] = result[
                        :, tile * LANES : (tile + 1) * LANES
                    ]
                at += count

        planes_loop(unit.depth, gather)
        for seg in unit.segs:
            self.fold_kernel(m, unit, seg)

    def fold_kernel(self, m, unit, seg):
        r = self.refs
        G, rep, wgv = r.G, r.rep, r.wgv
        cin, cout, tiles = seg.cin, seg.cout, unit.tiles
        width = 3 if seg.taps == 3 else 1
        found = links(self.k, unit, seg)
        off = seg.off

        def fold(d):
            for column in range(width):
                tap = d * width + column
                totals = []
                for tile in range(seg.tiles):
                    total = None
                    for row, which, wanted in found:
                        if which != column:
                            continue
                        piece = G[d * tiles + seg.tile + tile, row : row + cin]
                        if cout <= LANES:
                            local = self.local_blocks(seg, tile, wanted)
                            if not local:
                                continue
                            piece = self.keep(piece, cout, local)
                        total = piece if total is None else total + piece
                    totals.append(total)
                if cout > LANES:
                    for tile in range(2):
                        wgv[m, pl.ds(off + tap * (2 * cin) + tile, cin, stride=2)] = totals[tile]
                    continue
                total = None
                for piece in totals:
                    if piece is not None:
                        total = piece if total is None else total + piece
                if cout == LANES:
                    wgv[m, pl.ds(pl.multiple_of(off + tap * cin, 8), cin)] = total
                else:
                    rep[pl.ds(pl.multiple_of(tap * cin, cin), cin)] = self.spread(total, cout)

        planes_loop(unit.depth, fold)
        if cout < LANES:
            ratio = LANES // cout
            count = width * width * cin // ratio
            total = None
            for part in range(ratio):
                piece = self.keep(rep[pl.ds(part, count, stride=ratio)], cout, [part])
                total = piece if total is None else total + piece
            wgv[m, off : off + count] = total

    def backward(self, m):
        e = MODULES + m
        self.send_back(m)
        for name in ("g", "f", "e", "d", "u"):
            if name in self.units:
                for seg in self.units[name].segs:
                    if seg.dest >= 0:
                        self.arrived(e, seg.dest).wait_recv()
                self.back_unit(m, self.units[name])
        for other in self.others():
            self.message(e, other).wait_send()
        self.back_unit(m, self.units["b"])
        self.back_unit(m, self.units["a"])


STATS = 20
NAMES = list(dict(x=0, cot=0, w=0, gains=0, shifts=0, masks=0, out=0, gin=0, wg=0, gg=0))


def scratch_table(rows, weight_rows):
    def half(count):
        return pltpu.VMEM((count, rows, LANES), jnp.bfloat16)

    def full(count):
        return pltpu.VMEM((count, rows, LANES), jnp.float32)

    def expanded(depth, deep, wide):
        return pltpu.VMEM((MODULES * depth, deep, wide), jnp.bfloat16)

    return dict(
        hC=half(2 * 20),
        hE=half(2 * 20),
        hR=half(2 * 6),
        uC=half(2 * 20),
        uE=half(2 * 20),
        uR=half(2 * 6),
        tC=half(2 * 18),
        tE=half(2 * 9),
        c1C=half(2 * 5),
        c1E=half(2 * 5),
        c2C=half(2 * 5),
        c2E=half(2 * 5),
        c3C=half(2 * 3),
        c3E=half(2 * 3),
        dC=half(20),
        dE=half(20),
        dR=half(6),
        hf=full(2 * 16),
        s=full(2 * 16),
        za=full(2 * 16),
        zb=full(2 * 16),
        zd=full(2 * 16),
        zu=full(2 * 8),
        ze=full(2 * 4),
        zf=full(2 * 2),
        zg=full(2 * 2),
        gt=full(16),
        gu=full(16),
        gc1=full(4),
        gc2=full(4),
        gc3=full(2),
        dyb=full(16),
        sb=half(4 * 32),
        rb=half(4 * 32),
        st=pltpu.VMEM((MODULES * STATS, 8, LANES), jnp.float32),
        Ta=expanded(3, 768, 256),
        Tb=expanded(3, 768, 256),
        Td=expanded(3, 384, 512),
        Tu=expanded(1, 256, 768),
        Te=expanded(3, 256, 256),
        Tf=expanded(3, 256, 128),
        Tg=expanded(3, 256, 256),
        wv=pltpu.VMEM((weight_rows, LANES), jnp.bfloat16),
        wf=pltpu.VMEM((4608, LANES), jnp.float32),
        rep=pltpu.VMEM((640, LANES), jnp.float32),
        G=pltpu.VMEM((12, 768, LANES), jnp.float32),
        wgv=pltpu.VMEM((MODULES, weight_rows, LANES), jnp.float32),
        wsem=pltpu.SemaphoreType.DMA((5,)),
        ssem=pltpu.SemaphoreType.DMA((16,)),
        rsem=pltpu.SemaphoreType.DMA((16,)),
        osem=pltpu.SemaphoreType.DMA((2,)),
    )


def whole_kernel(names, rows, cells, share, *args):
    refs = SimpleNamespace(**dict(zip(names, args)))
    me = lax.axis_index("branch")
    core = lax.axis_index("crops") % 2
    mask_ref = refs.masks

    class Lazy:
        def __getitem__(self, index):
            return mask_ref[index]

    barrier = pltpu.get_barrier_semaphore()
    for step in range(1, 4):
        pl.semaphore_signal(
            barrier,
            inc=1,
            device_id={"branch": lax.rem(me + step, 4)},
            device_id_type=pl.DeviceIdType.MESH,
        )
    pl.semaphore_wait(barrier, 3)
    refs.wgv[...] = jnp.zeros(refs.wgv.shape, jnp.float32)
    refs.gg[...] = jnp.zeros(refs.gg.shape, jnp.float32)
    for k in range(4):

        @pl.when(me == k)
        def _():
            branch = Branch(k, rows, cells, share, refs, Lazy(), core)
            branch.start()

            def ahead(m, carry):
                branch.forward(m)
                return carry

            def back(step, carry):
                m = MODULES - 1 - step
                branch.backward(m)
                pltpu.make_async_copy(
                    refs.wgv.at[m], refs.wg.at[m], refs.osem.at[m]
                ).start()
                return carry

            lax.fori_loop(0, MODULES, ahead, 0)
            lax.fori_loop(0, MODULES, back, 0)

    for m in range(MODULES):
        pltpu.make_async_copy(refs.wgv.at[m], refs.wg.at[m], refs.osem.at[m]).wait()


def whole_call(rows, cells, share, weight_rows, x, cot, w, gains, shifts, masks):
    table = scratch_table(rows, weight_rows)
    vmem = pl.BlockSpec(memory_space=pltpu.VMEM)
    hbm = pl.BlockSpec(memory_space=pl.ANY)
    return pl.pallas_call(
        partial(whole_kernel, NAMES + list(table), rows, cells, share),
        out_shape=(
            jax.ShapeDtypeStruct((16, rows, LANES), jnp.bfloat16),
            jax.ShapeDtypeStruct((16, rows, LANES), jnp.float32),
            jax.ShapeDtypeStruct((MODULES, weight_rows, LANES), jnp.float32),
            jax.ShapeDtypeStruct((MODULES, 2, SLOTS, 256), jnp.float32),
        ),
        in_specs=[vmem, vmem, hbm, vmem, vmem, vmem],
        out_specs=(vmem, vmem, hbm, vmem),
        scratch_shapes=list(table.values()),
        compiler_params=pltpu.CompilerParams(
            collective_id=0, has_side_effects=True, vmem_limit_bytes=62 * 1024 * 1024
        ),
    )(x, cot, w, gains, shifts, masks)


def mask_table(rows, core, small, large):
    tables = []
    for count, high, wide in ((large, LH // 8, LW // 8), (small, SH // 8, SW // 8)):
        row = np.arange(rows)
        valid = row < count * high * wide
        across, along = row % wide, (row // wide) % high
        six = wide == 6
        tables.append(
            np.stack(
                [
                    valid,
                    valid & (across > 0),
                    valid & (across < wide - 1),
                    valid & (along > 0) & six,
                    valid & (along > 0) & (not six),
                    valid & (along < high - 1) & six,
                    valid & (along < high - 1) & (not six),
                ]
            )
        )
    stacked = np.stack(tables).astype(np.float32)[..., None]
    chosen = lax.dynamic_index_in_dim(jnp.asarray(stacked), core, 0, keepdims=False)
    return jnp.broadcast_to(chosen, (MASKS, rows, LANES))


def group_units(k, large, rows, picked):
    planes = 8 >> k
    high, wide = (LH // 8, LW // 8) if large else (SH // 8, SW // 8)
    count = picked.shape[1]
    used = high * planes * wide * 2
    cells = picked[:, :, :used].reshape(2, count, high, planes, wide, 2, LANES)
    cells = cells.transpose(0, 5, 3, 1, 2, 4, 6).reshape(2, 2 * planes, count * high * wide, LANES)
    return jnp.pad(
        cells, ((0, 0), (0, 16 - 2 * planes), (0, rows - count * high * wide), (0, 0))
    )


def crop_canvas(k, large, units, crop):
    planes = 8 >> k
    high, wide = (LH // 8, LW // 8) if large else (SH // 8, SW // 8)
    cells = lax.dynamic_slice_in_dim(units[: 2 * planes], crop * high * wide, high * wide, axis=1)
    cells = cells.reshape(2, planes, high, wide, LANES).transpose(2, 1, 3, 0, 4)
    flat = cells.reshape(high * planes * wide * 2, LANES)
    return jnp.pad(flat, ((0, ROWS - flat.shape[0]), (0, 0)))


def on_device_grouped(features, weights, gains, shifts, cotangent, size_group):
    shard = lax.axis_index("crops")
    count = lax.axis_size("crops")
    core = shard % 2
    large = count // 4
    small = count - large
    rows = group_rows(count)
    weight_rows = weights.shape[2] // LANES
    case = lax.axis_index("branch") * 2 + core

    pair = jnp.stack([features[0], cotangent[0]])
    gathered = lax.all_gather(pair, "crops", axis=1)
    large_list = jnp.argsort(1 - size_group, stable=True)[:large]
    small_list = jnp.argsort(size_group, stable=True)[:small]
    rank = jnp.where(
        size_group == 1, jnp.cumsum(size_group) - 1, jnp.cumsum(1 - size_group) - 1
    )

    def picking(k, is_large):
        def run(blocks):
            chosen = jnp.take(blocks, large_list if is_large else small_list, axis=1)
            return group_units(k, is_large, rows, chosen)

        return run

    units = lax.switch(
        case, [picking(k, not core_at) for k in range(4) for core_at in range(2)], gathered
    )
    out, grad, weight_grad, table_grad = whole_call(
        rows,
        (small * (SH // 8) * (SW // 8), large * (LH // 8) * (LW // 8)),
        2 * weight_rows // count,
        weight_rows,
        units[0],
        units[1],
        weights[0].reshape(MODULES, weight_rows, LANES),
        gains[0],
        shifts[0],
        mask_table(rows, core, small, large),
    )

    def packing(k, is_large):
        def run(out, grad, crops):
            return (
                jnp.stack([crop_canvas(k, is_large, out, crops[i]) for i in range(2)]),
                jnp.stack([crop_canvas(k, is_large, grad, crops[i]) for i in range(2)]),
            )

        return run

    partner = shard + 1 - 2 * core
    mine = rank[shard]
    theirs = rank[partner]
    limit = jnp.where(core == 0, large, small) - 1
    crops = jnp.minimum(jnp.stack([mine, theirs]), limit)
    out, grad = lax.switch(
        case,
        [packing(k, not core_at) for k in range(4) for core_at in range(2)],
        out,
        grad,
        crops,
    )
    swap = [(i, i ^ 1) for i in range(count)]
    share = weight_rows // count
    wide = gains.shape[3] // count

    def slices(at):
        return (
            lax.dynamic_slice_in_dim(weight_grad, at * share, share, axis=1),
            lax.dynamic_slice_in_dim(table_grad, at * wide, wide, axis=3),
        )

    sent = (out[1], grad[1], *slices(partner))
    got = lax.ppermute(sent, "crops", swap)
    own = size_group[shard] != core
    out = jnp.where(own, out[0], got[0])
    grad = jnp.where(own, grad[0], got[1])
    kept = slices(shard)
    weight_out = (kept[0] + got[2]).reshape(MODULES, share * LANES)
    table_out = kept[1] + got[3]
    return (out[None], grad[None], weight_out[None], table_out[None, :, 0], table_out[None, :, 1])


def group_rows(count):
    large = count // 4
    rows = max(large * (LH // 8) * (LW // 8), (count - large) * (SH // 8) * (SW // 8))
    return -(-rows // 16) * 16


def fits(count):
    return count % 8 == 0 and group_rows(count) <= 96


def solution(mesh):
    placed = (
        P("branch", "crops", None),
        P("branch", None, None),
        P("branch", None, None, None),
        P("branch", None, None, None),
        P("branch", "crops", None),
        P(),
    )
    return jax.shard_map(
        on_device_grouped if fits(mesh.shape["crops"]) else on_device,
        mesh=mesh,
        in_specs=placed,
        out_specs=(
            P("branch", "crops", None),
            P("branch", "crops", None),
            P("branch", None, "crops"),
            P("branch", None, None, "crops"),
            P("branch", None, None, "crops"),
        ),
        check_vma=False,
    )
```

```python
from functools import partial
from types import SimpleNamespace
import math

import jax
import jax.numpy as jnp
import numpy as np
from jax import lax
from jax.experimental import pallas as pl
from jax.experimental.layout import Layout, with_layout_constraint
from jax.experimental.pallas import tpu as pltpu
from jax.sharding import PartitionSpec as P

C0 = 32
BLOCKS = 1
MODULES = 2
CROPS_DEV = 1
SH = 32
SW = 24
LH = 64
LW = 48
ROWS = 768
MSG_ROWS = 384


EPS = 1e-05


def as_sent(x):

    def short(part):
        return part.astype(jnp.bfloat16) if part.dtype == jnp.float32 else part

    return jax.tree.map(short, x)


def sender_plan(branch_index, top_channels, blocks):
    channels = top_channels << branch_index
    operations = []
    for block_index in range(blocks):
        operations.append(
            SimpleNamespace(
                phase=2 * block_index,
                source=("h", block_index),
                level=branch_index,
                cin=channels,
                cout=channels,
                stride=1,
                taps=3,
                act="silu",
                output=("u", block_index),
                skip=None,
                dest=-1,
            )
        )
        operations.append(
            SimpleNamespace(
                phase=2 * block_index + 1,
                source=("u", block_index),
                level=branch_index,
                cin=channels,
                cout=channels,
                stride=1,
                taps=3,
                act="res",
                output=("h", block_index + 1),
                skip=("h", block_index),
                dest=-1,
            )
        )
    top_name = ("h", blocks)
    for target in range(branch_index):
        operations.append(
            SimpleNamespace(
                phase=2 * blocks,
                source=top_name,
                level=branch_index,
                cin=channels,
                cout=top_channels << target,
                stride=1,
                taps=1,
                act="none",
                output=None,
                skip=None,
                dest=target,
            )
        )
    for target in range(branch_index + 1, 4):
        for depth_step in range(1, target - branch_index + 1):
            is_last = depth_step == target - branch_index
            operations.append(
                SimpleNamespace(
                    phase=2 * blocks + depth_step - 1,
                    source=top_name if depth_step == 1 else ("chain", target, depth_step - 1),
                    level=branch_index + depth_step,
                    cin=channels,
                    cout=top_channels << target if is_last else channels,
                    stride=2,
                    taps=3,
                    act="none" if is_last else "silu",
                    output=None if is_last else ("chain", target, depth_step),
                    skip=None,
                    dest=target if is_last else -1,
                )
            )
    for position, operation in enumerate(operations):
        operation.slot = position
        operation.size = (
            operation.taps * operation.taps * operation.cin * operation.cout
        )
        if operation.taps == 1:
            operation.kshape = (operation.cin, operation.cout)
        else:
            operation.kshape = (3, 3, operation.cin, operation.cout)
    return operations


def phase_lengths(top_channels, blocks):
    phase_count = 2 * blocks + 3
    lengths = [0] * phase_count
    for branch_index in range(4):
        per_phase = [0] * phase_count
        for operation in sender_plan(branch_index, top_channels, blocks):
            per_phase[operation.phase] += operation.size
        lengths = [max(current, candidate) for current, candidate in zip(lengths, per_phase)]
    return lengths


def weighted_plan(branch_index, top_channels, blocks):
    lengths = phase_lengths(top_channels, blocks)
    starts = [sum(lengths[:phase_index]) for phase_index in range(len(lengths))]
    running = [0] * len(lengths)
    operations = sender_plan(branch_index, top_channels, blocks)
    for operation in operations:
        phase_index = operation.phase
        operation.inner = running[phase_index]
        operation.offset = starts[phase_index] + running[phase_index]
        operation.position = sum(
            (1 for earlier in operations[: operation.slot] if earlier.phase == phase_index)
        )
        running[phase_index] += operation.size
    return operations


def phase_operations(branch_index, phase_index):
    return [
        operation
        for operation in weighted_plan(branch_index, C0, BLOCKS)
        if operation.phase == phase_index
    ]


def input_names(operations):
    source_names = []
    for operation in operations:
        if operation.source not in source_names:
            source_names.append(operation.source)
    return source_names


def silu_slope(value):
    sigmoid = jax.nn.sigmoid(value)
    return sigmoid * (1.0 + value * (1.0 - sigmoid))


def crop_cells(size_kind):
    return (LH, LW) if size_kind else (SH, SW)


def map_dims(size_kind, level, channels):
    height, breadth = crop_cells(size_kind)
    return (CROPS_DEV, height >> level, breadth >> level, channels)


def source_dims(branch_index, size_kind, map_name):
    level = branch_index + map_name[2] if map_name[0] == "chain" else branch_index
    return map_dims(size_kind, level, C0 << branch_index)


def preact_dims(size_kind, operation):
    return map_dims(size_kind, operation.level, operation.cout)


def to_canvas(arrays, value_type):
    if not arrays:
        return jnp.zeros((ROWS, 128), value_type)
    flattened = jnp.concatenate([array.reshape(-1).astype(value_type) for array in arrays])
    return jnp.pad(flattened, (0, ROWS * 128 - flattened.shape[0])).reshape(ROWS, 128)


def from_canvas(canvas, dims_list):
    flattened = canvas.reshape(-1)
    pieces = []
    offset = 0
    for dims_entry in dims_list:
        count_here = math.prod(dims_entry)
        pieces.append(flattened[offset : offset + count_here].reshape(dims_entry))
        offset += count_here
    return pieces


def to_slot(array):
    flattened = array.reshape(-1)
    return jnp.pad(flattened, (0, MSG_ROWS * 128 - flattened.shape[0])).reshape(MSG_ROWS, 128)


def from_slot(slot_rows, dims_entry):
    return slot_rows.reshape(-1)[: math.prod(dims_entry)].reshape(dims_entry)


def upsample(message, factor):
    crop_count, height, breadth, channels = message.shape
    widened = jnp.broadcast_to(
        message[:, :, None, :, None, :], (crop_count, height, factor, breadth, factor, channels)
    )
    return widened.reshape(crop_count, height * factor, breadth * factor, channels)


def block_pool(array, factor):
    crop_count, height, breadth, channels = array.shape
    return array.reshape(
        crop_count, height // factor, factor, breadth // factor, factor, channels
    ).sum(axis=(2, 4))


def kernel_piece(module_weights, operation):
    start = operation.offset
    return module_weights[start : start + operation.size].reshape(operation.kshape)


def conv_forward(operation, source, kernel):
    if operation.taps == 1:
        return jnp.einsum("nhwc,cd->nhwd", source, kernel, preferred_element_type=jnp.float32)
    stride = operation.stride
    return lax.conv_general_dilated(
        source,
        kernel,
        (stride, stride),
        ((1, 1), (1, 1)),
        dimension_numbers=("NHWC", "HWIO", "NHWC"),
        preferred_element_type=jnp.float32,
    )


def conv_backward(operation, source, kernel, upstream):
    if operation.taps == 1:
        source_grad = jnp.einsum(
            "nhwd,cd->nhwc", upstream, kernel, preferred_element_type=jnp.float32
        )
        kernel_grad = jnp.einsum(
            "nhwc,nhwd->cd", source, upstream, preferred_element_type=jnp.float32
        )
        return (source_grad, kernel_grad)
    stride = operation.stride
    flipped = jnp.transpose(kernel[::-1, ::-1], (0, 1, 3, 2))
    high_pad = 2 if stride == 2 else 1
    source_grad = lax.conv_general_dilated(
        upstream,
        flipped,
        (1, 1),
        ((1, high_pad), (1, high_pad)),
        lhs_dilation=(stride, stride),
        dimension_numbers=("NHWC", "HWIO", "NHWC"),
        preferred_element_type=jnp.float32,
    )
    kernel_grad = lax.conv_general_dilated(
        source,
        upstream,
        (1, 1),
        ((1, 2 - stride), (1, 2 - stride)),
        rhs_dilation=(stride, stride),
        dimension_numbers=("CHWN", "IHWO", "NHWC"),
        preferred_element_type=jnp.float32,
    )
    return (source_grad, jnp.transpose(kernel_grad, (1, 2, 0, 3)))


def cell_total(counts, size_kind, level):
    height, breadth = crop_cells(size_kind)
    return counts[size_kind] * float(CROPS_DEV * (height >> level) * (breadth >> level))


def norm_terms(totals, counts, size_kind, operation):
    cells_here = cell_total(counts, size_kind, operation.level)
    channels = operation.cout
    position = operation.position
    average = totals[size_kind, 0, position, :channels] / cells_here
    variance = totals[size_kind, 1, position, :channels] / cells_here - average * average
    return (average, lax.rsqrt(variance + EPS))


def forward_conv(branch_index, size_kind, phase_index, source_canvas, module_weights):
    operations = phase_operations(branch_index, phase_index)
    source_names = input_names(operations)
    pieces = from_canvas(
        source_canvas, [source_dims(branch_index, size_kind, map_name) for map_name in source_names]
    )
    sources = {
        map_name: piece.astype(jnp.bfloat16) for map_name, piece in zip(source_names, pieces)
    }
    preacts = []
    totals = jnp.zeros((2, 2, 3, 8 * C0), jnp.float32)
    for operation in operations:
        preact = conv_forward(
            operation, sources[operation.source], kernel_piece(module_weights, operation)
        )
        preacts.append(preact)
        channels = operation.cout
        position = operation.position
        totals = totals.at[size_kind, 0, position, :channels].set(jnp.sum(preact, axis=(0, 1, 2)))
        totals = totals.at[size_kind, 1, position, :channels].set(
            jnp.sum(preact * preact, axis=(0, 1, 2))
        )
    return (to_canvas(preacts, jnp.float32), totals)


def forward_norm(
    branch_index,
    size_kind,
    phase_index,
    preact_canvas,
    totals,
    counts,
    module_gains,
    module_shifts,
    skip_canvas,
    message_buffer,
):
    operations = phase_operations(branch_index, phase_index)
    preacts = from_canvas(
        preact_canvas, [preact_dims(size_kind, operation) for operation in operations]
    )
    skip_map = from_canvas(skip_canvas, [map_dims(size_kind, branch_index, C0 << branch_index)])[0]
    produced = []
    for operation, preact in zip(operations, preacts):
        average, inverse_std = norm_terms(totals, counts, size_kind, operation)
        norm_slot = operation.slot
        channels = operation.cout
        normed = (preact - average) * inverse_std * module_gains[
            norm_slot, :channels
        ] + module_shifts[norm_slot, :channels]
        if operation.act == "silu":
            produced.append(jax.nn.silu(normed))
        elif operation.act == "res":
            produced.append(jax.nn.silu(normed + skip_map))
        else:
            message_buffer = message_buffer.at[operation.dest].set(
                to_slot(normed.astype(jnp.bfloat16))
            )
    return (to_canvas(produced, jnp.float32), message_buffer)


def receive_forward(branch_index, size_kind, top_canvas, received):
    channels = C0 << branch_index
    summed = from_canvas(top_canvas, [map_dims(size_kind, branch_index, channels)])[0]
    for sender in range(4):
        if sender < branch_index:
            summed = summed + from_slot(
                received[sender], map_dims(size_kind, branch_index, channels)
            ).astype(jnp.float32)
        elif sender > branch_index:
            coarse = from_slot(received[sender], map_dims(size_kind, sender, channels))
            summed = summed + upsample(coarse, 2 ** (sender - branch_index)).astype(jnp.float32)
    return (to_canvas([jax.nn.silu(summed)], jnp.float32), to_canvas([summed], jnp.float32))


def receive_backward(branch_index, size_kind, grad_canvas, summed_canvas):
    dims_here = map_dims(size_kind, branch_index, C0 << branch_index)
    upstream = from_canvas(grad_canvas, [dims_here])[0]
    summed = from_canvas(summed_canvas, [dims_here])[0]
    summed_grad = upstream * silu_slope(summed)
    buffer = jnp.zeros((4, MSG_ROWS, 128), jnp.bfloat16)
    for sender in range(4):
        if sender < branch_index:
            buffer = buffer.at[sender].set(to_slot(summed_grad.astype(jnp.bfloat16)))
        elif sender > branch_index:
            pooled = block_pool(summed_grad, 2 ** (sender - branch_index))
            buffer = buffer.at[sender].set(to_slot(pooled.astype(jnp.bfloat16)))
    return (to_canvas([summed_grad], jnp.float32), buffer)


def backward_stats(
    branch_index,
    size_kind,
    phase_index,
    dout_canvas,
    message_grads,
    preact_canvas,
    totals,
    counts,
    module_gains,
    module_shifts,
    skip_canvas,
):
    operations = phase_operations(branch_index, phase_index)
    preacts = from_canvas(
        preact_canvas, [preact_dims(size_kind, operation) for operation in operations]
    )
    producing = [operation for operation in operations if operation.act != "none"]
    output_grads = from_canvas(
        dout_canvas, [preact_dims(size_kind, operation) for operation in producing]
    )
    grads_by_name = {
        operation.output: piece for operation, piece in zip(producing, output_grads)
    }
    skip_map = from_canvas(skip_canvas, [map_dims(size_kind, branch_index, C0 << branch_index)])[0]
    upstreams = []
    skip_grads = []
    sums_local = jnp.zeros((2, 2, 3, 8 * C0), jnp.float32)
    for operation, preact in zip(operations, preacts):
        average, inverse_std = norm_terms(totals, counts, size_kind, operation)
        norm_slot = operation.slot
        channels = operation.cout
        centered = (preact - average) * inverse_std
        normed = centered * module_gains[norm_slot, :channels] + module_shifts[norm_slot, :channels]
        if operation.act == "silu":
            upstream = grads_by_name[operation.output] * silu_slope(normed)
        elif operation.act == "res":
            upstream = grads_by_name[operation.output] * silu_slope(normed + skip_map)
            skip_grads.append(upstream)
        else:
            upstream = from_slot(
                message_grads[operation.dest], preact_dims(size_kind, operation)
            ).astype(jnp.float32)
        upstreams.append(upstream)
        position = operation.position
        sums_local = sums_local.at[size_kind, 0, position, :channels].set(
            jnp.sum(upstream, axis=(0, 1, 2))
        )
        sums_local = sums_local.at[size_kind, 1, position, :channels].set(
            jnp.sum(upstream * centered, axis=(0, 1, 2))
        )
    return (to_canvas(upstreams, jnp.float32), sums_local, to_canvas(skip_grads, jnp.float32))


def backward_apply(
    branch_index,
    size_kind,
    phase_index,
    upstream_canvas,
    preact_canvas,
    totals,
    grad_totals,
    counts,
    source_canvas,
    module_weights,
    module_gains,
):
    operations = phase_operations(branch_index, phase_index)
    preacts = from_canvas(
        preact_canvas, [preact_dims(size_kind, operation) for operation in operations]
    )
    upstreams = from_canvas(
        upstream_canvas, [preact_dims(size_kind, operation) for operation in operations]
    )
    source_names = input_names(operations)
    source_list = [source_dims(branch_index, size_kind, map_name) for map_name in source_names]
    pieces = from_canvas(source_canvas, source_list)
    sources = {
        map_name: piece.astype(jnp.bfloat16) for map_name, piece in zip(source_names, pieces)
    }
    source_grads = {
        map_name: jnp.zeros(dims_entry, jnp.float32)
        for map_name, dims_entry in zip(source_names, source_list)
    }
    kernel_grads = []
    slot_count = module_gains.shape[0]
    gain_part = jnp.zeros((slot_count, 8 * C0), jnp.float32)
    shift_part = jnp.zeros((slot_count, 8 * C0), jnp.float32)
    for operation, preact, upstream in zip(operations, preacts, upstreams):
        average, inverse_std = norm_terms(totals, counts, size_kind, operation)
        cells_here = cell_total(counts, size_kind, operation.level)
        norm_slot = operation.slot
        channels = operation.cout
        position = operation.position
        centered = (preact - average) * inverse_std
        mean_upstream = grad_totals[size_kind, 0, position, :channels] / cells_here
        mean_cross = grad_totals[size_kind, 1, position, :channels] / cells_here
        preact_grad = (
            module_gains[norm_slot, :channels]
            * inverse_std
            * (upstream - mean_upstream - centered * mean_cross)
        )
        source_grad, kernel_grad = conv_backward(
            operation,
            sources[operation.source],
            kernel_piece(module_weights, operation),
            preact_grad.astype(jnp.bfloat16),
        )
        source_grads[operation.source] = source_grads[operation.source] + source_grad
        kernel_grads.append(kernel_grad.reshape(-1))
        gain_part = gain_part.at[norm_slot, :channels].set(
            grad_totals[0, 1, position, :channels] + grad_totals[1, 1, position, :channels]
        )
        shift_part = shift_part.at[norm_slot, :channels].set(
            grad_totals[0, 0, position, :channels] + grad_totals[1, 0, position, :channels]
        )
    phase_length = phase_lengths(C0, BLOCKS)[phase_index]
    if kernel_grads:
        joined = jnp.concatenate(kernel_grads)
        weight_part = jnp.pad(joined, (0, phase_length - joined.shape[0]))
    else:
        weight_part = jnp.zeros((phase_length,), jnp.float32)
    return (
        to_canvas([source_grads[map_name] for map_name in source_names], jnp.float32),
        weight_part,
        gain_part,
        shift_part,
    )


def on_device(features, weights, gains, shifts, cotangent, size_group):
    crop_shard = lax.axis_index("crops")
    shard_count = lax.axis_size("crops")
    crop_kind = size_group[crop_shard]
    large_count = jnp.sum(size_group).astype(jnp.float32)
    counts = jnp.stack([shard_count - large_count, large_count])
    case_index = lax.axis_index("branch") * 2 + crop_kind
    phase_total = 2 * BLOCKS + 3
    zero_canvas = jnp.zeros((ROWS, 128), jnp.float32)
    empty_buffer = jnp.zeros((4, MSG_ROWS, 128), jnp.bfloat16)

    def run_phase(function, statics, operands):
        branches_list = [
            partial(function, branch_index, size_kind, *statics)
            for branch_index in range(4)
            for size_kind in range(2)
        ]
        return lax.switch(case_index, branches_list, *operands)

    def statistics(local_totals):
        return lax.psum(local_totals, "crops")

    def module_forward(module, start_canvas, kept):
        module_weights = weights[0, module]
        module_gains = gains[0, module]
        module_shifts = shifts[0, module]
        record = SimpleNamespace(sources=[], preacts=[], totals=[])
        h_canvas = start_canvas
        u_canvas = zero_canvas
        chain_canvas = zero_canvas
        buffer = empty_buffer
        for phase_index in range(phase_total):
            if phase_index < 2 * BLOCKS:
                source = h_canvas if phase_index % 2 == 0 else u_canvas
            elif phase_index == 2 * BLOCKS:
                source = h_canvas
            else:
                source = chain_canvas
            preact, local_totals = run_phase(forward_conv, (phase_index,), (source, module_weights))
            global_totals = kept.totals[phase_index] if kept else statistics(local_totals)
            produced, buffer = run_phase(
                forward_norm,
                (phase_index,),
                (preact, global_totals, counts, module_gains, module_shifts, h_canvas, buffer),
            )
            record.sources.append(source)
            record.preacts.append(preact)
            record.totals.append(global_totals)
            if phase_index < 2 * BLOCKS:
                if phase_index % 2 == 0:
                    u_canvas = produced
                else:
                    h_canvas = produced
            else:
                chain_canvas = produced
        received = (
            kept.received
            if kept
            else jax.tree.map(
                lambda part, own: part.astype(own.dtype),
                lax.all_to_all(as_sent(buffer), "branch", split_axis=0, concat_axis=0, tiled=True),
                buffer,
            )
        )
        result, summed = run_phase(receive_forward, (), (h_canvas, received))
        record.summed = summed
        record.received = received
        return (result, record)

    checkpoints = [features[0].astype(jnp.float32)]
    first_records = []
    for module in range(MODULES):
        result, record = module_forward(module, checkpoints[-1], None)
        checkpoints.append(result)
        first_records.append(record)
    outputs = checkpoints[-1].astype(jnp.bfloat16)
    grad_canvas = cotangent[0].astype(jnp.float32)
    module_grads = [None] * MODULES
    gain_grads = [None] * MODULES
    shift_grads = [None] * MODULES
    for module in reversed(range(MODULES)):
        kept = None
        unused_result, record = module_forward(module, checkpoints[module], kept)
        module_module_weights = weights[0, module]
        module_module_gains = gains[0, module]
        module_module_shifts = shifts[0, module]
        summed_grad, back_buffer = run_phase(receive_backward, (), (grad_canvas, record.summed))
        message_grads = jax.tree.map(
            lambda part, own: part.astype(own.dtype),
            lax.all_to_all(as_sent(back_buffer), "branch", split_axis=0, concat_axis=0, tiled=True),
            back_buffer,
        )
        top_grad = summed_grad
        chain_grad = zero_canvas
        u_grad = zero_canvas
        pending_skip = zero_canvas
        weight_parts = [None] * phase_total
        gain_total = jnp.zeros(gains.shape[2:], jnp.float32)
        shift_total = jnp.zeros(gains.shape[2:], jnp.float32)
        for module_phase_index in reversed(range(phase_total)):
            if module_phase_index >= 2 * BLOCKS:
                output_grad = chain_grad
                skip_canvas = zero_canvas
            elif module_phase_index % 2 == 1:
                output_grad = top_grad
                skip_canvas = record.sources[module_phase_index - 1]
            else:
                output_grad = u_grad
                skip_canvas = zero_canvas
            module_preact = record.preacts[module_phase_index]
            totals = record.totals[module_phase_index]
            upstream, module_local_totals, skip_grad = run_phase(
                backward_stats,
                (module_phase_index,),
                (
                    output_grad,
                    message_grads,
                    module_preact,
                    totals,
                    counts,
                    module_module_gains,
                    module_module_shifts,
                    skip_canvas,
                ),
            )
            grad_totals = lax.psum(module_local_totals, "crops")
            source_grad, weight_parts[module_phase_index], gain_part, shift_part = run_phase(
                backward_apply,
                (module_phase_index,),
                (
                    upstream,
                    module_preact,
                    totals,
                    grad_totals,
                    counts,
                    record.sources[module_phase_index],
                    module_module_weights,
                    module_module_gains,
                ),
            )
            gain_total = gain_total + gain_part
            shift_total = shift_total + shift_part
            if module_phase_index > 2 * BLOCKS:
                chain_grad = source_grad
            elif module_phase_index == 2 * BLOCKS:
                top_grad = top_grad + source_grad
            elif module_phase_index % 2 == 1:
                u_grad = source_grad
                pending_skip = skip_grad
            else:
                top_grad = source_grad + pending_skip
        joined = jnp.concatenate(weight_parts)
        weight_grad = jnp.pad(joined, (0, weights.shape[2] - joined.shape[0]))
        grad_canvas, weight_grad, gain_grads[module], shift_grads[module] = (
            top_grad,
            weight_grad,
            gain_total,
            shift_total,
        )
        module_grads[module] = weight_grad
    weight_out = lax.psum_scatter(jnp.stack(module_grads), "crops", scatter_dimension=1, tiled=True)
    share = gains.shape[3] // shard_count
    gain_out = lax.dynamic_slice_in_dim(jnp.stack(gain_grads), crop_shard * share, share, axis=2)
    shift_out = lax.dynamic_slice_in_dim(jnp.stack(shift_grads), crop_shard * share, share, axis=2)
    return (outputs[None], grad_canvas[None], weight_out[None], gain_out[None], shift_out[None])


LANES = 128
SLOTS = 8
MASKS = 7
DOWN = (((1,), (0,)), ((), ()))
ACROSS = (((1,), (1,)), ((), ()))
ALONG = (((0,), (0,)), ((), ()))


def unit_table(k):
    operations = weighted_plan(k, C0, BLOCKS)
    planes = 8 >> k
    channels = C0 << k
    units = {}
    stat = 0

    def add(name, kind, source, lanes_in, planes_in, planes_out, members):
        nonlocal stat
        segs = []
        tile = 0
        for operation, lanes, chain in members:
            cout = operation.cout
            level = operation.level if operation.taps == 3 else operation.dest
            segs.append(
                SimpleNamespace(
                    slot=operation.slot,
                    off=operation.offset // LANES,
                    cin=operation.cin,
                    cout=cout,
                    taps=operation.taps,
                    tile=tile,
                    tiles=lanes // LANES,
                    blocks=max(1, (8 >> level)),
                    dest=operation.dest,
                    act=operation.act,
                    chain=chain,
                    up=k - operation.dest if operation.taps == 1 else 0,
                )
            )
            tile += lanes // LANES
        rows = {"s1": 768 if k == 3 else 512, "s2": lanes_in + LANES, "p1": 256}[kind]
        units[name] = SimpleNamespace(
            name=name,
            kind=kind,
            source=source,
            lanes_in=lanes_in,
            blocks_in=planes_in,
            planes_in=planes_in,
            planes=planes_out,
            segs=segs,
            tiles=tile,
            rows=rows,
            stat=stat,
            depth=1 if kind == "p1" else 3,
        )
        stat += tile

    add("a", "s1", "h", 256, planes, planes, [(operations[0], 256, None)])
    add("b", "s1", "u", 256, planes, planes, [(operations[1], 256, None)])
    ups = [operation for operation in operations if operation.taps == 1]
    if ups:
        add("u", "p1", "t", 256, planes, planes, [(operation, 256, None) for operation in ups])
    firsts, chains = [], {}
    for target in range(k + 1, 4):
        steps = [
            operation
            for operation in operations
            if operation.taps == 3 and operation.stride == 2
        ]
        start = sum(i - k for i in range(k + 1, target))
        chains[target] = steps[start : start + target - k]
        if target == k + 1:
            firsts.append((chains[target][0], 256, None))
        else:
            firsts.append((chains[target][0], LANES, "c1" if target == k + 2 else "c2"))
    if firsts:
        add("d", "s2", "t", 256, planes, planes // 2, firsts)
    if k <= 1:
        add("e", "s2", "c1", LANES, planes // 2, planes // 4, [(chains[k + 2][1], 256, None)])
    if k == 0:
        add("f", "s2", "c2", LANES, planes // 2, planes // 4, [(chains[3][1], LANES, "c3")])
        add("g", "s2", "c3", LANES, planes // 4, planes // 8, [(chains[3][2], 256, None)])
    return units


def links(k, unit, seg):
    cin = seg.cin
    count_in, count_out = unit.blocks_in, seg.blocks
    found = []
    if unit.kind == "p1":
        for plane in range(count_in):
            wide = 1 << seg.up
            found.append((plane * cin, 0, set(range(plane * wide, plane * wide + wide))))
        return found
    if unit.kind == "s1" and k == 3:
        return [(256 * tap, tap, {0}) for tap in range(3)]
    stride = 1 if unit.kind == "s1" else 2
    for plane in range(count_in):
        for tap in range(3):
            at = plane - tap + 1
            if at % stride == 0 and 0 <= at // stride < count_out:
                found.append((plane * cin, tap, {at // stride}))
    if stride == 1:
        found.append((256, 2, {count_out - 1}))
        found.append((512 - cin, 0, {0}))
    else:
        lanes_in = unit.lanes_in
        found.append((lanes_in + (count_in - 1) * cin - (lanes_in - LANES), 0, {0}))
    return found


def message_slot(k, other):
    return sum(2 * (8 >> max(k, before)) for before in range(other) if before != k)


def log2(value):
    return value.bit_length() - 1


def sigmoid_of(value):
    return 0.5 * jnp.tanh(0.5 * value) + 0.5


def silu_of(value):
    return value * sigmoid_of(value)


def slope_of(value):
    sigmoid = sigmoid_of(value)
    return sigmoid * (1.0 + value * (1.0 - sigmoid))


def planes_loop(count, body):
    if count == 1:
        body(0)
        return

    def step(index, carry):
        body(index)
        return carry

    lax.fori_loop(0, count, step, 0)


def planes_sum(count, body, initial):
    if count == 1:
        return body(0, initial)
    return lax.fori_loop(0, count, body, initial)


def partial_sum(value):
    rows = value.shape[0]
    return jnp.sum(value.reshape(rows // 8, 8, value.shape[1]), axis=0)


class Planes:
    def __init__(self, mode, tiles, planes, masks, rows, main, edge=None, right=None):
        self.mode, self.tiles, self.planes = mode, tiles, planes
        self.masks, self.rows = masks, rows
        self.main, self.edge, self.right = main, edge, right
        self.base = 1 if mode in ("s1", "wide", "s2") else 0
        extra = {"s1": 2, "wide": 2, "s2": 1, "dz2": 1, "p": 0}[mode]
        self.span = planes + extra
        self.unit = tiles * self.span

    def at(self, m, tile, plane):
        return m * self.unit + tile * self.span + plane + self.base

    def edge_at(self, m, tile, plane):
        if self.mode == "s2":
            return m * self.span + plane + self.base
        return self.at(m, tile, plane)

    def from_left(self, value):
        return pltpu.roll(value, 1, 0) * self.masks[1]

    def from_right(self, value):
        return pltpu.roll(value, self.rows - 1, 0) * self.masks[2]

    def store(self, m, tile, plane, value):
        where = self.at(m, tile, plane)
        self.main[where] = value.astype(jnp.bfloat16)
        if self.mode == "s1":
            side = self.from_right(value) if tile == 0 else self.from_left(value)
            self.edge[where] = side.astype(jnp.bfloat16)
        elif self.mode == "wide":
            self.edge[where] = self.from_left(value).astype(jnp.bfloat16)
            self.right[where] = self.from_right(value).astype(jnp.bfloat16)
        elif self.mode == "s2":
            if tile == self.tiles - 1:
                self.edge[self.edge_at(m, tile, plane)] = self.from_left(value).astype(jnp.bfloat16)
        elif self.mode == "dz2":
            self.edge[where] = self.from_right(value).astype(jnp.bfloat16)

    def close(self, m):
        rows = self.rows
        for tile in range(self.tiles):
            if self.mode in ("s1", "wide", "s2"):
                last = self.main[self.at(m, tile, self.planes - 1)].astype(jnp.float32)
                above = pltpu.roll(last, 6, 0) * self.masks[3] + pltpu.roll(last, 3, 0) * self.masks[4]
                self.store(m, tile, -1, above)
            if self.mode in ("s1", "wide", "dz2"):
                first = self.main[self.at(m, tile, 0)].astype(jnp.float32)
                below = (
                    pltpu.roll(first, rows - 6, 0) * self.masks[5]
                    + pltpu.roll(first, rows - 3, 0) * self.masks[6]
                )
                self.store(m, tile, self.planes, below)


class Branch:
    def __init__(self, k, rows, large, small, share, refs, masks, core):
        self.k, self.rows, self.refs, self.masks = k, rows, refs, masks
        self.units = unit_table(k)
        self.planes = 8 >> k
        self.core = core
        self.large, self.small, self.count = large, small, large + small
        self.cells = (small * (SH // 8) * (SW // 8), large * (LH // 8) * (LW // 8))
        self.quarter = lax.axis_index("crops") // 2
        self.share = share
        r = refs
        make = partial(Planes, masks=masks, rows=rows)
        one = "wide" if k == 3 else "s1"
        self.maps = dict(
            h=make(one, 2, self.planes, main=r.hC, edge=r.hE, right=r.hR),
            u=make(one, 2, self.planes, main=r.uC, edge=r.uE, right=r.uR),
            t=make("p" if k == 3 else "s2", 2, self.planes, main=r.tC, edge=r.tE),
        )
        if k <= 1:
            self.maps["c1"] = make("s2", 1, self.planes // 2, main=r.c1C, edge=r.c1E)
        if k == 0:
            self.maps["c2"] = make("s2", 1, 4, main=r.c2C, edge=r.c2E)
            self.maps["c3"] = make("s2", 1, 2, main=r.c3C, edge=r.c3E)
        self.grads = dict(t=r.gt, u=r.gu, c1=r.gc1, c2=r.gc2, c3=r.gc3)

    def lane_block(self, shape, cout):
        lanes = lax.broadcasted_iota(jnp.int32, shape, 1)
        return lanes >> log2(cout)

    def keep(self, value, cout, which):
        count = LANES // cout
        if len(which) == count:
            return value
        block = self.lane_block(value.shape, cout)
        mask = block == which[0]
        for entry in which[1:]:
            mask = mask | (block == entry)
        return jnp.where(mask, value, 0.0)

    def spread(self, value, cout):
        shift = LANES // 2
        while shift >= cout:
            value = value + pltpu.roll(value, shift, 1)
            shift //= 2
        return value

    def local_blocks(self, seg, tile, wanted):
        count = LANES // seg.cout
        return [q for q in range(count) if (tile * count + q) % seg.blocks in wanted]


    def fetch(self, m):
        r = self.refs
        copies = []
        lengths = [0] * (2 * BLOCKS + 3)
        starts = [sum(phase_lengths(C0, BLOCKS)[:p]) // LANES for p in range(len(lengths))]
        for operation in weighted_plan(self.k, C0, BLOCKS):
            lengths[operation.phase] += operation.size // LANES
        for phase, length in enumerate(lengths):
            if length:
                span = pl.ds(starts[phase], -(-length // 16) * 16)
                copies.append(
                    pltpu.make_async_copy(r.w.at[m, span], r.wv.at[span], r.wsem.at[phase])
                )
        return copies

    def expand(self, m):
        for unit in self.units.values():
            for seg in unit.segs:
                self.expand_one(m, unit, seg)

    def expand_one(self, m, unit, seg):
        r = self.refs
        target = getattr(r, "T" + unit.name)
        depth, cin, cout = unit.depth, seg.cin, seg.cout
        taps = seg.taps ** 2
        count = taps * cin * cout // LANES
        first = seg.off // 16 * 16
        skip = seg.off - first
        span = -(-(count + skip) // 16) * 16
        wf, rep = r.work, r.rep
        wf[0:span] = r.wv[first : first + span].astype(jnp.float32)
        if cout < LANES:
            ratio = LANES // cout
            flat = wf[skip : skip + count]
            for part in range(ratio):
                rep[pl.ds(part, count, stride=ratio)] = self.spread(
                    self.keep(flat, cout, [part]), cout
                )

        def tap_rows(tap, tile):
            if cout < LANES:
                return rep[pl.ds(pl.multiple_of(tap * cin, cin), cin)]
            if cout == LANES:
                return wf[pl.ds(pl.multiple_of(skip + tap * cin, 8), cin)]
            return wf[pl.ds(skip + tap * (2 * cin) + tile, cin, stride=2)]

        by_row = {}
        for row, tap, wanted in links(self.k, unit, seg):
            by_row.setdefault(row, []).append((tap, wanted))

        def fill(d):
            width = 3 if taps == 9 else 1
            for tile in range(seg.tiles):
                column = (seg.tile + tile) * LANES
                for row in range(0, unit.rows, cin):
                    total = None
                    for tap, wanted in by_row.get(row, []):
                        if cout <= LANES:
                            local = self.local_blocks(seg, tile, wanted)
                            if not local:
                                continue
                            piece = self.keep(tap_rows(d * width + tap, 0), cout, local)
                        else:
                            piece = tap_rows(d * width + tap, tile)
                        total = piece if total is None else total + piece
                    if total is None:
                        total = jnp.zeros((cin, LANES), jnp.float32)
                    target[m * depth + d, row : row + cin, column : column + LANES] = total.astype(
                        jnp.bfloat16
                    )

        planes_loop(depth, fill)


    def parts(self, unit, source):
        if unit.kind == "p1":
            return [(source.main, range(2), source.at)]
        if source.mode == "wide":
            return [
                (source.edge, range(2), source.at),
                (source.main, range(2), source.at),
                (source.right, range(2), source.at),
            ]
        if unit.kind == "s1":
            return [(source.main, range(2), source.at), (source.edge, range(2), source.at)]
        last = source.tiles - 1
        return [
            (source.main, range(source.tiles), source.at),
            (source.edge, [last], source.edge_at),
        ]

    def rows_of(self, unit, part, m, d, first, count):
        ref, tiles, at = part
        pieces = []
        for tile in tiles:
            if unit.kind == "s2":
                rows = [ref[at(m, tile, 2 * (first + q) + d - 1)] for q in range(count)]
                pieces.append(rows[0] if count == 1 else jnp.concatenate(rows, axis=0))
            else:
                shift = d - 1 if unit.kind == "s1" else 0
                pieces.append(
                    ref[pl.ds(at(m, tile, first + shift), count)].reshape(count * self.rows, LANES)
                )
        return pieces

    def conv(self, m, unit):
        r = self.refs
        source = self.maps[unit.source]
        target = getattr(r, "T" + unit.name)
        z = getattr(r, "z" + unit.name)
        planes, tiles, depth = unit.planes, unit.tiles, unit.depth
        chunk = min(planes, 4 if tiles <= 2 else 2)
        lanes = tiles * LANES

        def body(step, sums):
            first = step * chunk
            pieces = []
            for d in range(depth):
                for part in self.parts(unit, source):
                    pieces += self.rows_of(unit, part, m, d, first, chunk)
            left = jnp.concatenate(pieces, axis=1)
            right = target[pl.ds(m * depth, depth), 0 : unit.rows, 0:lanes]
            right = right.reshape(depth * unit.rows, lanes)
            result = lax.dot_general(left, right, DOWN, preferred_element_type=jnp.float32)
            for tile in range(tiles):
                block = result[:, tile * LANES : (tile + 1) * LANES]
                z[pl.ds(m * tiles * planes + tile * planes + first, chunk)] = block.reshape(
                    chunk, self.rows, LANES
                )
            return (sums[0] + partial_sum(result), sums[1] + partial_sum(result * result))

        zero = jnp.zeros((8, lanes), jnp.float32)
        sums = planes_sum(planes // chunk, body, (zero, zero))
        for seg in unit.segs:
            scale = self.per_cell(unit, seg)
            totals = self.fold(seg, sums)
            self.norm_rows(m, unit, seg, totals, scale)

    def per_cell(self, unit, seg):
        blocks = seg.tiles * LANES // seg.cout
        small, large = self.cells
        count = unit.planes * blocks
        return jnp.where(self.core == 0, 1.0 / (large * count), 1.0 / (small * count)).astype(
            jnp.float32
        )

    def fold(self, seg, sums):
        first = seg.tile
        found = []
        for value in sums:
            tiles = [
                value[:, (first + t) * LANES : (first + t + 1) * LANES] for t in range(seg.tiles)
            ]
            if seg.cout <= LANES:
                total = tiles[0]
                for tile in tiles[1:]:
                    total = total + tile
                total = jnp.sum(self.spread(total, seg.cout), axis=0, keepdims=True)
                found.append([total] * seg.tiles)
            else:
                found.append([jnp.sum(tile, axis=0, keepdims=True) for tile in tiles])
        return found

    def table_row(self, ref, m, seg, tile):
        slot = seg.slot
        if seg.cout > LANES:
            return ref[m, slot : slot + 1, tile * LANES : (tile + 1) * LANES]
        row = jnp.broadcast_to(ref[m, slot : slot + 1, 0:LANES], (8, LANES))
        if seg.cout < LANES:
            row = self.spread(self.keep(row, seg.cout, [0]), seg.cout)
        return row[0:1]

    def norm_rows(self, m, unit, seg, totals, scale):
        st = self.refs.st
        for tile in range(seg.tiles):
            average = totals[0][tile] * scale
            variance = totals[1][tile] * scale - average * average
            inverse = lax.rsqrt(variance + EPS)
            gain = self.table_row(self.refs.gains, m, seg, tile)
            shift = self.table_row(self.refs.shifts, m, seg, tile)
            where = m * STATS + unit.stat + seg.tile + tile
            factor = gain * inverse
            st[where, 0:1] = average
            st[where, 1:2] = inverse
            st[where, 2:3] = factor
            st[where, 3:4] = shift - average * factor

    def normed(self, m, unit, tile, plane):
        st = self.refs.st
        z = getattr(self.refs, "z" + unit.name)
        where = m * STATS + unit.stat + tile
        value = z[m * unit.tiles * unit.planes + tile * unit.planes + plane]
        return value * st[where, 2:3] + st[where, 3:4]

    def apply_a(self, m):
        unit, u = self.units["a"], self.maps["u"]

        def body(plane):
            for tile in range(2):
                value = silu_of(self.normed(m, unit, tile, plane)) * self.masks[0]
                u.store(m, tile, plane, value)

        planes_loop(self.planes, body)
        u.close(m)

    def apply_b(self, m):
        unit, top = self.units["b"], self.maps["t"]
        hf, s = self.refs.hf, self.refs.s

        def body(plane):
            for tile in range(2):
                where = m * 2 * self.planes + tile * self.planes + plane
                value = silu_of(self.normed(m, unit, tile, plane) + hf[where]) * self.masks[0]
                s[where] = value
                top.store(m, tile, plane, value)

        planes_loop(self.planes, body)
        top.close(m)

    def apply_rest(self, m, unit):
        sb = self.refs.sb
        for seg in unit.segs:
            chain = self.maps[seg.chain] if seg.chain else None

            def body(plane):
                for tile in range(seg.tiles):
                    value = self.normed(m, unit, seg.tile + tile, plane)
                    if chain is not None:
                        chain.store(m, tile, plane, silu_of(value) * self.masks[0])
                    else:
                        at = message_slot(self.k, seg.dest) + tile * unit.planes + plane
                        sb[at] = value.astype(jnp.bfloat16)

            planes_loop(unit.planes, body)
            if chain is not None:
                chain.close(m)
            else:
                self.message(m, seg.dest).start()

    def message(self, e, other):
        count = 2 * (8 >> max(self.k, other))
        r = self.refs
        return pltpu.make_async_remote_copy(
            src_ref=r.sb.at[pl.ds(message_slot(self.k, other), count)],
            dst_ref=r.rb.at[pl.ds(e * 16 + message_slot(other, self.k), count)],
            send_sem=r.ssem.at[e * 4 + other],
            recv_sem=r.rsem.at[e * 4 + self.k],
            device_id=dict(branch=other),
            device_id_type=pl.DeviceIdType.MESH,
        )

    def arrived(self, e, other):
        count = 2 * (8 >> max(self.k, other))
        r = self.refs
        at = message_slot(self.k, other)
        return pltpu.make_async_remote_copy(
            src_ref=r.sb.at[pl.ds(at, count)],
            dst_ref=r.rb.at[pl.ds(e * 16 + at, count)],
            send_sem=r.ssem.at[e * 4 + other],
            recv_sem=r.rsem.at[e * 4 + other],
            device_id=dict(branch=other),
            device_id_type=pl.DeviceIdType.MESH,
        )

    def others(self):
        return [other for other in range(4) if other != self.k]

    def settle(self, e):
        for other in self.others():
            self.message(e, other).wait_send()
        for other in self.others():
            self.arrived(e, other).wait_recv()

    def receive(self, m):
        r = self.refs
        s, rb, hf, out = r.s, r.rb, r.hf, r.outs
        h = self.maps["h"]

        def body(plane):
            for tile in range(2):
                where = m * 2 * self.planes + tile * self.planes + plane
                total = s[where]
                for other in self.others():
                    count = 8 >> max(self.k, other)
                    at = plane >> max(0, other - self.k)
                    slot = m * 16 + message_slot(self.k, other) + tile * count + at
                    total = total + rb[slot].astype(jnp.float32)
                s[where] = total
                value = silu_of(total) * self.masks[0]
                out[tile * self.planes + plane] = value.astype(jnp.bfloat16)

                @pl.when(m + 1 < MODULES)
                def _():
                    hf[2 * self.planes + tile * self.planes + plane] = value
                    h.store(1, tile, plane, value)

        planes_loop(self.planes, body)

        @pl.when(m + 1 < MODULES)
        def _():
            h.close(1)

    def take_feature(self, tile, plane, value):
        self.refs.hf[tile * self.planes + plane] = value
        self.maps["h"].store(0, tile, plane, value)

    def take_cotangent(self, tile, plane, value):
        self.refs.gin[tile * self.planes + plane] = value

    def member(self, kind, order):
        kinds = self.refs.kinds
        found, before = jnp.int32(0), jnp.int32(0)
        for at in range(self.count):
            same = kinds[at] == kind
            found = jnp.where(same & (before == order), at, found)
            before = before + same.astype(jnp.int32)
        return found

    def order(self, device):
        kinds = self.refs.kinds
        kind = kinds[device]
        before = jnp.int32(0)
        for at in range(self.count):
            before = before + ((kinds[at] == kind) & (at < device)).astype(jnp.int32)
        return before

    def unpack(self, t, consume):
        r = self.refs
        work, rows, planes = r.work, self.rows, self.planes
        full = SH * SW * C0 // LANES
        gath = r.gathc if t else r.gathx

        @pl.when(self.core == 0)
        def _():
            for at in range(self.large):
                block = gath[self.member(1, at)]
                work[at * ROWS : (at + 1) * ROWS] = block.astype(jnp.float32)

        @pl.when(self.core == 1)
        def _():
            for at in range(self.small):
                block = gath[self.member(0, at), 0:full]
                work[at * full : (at + 1) * full] = block.astype(jnp.float32)
            work[self.small * full : self.large * ROWS] = jnp.zeros(
                (self.large * ROWS - self.small * full, LANES), jnp.float32
            )

        deep = self.large * ROWS // 2
        right = jnp.concatenate([work[pl.ds(j, deep, stride=2)] for j in range(2)], axis=1)
        right = right.astype(jnp.bfloat16)
        cells = Cells(self.core, (rows, LANES), self.small, self.large)
        base = cells.crop * cells.pick(ROWS // 2, full // 2)
        base = base + cells.along * (planes * cells.wide) + cells.across
        base = jnp.where(cells.valid, base, -(1 << 20))
        lane = lax.broadcasted_iota(jnp.int32, (rows, LANES), 1)
        chunk = min(planes, 4)

        def body(step):
            pieces = []
            for q in range(chunk):
                goal = base + (step * chunk + q) * cells.wide
                pieces.append(one_hot(goal, lane, deep))
            left = pieces[0] if chunk == 1 else jnp.concatenate(pieces, axis=0)
            result = lax.dot_general(left, right, DOWN, preferred_element_type=jnp.float32)
            for q in range(chunk):
                for tile in range(2):
                    value = result[q * rows : (q + 1) * rows, tile * LANES : (tile + 1) * LANES]
                    consume(tile, step * chunk + q, value)

        planes_loop(planes // chunk, body)

    def pack_size(self):
        return 48 * self.planes, -(-self.planes * self.rows // LANES) * LANES

    def plan_pack(self):
        r = self.refs
        high, deep = self.pack_size()
        planes = self.planes
        q = lax.broadcasted_iota(jnp.int32, (high, LANES), 0)
        lane = lax.broadcasted_iota(jnp.int32, (high, LANES), 1)
        wide, tall = jnp.where(self.core == 0, 6, 3), jnp.where(self.core == 0, 8, 4)
        cell = jnp.where(self.core == 0, (q * 43691) >> 18, (q * 43691) >> 17)
        across = q - cell * wide
        plane = cell & (planes - 1)
        along = cell >> log2(planes)
        base = plane * self.rows + along * wide + across
        base = jnp.where(along < tall, base, -(1 << 20))
        shard = lax.axis_index("crops")
        for at, device in enumerate((shard, shard + 1 - 2 * self.core)):
            goal = base + self.order(device) * (wide * tall)
            r.hot[at, 0:high, 0:deep] = one_hot(goal, lane, deep)

    def pack(self, units, put):
        high, deep = self.pack_size()
        right = jnp.concatenate([units(tile) for tile in range(2)], axis=1)
        short = deep - right.shape[0]
        parts = [right.astype(jnp.bfloat16)]
        if right.dtype == jnp.float32:
            parts.append((right - parts[0].astype(jnp.float32)).astype(jnp.bfloat16))
        if short:
            empty = jnp.zeros((short, 2 * LANES), jnp.bfloat16)
            parts = [jnp.concatenate([part, empty], axis=0) for part in parts]
        for at in range(2):
            total = None
            for part in parts:
                piece = lax.dot_general(
                    self.refs.hot[at, 0:high, 0:deep],
                    part,
                    DOWN,
                    preferred_element_type=jnp.float32,
                )
                total = piece if total is None else total + piece
            for tile in range(2):
                put(at, pl.ds(tile, high, stride=2), total[:, tile * LANES : (tile + 1) * LANES])

    def pack_outputs(self):
        r = self.refs
        high = 2 * self.pack_size()[0]

        def put(at, where, value):
            r.work[pl.ds(at * ROWS + where.start, where.size, stride=2)] = value

        def units(tile):
            block = r.outs[tile * self.planes : (tile + 1) * self.planes]
            return block.reshape(self.planes * self.rows, LANES)

        self.pack(units, put)
        for at in range(2):
            r.blocks[at, 0:high] = r.work[at * ROWS : at * ROWS + high].astype(jnp.bfloat16)
            if high < ROWS:
                r.blocks[at, high:ROWS] = jnp.zeros((ROWS - high, LANES), jnp.bfloat16)

    def pack_gradient(self):
        r = self.refs
        high = 2 * self.pack_size()[0]

        def put(at, where, value):
            r.slopes[at, where] = value

        def units(tile):
            block = r.gin[tile * self.planes : (tile + 1) * self.planes]
            return block.reshape(self.planes * self.rows, LANES)

        self.pack(units, put)
        if high < ROWS:
            for at in range(2):
                r.slopes[at, high:ROWS] = jnp.zeros((ROWS - high, LANES), jnp.float32)

    def forward(self, m, gather):
        steps = iter(range(1, 4))

        def also():
            step = next(steps, None)
            if step is not None:

                @pl.when(m == 0)
                def _():
                    gather.step(1, step)

        self.conv(m, self.units["a"])
        self.apply_a(m)
        also()
        self.conv(m, self.units["b"])
        self.apply_b(m)
        also()
        for name in ("d", "u", "e", "f", "g"):
            if name in self.units:
                self.conv(m, self.units[name])
                self.apply_rest(m, self.units[name])
                also()
        for _ in range(3):
            also()

        @pl.when(m == MODULES - 1)
        def _():
            gather.collect(1)
            self.unpack(1, self.take_cotangent)
            self.plan_pack()

        self.settle(m)
        self.receive(m)


    def send_back(self, m):
        r = self.refs
        s, gin, gt, sb = r.s, r.gin, r.gt, r.sb
        e = MODULES + m

        def body(plane):
            for tile in range(2):
                at = tile * self.planes + plane
                value = gin[at] * slope_of(s[m * 2 * self.planes + at])
                gt[at] = value
                for other in range(self.k):
                    sb[message_slot(self.k, other) + at] = value.astype(jnp.bfloat16)

        planes_loop(self.planes, body)
        for other in reversed(self.others()):
            if other > self.k:
                count = 8 >> other
                wide = 1 << (other - self.k)

                def pool(plane):
                    for tile in range(2):
                        total = gt[tile * self.planes + plane * wide]
                        for step in range(1, wide):
                            total = total + gt[tile * self.planes + plane * wide + step]
                        slot = message_slot(self.k, other) + tile * count + plane
                        sb[slot] = total.astype(jnp.bfloat16)

                planes_loop(count, pool)
            self.message(e, other).start()

    def back_unit(self, m, unit):
        r = self.refs
        st, dyb, z = r.st, r.dyb, getattr(r, "z" + unit.name)
        name, planes, tiles = unit.name, unit.planes, unit.tiles
        e = MODULES + m
        sums = {}

        def upstream(seg, tile, plane, normed):
            at = tile * planes + plane
            if name == "b":
                hf = r.hf[m * 2 * planes + at]
                value = r.gt[at] * slope_of(normed + hf)
                r.gin[at] = value
                return value
            if name == "a":
                return r.gu[at] * slope_of(normed)
            if seg.chain:
                return self.grads[seg.chain][at] * slope_of(normed)
            return r.rb[e * 16 + message_slot(self.k, seg.dest) + at].astype(jnp.float32)

        for seg in unit.segs:

            def body(plane, carry):
                result = []
                for tile in range(seg.tiles):
                    at = (seg.tile + tile) * planes + plane
                    where = m * STATS + unit.stat + seg.tile + tile
                    value = z[m * tiles * planes + at]
                    normed = value * st[where, 2:3] + st[where, 3:4]
                    dy = upstream(seg, tile, plane, normed)
                    dyb[at] = dy
                    zhat = (value - st[where, 0:1]) * st[where, 1:2]
                    result.append(carry[2 * tile] + partial_sum(dy))
                    result.append(carry[2 * tile + 1] + partial_sum(dy * zhat))
                return tuple(result)

            zero = jnp.zeros((8, LANES), jnp.float32)
            found = planes_sum(planes, body, (zero,) * (2 * seg.tiles))
            pair = [
                jnp.concatenate([found[2 * tile + which] for tile in range(seg.tiles)], axis=1)
                for which in range(2)
            ]
            plain = SimpleNamespace(**vars(seg))
            plain.tile = 0
            totals = self.fold(plain, pair)
            self.table_grads(m, seg, totals)
            sums[seg.slot] = totals
        dz = self.dz_planes(unit)
        for seg in unit.segs:
            scale = self.per_cell(unit, seg)
            totals = sums[seg.slot]

            def apply(plane):
                for tile in range(seg.tiles):
                    at = (seg.tile + tile) * planes + plane
                    where = m * STATS + unit.stat + seg.tile + tile
                    zhat = (z[m * tiles * planes + at] - st[where, 0:1]) * st[where, 1:2]
                    inner = dyb[at] - totals[0][tile] * scale - zhat * (totals[1][tile] * scale)
                    dz.store(0, seg.tile + tile, plane, inner * st[where, 2:3] * self.masks[0])

            planes_loop(planes, apply)
        dz.close(0)
        self.back_data(m, unit, dz)
        first = min(seg.off for seg in unit.segs)
        last = max(seg.off + seg.taps**2 * seg.cin * seg.cout // LANES for seg in unit.segs)
        wanted = (self.quarter * self.share < last) & ((self.quarter + 1) * self.share > first)

        @pl.when(wanted)
        def _():
            self.back_kernel(m, unit, dz)

    def dz_planes(self, unit):
        r = self.refs
        mode = {"p1": "p", "s2": "dz2", "s1": "wide" if self.k == 3 else "s1"}[unit.kind]
        return Planes(
            mode,
            unit.tiles,
            unit.planes,
            self.masks,
            self.rows,
            r.dC,
            r.dE,
            r.dR,
        )

    def table_grads(self, m, seg, totals):
        gg = self.refs.gg
        slot = seg.slot
        for which, found in ((0, totals[1]), (1, totals[0])):
            if seg.cout > LANES:
                for tile in range(2):
                    gg[m, which, slot : slot + 1, tile * LANES : (tile + 1) * LANES] = found[tile]
            else:
                row = jnp.broadcast_to(found[0], (8, LANES))
                if seg.cout < LANES:
                    row = self.keep(row, seg.cout, [0])
                gg[m, which, slot : slot + 1, 0:LANES] = row[0:1]

    def wide_rows(self, ref, at, tiles, plane, count):
        pieces = [
            ref[pl.ds(at(0, tile, plane), count)].reshape(count * self.rows, LANES)
            for tile in range(tiles)
        ]
        return pieces[0] if tiles == 1 else jnp.concatenate(pieces, axis=1)

    def back_data(self, m, unit, dz):
        r = self.refs
        kind, tiles = unit.kind, unit.tiles
        target = getattr(r, "T" + unit.name)
        lanes = tiles * LANES
        rows = self.rows

        def kernel_rows(d, first, count):
            return target[m * unit.depth + d, first : first + count, 0:lanes]

        def product(left, right):
            return lax.dot_general(left, right, ACROSS, preferred_element_type=jnp.float32)

        def put(ref, tile, planes, first, count, value, step=1, add=False):
            block = value.reshape(count, rows, LANES)
            for q in range(count):
                at = tile * planes + first + q * step
                ref[at] = ref[at] + block[q] if add else block[q]

        planes = unit.planes
        if kind == "s1":
            goal = r.gu if unit.name == "b" else r.gin
            add = unit.name == "a"
            if self.k == 3:
                pairs = [(dz.right, 0), (dz.main, 256), (dz.edge, 512)]
            else:
                pairs = [(dz.main, 0), (dz.edge, 256)]
            chunk = min(planes, 4)

            def body(step):
                first = step * chunk
                total = None
                for d in range(3):
                    for ref, at in pairs:
                        left = self.wide_rows(ref, dz.at, 2, first + 1 - d, chunk)
                        piece = product(left, kernel_rows(d, at, 256))
                        total = piece if total is None else total + piece
                for tile in range(2):
                    put(
                        goal,
                        tile,
                        planes,
                        first,
                        chunk,
                        total[:, tile * LANES : (tile + 1) * LANES],
                        add=add,
                    )

            planes_loop(planes // chunk, body)
            return
        if kind == "p1":
            left = self.wide_rows(dz.main, dz.at, tiles, 0, planes)
            total = product(left, kernel_rows(0, 0, 256))
            for tile in range(2):
                put(
                    r.gt,
                    tile,
                    planes,
                    0,
                    planes,
                    total[:, tile * LANES : (tile + 1) * LANES],
                    add=True,
                )
            return
        goal = self.grads[unit.source]
        add = unit.source == "t"
        lanes_in = unit.lanes_in
        count_in = unit.planes_in
        for parity, terms in ((0, [(1, 0)]), (1, [(2, 0), (0, 1)])):
            total, side = None, None
            for d, offset in terms:
                left = self.wide_rows(dz.main, dz.at, tiles, offset, planes)
                piece = product(left, kernel_rows(d, 0, lanes_in))
                total = piece if total is None else total + piece
                left = self.wide_rows(dz.edge, dz.at, tiles, offset, planes)
                piece = product(left, kernel_rows(d, lanes_in, LANES))
                side = piece if side is None else side + piece
            for tile in range(lanes_in // LANES):
                value = total[:, tile * LANES : (tile + 1) * LANES]
                if tile == lanes_in // LANES - 1:
                    value = value + side
                put(goal, tile, count_in, parity, planes, value, step=2, add=add)

    def back_kernel(self, m, unit, dz):
        r = self.refs
        G, rep, wgv = r.work, r.rep, r.wgv
        tiles, planes = unit.tiles, unit.planes
        source = self.maps[unit.source]
        right = self.wide_rows(dz.main, dz.at, tiles, 0, planes)

        def gather(d):
            at = 0
            for part in self.parts(unit, source):
                pieces = self.rows_of(unit, part, m, d, 0, planes)
                left = pieces[0] if len(pieces) == 1 else jnp.concatenate(pieces, axis=1)
                count = left.shape[1]
                result = lax.dot_general(left, right, ALONG, preferred_element_type=jnp.float32)
                for tile in range(tiles):
                    row = pl.multiple_of((d * tiles + tile) * unit.rows + at, 8)
                    G[pl.ds(row, count)] = result[:, tile * LANES : (tile + 1) * LANES]
                at += count

        planes_loop(unit.depth, gather)
        for seg in unit.segs:
            self.fold_kernel(m, unit, seg)

    def fold_kernel(self, m, unit, seg):
        r = self.refs
        G, rep, wgv = r.work, r.rep, r.wgv
        cin, cout, tiles = seg.cin, seg.cout, unit.tiles
        width = 3 if seg.taps == 3 else 1
        found = links(self.k, unit, seg)
        off = seg.off

        def fold(d):
            for column in range(width):
                tap = d * width + column
                totals = []
                for tile in range(seg.tiles):
                    total = None
                    for row, which, wanted in found:
                        if which != column:
                            continue
                        at = pl.multiple_of((d * tiles + seg.tile + tile) * unit.rows + row, 8)
                        piece = G[pl.ds(at, cin)]
                        if cout <= LANES:
                            local = self.local_blocks(seg, tile, wanted)
                            if not local:
                                continue
                            piece = self.keep(piece, cout, local)
                        total = piece if total is None else total + piece
                    totals.append(total)
                if cout > LANES:
                    for tile in range(2):
                        wgv[pl.ds(off + tap * (2 * cin) + tile, cin, stride=2)] = totals[tile]
                    continue
                total = None
                for piece in totals:
                    if piece is not None:
                        total = piece if total is None else total + piece
                if cout == LANES:
                    wgv[pl.ds(pl.multiple_of(off + tap * cin, 8), cin)] = total
                else:
                    rep[pl.ds(pl.multiple_of(tap * cin, cin), cin)] = self.spread(total, cout)

        planes_loop(unit.depth, fold)
        if cout < LANES:
            ratio = LANES // cout
            count = width * width * cin // ratio
            total = None
            for part in range(ratio):
                piece = self.keep(rep[pl.ds(part, count, stride=ratio)], cout, [part])
                total = piece if total is None else total + piece
            wgv[off : off + count] = total

    def backward(self, m):
        e = MODULES + m
        self.send_back(m)
        for name in ("g", "f", "e", "d", "u"):
            if name in self.units:
                for seg in self.units[name].segs:
                    if seg.dest >= 0:
                        self.arrived(e, seg.dest).wait_recv()
                self.back_unit(m, self.units[name])
        for other in self.others():
            self.message(e, other).wait_send()
        self.back_unit(m, self.units["b"])
        self.back_unit(m, self.units["a"])


STATS = 20
NAMES = list(
    dict(x=0, cot=0, w=0, gains=0, shifts=0, kinds=0, out=0, grad=0, wg=0, gain=0, shift=0)
)


def one_hot(goal, lane, deep):
    pieces = [
        jnp.where(goal == lane + first, 1.0, 0.0).astype(jnp.bfloat16)
        for first in range(0, deep, LANES)
    ]
    return jnp.concatenate(pieces, axis=1)


class Cells:
    def __init__(self, core, shape, small, large):
        self.core = core
        row = lax.broadcasted_iota(jnp.int32, shape, 0)
        self.wide = self.pick(LW // 8, SW // 8)
        tall = self.pick(LH // 8, SH // 8)
        self.crop = self.pick((row * 43691) >> 21, (row * 43691) >> 19)
        inner = row - self.crop * (self.wide * tall)
        self.along = self.pick((inner * 43691) >> 18, (inner * 43691) >> 17)
        self.across = inner - self.along * self.wide
        self.valid = self.crop < self.pick(large, small)
        self.last = tall - 1

    def pick(self, large, small):
        return jnp.where(self.core == 0, large, small)


def fill_masks(refs, rows, core, small, large):
    cells = Cells(core, (rows, LANES), small, large)
    valid = cells.valid
    six = cells.wide == 6
    up, down = valid & (cells.along > 0), valid & (cells.along < cells.last)
    tables = (
        valid,
        valid & (cells.across > 0),
        valid & (cells.across < cells.wide - 1),
        up & six,
        up & jnp.logical_not(six),
        down & six,
        down & jnp.logical_not(six),
    )
    for at, table in enumerate(tables):
        refs.masks[at] = jnp.where(table, 1.0, 0.0)


class Gather:
    def __init__(self, refs, core, count):
        self.refs, self.core, self.count = refs, core, count
        self.z = lax.axis_index("crops") // 2
        self.last = count // 2 - 1

    def hop(self, t, source, right):
        r = self.refs
        at = source * 2 + self.core
        gath = r.gathc if t else r.gathx
        to = self.z + 1 if right else self.z - 1
        return pltpu.make_async_remote_copy(
            src_ref=gath.at[at],
            dst_ref=gath.at[at],
            send_sem=r.hsem.at[(t * (self.last + 1) + source) * 3 + (0 if right else 1)],
            recv_sem=r.gsem.at[t * self.count + at],
            device_id=dict(crops=to * 2 + self.core),
            device_id_type=pl.DeviceIdType.MESH,
        )

    def across(self, t, source, core, rows):
        r = self.refs
        at = source * 2 + core
        gath = r.gathc if t else r.gathx
        return pltpu.make_async_remote_copy(
            src_ref=gath.at[at, pl.ds(0, rows)],
            dst_ref=gath.at[at, pl.ds(0, rows)],
            send_sem=r.hsem.at[(t * (self.last + 1) + source) * 3 + 2],
            recv_sem=r.gsem.at[t * self.count + at],
            device_id=dict(crops=self.z * 2 + 1 - self.core),
            device_id_type=pl.DeviceIdType.MESH,
        )

    def each_core(self, action):
        for core, rows in ((0, SH * SW * C0 // LANES), (1, ROWS)):

            @pl.when(self.core == core)
            def _():
                action(core, rows)

    def send(self, t, source, rightward, leftward):
        if rightward:

            @pl.when(self.z < self.last)
            def _():
                self.hop(t, source, True).start()

        if leftward:

            @pl.when(self.z > 0)
            def _():
                self.hop(t, source, False).start()

        self.each_core(lambda core, rows: self.across(t, source, core, rows).start())

    def step(self, t, s):
        r = self.refs
        if s == 0:
            at = self.z * 2 + self.core
            if t:
                r.gathc[at] = r.cot[...]
            else:
                r.gathx[at] = r.x[...]
            self.send(t, self.z, True, True)
            return

        @pl.when(self.z >= s)
        def _():
            self.hop(t, self.z - s, True).wait_recv()
            self.send(t, self.z - s, True, False)

        @pl.when(self.z + s <= self.last)
        def _():
            self.hop(t, self.z + s, True).wait_recv()
            self.send(t, self.z + s, False, True)

    def collect(self, t):
        for source in range(self.last + 1):
            for core, rows in ((0, ROWS), (1, SH * SW * C0 // LANES)):

                @pl.when(self.core == core)
                def _():
                    self.across(t, source, 1 - core, rows).wait_recv()

    def finish(self, t):
        def sent(source, rightward, leftward):
            if rightward:

                @pl.when(self.z < self.last)
                def _():
                    self.hop(t, source, True).wait_send()

            if leftward:

                @pl.when(self.z > 0)
                def _():
                    self.hop(t, source, False).wait_send()

            self.each_core(lambda core, rows: self.across(t, source, core, rows).wait_send())

        sent(self.z, True, True)
        for s in range(1, self.last + 1):

            @pl.when(self.z >= s)
            def _():
                sent(self.z - s, True, False)

            @pl.when(self.z + s <= self.last)
            def _():
                sent(self.z + s, False, True)


def scratch_table(rows, weight_rows, count):
    def half(many):
        return pltpu.VMEM((many, rows, LANES), jnp.bfloat16)

    def full(many):
        return pltpu.VMEM((many, rows, LANES), jnp.float32)

    def expanded(depth, deep, wide):
        return pltpu.VMEM((MODULES * depth, deep, wide), jnp.bfloat16)

    _, span, _ = pair_rows(weight_rows, count)
    return dict(
        masks=full(MASKS),
        hC=half(2 * 20),
        hE=half(2 * 20),
        hR=half(2 * 6),
        uC=half(2 * 20),
        uE=half(2 * 20),
        uR=half(2 * 6),
        tC=half(2 * 18),
        tE=half(2 * 9),
        c1C=half(2 * 5),
        c1E=half(2 * 5),
        c2C=half(2 * 5),
        c2E=half(2 * 5),
        c3C=half(2 * 3),
        c3E=half(2 * 3),
        dC=half(20),
        dE=half(20),
        dR=half(6),
        outs=half(16),
        hf=full(2 * 16),
        s=full(2 * 16),
        za=full(2 * 16),
        zb=full(2 * 16),
        zd=full(2 * 16),
        zu=full(2 * 8),
        ze=full(2 * 4),
        zf=full(2 * 2),
        zg=full(2 * 2),
        gt=full(16),
        gu=full(16),
        gin=full(16),
        gc1=full(4),
        gc2=full(4),
        gc3=full(2),
        dyb=full(16),
        sb=half(16),
        rb=half(4 * 16),
        st=pltpu.VMEM((MODULES * STATS, 8, LANES), jnp.float32),
        Ta=expanded(3, 768, 256),
        Tb=expanded(3, 768, 256),
        Td=expanded(3, 384, 512),
        Tu=expanded(1, 256, 768),
        Te=expanded(3, 256, 256),
        Tf=expanded(3, 256, 128),
        Tg=expanded(3, 256, 256),
        wv=pltpu.VMEM((weight_rows, LANES), jnp.bfloat16),
        work=pltpu.VMEM((4608, LANES), jnp.float32),
        rep=pltpu.VMEM((640, LANES), jnp.float32),
        wgv=pltpu.VMEM((weight_rows, LANES), jnp.float32),
        wq=pltpu.VMEM((MODULES, 2 * weight_rows // count, LANES), jnp.float32),
        wr=pltpu.VMEM((MODULES, span, LANES), jnp.float32),
        gathx=pltpu.VMEM((count, ROWS, LANES), jnp.bfloat16),
        gathc=pltpu.VMEM((count, ROWS, LANES), jnp.bfloat16),
        hot=pltpu.VMEM((2, 384, 768), jnp.bfloat16),
        blocks=pltpu.VMEM((2, ROWS, LANES), jnp.bfloat16),
        slopes=pltpu.VMEM((2, ROWS, LANES), jnp.float32),
        blockr=pltpu.VMEM((ROWS, LANES), jnp.bfloat16),
        sloper=pltpu.VMEM((ROWS, LANES), jnp.float32),
        gg=pltpu.VMEM((MODULES, 2, SLOTS, 256), jnp.float32),
        ggr=pltpu.VMEM((MODULES, 2, SLOTS, 256), jnp.float32),
        wsem=pltpu.SemaphoreType.DMA((5,)),
        ssem=pltpu.SemaphoreType.DMA((16,)),
        rsem=pltpu.SemaphoreType.DMA((16,)),
        hsem=pltpu.SemaphoreType.DMA((3 * count,)),
        gsem=pltpu.SemaphoreType.DMA((2 * count,)),
        psem=pltpu.SemaphoreType.DMA((5,)),
        qsem=pltpu.SemaphoreType.DMA((5,)),
        osem=pltpu.SemaphoreType.DMA((1,)),
    )


def pair_rows(weight_rows, count):
    share = weight_rows // count
    low = share // 8 * 8
    return share, 2 * share - low, low


def greet(core, count):
    barrier = pltpu.get_barrier_semaphore()
    me, shard = lax.axis_index("branch"), lax.axis_index("crops")
    z = shard // 2

    def signal(**where):
        pl.semaphore_signal(barrier, inc=1, device_id=where, device_id_type=pl.DeviceIdType.MESH)

    for step in range(1, 4):
        signal(branch=lax.rem(me + step, 4))
    signal(crops=shard + 1 - 2 * core)

    @pl.when(z > 0)
    def _():
        signal(crops=shard - 2)

    @pl.when(z < count // 2 - 1)
    def _():
        signal(crops=shard + 2)

    ends = (z == 0).astype(jnp.int32) + (z == count // 2 - 1).astype(jnp.int32)
    pl.semaphore_wait(barrier, 6 - ends)


def whole_kernel(names, rows, large, small, *args):
    refs = SimpleNamespace(**dict(zip(names, args)))
    count = large + small
    me, shard = lax.axis_index("branch"), lax.axis_index("crops")
    core = shard % 2
    weight_rows = refs.wgv.shape[0]
    share, span, low = pair_rows(weight_rows, count)
    quarter = pl.multiple_of(shard // 2 * (2 * share), 8)

    class Lazy:
        def __getitem__(self, index):
            return refs.masks[index]

    def across(source, goal, index):
        return pltpu.make_async_remote_copy(
            src_ref=source,
            dst_ref=goal,
            send_sem=refs.psem.at[index],
            recv_sem=refs.qsem.at[index],
            device_id=dict(crops=shard + 1 - 2 * core),
            device_id_type=pl.DeviceIdType.MESH,
        )

    def kernel_pair(m):
        at = pl.multiple_of(low * (1 - core), 8)
        return across(refs.wq.at[m, pl.ds(at, span)], refs.wr.at[m], m)

    outputs_pair = across(refs.blocks.at[1], refs.blockr, 2)
    gradient_pair = across(refs.slopes.at[1], refs.sloper, 3)
    table_pair = across(refs.gg, refs.ggr, 4)
    gather = Gather(refs, core, count)

    def every(action):
        for k in range(4):

            @pl.when(me == k)
            def _():
                action(Branch(k, rows, large, small, 2 * share, refs, Lazy(), core))

    def begin(branch):
        for copy in branch.fetch(0):
            copy.start()

    def prepare(m):
        def run(branch):
            for copy in branch.fetch(m):
                copy.wait()
            branch.expand(m)
            if m + 1 < MODULES:
                for copy in branch.fetch(m + 1):
                    copy.start()

        return run

    def main(branch):
        branch.unpack(0, branch.take_feature)
        branch.maps["h"].close(0)
        gather.step(1, 0)

        def ahead(m, carry):
            branch.forward(m, gather)
            return carry

        def back(step, carry):
            m = MODULES - 1 - step
            branch.backward(m)
            refs.wq[m] = refs.wgv[pl.ds(quarter, 2 * share)]
            kernel_pair(m).start()
            return carry

        lax.fori_loop(0, MODULES, ahead, 0)
        branch.pack_outputs()
        outputs_pair.start()
        lax.fori_loop(0, MODULES, back, 0)
        branch.pack_gradient()
        gradient_pair.start()
        table_pair.start()

    every(begin)
    greet(core, count)
    gather.step(0, 0)
    every(prepare(0))
    gather.step(0, 1)
    fill_masks(refs, rows, core, small, large)
    refs.wgv[pl.ds(quarter, 2 * share)] = jnp.zeros((2 * share, LANES), jnp.float32)
    refs.gg[...] = jnp.zeros(refs.gg.shape, jnp.float32)
    every(prepare(1))
    gather.step(0, 2)
    gather.step(0, 3)
    gather.collect(0)
    every(main)

    for step in range(MODULES):
        m = MODULES - 1 - step
        kernel_pair(m).wait()
        mine = refs.wq[m, pl.ds(pl.multiple_of(low * core, 8), span)]
        refs.work[pl.ds(m, span, stride=MODULES)] = mine + refs.wr[m]
    skip = pl.multiple_of(core * (MODULES * (share - low)), 8)
    leave = pltpu.make_async_copy(
        refs.work.at[pl.ds(skip, MODULES * share)], refs.wg, refs.osem.at[0]
    )
    leave.start()
    outputs_pair.wait()
    gradient_pair.wait()
    table_pair.wait()
    own = refs.kinds[shard] != core
    refs.out[...] = jnp.where(own, refs.blocks[0].astype(jnp.float32), refs.blockr[...].astype(jnp.float32)).astype(jnp.bfloat16)
    refs.grad[...] = jnp.where(own, refs.slopes[0], refs.sloper[...])
    width = 256 // count
    for which, goal in ((0, refs.gain), (1, refs.shift)):
        for m in range(MODULES):
            total = refs.gg[m, which] + refs.ggr[m, which]
            found = None
            for at in range(count):
                piece = jnp.where(shard == at, total[:, at * width : (at + 1) * width], 0.0)
                found = piece if found is None else found + piece
            goal[m] = found
    gather.finish(0)
    gather.finish(1)
    leave.wait()


def whole_call(rows, large, small, x, cot, w, gains, shifts, kinds):
    count = large + small
    weight_rows = w.shape[1]
    table = scratch_table(rows, weight_rows, count)
    vmem = pl.BlockSpec(memory_space=pltpu.VMEM)
    hbm = pl.BlockSpec(memory_space=pl.ANY)
    smem = pl.BlockSpec(memory_space=pltpu.SMEM)
    tables = jax.ShapeDtypeStruct((MODULES, SLOTS, 256 // count), jnp.float32)
    return pl.pallas_call(
        partial(whole_kernel, NAMES + list(table), rows, large, small),
        out_shape=(
            jax.ShapeDtypeStruct((ROWS, LANES), jnp.bfloat16),
            jax.ShapeDtypeStruct((ROWS, LANES), jnp.float32),
            jax.ShapeDtypeStruct((MODULES * weight_rows // count, LANES), jnp.float32),
            tables,
            tables,
        ),
        in_specs=[vmem, vmem, hbm, vmem, vmem, smem],
        out_specs=(vmem, vmem, hbm, vmem, vmem),
        scratch_shapes=list(table.values()),
        compiler_params=pltpu.CompilerParams(
            collective_id=0, has_side_effects=True, vmem_limit_bytes=62 * 1024 * 1024
        ),
    )(x, cot, w, gains, shifts, kinds)


def on_device_grouped(features, weights, gains, shifts, cotangent, size_group):
    count = lax.axis_size("crops")
    large = count // 4
    weight_rows = weights.shape[2] // LANES
    out, grad, weight_grad, gain, shift = whole_call(
        group_rows(count),
        large,
        count - large,
        features[0],
        cotangent[0],
        weights[0].reshape(MODULES, weight_rows, LANES),
        gains[0],
        shifts[0],
        size_group,
    )
    share = weight_rows // count
    weight_grad = weight_grad.reshape(share, MODULES, LANES).transpose(1, 0, 2)
    weight_grad = with_layout_constraint(weight_grad, Layout((1, 0, 2)))
    return (
        out[None],
        grad[None],
        weight_grad.reshape(1, MODULES, share * LANES),
        gain[None],
        shift[None],
    )


def group_rows(count):
    large = count // 4
    rows = max(large * (LH // 8) * (LW // 8), (count - large) * (SH // 8) * (SW // 8))
    return -(-rows // 16) * 16


def fits(count):
    return count % 8 == 0 and group_rows(count) <= 96


def solution(mesh):
    placed = (
        P("branch", "crops", None),
        P("branch", None, None),
        P("branch", None, None, None),
        P("branch", None, None, None),
        P("branch", "crops", None),
        P(),
    )
    return jax.shard_map(
        on_device_grouped if fits(mesh.shape["crops"]) else on_device,
        mesh=mesh,
        in_specs=placed,
        out_specs=(
            P("branch", "crops", None),
            P("branch", "crops", None),
            P("branch", None, "crops"),
            P("branch", None, None, "crops"),
            P("branch", None, None, "crops"),
        ),
        check_vma=False,
    )
```

```python
from functools import partial
from types import SimpleNamespace
import math

import jax
import jax.numpy as jnp
import numpy as np
from jax import lax
from jax.experimental import pallas as pl
from jax.experimental.layout import Layout, with_layout_constraint
from jax.experimental.pallas import tpu as pltpu
from jax.sharding import PartitionSpec as P

C0 = 32
BLOCKS = 1
MODULES = 2
CROPS_DEV = 1
SH = 32
SW = 24
LH = 64
LW = 48
ROWS = 768
MSG_ROWS = 384


EPS = 1e-05


def as_sent(x):

    def short(part):
        return part.astype(jnp.bfloat16) if part.dtype == jnp.float32 else part

    return jax.tree.map(short, x)


def sender_plan(branch_index, top_channels, blocks):
    channels = top_channels << branch_index
    operations = []
    for block_index in range(blocks):
        operations.append(
            SimpleNamespace(
                phase=2 * block_index,
                source=("h", block_index),
                level=branch_index,
                cin=channels,
                cout=channels,
                stride=1,
                taps=3,
                act="silu",
                output=("u", block_index),
                skip=None,
                dest=-1,
            )
        )
        operations.append(
            SimpleNamespace(
                phase=2 * block_index + 1,
                source=("u", block_index),
                level=branch_index,
                cin=channels,
                cout=channels,
                stride=1,
                taps=3,
                act="res",
                output=("h", block_index + 1),
                skip=("h", block_index),
                dest=-1,
            )
        )
    top_name = ("h", blocks)
    for target in range(branch_index):
        operations.append(
            SimpleNamespace(
                phase=2 * blocks,
                source=top_name,
                level=branch_index,
                cin=channels,
                cout=top_channels << target,
                stride=1,
                taps=1,
                act="none",
                output=None,
                skip=None,
                dest=target,
            )
        )
    for target in range(branch_index + 1, 4):
        for depth_step in range(1, target - branch_index + 1):
            is_last = depth_step == target - branch_index
            operations.append(
                SimpleNamespace(
                    phase=2 * blocks + depth_step - 1,
                    source=top_name if depth_step == 1 else ("chain", target, depth_step - 1),
                    level=branch_index + depth_step,
                    cin=channels,
                    cout=top_channels << target if is_last else channels,
                    stride=2,
                    taps=3,
                    act="none" if is_last else "silu",
                    output=None if is_last else ("chain", target, depth_step),
                    skip=None,
                    dest=target if is_last else -1,
                )
            )
    for position, operation in enumerate(operations):
        operation.slot = position
        operation.size = (
            operation.taps * operation.taps * operation.cin * operation.cout
        )
        if operation.taps == 1:
            operation.kshape = (operation.cin, operation.cout)
        else:
            operation.kshape = (3, 3, operation.cin, operation.cout)
    return operations


def phase_lengths(top_channels, blocks):
    phase_count = 2 * blocks + 3
    lengths = [0] * phase_count
    for branch_index in range(4):
        per_phase = [0] * phase_count
        for operation in sender_plan(branch_index, top_channels, blocks):
            per_phase[operation.phase] += operation.size
        lengths = [max(current, candidate) for current, candidate in zip(lengths, per_phase)]
    return lengths


def weighted_plan(branch_index, top_channels, blocks):
    lengths = phase_lengths(top_channels, blocks)
    starts = [sum(lengths[:phase_index]) for phase_index in range(len(lengths))]
    running = [0] * len(lengths)
    operations = sender_plan(branch_index, top_channels, blocks)
    for operation in operations:
        phase_index = operation.phase
        operation.inner = running[phase_index]
        operation.offset = starts[phase_index] + running[phase_index]
        operation.position = sum(
            (1 for earlier in operations[: operation.slot] if earlier.phase == phase_index)
        )
        running[phase_index] += operation.size
    return operations


def phase_operations(branch_index, phase_index):
    return [
        operation
        for operation in weighted_plan(branch_index, C0, BLOCKS)
        if operation.phase == phase_index
    ]


def input_names(operations):
    source_names = []
    for operation in operations:
        if operation.source not in source_names:
            source_names.append(operation.source)
    return source_names


def silu_slope(value):
    sigmoid = jax.nn.sigmoid(value)
    return sigmoid * (1.0 + value * (1.0 - sigmoid))


def crop_cells(size_kind):
    return (LH, LW) if size_kind else (SH, SW)


def map_dims(size_kind, level, channels):
    height, breadth = crop_cells(size_kind)
    return (CROPS_DEV, height >> level, breadth >> level, channels)


def source_dims(branch_index, size_kind, map_name):
    level = branch_index + map_name[2] if map_name[0] == "chain" else branch_index
    return map_dims(size_kind, level, C0 << branch_index)


def preact_dims(size_kind, operation):
    return map_dims(size_kind, operation.level, operation.cout)


def to_canvas(arrays, value_type):
    if not arrays:
        return jnp.zeros((ROWS, 128), value_type)
    flattened = jnp.concatenate([array.reshape(-1).astype(value_type) for array in arrays])
    return jnp.pad(flattened, (0, ROWS * 128 - flattened.shape[0])).reshape(ROWS, 128)


def from_canvas(canvas, dims_list):
    flattened = canvas.reshape(-1)
    pieces = []
    offset = 0
    for dims_entry in dims_list:
        count_here = math.prod(dims_entry)
        pieces.append(flattened[offset : offset + count_here].reshape(dims_entry))
        offset += count_here
    return pieces


def to_slot(array):
    flattened = array.reshape(-1)
    return jnp.pad(flattened, (0, MSG_ROWS * 128 - flattened.shape[0])).reshape(MSG_ROWS, 128)


def from_slot(slot_rows, dims_entry):
    return slot_rows.reshape(-1)[: math.prod(dims_entry)].reshape(dims_entry)


def upsample(message, factor):
    crop_count, height, breadth, channels = message.shape
    widened = jnp.broadcast_to(
        message[:, :, None, :, None, :], (crop_count, height, factor, breadth, factor, channels)
    )
    return widened.reshape(crop_count, height * factor, breadth * factor, channels)


def block_pool(array, factor):
    crop_count, height, breadth, channels = array.shape
    return array.reshape(
        crop_count, height // factor, factor, breadth // factor, factor, channels
    ).sum(axis=(2, 4))


def kernel_piece(module_weights, operation):
    start = operation.offset
    return module_weights[start : start + operation.size].reshape(operation.kshape)


def conv_forward(operation, source, kernel):
    if operation.taps == 1:
        return jnp.einsum("nhwc,cd->nhwd", source, kernel, preferred_element_type=jnp.float32)
    stride = operation.stride
    return lax.conv_general_dilated(
        source,
        kernel,
        (stride, stride),
        ((1, 1), (1, 1)),
        dimension_numbers=("NHWC", "HWIO", "NHWC"),
        preferred_element_type=jnp.float32,
    )


def conv_backward(operation, source, kernel, upstream):
    if operation.taps == 1:
        source_grad = jnp.einsum(
            "nhwd,cd->nhwc", upstream, kernel, preferred_element_type=jnp.float32
        )
        kernel_grad = jnp.einsum(
            "nhwc,nhwd->cd", source, upstream, preferred_element_type=jnp.float32
        )
        return (source_grad, kernel_grad)
    stride = operation.stride
    flipped = jnp.transpose(kernel[::-1, ::-1], (0, 1, 3, 2))
    high_pad = 2 if stride == 2 else 1
    source_grad = lax.conv_general_dilated(
        upstream,
        flipped,
        (1, 1),
        ((1, high_pad), (1, high_pad)),
        lhs_dilation=(stride, stride),
        dimension_numbers=("NHWC", "HWIO", "NHWC"),
        preferred_element_type=jnp.float32,
    )
    kernel_grad = lax.conv_general_dilated(
        source,
        upstream,
        (1, 1),
        ((1, 2 - stride), (1, 2 - stride)),
        rhs_dilation=(stride, stride),
        dimension_numbers=("CHWN", "IHWO", "NHWC"),
        preferred_element_type=jnp.float32,
    )
    return (source_grad, jnp.transpose(kernel_grad, (1, 2, 0, 3)))


def cell_total(counts, size_kind, level):
    height, breadth = crop_cells(size_kind)
    return counts[size_kind] * float(CROPS_DEV * (height >> level) * (breadth >> level))


def norm_terms(totals, counts, size_kind, operation):
    cells_here = cell_total(counts, size_kind, operation.level)
    channels = operation.cout
    position = operation.position
    average = totals[size_kind, 0, position, :channels] / cells_here
    variance = totals[size_kind, 1, position, :channels] / cells_here - average * average
    return (average, lax.rsqrt(variance + EPS))


def forward_conv(branch_index, size_kind, phase_index, source_canvas, module_weights):
    operations = phase_operations(branch_index, phase_index)
    source_names = input_names(operations)
    pieces = from_canvas(
        source_canvas, [source_dims(branch_index, size_kind, map_name) for map_name in source_names]
    )
    sources = {
        map_name: piece.astype(jnp.bfloat16) for map_name, piece in zip(source_names, pieces)
    }
    preacts = []
    totals = jnp.zeros((2, 2, 3, 8 * C0), jnp.float32)
    for operation in operations:
        preact = conv_forward(
            operation, sources[operation.source], kernel_piece(module_weights, operation)
        )
        preacts.append(preact)
        channels = operation.cout
        position = operation.position
        totals = totals.at[size_kind, 0, position, :channels].set(jnp.sum(preact, axis=(0, 1, 2)))
        totals = totals.at[size_kind, 1, position, :channels].set(
            jnp.sum(preact * preact, axis=(0, 1, 2))
        )
    return (to_canvas(preacts, jnp.float32), totals)


def forward_norm(
    branch_index,
    size_kind,
    phase_index,
    preact_canvas,
    totals,
    counts,
    module_gains,
    module_shifts,
    skip_canvas,
    message_buffer,
):
    operations = phase_operations(branch_index, phase_index)
    preacts = from_canvas(
        preact_canvas, [preact_dims(size_kind, operation) for operation in operations]
    )
    skip_map = from_canvas(skip_canvas, [map_dims(size_kind, branch_index, C0 << branch_index)])[0]
    produced = []
    for operation, preact in zip(operations, preacts):
        average, inverse_std = norm_terms(totals, counts, size_kind, operation)
        norm_slot = operation.slot
        channels = operation.cout
        normed = (preact - average) * inverse_std * module_gains[
            norm_slot, :channels
        ] + module_shifts[norm_slot, :channels]
        if operation.act == "silu":
            produced.append(jax.nn.silu(normed))
        elif operation.act == "res":
            produced.append(jax.nn.silu(normed + skip_map))
        else:
            message_buffer = message_buffer.at[operation.dest].set(
                to_slot(normed.astype(jnp.bfloat16))
            )
    return (to_canvas(produced, jnp.float32), message_buffer)


def receive_forward(branch_index, size_kind, top_canvas, received):
    channels = C0 << branch_index
    summed = from_canvas(top_canvas, [map_dims(size_kind, branch_index, channels)])[0]
    for sender in range(4):
        if sender < branch_index:
            summed = summed + from_slot(
                received[sender], map_dims(size_kind, branch_index, channels)
            ).astype(jnp.float32)
        elif sender > branch_index:
            coarse = from_slot(received[sender], map_dims(size_kind, sender, channels))
            summed = summed + upsample(coarse, 2 ** (sender - branch_index)).astype(jnp.float32)
    return (to_canvas([jax.nn.silu(summed)], jnp.float32), to_canvas([summed], jnp.float32))


def receive_backward(branch_index, size_kind, grad_canvas, summed_canvas):
    dims_here = map_dims(size_kind, branch_index, C0 << branch_index)
    upstream = from_canvas(grad_canvas, [dims_here])[0]
    summed = from_canvas(summed_canvas, [dims_here])[0]
    summed_grad = upstream * silu_slope(summed)
    buffer = jnp.zeros((4, MSG_ROWS, 128), jnp.bfloat16)
    for sender in range(4):
        if sender < branch_index:
            buffer = buffer.at[sender].set(to_slot(summed_grad.astype(jnp.bfloat16)))
        elif sender > branch_index:
            pooled = block_pool(summed_grad, 2 ** (sender - branch_index))
            buffer = buffer.at[sender].set(to_slot(pooled.astype(jnp.bfloat16)))
    return (to_canvas([summed_grad], jnp.float32), buffer)


def backward_stats(
    branch_index,
    size_kind,
    phase_index,
    dout_canvas,
    message_grads,
    preact_canvas,
    totals,
    counts,
    module_gains,
    module_shifts,
    skip_canvas,
):
    operations = phase_operations(branch_index, phase_index)
    preacts = from_canvas(
        preact_canvas, [preact_dims(size_kind, operation) for operation in operations]
    )
    producing = [operation for operation in operations if operation.act != "none"]
    output_grads = from_canvas(
        dout_canvas, [preact_dims(size_kind, operation) for operation in producing]
    )
    grads_by_name = {
        operation.output: piece for operation, piece in zip(producing, output_grads)
    }
    skip_map = from_canvas(skip_canvas, [map_dims(size_kind, branch_index, C0 << branch_index)])[0]
    upstreams = []
    skip_grads = []
    sums_local = jnp.zeros((2, 2, 3, 8 * C0), jnp.float32)
    for operation, preact in zip(operations, preacts):
        average, inverse_std = norm_terms(totals, counts, size_kind, operation)
        norm_slot = operation.slot
        channels = operation.cout
        centered = (preact - average) * inverse_std
        normed = centered * module_gains[norm_slot, :channels] + module_shifts[norm_slot, :channels]
        if operation.act == "silu":
            upstream = grads_by_name[operation.output] * silu_slope(normed)
        elif operation.act == "res":
            upstream = grads_by_name[operation.output] * silu_slope(normed + skip_map)
            skip_grads.append(upstream)
        else:
            upstream = from_slot(
                message_grads[operation.dest], preact_dims(size_kind, operation)
            ).astype(jnp.float32)
        upstreams.append(upstream)
        position = operation.position
        sums_local = sums_local.at[size_kind, 0, position, :channels].set(
            jnp.sum(upstream, axis=(0, 1, 2))
        )
        sums_local = sums_local.at[size_kind, 1, position, :channels].set(
            jnp.sum(upstream * centered, axis=(0, 1, 2))
        )
    return (to_canvas(upstreams, jnp.float32), sums_local, to_canvas(skip_grads, jnp.float32))


def backward_apply(
    branch_index,
    size_kind,
    phase_index,
    upstream_canvas,
    preact_canvas,
    totals,
    grad_totals,
    counts,
    source_canvas,
    module_weights,
    module_gains,
):
    operations = phase_operations(branch_index, phase_index)
    preacts = from_canvas(
        preact_canvas, [preact_dims(size_kind, operation) for operation in operations]
    )
    upstreams = from_canvas(
        upstream_canvas, [preact_dims(size_kind, operation) for operation in operations]
    )
    source_names = input_names(operations)
    source_list = [source_dims(branch_index, size_kind, map_name) for map_name in source_names]
    pieces = from_canvas(source_canvas, source_list)
    sources = {
        map_name: piece.astype(jnp.bfloat16) for map_name, piece in zip(source_names, pieces)
    }
    source_grads = {
        map_name: jnp.zeros(dims_entry, jnp.float32)
        for map_name, dims_entry in zip(source_names, source_list)
    }
    kernel_grads = []
    slot_count = module_gains.shape[0]
    gain_part = jnp.zeros((slot_count, 8 * C0), jnp.float32)
    shift_part = jnp.zeros((slot_count, 8 * C0), jnp.float32)
    for operation, preact, upstream in zip(operations, preacts, upstreams):
        average, inverse_std = norm_terms(totals, counts, size_kind, operation)
        cells_here = cell_total(counts, size_kind, operation.level)
        norm_slot = operation.slot
        channels = operation.cout
        position = operation.position
        centered = (preact - average) * inverse_std
        mean_upstream = grad_totals[size_kind, 0, position, :channels] / cells_here
        mean_cross = grad_totals[size_kind, 1, position, :channels] / cells_here
        preact_grad = (
            module_gains[norm_slot, :channels]
            * inverse_std
            * (upstream - mean_upstream - centered * mean_cross)
        )
        source_grad, kernel_grad = conv_backward(
            operation,
            sources[operation.source],
            kernel_piece(module_weights, operation),
            preact_grad.astype(jnp.bfloat16),
        )
        source_grads[operation.source] = source_grads[operation.source] + source_grad
        kernel_grads.append(kernel_grad.reshape(-1))
        gain_part = gain_part.at[norm_slot, :channels].set(
            grad_totals[0, 1, position, :channels] + grad_totals[1, 1, position, :channels]
        )
        shift_part = shift_part.at[norm_slot, :channels].set(
            grad_totals[0, 0, position, :channels] + grad_totals[1, 0, position, :channels]
        )
    phase_length = phase_lengths(C0, BLOCKS)[phase_index]
    if kernel_grads:
        joined = jnp.concatenate(kernel_grads)
        weight_part = jnp.pad(joined, (0, phase_length - joined.shape[0]))
    else:
        weight_part = jnp.zeros((phase_length,), jnp.float32)
    return (
        to_canvas([source_grads[map_name] for map_name in source_names], jnp.float32),
        weight_part,
        gain_part,
        shift_part,
    )


def on_device(features, weights, gains, shifts, cotangent, size_group):
    crop_shard = lax.axis_index("crops")
    shard_count = lax.axis_size("crops")
    crop_kind = size_group[crop_shard]
    large_count = jnp.sum(size_group).astype(jnp.float32)
    counts = jnp.stack([shard_count - large_count, large_count])
    case_index = lax.axis_index("branch") * 2 + crop_kind
    phase_total = 2 * BLOCKS + 3
    zero_canvas = jnp.zeros((ROWS, 128), jnp.float32)
    empty_buffer = jnp.zeros((4, MSG_ROWS, 128), jnp.bfloat16)

    def run_phase(function, statics, operands):
        branches_list = [
            partial(function, branch_index, size_kind, *statics)
            for branch_index in range(4)
            for size_kind in range(2)
        ]
        return lax.switch(case_index, branches_list, *operands)

    def statistics(local_totals):
        return lax.psum(local_totals, "crops")

    def module_forward(module, start_canvas, kept):
        module_weights = weights[0, module]
        module_gains = gains[0, module]
        module_shifts = shifts[0, module]
        record = SimpleNamespace(sources=[], preacts=[], totals=[])
        h_canvas = start_canvas
        u_canvas = zero_canvas
        chain_canvas = zero_canvas
        buffer = empty_buffer
        for phase_index in range(phase_total):
            if phase_index < 2 * BLOCKS:
                source = h_canvas if phase_index % 2 == 0 else u_canvas
            elif phase_index == 2 * BLOCKS:
                source = h_canvas
            else:
                source = chain_canvas
            preact, local_totals = run_phase(forward_conv, (phase_index,), (source, module_weights))
            global_totals = kept.totals[phase_index] if kept else statistics(local_totals)
            produced, buffer = run_phase(
                forward_norm,
                (phase_index,),
                (preact, global_totals, counts, module_gains, module_shifts, h_canvas, buffer),
            )
            record.sources.append(source)
            record.preacts.append(preact)
            record.totals.append(global_totals)
            if phase_index < 2 * BLOCKS:
                if phase_index % 2 == 0:
                    u_canvas = produced
                else:
                    h_canvas = produced
            else:
                chain_canvas = produced
        received = (
            kept.received
            if kept
            else jax.tree.map(
                lambda part, own: part.astype(own.dtype),
                lax.all_to_all(as_sent(buffer), "branch", split_axis=0, concat_axis=0, tiled=True),
                buffer,
            )
        )
        result, summed = run_phase(receive_forward, (), (h_canvas, received))
        record.summed = summed
        record.received = received
        return (result, record)

    checkpoints = [features[0].astype(jnp.float32)]
    first_records = []
    for module in range(MODULES):
        result, record = module_forward(module, checkpoints[-1], None)
        checkpoints.append(result)
        first_records.append(record)
    outputs = checkpoints[-1].astype(jnp.bfloat16)
    grad_canvas = cotangent[0].astype(jnp.float32)
    module_grads = [None] * MODULES
    gain_grads = [None] * MODULES
    shift_grads = [None] * MODULES
    for module in reversed(range(MODULES)):
        kept = None
        unused_result, record = module_forward(module, checkpoints[module], kept)
        module_module_weights = weights[0, module]
        module_module_gains = gains[0, module]
        module_module_shifts = shifts[0, module]
        summed_grad, back_buffer = run_phase(receive_backward, (), (grad_canvas, record.summed))
        message_grads = jax.tree.map(
            lambda part, own: part.astype(own.dtype),
            lax.all_to_all(as_sent(back_buffer), "branch", split_axis=0, concat_axis=0, tiled=True),
            back_buffer,
        )
        top_grad = summed_grad
        chain_grad = zero_canvas
        u_grad = zero_canvas
        pending_skip = zero_canvas
        weight_parts = [None] * phase_total
        gain_total = jnp.zeros(gains.shape[2:], jnp.float32)
        shift_total = jnp.zeros(gains.shape[2:], jnp.float32)
        for module_phase_index in reversed(range(phase_total)):
            if module_phase_index >= 2 * BLOCKS:
                output_grad = chain_grad
                skip_canvas = zero_canvas
            elif module_phase_index % 2 == 1:
                output_grad = top_grad
                skip_canvas = record.sources[module_phase_index - 1]
            else:
                output_grad = u_grad
                skip_canvas = zero_canvas
            module_preact = record.preacts[module_phase_index]
            totals = record.totals[module_phase_index]
            upstream, module_local_totals, skip_grad = run_phase(
                backward_stats,
                (module_phase_index,),
                (
                    output_grad,
                    message_grads,
                    module_preact,
                    totals,
                    counts,
                    module_module_gains,
                    module_module_shifts,
                    skip_canvas,
                ),
            )
            grad_totals = lax.psum(module_local_totals, "crops")
            source_grad, weight_parts[module_phase_index], gain_part, shift_part = run_phase(
                backward_apply,
                (module_phase_index,),
                (
                    upstream,
                    module_preact,
                    totals,
                    grad_totals,
                    counts,
                    record.sources[module_phase_index],
                    module_module_weights,
                    module_module_gains,
                ),
            )
            gain_total = gain_total + gain_part
            shift_total = shift_total + shift_part
            if module_phase_index > 2 * BLOCKS:
                chain_grad = source_grad
            elif module_phase_index == 2 * BLOCKS:
                top_grad = top_grad + source_grad
            elif module_phase_index % 2 == 1:
                u_grad = source_grad
                pending_skip = skip_grad
            else:
                top_grad = source_grad + pending_skip
        joined = jnp.concatenate(weight_parts)
        weight_grad = jnp.pad(joined, (0, weights.shape[2] - joined.shape[0]))
        grad_canvas, weight_grad, gain_grads[module], shift_grads[module] = (
            top_grad,
            weight_grad,
            gain_total,
            shift_total,
        )
        module_grads[module] = weight_grad
    weight_out = lax.psum_scatter(jnp.stack(module_grads), "crops", scatter_dimension=1, tiled=True)
    share = gains.shape[3] // shard_count
    gain_out = lax.dynamic_slice_in_dim(jnp.stack(gain_grads), crop_shard * share, share, axis=2)
    shift_out = lax.dynamic_slice_in_dim(jnp.stack(shift_grads), crop_shard * share, share, axis=2)
    return (outputs[None], grad_canvas[None], weight_out[None], gain_out[None], shift_out[None])


LANES = 128
SLOTS = 8
MASKS = 7
DOWN = (((1,), (0,)), ((), ()))
ACROSS = (((1,), (1,)), ((), ()))
ALONG = (((0,), (0,)), ((), ()))


def unit_table(k):
    operations = weighted_plan(k, C0, BLOCKS)
    planes = 8 >> k
    channels = C0 << k
    units = {}
    stat = 0

    def add(name, kind, source, lanes_in, planes_in, planes_out, members):
        nonlocal stat
        segs = []
        tile = 0
        for operation, lanes, chain in members:
            cout = operation.cout
            level = operation.level if operation.taps == 3 else operation.dest
            segs.append(
                SimpleNamespace(
                    slot=operation.slot,
                    off=operation.offset // LANES,
                    cin=operation.cin,
                    cout=cout,
                    taps=operation.taps,
                    tile=tile,
                    tiles=lanes // LANES,
                    blocks=max(1, (8 >> level)),
                    dest=operation.dest,
                    act=operation.act,
                    chain=chain,
                    up=k - operation.dest if operation.taps == 1 else 0,
                )
            )
            tile += lanes // LANES
        rows = {"s1": 768 if k == 3 else 512, "s2": lanes_in + LANES, "p1": 256}[kind]
        units[name] = SimpleNamespace(
            name=name,
            kind=kind,
            source=source,
            lanes_in=lanes_in,
            blocks_in=planes_in,
            planes_in=planes_in,
            planes=planes_out,
            segs=segs,
            tiles=tile,
            rows=rows,
            stat=stat,
            depth=1 if kind == "p1" else 3,
        )
        stat += tile

    add("a", "s1", "h", 256, planes, planes, [(operations[0], 256, None)])
    add("b", "s1", "u", 256, planes, planes, [(operations[1], 256, None)])
    ups = [operation for operation in operations if operation.taps == 1]
    if ups:
        add("u", "p1", "t", 256, planes, planes, [(operation, 256, None) for operation in ups])
    firsts, chains = [], {}
    for target in range(k + 1, 4):
        steps = [
            operation
            for operation in operations
            if operation.taps == 3 and operation.stride == 2
        ]
        start = sum(i - k for i in range(k + 1, target))
        chains[target] = steps[start : start + target - k]
        if target == k + 1:
            firsts.append((chains[target][0], 256, None))
        else:
            firsts.append((chains[target][0], LANES, "c1" if target == k + 2 else "c2"))
    if firsts:
        add("d", "s2", "t", 256, planes, planes // 2, firsts)
    if k <= 1:
        add("e", "s2", "c1", LANES, planes // 2, planes // 4, [(chains[k + 2][1], 256, None)])
    if k == 0:
        add("f", "s2", "c2", LANES, planes // 2, planes // 4, [(chains[3][1], LANES, "c3")])
        add("g", "s2", "c3", LANES, planes // 4, planes // 8, [(chains[3][2], 256, None)])
    return units


def links(k, unit, seg):
    cin = seg.cin
    count_in, count_out = unit.blocks_in, seg.blocks
    found = []
    if unit.kind == "p1":
        for plane in range(count_in):
            wide = 1 << seg.up
            found.append((plane * cin, 0, set(range(plane * wide, plane * wide + wide))))
        return found
    if unit.kind == "s1" and k == 3:
        return [(256 * tap, tap, {0}) for tap in range(3)]
    stride = 1 if unit.kind == "s1" else 2
    for plane in range(count_in):
        for tap in range(3):
            at = plane - tap + 1
            if at % stride == 0 and 0 <= at // stride < count_out:
                found.append((plane * cin, tap, {at // stride}))
    if stride == 1:
        found.append((256, 2, {count_out - 1}))
        found.append((512 - cin, 0, {0}))
    else:
        lanes_in = unit.lanes_in
        found.append((lanes_in + (count_in - 1) * cin - (lanes_in - LANES), 0, {0}))
    return found


def message_slot(k, other):
    return sum(2 * (8 >> max(k, before)) for before in range(other) if before != k)


def log2(value):
    return value.bit_length() - 1


def sigmoid_of(value):
    return 0.5 * jnp.tanh(0.5 * value) + 0.5


def silu_of(value):
    return value * sigmoid_of(value)


def slope_of(value):
    sigmoid = sigmoid_of(value)
    return sigmoid * (1.0 + value * (1.0 - sigmoid))


def planes_loop(count, body, turns=1):
    def step(index, carry):
        for turn in range(turns):
            body(index * turns + turn)
        return carry

    turns = min(turns, count)
    if count == turns:
        step(0, 0)
    else:
        lax.fori_loop(0, count // turns, step, 0)


def planes_sum(count, body, initial, turns=1):
    def step(index, carry):
        for turn in range(turns):
            carry = body(index * turns + turn, carry)
        return carry

    turns = min(turns, count)
    if count == turns:
        return step(0, initial)
    return lax.fori_loop(0, count // turns, step, initial)


def partial_sum(value):
    rows = value.shape[0]
    return jnp.sum(value.reshape(rows // 8, 8, value.shape[1]), axis=0)


class Planes:
    def __init__(self, mode, tiles, planes, masks, rows, main, edge=None, right=None):
        self.mode, self.tiles, self.planes = mode, tiles, planes
        self.masks, self.rows = masks, rows
        self.main, self.edge, self.right = main, edge, right
        self.base = 1 if mode in ("s1", "wide", "s2") else 0
        extra = {"s1": 2, "wide": 2, "s2": 1, "dz2": 1, "p": 0}[mode]
        self.span = planes + extra
        self.unit = tiles * self.span

    def at(self, m, tile, plane):
        return m * self.unit + tile * self.span + plane + self.base

    def edge_at(self, m, tile, plane):
        if self.mode == "s2":
            return m * self.span + plane + self.base
        return self.at(m, tile, plane)

    def from_left(self, value):
        return pltpu.roll(value, 1, 0) * self.masks[1]

    def from_right(self, value):
        return pltpu.roll(value, self.rows - 1, 0) * self.masks[2]

    def store(self, m, tile, plane, value):
        where = self.at(m, tile, plane)
        self.main[where] = value.astype(jnp.bfloat16)
        if self.mode == "s1":
            side = self.from_right(value) if tile == 0 else self.from_left(value)
            self.edge[where] = side.astype(jnp.bfloat16)
        elif self.mode == "wide":
            self.edge[where] = self.from_left(value).astype(jnp.bfloat16)
            self.right[where] = self.from_right(value).astype(jnp.bfloat16)
        elif self.mode == "s2":
            if tile == self.tiles - 1:
                self.edge[self.edge_at(m, tile, plane)] = self.from_left(value).astype(jnp.bfloat16)
        elif self.mode == "dz2":
            self.edge[where] = self.from_right(value).astype(jnp.bfloat16)

    def close(self, m):
        rows = self.rows
        for tile in range(self.tiles):
            if self.mode in ("s1", "wide", "s2"):
                last = self.main[self.at(m, tile, self.planes - 1)].astype(jnp.float32)
                above = pltpu.roll(last, 6, 0) * self.masks[3] + pltpu.roll(last, 3, 0) * self.masks[4]
                self.store(m, tile, -1, above)
            if self.mode in ("s1", "wide", "dz2"):
                first = self.main[self.at(m, tile, 0)].astype(jnp.float32)
                below = (
                    pltpu.roll(first, rows - 6, 0) * self.masks[5]
                    + pltpu.roll(first, rows - 3, 0) * self.masks[6]
                )
                self.store(m, tile, self.planes, below)


class Branch:
    def __init__(self, k, rows, large, small, share, refs, masks, core):
        self.k, self.rows, self.refs, self.masks = k, rows, refs, masks
        self.units = unit_table(k)
        self.planes = 8 >> k
        self.core = core
        self.large, self.small, self.count = large, small, large + small
        self.cells = (small * (SH // 8) * (SW // 8), large * (LH // 8) * (LW // 8))
        self.quarter = lax.axis_index("crops") // 2
        self.share = share
        r = refs
        make = partial(Planes, masks=masks, rows=rows)
        one = "wide" if k == 3 else "s1"
        self.maps = dict(
            h=make(one, 2, self.planes, main=r.hC, edge=r.hE, right=r.hR),
            u=make(one, 2, self.planes, main=r.uC, edge=r.uE, right=r.uR),
            t=make("p" if k == 3 else "s2", 2, self.planes, main=r.tC, edge=r.tE),
        )
        if k <= 1:
            self.maps["c1"] = make("s2", 1, self.planes // 2, main=r.c1C, edge=r.c1E)
        if k == 0:
            self.maps["c2"] = make("s2", 1, 4, main=r.c2C, edge=r.c2E)
            self.maps["c3"] = make("s2", 1, 2, main=r.c3C, edge=r.c3E)
        self.grads = dict(t=r.gt, u=r.gu, c1=r.gc1, c2=r.gc2, c3=r.gc3)

    def lane_block(self, shape, cout):
        lanes = lax.broadcasted_iota(jnp.int32, shape, 1)
        return lanes >> log2(cout)

    def keep(self, value, cout, which):
        count = LANES // cout
        if len(which) == count:
            return value
        block = self.lane_block(value.shape, cout)
        mask = block == which[0]
        for entry in which[1:]:
            mask = mask | (block == entry)
        return jnp.where(mask, value, 0.0)

    def spread(self, value, cout):
        shift = LANES // 2
        while shift >= cout:
            value = value + pltpu.roll(value, shift, 1)
            shift //= 2
        return value

    def local_blocks(self, seg, tile, wanted):
        count = LANES // seg.cout
        return [q for q in range(count) if (tile * count + q) % seg.blocks in wanted]


    def segments(self):
        return [(unit, seg) for unit in self.units.values() for seg in unit.segs]

    def pieces(self, index):
        def split(seg):
            count = seg.taps**2 * seg.cin * seg.cout // LANES
            return max(1, count // PIECE), min(count, PIECE)

        found = [split(seg) for _, seg in self.segments()]
        return *found[index], sum(many for many, _ in found[:index])

    def fetch(self, index, piece):
        r = self.refs
        _, seg = self.segments()[index]
        _, count, before = self.pieces(index)
        slot = (before + piece) % 2
        return pltpu.make_async_copy(
            r.w.at[pl.ds(seg.off + piece * count, count)],
            r.raw.at[slot, pl.ds(0, count)],
            r.wsem.at[slot],
        )

    def widen(self, index):
        r = self.refs
        many, count, before = self.pieces(index)
        chunk = 16 if count % 16 == 0 else 8

        def convert(piece):
            def body(step):
                for q in range(chunk):
                    at = step * chunk + q
                    value = r.raw[(before + piece) % 2, at].astype(jnp.float32)
                    r.work[pl.ds(2 * (piece * count + at), 2)] = value

            planes_loop(count // chunk, body)

        def step(piece):
            self.fetch(index, piece).wait()
            self.fetch(index, piece + 1).start()
            convert(piece)

        if many > 1:
            planes_loop(many - 1, step)
        self.fetch(index, many - 1).wait()
        if index + 1 < len(self.segments()):
            self.fetch(index + 1, 0).start()
        convert(many - 1)

    def expand_one(self, m, unit, seg):
        r = self.refs
        target = getattr(r, "T" + unit.name)
        depth, cin, cout = unit.depth, seg.cin, seg.cout
        taps = seg.taps**2
        count = taps * cin * cout // LANES
        wf, rep = r.work, r.rep
        if cout < LANES:
            ratio = LANES // cout
            flat = wf[pl.ds(m, count, stride=2)]
            for part in range(ratio):
                rep[pl.ds(part, count, stride=ratio)] = self.spread(
                    self.keep(flat, cout, [part]), cout
                )

        def tap_rows(tap, tile):
            if cout < LANES:
                return rep[pl.ds(pl.multiple_of(tap * cin, cin), cin)]
            if cout == LANES:
                return wf[pl.ds(m + tap * (2 * cin), cin, stride=2)]
            return wf[pl.ds(m + tap * (4 * cin) + 2 * tile, cin, stride=4)]

        by_row = {}
        for row, tap, wanted in links(self.k, unit, seg):
            by_row.setdefault(row, []).append((tap, wanted))

        def fill(d):
            width = 3 if taps == 9 else 1
            for tile in range(seg.tiles):
                column = (seg.tile + tile) * LANES
                for row in range(0, unit.rows, cin):
                    total = None
                    for tap, wanted in by_row.get(row, []):
                        if cout <= LANES:
                            local = self.local_blocks(seg, tile, wanted)
                            if not local:
                                continue
                            piece = self.keep(tap_rows(d * width + tap, 0), cout, local)
                        else:
                            piece = tap_rows(d * width + tap, tile)
                        total = piece if total is None else total + piece
                    if total is None:
                        total = jnp.zeros((cin, LANES), jnp.float32)
                    target[m * depth + d, row : row + cin, column : column + LANES] = total.astype(
                        jnp.bfloat16
                    )

        planes_loop(depth, fill)


    def parts(self, unit, source):
        if unit.kind == "p1":
            return [(source.main, range(2), source.at)]
        if source.mode == "wide":
            return [
                (source.edge, range(2), source.at),
                (source.main, range(2), source.at),
                (source.right, range(2), source.at),
            ]
        if unit.kind == "s1":
            return [(source.main, range(2), source.at), (source.edge, range(2), source.at)]
        last = source.tiles - 1
        return [
            (source.main, range(source.tiles), source.at),
            (source.edge, [last], source.edge_at),
        ]

    def rows_of(self, unit, part, m, d, first, count):
        ref, tiles, at = part
        pieces = []
        for tile in tiles:
            if unit.kind == "s2":
                rows = [ref[at(m, tile, 2 * (first + q) + d - 1)] for q in range(count)]
                pieces.append(rows[0] if count == 1 else jnp.concatenate(rows, axis=0))
            else:
                shift = d - 1 if unit.kind == "s1" else 0
                pieces.append(
                    ref[pl.ds(at(m, tile, first + shift), count)].reshape(count * self.rows, LANES)
                )
        return pieces

    def conv(self, m, unit):
        r = self.refs
        source = self.maps[unit.source]
        target = getattr(r, "T" + unit.name)
        z = getattr(r, "z" + unit.name)
        planes, tiles, depth = unit.planes, unit.tiles, unit.depth
        chunk = min(planes, 4 if tiles <= 2 else 2)
        lanes = tiles * LANES

        def body(step, sums):
            first = step * chunk
            pieces = []
            for d in range(depth):
                for part in self.parts(unit, source):
                    pieces += self.rows_of(unit, part, m, d, first, chunk)
            left = jnp.concatenate(pieces, axis=1)
            right = target[pl.ds(m * depth, depth), 0 : unit.rows, 0:lanes]
            right = right.reshape(depth * unit.rows, lanes)
            result = lax.dot_general(left, right, DOWN, preferred_element_type=jnp.float32)
            for tile in range(tiles):
                block = result[:, tile * LANES : (tile + 1) * LANES]
                z[pl.ds(m * tiles * planes + tile * planes + first, chunk)] = block.reshape(
                    chunk, self.rows, LANES
                )
            return (sums[0] + partial_sum(result), sums[1] + partial_sum(result * result))

        zero = jnp.zeros((8, lanes), jnp.float32)
        sums = planes_sum(planes // chunk, body, (zero, zero))
        for seg in unit.segs:
            scale = self.per_cell(unit, seg)
            totals = self.fold(seg, sums)
            self.norm_rows(m, unit, seg, totals, scale)

    def per_cell(self, unit, seg):
        blocks = seg.tiles * LANES // seg.cout
        small, large = self.cells
        count = unit.planes * blocks
        return jnp.where(self.core == 0, 1.0 / (large * count), 1.0 / (small * count)).astype(
            jnp.float32
        )

    def fold(self, seg, sums):
        first = seg.tile
        found = []
        for value in sums:
            tiles = [
                value[:, (first + t) * LANES : (first + t + 1) * LANES] for t in range(seg.tiles)
            ]
            if seg.cout <= LANES:
                total = tiles[0]
                for tile in tiles[1:]:
                    total = total + tile
                total = jnp.sum(self.spread(total, seg.cout), axis=0, keepdims=True)
                found.append([total] * seg.tiles)
            else:
                found.append([jnp.sum(tile, axis=0, keepdims=True) for tile in tiles])
        return found

    def table_row(self, ref, m, seg, tile):
        slot = seg.slot
        if seg.cout > LANES:
            return ref[m, slot : slot + 1, tile * LANES : (tile + 1) * LANES]
        row = jnp.broadcast_to(ref[m, slot : slot + 1, 0:LANES], (8, LANES))
        if seg.cout < LANES:
            row = self.spread(self.keep(row, seg.cout, [0]), seg.cout)
        return row[0:1]

    def norm_rows(self, m, unit, seg, totals, scale):
        st = self.refs.st
        for tile in range(seg.tiles):
            average = totals[0][tile] * scale
            variance = totals[1][tile] * scale - average * average
            inverse = lax.rsqrt(variance + EPS)
            gain = self.table_row(self.refs.gains, m, seg, tile)
            shift = self.table_row(self.refs.shifts, m, seg, tile)
            where = m * STATS + unit.stat + seg.tile + tile
            factor = gain * inverse
            st[where, 0:1] = average
            st[where, 1:2] = inverse
            st[where, 2:3] = factor
            st[where, 3:4] = shift - average * factor

    def normed(self, m, unit, tile, plane):
        st = self.refs.st
        z = getattr(self.refs, "z" + unit.name)
        where = m * STATS + unit.stat + tile
        value = z[m * unit.tiles * unit.planes + tile * unit.planes + plane]
        return value * st[where, 2:3] + st[where, 3:4]

    def apply_a(self, m):
        unit, u = self.units["a"], self.maps["u"]

        def body(plane):
            for tile in range(2):
                value = silu_of(self.normed(m, unit, tile, plane)) * self.masks[0]
                u.store(m, tile, plane, value)

        planes_loop(self.planes, body, TURNS)
        u.close(m)

    def apply_b(self, m):
        unit, top = self.units["b"], self.maps["t"]
        hf, s = self.refs.hf, self.refs.s

        def body(plane):
            for tile in range(2):
                where = m * 2 * self.planes + tile * self.planes + plane
                value = silu_of(self.normed(m, unit, tile, plane) + hf[where]) * self.masks[0]
                s[where] = value
                top.store(m, tile, plane, value)

        planes_loop(self.planes, body, TURNS)
        top.close(m)

    def apply_rest(self, m, unit):
        sb = self.refs.sb
        for seg in unit.segs:
            chain = self.maps[seg.chain] if seg.chain else None

            def body(plane):
                for tile in range(seg.tiles):
                    value = self.normed(m, unit, seg.tile + tile, plane)
                    if chain is not None:
                        chain.store(m, tile, plane, silu_of(value) * self.masks[0])
                    else:
                        at = message_slot(self.k, seg.dest) + tile * unit.planes + plane
                        sb[at] = value.astype(jnp.bfloat16)

            planes_loop(unit.planes, body, TURNS)
            if chain is not None:
                chain.close(m)
            else:
                self.message(m, seg.dest).start()

    def message(self, e, other):
        count = 2 * (8 >> max(self.k, other))
        r = self.refs
        return pltpu.make_async_remote_copy(
            src_ref=r.sb.at[pl.ds(message_slot(self.k, other), count)],
            dst_ref=r.rb.at[pl.ds(e * 16 + message_slot(other, self.k), count)],
            send_sem=r.ssem.at[e * 4 + other],
            recv_sem=r.rsem.at[e * 4 + self.k],
            device_id=dict(branch=other),
            device_id_type=pl.DeviceIdType.MESH,
        )

    def arrived(self, e, other):
        count = 2 * (8 >> max(self.k, other))
        r = self.refs
        at = message_slot(self.k, other)
        return pltpu.make_async_remote_copy(
            src_ref=r.sb.at[pl.ds(at, count)],
            dst_ref=r.rb.at[pl.ds(e * 16 + at, count)],
            send_sem=r.ssem.at[e * 4 + other],
            recv_sem=r.rsem.at[e * 4 + other],
            device_id=dict(branch=other),
            device_id_type=pl.DeviceIdType.MESH,
        )

    def others(self):
        return [other for other in range(4) if other != self.k]

    def settle(self, e):
        for other in self.others():
            self.message(e, other).wait_send()
        for other in self.others():
            self.arrived(e, other).wait_recv()

    def receive(self, m):
        r = self.refs
        s, rb, hf, out = r.s, r.rb, r.hf, r.outs
        h = self.maps["h"]

        def body(plane):
            for tile in range(2):
                where = m * 2 * self.planes + tile * self.planes + plane
                total = s[where]
                for other in self.others():
                    count = 8 >> max(self.k, other)
                    at = plane >> max(0, other - self.k)
                    slot = m * 16 + message_slot(self.k, other) + tile * count + at
                    total = total + rb[slot].astype(jnp.float32)
                s[where] = total
                value = silu_of(total) * self.masks[0]
                out[tile * self.planes + plane] = value.astype(jnp.bfloat16)

                @pl.when(m + 1 < MODULES)
                def _():
                    hf[2 * self.planes + tile * self.planes + plane] = value
                    h.store(1, tile, plane, value)

        planes_loop(self.planes, body, TURNS)

        @pl.when(m + 1 < MODULES)
        def _():
            h.close(1)

    def take_feature(self, tile, plane, value):
        self.refs.hf[tile * self.planes + plane] = value
        self.maps["h"].store(0, tile, plane, value)

    def take_cotangent(self, tile, plane, value):
        self.refs.gin[tile * self.planes + plane] = value

    def member(self, kind, order):
        kinds = self.refs.kinds
        found, before = jnp.int32(0), jnp.int32(0)
        for at in range(self.count):
            same = kinds[at] == kind
            found = jnp.where(same & (before == order), at, found)
            before = before + same.astype(jnp.int32)
        return found

    def order(self, device):
        kinds = self.refs.kinds
        kind = kinds[device]
        before = jnp.int32(0)
        for at in range(self.count):
            before = before + ((kinds[at] == kind) & (at < device)).astype(jnp.int32)
        return before

    def unpack(self, t, consume):
        r = self.refs
        work, rows, planes = r.work, self.rows, self.planes
        full = SH * SW * C0 // LANES
        gath = r.gathc if t else r.gathx

        @pl.when(self.core == 0)
        def _():
            for at in range(self.large):
                block = gath[self.member(1, at)]
                work[at * ROWS : (at + 1) * ROWS] = block.astype(jnp.float32)

        @pl.when(self.core == 1)
        def _():
            for at in range(self.small):
                block = gath[self.member(0, at), 0:full]
                work[at * full : (at + 1) * full] = block.astype(jnp.float32)
            work[self.small * full : self.large * ROWS] = jnp.zeros(
                (self.large * ROWS - self.small * full, LANES), jnp.float32
            )

        deep = self.large * ROWS // 2
        right = jnp.concatenate([work[pl.ds(j, deep, stride=2)] for j in range(2)], axis=1)
        right = right.astype(jnp.bfloat16)
        cells = Cells(self.core, (rows, LANES), self.small, self.large)
        base = cells.crop * cells.pick(ROWS // 2, full // 2)
        base = base + cells.along * (planes * cells.wide) + cells.across
        base = jnp.where(cells.valid, base, -(1 << 20))
        lane = lax.broadcasted_iota(jnp.int32, (rows, LANES), 1)
        chunk = min(planes, 4)

        def body(step):
            pieces = []
            for q in range(chunk):
                goal = base + (step * chunk + q) * cells.wide
                pieces.append(one_hot(goal, lane, deep))
            left = pieces[0] if chunk == 1 else jnp.concatenate(pieces, axis=0)
            result = lax.dot_general(left, right, DOWN, preferred_element_type=jnp.float32)
            for q in range(chunk):
                for tile in range(2):
                    value = result[q * rows : (q + 1) * rows, tile * LANES : (tile + 1) * LANES]
                    consume(tile, step * chunk + q, value)

        planes_loop(planes // chunk, body)

    def pack_size(self):
        return 48 * self.planes, -(-self.planes * self.rows // LANES) * LANES

    def plan_pack(self):
        r = self.refs
        high, deep = self.pack_size()
        planes = self.planes
        q = lax.broadcasted_iota(jnp.int32, (high, LANES), 0)
        lane = lax.broadcasted_iota(jnp.int32, (high, LANES), 1)
        wide, tall = jnp.where(self.core == 0, 6, 3), jnp.where(self.core == 0, 8, 4)
        cell = jnp.where(self.core == 0, (q * 43691) >> 18, (q * 43691) >> 17)
        across = q - cell * wide
        plane = cell & (planes - 1)
        along = cell >> log2(planes)
        base = plane * self.rows + along * wide + across
        base = jnp.where(along < tall, base, -(1 << 20))
        shard = lax.axis_index("crops")
        for at, device in enumerate((shard, shard + 1 - 2 * self.core)):
            goal = base + self.order(device) * (wide * tall)
            r.hot[at, 0:high, 0:deep] = one_hot(goal, lane, deep)

    def pack(self, units, put):
        high, deep = self.pack_size()
        right = jnp.concatenate([units(tile) for tile in range(2)], axis=1)
        short = deep - right.shape[0]
        parts = [right.astype(jnp.bfloat16)]
        if right.dtype == jnp.float32:
            parts.append((right - parts[0].astype(jnp.float32)).astype(jnp.bfloat16))
        if short:
            empty = jnp.zeros((short, 2 * LANES), jnp.bfloat16)
            parts = [jnp.concatenate([part, empty], axis=0) for part in parts]
        for at in range(2):
            total = None
            for part in parts:
                piece = lax.dot_general(
                    self.refs.hot[at, 0:high, 0:deep],
                    part,
                    DOWN,
                    preferred_element_type=jnp.float32,
                )
                total = piece if total is None else total + piece
            for tile in range(2):
                put(at, pl.ds(tile, high, stride=2), total[:, tile * LANES : (tile + 1) * LANES])

    def pack_outputs(self):
        r = self.refs
        high = 2 * self.pack_size()[0]

        def put(at, where, value):
            r.work[pl.ds(at * ROWS + where.start, where.size, stride=2)] = value

        def units(tile):
            block = r.outs[tile * self.planes : (tile + 1) * self.planes]
            return block.reshape(self.planes * self.rows, LANES)

        self.pack(units, put)
        for at in range(2):
            r.blocks[at, 0:high] = r.work[at * ROWS : at * ROWS + high].astype(jnp.bfloat16)
            if high < ROWS:
                r.blocks[at, high:ROWS] = jnp.zeros((ROWS - high, LANES), jnp.bfloat16)

    def pack_gradient(self):
        r = self.refs
        high = 2 * self.pack_size()[0]

        def put(at, where, value):
            r.slopes[at, where] = value

        def units(tile):
            block = r.gin[tile * self.planes : (tile + 1) * self.planes]
            return block.reshape(self.planes * self.rows, LANES)

        self.pack(units, put)
        if high < ROWS:
            for at in range(2):
                r.slopes[at, high:ROWS] = jnp.zeros((ROWS - high, LANES), jnp.float32)

    def forward(self, m, gather):
        steps = iter(range(1, 4))

        def also():
            step = next(steps, None)
            if step is not None:

                @pl.when(m == 0)
                def _():
                    gather.step(1, step)

        self.conv(m, self.units["a"])
        self.apply_a(m)
        also()
        self.conv(m, self.units["b"])
        self.apply_b(m)
        also()
        for name in ("d", "u", "e", "f", "g"):
            if name in self.units:
                self.conv(m, self.units[name])
                self.apply_rest(m, self.units[name])
                also()
        for _ in range(3):
            also()

        @pl.when(m == MODULES - 1)
        def _():
            gather.collect(1)
            self.unpack(1, self.take_cotangent)
            self.plan_pack()

        self.settle(m)
        self.receive(m)


    def send_back(self, m):
        r = self.refs
        s, gin, gt, sb = r.s, r.gin, r.gt, r.sb
        e = MODULES + m

        def body(plane):
            for tile in range(2):
                at = tile * self.planes + plane
                value = gin[at] * slope_of(s[m * 2 * self.planes + at])
                gt[at] = value
                for other in range(self.k):
                    sb[message_slot(self.k, other) + at] = value.astype(jnp.bfloat16)

        planes_loop(self.planes, body, TURNS)
        for other in reversed(self.others()):
            if other > self.k:
                count = 8 >> other
                wide = 1 << (other - self.k)

                def pool(plane):
                    for tile in range(2):
                        total = gt[tile * self.planes + plane * wide]
                        for step in range(1, wide):
                            total = total + gt[tile * self.planes + plane * wide + step]
                        slot = message_slot(self.k, other) + tile * count + plane
                        sb[slot] = total.astype(jnp.bfloat16)

                planes_loop(count, pool, TURNS)
            self.message(e, other).start()

    def back_unit(self, m, unit):
        r = self.refs
        st, dyb, z = r.st, r.dyb, getattr(r, "z" + unit.name)
        name, planes, tiles = unit.name, unit.planes, unit.tiles
        e = MODULES + m
        sums = {}

        def upstream(seg, tile, plane, normed):
            at = tile * planes + plane
            if name == "b":
                hf = r.hf[m * 2 * planes + at]
                value = r.gt[at] * slope_of(normed + hf)
                r.gin[at] = value
                return value
            if name == "a":
                return r.gu[at] * slope_of(normed)
            if seg.chain:
                return self.grads[seg.chain][at] * slope_of(normed)
            return r.rb[e * 16 + message_slot(self.k, seg.dest) + at].astype(jnp.float32)

        for seg in unit.segs:

            def body(plane, carry):
                result = []
                for tile in range(seg.tiles):
                    at = (seg.tile + tile) * planes + plane
                    where = m * STATS + unit.stat + seg.tile + tile
                    value = z[m * tiles * planes + at]
                    normed = value * st[where, 2:3] + st[where, 3:4]
                    dy = upstream(seg, tile, plane, normed)
                    dyb[at] = dy
                    zhat = (value - st[where, 0:1]) * st[where, 1:2]
                    result.append(carry[2 * tile] + partial_sum(dy))
                    result.append(carry[2 * tile + 1] + partial_sum(dy * zhat))
                return tuple(result)

            zero = jnp.zeros((8, LANES), jnp.float32)
            found = planes_sum(planes, body, (zero,) * (2 * seg.tiles), TURNS)
            pair = [
                jnp.concatenate([found[2 * tile + which] for tile in range(seg.tiles)], axis=1)
                for which in range(2)
            ]
            plain = SimpleNamespace(**vars(seg))
            plain.tile = 0
            totals = self.fold(plain, pair)
            self.table_grads(m, seg, totals)
            sums[seg.slot] = totals
        dz = self.dz_planes(unit)
        for seg in unit.segs:
            scale = self.per_cell(unit, seg)
            totals = sums[seg.slot]

            def apply(plane):
                for tile in range(seg.tiles):
                    at = (seg.tile + tile) * planes + plane
                    where = m * STATS + unit.stat + seg.tile + tile
                    zhat = (z[m * tiles * planes + at] - st[where, 0:1]) * st[where, 1:2]
                    inner = dyb[at] - totals[0][tile] * scale - zhat * (totals[1][tile] * scale)
                    dz.store(0, seg.tile + tile, plane, inner * st[where, 2:3] * self.masks[0])

            planes_loop(planes, apply, TURNS)
        dz.close(0)
        self.back_data(m, unit, dz)
        first = min(seg.off for seg in unit.segs)
        last = max(seg.off + seg.taps**2 * seg.cin * seg.cout // LANES for seg in unit.segs)
        wanted = (self.quarter * self.share < last) & ((self.quarter + 1) * self.share > first)

        @pl.when(wanted)
        def _():
            self.back_kernel(m, unit, dz)

    def dz_planes(self, unit):
        r = self.refs
        mode = {"p1": "p", "s2": "dz2", "s1": "wide" if self.k == 3 else "s1"}[unit.kind]
        return Planes(
            mode,
            unit.tiles,
            unit.planes,
            self.masks,
            self.rows,
            r.dC,
            r.dE,
            r.dR,
        )

    def table_grads(self, m, seg, totals):
        gg = self.refs.gg
        slot = seg.slot
        for which, found in ((0, totals[1]), (1, totals[0])):
            if seg.cout > LANES:
                for tile in range(2):
                    gg[m, which, slot : slot + 1, tile * LANES : (tile + 1) * LANES] = found[tile]
            else:
                row = jnp.broadcast_to(found[0], (8, LANES))
                if seg.cout < LANES:
                    row = self.keep(row, seg.cout, [0])
                gg[m, which, slot : slot + 1, 0:LANES] = row[0:1]

    def wide_rows(self, ref, at, tiles, plane, count):
        pieces = [
            ref[pl.ds(at(0, tile, plane), count)].reshape(count * self.rows, LANES)
            for tile in range(tiles)
        ]
        return pieces[0] if tiles == 1 else jnp.concatenate(pieces, axis=1)

    def back_data(self, m, unit, dz):
        r = self.refs
        kind, tiles = unit.kind, unit.tiles
        target = getattr(r, "T" + unit.name)
        lanes = tiles * LANES
        rows = self.rows

        def kernel_rows(d, first, count):
            return target[m * unit.depth + d, first : first + count, 0:lanes]

        def product(left, right):
            return lax.dot_general(left, right, ACROSS, preferred_element_type=jnp.float32)

        def put(ref, tile, planes, first, count, value, step=1, add=False):
            block = value.reshape(count, rows, LANES)
            for q in range(count):
                at = tile * planes + first + q * step
                ref[at] = ref[at] + block[q] if add else block[q]

        planes = unit.planes
        if kind == "s1":
            goal = r.gu if unit.name == "b" else r.gin
            add = unit.name == "a"
            if self.k == 3:
                pairs = [(dz.right, 0), (dz.main, 256), (dz.edge, 512)]
            else:
                pairs = [(dz.main, 0), (dz.edge, 256)]
            chunk = min(planes, 4)

            def body(step):
                first = step * chunk
                total = None
                for d in range(3):
                    for ref, at in pairs:
                        left = self.wide_rows(ref, dz.at, 2, first + 1 - d, chunk)
                        piece = product(left, kernel_rows(d, at, 256))
                        total = piece if total is None else total + piece
                for tile in range(2):
                    put(
                        goal,
                        tile,
                        planes,
                        first,
                        chunk,
                        total[:, tile * LANES : (tile + 1) * LANES],
                        add=add,
                    )

            planes_loop(planes // chunk, body)
            return
        if kind == "p1":
            left = self.wide_rows(dz.main, dz.at, tiles, 0, planes)
            total = product(left, kernel_rows(0, 0, 256))
            for tile in range(2):
                put(
                    r.gt,
                    tile,
                    planes,
                    0,
                    planes,
                    total[:, tile * LANES : (tile + 1) * LANES],
                    add=True,
                )
            return
        goal = self.grads[unit.source]
        add = unit.source == "t"
        lanes_in = unit.lanes_in
        count_in = unit.planes_in
        for parity, terms in ((0, [(1, 0)]), (1, [(2, 0), (0, 1)])):
            total, side = None, None
            for d, offset in terms:
                left = self.wide_rows(dz.main, dz.at, tiles, offset, planes)
                piece = product(left, kernel_rows(d, 0, lanes_in))
                total = piece if total is None else total + piece
                left = self.wide_rows(dz.edge, dz.at, tiles, offset, planes)
                piece = product(left, kernel_rows(d, lanes_in, LANES))
                side = piece if side is None else side + piece
            for tile in range(lanes_in // LANES):
                value = total[:, tile * LANES : (tile + 1) * LANES]
                if tile == lanes_in // LANES - 1:
                    value = value + side
                put(goal, tile, count_in, parity, planes, value, step=2, add=add)

    def back_kernel(self, m, unit, dz):
        r = self.refs
        G, rep, wgv = r.work, r.rep, r.wgv
        tiles, planes = unit.tiles, unit.planes
        source = self.maps[unit.source]
        right = self.wide_rows(dz.main, dz.at, tiles, 0, planes)

        def gather(d):
            at = 0
            for part in self.parts(unit, source):
                pieces = self.rows_of(unit, part, m, d, 0, planes)
                left = pieces[0] if len(pieces) == 1 else jnp.concatenate(pieces, axis=1)
                count = left.shape[1]
                result = lax.dot_general(left, right, ALONG, preferred_element_type=jnp.float32)
                for tile in range(tiles):
                    row = pl.multiple_of((d * tiles + tile) * unit.rows + at, 8)
                    G[pl.ds(row, count)] = result[:, tile * LANES : (tile + 1) * LANES]
                at += count

        planes_loop(unit.depth, gather)
        for seg in unit.segs:
            self.fold_kernel(m, unit, seg)

    def fold_kernel(self, m, unit, seg):
        r = self.refs
        G, rep, wgv = r.work, r.rep, r.wgv
        cin, cout, tiles = seg.cin, seg.cout, unit.tiles
        width = 3 if seg.taps == 3 else 1
        found = links(self.k, unit, seg)
        off = seg.off

        def fold(d):
            for column in range(width):
                tap = d * width + column
                totals = []
                for tile in range(seg.tiles):
                    total = None
                    for row, which, wanted in found:
                        if which != column:
                            continue
                        at = pl.multiple_of((d * tiles + seg.tile + tile) * unit.rows + row, 8)
                        piece = G[pl.ds(at, cin)]
                        if cout <= LANES:
                            local = self.local_blocks(seg, tile, wanted)
                            if not local:
                                continue
                            piece = self.keep(piece, cout, local)
                        total = piece if total is None else total + piece
                    totals.append(total)
                if cout > LANES:
                    for tile in range(2):
                        wgv[pl.ds(off + tap * (2 * cin) + tile, cin, stride=2)] = totals[tile]
                    continue
                total = None
                for piece in totals:
                    if piece is not None:
                        total = piece if total is None else total + piece
                if cout == LANES:
                    wgv[pl.ds(pl.multiple_of(off + tap * cin, 8), cin)] = total
                else:
                    rep[pl.ds(pl.multiple_of(tap * cin, cin), cin)] = self.spread(total, cout)

        planes_loop(unit.depth, fold)
        if cout < LANES:
            ratio = LANES // cout
            count = width * width * cin // ratio
            total = None
            for part in range(ratio):
                piece = self.keep(rep[pl.ds(part, count, stride=ratio)], cout, [part])
                total = piece if total is None else total + piece
            wgv[off : off + count] = total

    def backward(self, m):
        e = MODULES + m
        self.send_back(m)
        for name in ("g", "f", "e", "d", "u"):
            if name in self.units:
                for seg in self.units[name].segs:
                    if seg.dest >= 0:
                        self.arrived(e, seg.dest).wait_recv()
                self.back_unit(m, self.units[name])
        for other in self.others():
            self.message(e, other).wait_send()
        self.back_unit(m, self.units["b"])
        self.back_unit(m, self.units["a"])


STATS = 20
TURNS = 2
PIECE = 288
NAMES = list(
    dict(x=0, cot=0, w=0, gains=0, shifts=0, kinds=0, out=0, grad=0, wg=0, gain=0, shift=0)
)


def one_hot(goal, lane, deep):
    pieces = [
        jnp.where(goal == lane + first, 1.0, 0.0).astype(jnp.bfloat16)
        for first in range(0, deep, LANES)
    ]
    return jnp.concatenate(pieces, axis=1)


class Cells:
    def __init__(self, core, shape, small, large):
        self.core = core
        row = lax.broadcasted_iota(jnp.int32, shape, 0)
        self.wide = self.pick(LW // 8, SW // 8)
        tall = self.pick(LH // 8, SH // 8)
        self.crop = self.pick((row * 43691) >> 21, (row * 43691) >> 19)
        inner = row - self.crop * (self.wide * tall)
        self.along = self.pick((inner * 43691) >> 18, (inner * 43691) >> 17)
        self.across = inner - self.along * self.wide
        self.valid = self.crop < self.pick(large, small)
        self.last = tall - 1

    def pick(self, large, small):
        return jnp.where(self.core == 0, large, small)


def fill_masks(refs, rows, core, small, large):
    cells = Cells(core, (rows, LANES), small, large)
    valid = cells.valid
    six = cells.wide == 6
    up, down = valid & (cells.along > 0), valid & (cells.along < cells.last)
    tables = (
        valid,
        valid & (cells.across > 0),
        valid & (cells.across < cells.wide - 1),
        up & six,
        up & jnp.logical_not(six),
        down & six,
        down & jnp.logical_not(six),
    )
    for at, table in enumerate(tables):
        refs.masks[at] = jnp.where(table, 1.0, 0.0)


class Gather:
    def __init__(self, refs, core, count):
        self.refs, self.core, self.count = refs, core, count
        self.z = lax.axis_index("crops") // 2
        self.last = count // 2 - 1

    def hop(self, t, source, right):
        r = self.refs
        at = source * 2 + self.core
        gath = r.gathc if t else r.gathx
        to = self.z + 1 if right else self.z - 1
        return pltpu.make_async_remote_copy(
            src_ref=gath.at[at],
            dst_ref=gath.at[at],
            send_sem=r.hsem.at[(t * (self.last + 1) + source) * 3 + (0 if right else 1)],
            recv_sem=r.gsem.at[t * self.count + at],
            device_id=dict(crops=to * 2 + self.core),
            device_id_type=pl.DeviceIdType.MESH,
        )

    def across(self, t, source, core, rows):
        r = self.refs
        at = source * 2 + core
        gath = r.gathc if t else r.gathx
        return pltpu.make_async_remote_copy(
            src_ref=gath.at[at, pl.ds(0, rows)],
            dst_ref=gath.at[at, pl.ds(0, rows)],
            send_sem=r.hsem.at[(t * (self.last + 1) + source) * 3 + 2],
            recv_sem=r.gsem.at[t * self.count + at],
            device_id=dict(crops=self.z * 2 + 1 - self.core),
            device_id_type=pl.DeviceIdType.MESH,
        )

    def each_core(self, action):
        for core, rows in ((0, SH * SW * C0 // LANES), (1, ROWS)):

            @pl.when(self.core == core)
            def _():
                action(core, rows)

    def send(self, t, source, rightward, leftward):
        if rightward:

            @pl.when(self.z < self.last)
            def _():
                self.hop(t, source, True).start()

        if leftward:

            @pl.when(self.z > 0)
            def _():
                self.hop(t, source, False).start()

        self.each_core(lambda core, rows: self.across(t, source, core, rows).start())

    def step(self, t, s):
        r = self.refs
        if s == 0:
            at = self.z * 2 + self.core
            if t:
                r.gathc[at] = r.cot[...]
            else:
                r.gathx[at] = r.x[...]
            self.send(t, self.z, True, True)
            return

        @pl.when(self.z >= s)
        def _():
            self.hop(t, self.z - s, True).wait_recv()
            self.send(t, self.z - s, True, False)

        @pl.when(self.z + s <= self.last)
        def _():
            self.hop(t, self.z + s, True).wait_recv()
            self.send(t, self.z + s, False, True)

    def collect(self, t):
        for source in range(self.last + 1):
            for core, rows in ((0, ROWS), (1, SH * SW * C0 // LANES)):

                @pl.when(self.core == core)
                def _():
                    self.across(t, source, 1 - core, rows).wait_recv()

    def finish(self, t):
        def sent(source, rightward, leftward):
            if rightward:

                @pl.when(self.z < self.last)
                def _():
                    self.hop(t, source, True).wait_send()

            if leftward:

                @pl.when(self.z > 0)
                def _():
                    self.hop(t, source, False).wait_send()

            self.each_core(lambda core, rows: self.across(t, source, core, rows).wait_send())

        sent(self.z, True, True)
        for s in range(1, self.last + 1):

            @pl.when(self.z >= s)
            def _():
                sent(self.z - s, True, False)

            @pl.when(self.z + s <= self.last)
            def _():
                sent(self.z + s, False, True)


def scratch_table(rows, weight_rows, count):
    def half(many):
        return pltpu.VMEM((many, rows, LANES), jnp.bfloat16)

    def full(many):
        return pltpu.VMEM((many, rows, LANES), jnp.float32)

    def expanded(depth, deep, wide):
        return pltpu.VMEM((MODULES * depth, deep, wide), jnp.bfloat16)

    _, span, _ = pair_rows(weight_rows, count)
    return dict(
        masks=full(MASKS),
        hC=half(2 * 20),
        hE=half(2 * 20),
        hR=half(2 * 6),
        uC=half(2 * 20),
        uE=half(2 * 20),
        uR=half(2 * 6),
        tC=half(2 * 18),
        tE=half(2 * 9),
        c1C=half(2 * 5),
        c1E=half(2 * 5),
        c2C=half(2 * 5),
        c2E=half(2 * 5),
        c3C=half(2 * 3),
        c3E=half(2 * 3),
        dC=half(20),
        dE=half(20),
        dR=half(6),
        outs=half(16),
        hf=full(2 * 16),
        s=full(2 * 16),
        za=full(2 * 16),
        zb=full(2 * 16),
        zd=full(2 * 16),
        zu=full(2 * 8),
        ze=full(2 * 4),
        zf=full(2 * 2),
        zg=full(2 * 2),
        gt=full(16),
        gu=full(16),
        gin=full(16),
        gc1=full(4),
        gc2=full(4),
        gc3=full(2),
        dyb=full(16),
        sb=half(16),
        rb=half(4 * 16),
        st=pltpu.VMEM((MODULES * STATS, 8, LANES), jnp.float32),
        Ta=expanded(3, 768, 256),
        Tb=expanded(3, 768, 256),
        Td=expanded(3, 384, 512),
        Tu=expanded(1, 256, 768),
        Te=expanded(3, 256, 256),
        Tf=expanded(3, 256, 128),
        Tg=expanded(3, 256, 256),
        raw=pltpu.VMEM((2, PIECE, MODULES, LANES), jnp.bfloat16),
        work=pltpu.VMEM((9216, LANES), jnp.float32),
        rep=pltpu.VMEM((640, LANES), jnp.float32),
        wgv=pltpu.VMEM((weight_rows, LANES), jnp.float32),
        wq=pltpu.VMEM((MODULES, 2 * weight_rows // count, LANES), jnp.float32),
        wr=pltpu.VMEM((MODULES, span, LANES), jnp.float32),
        gathx=pltpu.VMEM((count, ROWS, LANES), jnp.bfloat16),
        gathc=pltpu.VMEM((count, ROWS, LANES), jnp.bfloat16),
        hot=pltpu.VMEM((2, 384, 768), jnp.bfloat16),
        blocks=pltpu.VMEM((2, ROWS, LANES), jnp.bfloat16),
        slopes=pltpu.VMEM((2, ROWS, LANES), jnp.float32),
        blockr=pltpu.VMEM((ROWS, LANES), jnp.bfloat16),
        sloper=pltpu.VMEM((ROWS, LANES), jnp.float32),
        gg=pltpu.VMEM((MODULES, 2, SLOTS, 256), jnp.float32),
        ggr=pltpu.VMEM((MODULES, 2, SLOTS, 256), jnp.float32),
        wsem=pltpu.SemaphoreType.DMA((2,)),
        ssem=pltpu.SemaphoreType.DMA((16,)),
        rsem=pltpu.SemaphoreType.DMA((16,)),
        hsem=pltpu.SemaphoreType.DMA((3 * count,)),
        gsem=pltpu.SemaphoreType.DMA((2 * count,)),
        psem=pltpu.SemaphoreType.DMA((5,)),
        qsem=pltpu.SemaphoreType.DMA((5,)),
        osem=pltpu.SemaphoreType.DMA((1,)),
    )


def pair_rows(weight_rows, count):
    share = weight_rows // count
    low = share // 8 * 8
    return share, 2 * share - low, low


def greet(core, count):
    barrier = pltpu.get_barrier_semaphore()
    me, shard = lax.axis_index("branch"), lax.axis_index("crops")
    z = shard // 2

    def signal(**where):
        pl.semaphore_signal(barrier, inc=1, device_id=where, device_id_type=pl.DeviceIdType.MESH)

    for step in range(1, 4):
        signal(branch=lax.rem(me + step, 4))
    signal(crops=shard + 1 - 2 * core)

    @pl.when(z > 0)
    def _():
        signal(crops=shard - 2)

    @pl.when(z < count // 2 - 1)
    def _():
        signal(crops=shard + 2)

    ends = (z == 0).astype(jnp.int32) + (z == count // 2 - 1).astype(jnp.int32)
    pl.semaphore_wait(barrier, 6 - ends)


def whole_kernel(names, rows, large, small, *args):
    refs = SimpleNamespace(**dict(zip(names, args)))
    count = large + small
    me, shard = lax.axis_index("branch"), lax.axis_index("crops")
    core = shard % 2
    weight_rows = refs.wgv.shape[0]
    share, span, low = pair_rows(weight_rows, count)
    quarter = pl.multiple_of(shard // 2 * (2 * share), 8)

    class Lazy:
        def __getitem__(self, index):
            return refs.masks[index]

    def across(source, goal, index):
        return pltpu.make_async_remote_copy(
            src_ref=source,
            dst_ref=goal,
            send_sem=refs.psem.at[index],
            recv_sem=refs.qsem.at[index],
            device_id=dict(crops=shard + 1 - 2 * core),
            device_id_type=pl.DeviceIdType.MESH,
        )

    def kernel_pair(m):
        at = pl.multiple_of(low * (1 - core), 8)
        return across(refs.wq.at[m, pl.ds(at, span)], refs.wr.at[m], m)

    outputs_pair = across(refs.blocks.at[1], refs.blockr, 2)
    gradient_pair = across(refs.slopes.at[1], refs.sloper, 3)
    table_pair = across(refs.gg, refs.ggr, 4)
    gather = Gather(refs, core, count)

    def every(action):
        for k in range(4):

            @pl.when(me == k)
            def _():
                action(Branch(k, rows, large, small, 2 * share, refs, Lazy(), core))

    def begin(branch):
        branch.fetch(0, 0).start()

    def prepare(branch):
        found = branch.segments()
        stops = {0: 1, min(2, len(found) - 2): 2, len(found) - 1: 3}
        for index, (unit, seg) in enumerate(found):
            branch.widen(index)
            for m in range(MODULES):
                branch.expand_one(m, unit, seg)
            if index in stops:
                gather.step(0, stops[index])

    def main(branch):
        branch.unpack(0, branch.take_feature)
        branch.maps["h"].close(0)
        gather.step(1, 0)

        def ahead(m, carry):
            branch.forward(m, gather)
            return carry

        def back(step, carry):
            m = MODULES - 1 - step
            branch.backward(m)
            refs.wq[m] = refs.wgv[pl.ds(quarter, 2 * share)]
            kernel_pair(m).start()
            return carry

        lax.fori_loop(0, MODULES, ahead, 0)
        branch.pack_outputs()
        outputs_pair.start()
        lax.fori_loop(0, MODULES, back, 0)
        branch.pack_gradient()
        gradient_pair.start()
        table_pair.start()

    every(begin)
    greet(core, count)
    gather.step(0, 0)
    fill_masks(refs, rows, core, small, large)
    refs.wgv[pl.ds(quarter, 2 * share)] = jnp.zeros((2 * share, LANES), jnp.float32)
    refs.gg[...] = jnp.zeros(refs.gg.shape, jnp.float32)
    every(prepare)
    gather.collect(0)
    every(main)

    for step in range(MODULES):
        m = MODULES - 1 - step
        kernel_pair(m).wait()
        mine = refs.wq[m, pl.ds(pl.multiple_of(low * core, 8), span)]
        refs.work[pl.ds(m, span, stride=MODULES)] = mine + refs.wr[m]
    skip = pl.multiple_of(core * (MODULES * (share - low)), 8)
    leave = pltpu.make_async_copy(
        refs.work.at[pl.ds(skip, MODULES * share)], refs.wg, refs.osem.at[0]
    )
    leave.start()
    outputs_pair.wait()
    gradient_pair.wait()
    table_pair.wait()
    own = refs.kinds[shard] != core
    refs.out[...] = jnp.where(own, refs.blocks[0].astype(jnp.float32), refs.blockr[...].astype(jnp.float32)).astype(jnp.bfloat16)
    refs.grad[...] = jnp.where(own, refs.slopes[0], refs.sloper[...])
    width = 256 // count
    for which, goal in ((0, refs.gain), (1, refs.shift)):
        for m in range(MODULES):
            total = refs.gg[m, which] + refs.ggr[m, which]
            found = None
            for at in range(count):
                piece = jnp.where(shard == at, total[:, at * width : (at + 1) * width], 0.0)
                found = piece if found is None else found + piece
            goal[m] = found
    gather.finish(0)
    gather.finish(1)
    leave.wait()


def whole_call(rows, large, small, x, cot, w, gains, shifts, kinds):
    count = large + small
    weight_rows = w.shape[0]
    table = scratch_table(rows, weight_rows, count)
    vmem = pl.BlockSpec(memory_space=pltpu.VMEM)
    hbm = pl.BlockSpec(memory_space=pl.ANY)
    smem = pl.BlockSpec(memory_space=pltpu.SMEM)
    tables = jax.ShapeDtypeStruct((MODULES, SLOTS, 256 // count), jnp.float32)
    return pl.pallas_call(
        partial(whole_kernel, NAMES + list(table), rows, large, small),
        out_shape=(
            jax.ShapeDtypeStruct((ROWS, LANES), jnp.bfloat16),
            jax.ShapeDtypeStruct((ROWS, LANES), jnp.float32),
            jax.ShapeDtypeStruct((MODULES * weight_rows // count, LANES), jnp.float32),
            tables,
            tables,
        ),
        in_specs=[vmem, vmem, hbm, vmem, vmem, smem],
        out_specs=(vmem, vmem, hbm, vmem, vmem),
        scratch_shapes=list(table.values()),
        compiler_params=pltpu.CompilerParams(
            collective_id=0, has_side_effects=True, vmem_limit_bytes=62 * 1024 * 1024
        ),
    )(x, cot, w, gains, shifts, kinds)


def leave_kernel(*args):
    sources, goals, sems = args[:5], args[5:10], args[10]
    copies = [
        pltpu.make_async_copy(source, goal, sems.at[at])
        for at, (source, goal) in enumerate(zip(sources, goals))
    ]
    for copy in copies:
        copy.start()
    for copy in copies:
        copy.wait()


def leave_call(arrays):
    hbm = pl.BlockSpec(memory_space=pl.ANY)
    return pl.pallas_call(
        leave_kernel,
        out_shape=tuple(jax.ShapeDtypeStruct(array.shape, array.dtype) for array in arrays),
        in_specs=[hbm] * 5,
        out_specs=(hbm,) * 5,
        scratch_shapes=[pltpu.SemaphoreType.DMA((5,))],
    )(*arrays)


def on_device_grouped(features, weights, gains, shifts, cotangent, size_group):
    count = lax.axis_size("crops")
    large = count // 4
    weight_rows = weights.shape[2] // LANES
    results = whole_call(
        group_rows(count),
        large,
        count - large,
        features[0],
        cotangent[0],
        weights[0].reshape(MODULES, weight_rows, LANES).transpose(1, 0, 2),
        gains[0],
        shifts[0],
        size_group,
    )
    out, grad, weight_grad, gain, shift = leave_call(results)
    share = weight_rows // count
    weight_grad = weight_grad.reshape(share, MODULES, LANES).transpose(1, 0, 2)
    weight_grad = with_layout_constraint(weight_grad, Layout((1, 0, 2)))
    return (
        out[None],
        grad[None],
        weight_grad.reshape(1, MODULES, share * LANES),
        gain[None],
        shift[None],
    )


def group_rows(count):
    large = count // 4
    rows = max(large * (LH // 8) * (LW // 8), (count - large) * (SH // 8) * (SW // 8))
    return -(-rows // 16) * 16


def fits(count):
    return count % 8 == 0 and group_rows(count) <= 96


def solution(mesh):
    placed = (
        P("branch", "crops", None),
        P("branch", None, None),
        P("branch", None, None, None),
        P("branch", None, None, None),
        P("branch", "crops", None),
        P(),
    )
    return jax.shard_map(
        on_device_grouped if fits(mesh.shape["crops"]) else on_device,
        mesh=mesh,
        in_specs=placed,
        out_specs=(
            P("branch", "crops", None),
            P("branch", "crops", None),
            P("branch", None, "crops"),
            P("branch", None, None, "crops"),
            P("branch", None, None, "crops"),
        ),
        check_vma=False,
    )
```

```python
from functools import partial
from types import SimpleNamespace
import math

import jax
import jax.numpy as jnp
import numpy as np
from jax import lax
from jax.experimental import pallas as pl
from jax.experimental.layout import Layout, with_layout_constraint
from jax.experimental.pallas import tpu as pltpu
from jax.sharding import PartitionSpec as P

C0 = 32
BLOCKS = 1
MODULES = 2
CROPS_DEV = 1
SH = 32
SW = 24
LH = 64
LW = 48
ROWS = 768
MSG_ROWS = 384


EPS = 1e-05


def as_sent(x):

    def short(part):
        return part.astype(jnp.bfloat16) if part.dtype == jnp.float32 else part

    return jax.tree.map(short, x)


def sender_plan(branch_index, top_channels, blocks):
    channels = top_channels << branch_index
    operations = []
    for block_index in range(blocks):
        operations.append(
            SimpleNamespace(
                phase=2 * block_index,
                source=("h", block_index),
                level=branch_index,
                cin=channels,
                cout=channels,
                stride=1,
                taps=3,
                act="silu",
                output=("u", block_index),
                skip=None,
                dest=-1,
            )
        )
        operations.append(
            SimpleNamespace(
                phase=2 * block_index + 1,
                source=("u", block_index),
                level=branch_index,
                cin=channels,
                cout=channels,
                stride=1,
                taps=3,
                act="res",
                output=("h", block_index + 1),
                skip=("h", block_index),
                dest=-1,
            )
        )
    top_name = ("h", blocks)
    for target in range(branch_index):
        operations.append(
            SimpleNamespace(
                phase=2 * blocks,
                source=top_name,
                level=branch_index,
                cin=channels,
                cout=top_channels << target,
                stride=1,
                taps=1,
                act="none",
                output=None,
                skip=None,
                dest=target,
            )
        )
    for target in range(branch_index + 1, 4):
        for depth_step in range(1, target - branch_index + 1):
            is_last = depth_step == target - branch_index
            operations.append(
                SimpleNamespace(
                    phase=2 * blocks + depth_step - 1,
                    source=top_name if depth_step == 1 else ("chain", target, depth_step - 1),
                    level=branch_index + depth_step,
                    cin=channels,
                    cout=top_channels << target if is_last else channels,
                    stride=2,
                    taps=3,
                    act="none" if is_last else "silu",
                    output=None if is_last else ("chain", target, depth_step),
                    skip=None,
                    dest=target if is_last else -1,
                )
            )
    for position, operation in enumerate(operations):
        operation.slot = position
        operation.size = (
            operation.taps * operation.taps * operation.cin * operation.cout
        )
        if operation.taps == 1:
            operation.kshape = (operation.cin, operation.cout)
        else:
            operation.kshape = (3, 3, operation.cin, operation.cout)
    return operations


def phase_lengths(top_channels, blocks):
    phase_count = 2 * blocks + 3
    lengths = [0] * phase_count
    for branch_index in range(4):
        per_phase = [0] * phase_count
        for operation in sender_plan(branch_index, top_channels, blocks):
            per_phase[operation.phase] += operation.size
        lengths = [max(current, candidate) for current, candidate in zip(lengths, per_phase)]
    return lengths


def weighted_plan(branch_index, top_channels, blocks):
    lengths = phase_lengths(top_channels, blocks)
    starts = [sum(lengths[:phase_index]) for phase_index in range(len(lengths))]
    running = [0] * len(lengths)
    operations = sender_plan(branch_index, top_channels, blocks)
    for operation in operations:
        phase_index = operation.phase
        operation.inner = running[phase_index]
        operation.offset = starts[phase_index] + running[phase_index]
        operation.position = sum(
            (1 for earlier in operations[: operation.slot] if earlier.phase == phase_index)
        )
        running[phase_index] += operation.size
    return operations


def phase_operations(branch_index, phase_index):
    return [
        operation
        for operation in weighted_plan(branch_index, C0, BLOCKS)
        if operation.phase == phase_index
    ]


def input_names(operations):
    source_names = []
    for operation in operations:
        if operation.source not in source_names:
            source_names.append(operation.source)
    return source_names


def silu_slope(value):
    sigmoid = jax.nn.sigmoid(value)
    return sigmoid * (1.0 + value * (1.0 - sigmoid))


def crop_cells(size_kind):
    return (LH, LW) if size_kind else (SH, SW)


def map_dims(size_kind, level, channels):
    height, breadth = crop_cells(size_kind)
    return (CROPS_DEV, height >> level, breadth >> level, channels)


def source_dims(branch_index, size_kind, map_name):
    level = branch_index + map_name[2] if map_name[0] == "chain" else branch_index
    return map_dims(size_kind, level, C0 << branch_index)


def preact_dims(size_kind, operation):
    return map_dims(size_kind, operation.level, operation.cout)


def to_canvas(arrays, value_type):
    if not arrays:
        return jnp.zeros((ROWS, 128), value_type)
    flattened = jnp.concatenate([array.reshape(-1).astype(value_type) for array in arrays])
    return jnp.pad(flattened, (0, ROWS * 128 - flattened.shape[0])).reshape(ROWS, 128)


def from_canvas(canvas, dims_list):
    flattened = canvas.reshape(-1)
    pieces = []
    offset = 0
    for dims_entry in dims_list:
        count_here = math.prod(dims_entry)
        pieces.append(flattened[offset : offset + count_here].reshape(dims_entry))
        offset += count_here
    return pieces


def to_slot(array):
    flattened = array.reshape(-1)
    return jnp.pad(flattened, (0, MSG_ROWS * 128 - flattened.shape[0])).reshape(MSG_ROWS, 128)


def from_slot(slot_rows, dims_entry):
    return slot_rows.reshape(-1)[: math.prod(dims_entry)].reshape(dims_entry)


def upsample(message, factor):
    crop_count, height, breadth, channels = message.shape
    widened = jnp.broadcast_to(
        message[:, :, None, :, None, :], (crop_count, height, factor, breadth, factor, channels)
    )
    return widened.reshape(crop_count, height * factor, breadth * factor, channels)


def block_pool(array, factor):
    crop_count, height, breadth, channels = array.shape
    return array.reshape(
        crop_count, height // factor, factor, breadth // factor, factor, channels
    ).sum(axis=(2, 4))


def kernel_piece(module_weights, operation):
    start = operation.offset
    return module_weights[start : start + operation.size].reshape(operation.kshape)


def conv_forward(operation, source, kernel):
    if operation.taps == 1:
        return jnp.einsum("nhwc,cd->nhwd", source, kernel, preferred_element_type=jnp.float32)
    stride = operation.stride
    return lax.conv_general_dilated(
        source,
        kernel,
        (stride, stride),
        ((1, 1), (1, 1)),
        dimension_numbers=("NHWC", "HWIO", "NHWC"),
        preferred_element_type=jnp.float32,
    )


def conv_backward(operation, source, kernel, upstream):
    if operation.taps == 1:
        source_grad = jnp.einsum(
            "nhwd,cd->nhwc", upstream, kernel, preferred_element_type=jnp.float32
        )
        kernel_grad = jnp.einsum(
            "nhwc,nhwd->cd", source, upstream, preferred_element_type=jnp.float32
        )
        return (source_grad, kernel_grad)
    stride = operation.stride
    flipped = jnp.transpose(kernel[::-1, ::-1], (0, 1, 3, 2))
    high_pad = 2 if stride == 2 else 1
    source_grad = lax.conv_general_dilated(
        upstream,
        flipped,
        (1, 1),
        ((1, high_pad), (1, high_pad)),
        lhs_dilation=(stride, stride),
        dimension_numbers=("NHWC", "HWIO", "NHWC"),
        preferred_element_type=jnp.float32,
    )
    kernel_grad = lax.conv_general_dilated(
        source,
        upstream,
        (1, 1),
        ((1, 2 - stride), (1, 2 - stride)),
        rhs_dilation=(stride, stride),
        dimension_numbers=("CHWN", "IHWO", "NHWC"),
        preferred_element_type=jnp.float32,
    )
    return (source_grad, jnp.transpose(kernel_grad, (1, 2, 0, 3)))


def cell_total(counts, size_kind, level):
    height, breadth = crop_cells(size_kind)
    return counts[size_kind] * float(CROPS_DEV * (height >> level) * (breadth >> level))


def norm_terms(totals, counts, size_kind, operation):
    cells_here = cell_total(counts, size_kind, operation.level)
    channels = operation.cout
    position = operation.position
    average = totals[size_kind, 0, position, :channels] / cells_here
    variance = totals[size_kind, 1, position, :channels] / cells_here - average * average
    return (average, lax.rsqrt(variance + EPS))


def forward_conv(branch_index, size_kind, phase_index, source_canvas, module_weights):
    operations = phase_operations(branch_index, phase_index)
    source_names = input_names(operations)
    pieces = from_canvas(
        source_canvas, [source_dims(branch_index, size_kind, map_name) for map_name in source_names]
    )
    sources = {
        map_name: piece.astype(jnp.bfloat16) for map_name, piece in zip(source_names, pieces)
    }
    preacts = []
    totals = jnp.zeros((2, 2, 3, 8 * C0), jnp.float32)
    for operation in operations:
        preact = conv_forward(
            operation, sources[operation.source], kernel_piece(module_weights, operation)
        )
        preacts.append(preact)
        channels = operation.cout
        position = operation.position
        totals = totals.at[size_kind, 0, position, :channels].set(jnp.sum(preact, axis=(0, 1, 2)))
        totals = totals.at[size_kind, 1, position, :channels].set(
            jnp.sum(preact * preact, axis=(0, 1, 2))
        )
    return (to_canvas(preacts, jnp.float32), totals)


def forward_norm(
    branch_index,
    size_kind,
    phase_index,
    preact_canvas,
    totals,
    counts,
    module_gains,
    module_shifts,
    skip_canvas,
    message_buffer,
):
    operations = phase_operations(branch_index, phase_index)
    preacts = from_canvas(
        preact_canvas, [preact_dims(size_kind, operation) for operation in operations]
    )
    skip_map = from_canvas(skip_canvas, [map_dims(size_kind, branch_index, C0 << branch_index)])[0]
    produced = []
    for operation, preact in zip(operations, preacts):
        average, inverse_std = norm_terms(totals, counts, size_kind, operation)
        norm_slot = operation.slot
        channels = operation.cout
        normed = (preact - average) * inverse_std * module_gains[
            norm_slot, :channels
        ] + module_shifts[norm_slot, :channels]
        if operation.act == "silu":
            produced.append(jax.nn.silu(normed))
        elif operation.act == "res":
            produced.append(jax.nn.silu(normed + skip_map))
        else:
            message_buffer = message_buffer.at[operation.dest].set(
                to_slot(normed.astype(jnp.bfloat16))
            )
    return (to_canvas(produced, jnp.float32), message_buffer)


def receive_forward(branch_index, size_kind, top_canvas, received):
    channels = C0 << branch_index
    summed = from_canvas(top_canvas, [map_dims(size_kind, branch_index, channels)])[0]
    for sender in range(4):
        if sender < branch_index:
            summed = summed + from_slot(
                received[sender], map_dims(size_kind, branch_index, channels)
            ).astype(jnp.float32)
        elif sender > branch_index:
            coarse = from_slot(received[sender], map_dims(size_kind, sender, channels))
            summed = summed + upsample(coarse, 2 ** (sender - branch_index)).astype(jnp.float32)
    return (to_canvas([jax.nn.silu(summed)], jnp.float32), to_canvas([summed], jnp.float32))


def receive_backward(branch_index, size_kind, grad_canvas, summed_canvas):
    dims_here = map_dims(size_kind, branch_index, C0 << branch_index)
    upstream = from_canvas(grad_canvas, [dims_here])[0]
    summed = from_canvas(summed_canvas, [dims_here])[0]
    summed_grad = upstream * silu_slope(summed)
    buffer = jnp.zeros((4, MSG_ROWS, 128), jnp.bfloat16)
    for sender in range(4):
        if sender < branch_index:
            buffer = buffer.at[sender].set(to_slot(summed_grad.astype(jnp.bfloat16)))
        elif sender > branch_index:
            pooled = block_pool(summed_grad, 2 ** (sender - branch_index))
            buffer = buffer.at[sender].set(to_slot(pooled.astype(jnp.bfloat16)))
    return (to_canvas([summed_grad], jnp.float32), buffer)


def backward_stats(
    branch_index,
    size_kind,
    phase_index,
    dout_canvas,
    message_grads,
    preact_canvas,
    totals,
    counts,
    module_gains,
    module_shifts,
    skip_canvas,
):
    operations = phase_operations(branch_index, phase_index)
    preacts = from_canvas(
        preact_canvas, [preact_dims(size_kind, operation) for operation in operations]
    )
    producing = [operation for operation in operations if operation.act != "none"]
    output_grads = from_canvas(
        dout_canvas, [preact_dims(size_kind, operation) for operation in producing]
    )
    grads_by_name = {
        operation.output: piece for operation, piece in zip(producing, output_grads)
    }
    skip_map = from_canvas(skip_canvas, [map_dims(size_kind, branch_index, C0 << branch_index)])[0]
    upstreams = []
    skip_grads = []
    sums_local = jnp.zeros((2, 2, 3, 8 * C0), jnp.float32)
    for operation, preact in zip(operations, preacts):
        average, inverse_std = norm_terms(totals, counts, size_kind, operation)
        norm_slot = operation.slot
        channels = operation.cout
        centered = (preact - average) * inverse_std
        normed = centered * module_gains[norm_slot, :channels] + module_shifts[norm_slot, :channels]
        if operation.act == "silu":
            upstream = grads_by_name[operation.output] * silu_slope(normed)
        elif operation.act == "res":
            upstream = grads_by_name[operation.output] * silu_slope(normed + skip_map)
            skip_grads.append(upstream)
        else:
            upstream = from_slot(
                message_grads[operation.dest], preact_dims(size_kind, operation)
            ).astype(jnp.float32)
        upstreams.append(upstream)
        position = operation.position
        sums_local = sums_local.at[size_kind, 0, position, :channels].set(
            jnp.sum(upstream, axis=(0, 1, 2))
        )
        sums_local = sums_local.at[size_kind, 1, position, :channels].set(
            jnp.sum(upstream * centered, axis=(0, 1, 2))
        )
    return (to_canvas(upstreams, jnp.float32), sums_local, to_canvas(skip_grads, jnp.float32))


def backward_apply(
    branch_index,
    size_kind,
    phase_index,
    upstream_canvas,
    preact_canvas,
    totals,
    grad_totals,
    counts,
    source_canvas,
    module_weights,
    module_gains,
):
    operations = phase_operations(branch_index, phase_index)
    preacts = from_canvas(
        preact_canvas, [preact_dims(size_kind, operation) for operation in operations]
    )
    upstreams = from_canvas(
        upstream_canvas, [preact_dims(size_kind, operation) for operation in operations]
    )
    source_names = input_names(operations)
    source_list = [source_dims(branch_index, size_kind, map_name) for map_name in source_names]
    pieces = from_canvas(source_canvas, source_list)
    sources = {
        map_name: piece.astype(jnp.bfloat16) for map_name, piece in zip(source_names, pieces)
    }
    source_grads = {
        map_name: jnp.zeros(dims_entry, jnp.float32)
        for map_name, dims_entry in zip(source_names, source_list)
    }
    kernel_grads = []
    slot_count = module_gains.shape[0]
    gain_part = jnp.zeros((slot_count, 8 * C0), jnp.float32)
    shift_part = jnp.zeros((slot_count, 8 * C0), jnp.float32)
    for operation, preact, upstream in zip(operations, preacts, upstreams):
        average, inverse_std = norm_terms(totals, counts, size_kind, operation)
        cells_here = cell_total(counts, size_kind, operation.level)
        norm_slot = operation.slot
        channels = operation.cout
        position = operation.position
        centered = (preact - average) * inverse_std
        mean_upstream = grad_totals[size_kind, 0, position, :channels] / cells_here
        mean_cross = grad_totals[size_kind, 1, position, :channels] / cells_here
        preact_grad = (
            module_gains[norm_slot, :channels]
            * inverse_std
            * (upstream - mean_upstream - centered * mean_cross)
        )
        source_grad, kernel_grad = conv_backward(
            operation,
            sources[operation.source],
            kernel_piece(module_weights, operation),
            preact_grad.astype(jnp.bfloat16),
        )
        source_grads[operation.source] = source_grads[operation.source] + source_grad
        kernel_grads.append(kernel_grad.reshape(-1))
        gain_part = gain_part.at[norm_slot, :channels].set(
            grad_totals[0, 1, position, :channels] + grad_totals[1, 1, position, :channels]
        )
        shift_part = shift_part.at[norm_slot, :channels].set(
            grad_totals[0, 0, position, :channels] + grad_totals[1, 0, position, :channels]
        )
    phase_length = phase_lengths(C0, BLOCKS)[phase_index]
    if kernel_grads:
        joined = jnp.concatenate(kernel_grads)
        weight_part = jnp.pad(joined, (0, phase_length - joined.shape[0]))
    else:
        weight_part = jnp.zeros((phase_length,), jnp.float32)
    return (
        to_canvas([source_grads[map_name] for map_name in source_names], jnp.float32),
        weight_part,
        gain_part,
        shift_part,
    )


def on_device(features, weights, gains, shifts, cotangent, size_group):
    crop_shard = lax.axis_index("crops")
    shard_count = lax.axis_size("crops")
    crop_kind = size_group[crop_shard]
    large_count = jnp.sum(size_group).astype(jnp.float32)
    counts = jnp.stack([shard_count - large_count, large_count])
    case_index = lax.axis_index("branch") * 2 + crop_kind
    phase_total = 2 * BLOCKS + 3
    zero_canvas = jnp.zeros((ROWS, 128), jnp.float32)
    empty_buffer = jnp.zeros((4, MSG_ROWS, 128), jnp.bfloat16)

    def run_phase(function, statics, operands):
        branches_list = [
            partial(function, branch_index, size_kind, *statics)
            for branch_index in range(4)
            for size_kind in range(2)
        ]
        return lax.switch(case_index, branches_list, *operands)

    def statistics(local_totals):
        return lax.psum(local_totals, "crops")

    def module_forward(module, start_canvas, kept):
        module_weights = weights[0, module]
        module_gains = gains[0, module]
        module_shifts = shifts[0, module]
        record = SimpleNamespace(sources=[], preacts=[], totals=[])
        h_canvas = start_canvas
        u_canvas = zero_canvas
        chain_canvas = zero_canvas
        buffer = empty_buffer
        for phase_index in range(phase_total):
            if phase_index < 2 * BLOCKS:
                source = h_canvas if phase_index % 2 == 0 else u_canvas
            elif phase_index == 2 * BLOCKS:
                source = h_canvas
            else:
                source = chain_canvas
            preact, local_totals = run_phase(forward_conv, (phase_index,), (source, module_weights))
            global_totals = kept.totals[phase_index] if kept else statistics(local_totals)
            produced, buffer = run_phase(
                forward_norm,
                (phase_index,),
                (preact, global_totals, counts, module_gains, module_shifts, h_canvas, buffer),
            )
            record.sources.append(source)
            record.preacts.append(preact)
            record.totals.append(global_totals)
            if phase_index < 2 * BLOCKS:
                if phase_index % 2 == 0:
                    u_canvas = produced
                else:
                    h_canvas = produced
            else:
                chain_canvas = produced
        received = (
            kept.received
            if kept
            else jax.tree.map(
                lambda part, own: part.astype(own.dtype),
                lax.all_to_all(as_sent(buffer), "branch", split_axis=0, concat_axis=0, tiled=True),
                buffer,
            )
        )
        result, summed = run_phase(receive_forward, (), (h_canvas, received))
        record.summed = summed
        record.received = received
        return (result, record)

    checkpoints = [features[0].astype(jnp.float32)]
    first_records = []
    for module in range(MODULES):
        result, record = module_forward(module, checkpoints[-1], None)
        checkpoints.append(result)
        first_records.append(record)
    outputs = checkpoints[-1].astype(jnp.bfloat16)
    grad_canvas = cotangent[0].astype(jnp.float32)
    module_grads = [None] * MODULES
    gain_grads = [None] * MODULES
    shift_grads = [None] * MODULES
    for module in reversed(range(MODULES)):
        kept = None
        unused_result, record = module_forward(module, checkpoints[module], kept)
        module_module_weights = weights[0, module]
        module_module_gains = gains[0, module]
        module_module_shifts = shifts[0, module]
        summed_grad, back_buffer = run_phase(receive_backward, (), (grad_canvas, record.summed))
        message_grads = jax.tree.map(
            lambda part, own: part.astype(own.dtype),
            lax.all_to_all(as_sent(back_buffer), "branch", split_axis=0, concat_axis=0, tiled=True),
            back_buffer,
        )
        top_grad = summed_grad
        chain_grad = zero_canvas
        u_grad = zero_canvas
        pending_skip = zero_canvas
        weight_parts = [None] * phase_total
        gain_total = jnp.zeros(gains.shape[2:], jnp.float32)
        shift_total = jnp.zeros(gains.shape[2:], jnp.float32)
        for module_phase_index in reversed(range(phase_total)):
            if module_phase_index >= 2 * BLOCKS:
                output_grad = chain_grad
                skip_canvas = zero_canvas
            elif module_phase_index % 2 == 1:
                output_grad = top_grad
                skip_canvas = record.sources[module_phase_index - 1]
            else:
                output_grad = u_grad
                skip_canvas = zero_canvas
            module_preact = record.preacts[module_phase_index]
            totals = record.totals[module_phase_index]
            upstream, module_local_totals, skip_grad = run_phase(
                backward_stats,
                (module_phase_index,),
                (
                    output_grad,
                    message_grads,
                    module_preact,
                    totals,
                    counts,
                    module_module_gains,
                    module_module_shifts,
                    skip_canvas,
                ),
            )
            grad_totals = lax.psum(module_local_totals, "crops")
            source_grad, weight_parts[module_phase_index], gain_part, shift_part = run_phase(
                backward_apply,
                (module_phase_index,),
                (
                    upstream,
                    module_preact,
                    totals,
                    grad_totals,
                    counts,
                    record.sources[module_phase_index],
                    module_module_weights,
                    module_module_gains,
                ),
            )
            gain_total = gain_total + gain_part
            shift_total = shift_total + shift_part
            if module_phase_index > 2 * BLOCKS:
                chain_grad = source_grad
            elif module_phase_index == 2 * BLOCKS:
                top_grad = top_grad + source_grad
            elif module_phase_index % 2 == 1:
                u_grad = source_grad
                pending_skip = skip_grad
            else:
                top_grad = source_grad + pending_skip
        joined = jnp.concatenate(weight_parts)
        weight_grad = jnp.pad(joined, (0, weights.shape[2] - joined.shape[0]))
        grad_canvas, weight_grad, gain_grads[module], shift_grads[module] = (
            top_grad,
            weight_grad,
            gain_total,
            shift_total,
        )
        module_grads[module] = weight_grad
    weight_out = lax.psum_scatter(jnp.stack(module_grads), "crops", scatter_dimension=1, tiled=True)
    share = gains.shape[3] // shard_count
    gain_out = lax.dynamic_slice_in_dim(jnp.stack(gain_grads), crop_shard * share, share, axis=2)
    shift_out = lax.dynamic_slice_in_dim(jnp.stack(shift_grads), crop_shard * share, share, axis=2)
    return (outputs[None], grad_canvas[None], weight_out[None], gain_out[None], shift_out[None])


LANES = 128
SLOTS = 8
MASKS = 7
DOWN = (((1,), (0,)), ((), ()))
ACROSS = (((1,), (1,)), ((), ()))
ALONG = (((0,), (0,)), ((), ()))


def unit_table(k):
    operations = weighted_plan(k, C0, BLOCKS)
    planes = 8 >> k
    channels = C0 << k
    units = {}
    stat = 0

    def add(name, kind, source, lanes_in, planes_in, planes_out, members):
        nonlocal stat
        segs = []
        tile = 0
        for operation, lanes, chain in members:
            cout = operation.cout
            level = operation.level if operation.taps == 3 else operation.dest
            segs.append(
                SimpleNamespace(
                    slot=operation.slot,
                    off=operation.offset // LANES,
                    cin=operation.cin,
                    cout=cout,
                    taps=operation.taps,
                    tile=tile,
                    tiles=lanes // LANES,
                    blocks=max(1, (8 >> level)),
                    dest=operation.dest,
                    act=operation.act,
                    chain=chain,
                    up=k - operation.dest if operation.taps == 1 else 0,
                )
            )
            tile += lanes // LANES
        rows = {"s1": 768 if k == 3 else 512, "s2": lanes_in + LANES, "p1": 256}[kind]
        units[name] = SimpleNamespace(
            name=name,
            kind=kind,
            source=source,
            lanes_in=lanes_in,
            blocks_in=planes_in,
            planes_in=planes_in,
            planes=planes_out,
            segs=segs,
            tiles=tile,
            rows=rows,
            stat=stat,
            depth=1 if kind == "p1" else 3,
        )
        stat += tile

    add("a", "s1", "h", 256, planes, planes, [(operations[0], 256, None)])
    add("b", "s1", "u", 256, planes, planes, [(operations[1], 256, None)])
    ups = [operation for operation in operations if operation.taps == 1]
    if ups:
        add("u", "p1", "t", 256, planes, planes, [(operation, 256, None) for operation in ups])
    firsts, chains = [], {}
    for target in range(k + 1, 4):
        steps = [
            operation
            for operation in operations
            if operation.taps == 3 and operation.stride == 2
        ]
        start = sum(i - k for i in range(k + 1, target))
        chains[target] = steps[start : start + target - k]
        if target == k + 1:
            firsts.append((chains[target][0], 256, None))
        else:
            firsts.append((chains[target][0], LANES, "c1" if target == k + 2 else "c2"))
    if firsts:
        add("d", "s2", "t", 256, planes, planes // 2, firsts)
    if k <= 1:
        add("e", "s2", "c1", LANES, planes // 2, planes // 4, [(chains[k + 2][1], 256, None)])
    if k == 0:
        add("f", "s2", "c2", LANES, planes // 2, planes // 4, [(chains[3][1], LANES, "c3")])
        add("g", "s2", "c3", LANES, planes // 4, planes // 8, [(chains[3][2], 256, None)])
    return units


def links(k, unit, seg):
    cin = seg.cin
    count_in, count_out = unit.blocks_in, seg.blocks
    found = []
    if unit.kind == "p1":
        for plane in range(count_in):
            wide = 1 << seg.up
            found.append((plane * cin, 0, set(range(plane * wide, plane * wide + wide))))
        return found
    if unit.kind == "s1" and k == 3:
        return [(256 * tap, tap, {0}) for tap in range(3)]
    stride = 1 if unit.kind == "s1" else 2
    for plane in range(count_in):
        for tap in range(3):
            at = plane - tap + 1
            if at % stride == 0 and 0 <= at // stride < count_out:
                found.append((plane * cin, tap, {at // stride}))
    if stride == 1:
        found.append((256, 2, {count_out - 1}))
        found.append((512 - cin, 0, {0}))
    else:
        lanes_in = unit.lanes_in
        found.append((lanes_in + (count_in - 1) * cin - (lanes_in - LANES), 0, {0}))
    return found


def message_slot(k, other):
    return sum(2 * (8 >> max(k, before)) for before in range(other) if before != k)


def log2(value):
    return value.bit_length() - 1


def sigmoid_of(value):
    return 0.5 * jnp.tanh(0.5 * value) + 0.5


def silu_of(value):
    return value * sigmoid_of(value)


def slope_of(value):
    sigmoid = sigmoid_of(value)
    return sigmoid * (1.0 + value * (1.0 - sigmoid))


def planes_loop(count, body, turns=1):
    def step(index, carry):
        for turn in range(turns):
            body(index * turns + turn)
        return carry

    turns = min(turns, count)
    if count == turns:
        step(0, 0)
    else:
        lax.fori_loop(0, count // turns, step, 0)


def planes_sum(count, body, initial, turns=1):
    def step(index, carry):
        for turn in range(turns):
            carry = body(index * turns + turn, carry)
        return carry

    turns = min(turns, count)
    if count == turns:
        return step(0, initial)
    return lax.fori_loop(0, count // turns, step, initial)


def partial_sum(value):
    rows = value.shape[0]
    return jnp.sum(value.reshape(rows // 8, 8, value.shape[1]), axis=0)


class Planes:
    def __init__(self, mode, tiles, planes, masks, rows, main, edge=None, right=None):
        self.mode, self.tiles, self.planes = mode, tiles, planes
        self.masks, self.rows = masks, rows
        self.main, self.edge, self.right = main, edge, right
        self.base = 1 if mode in ("s1", "wide", "s2") else 0
        extra = {"s1": 2, "wide": 2, "s2": 1, "dz2": 1, "p": 0}[mode]
        self.span = planes + extra
        self.unit = tiles * self.span

    def at(self, m, tile, plane):
        return m * self.unit + tile * self.span + plane + self.base

    def edge_at(self, m, tile, plane):
        if self.mode == "s2":
            return m * self.span + plane + self.base
        return self.at(m, tile, plane)

    def from_left(self, value):
        return pltpu.roll(value, 1, 0) * self.masks[1]

    def from_right(self, value):
        return pltpu.roll(value, self.rows - 1, 0) * self.masks[2]

    def store(self, m, tile, plane, value):
        where = self.at(m, tile, plane)
        self.main[where] = value.astype(jnp.bfloat16)
        if self.mode == "s1":
            side = self.from_right(value) if tile == 0 else self.from_left(value)
            self.edge[where] = side.astype(jnp.bfloat16)
        elif self.mode == "wide":
            self.edge[where] = self.from_left(value).astype(jnp.bfloat16)
            self.right[where] = self.from_right(value).astype(jnp.bfloat16)
        elif self.mode == "s2":
            if tile == self.tiles - 1:
                self.edge[self.edge_at(m, tile, plane)] = self.from_left(value).astype(jnp.bfloat16)
        elif self.mode == "dz2":
            self.edge[where] = self.from_right(value).astype(jnp.bfloat16)

    def close(self, m):
        rows = self.rows
        for tile in range(self.tiles):
            if self.mode in ("s1", "wide", "s2"):
                last = self.main[self.at(m, tile, self.planes - 1)].astype(jnp.float32)
                above = pltpu.roll(last, 6, 0) * self.masks[3] + pltpu.roll(last, 3, 0) * self.masks[4]
                self.store(m, tile, -1, above)
            if self.mode in ("s1", "wide", "dz2"):
                first = self.main[self.at(m, tile, 0)].astype(jnp.float32)
                below = (
                    pltpu.roll(first, rows - 6, 0) * self.masks[5]
                    + pltpu.roll(first, rows - 3, 0) * self.masks[6]
                )
                self.store(m, tile, self.planes, below)


class Branch:
    def __init__(self, k, rows, large, small, share, refs, masks, core):
        self.k, self.rows, self.refs, self.masks = k, rows, refs, masks
        self.units = unit_table(k)
        self.planes = 8 >> k
        self.core = core
        self.large, self.small, self.count = large, small, large + small
        self.cells = (small * (SH // 8) * (SW // 8), large * (LH // 8) * (LW // 8))
        self.quarter = lax.axis_index("crops") // 2
        self.share = share
        r = refs
        make = partial(Planes, masks=masks, rows=rows)
        one = "wide" if k == 3 else "s1"
        self.maps = dict(
            h=make(one, 2, self.planes, main=r.hC, edge=r.hE, right=r.hR),
            u=make(one, 2, self.planes, main=r.uC, edge=r.uE, right=r.uR),
            t=make("p" if k == 3 else "s2", 2, self.planes, main=r.tC, edge=r.tE),
        )
        if k <= 1:
            self.maps["c1"] = make("s2", 1, self.planes // 2, main=r.c1C, edge=r.c1E)
        if k == 0:
            self.maps["c2"] = make("s2", 1, 4, main=r.c2C, edge=r.c2E)
            self.maps["c3"] = make("s2", 1, 2, main=r.c3C, edge=r.c3E)
        self.grads = dict(t=r.gt, u=r.gu, c1=r.gc1, c2=r.gc2, c3=r.gc3)

    def lane_block(self, shape, cout):
        lanes = lax.broadcasted_iota(jnp.int32, shape, 1)
        return lanes >> log2(cout)

    def keep(self, value, cout, which):
        count = LANES // cout
        if len(which) == count:
            return value
        block = self.lane_block(value.shape, cout)
        mask = block == which[0]
        for entry in which[1:]:
            mask = mask | (block == entry)
        return jnp.where(mask, value, 0.0)

    def spread(self, value, cout):
        shift = LANES // 2
        while shift >= cout:
            value = value + pltpu.roll(value, shift, 1)
            shift //= 2
        return value

    def local_blocks(self, seg, tile, wanted):
        count = LANES // seg.cout
        return [q for q in range(count) if (tile * count + q) % seg.blocks in wanted]


    def segments(self):
        return [(unit, seg) for unit in self.units.values() for seg in unit.segs]

    def pieces(self, index):
        def split(seg):
            count = seg.taps**2 * seg.cin * seg.cout // LANES
            return max(1, count // PIECE), min(count, PIECE)

        found = [split(seg) for _, seg in self.segments()]
        return *found[index], sum(many for many, _ in found[:index])

    def fetch(self, index, piece):
        r = self.refs
        _, seg = self.segments()[index]
        _, count, before = self.pieces(index)
        slot = (before + piece) % 2
        return pltpu.make_async_copy(
            r.w.at[pl.ds(2 * seg.off + piece * (2 * count), 2 * count)],
            r.raw.at[slot, pl.ds(0, 2 * count)],
            r.wsem.at[slot],
        )

    def widen(self, index):
        r = self.refs
        many, count, before = self.pieces(index)
        chunk = 2 * math.gcd(count, 144)

        def convert(piece):
            def body(step):
                at = pl.multiple_of(step * chunk, 16)
                value = r.raw[(before + piece) % 2, pl.ds(at, chunk)].astype(jnp.float32)
                r.work[pl.ds(pl.multiple_of(piece * (2 * count) + at, 16), chunk)] = value

            planes_loop(2 * count // chunk, body)

        def step(piece):
            self.fetch(index, piece).wait()
            self.fetch(index, piece + 1).start()
            convert(piece)

        if many > 1:
            planes_loop(many - 1, step)
        self.fetch(index, many - 1).wait()
        if index + 1 < len(self.segments()):
            self.fetch(index + 1, 0).start()
        convert(many - 1)

    def expand_one(self, m, unit, seg):
        r = self.refs
        target = getattr(r, "T" + unit.name)
        depth, cin, cout = unit.depth, seg.cin, seg.cout
        taps = seg.taps**2
        count = taps * cin * cout // LANES
        wf, rep = r.work, r.rep
        if cout < LANES:
            ratio = LANES // cout
            flat = wf[pl.ds(m, count, stride=2)]
            for part in range(ratio):
                rep[pl.ds(part, count, stride=ratio)] = self.spread(
                    self.keep(flat, cout, [part]), cout
                )

        def tap_rows(tap, tile):
            if cout < LANES:
                return rep[pl.ds(pl.multiple_of(tap * cin, cin), cin)]
            if cout == LANES:
                return wf[pl.ds(m + tap * (2 * cin), cin, stride=2)]
            return wf[pl.ds(m + tap * (4 * cin) + 2 * tile, cin, stride=4)]

        by_row = {}
        for row, tap, wanted in links(self.k, unit, seg):
            by_row.setdefault(row, []).append((tap, wanted))

        def fill(d):
            width = 3 if taps == 9 else 1
            for tile in range(seg.tiles):
                column = (seg.tile + tile) * LANES
                for row in range(0, unit.rows, cin):
                    total = None
                    for tap, wanted in by_row.get(row, []):
                        if cout <= LANES:
                            local = self.local_blocks(seg, tile, wanted)
                            if not local:
                                continue
                            piece = self.keep(tap_rows(d * width + tap, 0), cout, local)
                        else:
                            piece = tap_rows(d * width + tap, tile)
                        total = piece if total is None else total + piece
                    if total is None:
                        total = jnp.zeros((cin, LANES), jnp.float32)
                    target[m * depth + d, row : row + cin, column : column + LANES] = total.astype(
                        jnp.bfloat16
                    )

        planes_loop(depth, fill)


    def parts(self, unit, source):
        if unit.kind == "p1":
            return [(source.main, range(2), source.at)]
        if source.mode == "wide":
            return [
                (source.edge, range(2), source.at),
                (source.main, range(2), source.at),
                (source.right, range(2), source.at),
            ]
        if unit.kind == "s1":
            return [(source.main, range(2), source.at), (source.edge, range(2), source.at)]
        last = source.tiles - 1
        return [
            (source.main, range(source.tiles), source.at),
            (source.edge, [last], source.edge_at),
        ]

    def rows_of(self, unit, part, m, d, first, count):
        ref, tiles, at = part
        pieces = []
        for tile in tiles:
            if unit.kind == "s2":
                rows = [ref[at(m, tile, 2 * (first + q) + d - 1)] for q in range(count)]
                pieces.append(rows[0] if count == 1 else jnp.concatenate(rows, axis=0))
            else:
                shift = d - 1 if unit.kind == "s1" else 0
                pieces.append(
                    ref[pl.ds(at(m, tile, first + shift), count)].reshape(count * self.rows, LANES)
                )
        return pieces

    def conv(self, m, unit):
        r = self.refs
        source = self.maps[unit.source]
        target = getattr(r, "T" + unit.name)
        z = getattr(r, "z" + unit.name)
        planes, tiles, depth = unit.planes, unit.tiles, unit.depth
        chunk = min(planes, 4 if tiles <= 2 else 2)
        lanes = tiles * LANES

        def body(step, sums):
            first = step * chunk
            pieces = []
            for d in range(depth):
                for part in self.parts(unit, source):
                    pieces += self.rows_of(unit, part, m, d, first, chunk)
            left = jnp.concatenate(pieces, axis=1)
            right = target[pl.ds(m * depth, depth), 0 : unit.rows, 0:lanes]
            right = right.reshape(depth * unit.rows, lanes)
            result = lax.dot_general(left, right, DOWN, preferred_element_type=jnp.float32)
            for tile in range(tiles):
                block = result[:, tile * LANES : (tile + 1) * LANES]
                z[pl.ds(m * tiles * planes + tile * planes + first, chunk)] = block.reshape(
                    chunk, self.rows, LANES
                )
            return (sums[0] + partial_sum(result), sums[1] + partial_sum(result * result))

        zero = jnp.zeros((8, lanes), jnp.float32)
        sums = planes_sum(planes // chunk, body, (zero, zero))
        for seg in unit.segs:
            scale = self.per_cell(unit, seg)
            totals = self.fold(seg, sums)
            self.norm_rows(m, unit, seg, totals, scale)

    def per_cell(self, unit, seg):
        blocks = seg.tiles * LANES // seg.cout
        small, large = self.cells
        count = unit.planes * blocks
        return jnp.where(self.core == 0, 1.0 / (large * count), 1.0 / (small * count)).astype(
            jnp.float32
        )

    def fold(self, seg, sums):
        first = seg.tile
        found = []
        for value in sums:
            tiles = [
                value[:, (first + t) * LANES : (first + t + 1) * LANES] for t in range(seg.tiles)
            ]
            if seg.cout <= LANES:
                total = tiles[0]
                for tile in tiles[1:]:
                    total = total + tile
                total = jnp.sum(self.spread(total, seg.cout), axis=0, keepdims=True)
                found.append([total] * seg.tiles)
            else:
                found.append([jnp.sum(tile, axis=0, keepdims=True) for tile in tiles])
        return found

    def table_row(self, ref, m, seg, tile):
        slot = seg.slot
        if seg.cout > LANES:
            return ref[m, slot : slot + 1, tile * LANES : (tile + 1) * LANES]
        row = jnp.broadcast_to(ref[m, slot : slot + 1, 0:LANES], (8, LANES))
        if seg.cout < LANES:
            row = self.spread(self.keep(row, seg.cout, [0]), seg.cout)
        return row[0:1]

    def norm_rows(self, m, unit, seg, totals, scale):
        st = self.refs.st
        for tile in range(seg.tiles):
            average = totals[0][tile] * scale
            variance = totals[1][tile] * scale - average * average
            inverse = lax.rsqrt(variance + EPS)
            gain = self.table_row(self.refs.gains, m, seg, tile)
            shift = self.table_row(self.refs.shifts, m, seg, tile)
            where = m * STATS + unit.stat + seg.tile + tile
            factor = gain * inverse
            st[where, 0:1] = average
            st[where, 1:2] = inverse
            st[where, 2:3] = factor
            st[where, 3:4] = shift - average * factor

    def normed(self, m, unit, tile, plane):
        st = self.refs.st
        z = getattr(self.refs, "z" + unit.name)
        where = m * STATS + unit.stat + tile
        value = z[m * unit.tiles * unit.planes + tile * unit.planes + plane]
        return value * st[where, 2:3] + st[where, 3:4]

    def apply_a(self, m):
        unit, u = self.units["a"], self.maps["u"]

        def body(plane):
            for tile in range(2):
                value = silu_of(self.normed(m, unit, tile, plane)) * self.masks[0]
                u.store(m, tile, plane, value)

        planes_loop(self.planes, body, TURNS)
        u.close(m)

    def apply_b(self, m):
        unit, top = self.units["b"], self.maps["t"]
        hf, s = self.refs.hf, self.refs.s

        def body(plane):
            for tile in range(2):
                where = m * 2 * self.planes + tile * self.planes + plane
                value = silu_of(self.normed(m, unit, tile, plane) + hf[where]) * self.masks[0]
                s[where] = value
                top.store(m, tile, plane, value)

        planes_loop(self.planes, body, TURNS)
        top.close(m)

    def apply_rest(self, m, unit):
        sb = self.refs.sb
        for seg in unit.segs:
            chain = self.maps[seg.chain] if seg.chain else None

            def body(plane):
                for tile in range(seg.tiles):
                    value = self.normed(m, unit, seg.tile + tile, plane)
                    if chain is not None:
                        chain.store(m, tile, plane, silu_of(value) * self.masks[0])
                    else:
                        at = message_slot(self.k, seg.dest) + tile * unit.planes + plane
                        sb[at] = value.astype(jnp.bfloat16)

            planes_loop(unit.planes, body, TURNS)
            if chain is not None:
                chain.close(m)
            else:
                self.message(m, seg.dest).start()

    def message(self, e, other):
        count = 2 * (8 >> max(self.k, other))
        r = self.refs
        return pltpu.make_async_remote_copy(
            src_ref=r.sb.at[pl.ds(message_slot(self.k, other), count)],
            dst_ref=r.rb.at[pl.ds(e * 16 + message_slot(other, self.k), count)],
            send_sem=r.ssem.at[e * 4 + other],
            recv_sem=r.rsem.at[e * 4 + self.k],
            device_id=dict(branch=other),
            device_id_type=pl.DeviceIdType.MESH,
        )

    def arrived(self, e, other):
        count = 2 * (8 >> max(self.k, other))
        r = self.refs
        at = message_slot(self.k, other)
        return pltpu.make_async_remote_copy(
            src_ref=r.sb.at[pl.ds(at, count)],
            dst_ref=r.rb.at[pl.ds(e * 16 + at, count)],
            send_sem=r.ssem.at[e * 4 + other],
            recv_sem=r.rsem.at[e * 4 + other],
            device_id=dict(branch=other),
            device_id_type=pl.DeviceIdType.MESH,
        )

    def others(self):
        return [other for other in range(4) if other != self.k]

    def settle(self, e):
        for other in self.others():
            self.message(e, other).wait_send()
        for other in self.others():
            self.arrived(e, other).wait_recv()

    def receive(self, m):
        r = self.refs
        s, rb, hf, out = r.s, r.rb, r.hf, r.outs
        h = self.maps["h"]

        def body(plane):
            for tile in range(2):
                where = m * 2 * self.planes + tile * self.planes + plane
                total = s[where]
                for other in self.others():
                    count = 8 >> max(self.k, other)
                    at = plane >> max(0, other - self.k)
                    slot = m * 16 + message_slot(self.k, other) + tile * count + at
                    total = total + rb[slot].astype(jnp.float32)
                s[where] = total
                value = silu_of(total) * self.masks[0]
                out[tile * self.planes + plane] = value.astype(jnp.bfloat16)

                @pl.when(m + 1 < MODULES)
                def _():
                    hf[2 * self.planes + tile * self.planes + plane] = value
                    h.store(1, tile, plane, value)

        planes_loop(self.planes, body, TURNS)

        @pl.when(m + 1 < MODULES)
        def _():
            h.close(1)

    def take_feature(self, tile, plane, value):
        self.refs.hf[tile * self.planes + plane] = value
        self.maps["h"].store(0, tile, plane, value)

    def take_cotangent(self, tile, plane, value):
        self.refs.gin[tile * self.planes + plane] = value

    def member(self, kind, order):
        kinds = self.refs.kinds
        found, before = jnp.int32(0), jnp.int32(0)
        for at in range(self.count):
            same = kinds[at] == kind
            found = jnp.where(same & (before == order), at, found)
            before = before + same.astype(jnp.int32)
        return found

    def order(self, device):
        kinds = self.refs.kinds
        kind = kinds[device]
        before = jnp.int32(0)
        for at in range(self.count):
            before = before + ((kinds[at] == kind) & (at < device)).astype(jnp.int32)
        return before

    def unpack(self, t, consume):
        r = self.refs
        work, rows, planes = r.work, self.rows, self.planes
        full = SH * SW * C0 // LANES
        gath = r.gathc if t else r.gathx

        @pl.when(self.core == 0)
        def _():
            for at in range(self.large):
                block = gath[self.member(1, at)]
                work[at * ROWS : (at + 1) * ROWS] = block.astype(jnp.float32)

        @pl.when(self.core == 1)
        def _():
            for at in range(self.small):
                block = gath[self.member(0, at), 0:full]
                work[at * full : (at + 1) * full] = block.astype(jnp.float32)
            work[self.small * full : self.large * ROWS] = jnp.zeros(
                (self.large * ROWS - self.small * full, LANES), jnp.float32
            )

        deep = self.large * ROWS // 2
        right = jnp.concatenate([work[pl.ds(j, deep, stride=2)] for j in range(2)], axis=1)
        right = right.astype(jnp.bfloat16)
        cells = Cells(self.core, (rows, LANES), self.small, self.large)
        base = cells.crop * cells.pick(ROWS // 2, full // 2)
        base = base + cells.along * (planes * cells.wide) + cells.across
        base = jnp.where(cells.valid, base, -(1 << 20))
        lane = lax.broadcasted_iota(jnp.int32, (rows, LANES), 1)
        chunk = min(planes, 4)

        def body(step):
            pieces = []
            for q in range(chunk):
                goal = base + (step * chunk + q) * cells.wide
                pieces.append(one_hot(goal, lane, deep))
            left = pieces[0] if chunk == 1 else jnp.concatenate(pieces, axis=0)
            result = lax.dot_general(left, right, DOWN, preferred_element_type=jnp.float32)
            for q in range(chunk):
                for tile in range(2):
                    value = result[q * rows : (q + 1) * rows, tile * LANES : (tile + 1) * LANES]
                    consume(tile, step * chunk + q, value)

        planes_loop(planes // chunk, body)

    def pack_size(self):
        return 48 * self.planes, -(-self.planes * self.rows // LANES) * LANES

    def plan_pack(self):
        r = self.refs
        high, deep = self.pack_size()
        planes = self.planes
        q = lax.broadcasted_iota(jnp.int32, (high, LANES), 0)
        lane = lax.broadcasted_iota(jnp.int32, (high, LANES), 1)
        wide, tall = jnp.where(self.core == 0, 6, 3), jnp.where(self.core == 0, 8, 4)
        cell = jnp.where(self.core == 0, (q * 43691) >> 18, (q * 43691) >> 17)
        across = q - cell * wide
        plane = cell & (planes - 1)
        along = cell >> log2(planes)
        base = plane * self.rows + along * wide + across
        base = jnp.where(along < tall, base, -(1 << 20))
        shard = lax.axis_index("crops")
        for at, device in enumerate((shard, shard + 1 - 2 * self.core)):
            goal = base + self.order(device) * (wide * tall)
            r.hot[at, 0:high, 0:deep] = one_hot(goal, lane, deep)

    def pack(self, units, put):
        high, deep = self.pack_size()
        right = jnp.concatenate([units(tile) for tile in range(2)], axis=1)
        short = deep - right.shape[0]
        parts = [right.astype(jnp.bfloat16)]
        if right.dtype == jnp.float32:
            parts.append((right - parts[0].astype(jnp.float32)).astype(jnp.bfloat16))
        if short:
            empty = jnp.zeros((short, 2 * LANES), jnp.bfloat16)
            parts = [jnp.concatenate([part, empty], axis=0) for part in parts]
        for at in range(2):
            total = None
            for part in parts:
                piece = lax.dot_general(
                    self.refs.hot[at, 0:high, 0:deep],
                    part,
                    DOWN,
                    preferred_element_type=jnp.float32,
                )
                total = piece if total is None else total + piece
            for tile in range(2):
                put(at, pl.ds(tile, high, stride=2), total[:, tile * LANES : (tile + 1) * LANES])

    def pack_outputs(self):
        r = self.refs
        high = 2 * self.pack_size()[0]

        def put(at, where, value):
            r.work[pl.ds(at * ROWS + where.start, where.size, stride=2)] = value

        def units(tile):
            block = r.outs[tile * self.planes : (tile + 1) * self.planes]
            return block.reshape(self.planes * self.rows, LANES)

        self.pack(units, put)
        for at in range(2):
            r.blocks[at, 0:high] = r.work[at * ROWS : at * ROWS + high].astype(jnp.bfloat16)
            if high < ROWS:
                r.blocks[at, high:ROWS] = jnp.zeros((ROWS - high, LANES), jnp.bfloat16)

    def pack_gradient(self):
        r = self.refs
        high = 2 * self.pack_size()[0]

        def put(at, where, value):
            r.slopes[at, where] = value

        def units(tile):
            block = r.gin[tile * self.planes : (tile + 1) * self.planes]
            return block.reshape(self.planes * self.rows, LANES)

        self.pack(units, put)
        if high < ROWS:
            for at in range(2):
                r.slopes[at, high:ROWS] = jnp.zeros((ROWS - high, LANES), jnp.float32)

    def forward(self, m, gather):
        steps = iter(range(1, 4))

        def also():
            step = next(steps, None)
            if step is not None:

                @pl.when(m == 0)
                def _():
                    gather.step(1, step)

        self.conv(m, self.units["a"])
        self.apply_a(m)
        also()
        self.conv(m, self.units["b"])
        self.apply_b(m)
        also()
        for name in ("d", "u", "e", "f", "g"):
            if name in self.units:
                self.conv(m, self.units[name])
                self.apply_rest(m, self.units[name])
                also()
        for _ in range(3):
            also()

        @pl.when(m == MODULES - 1)
        def _():
            gather.collect(1)
            self.unpack(1, self.take_cotangent)
            self.plan_pack()

        self.settle(m)
        self.receive(m)


    def send_back(self, m):
        r = self.refs
        s, gin, gt, sb = r.s, r.gin, r.gt, r.sb
        e = MODULES + m

        def body(plane):
            for tile in range(2):
                at = tile * self.planes + plane
                value = gin[at] * slope_of(s[m * 2 * self.planes + at])
                gt[at] = value
                for other in range(self.k):
                    sb[message_slot(self.k, other) + at] = value.astype(jnp.bfloat16)

        planes_loop(self.planes, body, TURNS)
        for other in reversed(self.others()):
            if other > self.k:
                count = 8 >> other
                wide = 1 << (other - self.k)

                def pool(plane):
                    for tile in range(2):
                        total = gt[tile * self.planes + plane * wide]
                        for step in range(1, wide):
                            total = total + gt[tile * self.planes + plane * wide + step]
                        slot = message_slot(self.k, other) + tile * count + plane
                        sb[slot] = total.astype(jnp.bfloat16)

                planes_loop(count, pool, TURNS)
            self.message(e, other).start()

    def back_unit(self, m, unit):
        r = self.refs
        st, dyb, z = r.st, r.dyb, getattr(r, "z" + unit.name)
        name, planes, tiles = unit.name, unit.planes, unit.tiles
        e = MODULES + m
        sums = {}

        def upstream(seg, tile, plane, normed):
            at = tile * planes + plane
            if name == "b":
                hf = r.hf[m * 2 * planes + at]
                value = r.gt[at] * slope_of(normed + hf)
                r.gin[at] = value
                return value
            if name == "a":
                return r.gu[at] * slope_of(normed)
            if seg.chain:
                return self.grads[seg.chain][at] * slope_of(normed)
            return r.rb[e * 16 + message_slot(self.k, seg.dest) + at].astype(jnp.float32)

        for seg in unit.segs:

            def body(plane, carry):
                result = []
                for tile in range(seg.tiles):
                    at = (seg.tile + tile) * planes + plane
                    where = m * STATS + unit.stat + seg.tile + tile
                    value = z[m * tiles * planes + at]
                    normed = value * st[where, 2:3] + st[where, 3:4]
                    dy = upstream(seg, tile, plane, normed)
                    dyb[at] = dy
                    zhat = (value - st[where, 0:1]) * st[where, 1:2]
                    result.append(carry[2 * tile] + partial_sum(dy))
                    result.append(carry[2 * tile + 1] + partial_sum(dy * zhat))
                return tuple(result)

            zero = jnp.zeros((8, LANES), jnp.float32)
            found = planes_sum(planes, body, (zero,) * (2 * seg.tiles), TURNS)
            pair = [
                jnp.concatenate([found[2 * tile + which] for tile in range(seg.tiles)], axis=1)
                for which in range(2)
            ]
            plain = SimpleNamespace(**vars(seg))
            plain.tile = 0
            totals = self.fold(plain, pair)
            self.table_grads(m, seg, totals)
            sums[seg.slot] = totals
        dz = self.dz_planes(unit)
        for seg in unit.segs:
            scale = self.per_cell(unit, seg)
            totals = sums[seg.slot]

            def apply(plane):
                for tile in range(seg.tiles):
                    at = (seg.tile + tile) * planes + plane
                    where = m * STATS + unit.stat + seg.tile + tile
                    zhat = (z[m * tiles * planes + at] - st[where, 0:1]) * st[where, 1:2]
                    inner = dyb[at] - totals[0][tile] * scale - zhat * (totals[1][tile] * scale)
                    dz.store(0, seg.tile + tile, plane, inner * st[where, 2:3] * self.masks[0])

            planes_loop(planes, apply, TURNS)
        dz.close(0)
        self.back_data(m, unit, dz)
        first = min(seg.off for seg in unit.segs)
        last = max(seg.off + seg.taps**2 * seg.cin * seg.cout // LANES for seg in unit.segs)
        wanted = (self.quarter * self.share < last) & ((self.quarter + 1) * self.share > first)

        @pl.when(wanted)
        def _():
            self.back_kernel(m, unit, dz)

    def dz_planes(self, unit):
        r = self.refs
        mode = {"p1": "p", "s2": "dz2", "s1": "wide" if self.k == 3 else "s1"}[unit.kind]
        return Planes(
            mode,
            unit.tiles,
            unit.planes,
            self.masks,
            self.rows,
            r.dC,
            r.dE,
            r.dR,
        )

    def table_grads(self, m, seg, totals):
        gg = self.refs.gg
        slot = seg.slot
        for which, found in ((0, totals[1]), (1, totals[0])):
            if seg.cout > LANES:
                for tile in range(2):
                    gg[m, which, slot : slot + 1, tile * LANES : (tile + 1) * LANES] = found[tile]
            else:
                row = jnp.broadcast_to(found[0], (8, LANES))
                if seg.cout < LANES:
                    row = self.keep(row, seg.cout, [0])
                gg[m, which, slot : slot + 1, 0:LANES] = row[0:1]

    def wide_rows(self, ref, at, tiles, plane, count):
        pieces = [
            ref[pl.ds(at(0, tile, plane), count)].reshape(count * self.rows, LANES)
            for tile in range(tiles)
        ]
        return pieces[0] if tiles == 1 else jnp.concatenate(pieces, axis=1)

    def back_data(self, m, unit, dz):
        r = self.refs
        kind, tiles = unit.kind, unit.tiles
        target = getattr(r, "T" + unit.name)
        lanes = tiles * LANES
        rows = self.rows

        def kernel_rows(d, first, count):
            return target[m * unit.depth + d, first : first + count, 0:lanes]

        def product(left, right):
            return lax.dot_general(left, right, ACROSS, preferred_element_type=jnp.float32)

        def put(ref, tile, planes, first, count, value, step=1, add=False):
            block = value.reshape(count, rows, LANES)
            for q in range(count):
                at = tile * planes + first + q * step
                ref[at] = ref[at] + block[q] if add else block[q]

        planes = unit.planes
        if kind == "s1":
            goal = r.gu if unit.name == "b" else r.gin
            add = unit.name == "a"
            if self.k == 3:
                pairs = [(dz.right, 0), (dz.main, 256), (dz.edge, 512)]
            else:
                pairs = [(dz.main, 0), (dz.edge, 256)]
            chunk = min(planes, 4)

            def body(step):
                first = step * chunk
                total = None
                for d in range(3):
                    for ref, at in pairs:
                        left = self.wide_rows(ref, dz.at, 2, first + 1 - d, chunk)
                        piece = product(left, kernel_rows(d, at, 256))
                        total = piece if total is None else total + piece
                for tile in range(2):
                    put(
                        goal,
                        tile,
                        planes,
                        first,
                        chunk,
                        total[:, tile * LANES : (tile + 1) * LANES],
                        add=add,
                    )

            planes_loop(planes // chunk, body)
            return
        if kind == "p1":
            left = self.wide_rows(dz.main, dz.at, tiles, 0, planes)
            total = product(left, kernel_rows(0, 0, 256))
            for tile in range(2):
                put(
                    r.gt,
                    tile,
                    planes,
                    0,
                    planes,
                    total[:, tile * LANES : (tile + 1) * LANES],
                    add=True,
                )
            return
        goal = self.grads[unit.source]
        add = unit.source == "t"
        lanes_in = unit.lanes_in
        count_in = unit.planes_in
        for parity, terms in ((0, [(1, 0)]), (1, [(2, 0), (0, 1)])):
            total, side = None, None
            for d, offset in terms:
                left = self.wide_rows(dz.main, dz.at, tiles, offset, planes)
                piece = product(left, kernel_rows(d, 0, lanes_in))
                total = piece if total is None else total + piece
                left = self.wide_rows(dz.edge, dz.at, tiles, offset, planes)
                piece = product(left, kernel_rows(d, lanes_in, LANES))
                side = piece if side is None else side + piece
            for tile in range(lanes_in // LANES):
                value = total[:, tile * LANES : (tile + 1) * LANES]
                if tile == lanes_in // LANES - 1:
                    value = value + side
                put(goal, tile, count_in, parity, planes, value, step=2, add=add)

    def back_kernel(self, m, unit, dz):
        r = self.refs
        G, rep, wgv = r.work, r.rep, r.wgv
        tiles, planes = unit.tiles, unit.planes
        source = self.maps[unit.source]
        right = self.wide_rows(dz.main, dz.at, tiles, 0, planes)

        def gather(d):
            at = 0
            for part in self.parts(unit, source):
                pieces = self.rows_of(unit, part, m, d, 0, planes)
                left = pieces[0] if len(pieces) == 1 else jnp.concatenate(pieces, axis=1)
                count = left.shape[1]
                result = lax.dot_general(left, right, ALONG, preferred_element_type=jnp.float32)
                for tile in range(tiles):
                    row = pl.multiple_of((d * tiles + tile) * unit.rows + at, 8)
                    G[pl.ds(row, count)] = result[:, tile * LANES : (tile + 1) * LANES]
                at += count

        planes_loop(unit.depth, gather)
        for seg in unit.segs:
            self.fold_kernel(m, unit, seg)

    def fold_kernel(self, m, unit, seg):
        r = self.refs
        G, rep, wgv = r.work, r.rep, r.wgv
        cin, cout, tiles = seg.cin, seg.cout, unit.tiles
        width = 3 if seg.taps == 3 else 1
        found = links(self.k, unit, seg)
        off = seg.off

        def fold(d):
            for column in range(width):
                tap = d * width + column
                totals = []
                for tile in range(seg.tiles):
                    total = None
                    for row, which, wanted in found:
                        if which != column:
                            continue
                        at = pl.multiple_of((d * tiles + seg.tile + tile) * unit.rows + row, 8)
                        piece = G[pl.ds(at, cin)]
                        if cout <= LANES:
                            local = self.local_blocks(seg, tile, wanted)
                            if not local:
                                continue
                            piece = self.keep(piece, cout, local)
                        total = piece if total is None else total + piece
                    totals.append(total)
                if cout > LANES:
                    for tile in range(2):
                        wgv[pl.ds(off + tap * (2 * cin) + tile, cin, stride=2)] = totals[tile]
                    continue
                total = None
                for piece in totals:
                    if piece is not None:
                        total = piece if total is None else total + piece
                if cout == LANES:
                    wgv[pl.ds(pl.multiple_of(off + tap * cin, 8), cin)] = total
                else:
                    rep[pl.ds(pl.multiple_of(tap * cin, cin), cin)] = self.spread(total, cout)

        planes_loop(unit.depth, fold)
        if cout < LANES:
            ratio = LANES // cout
            count = width * width * cin // ratio
            total = None
            for part in range(ratio):
                piece = self.keep(rep[pl.ds(part, count, stride=ratio)], cout, [part])
                total = piece if total is None else total + piece
            wgv[off : off + count] = total

    def backward(self, m):
        e = MODULES + m
        self.send_back(m)
        for name in ("g", "f", "e", "d", "u"):
            if name in self.units:
                for seg in self.units[name].segs:
                    if seg.dest >= 0:
                        self.arrived(e, seg.dest).wait_recv()
                self.back_unit(m, self.units[name])
        for other in self.others():
            self.message(e, other).wait_send()
        self.back_unit(m, self.units["b"])
        self.back_unit(m, self.units["a"])


STATS = 20
TURNS = 2
PIECE = 1152
NAMES = list(
    dict(x=0, cot=0, w=0, gains=0, shifts=0, kinds=0, out=0, grad=0, wg=0, gain=0, shift=0)
)


def one_hot(goal, lane, deep):
    pieces = [
        jnp.where(goal == lane + first, 1.0, 0.0).astype(jnp.bfloat16)
        for first in range(0, deep, LANES)
    ]
    return jnp.concatenate(pieces, axis=1)


class Cells:
    def __init__(self, core, shape, small, large):
        self.core = core
        row = lax.broadcasted_iota(jnp.int32, shape, 0)
        self.wide = self.pick(LW // 8, SW // 8)
        tall = self.pick(LH // 8, SH // 8)
        self.crop = self.pick((row * 43691) >> 21, (row * 43691) >> 19)
        inner = row - self.crop * (self.wide * tall)
        self.along = self.pick((inner * 43691) >> 18, (inner * 43691) >> 17)
        self.across = inner - self.along * self.wide
        self.valid = self.crop < self.pick(large, small)
        self.last = tall - 1

    def pick(self, large, small):
        return jnp.where(self.core == 0, large, small)


def fill_masks(refs, rows, core, small, large):
    cells = Cells(core, (rows, LANES), small, large)
    valid = cells.valid
    six = cells.wide == 6
    up, down = valid & (cells.along > 0), valid & (cells.along < cells.last)
    tables = (
        valid,
        valid & (cells.across > 0),
        valid & (cells.across < cells.wide - 1),
        up & six,
        up & jnp.logical_not(six),
        down & six,
        down & jnp.logical_not(six),
    )
    for at, table in enumerate(tables):
        refs.masks[at] = jnp.where(table, 1.0, 0.0)


class Gather:
    def __init__(self, refs, core, count):
        self.refs, self.core, self.count = refs, core, count
        self.z = lax.axis_index("crops") // 2
        self.last = count // 2 - 1

    def hop(self, t, source, right):
        r = self.refs
        at = source * 2 + self.core
        gath = r.gathc if t else r.gathx
        to = self.z + 1 if right else self.z - 1
        return pltpu.make_async_remote_copy(
            src_ref=gath.at[at],
            dst_ref=gath.at[at],
            send_sem=r.hsem.at[(t * (self.last + 1) + source) * 3 + (0 if right else 1)],
            recv_sem=r.gsem.at[t * self.count + at],
            device_id=dict(crops=to * 2 + self.core),
            device_id_type=pl.DeviceIdType.MESH,
        )

    def across(self, t, source, core, rows):
        r = self.refs
        at = source * 2 + core
        gath = r.gathc if t else r.gathx
        return pltpu.make_async_remote_copy(
            src_ref=gath.at[at, pl.ds(0, rows)],
            dst_ref=gath.at[at, pl.ds(0, rows)],
            send_sem=r.hsem.at[(t * (self.last + 1) + source) * 3 + 2],
            recv_sem=r.gsem.at[t * self.count + at],
            device_id=dict(crops=self.z * 2 + 1 - self.core),
            device_id_type=pl.DeviceIdType.MESH,
        )

    def each_core(self, action):
        for core, rows in ((0, SH * SW * C0 // LANES), (1, ROWS)):

            @pl.when(self.core == core)
            def _():
                action(core, rows)

    def send(self, t, source, rightward, leftward):
        if rightward:

            @pl.when(self.z < self.last)
            def _():
                self.hop(t, source, True).start()

        if leftward:

            @pl.when(self.z > 0)
            def _():
                self.hop(t, source, False).start()

        self.each_core(lambda core, rows: self.across(t, source, core, rows).start())

    def step(self, t, s):
        r = self.refs
        if s == 0:
            at = self.z * 2 + self.core
            if t:
                r.gathc[at] = r.cot[...]
            else:
                r.gathx[at] = r.x[...]
            self.send(t, self.z, True, True)
            return

        @pl.when(self.z >= s)
        def _():
            self.hop(t, self.z - s, True).wait_recv()
            self.send(t, self.z - s, True, False)

        @pl.when(self.z + s <= self.last)
        def _():
            self.hop(t, self.z + s, True).wait_recv()
            self.send(t, self.z + s, False, True)

    def collect(self, t):
        for source in range(self.last + 1):
            for core, rows in ((0, ROWS), (1, SH * SW * C0 // LANES)):

                @pl.when(self.core == core)
                def _():
                    self.across(t, source, 1 - core, rows).wait_recv()

    def finish(self, t):
        def sent(source, rightward, leftward):
            if rightward:

                @pl.when(self.z < self.last)
                def _():
                    self.hop(t, source, True).wait_send()

            if leftward:

                @pl.when(self.z > 0)
                def _():
                    self.hop(t, source, False).wait_send()

            self.each_core(lambda core, rows: self.across(t, source, core, rows).wait_send())

        sent(self.z, True, True)
        for s in range(1, self.last + 1):

            @pl.when(self.z >= s)
            def _():
                sent(self.z - s, True, False)

            @pl.when(self.z + s <= self.last)
            def _():
                sent(self.z + s, False, True)


def scratch_table(rows, weight_rows, count):
    def half(many):
        return pltpu.VMEM((many, rows, LANES), jnp.bfloat16)

    def full(many):
        return pltpu.VMEM((many, rows, LANES), jnp.float32)

    def expanded(depth, deep, wide):
        return pltpu.VMEM((MODULES * depth, deep, wide), jnp.bfloat16)

    _, span, _ = pair_rows(weight_rows, count)
    return dict(
        masks=full(MASKS),
        hC=half(2 * 20),
        hE=half(2 * 20),
        hR=half(2 * 6),
        uC=half(2 * 20),
        uE=half(2 * 20),
        uR=half(2 * 6),
        tC=half(2 * 18),
        tE=half(2 * 9),
        c1C=half(2 * 5),
        c1E=half(2 * 5),
        c2C=half(2 * 5),
        c2E=half(2 * 5),
        c3C=half(2 * 3),
        c3E=half(2 * 3),
        dC=half(20),
        dE=half(20),
        dR=half(6),
        outs=half(16),
        hf=full(2 * 16),
        s=full(2 * 16),
        za=full(2 * 16),
        zb=full(2 * 16),
        zd=full(2 * 16),
        zu=full(2 * 8),
        ze=full(2 * 4),
        zf=full(2 * 2),
        zg=full(2 * 2),
        gt=full(16),
        gu=full(16),
        gin=full(16),
        gc1=full(4),
        gc2=full(4),
        gc3=full(2),
        dyb=full(16),
        sb=half(16),
        rb=half(4 * 16),
        st=pltpu.VMEM((MODULES * STATS, 8, LANES), jnp.float32),
        Ta=expanded(3, 768, 256),
        Tb=expanded(3, 768, 256),
        Td=expanded(3, 384, 512),
        Tu=expanded(1, 256, 768),
        Te=expanded(3, 256, 256),
        Tf=expanded(3, 256, 128),
        Tg=expanded(3, 256, 256),
        raw=pltpu.VMEM((2, 2 * PIECE, LANES), jnp.bfloat16),
        work=pltpu.VMEM((9216, LANES), jnp.float32),
        rep=pltpu.VMEM((640, LANES), jnp.float32),
        wgv=pltpu.VMEM((weight_rows, LANES), jnp.float32),
        wq=pltpu.VMEM((MODULES, 2 * weight_rows // count, LANES), jnp.float32),
        wr=pltpu.VMEM((MODULES, span, LANES), jnp.float32),
        gathx=pltpu.VMEM((count, ROWS, LANES), jnp.bfloat16),
        gathc=pltpu.VMEM((count, ROWS, LANES), jnp.bfloat16),
        hot=pltpu.VMEM((2, 384, 768), jnp.bfloat16),
        blocks=pltpu.VMEM((2, ROWS, LANES), jnp.bfloat16),
        slopes=pltpu.VMEM((2, ROWS, LANES), jnp.float32),
        blockr=pltpu.VMEM((ROWS, LANES), jnp.bfloat16),
        sloper=pltpu.VMEM((ROWS, LANES), jnp.float32),
        gg=pltpu.VMEM((MODULES, 2, SLOTS, 256), jnp.float32),
        ggr=pltpu.VMEM((MODULES, 2, SLOTS, 256), jnp.float32),
        wsem=pltpu.SemaphoreType.DMA((2,)),
        ssem=pltpu.SemaphoreType.DMA((16,)),
        rsem=pltpu.SemaphoreType.DMA((16,)),
        hsem=pltpu.SemaphoreType.DMA((3 * count,)),
        gsem=pltpu.SemaphoreType.DMA((2 * count,)),
        psem=pltpu.SemaphoreType.DMA((5,)),
        qsem=pltpu.SemaphoreType.DMA((5,)),
        osem=pltpu.SemaphoreType.DMA((1,)),
    )


def pair_rows(weight_rows, count):
    share = weight_rows // count
    low = share // 8 * 8
    return share, 2 * share - low, low


def greet(core, count):
    barrier = pltpu.get_barrier_semaphore()
    me, shard = lax.axis_index("branch"), lax.axis_index("crops")
    z = shard // 2

    def signal(**where):
        pl.semaphore_signal(barrier, inc=1, device_id=where, device_id_type=pl.DeviceIdType.MESH)

    for step in range(1, 4):
        signal(branch=lax.rem(me + step, 4))
    signal(crops=shard + 1 - 2 * core)

    @pl.when(z > 0)
    def _():
        signal(crops=shard - 2)

    @pl.when(z < count // 2 - 1)
    def _():
        signal(crops=shard + 2)

    ends = (z == 0).astype(jnp.int32) + (z == count // 2 - 1).astype(jnp.int32)
    pl.semaphore_wait(barrier, 6 - ends)


def whole_kernel(names, rows, large, small, *args):
    refs = SimpleNamespace(**dict(zip(names, args)))
    count = large + small
    me, shard = lax.axis_index("branch"), lax.axis_index("crops")
    core = shard % 2
    weight_rows = refs.wgv.shape[0]
    share, span, low = pair_rows(weight_rows, count)
    quarter = pl.multiple_of(shard // 2 * (2 * share), 8)

    class Lazy:
        def __getitem__(self, index):
            return refs.masks[index]

    def across(source, goal, index):
        return pltpu.make_async_remote_copy(
            src_ref=source,
            dst_ref=goal,
            send_sem=refs.psem.at[index],
            recv_sem=refs.qsem.at[index],
            device_id=dict(crops=shard + 1 - 2 * core),
            device_id_type=pl.DeviceIdType.MESH,
        )

    def kernel_pair(m):
        at = pl.multiple_of(low * (1 - core), 8)
        return across(refs.wq.at[m, pl.ds(at, span)], refs.wr.at[m], m)

    outputs_pair = across(refs.blocks.at[1], refs.blockr, 2)
    gradient_pair = across(refs.slopes.at[1], refs.sloper, 3)
    table_pair = across(refs.gg, refs.ggr, 4)
    gather = Gather(refs, core, count)

    def every(action):
        for k in range(4):

            @pl.when(me == k)
            def _():
                action(Branch(k, rows, large, small, 2 * share, refs, Lazy(), core))

    def begin(branch):
        branch.fetch(0, 0).start()

    def prepare(branch):
        found = branch.segments()
        stops = {0: 1, min(2, len(found) - 2): 2, len(found) - 1: 3}
        for index, (unit, seg) in enumerate(found):
            branch.widen(index)
            for m in range(MODULES):
                branch.expand_one(m, unit, seg)
            if index in stops:
                gather.step(0, stops[index])

    def main(branch):
        branch.unpack(0, branch.take_feature)
        branch.maps["h"].close(0)
        gather.step(1, 0)

        def ahead(m, carry):
            branch.forward(m, gather)
            return carry

        def back(step, carry):
            m = MODULES - 1 - step
            branch.backward(m)
            refs.wq[m] = refs.wgv[pl.ds(quarter, 2 * share)]
            kernel_pair(m).start()
            return carry

        lax.fori_loop(0, MODULES, ahead, 0)
        branch.pack_outputs()
        outputs_pair.start()
        lax.fori_loop(0, MODULES, back, 0)
        branch.pack_gradient()
        gradient_pair.start()
        table_pair.start()

    every(begin)
    greet(core, count)
    gather.step(0, 0)
    fill_masks(refs, rows, core, small, large)
    refs.wgv[pl.ds(quarter, 2 * share)] = jnp.zeros((2 * share, LANES), jnp.float32)
    refs.gg[...] = jnp.zeros(refs.gg.shape, jnp.float32)
    every(prepare)
    gather.collect(0)
    every(main)

    for step in range(MODULES):
        m = MODULES - 1 - step
        kernel_pair(m).wait()
        mine = refs.wq[m, pl.ds(pl.multiple_of(low * core, 8), span)]
        refs.work[pl.ds(m, span, stride=MODULES)] = mine + refs.wr[m]
    skip = pl.multiple_of(core * (MODULES * (share - low)), 8)
    leave = pltpu.make_async_copy(
        refs.work.at[pl.ds(skip, MODULES * share)], refs.wg, refs.osem.at[0]
    )
    leave.start()
    outputs_pair.wait()
    gradient_pair.wait()
    table_pair.wait()
    own = refs.kinds[shard] != core
    refs.out[...] = jnp.where(own, refs.blocks[0].astype(jnp.float32), refs.blockr[...].astype(jnp.float32)).astype(jnp.bfloat16)
    refs.grad[...] = jnp.where(own, refs.slopes[0], refs.sloper[...])
    width = 256 // count
    for which, goal in ((0, refs.gain), (1, refs.shift)):
        for m in range(MODULES):
            total = refs.gg[m, which] + refs.ggr[m, which]
            found = None
            for at in range(count):
                piece = jnp.where(shard == at, total[:, at * width : (at + 1) * width], 0.0)
                found = piece if found is None else found + piece
            goal[m] = found
    gather.finish(0)
    gather.finish(1)
    leave.wait()


def whole_call(rows, large, small, x, cot, w, gains, shifts, kinds):
    count = large + small
    weight_rows = w.shape[0] // MODULES
    table = scratch_table(rows, weight_rows, count)
    vmem = pl.BlockSpec(memory_space=pltpu.VMEM)
    hbm = pl.BlockSpec(memory_space=pl.ANY)
    smem = pl.BlockSpec(memory_space=pltpu.SMEM)
    tables = jax.ShapeDtypeStruct((MODULES, SLOTS, 256 // count), jnp.float32)
    return pl.pallas_call(
        partial(whole_kernel, NAMES + list(table), rows, large, small),
        out_shape=(
            jax.ShapeDtypeStruct((ROWS, LANES), jnp.bfloat16),
            jax.ShapeDtypeStruct((ROWS, LANES), jnp.float32),
            jax.ShapeDtypeStruct((MODULES * weight_rows // count, LANES), jnp.float32),
            tables,
            tables,
        ),
        in_specs=[vmem, vmem, hbm, vmem, vmem, smem],
        out_specs=(vmem, vmem, hbm, vmem, vmem),
        scratch_shapes=list(table.values()),
        compiler_params=pltpu.CompilerParams(
            collective_id=0, has_side_effects=True, vmem_limit_bytes=62 * 1024 * 1024
        ),
    )(x, cot, w, gains, shifts, kinds)


def leave_kernel(*refs):
    for source, goal in zip(refs[:5], refs[5:]):
        goal[...] = source[...]


def leave_call(arrays):
    vmem = pl.BlockSpec(memory_space=pltpu.VMEM)
    return pl.pallas_call(
        leave_kernel,
        out_shape=tuple(jax.ShapeDtypeStruct(array.shape, array.dtype) for array in arrays),
        in_specs=[vmem] * 5,
        out_specs=(vmem,) * 5,
    )(*arrays)


def on_device_grouped(features, weights, gains, shifts, cotangent, size_group):
    count = lax.axis_size("crops")
    large = count // 4
    weight_rows = weights.shape[2] // LANES
    results = whole_call(
        group_rows(count),
        large,
        count - large,
        features[0],
        cotangent[0],
        weights[0]
        .reshape(MODULES, weight_rows, LANES)
        .transpose(1, 0, 2)
        .reshape(MODULES * weight_rows, LANES),
        gains[0],
        shifts[0],
        size_group,
    )
    out, grad, weight_grad, gain, shift = leave_call(results)
    share = weight_rows // count
    weight_grad = weight_grad.reshape(share, MODULES, LANES).transpose(1, 0, 2)
    weight_grad = with_layout_constraint(weight_grad, Layout((1, 0, 2)))
    return (
        out[None],
        grad[None],
        weight_grad.reshape(1, MODULES, share * LANES),
        gain[None],
        shift[None],
    )


def group_rows(count):
    large = count // 4
    rows = max(large * (LH // 8) * (LW // 8), (count - large) * (SH // 8) * (SW // 8))
    return -(-rows // 16) * 16


def fits(count):
    return count % 8 == 0 and group_rows(count) <= 96


def solution(mesh):
    placed = (
        P("branch", "crops", None),
        P("branch", None, None),
        P("branch", None, None, None),
        P("branch", None, None, None),
        P("branch", "crops", None),
        P(),
    )
    return jax.shard_map(
        on_device_grouped if fits(mesh.shape["crops"]) else on_device,
        mesh=mesh,
        in_specs=placed,
        out_specs=(
            P("branch", "crops", None),
            P("branch", "crops", None),
            P("branch", None, "crops"),
            P("branch", None, None, "crops"),
            P("branch", None, None, "crops"),
        ),
        check_vma=False,
    )
```

```python
from functools import partial
from types import SimpleNamespace
import math

import jax
import jax.numpy as jnp
import numpy as np
from jax import lax
from jax.experimental import pallas as pl
from jax.experimental.layout import Layout, with_layout_constraint
from jax.experimental.pallas import tpu as pltpu
from jax.sharding import PartitionSpec as P

C0 = 32
BLOCKS = 1
MODULES = 2
CROPS_DEV = 1
SH = 32
SW = 24
LH = 64
LW = 48
ROWS = 768
MSG_ROWS = 384


EPS = 1e-05


def as_sent(x):

    def short(part):
        return part.astype(jnp.bfloat16) if part.dtype == jnp.float32 else part

    return jax.tree.map(short, x)


def sender_plan(branch_index, top_channels, blocks):
    channels = top_channels << branch_index
    operations = []
    for block_index in range(blocks):
        operations.append(
            SimpleNamespace(
                phase=2 * block_index,
                source=("h", block_index),
                level=branch_index,
                cin=channels,
                cout=channels,
                stride=1,
                taps=3,
                act="silu",
                output=("u", block_index),
                skip=None,
                dest=-1,
            )
        )
        operations.append(
            SimpleNamespace(
                phase=2 * block_index + 1,
                source=("u", block_index),
                level=branch_index,
                cin=channels,
                cout=channels,
                stride=1,
                taps=3,
                act="res",
                output=("h", block_index + 1),
                skip=("h", block_index),
                dest=-1,
            )
        )
    top_name = ("h", blocks)
    for target in range(branch_index):
        operations.append(
            SimpleNamespace(
                phase=2 * blocks,
                source=top_name,
                level=branch_index,
                cin=channels,
                cout=top_channels << target,
                stride=1,
                taps=1,
                act="none",
                output=None,
                skip=None,
                dest=target,
            )
        )
    for target in range(branch_index + 1, 4):
        for depth_step in range(1, target - branch_index + 1):
            is_last = depth_step == target - branch_index
            operations.append(
                SimpleNamespace(
                    phase=2 * blocks + depth_step - 1,
                    source=top_name if depth_step == 1 else ("chain", target, depth_step - 1),
                    level=branch_index + depth_step,
                    cin=channels,
                    cout=top_channels << target if is_last else channels,
                    stride=2,
                    taps=3,
                    act="none" if is_last else "silu",
                    output=None if is_last else ("chain", target, depth_step),
                    skip=None,
                    dest=target if is_last else -1,
                )
            )
    for position, operation in enumerate(operations):
        operation.slot = position
        operation.size = (
            operation.taps * operation.taps * operation.cin * operation.cout
        )
        if operation.taps == 1:
            operation.kshape = (operation.cin, operation.cout)
        else:
            operation.kshape = (3, 3, operation.cin, operation.cout)
    return operations


def phase_lengths(top_channels, blocks):
    phase_count = 2 * blocks + 3
    lengths = [0] * phase_count
    for branch_index in range(4):
        per_phase = [0] * phase_count
        for operation in sender_plan(branch_index, top_channels, blocks):
            per_phase[operation.phase] += operation.size
        lengths = [max(current, candidate) for current, candidate in zip(lengths, per_phase)]
    return lengths


def weighted_plan(branch_index, top_channels, blocks):
    lengths = phase_lengths(top_channels, blocks)
    starts = [sum(lengths[:phase_index]) for phase_index in range(len(lengths))]
    running = [0] * len(lengths)
    operations = sender_plan(branch_index, top_channels, blocks)
    for operation in operations:
        phase_index = operation.phase
        operation.inner = running[phase_index]
        operation.offset = starts[phase_index] + running[phase_index]
        operation.position = sum(
            (1 for earlier in operations[: operation.slot] if earlier.phase == phase_index)
        )
        running[phase_index] += operation.size
    return operations


def phase_operations(branch_index, phase_index):
    return [
        operation
        for operation in weighted_plan(branch_index, C0, BLOCKS)
        if operation.phase == phase_index
    ]


def input_names(operations):
    source_names = []
    for operation in operations:
        if operation.source not in source_names:
            source_names.append(operation.source)
    return source_names


def silu_slope(value):
    sigmoid = jax.nn.sigmoid(value)
    return sigmoid * (1.0 + value * (1.0 - sigmoid))


def crop_cells(size_kind):
    return (LH, LW) if size_kind else (SH, SW)


def map_dims(size_kind, level, channels):
    height, breadth = crop_cells(size_kind)
    return (CROPS_DEV, height >> level, breadth >> level, channels)


def source_dims(branch_index, size_kind, map_name):
    level = branch_index + map_name[2] if map_name[0] == "chain" else branch_index
    return map_dims(size_kind, level, C0 << branch_index)


def preact_dims(size_kind, operation):
    return map_dims(size_kind, operation.level, operation.cout)


def to_canvas(arrays, value_type):
    if not arrays:
        return jnp.zeros((ROWS, 128), value_type)
    flattened = jnp.concatenate([array.reshape(-1).astype(value_type) for array in arrays])
    return jnp.pad(flattened, (0, ROWS * 128 - flattened.shape[0])).reshape(ROWS, 128)


def from_canvas(canvas, dims_list):
    flattened = canvas.reshape(-1)
    pieces = []
    offset = 0
    for dims_entry in dims_list:
        count_here = math.prod(dims_entry)
        pieces.append(flattened[offset : offset + count_here].reshape(dims_entry))
        offset += count_here
    return pieces


def to_slot(array):
    flattened = array.reshape(-1)
    return jnp.pad(flattened, (0, MSG_ROWS * 128 - flattened.shape[0])).reshape(MSG_ROWS, 128)


def from_slot(slot_rows, dims_entry):
    return slot_rows.reshape(-1)[: math.prod(dims_entry)].reshape(dims_entry)


def upsample(message, factor):
    crop_count, height, breadth, channels = message.shape
    widened = jnp.broadcast_to(
        message[:, :, None, :, None, :], (crop_count, height, factor, breadth, factor, channels)
    )
    return widened.reshape(crop_count, height * factor, breadth * factor, channels)


def block_pool(array, factor):
    crop_count, height, breadth, channels = array.shape
    return array.reshape(
        crop_count, height // factor, factor, breadth // factor, factor, channels
    ).sum(axis=(2, 4))


def kernel_piece(module_weights, operation):
    start = operation.offset
    return module_weights[start : start + operation.size].reshape(operation.kshape)


def conv_forward(operation, source, kernel):
    if operation.taps == 1:
        return jnp.einsum("nhwc,cd->nhwd", source, kernel, preferred_element_type=jnp.float32)
    stride = operation.stride
    return lax.conv_general_dilated(
        source,
        kernel,
        (stride, stride),
        ((1, 1), (1, 1)),
        dimension_numbers=("NHWC", "HWIO", "NHWC"),
        preferred_element_type=jnp.float32,
    )


def conv_backward(operation, source, kernel, upstream):
    if operation.taps == 1:
        source_grad = jnp.einsum(
            "nhwd,cd->nhwc", upstream, kernel, preferred_element_type=jnp.float32
        )
        kernel_grad = jnp.einsum(
            "nhwc,nhwd->cd", source, upstream, preferred_element_type=jnp.float32
        )
        return (source_grad, kernel_grad)
    stride = operation.stride
    flipped = jnp.transpose(kernel[::-1, ::-1], (0, 1, 3, 2))
    high_pad = 2 if stride == 2 else 1
    source_grad = lax.conv_general_dilated(
        upstream,
        flipped,
        (1, 1),
        ((1, high_pad), (1, high_pad)),
        lhs_dilation=(stride, stride),
        dimension_numbers=("NHWC", "HWIO", "NHWC"),
        preferred_element_type=jnp.float32,
    )
    kernel_grad = lax.conv_general_dilated(
        source,
        upstream,
        (1, 1),
        ((1, 2 - stride), (1, 2 - stride)),
        rhs_dilation=(stride, stride),
        dimension_numbers=("CHWN", "IHWO", "NHWC"),
        preferred_element_type=jnp.float32,
    )
    return (source_grad, jnp.transpose(kernel_grad, (1, 2, 0, 3)))


def cell_total(counts, size_kind, level):
    height, breadth = crop_cells(size_kind)
    return counts[size_kind] * float(CROPS_DEV * (height >> level) * (breadth >> level))


def norm_terms(totals, counts, size_kind, operation):
    cells_here = cell_total(counts, size_kind, operation.level)
    channels = operation.cout
    position = operation.position
    average = totals[size_kind, 0, position, :channels] / cells_here
    variance = totals[size_kind, 1, position, :channels] / cells_here - average * average
    return (average, lax.rsqrt(variance + EPS))


def forward_conv(branch_index, size_kind, phase_index, source_canvas, module_weights):
    operations = phase_operations(branch_index, phase_index)
    source_names = input_names(operations)
    pieces = from_canvas(
        source_canvas, [source_dims(branch_index, size_kind, map_name) for map_name in source_names]
    )
    sources = {
        map_name: piece.astype(jnp.bfloat16) for map_name, piece in zip(source_names, pieces)
    }
    preacts = []
    totals = jnp.zeros((2, 2, 3, 8 * C0), jnp.float32)
    for operation in operations:
        preact = conv_forward(
            operation, sources[operation.source], kernel_piece(module_weights, operation)
        )
        preacts.append(preact)
        channels = operation.cout
        position = operation.position
        totals = totals.at[size_kind, 0, position, :channels].set(jnp.sum(preact, axis=(0, 1, 2)))
        totals = totals.at[size_kind, 1, position, :channels].set(
            jnp.sum(preact * preact, axis=(0, 1, 2))
        )
    return (to_canvas(preacts, jnp.float32), totals)


def forward_norm(
    branch_index,
    size_kind,
    phase_index,
    preact_canvas,
    totals,
    counts,
    module_gains,
    module_shifts,
    skip_canvas,
    message_buffer,
):
    operations = phase_operations(branch_index, phase_index)
    preacts = from_canvas(
        preact_canvas, [preact_dims(size_kind, operation) for operation in operations]
    )
    skip_map = from_canvas(skip_canvas, [map_dims(size_kind, branch_index, C0 << branch_index)])[0]
    produced = []
    for operation, preact in zip(operations, preacts):
        average, inverse_std = norm_terms(totals, counts, size_kind, operation)
        norm_slot = operation.slot
        channels = operation.cout
        normed = (preact - average) * inverse_std * module_gains[
            norm_slot, :channels
        ] + module_shifts[norm_slot, :channels]
        if operation.act == "silu":
            produced.append(jax.nn.silu(normed))
        elif operation.act == "res":
            produced.append(jax.nn.silu(normed + skip_map))
        else:
            message_buffer = message_buffer.at[operation.dest].set(
                to_slot(normed.astype(jnp.bfloat16))
            )
    return (to_canvas(produced, jnp.float32), message_buffer)


def receive_forward(branch_index, size_kind, top_canvas, received):
    channels = C0 << branch_index
    summed = from_canvas(top_canvas, [map_dims(size_kind, branch_index, channels)])[0]
    for sender in range(4):
        if sender < branch_index:
            summed = summed + from_slot(
                received[sender], map_dims(size_kind, branch_index, channels)
            ).astype(jnp.float32)
        elif sender > branch_index:
            coarse = from_slot(received[sender], map_dims(size_kind, sender, channels))
            summed = summed + upsample(coarse, 2 ** (sender - branch_index)).astype(jnp.float32)
    return (to_canvas([jax.nn.silu(summed)], jnp.float32), to_canvas([summed], jnp.float32))


def receive_backward(branch_index, size_kind, grad_canvas, summed_canvas):
    dims_here = map_dims(size_kind, branch_index, C0 << branch_index)
    upstream = from_canvas(grad_canvas, [dims_here])[0]
    summed = from_canvas(summed_canvas, [dims_here])[0]
    summed_grad = upstream * silu_slope(summed)
    buffer = jnp.zeros((4, MSG_ROWS, 128), jnp.bfloat16)
    for sender in range(4):
        if sender < branch_index:
            buffer = buffer.at[sender].set(to_slot(summed_grad.astype(jnp.bfloat16)))
        elif sender > branch_index:
            pooled = block_pool(summed_grad, 2 ** (sender - branch_index))
            buffer = buffer.at[sender].set(to_slot(pooled.astype(jnp.bfloat16)))
    return (to_canvas([summed_grad], jnp.float32), buffer)


def backward_stats(
    branch_index,
    size_kind,
    phase_index,
    dout_canvas,
    message_grads,
    preact_canvas,
    totals,
    counts,
    module_gains,
    module_shifts,
    skip_canvas,
):
    operations = phase_operations(branch_index, phase_index)
    preacts = from_canvas(
        preact_canvas, [preact_dims(size_kind, operation) for operation in operations]
    )
    producing = [operation for operation in operations if operation.act != "none"]
    output_grads = from_canvas(
        dout_canvas, [preact_dims(size_kind, operation) for operation in producing]
    )
    grads_by_name = {
        operation.output: piece for operation, piece in zip(producing, output_grads)
    }
    skip_map = from_canvas(skip_canvas, [map_dims(size_kind, branch_index, C0 << branch_index)])[0]
    upstreams = []
    skip_grads = []
    sums_local = jnp.zeros((2, 2, 3, 8 * C0), jnp.float32)
    for operation, preact in zip(operations, preacts):
        average, inverse_std = norm_terms(totals, counts, size_kind, operation)
        norm_slot = operation.slot
        channels = operation.cout
        centered = (preact - average) * inverse_std
        normed = centered * module_gains[norm_slot, :channels] + module_shifts[norm_slot, :channels]
        if operation.act == "silu":
            upstream = grads_by_name[operation.output] * silu_slope(normed)
        elif operation.act == "res":
            upstream = grads_by_name[operation.output] * silu_slope(normed + skip_map)
            skip_grads.append(upstream)
        else:
            upstream = from_slot(
                message_grads[operation.dest], preact_dims(size_kind, operation)
            ).astype(jnp.float32)
        upstreams.append(upstream)
        position = operation.position
        sums_local = sums_local.at[size_kind, 0, position, :channels].set(
            jnp.sum(upstream, axis=(0, 1, 2))
        )
        sums_local = sums_local.at[size_kind, 1, position, :channels].set(
            jnp.sum(upstream * centered, axis=(0, 1, 2))
        )
    return (to_canvas(upstreams, jnp.float32), sums_local, to_canvas(skip_grads, jnp.float32))


def backward_apply(
    branch_index,
    size_kind,
    phase_index,
    upstream_canvas,
    preact_canvas,
    totals,
    grad_totals,
    counts,
    source_canvas,
    module_weights,
    module_gains,
):
    operations = phase_operations(branch_index, phase_index)
    preacts = from_canvas(
        preact_canvas, [preact_dims(size_kind, operation) for operation in operations]
    )
    upstreams = from_canvas(
        upstream_canvas, [preact_dims(size_kind, operation) for operation in operations]
    )
    source_names = input_names(operations)
    source_list = [source_dims(branch_index, size_kind, map_name) for map_name in source_names]
    pieces = from_canvas(source_canvas, source_list)
    sources = {
        map_name: piece.astype(jnp.bfloat16) for map_name, piece in zip(source_names, pieces)
    }
    source_grads = {
        map_name: jnp.zeros(dims_entry, jnp.float32)
        for map_name, dims_entry in zip(source_names, source_list)
    }
    kernel_grads = []
    slot_count = module_gains.shape[0]
    gain_part = jnp.zeros((slot_count, 8 * C0), jnp.float32)
    shift_part = jnp.zeros((slot_count, 8 * C0), jnp.float32)
    for operation, preact, upstream in zip(operations, preacts, upstreams):
        average, inverse_std = norm_terms(totals, counts, size_kind, operation)
        cells_here = cell_total(counts, size_kind, operation.level)
        norm_slot = operation.slot
        channels = operation.cout
        position = operation.position
        centered = (preact - average) * inverse_std
        mean_upstream = grad_totals[size_kind, 0, position, :channels] / cells_here
        mean_cross = grad_totals[size_kind, 1, position, :channels] / cells_here
        preact_grad = (
            module_gains[norm_slot, :channels]
            * inverse_std
            * (upstream - mean_upstream - centered * mean_cross)
        )
        source_grad, kernel_grad = conv_backward(
            operation,
            sources[operation.source],
            kernel_piece(module_weights, operation),
            preact_grad.astype(jnp.bfloat16),
        )
        source_grads[operation.source] = source_grads[operation.source] + source_grad
        kernel_grads.append(kernel_grad.reshape(-1))
        gain_part = gain_part.at[norm_slot, :channels].set(
            grad_totals[0, 1, position, :channels] + grad_totals[1, 1, position, :channels]
        )
        shift_part = shift_part.at[norm_slot, :channels].set(
            grad_totals[0, 0, position, :channels] + grad_totals[1, 0, position, :channels]
        )
    phase_length = phase_lengths(C0, BLOCKS)[phase_index]
    if kernel_grads:
        joined = jnp.concatenate(kernel_grads)
        weight_part = jnp.pad(joined, (0, phase_length - joined.shape[0]))
    else:
        weight_part = jnp.zeros((phase_length,), jnp.float32)
    return (
        to_canvas([source_grads[map_name] for map_name in source_names], jnp.float32),
        weight_part,
        gain_part,
        shift_part,
    )


def on_device(features, weights, gains, shifts, cotangent, size_group):
    crop_shard = lax.axis_index("crops")
    shard_count = lax.axis_size("crops")
    crop_kind = size_group[crop_shard]
    large_count = jnp.sum(size_group).astype(jnp.float32)
    counts = jnp.stack([shard_count - large_count, large_count])
    case_index = lax.axis_index("branch") * 2 + crop_kind
    phase_total = 2 * BLOCKS + 3
    zero_canvas = jnp.zeros((ROWS, 128), jnp.float32)
    empty_buffer = jnp.zeros((4, MSG_ROWS, 128), jnp.bfloat16)

    def run_phase(function, statics, operands):
        branches_list = [
            partial(function, branch_index, size_kind, *statics)
            for branch_index in range(4)
            for size_kind in range(2)
        ]
        return lax.switch(case_index, branches_list, *operands)

    def statistics(local_totals):
        return lax.psum(local_totals, "crops")

    def module_forward(module, start_canvas, kept):
        module_weights = weights[0, module]
        module_gains = gains[0, module]
        module_shifts = shifts[0, module]
        record = SimpleNamespace(sources=[], preacts=[], totals=[])
        h_canvas = start_canvas
        u_canvas = zero_canvas
        chain_canvas = zero_canvas
        buffer = empty_buffer
        for phase_index in range(phase_total):
            if phase_index < 2 * BLOCKS:
                source = h_canvas if phase_index % 2 == 0 else u_canvas
            elif phase_index == 2 * BLOCKS:
                source = h_canvas
            else:
                source = chain_canvas
            preact, local_totals = run_phase(forward_conv, (phase_index,), (source, module_weights))
            global_totals = kept.totals[phase_index] if kept else statistics(local_totals)
            produced, buffer = run_phase(
                forward_norm,
                (phase_index,),
                (preact, global_totals, counts, module_gains, module_shifts, h_canvas, buffer),
            )
            record.sources.append(source)
            record.preacts.append(preact)
            record.totals.append(global_totals)
            if phase_index < 2 * BLOCKS:
                if phase_index % 2 == 0:
                    u_canvas = produced
                else:
                    h_canvas = produced
            else:
                chain_canvas = produced
        received = (
            kept.received
            if kept
            else jax.tree.map(
                lambda part, own: part.astype(own.dtype),
                lax.all_to_all(as_sent(buffer), "branch", split_axis=0, concat_axis=0, tiled=True),
                buffer,
            )
        )
        result, summed = run_phase(receive_forward, (), (h_canvas, received))
        record.summed = summed
        record.received = received
        return (result, record)

    checkpoints = [features[0].astype(jnp.float32)]
    first_records = []
    for module in range(MODULES):
        result, record = module_forward(module, checkpoints[-1], None)
        checkpoints.append(result)
        first_records.append(record)
    outputs = checkpoints[-1].astype(jnp.bfloat16)
    grad_canvas = cotangent[0].astype(jnp.float32)
    module_grads = [None] * MODULES
    gain_grads = [None] * MODULES
    shift_grads = [None] * MODULES
    for module in reversed(range(MODULES)):
        kept = None
        unused_result, record = module_forward(module, checkpoints[module], kept)
        module_module_weights = weights[0, module]
        module_module_gains = gains[0, module]
        module_module_shifts = shifts[0, module]
        summed_grad, back_buffer = run_phase(receive_backward, (), (grad_canvas, record.summed))
        message_grads = jax.tree.map(
            lambda part, own: part.astype(own.dtype),
            lax.all_to_all(as_sent(back_buffer), "branch", split_axis=0, concat_axis=0, tiled=True),
            back_buffer,
        )
        top_grad = summed_grad
        chain_grad = zero_canvas
        u_grad = zero_canvas
        pending_skip = zero_canvas
        weight_parts = [None] * phase_total
        gain_total = jnp.zeros(gains.shape[2:], jnp.float32)
        shift_total = jnp.zeros(gains.shape[2:], jnp.float32)
        for module_phase_index in reversed(range(phase_total)):
            if module_phase_index >= 2 * BLOCKS:
                output_grad = chain_grad
                skip_canvas = zero_canvas
            elif module_phase_index % 2 == 1:
                output_grad = top_grad
                skip_canvas = record.sources[module_phase_index - 1]
            else:
                output_grad = u_grad
                skip_canvas = zero_canvas
            module_preact = record.preacts[module_phase_index]
            totals = record.totals[module_phase_index]
            upstream, module_local_totals, skip_grad = run_phase(
                backward_stats,
                (module_phase_index,),
                (
                    output_grad,
                    message_grads,
                    module_preact,
                    totals,
                    counts,
                    module_module_gains,
                    module_module_shifts,
                    skip_canvas,
                ),
            )
            grad_totals = lax.psum(module_local_totals, "crops")
            source_grad, weight_parts[module_phase_index], gain_part, shift_part = run_phase(
                backward_apply,
                (module_phase_index,),
                (
                    upstream,
                    module_preact,
                    totals,
                    grad_totals,
                    counts,
                    record.sources[module_phase_index],
                    module_module_weights,
                    module_module_gains,
                ),
            )
            gain_total = gain_total + gain_part
            shift_total = shift_total + shift_part
            if module_phase_index > 2 * BLOCKS:
                chain_grad = source_grad
            elif module_phase_index == 2 * BLOCKS:
                top_grad = top_grad + source_grad
            elif module_phase_index % 2 == 1:
                u_grad = source_grad
                pending_skip = skip_grad
            else:
                top_grad = source_grad + pending_skip
        joined = jnp.concatenate(weight_parts)
        weight_grad = jnp.pad(joined, (0, weights.shape[2] - joined.shape[0]))
        grad_canvas, weight_grad, gain_grads[module], shift_grads[module] = (
            top_grad,
            weight_grad,
            gain_total,
            shift_total,
        )
        module_grads[module] = weight_grad
    weight_out = lax.psum_scatter(jnp.stack(module_grads), "crops", scatter_dimension=1, tiled=True)
    share = gains.shape[3] // shard_count
    gain_out = lax.dynamic_slice_in_dim(jnp.stack(gain_grads), crop_shard * share, share, axis=2)
    shift_out = lax.dynamic_slice_in_dim(jnp.stack(shift_grads), crop_shard * share, share, axis=2)
    return (outputs[None], grad_canvas[None], weight_out[None], gain_out[None], shift_out[None])


LANES = 128
SLOTS = 8
MASKS = 7
DOWN = (((1,), (0,)), ((), ()))
ACROSS = (((1,), (1,)), ((), ()))
ALONG = (((0,), (0,)), ((), ()))


def unit_table(k):
    operations = weighted_plan(k, C0, BLOCKS)
    planes = 8 >> k
    channels = C0 << k
    units = {}
    stat = 0

    def add(name, kind, source, lanes_in, planes_in, planes_out, members):
        nonlocal stat
        segs = []
        tile = 0
        for operation, lanes, chain in members:
            cout = operation.cout
            level = operation.level if operation.taps == 3 else operation.dest
            segs.append(
                SimpleNamespace(
                    slot=operation.slot,
                    off=operation.offset // LANES,
                    cin=operation.cin,
                    cout=cout,
                    taps=operation.taps,
                    tile=tile,
                    tiles=lanes // LANES,
                    blocks=max(1, (8 >> level)),
                    dest=operation.dest,
                    act=operation.act,
                    chain=chain,
                    up=k - operation.dest if operation.taps == 1 else 0,
                )
            )
            tile += lanes // LANES
        rows = {"s1": 768 if k == 3 else 512, "s2": lanes_in + LANES, "p1": 256}[kind]
        units[name] = SimpleNamespace(
            name=name,
            kind=kind,
            source=source,
            lanes_in=lanes_in,
            blocks_in=planes_in,
            planes_in=planes_in,
            planes=planes_out,
            segs=segs,
            tiles=tile,
            rows=rows,
            stat=stat,
            depth=1 if kind == "p1" else 3,
        )
        stat += tile

    add("a", "s1", "h", 256, planes, planes, [(operations[0], 256, None)])
    add("b", "s1", "u", 256, planes, planes, [(operations[1], 256, None)])
    ups = [operation for operation in operations if operation.taps == 1]
    if ups:
        add("u", "p1", "t", 256, planes, planes, [(operation, 256, None) for operation in ups])
    firsts, chains = [], {}
    for target in range(k + 1, 4):
        steps = [
            operation
            for operation in operations
            if operation.taps == 3 and operation.stride == 2
        ]
        start = sum(i - k for i in range(k + 1, target))
        chains[target] = steps[start : start + target - k]
        if target == k + 1:
            firsts.append((chains[target][0], 256, None))
        else:
            firsts.append((chains[target][0], LANES, "c1" if target == k + 2 else "c2"))
    if firsts:
        add("d", "s2", "t", 256, planes, planes // 2, firsts)
    if k <= 1:
        add("e", "s2", "c1", LANES, planes // 2, planes // 4, [(chains[k + 2][1], 256, None)])
    if k == 0:
        add("f", "s2", "c2", LANES, planes // 2, planes // 4, [(chains[3][1], LANES, "c3")])
        add("g", "s2", "c3", LANES, planes // 4, planes // 8, [(chains[3][2], 256, None)])
    return units


def links(k, unit, seg):
    cin = seg.cin
    count_in, count_out = unit.blocks_in, seg.blocks
    found = []
    if unit.kind == "p1":
        for plane in range(count_in):
            wide = 1 << seg.up
            found.append((plane * cin, 0, set(range(plane * wide, plane * wide + wide))))
        return found
    if unit.kind == "s1" and k == 3:
        return [(256 * tap, tap, {0}) for tap in range(3)]
    stride = 1 if unit.kind == "s1" else 2
    for plane in range(count_in):
        for tap in range(3):
            at = plane - tap + 1
            if at % stride == 0 and 0 <= at // stride < count_out:
                found.append((plane * cin, tap, {at // stride}))
    if stride == 1:
        found.append((256, 2, {count_out - 1}))
        found.append((512 - cin, 0, {0}))
    else:
        lanes_in = unit.lanes_in
        found.append((lanes_in + (count_in - 1) * cin - (lanes_in - LANES), 0, {0}))
    return found


def message_slot(k, other):
    return sum(2 * (8 >> max(k, before)) for before in range(other) if before != k)


def log2(value):
    return value.bit_length() - 1


def sigmoid_of(value):
    return 0.5 * jnp.tanh(0.5 * value) + 0.5


def silu_of(value):
    return value * sigmoid_of(value)


def slope_of(value):
    sigmoid = sigmoid_of(value)
    return sigmoid * (1.0 + value * (1.0 - sigmoid))


def planes_loop(count, body, turns=1):
    def step(index, carry):
        for turn in range(turns):
            body(index * turns + turn)
        return carry

    turns = min(turns, count)
    if count == turns:
        for index in range(count):
            body(index)
    else:
        lax.fori_loop(0, count // turns, step, 0)


def planes_sum(count, body, initial, turns=1):
    def step(index, carry):
        for turn in range(turns):
            carry = body(index * turns + turn, carry)
        return carry

    turns = min(turns, count)
    if count == turns:
        return step(0, initial)
    return lax.fori_loop(0, count // turns, step, initial)


def partial_sum(value):
    rows = value.shape[0]
    return jnp.sum(value.reshape(rows // 8, 8, value.shape[1]), axis=0)


class Planes:
    def __init__(self, mode, tiles, planes, masks, rows, main, edge=None, right=None):
        self.mode, self.tiles, self.planes = mode, tiles, planes
        self.masks, self.rows = masks, rows
        self.main, self.edge, self.right = main, edge, right
        self.base = 1 if mode in ("s1", "wide", "s2") else 0
        extra = {"s1": 2, "wide": 2, "s2": 1, "dz2": 1, "p": 0}[mode]
        self.span = planes + extra
        self.unit = tiles * self.span

    def at(self, m, tile, plane):
        return m * self.unit + tile * self.span + plane + self.base

    def edge_at(self, m, tile, plane):
        if self.mode == "s2":
            return m * self.span + plane + self.base
        return self.at(m, tile, plane)

    def from_left(self, value):
        return pltpu.roll(value, 1, 0) * self.masks[1]

    def from_right(self, value):
        return pltpu.roll(value, self.rows - 1, 0) * self.masks[2]

    def store(self, m, tile, plane, value):
        self.put(m, tile, plane, value)
        if isinstance(plane, int):
            if plane == self.planes - 1:
                self.put_above(m, tile, value)
            if plane == 0:
                self.put_below(m, tile, value)

    def put(self, m, tile, plane, value):
        where = self.at(m, tile, plane)
        self.main[where] = value.astype(jnp.bfloat16)
        if self.mode == "s1":
            side = self.from_right(value) if tile == 0 else self.from_left(value)
            self.edge[where] = side.astype(jnp.bfloat16)
        elif self.mode == "wide":
            self.edge[where] = self.from_left(value).astype(jnp.bfloat16)
            self.right[where] = self.from_right(value).astype(jnp.bfloat16)
        elif self.mode == "s2":
            if tile == self.tiles - 1:
                self.edge[self.edge_at(m, tile, plane)] = self.from_left(value).astype(jnp.bfloat16)
        elif self.mode == "dz2":
            self.edge[where] = self.from_right(value).astype(jnp.bfloat16)

    def put_above(self, m, tile, last):
        if self.mode in ("s1", "wide", "s2"):
            above = pltpu.roll(last, 6, 0) * self.masks[3] + pltpu.roll(last, 3, 0) * self.masks[4]
            self.put(m, tile, -1, above)

    def put_below(self, m, tile, first):
        if self.mode in ("s1", "wide", "dz2"):
            rows = self.rows
            below = (
                pltpu.roll(first, rows - 6, 0) * self.masks[5]
                + pltpu.roll(first, rows - 3, 0) * self.masks[6]
            )
            self.put(m, tile, self.planes, below)

    def close(self, m):
        for tile in range(self.tiles):
            last = self.main[self.at(m, tile, self.planes - 1)].astype(jnp.float32)
            self.put_above(m, tile, last)
            first = self.main[self.at(m, tile, 0)].astype(jnp.float32)
            self.put_below(m, tile, first)


class Branch:
    def __init__(self, k, rows, large, small, share, refs, masks, core):
        self.k, self.rows, self.refs, self.masks = k, rows, refs, masks
        self.units = unit_table(k)
        self.planes = 8 >> k
        self.core = core
        self.large, self.small, self.count = large, small, large + small
        self.cells = (small * (SH // 8) * (SW // 8), large * (LH // 8) * (LW // 8))
        self.quarter = lax.axis_index("crops") // 2
        self.share = share
        r = refs
        make = partial(Planes, masks=masks, rows=rows)
        one = "wide" if k == 3 else "s1"
        self.maps = dict(
            h=make(one, 2, self.planes, main=r.hC, edge=r.hE, right=r.hR),
            u=make(one, 2, self.planes, main=r.uC, edge=r.uE, right=r.uR),
            t=make("p" if k == 3 else "s2", 2, self.planes, main=r.tC, edge=r.tE),
        )
        if k <= 1:
            self.maps["c1"] = make("s2", 1, self.planes // 2, main=r.c1C, edge=r.c1E)
        if k == 0:
            self.maps["c2"] = make("s2", 1, 4, main=r.c2C, edge=r.c2E)
            self.maps["c3"] = make("s2", 1, 2, main=r.c3C, edge=r.c3E)
        self.grads = dict(t=r.gt, u=r.gu, c1=r.gc1, c2=r.gc2, c3=r.gc3)

    def lane_block(self, shape, cout):
        lanes = lax.broadcasted_iota(jnp.int32, shape, 1)
        return lanes >> log2(cout)

    def keep(self, value, cout, which):
        count = LANES // cout
        if len(which) == count:
            return value
        block = self.lane_block(value.shape, cout)
        mask = block == which[0]
        for entry in which[1:]:
            mask = mask | (block == entry)
        return jnp.where(mask, value, 0.0)

    def spread(self, value, cout):
        shift = LANES // 2
        while shift >= cout:
            value = value + pltpu.roll(value, shift, 1)
            shift //= 2
        return value

    def local_blocks(self, seg, tile, wanted):
        count = LANES // seg.cout
        return [q for q in range(count) if (tile * count + q) % seg.blocks in wanted]


    def segments(self):
        return [(unit, seg) for unit in self.units.values() for seg in unit.segs]

    def piece(self, index):
        def split(unit, seg):
            count = seg.taps**2 * seg.cin * seg.cout // LANES
            return unit.depth, count // unit.depth

        found = [split(unit, seg) for unit, seg in self.segments()]
        return *found[index], sum(many for many, _ in found[:index])

    def fetch(self, index, d):
        r = self.refs
        _, seg = self.segments()[index]
        _, count, before = self.piece(index)
        slot = (before + d) % 2
        return pltpu.make_async_copy(
            r.w.at[pl.ds(2 * seg.off + d * (2 * count), 2 * count)],
            r.raw.at[slot, pl.ds(0, 2 * count)],
            r.wsem.at[slot],
        )

    def expand(self, index):
        unit, seg = self.segments()[index]
        many = unit.depth

        def step(d):
            self.fetch(index, d).wait()
            self.fetch(index, d + 1).start()
            self.expand_row(index, d)

        if many > 1:
            planes_loop(many - 1, step)
        self.fetch(index, many - 1).wait()
        if index + 1 < len(self.segments()):
            self.fetch(index + 1, 0).start()
        self.expand_row(index, many - 1)
        for m in range(MODULES):
            self.spread_tables(m, unit, seg)

    def expand_row(self, index, d):
        r = self.refs
        unit, seg = self.segments()[index]
        _, count, before = self.piece(index)
        chunk = 2 * math.gcd(count, 192)
        wf, rep = r.work, r.rep

        def widen(step):
            at = pl.multiple_of(step * chunk, 16)
            value = r.raw[(before + d) % 2, pl.ds(at, chunk)].astype(jnp.float32)
            wf[pl.ds(at, chunk)] = value

        planes_loop(2 * count // chunk, widen)
        depth, cin, cout = unit.depth, seg.cin, seg.cout
        target = getattr(r, "T" + unit.name)
        twice = unit.kind == "s1" and self.k < 3
        across = getattr(r, "T" + unit.name + unit.name) if twice else None
        by_row = {}
        for row, tap, wanted in links(self.k, unit, seg):
            by_row.setdefault(row, []).append((tap, wanted))
        for m in range(MODULES):
            if cout < LANES:
                ratio = LANES // cout
                flat = wf[pl.ds(m, count, stride=2)]
                for part in range(ratio):
                    rep[pl.ds(part, count, stride=ratio)] = self.spread(
                        self.keep(flat, cout, [part]), cout
                    )

            def tap_rows(tap, tile):
                if cout < LANES:
                    return rep[tap * cin : (tap + 1) * cin]
                if cout == LANES:
                    return wf[pl.ds(m + tap * (2 * cin), cin, stride=2)]
                return wf[pl.ds(m + tap * (4 * cin) + 2 * tile, cin, stride=4)]

            for tile in range(seg.tiles):
                column = (seg.tile + tile) * LANES
                for row in range(0, unit.rows, cin):
                    total = None
                    for tap, wanted in by_row.get(row, []):
                        if cout <= LANES:
                            local = self.local_blocks(seg, tile, wanted)
                            if not local:
                                continue
                            piece = self.keep(tap_rows(tap, 0), cout, local)
                        else:
                            piece = tap_rows(tap, tile)
                        total = piece if total is None else total + piece
                    if total is None:
                        total = jnp.zeros((cin, LANES), jnp.float32)
                    block = total.astype(jnp.bfloat16)
                    target[m * depth + d, row : row + cin, column : column + LANES] = block
                    if across is not None:
                        first, lane = row % 256, row // 256 * 256 + column
                        across[m * depth + d, first : first + cin, lane : lane + LANES] = block


    def parts(self, unit, source):
        if unit.kind == "p1":
            return [(source.main, range(2), source.at)]
        if source.mode == "wide":
            return [
                (source.edge, range(2), source.at),
                (source.main, range(2), source.at),
                (source.right, range(2), source.at),
            ]
        if unit.kind == "s1":
            return [(source.main, range(2), source.at), (source.edge, range(2), source.at)]
        last = source.tiles - 1
        return [
            (source.main, range(source.tiles), source.at),
            (source.edge, [last], source.edge_at),
        ]

    def rows_of(self, unit, part, m, d, first, count):
        ref, tiles, at = part
        pieces = []
        for tile in tiles:
            if unit.kind == "s2":
                rows = [ref[at(m, tile, 2 * (first + q) + d - 1)] for q in range(count)]
                pieces.append(rows[0] if count == 1 else jnp.concatenate(rows, axis=0))
            else:
                shift = d - 1 if unit.kind == "s1" else 0
                pieces.append(
                    ref[pl.ds(at(m, tile, first + shift), count)].reshape(count * self.rows, LANES)
                )
        return pieces

    def conv(self, m, unit):
        r = self.refs
        source = self.maps[unit.source]
        target = getattr(r, "T" + unit.name)
        z = getattr(r, "z" + unit.name)
        planes, tiles, depth = unit.planes, unit.tiles, unit.depth
        chunk = min(planes, 4 if tiles <= 2 else 2)
        lanes = tiles * LANES

        def body(step, sums):
            first = step * chunk
            pieces = []
            for d in range(depth):
                for part in self.parts(unit, source):
                    pieces += self.rows_of(unit, part, m, d, first, chunk)
            left = jnp.concatenate(pieces, axis=1)
            right = target[pl.ds(m * depth, depth), 0 : unit.rows, 0:lanes]
            right = right.reshape(depth * unit.rows, lanes)
            result = lax.dot_general(left, right, DOWN, preferred_element_type=jnp.float32)
            for tile in range(tiles):
                block = result[:, tile * LANES : (tile + 1) * LANES]
                z[pl.ds(m * tiles * planes + tile * planes + first, chunk)] = block.reshape(
                    chunk, self.rows, LANES
                )
            return (sums[0] + partial_sum(result), sums[1] + partial_sum(result * result))

        zero = jnp.zeros((8, lanes), jnp.float32)
        sums = planes_sum(planes // chunk, body, (zero, zero))
        for seg in unit.segs:
            scale = self.per_cell(unit, seg)
            totals = self.fold(seg, sums)
            self.norm_rows(m, unit, seg, totals, scale)

    def per_cell(self, unit, seg):
        blocks = seg.tiles * LANES // seg.cout
        small, large = self.cells
        count = unit.planes * blocks
        return jnp.where(self.core == 0, 1.0 / (large * count), 1.0 / (small * count)).astype(
            jnp.float32
        )

    def fold(self, seg, sums):
        first = seg.tile
        found = []
        for value in sums:
            tiles = [
                value[:, (first + t) * LANES : (first + t + 1) * LANES] for t in range(seg.tiles)
            ]
            if seg.cout <= LANES:
                total = tiles[0]
                for tile in tiles[1:]:
                    total = total + tile
                total = jnp.sum(self.spread(total, seg.cout), axis=0, keepdims=True)
                found.append([total] * seg.tiles)
            else:
                found.append([jnp.sum(tile, axis=0, keepdims=True) for tile in tiles])
        return found

    def table_row(self, ref, m, seg, tile):
        slot = seg.slot
        if seg.cout > LANES:
            return ref[m, slot : slot + 1, tile * LANES : (tile + 1) * LANES]
        row = jnp.broadcast_to(ref[m, slot : slot + 1, 0:LANES], (8, LANES))
        if seg.cout < LANES:
            row = self.spread(self.keep(row, seg.cout, [0]), seg.cout)
        return row[0:1]

    def norm_rows(self, m, unit, seg, totals, scale):
        st = self.refs.st
        for tile in range(seg.tiles):
            average = totals[0][tile] * scale
            variance = totals[1][tile] * scale - average * average
            inverse = lax.rsqrt(variance + EPS)
            where = m * STATS + unit.stat + seg.tile + tile
            factor = st[where, 4:5] * inverse
            st[where, 0:1] = average
            st[where, 1:2] = inverse
            st[where, 2:3] = factor
            st[where, 3:4] = st[where, 5:6] - average * factor

    def spread_tables(self, m, unit, seg):
        st = self.refs.st
        for tile in range(seg.tiles):
            where = m * STATS + unit.stat + seg.tile + tile
            st[where, 4:5] = self.table_row(self.refs.gains, m, seg, tile)
            st[where, 5:6] = self.table_row(self.refs.shifts, m, seg, tile)

    def normed(self, m, unit, tile, plane):
        st = self.refs.st
        z = getattr(self.refs, "z" + unit.name)
        where = m * STATS + unit.stat + tile
        value = z[m * unit.tiles * unit.planes + tile * unit.planes + plane]
        return value * st[where, 2:3] + st[where, 3:4]

    def apply_a(self, m):
        unit, u = self.units["a"], self.maps["u"]

        def body(plane):
            for tile in range(2):
                value = silu_of(self.normed(m, unit, tile, plane)) * self.masks[0]
                u.store(m, tile, plane, value)

        planes_loop(self.planes, body, TURNS)

    def apply_b(self, m):
        unit, top = self.units["b"], self.maps["t"]
        hf, s = self.refs.hf, self.refs.s

        def body(plane):
            for tile in range(2):
                where = m * 2 * self.planes + tile * self.planes + plane
                value = silu_of(self.normed(m, unit, tile, plane) + hf[where]) * self.masks[0]
                s[where] = value
                top.store(m, tile, plane, value)

        planes_loop(self.planes, body, TURNS)

    def apply_rest(self, m, unit):
        sb = self.refs.sb
        for seg in unit.segs:
            chain = self.maps[seg.chain] if seg.chain else None

            def body(plane):
                for tile in range(seg.tiles):
                    value = self.normed(m, unit, seg.tile + tile, plane)
                    if chain is not None:
                        chain.store(m, tile, plane, silu_of(value) * self.masks[0])
                    else:
                        at = message_slot(self.k, seg.dest) + tile * unit.planes + plane
                        sb[at] = value.astype(jnp.bfloat16)

            planes_loop(unit.planes, body, TURNS)
            if chain is None:
                self.message(m, seg.dest).start()

    def message(self, e, other):
        count = 2 * (8 >> max(self.k, other))
        r = self.refs
        return pltpu.make_async_remote_copy(
            src_ref=r.sb.at[pl.ds(message_slot(self.k, other), count)],
            dst_ref=r.rb.at[pl.ds(e * 16 + message_slot(other, self.k), count)],
            send_sem=r.ssem.at[e * 4 + other],
            recv_sem=r.rsem.at[e * 4 + self.k],
            device_id=dict(branch=other),
            device_id_type=pl.DeviceIdType.MESH,
        )

    def arrived(self, e, other):
        count = 2 * (8 >> max(self.k, other))
        r = self.refs
        at = message_slot(self.k, other)
        return pltpu.make_async_remote_copy(
            src_ref=r.sb.at[pl.ds(at, count)],
            dst_ref=r.rb.at[pl.ds(e * 16 + at, count)],
            send_sem=r.ssem.at[e * 4 + other],
            recv_sem=r.rsem.at[e * 4 + other],
            device_id=dict(branch=other),
            device_id_type=pl.DeviceIdType.MESH,
        )

    def others(self):
        return [other for other in range(4) if other != self.k]

    def settle(self, e):
        for other in self.others():
            self.message(e, other).wait_send()
        for other in self.others():
            self.arrived(e, other).wait_recv()

    def receive(self, m):
        r = self.refs
        s, rb, hf, out = r.s, r.rb, r.hf, r.outs
        h = self.maps["h"]

        def total_at(tile, plane):
            where = m * 2 * self.planes + tile * self.planes + plane
            total = s[where]
            for other in self.others():
                count = 8 >> max(self.k, other)
                at = plane >> max(0, other - self.k)
                slot = m * 16 + message_slot(self.k, other) + tile * count + at
                total = total + rb[slot].astype(jnp.float32)
            s[where] = total
            return silu_of(total) * self.masks[0]

        @pl.when(m + 1 < MODULES)
        def _():
            for plane in range(self.planes):
                for tile in range(2):
                    value = total_at(tile, plane)
                    hf[(2 + tile) * self.planes + plane] = value
                    h.store(1, tile, plane, value)

        @pl.when(m + 1 == MODULES)
        def _():
            for plane in range(self.planes):
                for tile in range(2):
                    out[tile * self.planes + plane] = total_at(tile, plane).astype(jnp.bfloat16)

    def take_feature(self, tile, plane, value):
        self.refs.hf[tile * self.planes + plane] = value
        self.maps["h"].store(0, tile, plane, value)

    def take_cotangent(self, tile, plane, value):
        self.refs.gin[tile * self.planes + plane] = value

    def member(self, kind, order):
        kinds = self.refs.kinds
        found, before = jnp.int32(0), jnp.int32(0)
        for at in range(self.count):
            same = kinds[at] == kind
            found = jnp.where(same & (before == order), at, found)
            before = before + same.astype(jnp.int32)
        return found

    def order(self, device):
        kinds = self.refs.kinds
        kind = kinds[device]
        before = jnp.int32(0)
        for at in range(self.count):
            before = before + ((kinds[at] == kind) & (at < device)).astype(jnp.int32)
        return before

    def unpack(self, t, consume):
        r = self.refs
        work, rows, planes = r.work, self.rows, self.planes
        full = SH * SW * C0 // LANES
        gath = r.gathc if t else r.gathx

        @pl.when(self.core == 0)
        def _():
            for at in range(self.large):
                block = gath[self.member(1, at)]
                work[at * ROWS : (at + 1) * ROWS] = block.astype(jnp.float32)

        @pl.when(self.core == 1)
        def _():
            for at in range(self.small):
                block = gath[self.member(0, at), 0:full]
                work[at * full : (at + 1) * full] = block.astype(jnp.float32)
            work[self.small * full : self.large * ROWS] = jnp.zeros(
                (self.large * ROWS - self.small * full, LANES), jnp.float32
            )

        deep = self.large * ROWS // 2
        right = jnp.concatenate([work[pl.ds(j, deep, stride=2)] for j in range(2)], axis=1)
        right = right.astype(jnp.bfloat16)
        cells = Cells(self.core, (rows, LANES), self.small, self.large)
        base = cells.crop * cells.pick(ROWS // 2, full // 2)
        base = base + cells.along * (planes * cells.wide) + cells.across
        base = jnp.where(cells.valid, base, -(1 << 20))
        lane = lax.broadcasted_iota(jnp.int32, (rows, LANES), 1)
        chunk = min(planes, 4)

        def body(step):
            pieces = []
            for q in range(chunk):
                goal = base + (step * chunk + q) * cells.wide
                pieces.append(one_hot(goal, lane, deep))
            left = pieces[0] if chunk == 1 else jnp.concatenate(pieces, axis=0)
            result = lax.dot_general(left, right, DOWN, preferred_element_type=jnp.float32)
            for q in range(chunk):
                for tile in range(2):
                    value = result[q * rows : (q + 1) * rows, tile * LANES : (tile + 1) * LANES]
                    consume(tile, step * chunk + q, value)

        planes_loop(planes // chunk, body)

    def pack_size(self):
        return 48 * self.planes, -(-self.planes * self.rows // LANES) * LANES

    def plan_pack(self):
        r = self.refs
        high, deep = self.pack_size()
        planes = self.planes
        q = lax.broadcasted_iota(jnp.int32, (high, LANES), 0)
        lane = lax.broadcasted_iota(jnp.int32, (high, LANES), 1)
        wide, tall = jnp.where(self.core == 0, 6, 3), jnp.where(self.core == 0, 8, 4)
        cell = jnp.where(self.core == 0, (q * 43691) >> 18, (q * 43691) >> 17)
        across = q - cell * wide
        plane = cell & (planes - 1)
        along = cell >> log2(planes)
        base = plane * self.rows + along * wide + across
        base = jnp.where(along < tall, base, -(1 << 20))
        shard = lax.axis_index("crops")
        for at, device in enumerate((shard, shard + 1 - 2 * self.core)):
            goal = base + self.order(device) * (wide * tall)
            r.hot[at, 0:high, 0:deep] = one_hot(goal, lane, deep)

    def pack(self, units, put):
        high, deep = self.pack_size()
        right = jnp.concatenate([units(tile) for tile in range(2)], axis=1)
        short = deep - right.shape[0]
        parts = [right.astype(jnp.bfloat16)]
        if right.dtype == jnp.float32:
            parts.append((right - parts[0].astype(jnp.float32)).astype(jnp.bfloat16))
        if short:
            empty = jnp.zeros((short, 2 * LANES), jnp.bfloat16)
            parts = [jnp.concatenate([part, empty], axis=0) for part in parts]
        for at in range(2):
            total = None
            for part in parts:
                piece = lax.dot_general(
                    self.refs.hot[at, 0:high, 0:deep],
                    part,
                    DOWN,
                    preferred_element_type=jnp.float32,
                )
                total = piece if total is None else total + piece
            for tile in range(2):
                put(at, pl.ds(tile, high, stride=2), total[:, tile * LANES : (tile + 1) * LANES])

    def pack_outputs(self):
        r = self.refs
        high = 2 * self.pack_size()[0]

        def put(at, where, value):
            r.work[pl.ds(at * ROWS + where.start, where.size, stride=2)] = value

        def units(tile):
            block = r.outs[tile * self.planes : (tile + 1) * self.planes]
            return block.reshape(self.planes * self.rows, LANES)

        self.pack(units, put)
        for at in range(2):
            r.blocks[at, 0:high] = r.work[at * ROWS : at * ROWS + high].astype(jnp.bfloat16)
            if high < ROWS:
                r.blocks[at, high:ROWS] = jnp.zeros((ROWS - high, LANES), jnp.bfloat16)

    def pack_gradient(self):
        r = self.refs
        high = 2 * self.pack_size()[0]

        def put(at, where, value):
            r.slopes[at, where] = value

        def units(tile):
            block = r.gin[tile * self.planes : (tile + 1) * self.planes]
            return block.reshape(self.planes * self.rows, LANES)

        self.pack(units, put)
        if high < ROWS:
            for at in range(2):
                r.slopes[at, high:ROWS] = jnp.zeros((ROWS - high, LANES), jnp.float32)

    def forward(self, m, gather):
        steps = iter(range(1, 4))

        def also():
            step = next(steps, None)
            if step is not None:

                @pl.when(m == 0)
                def _():
                    gather.step(1, step)

        self.conv(m, self.units["a"])
        self.apply_a(m)
        also()
        self.conv(m, self.units["b"])
        self.apply_b(m)
        also()
        for name in ("d", "u", "e", "f", "g"):
            if name in self.units:
                self.conv(m, self.units[name])
                self.apply_rest(m, self.units[name])
                also()
        for _ in range(3):
            also()

        @pl.when(m == MODULES - 1)
        def _():
            gather.collect(1)
            self.unpack(1, self.take_cotangent)
            self.plan_pack()

        self.settle(m)
        self.receive(m)


    def send_back(self, m):
        r = self.refs
        s, gin, gt, sb = r.s, r.gin, r.gt, r.sb
        e = MODULES + m

        def body(plane):
            for tile in range(2):
                at = tile * self.planes + plane
                value = gin[at] * slope_of(s[m * 2 * self.planes + at])
                gt[at] = value
                for other in range(self.k):
                    sb[message_slot(self.k, other) + at] = value.astype(jnp.bfloat16)

        planes_loop(self.planes, body, TURNS)
        for other in reversed(self.others()):
            if other > self.k:
                count = 8 >> other
                wide = 1 << (other - self.k)

                def pool(plane):
                    for tile in range(2):
                        total = gt[tile * self.planes + plane * wide]
                        for step in range(1, wide):
                            total = total + gt[tile * self.planes + plane * wide + step]
                        slot = message_slot(self.k, other) + tile * count + plane
                        sb[slot] = total.astype(jnp.bfloat16)

                planes_loop(count, pool, TURNS)
            self.message(e, other).start()

    def back_unit(self, m, unit):
        r = self.refs
        st, dyb, z = r.st, r.dyb, getattr(r, "z" + unit.name)
        name, planes, tiles = unit.name, unit.planes, unit.tiles
        e = MODULES + m
        sums = {}

        def upstream(seg, tile, plane, normed):
            at = tile * planes + plane
            if name == "b":
                hf = r.hf[m * 2 * planes + at]
                value = r.gt[at] * slope_of(normed + hf)
                r.gin[at] = value
                return value
            if name == "a":
                return r.gu[at] * slope_of(normed)
            if seg.chain:
                return self.grads[seg.chain][at] * slope_of(normed)
            return r.rb[e * 16 + message_slot(self.k, seg.dest) + at].astype(jnp.float32)

        for seg in unit.segs:

            def body(plane, carry):
                result = []
                for tile in range(seg.tiles):
                    at = (seg.tile + tile) * planes + plane
                    where = m * STATS + unit.stat + seg.tile + tile
                    value = z[m * tiles * planes + at]
                    normed = value * st[where, 2:3] + st[where, 3:4]
                    dy = upstream(seg, tile, plane, normed)
                    dyb[at] = dy
                    zhat = (value - st[where, 0:1]) * st[where, 1:2]
                    result.append(carry[2 * tile] + partial_sum(dy))
                    result.append(carry[2 * tile + 1] + partial_sum(dy * zhat))
                return tuple(result)

            zero = jnp.zeros((8, LANES), jnp.float32)
            found = planes_sum(planes, body, (zero,) * (2 * seg.tiles), TURNS)
            pair = [
                jnp.concatenate([found[2 * tile + which] for tile in range(seg.tiles)], axis=1)
                for which in range(2)
            ]
            plain = SimpleNamespace(**vars(seg))
            plain.tile = 0
            totals = self.fold(plain, pair)
            self.table_grads(m, seg, totals)
            sums[seg.slot] = totals
        dz = self.dz_planes(unit)
        for seg in unit.segs:
            scale = self.per_cell(unit, seg)
            totals = sums[seg.slot]

            def apply(plane):
                for tile in range(seg.tiles):
                    at = (seg.tile + tile) * planes + plane
                    where = m * STATS + unit.stat + seg.tile + tile
                    zhat = (z[m * tiles * planes + at] - st[where, 0:1]) * st[where, 1:2]
                    inner = dyb[at] - totals[0][tile] * scale - zhat * (totals[1][tile] * scale)
                    dz.store(0, seg.tile + tile, plane, inner * st[where, 2:3] * self.masks[0])

            planes_loop(planes, apply, TURNS)
        self.back_data(m, unit, dz)
        first = min(seg.off for seg in unit.segs)
        last = max(seg.off + seg.taps**2 * seg.cin * seg.cout // LANES for seg in unit.segs)
        wanted = (self.quarter * self.share < last) & ((self.quarter + 1) * self.share > first)

        @pl.when(wanted)
        def _():
            self.back_kernel(m, unit, dz)

    def dz_planes(self, unit):
        r = self.refs
        mode = {"p1": "p", "s2": "dz2", "s1": "wide" if self.k == 3 else "s1"}[unit.kind]
        return Planes(
            mode,
            unit.tiles,
            unit.planes,
            self.masks,
            self.rows,
            r.dC,
            r.dE,
            r.dR,
        )

    def table_grads(self, m, seg, totals):
        gg = self.refs.gg
        slot = seg.slot
        for which, found in ((0, totals[1]), (1, totals[0])):
            if seg.cout > LANES:
                for tile in range(2):
                    gg[m, which, slot : slot + 1, tile * LANES : (tile + 1) * LANES] = found[tile]
            else:
                row = jnp.broadcast_to(found[0], (8, LANES))
                if seg.cout < LANES:
                    row = self.keep(row, seg.cout, [0])
                gg[m, which, slot : slot + 1, 0:LANES] = row[0:1]

    def wide_rows(self, ref, at, tiles, plane, count):
        pieces = [
            ref[pl.ds(at(0, tile, plane), count)].reshape(count * self.rows, LANES)
            for tile in range(tiles)
        ]
        return pieces[0] if tiles == 1 else jnp.concatenate(pieces, axis=1)

    def back_data(self, m, unit, dz):
        r = self.refs
        kind, tiles = unit.kind, unit.tiles
        target = getattr(r, "T" + unit.name)
        lanes = tiles * LANES
        rows = self.rows

        def kernel_rows(d, first, count):
            return target[m * unit.depth + d, first : first + count, 0:lanes]

        def product(left, right):
            return lax.dot_general(left, right, ACROSS, preferred_element_type=jnp.float32)

        def put(ref, tile, planes, first, count, value, step=1, add=False):
            block = value.reshape(count, rows, LANES)
            for q in range(count):
                at = tile * planes + first + q * step
                ref[at] = ref[at] + block[q] if add else block[q]

        planes = unit.planes
        if kind == "s1":
            goal = r.gu if unit.name == "b" else r.gin
            add = unit.name == "a"
            chunk = min(planes, 4)
            across = getattr(r, "T" + unit.name + unit.name)

            def body(step):
                first = step * chunk
                if self.k == 3:
                    total = None
                    for d in range(3):
                        for ref, at in ((dz.right, 0), (dz.main, 256), (dz.edge, 512)):
                            left = self.wide_rows(ref, dz.at, 2, first + 1 - d, chunk)
                            piece = product(left, kernel_rows(d, at, 256))
                            total = piece if total is None else total + piece
                else:
                    left = [
                        self.wide_rows(ref, dz.at, 2, first + 1 - d, chunk)
                        for d in range(3)
                        for ref in (dz.main, dz.edge)
                    ]
                    right = [across[m * 3 + d] for d in range(3)]
                    total = product(
                        jnp.concatenate(left, axis=1), jnp.concatenate(right, axis=1)
                    )
                for tile in range(2):
                    put(
                        goal,
                        tile,
                        planes,
                        first,
                        chunk,
                        total[:, tile * LANES : (tile + 1) * LANES],
                        add=add,
                    )

            planes_loop(planes // chunk, body)
            return
        if kind == "p1":
            left = self.wide_rows(dz.main, dz.at, tiles, 0, planes)
            total = product(left, kernel_rows(0, 0, 256))
            for tile in range(2):
                put(
                    r.gt,
                    tile,
                    planes,
                    0,
                    planes,
                    total[:, tile * LANES : (tile + 1) * LANES],
                    add=True,
                )
            return
        goal = self.grads[unit.source]
        add = unit.source == "t"
        lanes_in = unit.lanes_in
        count_in = unit.planes_in
        for parity, terms in ((0, [(1, 0)]), (1, [(2, 0), (0, 1)])):
            total, side = None, None
            for d, offset in terms:
                left = self.wide_rows(dz.main, dz.at, tiles, offset, planes)
                piece = product(left, kernel_rows(d, 0, lanes_in))
                total = piece if total is None else total + piece
                left = self.wide_rows(dz.edge, dz.at, tiles, offset, planes)
                piece = product(left, kernel_rows(d, lanes_in, LANES))
                side = piece if side is None else side + piece
            for tile in range(lanes_in // LANES):
                value = total[:, tile * LANES : (tile + 1) * LANES]
                if tile == lanes_in // LANES - 1:
                    value = value + side
                put(goal, tile, count_in, parity, planes, value, step=2, add=add)

    def back_kernel(self, m, unit, dz):
        r = self.refs
        G = r.work
        tiles, planes = unit.tiles, unit.planes
        source = self.maps[unit.source]
        right = self.wide_rows(dz.main, dz.at, tiles, 0, planes)

        def rows_for(d):
            found = []
            for part in self.parts(unit, source):
                found.append(self.rows_of(unit, part, m, d, 0, planes))
            return found

        if self.k < 3:
            pieces = [piece for d in range(unit.depth) for part in rows_for(d) for piece in part]
            left = jnp.concatenate(pieces, axis=1)
            result = lax.dot_general(right, left, ALONG, preferred_element_type=jnp.float32)
            lanes = tiles * LANES
            for at in range(len(pieces)):
                G[at * lanes : (at + 1) * lanes] = result[:, at * LANES : (at + 1) * LANES]
            for seg in unit.segs:
                self.fold_across(unit, seg)
            return

        def gather(d):
            at = 0
            for pieces in rows_for(d):
                left = pieces[0] if len(pieces) == 1 else jnp.concatenate(pieces, axis=1)
                count = left.shape[1]
                result = lax.dot_general(left, right, ALONG, preferred_element_type=jnp.float32)
                for tile in range(tiles):
                    row = pl.multiple_of((d * tiles + tile) * unit.rows + at, 8)
                    G[pl.ds(row, count)] = result[:, tile * LANES : (tile + 1) * LANES]
                at += count

        planes_loop(unit.depth, gather)
        for seg in unit.segs:
            self.fold_kernel(m, unit, seg)

    def fold_across(self, unit, seg):
        r = self.refs
        G, rep, pile, wgv = r.work, r.rep, r.pile, r.wgv
        cin, cout, lanes = seg.cin, seg.cout, unit.tiles * LANES
        width = 3 if seg.taps == 3 else 1
        taps = width * width
        found = links(self.k, unit, seg)
        blocks = seg.tiles * LANES // cout
        for d in range(unit.depth):
            for column in range(width):
                total = None
                for row, which, wanted in found:
                    if which != column:
                        continue
                    tile, within = divmod(d * unit.rows + row, LANES)
                    for block in range(blocks):
                        if block % seg.blocks not in wanted:
                            continue
                        at = tile * lanes + seg.tile * LANES + block * cout
                        piece = self.keep(G[at : at + cout], cin, [within // cin])
                        total = piece if total is None else total + piece
                at = (d * width + column) * cout
                pile[at : at + cout] = self.spread(total, cin)
        off = seg.off
        for first in range(0, taps * cout, LANES):
            turned = jnp.transpose(pile[first : first + LANES])[0:cin]
            if cout > LANES:
                tap, half = divmod(first // LANES, 2)
                wgv[pl.ds(off + tap * (2 * cin) + half, cin, stride=2)] = turned
            elif cout == LANES:
                tap = first // LANES
                wgv[off + tap * cin : off + (tap + 1) * cin] = turned
            else:
                for block in range(LANES // cout):
                    tap = first // cout + block
                    if tap < taps:
                        value = self.spread(self.keep(turned, cout, [block]), cout)
                        rep[tap * cin : (tap + 1) * cin] = value
        if cout < LANES:
            ratio = LANES // cout
            count = taps * cin // ratio
            total = None
            for part in range(ratio):
                piece = self.keep(rep[pl.ds(part, count, stride=ratio)], cout, [part])
                total = piece if total is None else total + piece
            wgv[off : off + count] = total

    def fold_kernel(self, m, unit, seg):
        r = self.refs
        G, rep, wgv = r.work, r.rep, r.wgv
        cin, cout, tiles = seg.cin, seg.cout, unit.tiles
        width = 3 if seg.taps == 3 else 1
        found = links(self.k, unit, seg)
        off = seg.off

        def fold(d):
            for column in range(width):
                tap = d * width + column
                totals = []
                for tile in range(seg.tiles):
                    total = None
                    for row, which, wanted in found:
                        if which != column:
                            continue
                        at = pl.multiple_of((d * tiles + seg.tile + tile) * unit.rows + row, 8)
                        piece = G[pl.ds(at, cin)]
                        if cout <= LANES:
                            local = self.local_blocks(seg, tile, wanted)
                            if not local:
                                continue
                            piece = self.keep(piece, cout, local)
                        total = piece if total is None else total + piece
                    totals.append(total)
                if cout > LANES:
                    for tile in range(2):
                        wgv[pl.ds(off + tap * (2 * cin) + tile, cin, stride=2)] = totals[tile]
                    continue
                total = None
                for piece in totals:
                    if piece is not None:
                        total = piece if total is None else total + piece
                if cout == LANES:
                    wgv[pl.ds(pl.multiple_of(off + tap * cin, 8), cin)] = total
                else:
                    rep[pl.ds(pl.multiple_of(tap * cin, cin), cin)] = self.spread(total, cout)

        planes_loop(unit.depth, fold)
        if cout < LANES:
            ratio = LANES // cout
            count = width * width * cin // ratio
            total = None
            for part in range(ratio):
                piece = self.keep(rep[pl.ds(part, count, stride=ratio)], cout, [part])
                total = piece if total is None else total + piece
            wgv[off : off + count] = total

    def backward(self, m):
        e = MODULES + m
        self.send_back(m)
        for name in ("g", "f", "e", "d", "u"):
            if name in self.units:
                for seg in self.units[name].segs:
                    if seg.dest >= 0:
                        self.arrived(e, seg.dest).wait_recv()
                self.back_unit(m, self.units[name])
        for other in self.others():
            self.message(e, other).wait_send()
        self.back_unit(m, self.units["b"])
        self.back_unit(m, self.units["a"])


STATS = 20
TURNS = 8
NAMES = list(
    dict(x=0, cot=0, w=0, gains=0, shifts=0, kinds=0, out=0, grad=0, wg=0, gain=0, shift=0)
)


def one_hot(goal, lane, deep):
    pieces = [
        jnp.where(goal == lane + first, 1.0, 0.0).astype(jnp.bfloat16)
        for first in range(0, deep, LANES)
    ]
    return jnp.concatenate(pieces, axis=1)


class Cells:
    def __init__(self, core, shape, small, large):
        self.core = core
        row = lax.broadcasted_iota(jnp.int32, shape, 0)
        self.wide = self.pick(LW // 8, SW // 8)
        tall = self.pick(LH // 8, SH // 8)
        self.crop = self.pick((row * 43691) >> 21, (row * 43691) >> 19)
        inner = row - self.crop * (self.wide * tall)
        self.along = self.pick((inner * 43691) >> 18, (inner * 43691) >> 17)
        self.across = inner - self.along * self.wide
        self.valid = self.crop < self.pick(large, small)
        self.last = tall - 1

    def pick(self, large, small):
        return jnp.where(self.core == 0, large, small)


def fill_masks(refs, rows, core, small, large):
    cells = Cells(core, (rows, LANES), small, large)
    valid = cells.valid
    six = cells.wide == 6
    up, down = valid & (cells.along > 0), valid & (cells.along < cells.last)
    tables = (
        valid,
        valid & (cells.across > 0),
        valid & (cells.across < cells.wide - 1),
        up & six,
        up & jnp.logical_not(six),
        down & six,
        down & jnp.logical_not(six),
    )
    for at, table in enumerate(tables):
        refs.masks[at] = jnp.where(table, 1.0, 0.0)


class Gather:
    def __init__(self, refs, core, count):
        self.refs, self.core, self.count = refs, core, count
        self.z = lax.axis_index("crops") // 2
        self.last = count // 2 - 1

    def hop(self, t, source, right):
        r = self.refs
        at = source * 2 + self.core
        gath = r.gathc if t else r.gathx
        to = self.z + 1 if right else self.z - 1
        return pltpu.make_async_remote_copy(
            src_ref=gath.at[at],
            dst_ref=gath.at[at],
            send_sem=r.hsem.at[(t * (self.last + 1) + source) * 3 + (0 if right else 1)],
            recv_sem=r.gsem.at[t * self.count + at],
            device_id=dict(crops=to * 2 + self.core),
            device_id_type=pl.DeviceIdType.MESH,
        )

    def across(self, t, source, core, rows):
        r = self.refs
        at = source * 2 + core
        gath = r.gathc if t else r.gathx
        return pltpu.make_async_remote_copy(
            src_ref=gath.at[at, pl.ds(0, rows)],
            dst_ref=gath.at[at, pl.ds(0, rows)],
            send_sem=r.hsem.at[(t * (self.last + 1) + source) * 3 + 2],
            recv_sem=r.gsem.at[t * self.count + at],
            device_id=dict(crops=self.z * 2 + 1 - self.core),
            device_id_type=pl.DeviceIdType.MESH,
        )

    def each_core(self, action):
        for core, rows in ((0, SH * SW * C0 // LANES), (1, ROWS)):

            @pl.when(self.core == core)
            def _():
                action(core, rows)

    def send(self, t, source, rightward, leftward):
        if rightward:

            @pl.when(self.z < self.last)
            def _():
                self.hop(t, source, True).start()

        if leftward:

            @pl.when(self.z > 0)
            def _():
                self.hop(t, source, False).start()

        self.each_core(lambda core, rows: self.across(t, source, core, rows).start())

    def step(self, t, s):
        r = self.refs
        if s == 0:
            at = self.z * 2 + self.core
            if t:
                r.gathc[at] = r.cot[...]
            else:
                r.gathx[at] = r.x[...]
            self.send(t, self.z, True, True)
            return

        @pl.when(self.z >= s)
        def _():
            self.hop(t, self.z - s, True).wait_recv()
            self.send(t, self.z - s, True, False)

        @pl.when(self.z + s <= self.last)
        def _():
            self.hop(t, self.z + s, True).wait_recv()
            self.send(t, self.z + s, False, True)

    def collect(self, t):
        for source in range(self.last + 1):
            for core, rows in ((0, ROWS), (1, SH * SW * C0 // LANES)):

                @pl.when(self.core == core)
                def _():
                    self.across(t, source, 1 - core, rows).wait_recv()

    def finish(self, t):
        def sent(source, rightward, leftward):
            if rightward:

                @pl.when(self.z < self.last)
                def _():
                    self.hop(t, source, True).wait_send()

            if leftward:

                @pl.when(self.z > 0)
                def _():
                    self.hop(t, source, False).wait_send()

            self.each_core(lambda core, rows: self.across(t, source, core, rows).wait_send())

        sent(self.z, True, True)
        for s in range(1, self.last + 1):

            @pl.when(self.z >= s)
            def _():
                sent(self.z - s, True, False)

            @pl.when(self.z + s <= self.last)
            def _():
                sent(self.z + s, False, True)


def scratch_table(rows, weight_rows, count):
    def half(many):
        return pltpu.VMEM((many, rows, LANES), jnp.bfloat16)

    def full(many):
        return pltpu.VMEM((many, rows, LANES), jnp.float32)

    def expanded(depth, deep, wide):
        return pltpu.VMEM((MODULES * depth, deep, wide), jnp.bfloat16)

    _, span, _ = pair_rows(weight_rows, count)
    return dict(
        masks=full(MASKS),
        hC=half(2 * 20),
        hE=half(2 * 20),
        hR=half(2 * 6),
        uC=half(2 * 20),
        uE=half(2 * 20),
        uR=half(2 * 6),
        tC=half(2 * 18),
        tE=half(2 * 9),
        c1C=half(2 * 5),
        c1E=half(2 * 5),
        c2C=half(2 * 5),
        c2E=half(2 * 5),
        c3C=half(2 * 3),
        c3E=half(2 * 3),
        dC=half(20),
        dE=half(20),
        dR=half(6),
        outs=half(16),
        hf=full(2 * 16),
        s=full(2 * 16),
        za=full(2 * 16),
        zb=full(2 * 16),
        zd=full(2 * 16),
        zu=full(2 * 8),
        ze=full(2 * 4),
        zf=full(2 * 2),
        zg=full(2 * 2),
        gt=full(16),
        gu=full(16),
        gin=full(16),
        gc1=full(4),
        gc2=full(4),
        gc3=full(2),
        dyb=full(16),
        sb=half(16),
        rb=half(4 * 16),
        st=pltpu.VMEM((MODULES * STATS, 8, LANES), jnp.float32),
        Ta=expanded(3, 768, 256),
        Tb=expanded(3, 768, 256),
        Taa=expanded(3, 256, 512),
        Tbb=expanded(3, 256, 512),
        Td=expanded(3, 384, 512),
        Tu=expanded(1, 256, 768),
        Te=expanded(3, 256, 256),
        Tf=expanded(3, 256, 128),
        Tg=expanded(3, 256, 256),
        raw=pltpu.VMEM((2, 3072, LANES), jnp.bfloat16),
        work=pltpu.VMEM((4608, LANES), jnp.float32),
        rep=pltpu.VMEM((640, LANES), jnp.float32),
        pile=pltpu.VMEM((2304, LANES), jnp.float32),
        wgv=pltpu.VMEM((weight_rows, LANES), jnp.float32),
        wq=pltpu.VMEM((MODULES, 2 * weight_rows // count, LANES), jnp.float32),
        wr=pltpu.VMEM((MODULES, span, LANES), jnp.float32),
        gathx=pltpu.VMEM((count, ROWS, LANES), jnp.bfloat16),
        gathc=pltpu.VMEM((count, ROWS, LANES), jnp.bfloat16),
        hot=pltpu.VMEM((2, 384, 768), jnp.bfloat16),
        blocks=pltpu.VMEM((2, ROWS, LANES), jnp.bfloat16),
        slopes=pltpu.VMEM((2, ROWS, LANES), jnp.float32),
        blockr=pltpu.VMEM((ROWS, LANES), jnp.bfloat16),
        sloper=pltpu.VMEM((ROWS, LANES), jnp.float32),
        gg=pltpu.VMEM((MODULES, 2, SLOTS, 256), jnp.float32),
        ggr=pltpu.VMEM((MODULES, 2, SLOTS, 256), jnp.float32),
        wsem=pltpu.SemaphoreType.DMA((2,)),
        ssem=pltpu.SemaphoreType.DMA((16,)),
        rsem=pltpu.SemaphoreType.DMA((16,)),
        hsem=pltpu.SemaphoreType.DMA((3 * count,)),
        gsem=pltpu.SemaphoreType.DMA((2 * count,)),
        psem=pltpu.SemaphoreType.DMA((5,)),
        qsem=pltpu.SemaphoreType.DMA((5,)),
        osem=pltpu.SemaphoreType.DMA((1,)),
    )


def pair_rows(weight_rows, count):
    share = weight_rows // count
    low = share // 8 * 8
    return share, 2 * share - low, low


def greet(core, count):
    barrier = pltpu.get_barrier_semaphore()
    me, shard = lax.axis_index("branch"), lax.axis_index("crops")
    z = shard // 2

    def signal(**where):
        pl.semaphore_signal(barrier, inc=1, device_id=where, device_id_type=pl.DeviceIdType.MESH)

    for step in range(1, 4):
        signal(branch=lax.rem(me + step, 4))
    signal(crops=shard + 1 - 2 * core)

    @pl.when(z > 0)
    def _():
        signal(crops=shard - 2)

    @pl.when(z < count // 2 - 1)
    def _():
        signal(crops=shard + 2)

    ends = (z == 0).astype(jnp.int32) + (z == count // 2 - 1).astype(jnp.int32)
    pl.semaphore_wait(barrier, 6 - ends)


def whole_kernel(names, rows, large, small, *args):
    refs = SimpleNamespace(**dict(zip(names, args)))
    count = large + small
    me, shard = lax.axis_index("branch"), lax.axis_index("crops")
    core = shard % 2
    weight_rows = refs.wgv.shape[0]
    share, span, low = pair_rows(weight_rows, count)
    quarter = pl.multiple_of(shard // 2 * (2 * share), 8)

    class Lazy:
        def __getitem__(self, index):
            return refs.masks[index]

    def across(source, goal, index):
        return pltpu.make_async_remote_copy(
            src_ref=source,
            dst_ref=goal,
            send_sem=refs.psem.at[index],
            recv_sem=refs.qsem.at[index],
            device_id=dict(crops=shard + 1 - 2 * core),
            device_id_type=pl.DeviceIdType.MESH,
        )

    def kernel_pair(m):
        at = pl.multiple_of(low * (1 - core), 8)
        return across(refs.wq.at[m, pl.ds(at, span)], refs.wr.at[m], m)

    outputs_pair = across(refs.blocks.at[1], refs.blockr, 2)
    gradient_pair = across(refs.slopes.at[1], refs.sloper, 3)
    table_pair = across(refs.gg, refs.ggr, 4)
    gather = Gather(refs, core, count)

    def every(action):
        for k in range(4):

            @pl.when(me == k)
            def _():
                action(Branch(k, rows, large, small, 2 * share, refs, Lazy(), core))

    def begin(branch):
        branch.fetch(0, 0).start()

    def prepare(branch):
        found = branch.segments()
        stops = {0: 1, min(2, len(found) - 2): 2, len(found) - 1: 3}
        for index, (unit, seg) in enumerate(found):
            branch.expand(index)
            if index in stops:
                gather.step(0, stops[index])

    def main(branch):
        branch.unpack(0, branch.take_feature)
        branch.maps["h"].close(0)
        gather.step(1, 0)

        def ahead(m, carry):
            branch.forward(m, gather)
            return carry

        def back(step, carry):
            m = MODULES - 1 - step
            branch.backward(m)
            refs.wq[m] = refs.wgv[pl.ds(quarter, 2 * share)]
            kernel_pair(m).start()
            return carry

        lax.fori_loop(0, MODULES, ahead, 0)
        branch.pack_outputs()
        outputs_pair.start()
        lax.fori_loop(0, MODULES, back, 0)
        branch.pack_gradient()
        gradient_pair.start()
        table_pair.start()

    every(begin)
    greet(core, count)
    gather.step(0, 0)
    fill_masks(refs, rows, core, small, large)
    refs.wgv[pl.ds(quarter, 2 * share)] = jnp.zeros((2 * share, LANES), jnp.float32)
    refs.gg[...] = jnp.zeros(refs.gg.shape, jnp.float32)
    every(prepare)
    gather.collect(0)
    every(main)

    for step in range(MODULES):
        m = MODULES - 1 - step
        kernel_pair(m).wait()
        mine = refs.wq[m, pl.ds(pl.multiple_of(low * core, 8), span)]
        refs.work[pl.ds(m, span, stride=MODULES)] = mine + refs.wr[m]
    skip = pl.multiple_of(core * (MODULES * (share - low)), 8)
    leave = pltpu.make_async_copy(
        refs.work.at[pl.ds(skip, MODULES * share)], refs.wg, refs.osem.at[0]
    )
    leave.start()
    outputs_pair.wait()
    gradient_pair.wait()
    table_pair.wait()
    own = refs.kinds[shard] != core
    refs.out[...] = jnp.where(own, refs.blocks[0].astype(jnp.float32), refs.blockr[...].astype(jnp.float32)).astype(jnp.bfloat16)
    refs.grad[...] = jnp.where(own, refs.slopes[0], refs.sloper[...])
    width = 256 // count
    for which, goal in ((0, refs.gain), (1, refs.shift)):
        for m in range(MODULES):
            total = refs.gg[m, which] + refs.ggr[m, which]
            found = None
            for at in range(count):
                piece = jnp.where(shard == at, total[:, at * width : (at + 1) * width], 0.0)
                found = piece if found is None else found + piece
            goal[m] = found
    gather.finish(0)
    gather.finish(1)
    leave.wait()


def whole_call(rows, large, small, x, cot, w, gains, shifts, kinds):
    count = large + small
    weight_rows = w.shape[0] // MODULES
    table = scratch_table(rows, weight_rows, count)
    vmem = pl.BlockSpec(memory_space=pltpu.VMEM)
    hbm = pl.BlockSpec(memory_space=pl.ANY)
    smem = pl.BlockSpec(memory_space=pltpu.SMEM)
    tables = jax.ShapeDtypeStruct((MODULES, SLOTS, 256 // count), jnp.float32)
    return pl.pallas_call(
        partial(whole_kernel, NAMES + list(table), rows, large, small),
        out_shape=(
            jax.ShapeDtypeStruct((ROWS, LANES), jnp.bfloat16),
            jax.ShapeDtypeStruct((ROWS, LANES), jnp.float32),
            jax.ShapeDtypeStruct((MODULES * weight_rows // count, LANES), jnp.float32),
            tables,
            tables,
        ),
        in_specs=[vmem, vmem, hbm, vmem, vmem, smem],
        out_specs=(vmem, vmem, hbm, vmem, vmem),
        scratch_shapes=list(table.values()),
        compiler_params=pltpu.CompilerParams(
            collective_id=0, has_side_effects=True, vmem_limit_bytes=62 * 1024 * 1024
        ),
    )(x, cot, w, gains, shifts, kinds)


def leave_kernel(*refs):
    for source, goal in zip(refs[:5], refs[5:]):
        goal[...] = source[...]


def leave_call(arrays):
    vmem = pl.BlockSpec(memory_space=pltpu.VMEM)
    return pl.pallas_call(
        leave_kernel,
        out_shape=tuple(jax.ShapeDtypeStruct(array.shape, array.dtype) for array in arrays),
        in_specs=[vmem] * 5,
        out_specs=(vmem,) * 5,
    )(*arrays)


def on_device_grouped(features, weights, gains, shifts, cotangent, size_group):
    count = lax.axis_size("crops")
    large = count // 4
    weight_rows = weights.shape[2] // LANES
    results = whole_call(
        group_rows(count),
        large,
        count - large,
        features[0],
        cotangent[0],
        weights[0]
        .reshape(MODULES, weight_rows, LANES)
        .transpose(1, 0, 2)
        .reshape(MODULES * weight_rows, LANES),
        gains[0],
        shifts[0],
        size_group,
    )
    out, grad, weight_grad, gain, shift = leave_call(results)
    share = weight_rows // count
    weight_grad = weight_grad.reshape(share, MODULES, LANES).transpose(1, 0, 2)
    weight_grad = with_layout_constraint(weight_grad, Layout((1, 0, 2)))
    return (
        out[None],
        grad[None],
        weight_grad.reshape(1, MODULES, share * LANES),
        gain[None],
        shift[None],
    )


def group_rows(count):
    large = count // 4
    rows = max(large * (LH // 8) * (LW // 8), (count - large) * (SH // 8) * (SW // 8))
    return -(-rows // 16) * 16


def fits(count):
    return count % 8 == 0 and group_rows(count) <= 96


def solution(mesh):
    placed = (
        P("branch", "crops", None),
        P("branch", None, None),
        P("branch", None, None, None),
        P("branch", None, None, None),
        P("branch", "crops", None),
        P(),
    )
    return jax.shard_map(
        on_device_grouped if fits(mesh.shape["crops"]) else on_device,
        mesh=mesh,
        in_specs=placed,
        out_specs=(
            P("branch", "crops", None),
            P("branch", "crops", None),
            P("branch", None, "crops"),
            P("branch", None, None, "crops"),
            P("branch", None, None, "crops"),
        ),
        check_vma=False,
    )
```

```python
from functools import partial
from types import SimpleNamespace
import math

import jax
import jax.numpy as jnp
import numpy as np
from jax import lax
from jax.experimental import pallas as pl
from jax.experimental.layout import Layout, with_layout_constraint
from jax.experimental.pallas import tpu as pltpu
from jax.sharding import PartitionSpec as P

C0 = 32
BLOCKS = 1
MODULES = 2
CROPS_DEV = 1
SH = 32
SW = 24
LH = 64
LW = 48
ROWS = 768
MSG_ROWS = 384


EPS = 1e-05


def as_sent(x):

    def short(part):
        return part.astype(jnp.bfloat16) if part.dtype == jnp.float32 else part

    return jax.tree.map(short, x)


def sender_plan(branch_index, top_channels, blocks):
    channels = top_channels << branch_index
    operations = []
    for block_index in range(blocks):
        operations.append(
            SimpleNamespace(
                phase=2 * block_index,
                source=("h", block_index),
                level=branch_index,
                cin=channels,
                cout=channels,
                stride=1,
                taps=3,
                act="silu",
                output=("u", block_index),
                skip=None,
                dest=-1,
            )
        )
        operations.append(
            SimpleNamespace(
                phase=2 * block_index + 1,
                source=("u", block_index),
                level=branch_index,
                cin=channels,
                cout=channels,
                stride=1,
                taps=3,
                act="res",
                output=("h", block_index + 1),
                skip=("h", block_index),
                dest=-1,
            )
        )
    top_name = ("h", blocks)
    for target in range(branch_index):
        operations.append(
            SimpleNamespace(
                phase=2 * blocks,
                source=top_name,
                level=branch_index,
                cin=channels,
                cout=top_channels << target,
                stride=1,
                taps=1,
                act="none",
                output=None,
                skip=None,
                dest=target,
            )
        )
    for target in range(branch_index + 1, 4):
        for depth_step in range(1, target - branch_index + 1):
            is_last = depth_step == target - branch_index
            operations.append(
                SimpleNamespace(
                    phase=2 * blocks + depth_step - 1,
                    source=top_name if depth_step == 1 else ("chain", target, depth_step - 1),
                    level=branch_index + depth_step,
                    cin=channels,
                    cout=top_channels << target if is_last else channels,
                    stride=2,
                    taps=3,
                    act="none" if is_last else "silu",
                    output=None if is_last else ("chain", target, depth_step),
                    skip=None,
                    dest=target if is_last else -1,
                )
            )
    for position, operation in enumerate(operations):
        operation.slot = position
        operation.size = (
            operation.taps * operation.taps * operation.cin * operation.cout
        )
        if operation.taps == 1:
            operation.kshape = (operation.cin, operation.cout)
        else:
            operation.kshape = (3, 3, operation.cin, operation.cout)
    return operations


def phase_lengths(top_channels, blocks):
    phase_count = 2 * blocks + 3
    lengths = [0] * phase_count
    for branch_index in range(4):
        per_phase = [0] * phase_count
        for operation in sender_plan(branch_index, top_channels, blocks):
            per_phase[operation.phase] += operation.size
        lengths = [max(current, candidate) for current, candidate in zip(lengths, per_phase)]
    return lengths


def weighted_plan(branch_index, top_channels, blocks):
    lengths = phase_lengths(top_channels, blocks)
    starts = [sum(lengths[:phase_index]) for phase_index in range(len(lengths))]
    running = [0] * len(lengths)
    operations = sender_plan(branch_index, top_channels, blocks)
    for operation in operations:
        phase_index = operation.phase
        operation.inner = running[phase_index]
        operation.offset = starts[phase_index] + running[phase_index]
        operation.position = sum(
            (1 for earlier in operations[: operation.slot] if earlier.phase == phase_index)
        )
        running[phase_index] += operation.size
    return operations


def phase_operations(branch_index, phase_index):
    return [
        operation
        for operation in weighted_plan(branch_index, C0, BLOCKS)
        if operation.phase == phase_index
    ]


def input_names(operations):
    source_names = []
    for operation in operations:
        if operation.source not in source_names:
            source_names.append(operation.source)
    return source_names


def silu_slope(value):
    sigmoid = jax.nn.sigmoid(value)
    return sigmoid * (1.0 + value * (1.0 - sigmoid))


def crop_cells(size_kind):
    return (LH, LW) if size_kind else (SH, SW)


def map_dims(size_kind, level, channels):
    height, breadth = crop_cells(size_kind)
    return (CROPS_DEV, height >> level, breadth >> level, channels)


def source_dims(branch_index, size_kind, map_name):
    level = branch_index + map_name[2] if map_name[0] == "chain" else branch_index
    return map_dims(size_kind, level, C0 << branch_index)


def preact_dims(size_kind, operation):
    return map_dims(size_kind, operation.level, operation.cout)


def to_canvas(arrays, value_type):
    if not arrays:
        return jnp.zeros((ROWS, 128), value_type)
    flattened = jnp.concatenate([array.reshape(-1).astype(value_type) for array in arrays])
    return jnp.pad(flattened, (0, ROWS * 128 - flattened.shape[0])).reshape(ROWS, 128)


def from_canvas(canvas, dims_list):
    flattened = canvas.reshape(-1)
    pieces = []
    offset = 0
    for dims_entry in dims_list:
        count_here = math.prod(dims_entry)
        pieces.append(flattened[offset : offset + count_here].reshape(dims_entry))
        offset += count_here
    return pieces


def to_slot(array):
    flattened = array.reshape(-1)
    return jnp.pad(flattened, (0, MSG_ROWS * 128 - flattened.shape[0])).reshape(MSG_ROWS, 128)


def from_slot(slot_rows, dims_entry):
    return slot_rows.reshape(-1)[: math.prod(dims_entry)].reshape(dims_entry)


def upsample(message, factor):
    crop_count, height, breadth, channels = message.shape
    widened = jnp.broadcast_to(
        message[:, :, None, :, None, :], (crop_count, height, factor, breadth, factor, channels)
    )
    return widened.reshape(crop_count, height * factor, breadth * factor, channels)


def block_pool(array, factor):
    crop_count, height, breadth, channels = array.shape
    return array.reshape(
        crop_count, height // factor, factor, breadth // factor, factor, channels
    ).sum(axis=(2, 4))


def kernel_piece(module_weights, operation):
    start = operation.offset
    return module_weights[start : start + operation.size].reshape(operation.kshape)


def conv_forward(operation, source, kernel):
    if operation.taps == 1:
        return jnp.einsum("nhwc,cd->nhwd", source, kernel, preferred_element_type=jnp.float32)
    stride = operation.stride
    return lax.conv_general_dilated(
        source,
        kernel,
        (stride, stride),
        ((1, 1), (1, 1)),
        dimension_numbers=("NHWC", "HWIO", "NHWC"),
        preferred_element_type=jnp.float32,
    )


def conv_backward(operation, source, kernel, upstream):
    if operation.taps == 1:
        source_grad = jnp.einsum(
            "nhwd,cd->nhwc", upstream, kernel, preferred_element_type=jnp.float32
        )
        kernel_grad = jnp.einsum(
            "nhwc,nhwd->cd", source, upstream, preferred_element_type=jnp.float32
        )
        return (source_grad, kernel_grad)
    stride = operation.stride
    flipped = jnp.transpose(kernel[::-1, ::-1], (0, 1, 3, 2))
    high_pad = 2 if stride == 2 else 1
    source_grad = lax.conv_general_dilated(
        upstream,
        flipped,
        (1, 1),
        ((1, high_pad), (1, high_pad)),
        lhs_dilation=(stride, stride),
        dimension_numbers=("NHWC", "HWIO", "NHWC"),
        preferred_element_type=jnp.float32,
    )
    kernel_grad = lax.conv_general_dilated(
        source,
        upstream,
        (1, 1),
        ((1, 2 - stride), (1, 2 - stride)),
        rhs_dilation=(stride, stride),
        dimension_numbers=("CHWN", "IHWO", "NHWC"),
        preferred_element_type=jnp.float32,
    )
    return (source_grad, jnp.transpose(kernel_grad, (1, 2, 0, 3)))


def cell_total(counts, size_kind, level):
    height, breadth = crop_cells(size_kind)
    return counts[size_kind] * float(CROPS_DEV * (height >> level) * (breadth >> level))


def norm_terms(totals, counts, size_kind, operation):
    cells_here = cell_total(counts, size_kind, operation.level)
    channels = operation.cout
    position = operation.position
    average = totals[size_kind, 0, position, :channels] / cells_here
    variance = totals[size_kind, 1, position, :channels] / cells_here - average * average
    return (average, lax.rsqrt(variance + EPS))


def forward_conv(branch_index, size_kind, phase_index, source_canvas, module_weights):
    operations = phase_operations(branch_index, phase_index)
    source_names = input_names(operations)
    pieces = from_canvas(
        source_canvas, [source_dims(branch_index, size_kind, map_name) for map_name in source_names]
    )
    sources = {
        map_name: piece.astype(jnp.bfloat16) for map_name, piece in zip(source_names, pieces)
    }
    preacts = []
    totals = jnp.zeros((2, 2, 3, 8 * C0), jnp.float32)
    for operation in operations:
        preact = conv_forward(
            operation, sources[operation.source], kernel_piece(module_weights, operation)
        )
        preacts.append(preact)
        channels = operation.cout
        position = operation.position
        totals = totals.at[size_kind, 0, position, :channels].set(jnp.sum(preact, axis=(0, 1, 2)))
        totals = totals.at[size_kind, 1, position, :channels].set(
            jnp.sum(preact * preact, axis=(0, 1, 2))
        )
    return (to_canvas(preacts, jnp.float32), totals)


def forward_norm(
    branch_index,
    size_kind,
    phase_index,
    preact_canvas,
    totals,
    counts,
    module_gains,
    module_shifts,
    skip_canvas,
    message_buffer,
):
    operations = phase_operations(branch_index, phase_index)
    preacts = from_canvas(
        preact_canvas, [preact_dims(size_kind, operation) for operation in operations]
    )
    skip_map = from_canvas(skip_canvas, [map_dims(size_kind, branch_index, C0 << branch_index)])[0]
    produced = []
    for operation, preact in zip(operations, preacts):
        average, inverse_std = norm_terms(totals, counts, size_kind, operation)
        norm_slot = operation.slot
        channels = operation.cout
        normed = (preact - average) * inverse_std * module_gains[
            norm_slot, :channels
        ] + module_shifts[norm_slot, :channels]
        if operation.act == "silu":
            produced.append(jax.nn.silu(normed))
        elif operation.act == "res":
            produced.append(jax.nn.silu(normed + skip_map))
        else:
            message_buffer = message_buffer.at[operation.dest].set(
                to_slot(normed.astype(jnp.bfloat16))
            )
    return (to_canvas(produced, jnp.float32), message_buffer)


def receive_forward(branch_index, size_kind, top_canvas, received):
    channels = C0 << branch_index
    summed = from_canvas(top_canvas, [map_dims(size_kind, branch_index, channels)])[0]
    for sender in range(4):
        if sender < branch_index:
            summed = summed + from_slot(
                received[sender], map_dims(size_kind, branch_index, channels)
            ).astype(jnp.float32)
        elif sender > branch_index:
            coarse = from_slot(received[sender], map_dims(size_kind, sender, channels))
            summed = summed + upsample(coarse, 2 ** (sender - branch_index)).astype(jnp.float32)
    return (to_canvas([jax.nn.silu(summed)], jnp.float32), to_canvas([summed], jnp.float32))


def receive_backward(branch_index, size_kind, grad_canvas, summed_canvas):
    dims_here = map_dims(size_kind, branch_index, C0 << branch_index)
    upstream = from_canvas(grad_canvas, [dims_here])[0]
    summed = from_canvas(summed_canvas, [dims_here])[0]
    summed_grad = upstream * silu_slope(summed)
    buffer = jnp.zeros((4, MSG_ROWS, 128), jnp.bfloat16)
    for sender in range(4):
        if sender < branch_index:
            buffer = buffer.at[sender].set(to_slot(summed_grad.astype(jnp.bfloat16)))
        elif sender > branch_index:
            pooled = block_pool(summed_grad, 2 ** (sender - branch_index))
            buffer = buffer.at[sender].set(to_slot(pooled.astype(jnp.bfloat16)))
    return (to_canvas([summed_grad], jnp.float32), buffer)


def backward_stats(
    branch_index,
    size_kind,
    phase_index,
    dout_canvas,
    message_grads,
    preact_canvas,
    totals,
    counts,
    module_gains,
    module_shifts,
    skip_canvas,
):
    operations = phase_operations(branch_index, phase_index)
    preacts = from_canvas(
        preact_canvas, [preact_dims(size_kind, operation) for operation in operations]
    )
    producing = [operation for operation in operations if operation.act != "none"]
    output_grads = from_canvas(
        dout_canvas, [preact_dims(size_kind, operation) for operation in producing]
    )
    grads_by_name = {
        operation.output: piece for operation, piece in zip(producing, output_grads)
    }
    skip_map = from_canvas(skip_canvas, [map_dims(size_kind, branch_index, C0 << branch_index)])[0]
    upstreams = []
    skip_grads = []
    sums_local = jnp.zeros((2, 2, 3, 8 * C0), jnp.float32)
    for operation, preact in zip(operations, preacts):
        average, inverse_std = norm_terms(totals, counts, size_kind, operation)
        norm_slot = operation.slot
        channels = operation.cout
        centered = (preact - average) * inverse_std
        normed = centered * module_gains[norm_slot, :channels] + module_shifts[norm_slot, :channels]
        if operation.act == "silu":
            upstream = grads_by_name[operation.output] * silu_slope(normed)
        elif operation.act == "res":
            upstream = grads_by_name[operation.output] * silu_slope(normed + skip_map)
            skip_grads.append(upstream)
        else:
            upstream = from_slot(
                message_grads[operation.dest], preact_dims(size_kind, operation)
            ).astype(jnp.float32)
        upstreams.append(upstream)
        position = operation.position
        sums_local = sums_local.at[size_kind, 0, position, :channels].set(
            jnp.sum(upstream, axis=(0, 1, 2))
        )
        sums_local = sums_local.at[size_kind, 1, position, :channels].set(
            jnp.sum(upstream * centered, axis=(0, 1, 2))
        )
    return (to_canvas(upstreams, jnp.float32), sums_local, to_canvas(skip_grads, jnp.float32))


def backward_apply(
    branch_index,
    size_kind,
    phase_index,
    upstream_canvas,
    preact_canvas,
    totals,
    grad_totals,
    counts,
    source_canvas,
    module_weights,
    module_gains,
):
    operations = phase_operations(branch_index, phase_index)
    preacts = from_canvas(
        preact_canvas, [preact_dims(size_kind, operation) for operation in operations]
    )
    upstreams = from_canvas(
        upstream_canvas, [preact_dims(size_kind, operation) for operation in operations]
    )
    source_names = input_names(operations)
    source_list = [source_dims(branch_index, size_kind, map_name) for map_name in source_names]
    pieces = from_canvas(source_canvas, source_list)
    sources = {
        map_name: piece.astype(jnp.bfloat16) for map_name, piece in zip(source_names, pieces)
    }
    source_grads = {
        map_name: jnp.zeros(dims_entry, jnp.float32)
        for map_name, dims_entry in zip(source_names, source_list)
    }
    kernel_grads = []
    slot_count = module_gains.shape[0]
    gain_part = jnp.zeros((slot_count, 8 * C0), jnp.float32)
    shift_part = jnp.zeros((slot_count, 8 * C0), jnp.float32)
    for operation, preact, upstream in zip(operations, preacts, upstreams):
        average, inverse_std = norm_terms(totals, counts, size_kind, operation)
        cells_here = cell_total(counts, size_kind, operation.level)
        norm_slot = operation.slot
        channels = operation.cout
        position = operation.position
        centered = (preact - average) * inverse_std
        mean_upstream = grad_totals[size_kind, 0, position, :channels] / cells_here
        mean_cross = grad_totals[size_kind, 1, position, :channels] / cells_here
        preact_grad = (
            module_gains[norm_slot, :channels]
            * inverse_std
            * (upstream - mean_upstream - centered * mean_cross)
        )
        source_grad, kernel_grad = conv_backward(
            operation,
            sources[operation.source],
            kernel_piece(module_weights, operation),
            preact_grad.astype(jnp.bfloat16),
        )
        source_grads[operation.source] = source_grads[operation.source] + source_grad
        kernel_grads.append(kernel_grad.reshape(-1))
        gain_part = gain_part.at[norm_slot, :channels].set(
            grad_totals[0, 1, position, :channels] + grad_totals[1, 1, position, :channels]
        )
        shift_part = shift_part.at[norm_slot, :channels].set(
            grad_totals[0, 0, position, :channels] + grad_totals[1, 0, position, :channels]
        )
    phase_length = phase_lengths(C0, BLOCKS)[phase_index]
    if kernel_grads:
        joined = jnp.concatenate(kernel_grads)
        weight_part = jnp.pad(joined, (0, phase_length - joined.shape[0]))
    else:
        weight_part = jnp.zeros((phase_length,), jnp.float32)
    return (
        to_canvas([source_grads[map_name] for map_name in source_names], jnp.float32),
        weight_part,
        gain_part,
        shift_part,
    )


def on_device(features, weights, gains, shifts, cotangent, size_group):
    crop_shard = lax.axis_index("crops")
    shard_count = lax.axis_size("crops")
    crop_kind = size_group[crop_shard]
    large_count = jnp.sum(size_group).astype(jnp.float32)
    counts = jnp.stack([shard_count - large_count, large_count])
    case_index = lax.axis_index("branch") * 2 + crop_kind
    phase_total = 2 * BLOCKS + 3
    zero_canvas = jnp.zeros((ROWS, 128), jnp.float32)
    empty_buffer = jnp.zeros((4, MSG_ROWS, 128), jnp.bfloat16)

    def run_phase(function, statics, operands):
        branches_list = [
            partial(function, branch_index, size_kind, *statics)
            for branch_index in range(4)
            for size_kind in range(2)
        ]
        return lax.switch(case_index, branches_list, *operands)

    def statistics(local_totals):
        return lax.psum(local_totals, "crops")

    def module_forward(module, start_canvas, kept):
        module_weights = weights[0, module]
        module_gains = gains[0, module]
        module_shifts = shifts[0, module]
        record = SimpleNamespace(sources=[], preacts=[], totals=[])
        h_canvas = start_canvas
        u_canvas = zero_canvas
        chain_canvas = zero_canvas
        buffer = empty_buffer
        for phase_index in range(phase_total):
            if phase_index < 2 * BLOCKS:
                source = h_canvas if phase_index % 2 == 0 else u_canvas
            elif phase_index == 2 * BLOCKS:
                source = h_canvas
            else:
                source = chain_canvas
            preact, local_totals = run_phase(forward_conv, (phase_index,), (source, module_weights))
            global_totals = kept.totals[phase_index] if kept else statistics(local_totals)
            produced, buffer = run_phase(
                forward_norm,
                (phase_index,),
                (preact, global_totals, counts, module_gains, module_shifts, h_canvas, buffer),
            )
            record.sources.append(source)
            record.preacts.append(preact)
            record.totals.append(global_totals)
            if phase_index < 2 * BLOCKS:
                if phase_index % 2 == 0:
                    u_canvas = produced
                else:
                    h_canvas = produced
            else:
                chain_canvas = produced
        received = (
            kept.received
            if kept
            else jax.tree.map(
                lambda part, own: part.astype(own.dtype),
                lax.all_to_all(as_sent(buffer), "branch", split_axis=0, concat_axis=0, tiled=True),
                buffer,
            )
        )
        result, summed = run_phase(receive_forward, (), (h_canvas, received))
        record.summed = summed
        record.received = received
        return (result, record)

    checkpoints = [features[0].astype(jnp.float32)]
    first_records = []
    for module in range(MODULES):
        result, record = module_forward(module, checkpoints[-1], None)
        checkpoints.append(result)
        first_records.append(record)
    outputs = checkpoints[-1].astype(jnp.bfloat16)
    grad_canvas = cotangent[0].astype(jnp.float32)
    module_grads = [None] * MODULES
    gain_grads = [None] * MODULES
    shift_grads = [None] * MODULES
    for module in reversed(range(MODULES)):
        kept = None
        unused_result, record = module_forward(module, checkpoints[module], kept)
        module_module_weights = weights[0, module]
        module_module_gains = gains[0, module]
        module_module_shifts = shifts[0, module]
        summed_grad, back_buffer = run_phase(receive_backward, (), (grad_canvas, record.summed))
        message_grads = jax.tree.map(
            lambda part, own: part.astype(own.dtype),
            lax.all_to_all(as_sent(back_buffer), "branch", split_axis=0, concat_axis=0, tiled=True),
            back_buffer,
        )
        top_grad = summed_grad
        chain_grad = zero_canvas
        u_grad = zero_canvas
        pending_skip = zero_canvas
        weight_parts = [None] * phase_total
        gain_total = jnp.zeros(gains.shape[2:], jnp.float32)
        shift_total = jnp.zeros(gains.shape[2:], jnp.float32)
        for module_phase_index in reversed(range(phase_total)):
            if module_phase_index >= 2 * BLOCKS:
                output_grad = chain_grad
                skip_canvas = zero_canvas
            elif module_phase_index % 2 == 1:
                output_grad = top_grad
                skip_canvas = record.sources[module_phase_index - 1]
            else:
                output_grad = u_grad
                skip_canvas = zero_canvas
            module_preact = record.preacts[module_phase_index]
            totals = record.totals[module_phase_index]
            upstream, module_local_totals, skip_grad = run_phase(
                backward_stats,
                (module_phase_index,),
                (
                    output_grad,
                    message_grads,
                    module_preact,
                    totals,
                    counts,
                    module_module_gains,
                    module_module_shifts,
                    skip_canvas,
                ),
            )
            grad_totals = lax.psum(module_local_totals, "crops")
            source_grad, weight_parts[module_phase_index], gain_part, shift_part = run_phase(
                backward_apply,
                (module_phase_index,),
                (
                    upstream,
                    module_preact,
                    totals,
                    grad_totals,
                    counts,
                    record.sources[module_phase_index],
                    module_module_weights,
                    module_module_gains,
                ),
            )
            gain_total = gain_total + gain_part
            shift_total = shift_total + shift_part
            if module_phase_index > 2 * BLOCKS:
                chain_grad = source_grad
            elif module_phase_index == 2 * BLOCKS:
                top_grad = top_grad + source_grad
            elif module_phase_index % 2 == 1:
                u_grad = source_grad
                pending_skip = skip_grad
            else:
                top_grad = source_grad + pending_skip
        joined = jnp.concatenate(weight_parts)
        weight_grad = jnp.pad(joined, (0, weights.shape[2] - joined.shape[0]))
        grad_canvas, weight_grad, gain_grads[module], shift_grads[module] = (
            top_grad,
            weight_grad,
            gain_total,
            shift_total,
        )
        module_grads[module] = weight_grad
    weight_out = lax.psum_scatter(jnp.stack(module_grads), "crops", scatter_dimension=1, tiled=True)
    share = gains.shape[3] // shard_count
    gain_out = lax.dynamic_slice_in_dim(jnp.stack(gain_grads), crop_shard * share, share, axis=2)
    shift_out = lax.dynamic_slice_in_dim(jnp.stack(shift_grads), crop_shard * share, share, axis=2)
    return (outputs[None], grad_canvas[None], weight_out[None], gain_out[None], shift_out[None])


LANES = 128
SLOTS = 8
MASKS = 7
DOWN = (((1,), (0,)), ((), ()))
ACROSS = (((1,), (1,)), ((), ()))
ALONG = (((0,), (0,)), ((), ()))


def unit_table(k):
    operations = weighted_plan(k, C0, BLOCKS)
    planes = 8 >> k
    channels = C0 << k
    units = {}
    stat = 0

    def add(name, kind, source, lanes_in, planes_in, planes_out, members):
        nonlocal stat
        segs = []
        tile = 0
        for operation, lanes, chain in members:
            cout = operation.cout
            level = operation.level if operation.taps == 3 else operation.dest
            segs.append(
                SimpleNamespace(
                    slot=operation.slot,
                    off=operation.offset // LANES,
                    cin=operation.cin,
                    cout=cout,
                    taps=operation.taps,
                    tile=tile,
                    tiles=lanes // LANES,
                    blocks=max(1, (8 >> level)),
                    dest=operation.dest,
                    act=operation.act,
                    chain=chain,
                    up=k - operation.dest if operation.taps == 1 else 0,
                )
            )
            tile += lanes // LANES
        rows = {"s1": 768 if k == 3 else 512, "s2": lanes_in + LANES, "p1": 256}[kind]
        units[name] = SimpleNamespace(
            name=name,
            kind=kind,
            source=source,
            lanes_in=lanes_in,
            blocks_in=planes_in,
            planes_in=planes_in,
            planes=planes_out,
            segs=segs,
            tiles=tile,
            rows=rows,
            stat=stat,
            depth=1 if kind == "p1" else 3,
        )
        stat += tile

    add("a", "s1", "h", 256, planes, planes, [(operations[0], 256, None)])
    add("b", "s1", "u", 256, planes, planes, [(operations[1], 256, None)])
    ups = [operation for operation in operations if operation.taps == 1]
    if ups:
        add("u", "p1", "t", 256, planes, planes, [(operation, 256, None) for operation in ups])
    firsts, chains = [], {}
    for target in range(k + 1, 4):
        steps = [
            operation
            for operation in operations
            if operation.taps == 3 and operation.stride == 2
        ]
        start = sum(i - k for i in range(k + 1, target))
        chains[target] = steps[start : start + target - k]
        if target == k + 1:
            firsts.append((chains[target][0], 256, None))
        else:
            firsts.append((chains[target][0], LANES, "c1" if target == k + 2 else "c2"))
    if firsts:
        add("d", "s2", "t", 256, planes, planes // 2, firsts)
    if k <= 1:
        add("e", "s2", "c1", LANES, planes // 2, planes // 4, [(chains[k + 2][1], 256, None)])
    if k == 0:
        add("f", "s2", "c2", LANES, planes // 2, planes // 4, [(chains[3][1], LANES, "c3")])
        add("g", "s2", "c3", LANES, planes // 4, planes // 8, [(chains[3][2], 256, None)])
    return units


def links(k, unit, seg):
    cin = seg.cin
    count_in, count_out = unit.blocks_in, seg.blocks
    found = []
    if unit.kind == "p1":
        for plane in range(count_in):
            wide = 1 << seg.up
            found.append((plane * cin, 0, set(range(plane * wide, plane * wide + wide))))
        return found
    if unit.kind == "s1" and k == 3:
        return [(256 * tap, tap, {0}) for tap in range(3)]
    stride = 1 if unit.kind == "s1" else 2
    for plane in range(count_in):
        for tap in range(3):
            at = plane - tap + 1
            if at % stride == 0 and 0 <= at // stride < count_out:
                found.append((plane * cin, tap, {at // stride}))
    if stride == 1:
        found.append((256, 2, {count_out - 1}))
        found.append((512 - cin, 0, {0}))
    else:
        lanes_in = unit.lanes_in
        found.append((lanes_in + (count_in - 1) * cin - (lanes_in - LANES), 0, {0}))
    return found


def message_slot(k, other):
    return sum(2 * (8 >> max(k, before)) for before in range(other) if before != k)


def log2(value):
    return value.bit_length() - 1


def sigmoid_of(value):
    return 0.5 * jnp.tanh(0.5 * value) + 0.5


def silu_of(value):
    return value * sigmoid_of(value)


def slope_of(value):
    sigmoid = sigmoid_of(value)
    return sigmoid * (1.0 + value * (1.0 - sigmoid))


def planes_loop(count, body, turns=1):
    def step(index, carry):
        for turn in range(turns):
            body(index * turns + turn)
        return carry

    turns = min(turns, count)
    if count == turns:
        for index in range(count):
            body(index)
    else:
        lax.fori_loop(0, count // turns, step, 0)


def planes_sum(count, body, initial, turns=1):
    def step(index, carry):
        for turn in range(turns):
            carry = body(index * turns + turn, carry)
        return carry

    turns = min(turns, count)
    if count == turns:
        return step(0, initial)
    return lax.fori_loop(0, count // turns, step, initial)


def partial_sum(value):
    rows = value.shape[0]
    return jnp.sum(value.reshape(rows // 8, 8, value.shape[1]), axis=0)


class Planes:
    def __init__(self, mode, tiles, planes, masks, rows, main, edge=None, right=None):
        self.mode, self.tiles, self.planes = mode, tiles, planes
        self.masks, self.rows = masks, rows
        self.main, self.edge, self.right = main, edge, right
        self.base = 1 if mode in ("s1", "wide", "s2") else 0
        extra = {"s1": 2, "wide": 2, "s2": 1, "dz2": 1, "p": 0}[mode]
        self.span = planes + extra
        self.unit = tiles * self.span

    def at(self, m, tile, plane):
        return m * self.unit + tile * self.span + plane + self.base

    def edge_at(self, m, tile, plane):
        if self.mode == "s2":
            return m * self.span + plane + self.base
        return self.at(m, tile, plane)

    def from_left(self, value):
        return pltpu.roll(value, 1, 0) * self.masks[1]

    def from_right(self, value):
        return pltpu.roll(value, self.rows - 1, 0) * self.masks[2]

    def store(self, m, tile, plane, value):
        self.put(m, tile, plane, value)

    def put(self, m, tile, plane, value):
        where = self.at(m, tile, plane)
        self.main[where] = value.astype(jnp.bfloat16)
        if self.mode == "s1":
            side = self.from_right(value) if tile == 0 else self.from_left(value)
            self.edge[where] = side.astype(jnp.bfloat16)
        elif self.mode == "wide":
            self.edge[where] = self.from_left(value).astype(jnp.bfloat16)
            self.right[where] = self.from_right(value).astype(jnp.bfloat16)
        elif self.mode == "s2":
            if tile == self.tiles - 1:
                self.edge[self.edge_at(m, tile, plane)] = self.from_left(value).astype(jnp.bfloat16)
        elif self.mode == "dz2":
            self.edge[where] = self.from_right(value).astype(jnp.bfloat16)

    def put_above(self, m, tile, last):
        if self.mode in ("s1", "wide", "s2"):
            above = pltpu.roll(last, 6, 0) * self.masks[3] + pltpu.roll(last, 3, 0) * self.masks[4]
            self.put(m, tile, -1, above)

    def put_below(self, m, tile, first):
        if self.mode in ("s1", "wide", "dz2"):
            rows = self.rows
            below = (
                pltpu.roll(first, rows - 6, 0) * self.masks[5]
                + pltpu.roll(first, rows - 3, 0) * self.masks[6]
            )
            self.put(m, tile, self.planes, below)

    def close(self, m):
        for tile in range(self.tiles):
            last = self.main[self.at(m, tile, self.planes - 1)].astype(jnp.float32)
            self.put_above(m, tile, last)
            first = self.main[self.at(m, tile, 0)].astype(jnp.float32)
            self.put_below(m, tile, first)


class Branch:
    def __init__(self, k, rows, large, small, share, refs, masks, core):
        self.k, self.rows, self.refs, self.masks = k, rows, refs, masks
        self.units = unit_table(k)
        self.planes = 8 >> k
        self.core = core
        self.large, self.small, self.count = large, small, large + small
        self.cells = (small * (SH // 8) * (SW // 8), large * (LH // 8) * (LW // 8))
        self.quarter = lax.axis_index("crops") // 2
        self.share = share
        r = refs
        make = partial(Planes, masks=masks, rows=rows)
        one = "wide" if k == 3 else "s1"
        self.maps = dict(
            h=make(one, 2, self.planes, main=r.hC, edge=r.hE, right=r.hR),
            u=make(one, 2, self.planes, main=r.uC, edge=r.uE, right=r.uR),
            t=make("p" if k == 3 else "s2", 2, self.planes, main=r.tC, edge=r.tE),
        )
        if k <= 1:
            self.maps["c1"] = make("s2", 1, self.planes // 2, main=r.c1C, edge=r.c1E)
        if k == 0:
            self.maps["c2"] = make("s2", 1, 4, main=r.c2C, edge=r.c2E)
            self.maps["c3"] = make("s2", 1, 2, main=r.c3C, edge=r.c3E)
        self.grads = dict(t=r.gt, u=r.gu, c1=r.gc1, c2=r.gc2, c3=r.gc3)

    def lane_block(self, shape, cout):
        lanes = lax.broadcasted_iota(jnp.int32, shape, 1)
        return lanes >> log2(cout)

    def keep(self, value, cout, which):
        count = LANES // cout
        if len(which) == count:
            return value
        block = self.lane_block(value.shape, cout)
        mask = block == which[0]
        for entry in which[1:]:
            mask = mask | (block == entry)
        return jnp.where(mask, value, 0.0)

    def spread(self, value, cout):
        shift = LANES // 2
        while shift >= cout:
            value = value + pltpu.roll(value, shift, 1)
            shift //= 2
        return value

    def local_blocks(self, seg, tile, wanted):
        count = LANES // seg.cout
        return [q for q in range(count) if (tile * count + q) % seg.blocks in wanted]


    def segments(self):
        return [(unit, seg) for unit in self.units.values() for seg in unit.segs]

    def pieces(self):
        found, place = [], 0
        for index, (unit, seg) in enumerate(self.segments()):
            count = 2 * seg.taps**2 * seg.cin * seg.cout // LANES
            if self.k < 3:
                found.append((index, 0, count, place, index))
                place += count
            else:
                for d in range(unit.depth):
                    slot = len(found) % 3
                    found.append((index, d, count // unit.depth, slot * 3072, slot))
        return found

    def fetch(self, at):
        r = self.refs
        index, d, count, place, sem = self.pieces()[at]
        _, seg = self.segments()[index]
        return pltpu.make_async_copy(
            r.w.at[pl.ds(2 * seg.off + d * count, count)],
            r.raw.at[pl.ds(place, count)],
            r.wsem.at[sem],
        )

    def fetch_first(self):
        for at in range(len(self.pieces()) if self.k < 3 else 3):
            self.fetch(at).start()

    def expand(self, index):
        unit, seg = self.segments()[index]
        pieces = self.pieces()
        mine = [at for at, piece in enumerate(pieces) if piece[0] == index]
        if self.k < 3:
            (at,) = mine
            self.fetch(at).wait()
            count = pieces[at][2] // unit.depth
            planes_loop(
                unit.depth,
                lambda d: self.expand_row(unit, seg, d, count, pieces[at][3] + d * count),
            )
        else:
            for d, at in enumerate(mine):
                self.fetch(at).wait()
                self.expand_row(unit, seg, d, pieces[at][2], pieces[at][3])
                if at + 3 < len(pieces):
                    self.fetch(at + 3).start()
        for m in range(MODULES):
            self.spread_tables(m, unit, seg)

    def expand_row(self, unit, seg, d, count, place):
        r = self.refs
        chunk = math.gcd(count, 384)
        wf, rep = r.work, r.rep

        def widen(step):
            at = pl.multiple_of(step * chunk, 16)
            value = r.raw[pl.ds(pl.multiple_of(place + at, 16), chunk)].astype(jnp.float32)
            wf[pl.ds(at, chunk)] = value

        planes_loop(count // chunk, widen)
        count = count // MODULES
        depth, cin, cout = unit.depth, seg.cin, seg.cout
        target = getattr(r, "T" + unit.name)
        twice = unit.kind == "s1" and self.k < 3
        across = getattr(r, "T" + unit.name + unit.name) if twice else None
        by_row = {}
        for row, tap, wanted in links(self.k, unit, seg):
            by_row.setdefault(row, []).append((tap, wanted))

        def module(m):
            if cout < LANES:
                ratio = LANES // cout
                flat = wf[pl.ds(m, count, stride=2)]
                for part in range(ratio):
                    rep[pl.ds(part, count, stride=ratio)] = self.spread(
                        self.keep(flat, cout, [part]), cout
                    )

            def tap_rows(tap, tile):
                if cout < LANES:
                    return rep[tap * cin : (tap + 1) * cin]
                if cout == LANES:
                    return wf[pl.ds(m + tap * (2 * cin), cin, stride=2)]
                return wf[pl.ds(m + tap * (4 * cin) + 2 * tile, cin, stride=4)]

            for tile in range(seg.tiles):
                column = (seg.tile + tile) * LANES
                for row in range(0, unit.rows, cin):
                    total = None
                    for tap, wanted in by_row.get(row, []):
                        if cout <= LANES:
                            local = self.local_blocks(seg, tile, wanted)
                            if not local:
                                continue
                            piece = self.keep(tap_rows(tap, 0), cout, local)
                        else:
                            piece = tap_rows(tap, tile)
                        total = piece if total is None else total + piece
                    if total is None:
                        total = jnp.zeros((cin, LANES), jnp.float32)
                    block = total.astype(jnp.bfloat16)
                    target[m * depth + d, row : row + cin, column : column + LANES] = block
                    if across is not None:
                        first, lane = row % 256, row // 256 * 256 + column
                        across[m * depth + d, first : first + cin, lane : lane + LANES] = block

        planes_loop(MODULES, module)


    def parts(self, unit, source):
        if unit.kind == "p1":
            return [(source.main, range(2), source.at)]
        if source.mode == "wide":
            return [
                (source.edge, range(2), source.at),
                (source.main, range(2), source.at),
                (source.right, range(2), source.at),
            ]
        if unit.kind == "s1":
            return [(source.main, range(2), source.at), (source.edge, range(2), source.at)]
        last = source.tiles - 1
        return [
            (source.main, range(source.tiles), source.at),
            (source.edge, [last], source.edge_at),
        ]

    def rows_of(self, unit, part, m, d, first, count):
        ref, tiles, at = part
        pieces = []
        for tile in tiles:
            if unit.kind == "s2":
                rows = [ref[at(m, tile, 2 * (first + q) + d - 1)] for q in range(count)]
                pieces.append(rows[0] if count == 1 else jnp.concatenate(rows, axis=0))
            else:
                shift = d - 1 if unit.kind == "s1" else 0
                pieces.append(
                    ref[pl.ds(at(m, tile, first + shift), count)].reshape(count * self.rows, LANES)
                )
        return pieces

    def conv(self, m, unit):
        r = self.refs
        source = self.maps[unit.source]
        target = getattr(r, "T" + unit.name)
        z = getattr(r, "z" + unit.name)
        planes, tiles, depth = unit.planes, unit.tiles, unit.depth
        chunk = min(planes, 4 if tiles <= 2 else 2)
        lanes = tiles * LANES

        def body(step, sums):
            first = step * chunk
            pieces = []
            for d in range(depth):
                for part in self.parts(unit, source):
                    pieces += self.rows_of(unit, part, m, d, first, chunk)
            left = jnp.concatenate(pieces, axis=1)
            right = target[pl.ds(m * depth, depth), 0 : unit.rows, 0:lanes]
            right = right.reshape(depth * unit.rows, lanes)
            result = lax.dot_general(left, right, DOWN, preferred_element_type=jnp.float32)
            for tile in range(tiles):
                block = result[:, tile * LANES : (tile + 1) * LANES]
                z[pl.ds(m * tiles * planes + tile * planes + first, chunk)] = block.reshape(
                    chunk, self.rows, LANES
                )
            return (sums[0] + partial_sum(result), sums[1] + partial_sum(result * result))

        zero = jnp.zeros((8, lanes), jnp.float32)
        sums = planes_sum(planes // chunk, body, (zero, zero))
        for seg in unit.segs:
            scale = self.per_cell(unit, seg)
            totals = self.fold(seg, sums)
            self.norm_rows(m, unit, seg, totals, scale)

    def per_cell(self, unit, seg):
        blocks = seg.tiles * LANES // seg.cout
        small, large = self.cells
        count = unit.planes * blocks
        return jnp.where(self.core == 0, 1.0 / (large * count), 1.0 / (small * count)).astype(
            jnp.float32
        )

    def fold(self, seg, sums):
        first = seg.tile
        found = []
        for value in sums:
            tiles = [
                value[:, (first + t) * LANES : (first + t + 1) * LANES] for t in range(seg.tiles)
            ]
            if seg.cout <= LANES:
                total = tiles[0]
                for tile in tiles[1:]:
                    total = total + tile
                total = jnp.sum(self.spread(total, seg.cout), axis=0, keepdims=True)
                found.append([total] * seg.tiles)
            else:
                found.append([jnp.sum(tile, axis=0, keepdims=True) for tile in tiles])
        return found

    def table_row(self, ref, m, seg, tile):
        slot = seg.slot
        if seg.cout > LANES:
            return ref[m, slot : slot + 1, tile * LANES : (tile + 1) * LANES]
        row = jnp.broadcast_to(ref[m, slot : slot + 1, 0:LANES], (8, LANES))
        if seg.cout < LANES:
            row = self.spread(self.keep(row, seg.cout, [0]), seg.cout)
        return row[0:1]

    def norm_rows(self, m, unit, seg, totals, scale):
        st = self.refs.st
        for tile in range(seg.tiles):
            average = totals[0][tile] * scale
            variance = totals[1][tile] * scale - average * average
            inverse = lax.rsqrt(variance + EPS)
            where = m * STATS + unit.stat + seg.tile + tile
            factor = st[where, 4:5] * inverse
            st[where, 0:1] = average
            st[where, 1:2] = inverse
            st[where, 2:3] = factor
            st[where, 3:4] = st[where, 5:6] - average * factor

    def spread_tables(self, m, unit, seg):
        st = self.refs.st
        for tile in range(seg.tiles):
            where = m * STATS + unit.stat + seg.tile + tile
            st[where, 4:5] = self.table_row(self.refs.gains, m, seg, tile)
            st[where, 5:6] = self.table_row(self.refs.shifts, m, seg, tile)

    def normed(self, m, unit, tile, plane):
        st = self.refs.st
        z = getattr(self.refs, "z" + unit.name)
        where = m * STATS + unit.stat + tile
        value = z[m * unit.tiles * unit.planes + tile * unit.planes + plane]
        return value * st[where, 2:3] + st[where, 3:4]

    def apply_a(self, m):
        unit, u = self.units["a"], self.maps["u"]

        def body(plane):
            for tile in range(2):
                value = silu_of(self.normed(m, unit, tile, plane)) * self.masks[0]
                u.store(m, tile, plane, value)

        planes_loop(self.planes, body, TURNS)
        u.close(m)

    def apply_b(self, m):
        unit, top = self.units["b"], self.maps["t"]
        hf, s = self.refs.hf, self.refs.s

        def body(plane):
            for tile in range(2):
                where = m * 2 * self.planes + tile * self.planes + plane
                value = silu_of(self.normed(m, unit, tile, plane) + hf[where]) * self.masks[0]
                s[where] = value
                top.store(m, tile, plane, value)

        planes_loop(self.planes, body, TURNS)
        top.close(m)

    def apply_rest(self, m, unit):
        sb = self.refs.sb
        for seg in unit.segs:
            chain = self.maps[seg.chain] if seg.chain else None

            def body(plane):
                for tile in range(seg.tiles):
                    value = self.normed(m, unit, seg.tile + tile, plane)
                    if chain is not None:
                        chain.store(m, tile, plane, silu_of(value) * self.masks[0])
                    else:
                        at = message_slot(self.k, seg.dest) + tile * unit.planes + plane
                        sb[at] = value.astype(jnp.bfloat16)

            planes_loop(unit.planes, body, TURNS)
            if chain is not None:
                chain.close(m)
            else:
                self.message(m, seg.dest).start()

    def message(self, e, other):
        count = 2 * (8 >> max(self.k, other))
        r = self.refs
        return pltpu.make_async_remote_copy(
            src_ref=r.sb.at[pl.ds(message_slot(self.k, other), count)],
            dst_ref=r.rb.at[pl.ds(e * 16 + message_slot(other, self.k), count)],
            send_sem=r.ssem.at[e * 4 + other],
            recv_sem=r.rsem.at[e * 4 + self.k],
            device_id=dict(branch=other),
            device_id_type=pl.DeviceIdType.MESH,
        )

    def arrived(self, e, other):
        count = 2 * (8 >> max(self.k, other))
        r = self.refs
        at = message_slot(self.k, other)
        return pltpu.make_async_remote_copy(
            src_ref=r.sb.at[pl.ds(at, count)],
            dst_ref=r.rb.at[pl.ds(e * 16 + at, count)],
            send_sem=r.ssem.at[e * 4 + other],
            recv_sem=r.rsem.at[e * 4 + other],
            device_id=dict(branch=other),
            device_id_type=pl.DeviceIdType.MESH,
        )

    def others(self):
        return [other for other in range(4) if other != self.k]

    def settle(self, e):
        for other in self.others():
            self.message(e, other).wait_send()
        for other in self.others():
            self.arrived(e, other).wait_recv()

    def receive(self, m):
        r = self.refs
        s, rb, hf, out = r.s, r.rb, r.hf, r.outs
        h = self.maps["h"]

        def total_at(tile, plane):
            where = m * 2 * self.planes + tile * self.planes + plane
            total = s[where]
            for other in self.others():
                count = 8 >> max(self.k, other)
                at = plane >> max(0, other - self.k)
                slot = m * 16 + message_slot(self.k, other) + tile * count + at
                total = total + rb[slot].astype(jnp.float32)
            s[where] = total
            return silu_of(total) * self.masks[0]

        def onward(plane):
            for tile in range(2):
                value = total_at(tile, plane)
                hf[(2 + tile) * self.planes + plane] = value
                h.store(1, tile, plane, value)

        def finish(plane):
            for tile in range(2):
                out[tile * self.planes + plane] = total_at(tile, plane).astype(jnp.bfloat16)

        @pl.when(m + 1 < MODULES)
        def _():
            planes_loop(self.planes, onward)
            h.close(1)

        @pl.when(m + 1 == MODULES)
        def _():
            planes_loop(self.planes, finish)

    def take_feature(self, tile, plane, value):
        self.refs.hf[tile * self.planes + plane] = value
        self.maps["h"].store(0, tile, plane, value)

    def take_cotangent(self, tile, plane, value):
        self.refs.gin[tile * self.planes + plane] = value

    def member(self, kind, order):
        kinds = self.refs.kinds
        found, before = jnp.int32(0), jnp.int32(0)
        for at in range(self.count):
            same = kinds[at] == kind
            found = jnp.where(same & (before == order), at, found)
            before = before + same.astype(jnp.int32)
        return found

    def order(self, device):
        kinds = self.refs.kinds
        kind = kinds[device]
        before = jnp.int32(0)
        for at in range(self.count):
            before = before + ((kinds[at] == kind) & (at < device)).astype(jnp.int32)
        return before

    def unpack(self, t, consume):
        r = self.refs
        work, rows, planes = r.work, self.rows, self.planes
        full = SH * SW * C0 // LANES
        gath = r.gathc if t else r.gathx

        @pl.when(self.core == 0)
        def _():
            for at in range(self.large):
                block = gath[self.member(1, at)]
                work[at * ROWS : (at + 1) * ROWS] = block.astype(jnp.float32)

        @pl.when(self.core == 1)
        def _():
            for at in range(self.small):
                block = gath[self.member(0, at), 0:full]
                work[at * full : (at + 1) * full] = block.astype(jnp.float32)
            work[self.small * full : self.large * ROWS] = jnp.zeros(
                (self.large * ROWS - self.small * full, LANES), jnp.float32
            )

        deep = self.large * ROWS // 2
        right = jnp.concatenate([work[pl.ds(j, deep, stride=2)] for j in range(2)], axis=1)
        right = right.astype(jnp.bfloat16)
        cells = Cells(self.core, (rows, LANES), self.small, self.large)
        base = cells.crop * cells.pick(ROWS // 2, full // 2)
        base = base + cells.along * (planes * cells.wide) + cells.across
        base = jnp.where(cells.valid, base, -(1 << 20))
        lane = lax.broadcasted_iota(jnp.int32, (rows, LANES), 1)
        chunk = min(planes, 4)

        def body(step):
            pieces = []
            for q in range(chunk):
                goal = base + (step * chunk + q) * cells.wide
                pieces.append(one_hot(goal, lane, deep))
            left = pieces[0] if chunk == 1 else jnp.concatenate(pieces, axis=0)
            result = lax.dot_general(left, right, DOWN, preferred_element_type=jnp.float32)
            for q in range(chunk):
                for tile in range(2):
                    value = result[q * rows : (q + 1) * rows, tile * LANES : (tile + 1) * LANES]
                    consume(tile, step * chunk + q, value)

        planes_loop(planes // chunk, body)

    def pack_size(self):
        return 48 * self.planes, -(-self.planes * self.rows // LANES) * LANES

    def plan_pack(self):
        r = self.refs
        high, deep = self.pack_size()
        planes = self.planes
        q = lax.broadcasted_iota(jnp.int32, (high, LANES), 0)
        lane = lax.broadcasted_iota(jnp.int32, (high, LANES), 1)
        wide, tall = jnp.where(self.core == 0, 6, 3), jnp.where(self.core == 0, 8, 4)
        cell = jnp.where(self.core == 0, (q * 43691) >> 18, (q * 43691) >> 17)
        across = q - cell * wide
        plane = cell & (planes - 1)
        along = cell >> log2(planes)
        base = plane * self.rows + along * wide + across
        base = jnp.where(along < tall, base, -(1 << 20))
        shard = lax.axis_index("crops")
        for at, device in enumerate((shard, shard + 1 - 2 * self.core)):
            goal = base + self.order(device) * (wide * tall)
            r.hot[at, 0:high, 0:deep] = one_hot(goal, lane, deep)

    def pack(self, units, put):
        high, deep = self.pack_size()
        right = jnp.concatenate([units(tile) for tile in range(2)], axis=1)
        short = deep - right.shape[0]
        parts = [right.astype(jnp.bfloat16)]
        if right.dtype == jnp.float32:
            parts.append((right - parts[0].astype(jnp.float32)).astype(jnp.bfloat16))
        if short:
            empty = jnp.zeros((short, 2 * LANES), jnp.bfloat16)
            parts = [jnp.concatenate([part, empty], axis=0) for part in parts]
        for at in range(2):
            total = None
            for part in parts:
                piece = lax.dot_general(
                    self.refs.hot[at, 0:high, 0:deep],
                    part,
                    DOWN,
                    preferred_element_type=jnp.float32,
                )
                total = piece if total is None else total + piece
            for tile in range(2):
                put(at, pl.ds(tile, high, stride=2), total[:, tile * LANES : (tile + 1) * LANES])

    def pack_outputs(self):
        r = self.refs
        high = 2 * self.pack_size()[0]

        def put(at, where, value):
            r.work[pl.ds(at * ROWS + where.start, where.size, stride=2)] = value

        def units(tile):
            block = r.outs[tile * self.planes : (tile + 1) * self.planes]
            return block.reshape(self.planes * self.rows, LANES)

        self.pack(units, put)
        for at in range(2):
            r.blocks[at, 0:high] = r.work[at * ROWS : at * ROWS + high].astype(jnp.bfloat16)
            if high < ROWS:
                r.blocks[at, high:ROWS] = jnp.zeros((ROWS - high, LANES), jnp.bfloat16)

    def pack_gradient(self):
        r = self.refs
        high = 2 * self.pack_size()[0]

        def put(at, where, value):
            r.slopes[at, where] = value

        def units(tile):
            block = r.gin[tile * self.planes : (tile + 1) * self.planes]
            return block.reshape(self.planes * self.rows, LANES)

        self.pack(units, put)
        if high < ROWS:
            for at in range(2):
                r.slopes[at, high:ROWS] = jnp.zeros((ROWS - high, LANES), jnp.float32)

    def forward(self, m, gather):
        steps = iter(range(1, 4))

        def also():
            step = next(steps, None)
            if step is not None:

                @pl.when(m == 0)
                def _():
                    gather.step(1, step)

        self.conv(m, self.units["a"])
        self.apply_a(m)
        also()
        self.conv(m, self.units["b"])
        self.apply_b(m)
        also()
        for name in ("d", "u", "e", "f", "g"):
            if name in self.units:
                self.conv(m, self.units[name])
                self.apply_rest(m, self.units[name])
                also()
        for _ in range(3):
            also()

        @pl.when(m == MODULES - 1)
        def _():
            gather.collect(1)
            self.unpack(1, self.take_cotangent)
            self.plan_pack()

        self.settle(m)
        self.receive(m)


    def send_back(self, m):
        r = self.refs
        s, gin, gt, sb = r.s, r.gin, r.gt, r.sb
        e = MODULES + m

        def body(plane):
            for tile in range(2):
                at = tile * self.planes + plane
                value = gin[at] * slope_of(s[m * 2 * self.planes + at])
                gt[at] = value
                for other in range(self.k):
                    sb[message_slot(self.k, other) + at] = value.astype(jnp.bfloat16)

        planes_loop(self.planes, body, TURNS)
        for other in reversed(self.others()):
            if other > self.k:
                count = 8 >> other
                wide = 1 << (other - self.k)

                def pool(plane):
                    for tile in range(2):
                        total = gt[tile * self.planes + plane * wide]
                        for step in range(1, wide):
                            total = total + gt[tile * self.planes + plane * wide + step]
                        slot = message_slot(self.k, other) + tile * count + plane
                        sb[slot] = total.astype(jnp.bfloat16)

                planes_loop(count, pool, TURNS)
            self.message(e, other).start()

    def back_unit(self, m, unit):
        r = self.refs
        st, dyb, z = r.st, r.dyb, getattr(r, "z" + unit.name)
        name, planes, tiles = unit.name, unit.planes, unit.tiles
        e = MODULES + m
        sums = {}

        def upstream(seg, tile, plane, normed):
            at = tile * planes + plane
            if name == "b":
                hf = r.hf[m * 2 * planes + at]
                value = r.gt[at] * slope_of(normed + hf)
                r.gin[at] = value
                return value
            if name == "a":
                return r.gu[at] * slope_of(normed)
            if seg.chain:
                return self.grads[seg.chain][at] * slope_of(normed)
            return r.rb[e * 16 + message_slot(self.k, seg.dest) + at].astype(jnp.float32)

        for seg in unit.segs:

            def body(plane, carry):
                result = []
                for tile in range(seg.tiles):
                    at = (seg.tile + tile) * planes + plane
                    where = m * STATS + unit.stat + seg.tile + tile
                    value = z[m * tiles * planes + at]
                    normed = value * st[where, 2:3] + st[where, 3:4]
                    dy = upstream(seg, tile, plane, normed)
                    dyb[at] = dy
                    zhat = (value - st[where, 0:1]) * st[where, 1:2]
                    result.append(carry[2 * tile] + partial_sum(dy))
                    result.append(carry[2 * tile + 1] + partial_sum(dy * zhat))
                return tuple(result)

            zero = jnp.zeros((8, LANES), jnp.float32)
            found = planes_sum(planes, body, (zero,) * (2 * seg.tiles), TURNS)
            pair = [
                jnp.concatenate([found[2 * tile + which] for tile in range(seg.tiles)], axis=1)
                for which in range(2)
            ]
            plain = SimpleNamespace(**vars(seg))
            plain.tile = 0
            totals = self.fold(plain, pair)
            self.table_grads(m, seg, totals)
            sums[seg.slot] = totals
        dz = self.dz_planes(unit)
        for seg in unit.segs:
            scale = self.per_cell(unit, seg)
            totals = sums[seg.slot]

            def apply(plane):
                for tile in range(seg.tiles):
                    at = (seg.tile + tile) * planes + plane
                    where = m * STATS + unit.stat + seg.tile + tile
                    zhat = (z[m * tiles * planes + at] - st[where, 0:1]) * st[where, 1:2]
                    inner = dyb[at] - totals[0][tile] * scale - zhat * (totals[1][tile] * scale)
                    dz.store(0, seg.tile + tile, plane, inner * st[where, 2:3] * self.masks[0])

            planes_loop(planes, apply, TURNS)
        dz.close(0)
        self.back_data(m, unit, dz)
        first = min(seg.off for seg in unit.segs)
        last = max(seg.off + seg.taps**2 * seg.cin * seg.cout // LANES for seg in unit.segs)
        wanted = (self.quarter * self.share < last) & ((self.quarter + 1) * self.share > first)

        @pl.when(wanted)
        def _():
            self.back_kernel(m, unit, dz)

    def dz_planes(self, unit):
        r = self.refs
        mode = {"p1": "p", "s2": "dz2", "s1": "wide" if self.k == 3 else "s1"}[unit.kind]
        return Planes(
            mode,
            unit.tiles,
            unit.planes,
            self.masks,
            self.rows,
            r.dC,
            r.dE,
            r.dR,
        )

    def table_grads(self, m, seg, totals):
        gg = self.refs.gg
        slot = seg.slot
        for which, found in ((0, totals[1]), (1, totals[0])):
            if seg.cout > LANES:
                for tile in range(2):
                    gg[m, which, slot : slot + 1, tile * LANES : (tile + 1) * LANES] = found[tile]
            else:
                row = jnp.broadcast_to(found[0], (8, LANES))
                if seg.cout < LANES:
                    row = self.keep(row, seg.cout, [0])
                gg[m, which, slot : slot + 1, 0:LANES] = row[0:1]

    def wide_rows(self, ref, at, tiles, plane, count):
        pieces = [
            ref[pl.ds(at(0, tile, plane), count)].reshape(count * self.rows, LANES)
            for tile in range(tiles)
        ]
        return pieces[0] if tiles == 1 else jnp.concatenate(pieces, axis=1)

    def back_data(self, m, unit, dz):
        r = self.refs
        kind, tiles = unit.kind, unit.tiles
        target = getattr(r, "T" + unit.name)
        lanes = tiles * LANES
        rows = self.rows

        def kernel_rows(d, first, count):
            return target[m * unit.depth + d, first : first + count, 0:lanes]

        def product(left, right):
            return lax.dot_general(left, right, ACROSS, preferred_element_type=jnp.float32)

        def put(ref, tile, planes, first, count, value, step=1, add=False):
            block = value.reshape(count, rows, LANES)
            for q in range(count):
                at = tile * planes + first + q * step
                ref[at] = ref[at] + block[q] if add else block[q]

        planes = unit.planes
        if kind == "s1":
            goal = r.gu if unit.name == "b" else r.gin
            add = unit.name == "a"
            chunk = min(planes, 4)
            across = getattr(r, "T" + unit.name + unit.name)

            def body(step):
                first = step * chunk
                if self.k == 3:
                    total = None
                    for d in range(3):
                        for ref, at in ((dz.right, 0), (dz.main, 256), (dz.edge, 512)):
                            left = self.wide_rows(ref, dz.at, 2, first + 1 - d, chunk)
                            piece = product(left, kernel_rows(d, at, 256))
                            total = piece if total is None else total + piece
                else:
                    left = [
                        self.wide_rows(ref, dz.at, 2, first + 1 - d, chunk)
                        for d in range(3)
                        for ref in (dz.main, dz.edge)
                    ]
                    right = [across[m * 3 + d] for d in range(3)]
                    total = product(
                        jnp.concatenate(left, axis=1), jnp.concatenate(right, axis=1)
                    )
                for tile in range(2):
                    put(
                        goal,
                        tile,
                        planes,
                        first,
                        chunk,
                        total[:, tile * LANES : (tile + 1) * LANES],
                        add=add,
                    )

            planes_loop(planes // chunk, body)
            return
        if kind == "p1":
            left = self.wide_rows(dz.main, dz.at, tiles, 0, planes)
            total = product(left, kernel_rows(0, 0, 256))
            for tile in range(2):
                put(
                    r.gt,
                    tile,
                    planes,
                    0,
                    planes,
                    total[:, tile * LANES : (tile + 1) * LANES],
                    add=True,
                )
            return
        goal = self.grads[unit.source]
        add = unit.source == "t"
        lanes_in = unit.lanes_in
        count_in = unit.planes_in
        for parity, terms in ((0, [(1, 0)]), (1, [(2, 0), (0, 1)])):
            total, side = None, None
            for d, offset in terms:
                left = self.wide_rows(dz.main, dz.at, tiles, offset, planes)
                piece = product(left, kernel_rows(d, 0, lanes_in))
                total = piece if total is None else total + piece
                left = self.wide_rows(dz.edge, dz.at, tiles, offset, planes)
                piece = product(left, kernel_rows(d, lanes_in, LANES))
                side = piece if side is None else side + piece
            for tile in range(lanes_in // LANES):
                value = total[:, tile * LANES : (tile + 1) * LANES]
                if tile == lanes_in // LANES - 1:
                    value = value + side
                put(goal, tile, count_in, parity, planes, value, step=2, add=add)

    def back_kernel(self, m, unit, dz):
        r = self.refs
        G, rep, wgv = r.work, r.rep, r.wgv
        tiles, planes = unit.tiles, unit.planes
        source = self.maps[unit.source]
        right = self.wide_rows(dz.main, dz.at, tiles, 0, planes)

        def gather(d):
            at = 0
            for part in self.parts(unit, source):
                pieces = self.rows_of(unit, part, m, d, 0, planes)
                left = pieces[0] if len(pieces) == 1 else jnp.concatenate(pieces, axis=1)
                count = left.shape[1]
                result = lax.dot_general(left, right, ALONG, preferred_element_type=jnp.float32)
                for tile in range(tiles):
                    row = pl.multiple_of((d * tiles + tile) * unit.rows + at, 8)
                    G[pl.ds(row, count)] = result[:, tile * LANES : (tile + 1) * LANES]
                at += count

        planes_loop(unit.depth, gather)
        for seg in unit.segs:
            self.fold_kernel(m, unit, seg)

    def fold_kernel(self, m, unit, seg):
        r = self.refs
        G, rep, wgv = r.work, r.rep, r.wgv
        cin, cout, tiles = seg.cin, seg.cout, unit.tiles
        width = 3 if seg.taps == 3 else 1
        found = links(self.k, unit, seg)
        off = seg.off

        def fold(d):
            for column in range(width):
                tap = d * width + column
                totals = []
                for tile in range(seg.tiles):
                    total = None
                    for row, which, wanted in found:
                        if which != column:
                            continue
                        at = pl.multiple_of((d * tiles + seg.tile + tile) * unit.rows + row, 8)
                        piece = G[pl.ds(at, cin)]
                        if cout <= LANES:
                            local = self.local_blocks(seg, tile, wanted)
                            if not local:
                                continue
                            piece = self.keep(piece, cout, local)
                        total = piece if total is None else total + piece
                    totals.append(total)
                if cout > LANES:
                    for tile in range(2):
                        wgv[pl.ds(off + tap * (2 * cin) + tile, cin, stride=2)] = totals[tile]
                    continue
                total = None
                for piece in totals:
                    if piece is not None:
                        total = piece if total is None else total + piece
                if cout == LANES:
                    wgv[pl.ds(pl.multiple_of(off + tap * cin, 8), cin)] = total
                else:
                    rep[pl.ds(pl.multiple_of(tap * cin, cin), cin)] = self.spread(total, cout)

        planes_loop(unit.depth, fold)
        if cout < LANES:
            ratio = LANES // cout
            count = width * width * cin // ratio
            total = None
            for part in range(ratio):
                piece = self.keep(rep[pl.ds(part, count, stride=ratio)], cout, [part])
                total = piece if total is None else total + piece
            wgv[off : off + count] = total

    def backward(self, m):
        e = MODULES + m
        self.send_back(m)
        for name in ("g", "f", "e", "d", "u"):
            if name in self.units:
                for seg in self.units[name].segs:
                    if seg.dest >= 0:
                        self.arrived(e, seg.dest).wait_recv()
                self.back_unit(m, self.units[name])
        for other in self.others():
            self.message(e, other).wait_send()
        self.back_unit(m, self.units["b"])
        self.back_unit(m, self.units["a"])


STATS = 20
TURNS = 1
NAMES = list(
    dict(x=0, cot=0, w=0, gains=0, shifts=0, kinds=0, out=0, grad=0, wg=0, gain=0, shift=0)
)


def one_hot(goal, lane, deep):
    pieces = [
        jnp.where(goal == lane + first, 1.0, 0.0).astype(jnp.bfloat16)
        for first in range(0, deep, LANES)
    ]
    return jnp.concatenate(pieces, axis=1)


class Cells:
    def __init__(self, core, shape, small, large):
        self.core = core
        row = lax.broadcasted_iota(jnp.int32, shape, 0)
        self.wide = self.pick(LW // 8, SW // 8)
        tall = self.pick(LH // 8, SH // 8)
        self.crop = self.pick((row * 43691) >> 21, (row * 43691) >> 19)
        inner = row - self.crop * (self.wide * tall)
        self.along = self.pick((inner * 43691) >> 18, (inner * 43691) >> 17)
        self.across = inner - self.along * self.wide
        self.valid = self.crop < self.pick(large, small)
        self.last = tall - 1

    def pick(self, large, small):
        return jnp.where(self.core == 0, large, small)


def fill_masks(refs, rows, core, small, large):
    cells = Cells(core, (rows, LANES), small, large)
    valid = cells.valid
    six = cells.wide == 6
    up, down = valid & (cells.along > 0), valid & (cells.along < cells.last)
    tables = (
        valid,
        valid & (cells.across > 0),
        valid & (cells.across < cells.wide - 1),
        up & six,
        up & jnp.logical_not(six),
        down & six,
        down & jnp.logical_not(six),
    )
    for at, table in enumerate(tables):
        refs.masks[at] = jnp.where(table, 1.0, 0.0)


class Gather:
    def __init__(self, refs, core, count):
        self.refs, self.core, self.count = refs, core, count
        self.z = lax.axis_index("crops") // 2
        self.last = count // 2 - 1

    def hop(self, t, source, right):
        r = self.refs
        at = source * 2 + self.core
        gath = r.gathc if t else r.gathx
        to = self.z + 1 if right else self.z - 1
        return pltpu.make_async_remote_copy(
            src_ref=gath.at[at],
            dst_ref=gath.at[at],
            send_sem=r.hsem.at[(t * (self.last + 1) + source) * 3 + (0 if right else 1)],
            recv_sem=r.gsem.at[t * self.count + at],
            device_id=dict(crops=to * 2 + self.core),
            device_id_type=pl.DeviceIdType.MESH,
        )

    def across(self, t, source, core, rows):
        r = self.refs
        at = source * 2 + core
        gath = r.gathc if t else r.gathx
        return pltpu.make_async_remote_copy(
            src_ref=gath.at[at, pl.ds(0, rows)],
            dst_ref=gath.at[at, pl.ds(0, rows)],
            send_sem=r.hsem.at[(t * (self.last + 1) + source) * 3 + 2],
            recv_sem=r.gsem.at[t * self.count + at],
            device_id=dict(crops=self.z * 2 + 1 - self.core),
            device_id_type=pl.DeviceIdType.MESH,
        )

    def each_core(self, action):
        for core, rows in ((0, SH * SW * C0 // LANES), (1, ROWS)):

            @pl.when(self.core == core)
            def _():
                action(core, rows)

    def send(self, t, source, rightward, leftward):
        if rightward:

            @pl.when(self.z < self.last)
            def _():
                self.hop(t, source, True).start()

        if leftward:

            @pl.when(self.z > 0)
            def _():
                self.hop(t, source, False).start()

        self.each_core(lambda core, rows: self.across(t, source, core, rows).start())

    def step(self, t, s):
        r = self.refs
        if s == 0:
            at = self.z * 2 + self.core
            if t:
                r.gathc[at] = r.cot[...]
            else:
                r.gathx[at] = r.x[...]
            self.send(t, self.z, True, True)
            return

        @pl.when(self.z >= s)
        def _():
            self.hop(t, self.z - s, True).wait_recv()
            self.send(t, self.z - s, True, False)

        @pl.when(self.z + s <= self.last)
        def _():
            self.hop(t, self.z + s, True).wait_recv()
            self.send(t, self.z + s, False, True)

    def collect(self, t):
        for source in range(self.last + 1):
            for core, rows in ((0, ROWS), (1, SH * SW * C0 // LANES)):

                @pl.when(self.core == core)
                def _():
                    self.across(t, source, 1 - core, rows).wait_recv()

    def finish(self, t):
        def sent(source, rightward, leftward):
            if rightward:

                @pl.when(self.z < self.last)
                def _():
                    self.hop(t, source, True).wait_send()

            if leftward:

                @pl.when(self.z > 0)
                def _():
                    self.hop(t, source, False).wait_send()

            self.each_core(lambda core, rows: self.across(t, source, core, rows).wait_send())

        sent(self.z, True, True)
        for s in range(1, self.last + 1):

            @pl.when(self.z >= s)
            def _():
                sent(self.z - s, True, False)

            @pl.when(self.z + s <= self.last)
            def _():
                sent(self.z + s, False, True)


def scratch_table(rows, weight_rows, count):
    def half(many):
        return pltpu.VMEM((many, rows, LANES), jnp.bfloat16)

    def full(many):
        return pltpu.VMEM((many, rows, LANES), jnp.float32)

    def expanded(depth, deep, wide):
        return pltpu.VMEM((MODULES * depth, deep, wide), jnp.bfloat16)

    _, span, _ = pair_rows(weight_rows, count)
    return dict(
        masks=full(MASKS),
        hC=half(2 * 20),
        hE=half(2 * 20),
        hR=half(2 * 6),
        uC=half(2 * 20),
        uE=half(2 * 20),
        uR=half(2 * 6),
        tC=half(2 * 18),
        tE=half(2 * 9),
        c1C=half(2 * 5),
        c1E=half(2 * 5),
        c2C=half(2 * 5),
        c2E=half(2 * 5),
        c3C=half(2 * 3),
        c3E=half(2 * 3),
        dC=half(20),
        dE=half(20),
        dR=half(6),
        outs=half(16),
        hf=full(2 * 16),
        s=full(2 * 16),
        za=full(2 * 16),
        zb=full(2 * 16),
        zd=full(2 * 16),
        zu=full(2 * 8),
        ze=full(2 * 4),
        zf=full(2 * 2),
        zg=full(2 * 2),
        gt=full(16),
        gu=full(16),
        gin=full(16),
        gc1=full(4),
        gc2=full(4),
        gc3=full(2),
        dyb=full(16),
        sb=half(16),
        rb=half(4 * 16),
        st=pltpu.VMEM((MODULES * STATS, 8, LANES), jnp.float32),
        Ta=expanded(3, 768, 256),
        Tb=expanded(3, 768, 256),
        Taa=expanded(3, 256, 512),
        Tbb=expanded(3, 256, 512),
        Td=expanded(3, 384, 512),
        Tu=expanded(1, 256, 768),
        Te=expanded(3, 256, 256),
        Tf=expanded(3, 256, 128),
        Tg=expanded(3, 256, 256),
        raw=pltpu.VMEM((9408, LANES), jnp.bfloat16),
        work=pltpu.VMEM((4608, LANES), jnp.float32),
        rep=pltpu.VMEM((640, LANES), jnp.float32),
        wgv=pltpu.VMEM((weight_rows, LANES), jnp.float32),
        wq=pltpu.VMEM((MODULES, 2 * weight_rows // count, LANES), jnp.float32),
        wr=pltpu.VMEM((MODULES, span, LANES), jnp.float32),
        gathx=pltpu.VMEM((count, ROWS, LANES), jnp.bfloat16),
        gathc=pltpu.VMEM((count, ROWS, LANES), jnp.bfloat16),
        hot=pltpu.VMEM((2, 384, 768), jnp.bfloat16),
        blocks=pltpu.VMEM((2, ROWS, LANES), jnp.bfloat16),
        slopes=pltpu.VMEM((2, ROWS, LANES), jnp.float32),
        blockr=pltpu.VMEM((ROWS, LANES), jnp.bfloat16),
        sloper=pltpu.VMEM((ROWS, LANES), jnp.float32),
        gg=pltpu.VMEM((MODULES, 2, SLOTS, 256), jnp.float32),
        ggr=pltpu.VMEM((MODULES, 2, SLOTS, 256), jnp.float32),
        wsem=pltpu.SemaphoreType.DMA((8,)),
        ssem=pltpu.SemaphoreType.DMA((16,)),
        rsem=pltpu.SemaphoreType.DMA((16,)),
        hsem=pltpu.SemaphoreType.DMA((3 * count,)),
        gsem=pltpu.SemaphoreType.DMA((2 * count,)),
        psem=pltpu.SemaphoreType.DMA((5,)),
        qsem=pltpu.SemaphoreType.DMA((5,)),
        osem=pltpu.SemaphoreType.DMA((1,)),
    )


def pair_rows(weight_rows, count):
    share = weight_rows // count
    low = share // 8 * 8
    return share, 2 * share - low, low


def greet(core, count):
    barrier = pltpu.get_barrier_semaphore()
    me, shard = lax.axis_index("branch"), lax.axis_index("crops")
    z = shard // 2

    def signal(**where):
        pl.semaphore_signal(barrier, inc=1, device_id=where, device_id_type=pl.DeviceIdType.MESH)

    for step in range(1, 4):
        signal(branch=lax.rem(me + step, 4))
    signal(crops=shard + 1 - 2 * core)

    @pl.when(z > 0)
    def _():
        signal(crops=shard - 2)

    @pl.when(z < count // 2 - 1)
    def _():
        signal(crops=shard + 2)

    ends = (z == 0).astype(jnp.int32) + (z == count // 2 - 1).astype(jnp.int32)
    pl.semaphore_wait(barrier, 6 - ends)


def whole_kernel(names, rows, large, small, *args):
    refs = SimpleNamespace(**dict(zip(names, args)))
    count = large + small
    me, shard = lax.axis_index("branch"), lax.axis_index("crops")
    core = shard % 2
    weight_rows = refs.wgv.shape[0]
    share, span, low = pair_rows(weight_rows, count)
    quarter = pl.multiple_of(shard // 2 * (2 * share), 8)

    class Lazy:
        def __getitem__(self, index):
            return refs.masks[index]

    def across(source, goal, index):
        return pltpu.make_async_remote_copy(
            src_ref=source,
            dst_ref=goal,
            send_sem=refs.psem.at[index],
            recv_sem=refs.qsem.at[index],
            device_id=dict(crops=shard + 1 - 2 * core),
            device_id_type=pl.DeviceIdType.MESH,
        )

    def kernel_pair(m):
        at = pl.multiple_of(low * (1 - core), 8)
        return across(refs.wq.at[m, pl.ds(at, span)], refs.wr.at[m], m)

    outputs_pair = across(refs.blocks.at[1], refs.blockr, 2)
    gradient_pair = across(refs.slopes.at[1], refs.sloper, 3)
    table_pair = across(refs.gg, refs.ggr, 4)
    gather = Gather(refs, core, count)

    def every(action):
        for k in range(4):

            @pl.when(me == k)
            def _():
                action(Branch(k, rows, large, small, 2 * share, refs, Lazy(), core))

    def begin(branch):
        branch.fetch_first()

    def prepare(branch):
        found = branch.segments()
        stops = {0: 1, min(2, len(found) - 2): 2, len(found) - 1: 3}
        for index, (unit, seg) in enumerate(found):
            branch.expand(index)
            if index in stops:
                gather.step(0, stops[index])

    def main(branch):
        branch.unpack(0, branch.take_feature)
        branch.maps["h"].close(0)
        gather.step(1, 0)

        def ahead(m, carry):
            branch.forward(m, gather)
            return carry

        def back(step, carry):
            m = MODULES - 1 - step
            branch.backward(m)
            refs.wq[m] = refs.wgv[pl.ds(quarter, 2 * share)]
            kernel_pair(m).start()
            return carry

        lax.fori_loop(0, MODULES, ahead, 0)
        branch.pack_outputs()
        outputs_pair.start()
        lax.fori_loop(0, MODULES, back, 0)
        branch.pack_gradient()
        gradient_pair.start()
        table_pair.start()

    every(begin)
    greet(core, count)
    gather.step(0, 0)
    fill_masks(refs, rows, core, small, large)
    refs.wgv[pl.ds(quarter, 2 * share)] = jnp.zeros((2 * share, LANES), jnp.float32)
    refs.gg[...] = jnp.zeros(refs.gg.shape, jnp.float32)
    every(prepare)
    gather.collect(0)
    every(main)

    for step in range(MODULES):
        m = MODULES - 1 - step
        kernel_pair(m).wait()
        mine = refs.wq[m, pl.ds(pl.multiple_of(low * core, 8), span)]
        refs.work[pl.ds(m, span, stride=MODULES)] = mine + refs.wr[m]
    skip = pl.multiple_of(core * (MODULES * (share - low)), 8)
    leave = pltpu.make_async_copy(
        refs.work.at[pl.ds(skip, MODULES * share)], refs.wg, refs.osem.at[0]
    )
    leave.start()
    outputs_pair.wait()
    gradient_pair.wait()
    table_pair.wait()
    own = refs.kinds[shard] != core
    refs.out[...] = jnp.where(own, refs.blocks[0].astype(jnp.float32), refs.blockr[...].astype(jnp.float32)).astype(jnp.bfloat16)
    refs.grad[...] = jnp.where(own, refs.slopes[0], refs.sloper[...])
    width = 256 // count
    for which, goal in ((0, refs.gain), (1, refs.shift)):
        for m in range(MODULES):
            total = refs.gg[m, which] + refs.ggr[m, which]
            found = None
            for at in range(count):
                piece = jnp.where(shard == at, total[:, at * width : (at + 1) * width], 0.0)
                found = piece if found is None else found + piece
            goal[m] = found
    gather.finish(0)
    gather.finish(1)
    leave.wait()


def whole_call(rows, large, small, x, cot, w, gains, shifts, kinds):
    count = large + small
    weight_rows = w.shape[0] // MODULES
    table = scratch_table(rows, weight_rows, count)
    vmem = pl.BlockSpec(memory_space=pltpu.VMEM)
    hbm = pl.BlockSpec(memory_space=pl.ANY)
    smem = pl.BlockSpec(memory_space=pltpu.SMEM)
    tables = jax.ShapeDtypeStruct((MODULES, SLOTS, 256 // count), jnp.float32)
    return pl.pallas_call(
        partial(whole_kernel, NAMES + list(table), rows, large, small),
        out_shape=(
            jax.ShapeDtypeStruct((ROWS, LANES), jnp.bfloat16),
            jax.ShapeDtypeStruct((ROWS, LANES), jnp.float32),
            jax.ShapeDtypeStruct((MODULES * weight_rows // count, LANES), jnp.float32),
            tables,
            tables,
        ),
        in_specs=[vmem, vmem, hbm, vmem, vmem, smem],
        out_specs=(vmem, vmem, hbm, vmem, vmem),
        scratch_shapes=list(table.values()),
        compiler_params=pltpu.CompilerParams(
            collective_id=0, has_side_effects=True, vmem_limit_bytes=62 * 1024 * 1024
        ),
    )(x, cot, w, gains, shifts, kinds)


def leave_kernel(*refs):
    for source, goal in zip(refs[:5], refs[5:]):
        goal[...] = source[...]


def leave_call(arrays):
    vmem = pl.BlockSpec(memory_space=pltpu.VMEM)
    return pl.pallas_call(
        leave_kernel,
        out_shape=tuple(jax.ShapeDtypeStruct(array.shape, array.dtype) for array in arrays),
        in_specs=[vmem] * 5,
        out_specs=(vmem,) * 5,
    )(*arrays)


def on_device_grouped(features, weights, gains, shifts, cotangent, size_group):
    count = lax.axis_size("crops")
    large = count // 4
    weight_rows = weights.shape[2] // LANES
    results = whole_call(
        group_rows(count),
        large,
        count - large,
        features[0],
        cotangent[0],
        weights[0]
        .reshape(MODULES, weight_rows, LANES)
        .transpose(1, 0, 2)
        .reshape(MODULES * weight_rows, LANES),
        gains[0],
        shifts[0],
        size_group,
    )
    out, grad, weight_grad, gain, shift = leave_call(results)
    share = weight_rows // count
    weight_grad = weight_grad.reshape(share, MODULES, LANES).transpose(1, 0, 2)
    weight_grad = with_layout_constraint(weight_grad, Layout((1, 0, 2)))
    return (
        out[None],
        grad[None],
        weight_grad.reshape(1, MODULES, share * LANES),
        gain[None],
        shift[None],
    )


def group_rows(count):
    large = count // 4
    rows = max(large * (LH // 8) * (LW // 8), (count - large) * (SH // 8) * (SW // 8))
    return -(-rows // 16) * 16


def fits(count):
    return count % 8 == 0 and group_rows(count) <= 96


def solution(mesh):
    placed = (
        P("branch", "crops", None),
        P("branch", None, None),
        P("branch", None, None, None),
        P("branch", None, None, None),
        P("branch", "crops", None),
        P(),
    )
    return jax.shard_map(
        on_device_grouped if fits(mesh.shape["crops"]) else on_device,
        mesh=mesh,
        in_specs=placed,
        out_specs=(
            P("branch", "crops", None),
            P("branch", "crops", None),
            P("branch", None, "crops"),
            P("branch", None, None, "crops"),
            P("branch", None, None, "crops"),
        ),
        check_vma=False,
    )
```

```python
from functools import partial
from types import SimpleNamespace
import math

import jax
import jax.numpy as jnp
import numpy as np
from jax import lax
from jax.experimental import pallas as pl
from jax.experimental.layout import Layout, with_layout_constraint
from jax.experimental.pallas import tpu as pltpu
from jax.sharding import PartitionSpec as P

C0 = 32
BLOCKS = 1
MODULES = 2
CROPS_DEV = 1
SH = 32
SW = 24
LH = 64
LW = 48
ROWS = 768
MSG_ROWS = 384


EPS = 1e-05


def as_sent(x):

    def short(part):
        return part.astype(jnp.bfloat16) if part.dtype == jnp.float32 else part

    return jax.tree.map(short, x)


def sender_plan(branch_index, top_channels, blocks):
    channels = top_channels << branch_index
    operations = []
    for block_index in range(blocks):
        operations.append(
            SimpleNamespace(
                phase=2 * block_index,
                source=("h", block_index),
                level=branch_index,
                cin=channels,
                cout=channels,
                stride=1,
                taps=3,
                act="silu",
                output=("u", block_index),
                skip=None,
                dest=-1,
            )
        )
        operations.append(
            SimpleNamespace(
                phase=2 * block_index + 1,
                source=("u", block_index),
                level=branch_index,
                cin=channels,
                cout=channels,
                stride=1,
                taps=3,
                act="res",
                output=("h", block_index + 1),
                skip=("h", block_index),
                dest=-1,
            )
        )
    top_name = ("h", blocks)
    for target in range(branch_index):
        operations.append(
            SimpleNamespace(
                phase=2 * blocks,
                source=top_name,
                level=branch_index,
                cin=channels,
                cout=top_channels << target,
                stride=1,
                taps=1,
                act="none",
                output=None,
                skip=None,
                dest=target,
            )
        )
    for target in range(branch_index + 1, 4):
        for depth_step in range(1, target - branch_index + 1):
            is_last = depth_step == target - branch_index
            operations.append(
                SimpleNamespace(
                    phase=2 * blocks + depth_step - 1,
                    source=top_name if depth_step == 1 else ("chain", target, depth_step - 1),
                    level=branch_index + depth_step,
                    cin=channels,
                    cout=top_channels << target if is_last else channels,
                    stride=2,
                    taps=3,
                    act="none" if is_last else "silu",
                    output=None if is_last else ("chain", target, depth_step),
                    skip=None,
                    dest=target if is_last else -1,
                )
            )
    for position, operation in enumerate(operations):
        operation.slot = position
        operation.size = (
            operation.taps * operation.taps * operation.cin * operation.cout
        )
        if operation.taps == 1:
            operation.kshape = (operation.cin, operation.cout)
        else:
            operation.kshape = (3, 3, operation.cin, operation.cout)
    return operations


def phase_lengths(top_channels, blocks):
    phase_count = 2 * blocks + 3
    lengths = [0] * phase_count
    for branch_index in range(4):
        per_phase = [0] * phase_count
        for operation in sender_plan(branch_index, top_channels, blocks):
            per_phase[operation.phase] += operation.size
        lengths = [max(current, candidate) for current, candidate in zip(lengths, per_phase)]
    return lengths


def weighted_plan(branch_index, top_channels, blocks):
    lengths = phase_lengths(top_channels, blocks)
    starts = [sum(lengths[:phase_index]) for phase_index in range(len(lengths))]
    running = [0] * len(lengths)
    operations = sender_plan(branch_index, top_channels, blocks)
    for operation in operations:
        phase_index = operation.phase
        operation.inner = running[phase_index]
        operation.offset = starts[phase_index] + running[phase_index]
        operation.position = sum(
            (1 for earlier in operations[: operation.slot] if earlier.phase == phase_index)
        )
        running[phase_index] += operation.size
    return operations


def phase_operations(branch_index, phase_index):
    return [
        operation
        for operation in weighted_plan(branch_index, C0, BLOCKS)
        if operation.phase == phase_index
    ]


def input_names(operations):
    source_names = []
    for operation in operations:
        if operation.source not in source_names:
            source_names.append(operation.source)
    return source_names


def silu_slope(value):
    sigmoid = jax.nn.sigmoid(value)
    return sigmoid * (1.0 + value * (1.0 - sigmoid))


def crop_cells(size_kind):
    return (LH, LW) if size_kind else (SH, SW)


def map_dims(size_kind, level, channels):
    height, breadth = crop_cells(size_kind)
    return (CROPS_DEV, height >> level, breadth >> level, channels)


def source_dims(branch_index, size_kind, map_name):
    level = branch_index + map_name[2] if map_name[0] == "chain" else branch_index
    return map_dims(size_kind, level, C0 << branch_index)


def preact_dims(size_kind, operation):
    return map_dims(size_kind, operation.level, operation.cout)


def to_canvas(arrays, value_type):
    if not arrays:
        return jnp.zeros((ROWS, 128), value_type)
    flattened = jnp.concatenate([array.reshape(-1).astype(value_type) for array in arrays])
    return jnp.pad(flattened, (0, ROWS * 128 - flattened.shape[0])).reshape(ROWS, 128)


def from_canvas(canvas, dims_list):
    flattened = canvas.reshape(-1)
    pieces = []
    offset = 0
    for dims_entry in dims_list:
        count_here = math.prod(dims_entry)
        pieces.append(flattened[offset : offset + count_here].reshape(dims_entry))
        offset += count_here
    return pieces


def to_slot(array):
    flattened = array.reshape(-1)
    return jnp.pad(flattened, (0, MSG_ROWS * 128 - flattened.shape[0])).reshape(MSG_ROWS, 128)


def from_slot(slot_rows, dims_entry):
    return slot_rows.reshape(-1)[: math.prod(dims_entry)].reshape(dims_entry)


def upsample(message, factor):
    crop_count, height, breadth, channels = message.shape
    widened = jnp.broadcast_to(
        message[:, :, None, :, None, :], (crop_count, height, factor, breadth, factor, channels)
    )
    return widened.reshape(crop_count, height * factor, breadth * factor, channels)


def block_pool(array, factor):
    crop_count, height, breadth, channels = array.shape
    return array.reshape(
        crop_count, height // factor, factor, breadth // factor, factor, channels
    ).sum(axis=(2, 4))


def kernel_piece(module_weights, operation):
    start = operation.offset
    return module_weights[start : start + operation.size].reshape(operation.kshape)


def conv_forward(operation, source, kernel):
    if operation.taps == 1:
        return jnp.einsum("nhwc,cd->nhwd", source, kernel, preferred_element_type=jnp.float32)
    stride = operation.stride
    return lax.conv_general_dilated(
        source,
        kernel,
        (stride, stride),
        ((1, 1), (1, 1)),
        dimension_numbers=("NHWC", "HWIO", "NHWC"),
        preferred_element_type=jnp.float32,
    )


def conv_backward(operation, source, kernel, upstream):
    if operation.taps == 1:
        source_grad = jnp.einsum(
            "nhwd,cd->nhwc", upstream, kernel, preferred_element_type=jnp.float32
        )
        kernel_grad = jnp.einsum(
            "nhwc,nhwd->cd", source, upstream, preferred_element_type=jnp.float32
        )
        return (source_grad, kernel_grad)
    stride = operation.stride
    flipped = jnp.transpose(kernel[::-1, ::-1], (0, 1, 3, 2))
    high_pad = 2 if stride == 2 else 1
    source_grad = lax.conv_general_dilated(
        upstream,
        flipped,
        (1, 1),
        ((1, high_pad), (1, high_pad)),
        lhs_dilation=(stride, stride),
        dimension_numbers=("NHWC", "HWIO", "NHWC"),
        preferred_element_type=jnp.float32,
    )
    kernel_grad = lax.conv_general_dilated(
        source,
        upstream,
        (1, 1),
        ((1, 2 - stride), (1, 2 - stride)),
        rhs_dilation=(stride, stride),
        dimension_numbers=("CHWN", "IHWO", "NHWC"),
        preferred_element_type=jnp.float32,
    )
    return (source_grad, jnp.transpose(kernel_grad, (1, 2, 0, 3)))


def cell_total(counts, size_kind, level):
    height, breadth = crop_cells(size_kind)
    return counts[size_kind] * float(CROPS_DEV * (height >> level) * (breadth >> level))


def norm_terms(totals, counts, size_kind, operation):
    cells_here = cell_total(counts, size_kind, operation.level)
    channels = operation.cout
    position = operation.position
    average = totals[size_kind, 0, position, :channels] / cells_here
    variance = totals[size_kind, 1, position, :channels] / cells_here - average * average
    return (average, lax.rsqrt(variance + EPS))


def forward_conv(branch_index, size_kind, phase_index, source_canvas, module_weights):
    operations = phase_operations(branch_index, phase_index)
    source_names = input_names(operations)
    pieces = from_canvas(
        source_canvas, [source_dims(branch_index, size_kind, map_name) for map_name in source_names]
    )
    sources = {
        map_name: piece.astype(jnp.bfloat16) for map_name, piece in zip(source_names, pieces)
    }
    preacts = []
    totals = jnp.zeros((2, 2, 3, 8 * C0), jnp.float32)
    for operation in operations:
        preact = conv_forward(
            operation, sources[operation.source], kernel_piece(module_weights, operation)
        )
        preacts.append(preact)
        channels = operation.cout
        position = operation.position
        totals = totals.at[size_kind, 0, position, :channels].set(jnp.sum(preact, axis=(0, 1, 2)))
        totals = totals.at[size_kind, 1, position, :channels].set(
            jnp.sum(preact * preact, axis=(0, 1, 2))
        )
    return (to_canvas(preacts, jnp.float32), totals)


def forward_norm(
    branch_index,
    size_kind,
    phase_index,
    preact_canvas,
    totals,
    counts,
    module_gains,
    module_shifts,
    skip_canvas,
    message_buffer,
):
    operations = phase_operations(branch_index, phase_index)
    preacts = from_canvas(
        preact_canvas, [preact_dims(size_kind, operation) for operation in operations]
    )
    skip_map = from_canvas(skip_canvas, [map_dims(size_kind, branch_index, C0 << branch_index)])[0]
    produced = []
    for operation, preact in zip(operations, preacts):
        average, inverse_std = norm_terms(totals, counts, size_kind, operation)
        norm_slot = operation.slot
        channels = operation.cout
        normed = (preact - average) * inverse_std * module_gains[
            norm_slot, :channels
        ] + module_shifts[norm_slot, :channels]
        if operation.act == "silu":
            produced.append(jax.nn.silu(normed))
        elif operation.act == "res":
            produced.append(jax.nn.silu(normed + skip_map))
        else:
            message_buffer = message_buffer.at[operation.dest].set(
                to_slot(normed.astype(jnp.bfloat16))
            )
    return (to_canvas(produced, jnp.float32), message_buffer)


def receive_forward(branch_index, size_kind, top_canvas, received):
    channels = C0 << branch_index
    summed = from_canvas(top_canvas, [map_dims(size_kind, branch_index, channels)])[0]
    for sender in range(4):
        if sender < branch_index:
            summed = summed + from_slot(
                received[sender], map_dims(size_kind, branch_index, channels)
            ).astype(jnp.float32)
        elif sender > branch_index:
            coarse = from_slot(received[sender], map_dims(size_kind, sender, channels))
            summed = summed + upsample(coarse, 2 ** (sender - branch_index)).astype(jnp.float32)
    return (to_canvas([jax.nn.silu(summed)], jnp.float32), to_canvas([summed], jnp.float32))


def receive_backward(branch_index, size_kind, grad_canvas, summed_canvas):
    dims_here = map_dims(size_kind, branch_index, C0 << branch_index)
    upstream = from_canvas(grad_canvas, [dims_here])[0]
    summed = from_canvas(summed_canvas, [dims_here])[0]
    summed_grad = upstream * silu_slope(summed)
    buffer = jnp.zeros((4, MSG_ROWS, 128), jnp.bfloat16)
    for sender in range(4):
        if sender < branch_index:
            buffer = buffer.at[sender].set(to_slot(summed_grad.astype(jnp.bfloat16)))
        elif sender > branch_index:
            pooled = block_pool(summed_grad, 2 ** (sender - branch_index))
            buffer = buffer.at[sender].set(to_slot(pooled.astype(jnp.bfloat16)))
    return (to_canvas([summed_grad], jnp.float32), buffer)


def backward_stats(
    branch_index,
    size_kind,
    phase_index,
    dout_canvas,
    message_grads,
    preact_canvas,
    totals,
    counts,
    module_gains,
    module_shifts,
    skip_canvas,
):
    operations = phase_operations(branch_index, phase_index)
    preacts = from_canvas(
        preact_canvas, [preact_dims(size_kind, operation) for operation in operations]
    )
    producing = [operation for operation in operations if operation.act != "none"]
    output_grads = from_canvas(
        dout_canvas, [preact_dims(size_kind, operation) for operation in producing]
    )
    grads_by_name = {
        operation.output: piece for operation, piece in zip(producing, output_grads)
    }
    skip_map = from_canvas(skip_canvas, [map_dims(size_kind, branch_index, C0 << branch_index)])[0]
    upstreams = []
    skip_grads = []
    sums_local = jnp.zeros((2, 2, 3, 8 * C0), jnp.float32)
    for operation, preact in zip(operations, preacts):
        average, inverse_std = norm_terms(totals, counts, size_kind, operation)
        norm_slot = operation.slot
        channels = operation.cout
        centered = (preact - average) * inverse_std
        normed = centered * module_gains[norm_slot, :channels] + module_shifts[norm_slot, :channels]
        if operation.act == "silu":
            upstream = grads_by_name[operation.output] * silu_slope(normed)
        elif operation.act == "res":
            upstream = grads_by_name[operation.output] * silu_slope(normed + skip_map)
            skip_grads.append(upstream)
        else:
            upstream = from_slot(
                message_grads[operation.dest], preact_dims(size_kind, operation)
            ).astype(jnp.float32)
        upstreams.append(upstream)
        position = operation.position
        sums_local = sums_local.at[size_kind, 0, position, :channels].set(
            jnp.sum(upstream, axis=(0, 1, 2))
        )
        sums_local = sums_local.at[size_kind, 1, position, :channels].set(
            jnp.sum(upstream * centered, axis=(0, 1, 2))
        )
    return (to_canvas(upstreams, jnp.float32), sums_local, to_canvas(skip_grads, jnp.float32))


def backward_apply(
    branch_index,
    size_kind,
    phase_index,
    upstream_canvas,
    preact_canvas,
    totals,
    grad_totals,
    counts,
    source_canvas,
    module_weights,
    module_gains,
):
    operations = phase_operations(branch_index, phase_index)
    preacts = from_canvas(
        preact_canvas, [preact_dims(size_kind, operation) for operation in operations]
    )
    upstreams = from_canvas(
        upstream_canvas, [preact_dims(size_kind, operation) for operation in operations]
    )
    source_names = input_names(operations)
    source_list = [source_dims(branch_index, size_kind, map_name) for map_name in source_names]
    pieces = from_canvas(source_canvas, source_list)
    sources = {
        map_name: piece.astype(jnp.bfloat16) for map_name, piece in zip(source_names, pieces)
    }
    source_grads = {
        map_name: jnp.zeros(dims_entry, jnp.float32)
        for map_name, dims_entry in zip(source_names, source_list)
    }
    kernel_grads = []
    slot_count = module_gains.shape[0]
    gain_part = jnp.zeros((slot_count, 8 * C0), jnp.float32)
    shift_part = jnp.zeros((slot_count, 8 * C0), jnp.float32)
    for operation, preact, upstream in zip(operations, preacts, upstreams):
        average, inverse_std = norm_terms(totals, counts, size_kind, operation)
        cells_here = cell_total(counts, size_kind, operation.level)
        norm_slot = operation.slot
        channels = operation.cout
        position = operation.position
        centered = (preact - average) * inverse_std
        mean_upstream = grad_totals[size_kind, 0, position, :channels] / cells_here
        mean_cross = grad_totals[size_kind, 1, position, :channels] / cells_here
        preact_grad = (
            module_gains[norm_slot, :channels]
            * inverse_std
            * (upstream - mean_upstream - centered * mean_cross)
        )
        source_grad, kernel_grad = conv_backward(
            operation,
            sources[operation.source],
            kernel_piece(module_weights, operation),
            preact_grad.astype(jnp.bfloat16),
        )
        source_grads[operation.source] = source_grads[operation.source] + source_grad
        kernel_grads.append(kernel_grad.reshape(-1))
        gain_part = gain_part.at[norm_slot, :channels].set(
            grad_totals[0, 1, position, :channels] + grad_totals[1, 1, position, :channels]
        )
        shift_part = shift_part.at[norm_slot, :channels].set(
            grad_totals[0, 0, position, :channels] + grad_totals[1, 0, position, :channels]
        )
    phase_length = phase_lengths(C0, BLOCKS)[phase_index]
    if kernel_grads:
        joined = jnp.concatenate(kernel_grads)
        weight_part = jnp.pad(joined, (0, phase_length - joined.shape[0]))
    else:
        weight_part = jnp.zeros((phase_length,), jnp.float32)
    return (
        to_canvas([source_grads[map_name] for map_name in source_names], jnp.float32),
        weight_part,
        gain_part,
        shift_part,
    )


def on_device(features, weights, gains, shifts, cotangent, size_group):
    crop_shard = lax.axis_index("crops")
    shard_count = lax.axis_size("crops")
    crop_kind = size_group[crop_shard]
    large_count = jnp.sum(size_group).astype(jnp.float32)
    counts = jnp.stack([shard_count - large_count, large_count])
    case_index = lax.axis_index("branch") * 2 + crop_kind
    phase_total = 2 * BLOCKS + 3
    zero_canvas = jnp.zeros((ROWS, 128), jnp.float32)
    empty_buffer = jnp.zeros((4, MSG_ROWS, 128), jnp.bfloat16)

    def run_phase(function, statics, operands):
        branches_list = [
            partial(function, branch_index, size_kind, *statics)
            for branch_index in range(4)
            for size_kind in range(2)
        ]
        return lax.switch(case_index, branches_list, *operands)

    def statistics(local_totals):
        return lax.psum(local_totals, "crops")

    def module_forward(module, start_canvas, kept):
        module_weights = weights[0, module]
        module_gains = gains[0, module]
        module_shifts = shifts[0, module]
        record = SimpleNamespace(sources=[], preacts=[], totals=[])
        h_canvas = start_canvas
        u_canvas = zero_canvas
        chain_canvas = zero_canvas
        buffer = empty_buffer
        for phase_index in range(phase_total):
            if phase_index < 2 * BLOCKS:
                source = h_canvas if phase_index % 2 == 0 else u_canvas
            elif phase_index == 2 * BLOCKS:
                source = h_canvas
            else:
                source = chain_canvas
            preact, local_totals = run_phase(forward_conv, (phase_index,), (source, module_weights))
            global_totals = kept.totals[phase_index] if kept else statistics(local_totals)
            produced, buffer = run_phase(
                forward_norm,
                (phase_index,),
                (preact, global_totals, counts, module_gains, module_shifts, h_canvas, buffer),
            )
            record.sources.append(source)
            record.preacts.append(preact)
            record.totals.append(global_totals)
            if phase_index < 2 * BLOCKS:
                if phase_index % 2 == 0:
                    u_canvas = produced
                else:
                    h_canvas = produced
            else:
                chain_canvas = produced
        received = (
            kept.received
            if kept
            else jax.tree.map(
                lambda part, own: part.astype(own.dtype),
                lax.all_to_all(as_sent(buffer), "branch", split_axis=0, concat_axis=0, tiled=True),
                buffer,
            )
        )
        result, summed = run_phase(receive_forward, (), (h_canvas, received))
        record.summed = summed
        record.received = received
        return (result, record)

    checkpoints = [features[0].astype(jnp.float32)]
    first_records = []
    for module in range(MODULES):
        result, record = module_forward(module, checkpoints[-1], None)
        checkpoints.append(result)
        first_records.append(record)
    outputs = checkpoints[-1].astype(jnp.bfloat16)
    grad_canvas = cotangent[0].astype(jnp.float32)
    module_grads = [None] * MODULES
    gain_grads = [None] * MODULES
    shift_grads = [None] * MODULES
    for module in reversed(range(MODULES)):
        kept = None
        unused_result, record = module_forward(module, checkpoints[module], kept)
        module_module_weights = weights[0, module]
        module_module_gains = gains[0, module]
        module_module_shifts = shifts[0, module]
        summed_grad, back_buffer = run_phase(receive_backward, (), (grad_canvas, record.summed))
        message_grads = jax.tree.map(
            lambda part, own: part.astype(own.dtype),
            lax.all_to_all(as_sent(back_buffer), "branch", split_axis=0, concat_axis=0, tiled=True),
            back_buffer,
        )
        top_grad = summed_grad
        chain_grad = zero_canvas
        u_grad = zero_canvas
        pending_skip = zero_canvas
        weight_parts = [None] * phase_total
        gain_total = jnp.zeros(gains.shape[2:], jnp.float32)
        shift_total = jnp.zeros(gains.shape[2:], jnp.float32)
        for module_phase_index in reversed(range(phase_total)):
            if module_phase_index >= 2 * BLOCKS:
                output_grad = chain_grad
                skip_canvas = zero_canvas
            elif module_phase_index % 2 == 1:
                output_grad = top_grad
                skip_canvas = record.sources[module_phase_index - 1]
            else:
                output_grad = u_grad
                skip_canvas = zero_canvas
            module_preact = record.preacts[module_phase_index]
            totals = record.totals[module_phase_index]
            upstream, module_local_totals, skip_grad = run_phase(
                backward_stats,
                (module_phase_index,),
                (
                    output_grad,
                    message_grads,
                    module_preact,
                    totals,
                    counts,
                    module_module_gains,
                    module_module_shifts,
                    skip_canvas,
                ),
            )
            grad_totals = lax.psum(module_local_totals, "crops")
            source_grad, weight_parts[module_phase_index], gain_part, shift_part = run_phase(
                backward_apply,
                (module_phase_index,),
                (
                    upstream,
                    module_preact,
                    totals,
                    grad_totals,
                    counts,
                    record.sources[module_phase_index],
                    module_module_weights,
                    module_module_gains,
                ),
            )
            gain_total = gain_total + gain_part
            shift_total = shift_total + shift_part
            if module_phase_index > 2 * BLOCKS:
                chain_grad = source_grad
            elif module_phase_index == 2 * BLOCKS:
                top_grad = top_grad + source_grad
            elif module_phase_index % 2 == 1:
                u_grad = source_grad
                pending_skip = skip_grad
            else:
                top_grad = source_grad + pending_skip
        joined = jnp.concatenate(weight_parts)
        weight_grad = jnp.pad(joined, (0, weights.shape[2] - joined.shape[0]))
        grad_canvas, weight_grad, gain_grads[module], shift_grads[module] = (
            top_grad,
            weight_grad,
            gain_total,
            shift_total,
        )
        module_grads[module] = weight_grad
    weight_out = lax.psum_scatter(jnp.stack(module_grads), "crops", scatter_dimension=1, tiled=True)
    share = gains.shape[3] // shard_count
    gain_out = lax.dynamic_slice_in_dim(jnp.stack(gain_grads), crop_shard * share, share, axis=2)
    shift_out = lax.dynamic_slice_in_dim(jnp.stack(shift_grads), crop_shard * share, share, axis=2)
    return (outputs[None], grad_canvas[None], weight_out[None], gain_out[None], shift_out[None])


LANES = 128
SLOTS = 8
MASKS = 7
DOWN = (((1,), (0,)), ((), ()))
ACROSS = (((1,), (1,)), ((), ()))
ALONG = (((0,), (0,)), ((), ()))


def unit_table(k):
    operations = weighted_plan(k, C0, BLOCKS)
    planes = 8 >> k
    channels = C0 << k
    units = {}
    stat = 0

    def add(name, kind, source, lanes_in, planes_in, planes_out, members):
        nonlocal stat
        segs = []
        tile = 0
        for operation, lanes, chain in members:
            cout = operation.cout
            level = operation.level if operation.taps == 3 else operation.dest
            segs.append(
                SimpleNamespace(
                    slot=operation.slot,
                    off=operation.offset // LANES,
                    cin=operation.cin,
                    cout=cout,
                    taps=operation.taps,
                    tile=tile,
                    tiles=lanes // LANES,
                    blocks=max(1, (8 >> level)),
                    dest=operation.dest,
                    act=operation.act,
                    chain=chain,
                    up=k - operation.dest if operation.taps == 1 else 0,
                )
            )
            tile += lanes // LANES
        rows = {"s1": 768 if k == 3 else 512, "s2": lanes_in + LANES, "p1": 256}[kind]
        units[name] = SimpleNamespace(
            name=name,
            kind=kind,
            source=source,
            lanes_in=lanes_in,
            blocks_in=planes_in,
            planes_in=planes_in,
            planes=planes_out,
            segs=segs,
            tiles=tile,
            rows=rows,
            stat=stat,
            depth=1 if kind == "p1" else 3,
        )
        stat += tile

    add("a", "s1", "h", 256, planes, planes, [(operations[0], 256, None)])
    add("b", "s1", "u", 256, planes, planes, [(operations[1], 256, None)])
    ups = [operation for operation in operations if operation.taps == 1]
    if ups:
        add("u", "p1", "t", 256, planes, planes, [(operation, 256, None) for operation in ups])
    firsts, chains = [], {}
    for target in range(k + 1, 4):
        steps = [
            operation
            for operation in operations
            if operation.taps == 3 and operation.stride == 2
        ]
        start = sum(i - k for i in range(k + 1, target))
        chains[target] = steps[start : start + target - k]
        if target == k + 1:
            firsts.append((chains[target][0], 256, None))
        else:
            firsts.append((chains[target][0], LANES, "c1" if target == k + 2 else "c2"))
    if firsts:
        add("d", "s2", "t", 256, planes, planes // 2, firsts)
    if k <= 1:
        add("e", "s2", "c1", LANES, planes // 2, planes // 4, [(chains[k + 2][1], 256, None)])
    if k == 0:
        add("f", "s2", "c2", LANES, planes // 2, planes // 4, [(chains[3][1], LANES, "c3")])
        add("g", "s2", "c3", LANES, planes // 4, planes // 8, [(chains[3][2], 256, None)])
    return units


def links(k, unit, seg):
    cin = seg.cin
    count_in, count_out = unit.blocks_in, seg.blocks
    found = []
    if unit.kind == "p1":
        for plane in range(count_in):
            wide = 1 << seg.up
            found.append((plane * cin, 0, set(range(plane * wide, plane * wide + wide))))
        return found
    if unit.kind == "s1" and k == 3:
        return [(256 * tap, tap, {0}) for tap in range(3)]
    stride = 1 if unit.kind == "s1" else 2
    for plane in range(count_in):
        for tap in range(3):
            at = plane - tap + 1
            if at % stride == 0 and 0 <= at // stride < count_out:
                found.append((plane * cin, tap, {at // stride}))
    if stride == 1:
        found.append((256, 2, {count_out - 1}))
        found.append((512 - cin, 0, {0}))
    else:
        lanes_in = unit.lanes_in
        found.append((lanes_in + (count_in - 1) * cin - (lanes_in - LANES), 0, {0}))
    return found


def message_slot(k, other):
    return sum(2 * (8 >> max(k, before)) for before in range(other) if before != k)


def log2(value):
    return value.bit_length() - 1


def sigmoid_of(value):
    return 0.5 * jnp.tanh(0.5 * value) + 0.5


def silu_of(value):
    return value * sigmoid_of(value)


def slope_of(value):
    sigmoid = sigmoid_of(value)
    return sigmoid * (1.0 + value * (1.0 - sigmoid))


def planes_loop(count, body, turns=1):
    def step(index, carry):
        for turn in range(turns):
            body(index * turns + turn)
        return carry

    turns = min(turns, count)
    if count == turns:
        for index in range(count):
            body(index)
    else:
        lax.fori_loop(0, count // turns, step, 0)


def planes_sum(count, body, initial, turns=1):
    def step(index, carry):
        for turn in range(turns):
            carry = body(index * turns + turn, carry)
        return carry

    turns = min(turns, count)
    if count == turns:
        return step(0, initial)
    return lax.fori_loop(0, count // turns, step, initial)


def partial_sum(value):
    rows = value.shape[0]
    return jnp.sum(value.reshape(rows // 8, 8, value.shape[1]), axis=0)


class Planes:
    def __init__(self, mode, tiles, planes, masks, rows, main, edge=None, right=None):
        self.mode, self.tiles, self.planes = mode, tiles, planes
        self.masks, self.rows = masks, rows
        self.main, self.edge, self.right = main, edge, right
        self.base = 1 if mode in ("s1", "wide", "s2") else 0
        extra = {"s1": 2, "wide": 2, "s2": 1, "dz2": 1, "p": 0}[mode]
        self.span = planes + extra
        self.unit = tiles * self.span

    def at(self, m, tile, plane):
        return m * self.unit + tile * self.span + plane + self.base

    def edge_at(self, m, tile, plane):
        if self.mode == "s2":
            return m * self.span + plane + self.base
        return self.at(m, tile, plane)

    def from_left(self, value):
        return pltpu.roll(value, 1, 0) * self.masks[1]

    def from_right(self, value):
        return pltpu.roll(value, self.rows - 1, 0) * self.masks[2]

    def store(self, m, tile, plane, value):
        self.put(m, tile, plane, value)

    def put(self, m, tile, plane, value):
        where = self.at(m, tile, plane)
        self.main[where] = value.astype(jnp.bfloat16)
        if self.mode == "s1":
            side = self.from_right(value) if tile == 0 else self.from_left(value)
            self.edge[where] = side.astype(jnp.bfloat16)
        elif self.mode == "wide":
            self.edge[where] = self.from_left(value).astype(jnp.bfloat16)
            self.right[where] = self.from_right(value).astype(jnp.bfloat16)
        elif self.mode == "s2":
            if tile == self.tiles - 1:
                self.edge[self.edge_at(m, tile, plane)] = self.from_left(value).astype(jnp.bfloat16)
        elif self.mode == "dz2":
            self.edge[where] = self.from_right(value).astype(jnp.bfloat16)

    def put_above(self, m, tile, last):
        if self.mode in ("s1", "wide", "s2"):
            above = pltpu.roll(last, 6, 0) * self.masks[3] + pltpu.roll(last, 3, 0) * self.masks[4]
            self.put(m, tile, -1, above)

    def put_below(self, m, tile, first):
        if self.mode in ("s1", "wide", "dz2"):
            rows = self.rows
            below = (
                pltpu.roll(first, rows - 6, 0) * self.masks[5]
                + pltpu.roll(first, rows - 3, 0) * self.masks[6]
            )
            self.put(m, tile, self.planes, below)

    def close(self, m):
        for tile in range(self.tiles):
            last = self.main[self.at(m, tile, self.planes - 1)].astype(jnp.float32)
            self.put_above(m, tile, last)
            first = self.main[self.at(m, tile, 0)].astype(jnp.float32)
            self.put_below(m, tile, first)


class Branch:
    def __init__(self, k, rows, large, small, share, refs, masks, core):
        self.k, self.rows, self.refs, self.masks = k, rows, refs, masks
        self.units = unit_table(k)
        self.planes = 8 >> k
        self.core = core
        self.large, self.small, self.count = large, small, large + small
        self.cells = (small * (SH // 8) * (SW // 8), large * (LH // 8) * (LW // 8))
        self.quarter = lax.axis_index("crops") // 2
        self.share = share
        r = refs
        make = partial(Planes, masks=masks, rows=rows)
        one = "wide" if k == 3 else "s1"
        self.maps = dict(
            h=make(one, 2, self.planes, main=r.hC, edge=r.hE, right=r.hR),
            u=make(one, 2, self.planes, main=r.uC, edge=r.uE, right=r.uR),
            t=make("p" if k == 3 else "s2", 2, self.planes, main=r.tC, edge=r.tE),
        )
        if k <= 1:
            self.maps["c1"] = make("s2", 1, self.planes // 2, main=r.c1C, edge=r.c1E)
        if k == 0:
            self.maps["c2"] = make("s2", 1, 4, main=r.c2C, edge=r.c2E)
            self.maps["c3"] = make("s2", 1, 2, main=r.c3C, edge=r.c3E)
        self.grads = dict(t=r.gt, u=r.gu, c1=r.gc1, c2=r.gc2, c3=r.gc3)

    def lane_block(self, shape, cout):
        lanes = lax.broadcasted_iota(jnp.int32, shape, 1)
        return lanes >> log2(cout)

    def keep(self, value, cout, which):
        count = LANES // cout
        if len(which) == count:
            return value
        block = self.lane_block(value.shape, cout)
        mask = block == which[0]
        for entry in which[1:]:
            mask = mask | (block == entry)
        return jnp.where(mask, value, 0.0)

    def spread(self, value, cout):
        shift = LANES // 2
        while shift >= cout:
            value = value + pltpu.roll(value, shift, 1)
            shift //= 2
        return value

    def local_blocks(self, seg, tile, wanted):
        count = LANES // seg.cout
        return [q for q in range(count) if (tile * count + q) % seg.blocks in wanted]


    def segments(self):
        return [(unit, seg) for unit in self.units.values() for seg in unit.segs]

    def pieces(self):
        found, place = [], 0
        for index, (unit, seg) in enumerate(self.segments()):
            count = 2 * seg.taps**2 * seg.cin * seg.cout // LANES
            if self.k < 3:
                found.append((index, 0, count, place, index))
                place += count
            else:
                for d in range(unit.depth):
                    slot = len(found) % 3
                    found.append((index, d, count // unit.depth, slot * 3072, slot))
        return found

    def fetch(self, at):
        r = self.refs
        index, d, count, place, sem = self.pieces()[at]
        _, seg = self.segments()[index]
        return pltpu.make_async_copy(
            r.w.at[pl.ds(2 * seg.off + d * count, count)],
            r.raw.at[pl.ds(place, count)],
            r.wsem.at[sem],
        )

    def fetch_first(self):
        for at in range(len(self.pieces()) if self.k < 3 else 3):
            self.fetch(at).start()

    def expand(self, index):
        unit, seg = self.segments()[index]
        pieces = self.pieces()
        mine = [at for at, piece in enumerate(pieces) if piece[0] == index]
        if self.k < 3:
            (at,) = mine
            self.fetch(at).wait()
            count = pieces[at][2] // unit.depth
            planes_loop(
                unit.depth,
                lambda d: self.expand_row(unit, seg, d, count, pieces[at][3] + d * count),
            )
        else:
            for d, at in enumerate(mine):
                self.fetch(at).wait()
                self.expand_row(unit, seg, d, pieces[at][2], pieces[at][3])
                if at + 3 < len(pieces):
                    self.fetch(at + 3).start()
        for m in range(MODULES):
            self.spread_tables(m, unit, seg)

    def expand_row(self, unit, seg, d, count, place):
        r = self.refs
        chunk = math.gcd(count, 384)
        wf, rep = r.work, r.rep

        def widen(step):
            at = pl.multiple_of(step * chunk, 16)
            value = r.raw[pl.ds(pl.multiple_of(place + at, 16), chunk)].astype(jnp.float32)
            wf[pl.ds(at, chunk)] = value

        planes_loop(count // chunk, widen)
        count = count // MODULES
        depth, cin, cout = unit.depth, seg.cin, seg.cout
        target = getattr(r, "T" + unit.name)
        twice = unit.kind == "s1" and self.k < 3
        across = getattr(r, "T" + unit.name + unit.name) if twice else None
        by_row = {}
        for row, tap, wanted in links(self.k, unit, seg):
            by_row.setdefault(row, []).append((tap, wanted))

        def module(m):
            if cout < LANES:
                ratio = LANES // cout
                flat = wf[pl.ds(m, count, stride=2)]
                for part in range(ratio):
                    rep[pl.ds(part, count, stride=ratio)] = self.spread(
                        self.keep(flat, cout, [part]), cout
                    )

            def tap_rows(tap, tile):
                if cout < LANES:
                    return rep[tap * cin : (tap + 1) * cin]
                if cout == LANES:
                    return wf[pl.ds(m + tap * (2 * cin), cin, stride=2)]
                return wf[pl.ds(m + tap * (4 * cin) + 2 * tile, cin, stride=4)]

            for tile in range(seg.tiles):
                column = (seg.tile + tile) * LANES
                for row in range(0, unit.rows, cin):
                    total = None
                    for tap, wanted in by_row.get(row, []):
                        if cout <= LANES:
                            local = self.local_blocks(seg, tile, wanted)
                            if not local:
                                continue
                            piece = self.keep(tap_rows(tap, 0), cout, local)
                        else:
                            piece = tap_rows(tap, tile)
                        total = piece if total is None else total + piece
                    if total is None:
                        total = jnp.zeros((cin, LANES), jnp.float32)
                    block = total.astype(jnp.bfloat16)
                    target[m * depth + d, row : row + cin, column : column + LANES] = block
                    if across is not None:
                        first, lane = row % 256, row // 256 * 256 + column
                        across[m * depth + d, first : first + cin, lane : lane + LANES] = block

        planes_loop(MODULES, module)


    def parts(self, unit, source):
        if unit.kind == "p1":
            return [(source.main, range(2), source.at)]
        if source.mode == "wide":
            return [
                (source.edge, range(2), source.at),
                (source.main, range(2), source.at),
                (source.right, range(2), source.at),
            ]
        if unit.kind == "s1":
            return [(source.main, range(2), source.at), (source.edge, range(2), source.at)]
        last = source.tiles - 1
        return [
            (source.main, range(source.tiles), source.at),
            (source.edge, [last], source.edge_at),
        ]

    def rows_of(self, unit, part, m, d, first, count):
        ref, tiles, at = part
        pieces = []
        for tile in tiles:
            if unit.kind == "s2":
                rows = [ref[at(m, tile, 2 * (first + q) + d - 1)] for q in range(count)]
                pieces.append(rows[0] if count == 1 else jnp.concatenate(rows, axis=0))
            else:
                shift = d - 1 if unit.kind == "s1" else 0
                pieces.append(
                    ref[pl.ds(at(m, tile, first + shift), count)].reshape(count * self.rows, LANES)
                )
        return pieces

    def conv(self, m, unit):
        r = self.refs
        source = self.maps[unit.source]
        target = getattr(r, "T" + unit.name)
        z = getattr(r, "z" + unit.name)
        planes, tiles, depth = unit.planes, unit.tiles, unit.depth
        chunk = 1
        lanes = tiles * LANES

        def body(step, sums):
            first = step * chunk
            pieces = []
            for d in range(depth):
                for part in self.parts(unit, source):
                    pieces += self.rows_of(unit, part, m, d, first, chunk)
            left = jnp.concatenate(pieces, axis=1)
            right = target[pl.ds(m * depth, depth), 0 : unit.rows, 0:lanes]
            right = right.reshape(depth * unit.rows, lanes)
            result = lax.dot_general(left, right, DOWN, preferred_element_type=jnp.float32)
            for tile in range(tiles):
                block = result[:, tile * LANES : (tile + 1) * LANES]
                z[pl.ds(m * tiles * planes + tile * planes + first, chunk)] = block.reshape(
                    chunk, self.rows, LANES
                )
            return (sums[0] + partial_sum(result), sums[1] + partial_sum(result * result))

        zero = jnp.zeros((8, lanes), jnp.float32)
        sums = planes_sum(planes // chunk, body, (zero, zero))
        for seg in unit.segs:
            scale = self.per_cell(unit, seg)
            totals = self.fold(seg, sums)
            self.norm_rows(m, unit, seg, totals, scale)

    def per_cell(self, unit, seg):
        blocks = seg.tiles * LANES // seg.cout
        small, large = self.cells
        count = unit.planes * blocks
        return jnp.where(self.core == 0, 1.0 / (large * count), 1.0 / (small * count)).astype(
            jnp.float32
        )

    def fold(self, seg, sums):
        first = seg.tile
        found = []
        for value in sums:
            tiles = [
                value[:, (first + t) * LANES : (first + t + 1) * LANES] for t in range(seg.tiles)
            ]
            if seg.cout <= LANES:
                total = tiles[0]
                for tile in tiles[1:]:
                    total = total + tile
                total = jnp.sum(self.spread(total, seg.cout), axis=0, keepdims=True)
                found.append([total] * seg.tiles)
            else:
                found.append([jnp.sum(tile, axis=0, keepdims=True) for tile in tiles])
        return found

    def table_row(self, ref, m, seg, tile):
        slot = seg.slot
        if seg.cout > LANES:
            return ref[m, slot : slot + 1, tile * LANES : (tile + 1) * LANES]
        row = jnp.broadcast_to(ref[m, slot : slot + 1, 0:LANES], (8, LANES))
        if seg.cout < LANES:
            row = self.spread(self.keep(row, seg.cout, [0]), seg.cout)
        return row[0:1]

    def norm_rows(self, m, unit, seg, totals, scale):
        st = self.refs.st
        for tile in range(seg.tiles):
            average = totals[0][tile] * scale
            variance = totals[1][tile] * scale - average * average
            inverse = lax.rsqrt(variance + EPS)
            where = m * STATS + unit.stat + seg.tile + tile
            factor = st[where, 4:5] * inverse
            st[where, 0:1] = average
            st[where, 1:2] = inverse
            st[where, 2:3] = factor
            st[where, 3:4] = st[where, 5:6] - average * factor

    def spread_tables(self, m, unit, seg):
        st = self.refs.st
        for tile in range(seg.tiles):
            where = m * STATS + unit.stat + seg.tile + tile
            st[where, 4:5] = self.table_row(self.refs.gains, m, seg, tile)
            st[where, 5:6] = self.table_row(self.refs.shifts, m, seg, tile)

    def normed(self, m, unit, tile, plane):
        st = self.refs.st
        z = getattr(self.refs, "z" + unit.name)
        where = m * STATS + unit.stat + tile
        value = z[m * unit.tiles * unit.planes + tile * unit.planes + plane]
        return value * st[where, 2:3] + st[where, 3:4]

    def apply_a(self, m):
        unit, u = self.units["a"], self.maps["u"]

        def body(plane):
            for tile in range(2):
                value = silu_of(self.normed(m, unit, tile, plane)) * self.masks[0]
                u.store(m, tile, plane, value)

        planes_loop(self.planes, body, TURNS)
        u.close(m)

    def apply_b(self, m):
        unit, top = self.units["b"], self.maps["t"]
        hf, s = self.refs.hf, self.refs.s

        def body(plane):
            for tile in range(2):
                where = m * 2 * self.planes + tile * self.planes + plane
                value = silu_of(self.normed(m, unit, tile, plane) + hf[where]) * self.masks[0]
                s[where] = value
                top.store(m, tile, plane, value)

        planes_loop(self.planes, body, TURNS)
        top.close(m)

    def apply_rest(self, m, unit):
        sb = self.refs.sb
        for seg in unit.segs:
            chain = self.maps[seg.chain] if seg.chain else None

            def body(plane):
                for tile in range(seg.tiles):
                    value = self.normed(m, unit, seg.tile + tile, plane)
                    if chain is not None:
                        chain.store(m, tile, plane, silu_of(value) * self.masks[0])
                    else:
                        at = message_slot(self.k, seg.dest) + tile * unit.planes + plane
                        sb[at] = value.astype(jnp.bfloat16)

            planes_loop(unit.planes, body, TURNS)
            if chain is not None:
                chain.close(m)
            else:
                self.message(m, seg.dest).start()

    def message(self, e, other):
        count = 2 * (8 >> max(self.k, other))
        r = self.refs
        return pltpu.make_async_remote_copy(
            src_ref=r.sb.at[pl.ds(message_slot(self.k, other), count)],
            dst_ref=r.rb.at[pl.ds(e * 16 + message_slot(other, self.k), count)],
            send_sem=r.ssem.at[e * 4 + other],
            recv_sem=r.rsem.at[e * 4 + self.k],
            device_id=dict(branch=other),
            device_id_type=pl.DeviceIdType.MESH,
        )

    def arrived(self, e, other):
        count = 2 * (8 >> max(self.k, other))
        r = self.refs
        at = message_slot(self.k, other)
        return pltpu.make_async_remote_copy(
            src_ref=r.sb.at[pl.ds(at, count)],
            dst_ref=r.rb.at[pl.ds(e * 16 + at, count)],
            send_sem=r.ssem.at[e * 4 + other],
            recv_sem=r.rsem.at[e * 4 + other],
            device_id=dict(branch=other),
            device_id_type=pl.DeviceIdType.MESH,
        )

    def others(self):
        return [other for other in range(4) if other != self.k]

    def settle(self, e):
        for other in self.others():
            self.message(e, other).wait_send()
        for other in self.others():
            self.arrived(e, other).wait_recv()

    def receive(self, m):
        r = self.refs
        s, rb, hf, out = r.s, r.rb, r.hf, r.outs
        h = self.maps["h"]

        def total_at(tile, plane):
            where = m * 2 * self.planes + tile * self.planes + plane
            total = s[where]
            for other in self.others():
                count = 8 >> max(self.k, other)
                at = plane >> max(0, other - self.k)
                slot = m * 16 + message_slot(self.k, other) + tile * count + at
                total = total + rb[slot].astype(jnp.float32)
            s[where] = total
            return silu_of(total) * self.masks[0]

        def onward(plane):
            for tile in range(2):
                value = total_at(tile, plane)
                hf[(2 + tile) * self.planes + plane] = value
                h.store(1, tile, plane, value)

        def finish(plane):
            for tile in range(2):
                out[tile * self.planes + plane] = total_at(tile, plane).astype(jnp.bfloat16)

        @pl.when(m + 1 < MODULES)
        def _():
            planes_loop(self.planes, onward)
            h.close(1)

        @pl.when(m + 1 == MODULES)
        def _():
            planes_loop(self.planes, finish)

    def take_feature(self, tile, plane, value):
        self.refs.hf[tile * self.planes + plane] = value
        self.maps["h"].store(0, tile, plane, value)

    def take_cotangent(self, tile, plane, value):
        self.refs.gin[tile * self.planes + plane] = value

    def member(self, kind, order):
        kinds = self.refs.kinds
        found, before = jnp.int32(0), jnp.int32(0)
        for at in range(self.count):
            same = kinds[at] == kind
            found = jnp.where(same & (before == order), at, found)
            before = before + same.astype(jnp.int32)
        return found

    def order(self, device):
        kinds = self.refs.kinds
        kind = kinds[device]
        before = jnp.int32(0)
        for at in range(self.count):
            before = before + ((kinds[at] == kind) & (at < device)).astype(jnp.int32)
        return before

    def unpack(self, t, consume):
        r = self.refs
        work, rows, planes = r.work, self.rows, self.planes
        full = SH * SW * C0 // LANES
        gath = r.gathc if t else r.gathx

        @pl.when(self.core == 0)
        def _():
            for at in range(self.large):
                block = gath[self.member(1, at)]
                work[at * ROWS : (at + 1) * ROWS] = block.astype(jnp.float32)

        @pl.when(self.core == 1)
        def _():
            for at in range(self.small):
                block = gath[self.member(0, at), 0:full]
                work[at * full : (at + 1) * full] = block.astype(jnp.float32)
            work[self.small * full : self.large * ROWS] = jnp.zeros(
                (self.large * ROWS - self.small * full, LANES), jnp.float32
            )

        deep = self.large * ROWS // 2
        right = jnp.concatenate([work[pl.ds(j, deep, stride=2)] for j in range(2)], axis=1)
        right = right.astype(jnp.bfloat16)
        cells = Cells(self.core, (rows, LANES), self.small, self.large)
        base = cells.crop * cells.pick(ROWS // 2, full // 2)
        base = base + cells.along * (planes * cells.wide) + cells.across
        base = jnp.where(cells.valid, base, -(1 << 20))
        lane = lax.broadcasted_iota(jnp.int32, (rows, LANES), 1)
        chunk = 1

        def body(step):
            pieces = []
            for q in range(chunk):
                goal = base + (step * chunk + q) * cells.wide
                pieces.append(one_hot(goal, lane, deep))
            left = pieces[0] if chunk == 1 else jnp.concatenate(pieces, axis=0)
            result = lax.dot_general(left, right, DOWN, preferred_element_type=jnp.float32)
            for q in range(chunk):
                for tile in range(2):
                    value = result[q * rows : (q + 1) * rows, tile * LANES : (tile + 1) * LANES]
                    consume(tile, step * chunk + q, value)

        planes_loop(planes // chunk, body)

    def pack_size(self):
        return 48 * self.planes, -(-self.planes * self.rows // LANES) * LANES

    def plan_pack(self):
        r = self.refs
        high, deep = self.pack_size()
        planes = self.planes
        q = lax.broadcasted_iota(jnp.int32, (high, LANES), 0)
        lane = lax.broadcasted_iota(jnp.int32, (high, LANES), 1)
        wide, tall = jnp.where(self.core == 0, 6, 3), jnp.where(self.core == 0, 8, 4)
        cell = jnp.where(self.core == 0, (q * 43691) >> 18, (q * 43691) >> 17)
        across = q - cell * wide
        plane = cell & (planes - 1)
        along = cell >> log2(planes)
        base = plane * self.rows + along * wide + across
        base = jnp.where(along < tall, base, -(1 << 20))
        shard = lax.axis_index("crops")
        for at, device in enumerate((shard, shard + 1 - 2 * self.core)):
            goal = base + self.order(device) * (wide * tall)
            r.hot[at, 0:high, 0:deep] = one_hot(goal, lane, deep)

    def pack(self, units, put):
        high, deep = self.pack_size()
        right = jnp.concatenate([units(tile) for tile in range(2)], axis=1)
        short = deep - right.shape[0]
        parts = [right.astype(jnp.bfloat16)]
        if right.dtype == jnp.float32:
            parts.append((right - parts[0].astype(jnp.float32)).astype(jnp.bfloat16))
        if short:
            empty = jnp.zeros((short, 2 * LANES), jnp.bfloat16)
            parts = [jnp.concatenate([part, empty], axis=0) for part in parts]
        for at in range(2):
            total = None
            for part in parts:
                piece = lax.dot_general(
                    self.refs.hot[at, 0:high, 0:deep],
                    part,
                    DOWN,
                    preferred_element_type=jnp.float32,
                )
                total = piece if total is None else total + piece
            for tile in range(2):
                put(at, pl.ds(tile, high, stride=2), total[:, tile * LANES : (tile + 1) * LANES])

    def pack_outputs(self):
        r = self.refs
        high = 2 * self.pack_size()[0]

        def put(at, where, value):
            r.work[pl.ds(at * ROWS + where.start, where.size, stride=2)] = value

        def units(tile):
            block = r.outs[tile * self.planes : (tile + 1) * self.planes]
            return block.reshape(self.planes * self.rows, LANES)

        self.pack(units, put)
        for at in range(2):
            r.blocks[at, 0:high] = r.work[at * ROWS : at * ROWS + high].astype(jnp.bfloat16)
            if high < ROWS:
                r.blocks[at, high:ROWS] = jnp.zeros((ROWS - high, LANES), jnp.bfloat16)

    def pack_gradient(self):
        r = self.refs
        high = 2 * self.pack_size()[0]

        def put(at, where, value):
            r.slopes[at, where] = value

        def units(tile):
            block = r.gin[tile * self.planes : (tile + 1) * self.planes]
            return block.reshape(self.planes * self.rows, LANES)

        self.pack(units, put)
        if high < ROWS:
            for at in range(2):
                r.slopes[at, high:ROWS] = jnp.zeros((ROWS - high, LANES), jnp.float32)

    def forward(self, m, gather):
        steps = iter(range(1, 4))

        def also():
            step = next(steps, None)
            if step is not None:

                @pl.when(m == 0)
                def _():
                    gather.step(1, step)

        self.conv(m, self.units["a"])
        self.apply_a(m)
        also()
        self.conv(m, self.units["b"])
        self.apply_b(m)
        also()
        for name in ("d", "u", "e", "f", "g"):
            if name in self.units:
                self.conv(m, self.units[name])
                self.apply_rest(m, self.units[name])
                also()
        for _ in range(3):
            also()

        @pl.when(m == MODULES - 1)
        def _():
            gather.collect(1)
            self.unpack(1, self.take_cotangent)
            self.plan_pack()

        self.settle(m)
        self.receive(m)


    def send_back(self, m):
        r = self.refs
        s, gin, gt, sb = r.s, r.gin, r.gt, r.sb
        e = MODULES + m

        def body(plane):
            for tile in range(2):
                at = tile * self.planes + plane
                value = gin[at] * slope_of(s[m * 2 * self.planes + at])
                gt[at] = value
                for other in range(self.k):
                    sb[message_slot(self.k, other) + at] = value.astype(jnp.bfloat16)

        planes_loop(self.planes, body, TURNS)
        for other in reversed(self.others()):
            if other > self.k:
                count = 8 >> other
                wide = 1 << (other - self.k)

                def pool(plane):
                    for tile in range(2):
                        total = gt[tile * self.planes + plane * wide]
                        for step in range(1, wide):
                            total = total + gt[tile * self.planes + plane * wide + step]
                        slot = message_slot(self.k, other) + tile * count + plane
                        sb[slot] = total.astype(jnp.bfloat16)

                planes_loop(count, pool, TURNS)
            self.message(e, other).start()

    def back_unit(self, m, unit):
        r = self.refs
        st, dyb, z = r.st, r.dyb, getattr(r, "z" + unit.name)
        name, planes, tiles = unit.name, unit.planes, unit.tiles
        e = MODULES + m
        sums = {}

        def upstream(seg, tile, plane, normed):
            at = tile * planes + plane
            if name == "b":
                hf = r.hf[m * 2 * planes + at]
                value = r.gt[at] * slope_of(normed + hf)
                r.gin[at] = value
                return value
            if name == "a":
                return r.gu[at] * slope_of(normed)
            if seg.chain:
                return self.grads[seg.chain][at] * slope_of(normed)
            return r.rb[e * 16 + message_slot(self.k, seg.dest) + at].astype(jnp.float32)

        for seg in unit.segs:

            def body(plane, carry):
                result = []
                for tile in range(seg.tiles):
                    at = (seg.tile + tile) * planes + plane
                    where = m * STATS + unit.stat + seg.tile + tile
                    value = z[m * tiles * planes + at]
                    normed = value * st[where, 2:3] + st[where, 3:4]
                    dy = upstream(seg, tile, plane, normed)
                    dyb[at] = dy
                    zhat = (value - st[where, 0:1]) * st[where, 1:2]
                    result.append(carry[2 * tile] + partial_sum(dy))
                    result.append(carry[2 * tile + 1] + partial_sum(dy * zhat))
                return tuple(result)

            zero = jnp.zeros((8, LANES), jnp.float32)
            found = planes_sum(planes, body, (zero,) * (2 * seg.tiles), TURNS)
            pair = [
                jnp.concatenate([found[2 * tile + which] for tile in range(seg.tiles)], axis=1)
                for which in range(2)
            ]
            plain = SimpleNamespace(**vars(seg))
            plain.tile = 0
            totals = self.fold(plain, pair)
            self.table_grads(m, seg, totals)
            sums[seg.slot] = totals
        dz = self.dz_planes(unit)
        for seg in unit.segs:
            scale = self.per_cell(unit, seg)
            totals = sums[seg.slot]

            def apply(plane):
                for tile in range(seg.tiles):
                    at = (seg.tile + tile) * planes + plane
                    where = m * STATS + unit.stat + seg.tile + tile
                    zhat = (z[m * tiles * planes + at] - st[where, 0:1]) * st[where, 1:2]
                    inner = dyb[at] - totals[0][tile] * scale - zhat * (totals[1][tile] * scale)
                    dz.store(0, seg.tile + tile, plane, inner * st[where, 2:3] * self.masks[0])

            planes_loop(planes, apply, TURNS)
        dz.close(0)
        self.back_data(m, unit, dz)
        first = min(seg.off for seg in unit.segs)
        last = max(seg.off + seg.taps**2 * seg.cin * seg.cout // LANES for seg in unit.segs)
        wanted = (self.quarter * self.share < last) & ((self.quarter + 1) * self.share > first)

        @pl.when(wanted)
        def _():
            self.back_kernel(m, unit, dz)

    def dz_planes(self, unit):
        r = self.refs
        mode = {"p1": "p", "s2": "dz2", "s1": "wide" if self.k == 3 else "s1"}[unit.kind]
        return Planes(
            mode,
            unit.tiles,
            unit.planes,
            self.masks,
            self.rows,
            r.dC,
            r.dE,
            r.dR,
        )

    def table_grads(self, m, seg, totals):
        gg = self.refs.gg
        slot = seg.slot
        for which, found in ((0, totals[1]), (1, totals[0])):
            if seg.cout > LANES:
                for tile in range(2):
                    gg[m, which, slot : slot + 1, tile * LANES : (tile + 1) * LANES] = found[tile]
            else:
                row = jnp.broadcast_to(found[0], (8, LANES))
                if seg.cout < LANES:
                    row = self.keep(row, seg.cout, [0])
                gg[m, which, slot : slot + 1, 0:LANES] = row[0:1]

    def wide_rows(self, ref, at, tiles, plane, count):
        pieces = [
            ref[pl.ds(at(0, tile, plane), count)].reshape(count * self.rows, LANES)
            for tile in range(tiles)
        ]
        return pieces[0] if tiles == 1 else jnp.concatenate(pieces, axis=1)

    def back_data(self, m, unit, dz):
        r = self.refs
        kind, tiles = unit.kind, unit.tiles
        target = getattr(r, "T" + unit.name)
        lanes = tiles * LANES
        rows = self.rows

        def kernel_rows(d, first, count):
            return target[m * unit.depth + d, first : first + count, 0:lanes]

        def product(left, right):
            return lax.dot_general(left, right, ACROSS, preferred_element_type=jnp.float32)

        def put(ref, tile, planes, first, count, value, step=1, add=False):
            block = value.reshape(count, rows, LANES)
            for q in range(count):
                at = tile * planes + first + q * step
                ref[at] = ref[at] + block[q] if add else block[q]

        planes = unit.planes
        if kind == "s1":
            goal = r.gu if unit.name == "b" else r.gin
            add = unit.name == "a"
            chunk = 1
            across = getattr(r, "T" + unit.name + unit.name)

            def body(step):
                first = step * chunk
                if self.k == 3:
                    total = None
                    for d in range(3):
                        for ref, at in ((dz.right, 0), (dz.main, 256), (dz.edge, 512)):
                            left = self.wide_rows(ref, dz.at, 2, first + 1 - d, chunk)
                            piece = product(left, kernel_rows(d, at, 256))
                            total = piece if total is None else total + piece
                else:
                    left = [
                        self.wide_rows(ref, dz.at, 2, first + 1 - d, chunk)
                        for d in range(3)
                        for ref in (dz.main, dz.edge)
                    ]
                    right = [across[m * 3 + d] for d in range(3)]
                    total = product(
                        jnp.concatenate(left, axis=1), jnp.concatenate(right, axis=1)
                    )
                for tile in range(2):
                    put(
                        goal,
                        tile,
                        planes,
                        first,
                        chunk,
                        total[:, tile * LANES : (tile + 1) * LANES],
                        add=add,
                    )

            planes_loop(planes // chunk, body)
            return
        if kind == "p1":

            def whole_plane(plane):
                left = self.wide_rows(dz.main, dz.at, tiles, plane, 1)
                total = product(left, kernel_rows(0, 0, 256))
                for tile in range(2):
                    value = total[:, tile * LANES : (tile + 1) * LANES]
                    put(r.gt, tile, planes, plane, 1, value, add=True)

            planes_loop(planes, whole_plane)
            return
        goal = self.grads[unit.source]
        add = unit.source == "t"
        lanes_in = unit.lanes_in
        count_in = unit.planes_in

        def spread_plane(plane):
            for parity, terms in ((0, [(1, 0)]), (1, [(2, 0), (0, 1)])):
                total, side = None, None
                for d, offset in terms:
                    left = self.wide_rows(dz.main, dz.at, tiles, plane + offset, 1)
                    piece = product(left, kernel_rows(d, 0, lanes_in))
                    total = piece if total is None else total + piece
                    left = self.wide_rows(dz.edge, dz.at, tiles, plane + offset, 1)
                    piece = product(left, kernel_rows(d, lanes_in, LANES))
                    side = piece if side is None else side + piece
                for tile in range(lanes_in // LANES):
                    value = total[:, tile * LANES : (tile + 1) * LANES]
                    if tile == lanes_in // LANES - 1:
                        value = value + side
                    put(goal, tile, count_in, 2 * plane + parity, 1, value, add=add)

        planes_loop(planes, spread_plane)

    def back_kernel(self, m, unit, dz):
        r = self.refs
        G, rep, wgv = r.work, r.rep, r.wgv
        tiles, planes = unit.tiles, unit.planes
        source = self.maps[unit.source]
        right = self.wide_rows(dz.main, dz.at, tiles, 0, planes)

        def gather(d):
            at = 0
            for part in self.parts(unit, source):
                pieces = self.rows_of(unit, part, m, d, 0, planes)
                left = pieces[0] if len(pieces) == 1 else jnp.concatenate(pieces, axis=1)
                count = left.shape[1]
                result = lax.dot_general(left, right, ALONG, preferred_element_type=jnp.float32)
                for tile in range(tiles):
                    row = pl.multiple_of((d * tiles + tile) * unit.rows + at, 8)
                    G[pl.ds(row, count)] = result[:, tile * LANES : (tile + 1) * LANES]
                at += count

        planes_loop(unit.depth, gather)
        for seg in unit.segs:
            self.fold_kernel(m, unit, seg)

    def fold_kernel(self, m, unit, seg):
        r = self.refs
        G, rep, wgv = r.work, r.rep, r.wgv
        cin, cout, tiles = seg.cin, seg.cout, unit.tiles
        width = 3 if seg.taps == 3 else 1
        found = links(self.k, unit, seg)
        off = seg.off

        def fold(d):
            for column in range(width):
                tap = d * width + column
                totals = []
                for tile in range(seg.tiles):
                    total = None
                    for row, which, wanted in found:
                        if which != column:
                            continue
                        at = pl.multiple_of((d * tiles + seg.tile + tile) * unit.rows + row, 8)
                        piece = G[pl.ds(at, cin)]
                        if cout <= LANES:
                            local = self.local_blocks(seg, tile, wanted)
                            if not local:
                                continue
                            piece = self.keep(piece, cout, local)
                        total = piece if total is None else total + piece
                    totals.append(total)
                if cout > LANES:
                    for tile in range(2):
                        wgv[pl.ds(off + tap * (2 * cin) + tile, cin, stride=2)] = totals[tile]
                    continue
                total = None
                for piece in totals:
                    if piece is not None:
                        total = piece if total is None else total + piece
                if cout == LANES:
                    wgv[pl.ds(pl.multiple_of(off + tap * cin, 8), cin)] = total
                else:
                    rep[pl.ds(pl.multiple_of(tap * cin, cin), cin)] = self.spread(total, cout)

        planes_loop(unit.depth, fold)
        if cout < LANES:
            ratio = LANES // cout
            count = width * width * cin // ratio
            total = None
            for part in range(ratio):
                piece = self.keep(rep[pl.ds(part, count, stride=ratio)], cout, [part])
                total = piece if total is None else total + piece
            wgv[off : off + count] = total

    def backward(self, m):
        e = MODULES + m
        self.send_back(m)
        for name in ("g", "f", "e", "d", "u"):
            if name in self.units:
                for seg in self.units[name].segs:
                    if seg.dest >= 0:
                        self.arrived(e, seg.dest).wait_recv()
                self.back_unit(m, self.units[name])
        for other in self.others():
            self.message(e, other).wait_send()
        self.back_unit(m, self.units["b"])
        self.back_unit(m, self.units["a"])


STATS = 20
TURNS = 1
NAMES = list(
    dict(x=0, cot=0, w=0, gains=0, shifts=0, kinds=0, out=0, grad=0, wg=0, gain=0, shift=0)
)


def one_hot(goal, lane, deep):
    pieces = [
        jnp.where(goal == lane + first, 1.0, 0.0).astype(jnp.bfloat16)
        for first in range(0, deep, LANES)
    ]
    return jnp.concatenate(pieces, axis=1)


class Cells:
    def __init__(self, core, shape, small, large):
        self.core = core
        row = lax.broadcasted_iota(jnp.int32, shape, 0)
        self.wide = self.pick(LW // 8, SW // 8)
        tall = self.pick(LH // 8, SH // 8)
        self.crop = self.pick((row * 43691) >> 21, (row * 43691) >> 19)
        inner = row - self.crop * (self.wide * tall)
        self.along = self.pick((inner * 43691) >> 18, (inner * 43691) >> 17)
        self.across = inner - self.along * self.wide
        self.valid = self.crop < self.pick(large, small)
        self.last = tall - 1

    def pick(self, large, small):
        return jnp.where(self.core == 0, large, small)


def fill_masks(refs, rows, core, small, large):
    cells = Cells(core, (rows, LANES), small, large)
    valid = cells.valid
    six = cells.wide == 6
    up, down = valid & (cells.along > 0), valid & (cells.along < cells.last)
    tables = (
        valid,
        valid & (cells.across > 0),
        valid & (cells.across < cells.wide - 1),
        up & six,
        up & jnp.logical_not(six),
        down & six,
        down & jnp.logical_not(six),
    )
    for at, table in enumerate(tables):
        refs.masks[at] = jnp.where(table, 1.0, 0.0)


class Gather:
    def __init__(self, refs, core, count):
        self.refs, self.core, self.count = refs, core, count
        self.z = lax.axis_index("crops") // 2
        self.last = count // 2 - 1

    def hop(self, t, source, right):
        r = self.refs
        at = source * 2 + self.core
        gath = r.gathc if t else r.gathx
        to = self.z + 1 if right else self.z - 1
        return pltpu.make_async_remote_copy(
            src_ref=gath.at[at],
            dst_ref=gath.at[at],
            send_sem=r.hsem.at[(t * (self.last + 1) + source) * 3 + (0 if right else 1)],
            recv_sem=r.gsem.at[t * self.count + at],
            device_id=dict(crops=to * 2 + self.core),
            device_id_type=pl.DeviceIdType.MESH,
        )

    def across(self, t, source, core, rows):
        r = self.refs
        at = source * 2 + core
        gath = r.gathc if t else r.gathx
        return pltpu.make_async_remote_copy(
            src_ref=gath.at[at, pl.ds(0, rows)],
            dst_ref=gath.at[at, pl.ds(0, rows)],
            send_sem=r.hsem.at[(t * (self.last + 1) + source) * 3 + 2],
            recv_sem=r.gsem.at[t * self.count + at],
            device_id=dict(crops=self.z * 2 + 1 - self.core),
            device_id_type=pl.DeviceIdType.MESH,
        )

    def each_core(self, action):
        for core, rows in ((0, SH * SW * C0 // LANES), (1, ROWS)):

            @pl.when(self.core == core)
            def _():
                action(core, rows)

    def send(self, t, source, rightward, leftward):
        if rightward:

            @pl.when(self.z < self.last)
            def _():
                self.hop(t, source, True).start()

        if leftward:

            @pl.when(self.z > 0)
            def _():
                self.hop(t, source, False).start()

        self.each_core(lambda core, rows: self.across(t, source, core, rows).start())

    def step(self, t, s):
        r = self.refs
        if s == 0:
            at = self.z * 2 + self.core
            if t:
                r.gathc[at] = r.cot[...]
            else:
                r.gathx[at] = r.x[...]
            self.send(t, self.z, True, True)
            return

        @pl.when(self.z >= s)
        def _():
            self.hop(t, self.z - s, True).wait_recv()
            self.send(t, self.z - s, True, False)

        @pl.when(self.z + s <= self.last)
        def _():
            self.hop(t, self.z + s, True).wait_recv()
            self.send(t, self.z + s, False, True)

    def collect(self, t):
        for source in range(self.last + 1):
            for core, rows in ((0, ROWS), (1, SH * SW * C0 // LANES)):

                @pl.when(self.core == core)
                def _():
                    self.across(t, source, 1 - core, rows).wait_recv()

    def finish(self, t):
        def sent(source, rightward, leftward):
            if rightward:

                @pl.when(self.z < self.last)
                def _():
                    self.hop(t, source, True).wait_send()

            if leftward:

                @pl.when(self.z > 0)
                def _():
                    self.hop(t, source, False).wait_send()

            self.each_core(lambda core, rows: self.across(t, source, core, rows).wait_send())

        sent(self.z, True, True)
        for s in range(1, self.last + 1):

            @pl.when(self.z >= s)
            def _():
                sent(self.z - s, True, False)

            @pl.when(self.z + s <= self.last)
            def _():
                sent(self.z + s, False, True)


def scratch_table(rows, weight_rows, count):
    def half(many):
        return pltpu.VMEM((many, rows, LANES), jnp.bfloat16)

    def full(many):
        return pltpu.VMEM((many, rows, LANES), jnp.float32)

    def expanded(depth, deep, wide):
        return pltpu.VMEM((MODULES * depth, deep, wide), jnp.bfloat16)

    _, span, _ = pair_rows(weight_rows, count)
    return dict(
        masks=full(MASKS),
        hC=half(2 * 20),
        hE=half(2 * 20),
        hR=half(2 * 6),
        uC=half(2 * 20),
        uE=half(2 * 20),
        uR=half(2 * 6),
        tC=half(2 * 18),
        tE=half(2 * 9),
        c1C=half(2 * 5),
        c1E=half(2 * 5),
        c2C=half(2 * 5),
        c2E=half(2 * 5),
        c3C=half(2 * 3),
        c3E=half(2 * 3),
        dC=half(20),
        dE=half(20),
        dR=half(6),
        outs=half(16),
        hf=full(2 * 16),
        s=full(2 * 16),
        za=full(2 * 16),
        zb=full(2 * 16),
        zd=full(2 * 16),
        zu=full(2 * 8),
        ze=full(2 * 4),
        zf=full(2 * 2),
        zg=full(2 * 2),
        gt=full(16),
        gu=full(16),
        gin=full(16),
        gc1=full(4),
        gc2=full(4),
        gc3=full(2),
        dyb=full(16),
        sb=half(16),
        rb=half(4 * 16),
        st=pltpu.VMEM((MODULES * STATS, 8, LANES), jnp.float32),
        Ta=expanded(3, 768, 256),
        Tb=expanded(3, 768, 256),
        Taa=expanded(3, 256, 512),
        Tbb=expanded(3, 256, 512),
        Td=expanded(3, 384, 512),
        Tu=expanded(1, 256, 768),
        Te=expanded(3, 256, 256),
        Tf=expanded(3, 256, 128),
        Tg=expanded(3, 256, 256),
        raw=pltpu.VMEM((9408, LANES), jnp.bfloat16),
        work=pltpu.VMEM((4608, LANES), jnp.float32),
        rep=pltpu.VMEM((640, LANES), jnp.float32),
        wgv=pltpu.VMEM((weight_rows, LANES), jnp.float32),
        wq=pltpu.VMEM((MODULES, 2 * weight_rows // count, LANES), jnp.float32),
        wr=pltpu.VMEM((MODULES, span, LANES), jnp.float32),
        gathx=pltpu.VMEM((count, ROWS, LANES), jnp.bfloat16),
        gathc=pltpu.VMEM((count, ROWS, LANES), jnp.bfloat16),
        hot=pltpu.VMEM((2, 384, 768), jnp.bfloat16),
        blocks=pltpu.VMEM((2, ROWS, LANES), jnp.bfloat16),
        slopes=pltpu.VMEM((2, ROWS, LANES), jnp.float32),
        blockr=pltpu.VMEM((ROWS, LANES), jnp.bfloat16),
        sloper=pltpu.VMEM((ROWS, LANES), jnp.float32),
        gg=pltpu.VMEM((MODULES, 2, SLOTS, 256), jnp.float32),
        ggr=pltpu.VMEM((MODULES, 2, SLOTS, 256), jnp.float32),
        wsem=pltpu.SemaphoreType.DMA((8,)),
        ssem=pltpu.SemaphoreType.DMA((16,)),
        rsem=pltpu.SemaphoreType.DMA((16,)),
        hsem=pltpu.SemaphoreType.DMA((3 * count,)),
        gsem=pltpu.SemaphoreType.DMA((2 * count,)),
        psem=pltpu.SemaphoreType.DMA((5,)),
        qsem=pltpu.SemaphoreType.DMA((5,)),
        osem=pltpu.SemaphoreType.DMA((1,)),
    )


def pair_rows(weight_rows, count):
    share = weight_rows // count
    low = share // 8 * 8
    return share, 2 * share - low, low


def greet(core, count):
    barrier = pltpu.get_barrier_semaphore()
    me, shard = lax.axis_index("branch"), lax.axis_index("crops")
    z = shard // 2

    def signal(**where):
        pl.semaphore_signal(barrier, inc=1, device_id=where, device_id_type=pl.DeviceIdType.MESH)

    for step in range(1, 4):
        signal(branch=lax.rem(me + step, 4))
    signal(crops=shard + 1 - 2 * core)

    @pl.when(z > 0)
    def _():
        signal(crops=shard - 2)

    @pl.when(z < count // 2 - 1)
    def _():
        signal(crops=shard + 2)

    ends = (z == 0).astype(jnp.int32) + (z == count // 2 - 1).astype(jnp.int32)
    pl.semaphore_wait(barrier, 6 - ends)


def whole_kernel(names, rows, large, small, *args):
    refs = SimpleNamespace(**dict(zip(names, args)))
    count = large + small
    me, shard = lax.axis_index("branch"), lax.axis_index("crops")
    core = shard % 2
    weight_rows = refs.wgv.shape[0]
    share, span, low = pair_rows(weight_rows, count)
    quarter = pl.multiple_of(shard // 2 * (2 * share), 8)

    class Lazy:
        def __getitem__(self, index):
            return refs.masks[index]

    def across(source, goal, index):
        return pltpu.make_async_remote_copy(
            src_ref=source,
            dst_ref=goal,
            send_sem=refs.psem.at[index],
            recv_sem=refs.qsem.at[index],
            device_id=dict(crops=shard + 1 - 2 * core),
            device_id_type=pl.DeviceIdType.MESH,
        )

    def kernel_pair(m):
        at = pl.multiple_of(low * (1 - core), 8)
        return across(refs.wq.at[m, pl.ds(at, span)], refs.wr.at[m], m)

    outputs_pair = across(refs.blocks.at[1], refs.blockr, 2)
    gradient_pair = across(refs.slopes.at[1], refs.sloper, 3)
    table_pair = across(refs.gg, refs.ggr, 4)
    gather = Gather(refs, core, count)

    def every(action):
        for k in range(4):

            @pl.when(me == k)
            def _():
                action(Branch(k, rows, large, small, 2 * share, refs, Lazy(), core))

    def begin(branch):
        branch.fetch_first()

    def prepare(branch):
        found = branch.segments()
        stops = {0: 1, min(2, len(found) - 2): 2, len(found) - 1: 3}
        for index, (unit, seg) in enumerate(found):
            branch.expand(index)
            if index in stops:
                gather.step(0, stops[index])

    def main(branch):
        branch.unpack(0, branch.take_feature)
        branch.maps["h"].close(0)
        gather.step(1, 0)

        def ahead(m, carry):
            branch.forward(m, gather)
            return carry

        def back(step, carry):
            m = MODULES - 1 - step
            branch.backward(m)
            refs.wq[m] = refs.wgv[pl.ds(quarter, 2 * share)]
            kernel_pair(m).start()
            return carry

        lax.fori_loop(0, MODULES, ahead, 0)
        branch.pack_outputs()
        outputs_pair.start()
        lax.fori_loop(0, MODULES, back, 0)
        branch.pack_gradient()
        gradient_pair.start()
        table_pair.start()

    every(begin)
    greet(core, count)
    gather.step(0, 0)
    fill_masks(refs, rows, core, small, large)
    refs.wgv[pl.ds(quarter, 2 * share)] = jnp.zeros((2 * share, LANES), jnp.float32)
    refs.gg[...] = jnp.zeros(refs.gg.shape, jnp.float32)
    every(prepare)
    gather.collect(0)
    every(main)

    for step in range(MODULES):
        m = MODULES - 1 - step
        kernel_pair(m).wait()
        mine = refs.wq[m, pl.ds(pl.multiple_of(low * core, 8), span)]
        refs.work[pl.ds(m, span, stride=MODULES)] = mine + refs.wr[m]
    skip = pl.multiple_of(core * (MODULES * (share - low)), 8)
    leave = pltpu.make_async_copy(
        refs.work.at[pl.ds(skip, MODULES * share)], refs.wg, refs.osem.at[0]
    )
    leave.start()
    outputs_pair.wait()
    gradient_pair.wait()
    table_pair.wait()
    own = refs.kinds[shard] != core
    refs.out[...] = jnp.where(own, refs.blocks[0].astype(jnp.float32), refs.blockr[...].astype(jnp.float32)).astype(jnp.bfloat16)
    refs.grad[...] = jnp.where(own, refs.slopes[0], refs.sloper[...])
    width = 256 // count
    for which, goal in ((0, refs.gain), (1, refs.shift)):
        for m in range(MODULES):
            total = refs.gg[m, which] + refs.ggr[m, which]
            found = None
            for at in range(count):
                piece = jnp.where(shard == at, total[:, at * width : (at + 1) * width], 0.0)
                found = piece if found is None else found + piece
            goal[m] = found
    gather.finish(0)
    gather.finish(1)
    leave.wait()


def whole_call(rows, large, small, x, cot, w, gains, shifts, kinds):
    count = large + small
    weight_rows = w.shape[0] // MODULES
    table = scratch_table(rows, weight_rows, count)
    vmem = pl.BlockSpec(memory_space=pltpu.VMEM)
    hbm = pl.BlockSpec(memory_space=pl.ANY)
    smem = pl.BlockSpec(memory_space=pltpu.SMEM)
    tables = jax.ShapeDtypeStruct((MODULES, SLOTS, 256 // count), jnp.float32)
    return pl.pallas_call(
        partial(whole_kernel, NAMES + list(table), rows, large, small),
        out_shape=(
            jax.ShapeDtypeStruct((ROWS, LANES), jnp.bfloat16),
            jax.ShapeDtypeStruct((ROWS, LANES), jnp.float32),
            jax.ShapeDtypeStruct((MODULES * weight_rows // count, LANES), jnp.float32),
            tables,
            tables,
        ),
        in_specs=[vmem, vmem, hbm, vmem, vmem, smem],
        out_specs=(vmem, vmem, hbm, vmem, vmem),
        scratch_shapes=list(table.values()),
        compiler_params=pltpu.CompilerParams(
            collective_id=0, has_side_effects=True, vmem_limit_bytes=62 * 1024 * 1024
        ),
    )(x, cot, w, gains, shifts, kinds)


def leave_kernel(*refs):
    for source, goal in zip(refs[:5], refs[5:]):
        goal[...] = source[...]


def leave_call(arrays):
    vmem = pl.BlockSpec(memory_space=pltpu.VMEM)
    return pl.pallas_call(
        leave_kernel,
        out_shape=tuple(jax.ShapeDtypeStruct(array.shape, array.dtype) for array in arrays),
        in_specs=[vmem] * 5,
        out_specs=(vmem,) * 5,
    )(*arrays)


def on_device_grouped(features, weights, gains, shifts, cotangent, size_group):
    count = lax.axis_size("crops")
    large = count // 4
    weight_rows = weights.shape[2] // LANES
    results = whole_call(
        group_rows(count),
        large,
        count - large,
        features[0],
        cotangent[0],
        weights[0]
        .reshape(MODULES, weight_rows, LANES)
        .transpose(1, 0, 2)
        .reshape(MODULES * weight_rows, LANES),
        gains[0],
        shifts[0],
        size_group,
    )
    out, grad, weight_grad, gain, shift = leave_call(results)
    share = weight_rows // count
    weight_grad = weight_grad.reshape(share, MODULES, LANES).transpose(1, 0, 2)
    weight_grad = with_layout_constraint(weight_grad, Layout((1, 0, 2)))
    return (
        out[None],
        grad[None],
        weight_grad.reshape(1, MODULES, share * LANES),
        gain[None],
        shift[None],
    )


def group_rows(count):
    large = count // 4
    rows = max(large * (LH // 8) * (LW // 8), (count - large) * (SH // 8) * (SW // 8))
    return -(-rows // 16) * 16


def fits(count):
    return count % 8 == 0 and group_rows(count) <= 96


def solution(mesh):
    placed = (
        P("branch", "crops", None),
        P("branch", None, None),
        P("branch", None, None, None),
        P("branch", None, None, None),
        P("branch", "crops", None),
        P(),
    )
    return jax.shard_map(
        on_device_grouped if fits(mesh.shape["crops"]) else on_device,
        mesh=mesh,
        in_specs=placed,
        out_specs=(
            P("branch", "crops", None),
            P("branch", "crops", None),
            P("branch", None, "crops"),
            P("branch", None, None, "crops"),
            P("branch", None, None, "crops"),
        ),
        check_vma=False,
    )
```

```python
from functools import partial
from types import SimpleNamespace
import math

import jax
import jax.numpy as jnp
import numpy as np
from jax import lax
from jax.experimental import pallas as pl
from jax.experimental.layout import Layout, with_layout_constraint
from jax.experimental.pallas import tpu as pltpu
from jax.sharding import PartitionSpec as P

C0 = 32
BLOCKS = 1
MODULES = 2
CROPS_DEV = 1
SH = 32
SW = 24
LH = 64
LW = 48
ROWS = 768
MSG_ROWS = 384


EPS = 1e-05


def as_sent(x):

    def short(part):
        return part.astype(jnp.bfloat16) if part.dtype == jnp.float32 else part

    return jax.tree.map(short, x)


def sender_plan(branch_index, top_channels, blocks):
    channels = top_channels << branch_index
    operations = []
    for block_index in range(blocks):
        operations.append(
            SimpleNamespace(
                phase=2 * block_index,
                source=("h", block_index),
                level=branch_index,
                cin=channels,
                cout=channels,
                stride=1,
                taps=3,
                act="silu",
                output=("u", block_index),
                skip=None,
                dest=-1,
            )
        )
        operations.append(
            SimpleNamespace(
                phase=2 * block_index + 1,
                source=("u", block_index),
                level=branch_index,
                cin=channels,
                cout=channels,
                stride=1,
                taps=3,
                act="res",
                output=("h", block_index + 1),
                skip=("h", block_index),
                dest=-1,
            )
        )
    top_name = ("h", blocks)
    for target in range(branch_index):
        operations.append(
            SimpleNamespace(
                phase=2 * blocks,
                source=top_name,
                level=branch_index,
                cin=channels,
                cout=top_channels << target,
                stride=1,
                taps=1,
                act="none",
                output=None,
                skip=None,
                dest=target,
            )
        )
    for target in range(branch_index + 1, 4):
        for depth_step in range(1, target - branch_index + 1):
            is_last = depth_step == target - branch_index
            operations.append(
                SimpleNamespace(
                    phase=2 * blocks + depth_step - 1,
                    source=top_name if depth_step == 1 else ("chain", target, depth_step - 1),
                    level=branch_index + depth_step,
                    cin=channels,
                    cout=top_channels << target if is_last else channels,
                    stride=2,
                    taps=3,
                    act="none" if is_last else "silu",
                    output=None if is_last else ("chain", target, depth_step),
                    skip=None,
                    dest=target if is_last else -1,
                )
            )
    for position, operation in enumerate(operations):
        operation.slot = position
        operation.size = (
            operation.taps * operation.taps * operation.cin * operation.cout
        )
        if operation.taps == 1:
            operation.kshape = (operation.cin, operation.cout)
        else:
            operation.kshape = (3, 3, operation.cin, operation.cout)
    return operations


def phase_lengths(top_channels, blocks):
    phase_count = 2 * blocks + 3
    lengths = [0] * phase_count
    for branch_index in range(4):
        per_phase = [0] * phase_count
        for operation in sender_plan(branch_index, top_channels, blocks):
            per_phase[operation.phase] += operation.size
        lengths = [max(current, candidate) for current, candidate in zip(lengths, per_phase)]
    return lengths


def weighted_plan(branch_index, top_channels, blocks):
    lengths = phase_lengths(top_channels, blocks)
    starts = [sum(lengths[:phase_index]) for phase_index in range(len(lengths))]
    running = [0] * len(lengths)
    operations = sender_plan(branch_index, top_channels, blocks)
    for operation in operations:
        phase_index = operation.phase
        operation.inner = running[phase_index]
        operation.offset = starts[phase_index] + running[phase_index]
        operation.position = sum(
            (1 for earlier in operations[: operation.slot] if earlier.phase == phase_index)
        )
        running[phase_index] += operation.size
    return operations


def phase_operations(branch_index, phase_index):
    return [
        operation
        for operation in weighted_plan(branch_index, C0, BLOCKS)
        if operation.phase == phase_index
    ]


def input_names(operations):
    source_names = []
    for operation in operations:
        if operation.source not in source_names:
            source_names.append(operation.source)
    return source_names


def silu_slope(value):
    sigmoid = jax.nn.sigmoid(value)
    return sigmoid * (1.0 + value * (1.0 - sigmoid))


def crop_cells(size_kind):
    return (LH, LW) if size_kind else (SH, SW)


def map_dims(size_kind, level, channels):
    height, breadth = crop_cells(size_kind)
    return (CROPS_DEV, height >> level, breadth >> level, channels)


def source_dims(branch_index, size_kind, map_name):
    level = branch_index + map_name[2] if map_name[0] == "chain" else branch_index
    return map_dims(size_kind, level, C0 << branch_index)


def preact_dims(size_kind, operation):
    return map_dims(size_kind, operation.level, operation.cout)


def to_canvas(arrays, value_type):
    if not arrays:
        return jnp.zeros((ROWS, 128), value_type)
    flattened = jnp.concatenate([array.reshape(-1).astype(value_type) for array in arrays])
    return jnp.pad(flattened, (0, ROWS * 128 - flattened.shape[0])).reshape(ROWS, 128)


def from_canvas(canvas, dims_list):
    flattened = canvas.reshape(-1)
    pieces = []
    offset = 0
    for dims_entry in dims_list:
        count_here = math.prod(dims_entry)
        pieces.append(flattened[offset : offset + count_here].reshape(dims_entry))
        offset += count_here
    return pieces


def to_slot(array):
    flattened = array.reshape(-1)
    return jnp.pad(flattened, (0, MSG_ROWS * 128 - flattened.shape[0])).reshape(MSG_ROWS, 128)


def from_slot(slot_rows, dims_entry):
    return slot_rows.reshape(-1)[: math.prod(dims_entry)].reshape(dims_entry)


def upsample(message, factor):
    crop_count, height, breadth, channels = message.shape
    widened = jnp.broadcast_to(
        message[:, :, None, :, None, :], (crop_count, height, factor, breadth, factor, channels)
    )
    return widened.reshape(crop_count, height * factor, breadth * factor, channels)


def block_pool(array, factor):
    crop_count, height, breadth, channels = array.shape
    return array.reshape(
        crop_count, height // factor, factor, breadth // factor, factor, channels
    ).sum(axis=(2, 4))


def kernel_piece(module_weights, operation):
    start = operation.offset
    return module_weights[start : start + operation.size].reshape(operation.kshape)


def conv_forward(operation, source, kernel):
    if operation.taps == 1:
        return jnp.einsum("nhwc,cd->nhwd", source, kernel, preferred_element_type=jnp.float32)
    stride = operation.stride
    return lax.conv_general_dilated(
        source,
        kernel,
        (stride, stride),
        ((1, 1), (1, 1)),
        dimension_numbers=("NHWC", "HWIO", "NHWC"),
        preferred_element_type=jnp.float32,
    )


def conv_backward(operation, source, kernel, upstream):
    if operation.taps == 1:
        source_grad = jnp.einsum(
            "nhwd,cd->nhwc", upstream, kernel, preferred_element_type=jnp.float32
        )
        kernel_grad = jnp.einsum(
            "nhwc,nhwd->cd", source, upstream, preferred_element_type=jnp.float32
        )
        return (source_grad, kernel_grad)
    stride = operation.stride
    flipped = jnp.transpose(kernel[::-1, ::-1], (0, 1, 3, 2))
    high_pad = 2 if stride == 2 else 1
    source_grad = lax.conv_general_dilated(
        upstream,
        flipped,
        (1, 1),
        ((1, high_pad), (1, high_pad)),
        lhs_dilation=(stride, stride),
        dimension_numbers=("NHWC", "HWIO", "NHWC"),
        preferred_element_type=jnp.float32,
    )
    kernel_grad = lax.conv_general_dilated(
        source,
        upstream,
        (1, 1),
        ((1, 2 - stride), (1, 2 - stride)),
        rhs_dilation=(stride, stride),
        dimension_numbers=("CHWN", "IHWO", "NHWC"),
        preferred_element_type=jnp.float32,
    )
    return (source_grad, jnp.transpose(kernel_grad, (1, 2, 0, 3)))


def cell_total(counts, size_kind, level):
    height, breadth = crop_cells(size_kind)
    return counts[size_kind] * float(CROPS_DEV * (height >> level) * (breadth >> level))


def norm_terms(totals, counts, size_kind, operation):
    cells_here = cell_total(counts, size_kind, operation.level)
    channels = operation.cout
    position = operation.position
    average = totals[size_kind, 0, position, :channels] / cells_here
    variance = totals[size_kind, 1, position, :channels] / cells_here - average * average
    return (average, lax.rsqrt(variance + EPS))


def forward_conv(branch_index, size_kind, phase_index, source_canvas, module_weights):
    operations = phase_operations(branch_index, phase_index)
    source_names = input_names(operations)
    pieces = from_canvas(
        source_canvas, [source_dims(branch_index, size_kind, map_name) for map_name in source_names]
    )
    sources = {
        map_name: piece.astype(jnp.bfloat16) for map_name, piece in zip(source_names, pieces)
    }
    preacts = []
    totals = jnp.zeros((2, 2, 3, 8 * C0), jnp.float32)
    for operation in operations:
        preact = conv_forward(
            operation, sources[operation.source], kernel_piece(module_weights, operation)
        )
        preacts.append(preact)
        channels = operation.cout
        position = operation.position
        totals = totals.at[size_kind, 0, position, :channels].set(jnp.sum(preact, axis=(0, 1, 2)))
        totals = totals.at[size_kind, 1, position, :channels].set(
            jnp.sum(preact * preact, axis=(0, 1, 2))
        )
    return (to_canvas(preacts, jnp.float32), totals)


def forward_norm(
    branch_index,
    size_kind,
    phase_index,
    preact_canvas,
    totals,
    counts,
    module_gains,
    module_shifts,
    skip_canvas,
    message_buffer,
):
    operations = phase_operations(branch_index, phase_index)
    preacts = from_canvas(
        preact_canvas, [preact_dims(size_kind, operation) for operation in operations]
    )
    skip_map = from_canvas(skip_canvas, [map_dims(size_kind, branch_index, C0 << branch_index)])[0]
    produced = []
    for operation, preact in zip(operations, preacts):
        average, inverse_std = norm_terms(totals, counts, size_kind, operation)
        norm_slot = operation.slot
        channels = operation.cout
        normed = (preact - average) * inverse_std * module_gains[
            norm_slot, :channels
        ] + module_shifts[norm_slot, :channels]
        if operation.act == "silu":
            produced.append(jax.nn.silu(normed))
        elif operation.act == "res":
            produced.append(jax.nn.silu(normed + skip_map))
        else:
            message_buffer = message_buffer.at[operation.dest].set(
                to_slot(normed.astype(jnp.bfloat16))
            )
    return (to_canvas(produced, jnp.float32), message_buffer)


def receive_forward(branch_index, size_kind, top_canvas, received):
    channels = C0 << branch_index
    summed = from_canvas(top_canvas, [map_dims(size_kind, branch_index, channels)])[0]
    for sender in range(4):
        if sender < branch_index:
            summed = summed + from_slot(
                received[sender], map_dims(size_kind, branch_index, channels)
            ).astype(jnp.float32)
        elif sender > branch_index:
            coarse = from_slot(received[sender], map_dims(size_kind, sender, channels))
            summed = summed + upsample(coarse, 2 ** (sender - branch_index)).astype(jnp.float32)
    return (to_canvas([jax.nn.silu(summed)], jnp.float32), to_canvas([summed], jnp.float32))


def receive_backward(branch_index, size_kind, grad_canvas, summed_canvas):
    dims_here = map_dims(size_kind, branch_index, C0 << branch_index)
    upstream = from_canvas(grad_canvas, [dims_here])[0]
    summed = from_canvas(summed_canvas, [dims_here])[0]
    summed_grad = upstream * silu_slope(summed)
    buffer = jnp.zeros((4, MSG_ROWS, 128), jnp.bfloat16)
    for sender in range(4):
        if sender < branch_index:
            buffer = buffer.at[sender].set(to_slot(summed_grad.astype(jnp.bfloat16)))
        elif sender > branch_index:
            pooled = block_pool(summed_grad, 2 ** (sender - branch_index))
            buffer = buffer.at[sender].set(to_slot(pooled.astype(jnp.bfloat16)))
    return (to_canvas([summed_grad], jnp.float32), buffer)


def backward_stats(
    branch_index,
    size_kind,
    phase_index,
    dout_canvas,
    message_grads,
    preact_canvas,
    totals,
    counts,
    module_gains,
    module_shifts,
    skip_canvas,
):
    operations = phase_operations(branch_index, phase_index)
    preacts = from_canvas(
        preact_canvas, [preact_dims(size_kind, operation) for operation in operations]
    )
    producing = [operation for operation in operations if operation.act != "none"]
    output_grads = from_canvas(
        dout_canvas, [preact_dims(size_kind, operation) for operation in producing]
    )
    grads_by_name = {
        operation.output: piece for operation, piece in zip(producing, output_grads)
    }
    skip_map = from_canvas(skip_canvas, [map_dims(size_kind, branch_index, C0 << branch_index)])[0]
    upstreams = []
    skip_grads = []
    sums_local = jnp.zeros((2, 2, 3, 8 * C0), jnp.float32)
    for operation, preact in zip(operations, preacts):
        average, inverse_std = norm_terms(totals, counts, size_kind, operation)
        norm_slot = operation.slot
        channels = operation.cout
        centered = (preact - average) * inverse_std
        normed = centered * module_gains[norm_slot, :channels] + module_shifts[norm_slot, :channels]
        if operation.act == "silu":
            upstream = grads_by_name[operation.output] * silu_slope(normed)
        elif operation.act == "res":
            upstream = grads_by_name[operation.output] * silu_slope(normed + skip_map)
            skip_grads.append(upstream)
        else:
            upstream = from_slot(
                message_grads[operation.dest], preact_dims(size_kind, operation)
            ).astype(jnp.float32)
        upstreams.append(upstream)
        position = operation.position
        sums_local = sums_local.at[size_kind, 0, position, :channels].set(
            jnp.sum(upstream, axis=(0, 1, 2))
        )
        sums_local = sums_local.at[size_kind, 1, position, :channels].set(
            jnp.sum(upstream * centered, axis=(0, 1, 2))
        )
    return (to_canvas(upstreams, jnp.float32), sums_local, to_canvas(skip_grads, jnp.float32))


def backward_apply(
    branch_index,
    size_kind,
    phase_index,
    upstream_canvas,
    preact_canvas,
    totals,
    grad_totals,
    counts,
    source_canvas,
    module_weights,
    module_gains,
):
    operations = phase_operations(branch_index, phase_index)
    preacts = from_canvas(
        preact_canvas, [preact_dims(size_kind, operation) for operation in operations]
    )
    upstreams = from_canvas(
        upstream_canvas, [preact_dims(size_kind, operation) for operation in operations]
    )
    source_names = input_names(operations)
    source_list = [source_dims(branch_index, size_kind, map_name) for map_name in source_names]
    pieces = from_canvas(source_canvas, source_list)
    sources = {
        map_name: piece.astype(jnp.bfloat16) for map_name, piece in zip(source_names, pieces)
    }
    source_grads = {
        map_name: jnp.zeros(dims_entry, jnp.float32)
        for map_name, dims_entry in zip(source_names, source_list)
    }
    kernel_grads = []
    slot_count = module_gains.shape[0]
    gain_part = jnp.zeros((slot_count, 8 * C0), jnp.float32)
    shift_part = jnp.zeros((slot_count, 8 * C0), jnp.float32)
    for operation, preact, upstream in zip(operations, preacts, upstreams):
        average, inverse_std = norm_terms(totals, counts, size_kind, operation)
        cells_here = cell_total(counts, size_kind, operation.level)
        norm_slot = operation.slot
        channels = operation.cout
        position = operation.position
        centered = (preact - average) * inverse_std
        mean_upstream = grad_totals[size_kind, 0, position, :channels] / cells_here
        mean_cross = grad_totals[size_kind, 1, position, :channels] / cells_here
        preact_grad = (
            module_gains[norm_slot, :channels]
            * inverse_std
            * (upstream - mean_upstream - centered * mean_cross)
        )
        source_grad, kernel_grad = conv_backward(
            operation,
            sources[operation.source],
            kernel_piece(module_weights, operation),
            preact_grad.astype(jnp.bfloat16),
        )
        source_grads[operation.source] = source_grads[operation.source] + source_grad
        kernel_grads.append(kernel_grad.reshape(-1))
        gain_part = gain_part.at[norm_slot, :channels].set(
            grad_totals[0, 1, position, :channels] + grad_totals[1, 1, position, :channels]
        )
        shift_part = shift_part.at[norm_slot, :channels].set(
            grad_totals[0, 0, position, :channels] + grad_totals[1, 0, position, :channels]
        )
    phase_length = phase_lengths(C0, BLOCKS)[phase_index]
    if kernel_grads:
        joined = jnp.concatenate(kernel_grads)
        weight_part = jnp.pad(joined, (0, phase_length - joined.shape[0]))
    else:
        weight_part = jnp.zeros((phase_length,), jnp.float32)
    return (
        to_canvas([source_grads[map_name] for map_name in source_names], jnp.float32),
        weight_part,
        gain_part,
        shift_part,
    )


def on_device(features, weights, gains, shifts, cotangent, size_group):
    crop_shard = lax.axis_index("crops")
    shard_count = lax.axis_size("crops")
    crop_kind = size_group[crop_shard]
    large_count = jnp.sum(size_group).astype(jnp.float32)
    counts = jnp.stack([shard_count - large_count, large_count])
    case_index = lax.axis_index("branch") * 2 + crop_kind
    phase_total = 2 * BLOCKS + 3
    zero_canvas = jnp.zeros((ROWS, 128), jnp.float32)
    empty_buffer = jnp.zeros((4, MSG_ROWS, 128), jnp.bfloat16)

    def run_phase(function, statics, operands):
        branches_list = [
            partial(function, branch_index, size_kind, *statics)
            for branch_index in range(4)
            for size_kind in range(2)
        ]
        return lax.switch(case_index, branches_list, *operands)

    def statistics(local_totals):
        return lax.psum(local_totals, "crops")

    def module_forward(module, start_canvas, kept):
        module_weights = weights[0, module]
        module_gains = gains[0, module]
        module_shifts = shifts[0, module]
        record = SimpleNamespace(sources=[], preacts=[], totals=[])
        h_canvas = start_canvas
        u_canvas = zero_canvas
        chain_canvas = zero_canvas
        buffer = empty_buffer
        for phase_index in range(phase_total):
            if phase_index < 2 * BLOCKS:
                source = h_canvas if phase_index % 2 == 0 else u_canvas
            elif phase_index == 2 * BLOCKS:
                source = h_canvas
            else:
                source = chain_canvas
            preact, local_totals = run_phase(forward_conv, (phase_index,), (source, module_weights))
            global_totals = kept.totals[phase_index] if kept else statistics(local_totals)
            produced, buffer = run_phase(
                forward_norm,
                (phase_index,),
                (preact, global_totals, counts, module_gains, module_shifts, h_canvas, buffer),
            )
            record.sources.append(source)
            record.preacts.append(preact)
            record.totals.append(global_totals)
            if phase_index < 2 * BLOCKS:
                if phase_index % 2 == 0:
                    u_canvas = produced
                else:
                    h_canvas = produced
            else:
                chain_canvas = produced
        received = (
            kept.received
            if kept
            else jax.tree.map(
                lambda part, own: part.astype(own.dtype),
                lax.all_to_all(as_sent(buffer), "branch", split_axis=0, concat_axis=0, tiled=True),
                buffer,
            )
        )
        result, summed = run_phase(receive_forward, (), (h_canvas, received))
        record.summed = summed
        record.received = received
        return (result, record)

    checkpoints = [features[0].astype(jnp.float32)]
    first_records = []
    for module in range(MODULES):
        result, record = module_forward(module, checkpoints[-1], None)
        checkpoints.append(result)
        first_records.append(record)
    outputs = checkpoints[-1].astype(jnp.bfloat16)
    grad_canvas = cotangent[0].astype(jnp.float32)
    module_grads = [None] * MODULES
    gain_grads = [None] * MODULES
    shift_grads = [None] * MODULES
    for module in reversed(range(MODULES)):
        kept = None
        unused_result, record = module_forward(module, checkpoints[module], kept)
        module_module_weights = weights[0, module]
        module_module_gains = gains[0, module]
        module_module_shifts = shifts[0, module]
        summed_grad, back_buffer = run_phase(receive_backward, (), (grad_canvas, record.summed))
        message_grads = jax.tree.map(
            lambda part, own: part.astype(own.dtype),
            lax.all_to_all(as_sent(back_buffer), "branch", split_axis=0, concat_axis=0, tiled=True),
            back_buffer,
        )
        top_grad = summed_grad
        chain_grad = zero_canvas
        u_grad = zero_canvas
        pending_skip = zero_canvas
        weight_parts = [None] * phase_total
        gain_total = jnp.zeros(gains.shape[2:], jnp.float32)
        shift_total = jnp.zeros(gains.shape[2:], jnp.float32)
        for module_phase_index in reversed(range(phase_total)):
            if module_phase_index >= 2 * BLOCKS:
                output_grad = chain_grad
                skip_canvas = zero_canvas
            elif module_phase_index % 2 == 1:
                output_grad = top_grad
                skip_canvas = record.sources[module_phase_index - 1]
            else:
                output_grad = u_grad
                skip_canvas = zero_canvas
            module_preact = record.preacts[module_phase_index]
            totals = record.totals[module_phase_index]
            upstream, module_local_totals, skip_grad = run_phase(
                backward_stats,
                (module_phase_index,),
                (
                    output_grad,
                    message_grads,
                    module_preact,
                    totals,
                    counts,
                    module_module_gains,
                    module_module_shifts,
                    skip_canvas,
                ),
            )
            grad_totals = lax.psum(module_local_totals, "crops")
            source_grad, weight_parts[module_phase_index], gain_part, shift_part = run_phase(
                backward_apply,
                (module_phase_index,),
                (
                    upstream,
                    module_preact,
                    totals,
                    grad_totals,
                    counts,
                    record.sources[module_phase_index],
                    module_module_weights,
                    module_module_gains,
                ),
            )
            gain_total = gain_total + gain_part
            shift_total = shift_total + shift_part
            if module_phase_index > 2 * BLOCKS:
                chain_grad = source_grad
            elif module_phase_index == 2 * BLOCKS:
                top_grad = top_grad + source_grad
            elif module_phase_index % 2 == 1:
                u_grad = source_grad
                pending_skip = skip_grad
            else:
                top_grad = source_grad + pending_skip
        joined = jnp.concatenate(weight_parts)
        weight_grad = jnp.pad(joined, (0, weights.shape[2] - joined.shape[0]))
        grad_canvas, weight_grad, gain_grads[module], shift_grads[module] = (
            top_grad,
            weight_grad,
            gain_total,
            shift_total,
        )
        module_grads[module] = weight_grad
    weight_out = lax.psum_scatter(jnp.stack(module_grads), "crops", scatter_dimension=1, tiled=True)
    share = gains.shape[3] // shard_count
    gain_out = lax.dynamic_slice_in_dim(jnp.stack(gain_grads), crop_shard * share, share, axis=2)
    shift_out = lax.dynamic_slice_in_dim(jnp.stack(shift_grads), crop_shard * share, share, axis=2)
    return (outputs[None], grad_canvas[None], weight_out[None], gain_out[None], shift_out[None])


LANES = 128
SLOTS = 8
MASKS = 7
DOWN = (((1,), (0,)), ((), ()))
ACROSS = (((1,), (1,)), ((), ()))
ALONG = (((0,), (0,)), ((), ()))


def unit_table(k):
    operations = weighted_plan(k, C0, BLOCKS)
    planes = 8 >> k
    channels = C0 << k
    units = {}
    stat = 0

    def add(name, kind, source, lanes_in, planes_in, planes_out, members):
        nonlocal stat
        segs = []
        tile = 0
        for operation, lanes, chain in members:
            cout = operation.cout
            level = operation.level if operation.taps == 3 else operation.dest
            segs.append(
                SimpleNamespace(
                    slot=operation.slot,
                    off=operation.offset // LANES,
                    cin=operation.cin,
                    cout=cout,
                    taps=operation.taps,
                    tile=tile,
                    tiles=lanes // LANES,
                    blocks=max(1, (8 >> level)),
                    dest=operation.dest,
                    act=operation.act,
                    chain=chain,
                    up=k - operation.dest if operation.taps == 1 else 0,
                )
            )
            tile += lanes // LANES
        rows = {"s1": (384, 384, 512, 768)[k], "s2": lanes_in + LANES, "p1": 256}[kind]
        units[name] = SimpleNamespace(
            name=name,
            kind=kind,
            source=source,
            lanes_in=lanes_in,
            blocks_in=planes_in,
            planes_in=planes_in,
            planes=planes_out,
            segs=segs,
            tiles=tile,
            rows=rows,
            stat=stat,
            depth=1 if kind == "p1" else 3,
        )
        stat += tile

    add("a", "s1", "h", 256, planes, planes, [(operations[0], 256, None)])
    add("b", "s1", "u", 256, planes, planes, [(operations[1], 256, None)])
    ups = [operation for operation in operations if operation.taps == 1]
    if ups:
        add("u", "p1", "t", 256, planes, planes, [(operation, 256, None) for operation in ups])
    firsts, chains = [], {}
    for target in range(k + 1, 4):
        steps = [
            operation
            for operation in operations
            if operation.taps == 3 and operation.stride == 2
        ]
        start = sum(i - k for i in range(k + 1, target))
        chains[target] = steps[start : start + target - k]
        if target == k + 1:
            firsts.append((chains[target][0], 256, None))
        else:
            firsts.append((chains[target][0], LANES, "c1" if target == k + 2 else "c2"))
    if firsts:
        add("d", "s2", "t", 256, planes, planes // 2, firsts)
    if k <= 1:
        add("e", "s2", "c1", LANES, planes // 2, planes // 4, [(chains[k + 2][1], 256, None)])
    if k == 0:
        add("f", "s2", "c2", LANES, planes // 2, planes // 4, [(chains[3][1], LANES, "c3")])
        add("g", "s2", "c3", LANES, planes // 4, planes // 8, [(chains[3][2], 256, None)])
    return units


def links(k, unit, seg):
    cin = seg.cin
    count_in, count_out = unit.blocks_in, seg.blocks
    found = []
    if unit.kind == "p1":
        for plane in range(count_in):
            wide = 1 << seg.up
            found.append((plane * cin, 0, set(range(plane * wide, plane * wide + wide))))
        return found
    if unit.kind == "s1" and k == 3:
        return [(256 * tap, tap, {0}) for tap in range(3)]
    stride = 1 if unit.kind == "s1" else 2
    for plane in range(count_in):
        for tap in range(3):
            at = plane - tap + 1
            if at % stride == 0 and 0 <= at // stride < count_out:
                found.append((plane * cin, tap, {at // stride}))
    if stride == 1:
        found.append((256, 2, {count_out - 1}))
        found.append((unit.rows - cin, 0, {0}))
    else:
        lanes_in = unit.lanes_in
        found.append((lanes_in + (count_in - 1) * cin - (lanes_in - LANES), 0, {0}))
    return found


def message_slot(k, other):
    return sum(2 * (8 >> max(k, before)) for before in range(other) if before != k)


def log2(value):
    return value.bit_length() - 1


def sigmoid_of(value):
    return 0.5 * jnp.tanh(0.5 * value) + 0.5


def silu_of(value):
    return value * sigmoid_of(value)


def slope_of(value):
    sigmoid = sigmoid_of(value)
    return sigmoid * (1.0 + value * (1.0 - sigmoid))


def planes_loop(count, body, turns=1):
    def step(index, carry):
        for turn in range(turns):
            body(index * turns + turn)
        return carry

    turns = min(turns, count)
    if count == turns:
        for index in range(count):
            body(index)
    else:
        lax.fori_loop(0, count // turns, step, 0)


def planes_sum(count, body, initial, turns=1):
    def step(index, carry):
        for turn in range(turns):
            carry = body(index * turns + turn, carry)
        return carry

    turns = min(turns, count)
    if count == turns:
        return step(0, initial)
    return lax.fori_loop(0, count // turns, step, initial)


def partial_sum(value):
    rows = value.shape[0]
    return jnp.sum(value.reshape(rows // 8, 8, value.shape[1]), axis=0)


class Planes:
    def __init__(self, mode, tiles, planes, masks, rows, main, edge=None, right=None, narrow=False):
        self.narrow, self.pending = narrow, None
        self.mode, self.tiles, self.planes = mode, tiles, planes
        self.masks, self.rows = masks, rows
        self.main, self.edge, self.right = main, edge, right
        self.base = 1 if mode in ("s1", "wide", "s2") else 0
        extra = {"s1": 2, "wide": 2, "s2": 1, "dz2": 1, "p": 0}[mode]
        self.span = planes + extra
        self.unit = tiles * self.span

    def at(self, m, tile, plane):
        return m * self.unit + tile * self.span + plane + self.base

    def edge_at(self, m, tile, plane):
        if self.mode == "s2" or self.narrow:
            return m * self.span + plane + self.base
        return self.at(m, tile, plane)

    def from_left(self, value):
        return pltpu.roll(value, 1, 0) * self.masks[1]

    def from_right(self, value):
        return pltpu.roll(value, self.rows - 1, 0) * self.masks[2]

    def store(self, m, tile, plane, value):
        self.put(m, tile, plane, value)

    def put(self, m, tile, plane, value):
        where = self.at(m, tile, plane)
        self.main[where] = value.astype(jnp.bfloat16)
        if self.mode == "s1":
            side = self.from_right(value) if tile == 0 else self.from_left(value)
            if not self.narrow:
                self.edge[where] = side.astype(jnp.bfloat16)
            elif tile == 0:
                self.pending = side
            else:
                lane = lax.broadcasted_iota(jnp.int32, side.shape, 1)
                side = jnp.where(lane < LANES // 2, self.pending, side)
                self.edge[self.edge_at(m, tile, plane)] = side.astype(jnp.bfloat16)
        elif self.mode == "wide":
            self.edge[where] = self.from_left(value).astype(jnp.bfloat16)
            self.right[where] = self.from_right(value).astype(jnp.bfloat16)
        elif self.mode == "s2":
            if tile == self.tiles - 1:
                self.edge[self.edge_at(m, tile, plane)] = self.from_left(value).astype(jnp.bfloat16)
        elif self.mode == "dz2":
            self.edge[where] = self.from_right(value).astype(jnp.bfloat16)

    def put_above(self, m, tile, last):
        if self.mode in ("s1", "wide", "s2"):
            above = pltpu.roll(last, 6, 0) * self.masks[3] + pltpu.roll(last, 3, 0) * self.masks[4]
            self.put(m, tile, -1, above)

    def put_below(self, m, tile, first):
        if self.mode in ("s1", "wide", "dz2"):
            rows = self.rows
            below = (
                pltpu.roll(first, rows - 6, 0) * self.masks[5]
                + pltpu.roll(first, rows - 3, 0) * self.masks[6]
            )
            self.put(m, tile, self.planes, below)

    def close(self, m):
        for tile in range(self.tiles):
            last = self.main[self.at(m, tile, self.planes - 1)].astype(jnp.float32)
            self.put_above(m, tile, last)
        for tile in range(self.tiles):
            first = self.main[self.at(m, tile, 0)].astype(jnp.float32)
            self.put_below(m, tile, first)


class Branch:
    def __init__(self, k, rows, large, small, share, refs, masks, core):
        self.k, self.rows, self.refs, self.masks = k, rows, refs, masks
        self.units = unit_table(k)
        self.planes = 8 >> k
        self.core = core
        self.large, self.small, self.count = large, small, large + small
        self.cells = (small * (SH // 8) * (SW // 8), large * (LH // 8) * (LW // 8))
        self.quarter = lax.axis_index("crops") // 2
        self.share = share
        r = refs
        make = partial(Planes, masks=masks, rows=rows)
        make_one = partial(make, narrow=k <= 1)
        one = "wide" if k == 3 else "s1"
        self.maps = dict(
            h=make_one(one, 2, self.planes, main=r.hC, edge=r.hE, right=r.hR),
            u=make_one(one, 2, self.planes, main=r.uC, edge=r.uE, right=r.uR),
            t=make("p" if k == 3 else "s2", 2, self.planes, main=r.tC, edge=r.tE),
        )
        if k <= 1:
            self.maps["c1"] = make("s2", 1, self.planes // 2, main=r.c1C, edge=r.c1E)
        if k == 0:
            self.maps["c2"] = make("s2", 1, 4, main=r.c2C, edge=r.c2E)
            self.maps["c3"] = make("s2", 1, 2, main=r.c3C, edge=r.c3E)
        self.grads = dict(t=r.gt, u=r.gu, c1=r.gc1, c2=r.gc2, c3=r.gc3)

    def lane_block(self, shape, cout):
        lanes = lax.broadcasted_iota(jnp.int32, shape, 1)
        return lanes >> log2(cout)

    def keep(self, value, cout, which):
        count = LANES // cout
        if len(which) == count:
            return value
        block = self.lane_block(value.shape, cout)
        mask = block == which[0]
        for entry in which[1:]:
            mask = mask | (block == entry)
        return jnp.where(mask, value, 0.0)

    def spread(self, value, cout):
        shift = LANES // 2
        while shift >= cout:
            value = value + pltpu.roll(value, shift, 1)
            shift //= 2
        return value

    def local_blocks(self, seg, tile, wanted):
        count = LANES // seg.cout
        return [q for q in range(count) if (tile * count + q) % seg.blocks in wanted]


    def segments(self):
        return [(unit, seg) for unit in self.units.values() for seg in unit.segs]

    def pieces(self):
        found, place = [], 0
        for index, (unit, seg) in enumerate(self.segments()):
            count = 2 * seg.taps**2 * seg.cin * seg.cout // LANES
            if self.k < 3:
                found.append((index, 0, count, place, index))
                place += count
            else:
                for d in range(unit.depth):
                    slot = len(found) % 3
                    found.append((index, d, count // unit.depth, slot * 3072, slot))
        return found

    def fetch(self, at):
        r = self.refs
        index, d, count, place, sem = self.pieces()[at]
        _, seg = self.segments()[index]
        return pltpu.make_async_copy(
            r.w.at[pl.ds(2 * seg.off + d * count, count)],
            r.raw.at[pl.ds(place, count)],
            r.wsem.at[sem],
        )

    def fetch_first(self):
        for at in range(len(self.pieces()) if self.k < 3 else 3):
            self.fetch(at).start()

    def expand(self, index):
        unit, seg = self.segments()[index]
        pieces = self.pieces()
        mine = [at for at, piece in enumerate(pieces) if piece[0] == index]
        if self.k < 3:
            (at,) = mine
            self.fetch(at).wait()
            count = pieces[at][2] // unit.depth
            planes_loop(
                unit.depth,
                lambda d: self.expand_row(unit, seg, d, count, pieces[at][3] + d * count),
            )
        else:
            for d, at in enumerate(mine):
                self.fetch(at).wait()
                self.expand_row(unit, seg, d, pieces[at][2], pieces[at][3])
                if at + 3 < len(pieces):
                    self.fetch(at + 3).start()
        for m in range(MODULES):
            self.spread_tables(m, unit, seg)

    def expand_row(self, unit, seg, d, count, place):
        r = self.refs
        chunk = math.gcd(count, 384)
        wf, rep = r.work, r.rep

        def widen(step):
            at = pl.multiple_of(step * chunk, 16)
            value = r.raw[pl.ds(pl.multiple_of(place + at, 16), chunk)].astype(jnp.float32)
            wf[pl.ds(at, chunk)] = value

        planes_loop(count // chunk, widen)
        count = count // MODULES
        depth, cin, cout = unit.depth, seg.cin, seg.cout
        target = getattr(r, "T" + unit.name)
        twice = unit.kind == "s1" and self.k < 3
        across = getattr(r, "T" + unit.name + unit.name) if twice else None
        by_row = {}
        for row, tap, wanted in links(self.k, unit, seg):
            by_row.setdefault(row, []).append((tap, wanted))

        def module(m):
            if cout < LANES:
                ratio = LANES // cout
                flat = wf[pl.ds(m, count, stride=2)]
                for part in range(ratio):
                    rep[pl.ds(part, count, stride=ratio)] = self.spread(
                        self.keep(flat, cout, [part]), cout
                    )

            def tap_rows(tap, tile):
                if cout < LANES:
                    return rep[tap * cin : (tap + 1) * cin]
                if cout == LANES:
                    return wf[pl.ds(m + tap * (2 * cin), cin, stride=2)]
                return wf[pl.ds(m + tap * (4 * cin) + 2 * tile, cin, stride=4)]

            for tile in range(seg.tiles):
                column = (seg.tile + tile) * LANES
                for row in range(0, unit.rows, cin):
                    total = None
                    for tap, wanted in by_row.get(row, []):
                        if cout <= LANES:
                            local = self.local_blocks(seg, tile, wanted)
                            if not local:
                                continue
                            piece = self.keep(tap_rows(tap, 0), cout, local)
                        else:
                            piece = tap_rows(tap, tile)
                        total = piece if total is None else total + piece
                    if total is None:
                        total = jnp.zeros((cin, LANES), jnp.float32)
                    block = total.astype(jnp.bfloat16)
                    target[m * depth + d, row : row + cin, column : column + LANES] = block

            if not twice:
                return
            turned = []
            if cin == LANES:
                turned = [jnp.transpose(tap_rows(tap, 0)) for tap in range(3)]
            else:
                both = jnp.transpose(rep[0 : -(-3 * cin // LANES) * LANES])
                for tap in range(3):
                    first = tap * cin // LANES * LANES
                    value = both[0:cin, first : first + LANES]
                    value = self.keep(value, cin, [tap * cin % LANES // cin])
                    turned.append(self.spread(value, cin))
            for tile in range(2):
                for row in range(0, unit.rows, cin):
                    total = None
                    for tap, wanted in by_row.get(row, []):
                        local = self.local_blocks(seg, tile, wanted)
                        if local:
                            piece = self.keep(turned[2 - tap], cin, local)
                            total = piece if total is None else total + piece
                    if total is None:
                        total = jnp.zeros((cin, LANES), jnp.float32)
                    column = tile * LANES
                    across[m * depth + d, row : row + cin, column : column + LANES] = total.astype(
                        jnp.bfloat16
                    )

        planes_loop(MODULES, module)


    def parts(self, unit, source):
        if unit.kind == "p1":
            return [(source.main, range(2), source.at)]
        if source.mode == "wide":
            return [
                (source.edge, range(2), source.at),
                (source.main, range(2), source.at),
                (source.right, range(2), source.at),
            ]
        if unit.kind == "s1":
            tiles = [0] if source.narrow else range(2)
            return [(source.main, range(2), source.at), (source.edge, tiles, source.edge_at)]
        last = source.tiles - 1
        return [
            (source.main, range(source.tiles), source.at),
            (source.edge, [last], source.edge_at),
        ]

    def rows_of(self, unit, part, m, d, first, count):
        ref, tiles, at = part
        pieces = []
        for tile in tiles:
            if unit.kind == "s2":
                rows = [ref[at(m, tile, 2 * (first + q) + d - 1)] for q in range(count)]
                pieces.append(rows[0] if count == 1 else jnp.concatenate(rows, axis=0))
            else:
                shift = d - 1 if unit.kind == "s1" else 0
                pieces.append(
                    ref[pl.ds(at(m, tile, first + shift), count)].reshape(count * self.rows, LANES)
                )
        return pieces

    def conv(self, m, unit):
        r = self.refs
        source = self.maps[unit.source]
        target = getattr(r, "T" + unit.name)
        z = getattr(r, "z" + unit.name)
        planes, tiles, depth = unit.planes, unit.tiles, unit.depth
        chunk = min(planes, 4 if tiles <= 2 else 2)
        lanes = tiles * LANES

        def body(step, sums):
            first = step * chunk
            pieces = []
            for d in range(depth):
                for part in self.parts(unit, source):
                    pieces += self.rows_of(unit, part, m, d, first, chunk)
            left = jnp.concatenate(pieces, axis=1)
            right = target[pl.ds(m * depth, depth), 0 : unit.rows, 0:lanes]
            right = right.reshape(depth * unit.rows, lanes)
            result = lax.dot_general(left, right, DOWN, preferred_element_type=jnp.float32)
            for tile in range(tiles):
                block = result[:, tile * LANES : (tile + 1) * LANES]
                z[pl.ds(m * tiles * planes + tile * planes + first, chunk)] = block.reshape(
                    chunk, self.rows, LANES
                )
            return (sums[0] + partial_sum(result), sums[1] + partial_sum(result * result))

        zero = jnp.zeros((8, lanes), jnp.float32)
        sums = planes_sum(planes // chunk, body, (zero, zero))
        for seg in unit.segs:
            scale = self.per_cell(unit, seg)
            totals = self.fold(seg, sums)
            self.norm_rows(m, unit, seg, totals, scale)

    def per_cell(self, unit, seg):
        blocks = seg.tiles * LANES // seg.cout
        small, large = self.cells
        count = unit.planes * blocks
        return jnp.where(self.core == 0, 1.0 / (large * count), 1.0 / (small * count)).astype(
            jnp.float32
        )

    def fold(self, seg, sums):
        first = seg.tile
        found = []
        for value in sums:
            tiles = [
                value[:, (first + t) * LANES : (first + t + 1) * LANES] for t in range(seg.tiles)
            ]
            if seg.cout <= LANES:
                total = tiles[0]
                for tile in tiles[1:]:
                    total = total + tile
                total = jnp.sum(self.spread(total, seg.cout), axis=0, keepdims=True)
                found.append([total] * seg.tiles)
            else:
                found.append([jnp.sum(tile, axis=0, keepdims=True) for tile in tiles])
        return found

    def table_row(self, ref, m, seg, tile):
        slot = seg.slot
        if seg.cout > LANES:
            return ref[m, slot : slot + 1, tile * LANES : (tile + 1) * LANES]
        row = jnp.broadcast_to(ref[m, slot : slot + 1, 0:LANES], (8, LANES))
        if seg.cout < LANES:
            row = self.spread(self.keep(row, seg.cout, [0]), seg.cout)
        return row[0:1]

    def norm_rows(self, m, unit, seg, totals, scale):
        st = self.refs.st
        for tile in range(seg.tiles):
            average = totals[0][tile] * scale
            variance = totals[1][tile] * scale - average * average
            inverse = lax.rsqrt(variance + EPS)
            where = m * STATS + unit.stat + seg.tile + tile
            factor = st[where, 4:5] * inverse
            st[where, 0:1] = average
            st[where, 1:2] = inverse
            st[where, 2:3] = factor
            st[where, 3:4] = st[where, 5:6] - average * factor

    def spread_tables(self, m, unit, seg):
        st = self.refs.st
        for tile in range(seg.tiles):
            where = m * STATS + unit.stat + seg.tile + tile
            st[where, 4:5] = self.table_row(self.refs.gains, m, seg, tile)
            st[where, 5:6] = self.table_row(self.refs.shifts, m, seg, tile)

    def normed(self, m, unit, tile, plane):
        st = self.refs.st
        z = getattr(self.refs, "z" + unit.name)
        where = m * STATS + unit.stat + tile
        value = z[m * unit.tiles * unit.planes + tile * unit.planes + plane]
        return value * st[where, 2:3] + st[where, 3:4]

    def apply_a(self, m):
        unit, u = self.units["a"], self.maps["u"]

        def body(plane):
            for tile in range(2):
                value = silu_of(self.normed(m, unit, tile, plane)) * self.masks[0]
                u.store(m, tile, plane, value)

        planes_loop(self.planes, body, TURNS)
        u.close(m)

    def apply_b(self, m):
        unit, top = self.units["b"], self.maps["t"]
        hf, s = self.refs.hf, self.refs.s

        def body(plane):
            for tile in range(2):
                where = m * 2 * self.planes + tile * self.planes + plane
                value = silu_of(self.normed(m, unit, tile, plane) + hf[where]) * self.masks[0]
                s[where] = value
                top.store(m, tile, plane, value)

        planes_loop(self.planes, body, TURNS)
        top.close(m)

    def apply_rest(self, m, unit):
        sb = self.refs.sb
        for seg in unit.segs:
            chain = self.maps[seg.chain] if seg.chain else None

            def body(plane):
                for tile in range(seg.tiles):
                    value = self.normed(m, unit, seg.tile + tile, plane)
                    if chain is not None:
                        chain.store(m, tile, plane, silu_of(value) * self.masks[0])
                    else:
                        at = message_slot(self.k, seg.dest) + tile * unit.planes + plane
                        sb[at] = value.astype(jnp.bfloat16)

            planes_loop(unit.planes, body, TURNS)
            if chain is not None:
                chain.close(m)
            else:
                self.message(m, seg.dest).start()

    def message(self, e, other):
        count = 2 * (8 >> max(self.k, other))
        r = self.refs
        return pltpu.make_async_remote_copy(
            src_ref=r.sb.at[pl.ds(message_slot(self.k, other), count)],
            dst_ref=r.rb.at[pl.ds(e * 16 + message_slot(other, self.k), count)],
            send_sem=r.ssem.at[e * 4 + other],
            recv_sem=r.rsem.at[e * 4 + self.k],
            device_id=dict(branch=other),
            device_id_type=pl.DeviceIdType.MESH,
        )

    def arrived(self, e, other):
        count = 2 * (8 >> max(self.k, other))
        r = self.refs
        at = message_slot(self.k, other)
        return pltpu.make_async_remote_copy(
            src_ref=r.sb.at[pl.ds(at, count)],
            dst_ref=r.rb.at[pl.ds(e * 16 + at, count)],
            send_sem=r.ssem.at[e * 4 + other],
            recv_sem=r.rsem.at[e * 4 + other],
            device_id=dict(branch=other),
            device_id_type=pl.DeviceIdType.MESH,
        )

    def others(self):
        return [other for other in range(4) if other != self.k]

    def sent(self, e):
        for other in self.others():
            self.message(e, other).wait_send()

    def receive(self, m):
        r = self.refs
        s, rb, hf, out = r.s, r.rb, r.hf, r.outs
        h = self.maps["h"]

        def total_at(tile, plane):
            where = m * 2 * self.planes + tile * self.planes + plane
            total = s[where]
            for other in self.others():
                count = 8 >> max(self.k, other)
                at = plane >> max(0, other - self.k)
                slot = m * 16 + message_slot(self.k, other) + tile * count + at
                total = total + rb[slot].astype(jnp.float32)
            s[where] = total
            return silu_of(total) * self.masks[0]

        def onward(plane):
            for tile in range(2):
                value = total_at(tile, plane)
                hf[(2 + tile) * self.planes + plane] = value
                h.store(1, tile, plane, value)

        def finish(plane):
            for tile in range(2):
                out[tile * self.planes + plane] = total_at(tile, plane).astype(jnp.bfloat16)

        @pl.when(m + 1 < MODULES)
        def _():
            planes_loop(self.planes, onward)
            h.close(1)

        @pl.when(m + 1 == MODULES)
        def _():
            planes_loop(self.planes, finish)

    def take_feature(self, tile, plane, value):
        self.refs.hf[tile * self.planes + plane] = value
        self.maps["h"].store(0, tile, plane, value)

    def take_cotangent(self, tile, plane, value):
        self.refs.gin[tile * self.planes + plane] = value

    def member(self, kind, order):
        kinds = self.refs.kinds
        found, before = jnp.int32(0), jnp.int32(0)
        for at in range(self.count):
            same = kinds[at] == kind
            found = jnp.where(same & (before == order), at, found)
            before = before + same.astype(jnp.int32)
        return found

    def order(self, device):
        kinds = self.refs.kinds
        kind = kinds[device]
        before = jnp.int32(0)
        for at in range(self.count):
            before = before + ((kinds[at] == kind) & (at < device)).astype(jnp.int32)
        return before

    def unpack(self, t, consume):
        r = self.refs
        work, rows, planes = r.work, self.rows, self.planes
        full = SH * SW * C0 // LANES
        gath = r.gathc if t else r.gathx

        @pl.when(self.core == 0)
        def _():
            for at in range(self.large):
                block = gath[self.member(1, at)]
                work[at * ROWS : (at + 1) * ROWS] = block.astype(jnp.float32)

        @pl.when(self.core == 1)
        def _():
            for at in range(self.small):
                block = gath[self.member(0, at), 0:full]
                work[at * full : (at + 1) * full] = block.astype(jnp.float32)
            work[self.small * full : self.large * ROWS] = jnp.zeros(
                (self.large * ROWS - self.small * full, LANES), jnp.float32
            )

        deep = self.large * ROWS // 2
        right = jnp.concatenate([work[pl.ds(j, deep, stride=2)] for j in range(2)], axis=1)
        right = right.astype(jnp.bfloat16)
        cells = Cells(self.core, (rows, LANES), self.small, self.large)
        base = cells.crop * cells.pick(ROWS // 2, full // 2)
        base = base + cells.along * (planes * cells.wide) + cells.across
        base = jnp.where(cells.valid, base, -(1 << 20))
        lane = lax.broadcasted_iota(jnp.int32, (rows, LANES), 1)
        chunk = min(planes, 4)

        def body(step):
            pieces = []
            for q in range(chunk):
                goal = base + (step * chunk + q) * cells.wide
                pieces.append(one_hot(goal, lane, deep))
            left = pieces[0] if chunk == 1 else jnp.concatenate(pieces, axis=0)
            result = lax.dot_general(left, right, DOWN, preferred_element_type=jnp.float32)
            for q in range(chunk):
                for tile in range(2):
                    value = result[q * rows : (q + 1) * rows, tile * LANES : (tile + 1) * LANES]
                    consume(tile, step * chunk + q, value)

        planes_loop(planes // chunk, body)

    def pack_size(self):
        return 48 * self.planes, -(-self.planes * self.rows // LANES) * LANES

    def plan_pack(self):
        r = self.refs
        high, deep = self.pack_size()
        planes = self.planes
        q = lax.broadcasted_iota(jnp.int32, (high, LANES), 0)
        lane = lax.broadcasted_iota(jnp.int32, (high, LANES), 1)
        wide, tall = jnp.where(self.core == 0, 6, 3), jnp.where(self.core == 0, 8, 4)
        cell = jnp.where(self.core == 0, (q * 43691) >> 18, (q * 43691) >> 17)
        across = q - cell * wide
        plane = cell & (planes - 1)
        along = cell >> log2(planes)
        base = plane * self.rows + along * wide + across
        base = jnp.where(along < tall, base, -(1 << 20))
        shard = lax.axis_index("crops")
        for at, device in enumerate((shard, shard + 1 - 2 * self.core)):
            goal = base + self.order(device) * (wide * tall)
            r.hot[at, 0:high, 0:deep] = one_hot(goal, lane, deep)

    def pack(self, units, put):
        high, deep = self.pack_size()
        right = jnp.concatenate([units(tile) for tile in range(2)], axis=1)
        short = deep - right.shape[0]
        parts = [right.astype(jnp.bfloat16)]
        if right.dtype == jnp.float32:
            parts.append((right - parts[0].astype(jnp.float32)).astype(jnp.bfloat16))
        if short:
            empty = jnp.zeros((short, 2 * LANES), jnp.bfloat16)
            parts = [jnp.concatenate([part, empty], axis=0) for part in parts]
        for at in range(2):
            total = None
            for part in parts:
                piece = lax.dot_general(
                    self.refs.hot[at, 0:high, 0:deep],
                    part,
                    DOWN,
                    preferred_element_type=jnp.float32,
                )
                total = piece if total is None else total + piece
            for tile in range(2):
                put(at, pl.ds(tile, high, stride=2), total[:, tile * LANES : (tile + 1) * LANES])

    def pack_outputs(self):
        r = self.refs
        high = 2 * self.pack_size()[0]

        def put(at, where, value):
            r.work[pl.ds(at * ROWS + where.start, where.size, stride=2)] = value

        def units(tile):
            block = r.outs[tile * self.planes : (tile + 1) * self.planes]
            return block.reshape(self.planes * self.rows, LANES)

        self.pack(units, put)
        for at in range(2):
            r.blocks[at, 0:high] = r.work[at * ROWS : at * ROWS + high].astype(jnp.bfloat16)
            if high < ROWS:
                r.blocks[at, high:ROWS] = jnp.zeros((ROWS - high, LANES), jnp.bfloat16)

    def pack_gradient(self):
        r = self.refs
        high = 2 * self.pack_size()[0]

        def put(at, where, value):
            r.slopes[at, where] = value

        def units(tile):
            block = r.gin[tile * self.planes : (tile + 1) * self.planes]
            return block.reshape(self.planes * self.rows, LANES)

        self.pack(units, put)
        if high < ROWS:
            for at in range(2):
                r.slopes[at, high:ROWS] = jnp.zeros((ROWS - high, LANES), jnp.float32)

    def forward(self, m, gather):
        steps = iter(range(1, 4))

        def also():
            step = next(steps, None)
            if step is not None:

                @pl.when(m == 0)
                def _():
                    gather.step(1, step)

        self.conv(m, self.units["a"])
        self.apply_a(m)
        also()
        self.conv(m, self.units["b"])
        self.apply_b(m)
        also()

        @pl.when(m > 0)
        def _():
            self.sent(m - 1)

        for name in ("d", "u", "e", "f", "g"):
            if name in self.units:
                self.conv(m, self.units[name])
                self.apply_rest(m, self.units[name])
                also()
        for _ in range(3):
            also()

        @pl.when(m == MODULES - 1)
        def _():
            gather.collect(1)
            self.unpack(1, self.take_cotangent)

        for other in self.others():
            self.arrived(m, other).wait_recv()
        self.receive(m)


    def send_back(self, m):
        r = self.refs
        s, gin, gt, sb = r.s, r.gin, r.gt, r.sb
        e = MODULES + m

        def body(plane):
            for tile in range(2):
                at = tile * self.planes + plane
                value = gin[at] * slope_of(s[m * 2 * self.planes + at])
                gt[at] = value
                for other in range(self.k):
                    sb[message_slot(self.k, other) + at] = value.astype(jnp.bfloat16)

        planes_loop(self.planes, body, TURNS)
        for other in reversed(self.others()):
            if other > self.k:
                count = 8 >> other
                wide = 1 << (other - self.k)

                def pool(plane):
                    for tile in range(2):
                        total = gt[tile * self.planes + plane * wide]
                        for step in range(1, wide):
                            total = total + gt[tile * self.planes + plane * wide + step]
                        slot = message_slot(self.k, other) + tile * count + plane
                        sb[slot] = total.astype(jnp.bfloat16)

                planes_loop(count, pool, TURNS)
            self.message(e, other).start()

    def back_unit(self, m, unit):
        r = self.refs
        st, dyb, z = r.st, r.dyb, getattr(r, "z" + unit.name)
        name, planes, tiles = unit.name, unit.planes, unit.tiles
        e = MODULES + m
        sums = {}

        def upstream(seg, tile, plane, normed):
            at = tile * planes + plane
            if name == "b":
                hf = r.hf[m * 2 * planes + at]
                value = r.gt[at] * slope_of(normed + hf)
                r.gin[at] = value
                return value
            if name == "a":
                return r.gu[at] * slope_of(normed)
            if seg.chain:
                return self.grads[seg.chain][at] * slope_of(normed)
            return r.rb[e * 16 + message_slot(self.k, seg.dest) + at].astype(jnp.float32)

        for seg in unit.segs:

            def body(plane, carry):
                result = []
                for tile in range(seg.tiles):
                    at = (seg.tile + tile) * planes + plane
                    where = m * STATS + unit.stat + seg.tile + tile
                    value = z[m * tiles * planes + at]
                    normed = value * st[where, 2:3] + st[where, 3:4]
                    dy = upstream(seg, tile, plane, normed)
                    dyb[at] = dy
                    zhat = (value - st[where, 0:1]) * st[where, 1:2]
                    result.append(carry[2 * tile] + partial_sum(dy))
                    result.append(carry[2 * tile + 1] + partial_sum(dy * zhat))
                return tuple(result)

            zero = jnp.zeros((8, LANES), jnp.float32)
            found = planes_sum(planes, body, (zero,) * (2 * seg.tiles), TURNS)
            pair = [
                jnp.concatenate([found[2 * tile + which] for tile in range(seg.tiles)], axis=1)
                for which in range(2)
            ]
            plain = SimpleNamespace(**vars(seg))
            plain.tile = 0
            totals = self.fold(plain, pair)
            self.table_grads(m, seg, totals)
            sums[seg.slot] = totals
        dz = self.dz_planes(unit)
        for seg in unit.segs:
            scale = self.per_cell(unit, seg)
            totals = sums[seg.slot]

            def apply(plane):
                for tile in range(seg.tiles):
                    at = (seg.tile + tile) * planes + plane
                    where = m * STATS + unit.stat + seg.tile + tile
                    zhat = (z[m * tiles * planes + at] - st[where, 0:1]) * st[where, 1:2]
                    inner = dyb[at] - totals[0][tile] * scale - zhat * (totals[1][tile] * scale)
                    dz.store(0, seg.tile + tile, plane, inner * st[where, 2:3] * self.masks[0])

            planes_loop(planes, apply, TURNS)
        dz.close(0)
        self.back_data(m, unit, dz)
        first = min(seg.off for seg in unit.segs)
        last = max(seg.off + seg.taps**2 * seg.cin * seg.cout // LANES for seg in unit.segs)
        wanted = (self.quarter * self.share < last) & ((self.quarter + 1) * self.share > first)

        @pl.when(wanted)
        def _():
            self.back_kernel(m, unit, dz)

    def dz_planes(self, unit):
        r = self.refs
        mode = {"p1": "p", "s2": "dz2", "s1": "wide" if self.k == 3 else "s1"}[unit.kind]
        return Planes(
            mode,
            unit.tiles,
            unit.planes,
            self.masks,
            self.rows,
            r.dC,
            r.dE,
            r.dR,
            self.k <= 1 and unit.kind == "s1",
        )

    def table_grads(self, m, seg, totals):
        gg = self.refs.gg
        slot = seg.slot
        for which, found in ((0, totals[1]), (1, totals[0])):
            if seg.cout > LANES:
                for tile in range(2):
                    gg[m, which, slot : slot + 1, tile * LANES : (tile + 1) * LANES] = found[tile]
            else:
                row = jnp.broadcast_to(found[0], (8, LANES))
                if seg.cout < LANES:
                    row = self.keep(row, seg.cout, [0])
                gg[m, which, slot : slot + 1, 0:LANES] = row[0:1]

    def wide_rows(self, ref, at, tiles, plane, count):
        pieces = [
            ref[pl.ds(at(0, tile, plane), count)].reshape(count * self.rows, LANES)
            for tile in range(tiles)
        ]
        return pieces[0] if tiles == 1 else jnp.concatenate(pieces, axis=1)

    def back_data(self, m, unit, dz):
        r = self.refs
        kind, tiles = unit.kind, unit.tiles
        target = getattr(r, "T" + unit.name)
        lanes = tiles * LANES
        rows = self.rows

        def kernel_rows(d, first, count):
            return target[m * unit.depth + d, first : first + count, 0:lanes]

        def product(left, right):
            return lax.dot_general(left, right, ACROSS, preferred_element_type=jnp.float32)

        def put(ref, tile, planes, first, count, value, step=1, add=False):
            block = value.reshape(count, rows, LANES)
            for q in range(count):
                at = tile * planes + first + q * step
                ref[at] = ref[at] + block[q] if add else block[q]

        planes = unit.planes
        if kind == "s1":
            goal = r.gu if unit.name == "b" else r.gin
            add = unit.name == "a"
            chunk = min(planes, 4)
            across = getattr(r, "T" + unit.name + unit.name)

            def body(step):
                first = step * chunk
                if self.k == 3:
                    total = None
                    for d in range(3):
                        for ref, at in ((dz.right, 0), (dz.main, 256), (dz.edge, 512)):
                            left = self.wide_rows(ref, dz.at, 2, first + 1 - d, chunk)
                            piece = product(left, kernel_rows(d, at, 256))
                            total = piece if total is None else total + piece
                else:
                    narrow = 1 if dz.narrow else 2
                    left = []
                    for d in range(3):
                        at = first + 1 - d
                        left.append(self.wide_rows(dz.main, dz.at, 2, at, chunk))
                        left.append(self.wide_rows(dz.edge, dz.edge_at, narrow, at, chunk))
                    right = across[pl.ds(m * 3, 3), 0 : unit.rows].reshape(3 * unit.rows, 256)
                    total = lax.dot_general(
                        jnp.concatenate(left, axis=1),
                        right,
                        DOWN,
                        preferred_element_type=jnp.float32,
                    )
                for tile in range(2):
                    put(
                        goal,
                        tile,
                        planes,
                        first,
                        chunk,
                        total[:, tile * LANES : (tile + 1) * LANES],
                        add=add,
                    )

            planes_loop(planes // chunk, body)
            return
        if kind == "p1":
            left = self.wide_rows(dz.main, dz.at, tiles, 0, planes)
            total = product(left, kernel_rows(0, 0, 256))
            for tile in range(2):
                put(
                    r.gt,
                    tile,
                    planes,
                    0,
                    planes,
                    total[:, tile * LANES : (tile + 1) * LANES],
                    add=True,
                )
            return
        goal = self.grads[unit.source]
        add = unit.source == "t"
        lanes_in = unit.lanes_in
        count_in = unit.planes_in
        for parity, terms in ((0, [(1, 0)]), (1, [(2, 0), (0, 1)])):
            total, side = None, None
            for d, offset in terms:
                left = self.wide_rows(dz.main, dz.at, tiles, offset, planes)
                piece = product(left, kernel_rows(d, 0, lanes_in))
                total = piece if total is None else total + piece
                left = self.wide_rows(dz.edge, dz.at, tiles, offset, planes)
                piece = product(left, kernel_rows(d, lanes_in, LANES))
                side = piece if side is None else side + piece
            for tile in range(lanes_in // LANES):
                value = total[:, tile * LANES : (tile + 1) * LANES]
                if tile == lanes_in // LANES - 1:
                    value = value + side
                put(goal, tile, count_in, parity, planes, value, step=2, add=add)

    def back_kernel(self, m, unit, dz):
        r = self.refs
        G, rep, wgv = r.work, r.rep, r.wgv
        tiles, planes = unit.tiles, unit.planes
        source = self.maps[unit.source]
        right = self.wide_rows(dz.main, dz.at, tiles, 0, planes)

        def gather(d):
            at = 0
            for part in self.parts(unit, source):
                pieces = self.rows_of(unit, part, m, d, 0, planes)
                left = pieces[0] if len(pieces) == 1 else jnp.concatenate(pieces, axis=1)
                count = left.shape[1]
                result = lax.dot_general(left, right, ALONG, preferred_element_type=jnp.float32)
                for tile in range(tiles):
                    row = pl.multiple_of((d * tiles + tile) * unit.rows + at, 8)
                    G[pl.ds(row, count)] = result[:, tile * LANES : (tile + 1) * LANES]
                at += count

        planes_loop(unit.depth, gather)
        for seg in unit.segs:
            self.fold_kernel(m, unit, seg)

    def fold_kernel(self, m, unit, seg):
        r = self.refs
        G, rep, wgv = r.work, r.rep, r.wgv
        cin, cout, tiles = seg.cin, seg.cout, unit.tiles
        width = 3 if seg.taps == 3 else 1
        found = links(self.k, unit, seg)
        off = seg.off

        def fold(d):
            for column in range(width):
                tap = d * width + column
                totals = []
                for tile in range(seg.tiles):
                    total = None
                    for row, which, wanted in found:
                        if which != column:
                            continue
                        at = pl.multiple_of((d * tiles + seg.tile + tile) * unit.rows + row, 8)
                        piece = G[pl.ds(at, cin)]
                        if cout <= LANES:
                            local = self.local_blocks(seg, tile, wanted)
                            if not local:
                                continue
                            piece = self.keep(piece, cout, local)
                        total = piece if total is None else total + piece
                    totals.append(total)
                if cout > LANES:
                    for tile in range(2):
                        wgv[pl.ds(off + tap * (2 * cin) + tile, cin, stride=2)] = totals[tile]
                    continue
                total = None
                for piece in totals:
                    if piece is not None:
                        total = piece if total is None else total + piece
                if cout == LANES:
                    wgv[pl.ds(pl.multiple_of(off + tap * cin, 8), cin)] = total
                else:
                    rep[pl.ds(pl.multiple_of(tap * cin, cin), cin)] = self.spread(total, cout)

        planes_loop(unit.depth, fold)
        if cout < LANES:
            ratio = LANES // cout
            count = width * width * cin // ratio
            total = None
            for part in range(ratio):
                piece = self.keep(rep[pl.ds(part, count, stride=ratio)], cout, [part])
                total = piece if total is None else total + piece
            wgv[off : off + count] = total

    def backward(self, m, meanwhile):
        e = MODULES + m
        last = m == MODULES - 1
        self.sent(jnp.where(last, m, e + 1))
        self.send_back(m)
        pl.when(last)(meanwhile)
        for name in ("g", "f", "e", "d", "u"):
            if name in self.units:
                for seg in self.units[name].segs:
                    if seg.dest >= 0:
                        self.arrived(e, seg.dest).wait_recv()
                self.back_unit(m, self.units[name])
        self.back_unit(m, self.units["b"])
        self.back_unit(m, self.units["a"])


STATS = 20
TURNS = 1
NAMES = list(
    dict(x=0, cot=0, w=0, gains=0, shifts=0, kinds=0, out=0, grad=0, wg=0, gain=0, shift=0)
)


def one_hot(goal, lane, deep):
    pieces = [
        jnp.where(goal == lane + first, 1.0, 0.0).astype(jnp.bfloat16)
        for first in range(0, deep, LANES)
    ]
    return jnp.concatenate(pieces, axis=1)


class Cells:
    def __init__(self, core, shape, small, large):
        self.core = core
        row = lax.broadcasted_iota(jnp.int32, shape, 0)
        self.wide = self.pick(LW // 8, SW // 8)
        tall = self.pick(LH // 8, SH // 8)
        self.crop = self.pick((row * 43691) >> 21, (row * 43691) >> 19)
        inner = row - self.crop * (self.wide * tall)
        self.along = self.pick((inner * 43691) >> 18, (inner * 43691) >> 17)
        self.across = inner - self.along * self.wide
        self.valid = self.crop < self.pick(large, small)
        self.last = tall - 1

    def pick(self, large, small):
        return jnp.where(self.core == 0, large, small)


def fill_masks(refs, rows, core, small, large):
    cells = Cells(core, (rows, LANES), small, large)
    valid = cells.valid
    six = cells.wide == 6
    up, down = valid & (cells.along > 0), valid & (cells.along < cells.last)
    tables = (
        valid,
        valid & (cells.across > 0),
        valid & (cells.across < cells.wide - 1),
        up & six,
        up & jnp.logical_not(six),
        down & six,
        down & jnp.logical_not(six),
    )
    for at, table in enumerate(tables):
        refs.masks[at] = jnp.where(table, 1.0, 0.0)


class Gather:
    def __init__(self, refs, core, count):
        self.refs, self.core, self.count = refs, core, count
        self.z = lax.axis_index("crops") // 2
        self.last = count // 2 - 1

    def hop(self, t, source, right):
        r = self.refs
        at = source * 2 + self.core
        gath = r.gathc if t else r.gathx
        to = self.z + 1 if right else self.z - 1
        return pltpu.make_async_remote_copy(
            src_ref=gath.at[at],
            dst_ref=gath.at[at],
            send_sem=r.hsem.at[(t * (self.last + 1) + source) * 3 + (0 if right else 1)],
            recv_sem=r.gsem.at[t * self.count + at],
            device_id=dict(crops=to * 2 + self.core),
            device_id_type=pl.DeviceIdType.MESH,
        )

    def across(self, t, source, core, rows):
        r = self.refs
        at = source * 2 + core
        gath = r.gathc if t else r.gathx
        return pltpu.make_async_remote_copy(
            src_ref=gath.at[at, pl.ds(0, rows)],
            dst_ref=gath.at[at, pl.ds(0, rows)],
            send_sem=r.hsem.at[(t * (self.last + 1) + source) * 3 + 2],
            recv_sem=r.gsem.at[t * self.count + at],
            device_id=dict(crops=self.z * 2 + 1 - self.core),
            device_id_type=pl.DeviceIdType.MESH,
        )

    def each_core(self, action):
        for core, rows in ((0, SH * SW * C0 // LANES), (1, ROWS)):

            @pl.when(self.core == core)
            def _():
                action(core, rows)

    def send(self, t, source, rightward, leftward):
        if rightward:

            @pl.when(self.z < self.last)
            def _():
                self.hop(t, source, True).start()

        if leftward:

            @pl.when(self.z > 0)
            def _():
                self.hop(t, source, False).start()

        self.each_core(lambda core, rows: self.across(t, source, core, rows).start())

    def step(self, t, s):
        r = self.refs
        if s == 0:
            at = self.z * 2 + self.core
            if t:
                r.gathc[at] = r.cot[...]
            else:
                r.gathx[at] = r.x[...]
            self.send(t, self.z, True, True)
            return

        @pl.when(self.z >= s)
        def _():
            self.hop(t, self.z - s, True).wait_recv()
            self.send(t, self.z - s, True, False)

        @pl.when(self.z + s <= self.last)
        def _():
            self.hop(t, self.z + s, True).wait_recv()
            self.send(t, self.z + s, False, True)

    def collect(self, t):
        for source in range(self.last + 1):
            for core, rows in ((0, ROWS), (1, SH * SW * C0 // LANES)):

                @pl.when(self.core == core)
                def _():
                    self.across(t, source, 1 - core, rows).wait_recv()

    def finish(self, t):
        def sent(source, rightward, leftward):
            if rightward:

                @pl.when(self.z < self.last)
                def _():
                    self.hop(t, source, True).wait_send()

            if leftward:

                @pl.when(self.z > 0)
                def _():
                    self.hop(t, source, False).wait_send()

            self.each_core(lambda core, rows: self.across(t, source, core, rows).wait_send())

        sent(self.z, True, True)
        for s in range(1, self.last + 1):

            @pl.when(self.z >= s)
            def _():
                sent(self.z - s, True, False)

            @pl.when(self.z + s <= self.last)
            def _():
                sent(self.z + s, False, True)


def scratch_table(rows, weight_rows, count):
    def half(many):
        return pltpu.VMEM((many, rows, LANES), jnp.bfloat16)

    def full(many):
        return pltpu.VMEM((many, rows, LANES), jnp.float32)

    def expanded(depth, deep, wide):
        return pltpu.VMEM((MODULES * depth, deep, wide), jnp.bfloat16)

    _, span, _ = pair_rows(weight_rows, count)
    return dict(
        masks=full(MASKS),
        hC=half(2 * 20),
        hE=half(2 * 10),
        hR=half(2 * 6),
        uC=half(2 * 20),
        uE=half(2 * 10),
        uR=half(2 * 6),
        tC=half(2 * 18),
        tE=half(2 * 9),
        c1C=half(2 * 5),
        c1E=half(2 * 5),
        c2C=half(2 * 5),
        c2E=half(2 * 5),
        c3C=half(2 * 3),
        c3E=half(2 * 3),
        dC=half(20),
        dE=half(20),
        dR=half(6),
        outs=half(16),
        hf=full(2 * 16),
        s=full(2 * 16),
        za=full(2 * 16),
        zb=full(2 * 16),
        zd=full(2 * 16),
        zu=full(2 * 8),
        ze=full(2 * 4),
        zf=full(2 * 2),
        zg=full(2 * 2),
        gt=full(16),
        gu=full(16),
        gin=full(16),
        gc1=full(4),
        gc2=full(4),
        gc3=full(2),
        dyb=full(16),
        sb=half(16),
        rb=half(4 * 16),
        st=pltpu.VMEM((MODULES * STATS, 8, LANES), jnp.float32),
        Ta=expanded(3, 768, 256),
        Tb=expanded(3, 768, 256),
        Taa=expanded(3, 512, 256),
        Tbb=expanded(3, 512, 256),
        Td=expanded(3, 384, 512),
        Tu=expanded(1, 256, 768),
        Te=expanded(3, 256, 256),
        Tf=expanded(3, 256, 128),
        Tg=expanded(3, 256, 256),
        raw=pltpu.VMEM((9408, LANES), jnp.bfloat16),
        work=pltpu.VMEM((4608, LANES), jnp.float32),
        rep=pltpu.VMEM((640, LANES), jnp.float32),
        wgv=pltpu.VMEM((weight_rows, LANES), jnp.float32),
        wq=pltpu.VMEM((MODULES, 2 * weight_rows // count, LANES), jnp.float32),
        wr=pltpu.VMEM((MODULES, span, LANES), jnp.float32),
        gathx=pltpu.VMEM((count, ROWS, LANES), jnp.bfloat16),
        gathc=pltpu.VMEM((count, ROWS, LANES), jnp.bfloat16),
        hot=pltpu.VMEM((2, 384, 768), jnp.bfloat16),
        blocks=pltpu.VMEM((2, ROWS, LANES), jnp.bfloat16),
        slopes=pltpu.VMEM((2, ROWS, LANES), jnp.float32),
        blockr=pltpu.VMEM((ROWS, LANES), jnp.bfloat16),
        sloper=pltpu.VMEM((ROWS, LANES), jnp.float32),
        gg=pltpu.VMEM((MODULES, 2, SLOTS, 256), jnp.float32),
        ggr=pltpu.VMEM((MODULES, 2, SLOTS, 256), jnp.float32),
        wsem=pltpu.SemaphoreType.DMA((8,)),
        ssem=pltpu.SemaphoreType.DMA((16,)),
        rsem=pltpu.SemaphoreType.DMA((16,)),
        hsem=pltpu.SemaphoreType.DMA((3 * count,)),
        gsem=pltpu.SemaphoreType.DMA((2 * count,)),
        psem=pltpu.SemaphoreType.DMA((5,)),
        qsem=pltpu.SemaphoreType.DMA((5,)),
        osem=pltpu.SemaphoreType.DMA((1,)),
    )


def pair_rows(weight_rows, count):
    share = weight_rows // count
    low = share // 8 * 8
    return share, 2 * share - low, low


def greet(core, count):
    barrier = pltpu.get_barrier_semaphore()
    me, shard = lax.axis_index("branch"), lax.axis_index("crops")
    z = shard // 2

    def signal(**where):
        pl.semaphore_signal(barrier, inc=1, device_id=where, device_id_type=pl.DeviceIdType.MESH)

    for step in range(1, 4):
        signal(branch=lax.rem(me + step, 4))
    signal(crops=shard + 1 - 2 * core)

    @pl.when(z > 0)
    def _():
        signal(crops=shard - 2)

    @pl.when(z < count // 2 - 1)
    def _():
        signal(crops=shard + 2)

    ends = (z == 0).astype(jnp.int32) + (z == count // 2 - 1).astype(jnp.int32)
    pl.semaphore_wait(barrier, 6 - ends)


def whole_kernel(names, rows, large, small, *args):
    refs = SimpleNamespace(**dict(zip(names, args)))
    count = large + small
    me, shard = lax.axis_index("branch"), lax.axis_index("crops")
    core = shard % 2
    weight_rows = refs.wgv.shape[0]
    share, span, low = pair_rows(weight_rows, count)
    quarter = pl.multiple_of(shard // 2 * (2 * share), 8)

    class Lazy:
        def __getitem__(self, index):
            return refs.masks[index]

    def across(source, goal, index):
        return pltpu.make_async_remote_copy(
            src_ref=source,
            dst_ref=goal,
            send_sem=refs.psem.at[index],
            recv_sem=refs.qsem.at[index],
            device_id=dict(crops=shard + 1 - 2 * core),
            device_id_type=pl.DeviceIdType.MESH,
        )

    def kernel_pair(m):
        at = pl.multiple_of(low * (1 - core), 8)
        return across(refs.wq.at[m, pl.ds(at, span)], refs.wr.at[m], m)

    outputs_pair = across(refs.blocks.at[1], refs.blockr, 2)
    gradient_pair = across(refs.slopes.at[1], refs.sloper, 3)
    table_pair = across(refs.gg, refs.ggr, 4)
    gather = Gather(refs, core, count)

    def every(action):
        for k in range(4):

            @pl.when(me == k)
            def _():
                action(Branch(k, rows, large, small, 2 * share, refs, Lazy(), core))

    def begin(branch):
        branch.fetch_first()

    def prepare(branch):
        found = branch.segments()
        stops = {0: 1, min(2, len(found) - 2): 2, len(found) - 1: 3}
        for index, (unit, seg) in enumerate(found):
            branch.expand(index)
            if index in stops:
                gather.step(0, stops[index])

    def main(branch):
        branch.unpack(0, branch.take_feature)
        branch.maps["h"].close(0)
        gather.step(1, 0)

        def ahead(m, carry):
            branch.forward(m, gather)
            return carry

        def meanwhile():
            branch.plan_pack()
            branch.pack_outputs()
            outputs_pair.start()

        def back(step, carry):
            m = MODULES - 1 - step
            branch.backward(m, meanwhile)
            refs.wq[m] = refs.wgv[pl.ds(quarter, 2 * share)]
            kernel_pair(m).start()
            return carry

        lax.fori_loop(0, MODULES, ahead, 0)
        lax.fori_loop(0, MODULES, back, 0)
        branch.sent(MODULES)
        branch.pack_gradient()
        gradient_pair.start()
        table_pair.start()

    every(begin)
    greet(core, count)
    gather.step(0, 0)
    fill_masks(refs, rows, core, small, large)
    refs.wgv[pl.ds(quarter, 2 * share)] = jnp.zeros((2 * share, LANES), jnp.float32)
    refs.gg[...] = jnp.zeros(refs.gg.shape, jnp.float32)
    every(prepare)
    gather.collect(0)
    every(main)

    for step in range(MODULES):
        m = MODULES - 1 - step
        kernel_pair(m).wait()
        mine = refs.wq[m, pl.ds(pl.multiple_of(low * core, 8), span)]
        refs.work[pl.ds(m, span, stride=MODULES)] = mine + refs.wr[m]
    skip = pl.multiple_of(core * (MODULES * (share - low)), 8)
    leave = pltpu.make_async_copy(
        refs.work.at[pl.ds(skip, MODULES * share)], refs.wg, refs.osem.at[0]
    )
    leave.start()
    outputs_pair.wait()
    gradient_pair.wait()
    table_pair.wait()
    own = refs.kinds[shard] != core
    refs.out[...] = jnp.where(own, refs.blocks[0].astype(jnp.float32), refs.blockr[...].astype(jnp.float32)).astype(jnp.bfloat16)
    refs.grad[...] = jnp.where(own, refs.slopes[0], refs.sloper[...])
    width = 256 // count
    for which, goal in ((0, refs.gain), (1, refs.shift)):
        for m in range(MODULES):
            total = refs.gg[m, which] + refs.ggr[m, which]
            found = None
            for at in range(count):
                piece = jnp.where(shard == at, total[:, at * width : (at + 1) * width], 0.0)
                found = piece if found is None else found + piece
            goal[m] = found
    gather.finish(0)
    gather.finish(1)
    leave.wait()


def whole_call(rows, large, small, x, cot, w, gains, shifts, kinds):
    count = large + small
    weight_rows = w.shape[0] // MODULES
    table = scratch_table(rows, weight_rows, count)
    vmem = pl.BlockSpec(memory_space=pltpu.VMEM)
    hbm = pl.BlockSpec(memory_space=pl.ANY)
    smem = pl.BlockSpec(memory_space=pltpu.SMEM)
    tables = jax.ShapeDtypeStruct((MODULES, SLOTS, 256 // count), jnp.float32)
    return pl.pallas_call(
        partial(whole_kernel, NAMES + list(table), rows, large, small),
        out_shape=(
            jax.ShapeDtypeStruct((ROWS, LANES), jnp.bfloat16),
            jax.ShapeDtypeStruct((ROWS, LANES), jnp.float32),
            jax.ShapeDtypeStruct((MODULES * weight_rows // count, LANES), jnp.float32),
            tables,
            tables,
        ),
        in_specs=[vmem, vmem, hbm, vmem, vmem, smem],
        out_specs=(vmem, vmem, hbm, vmem, vmem),
        scratch_shapes=list(table.values()),
        compiler_params=pltpu.CompilerParams(
            collective_id=0, has_side_effects=True, vmem_limit_bytes=62 * 1024 * 1024
        ),
    )(x, cot, w, gains, shifts, kinds)


def leave_kernel(*refs):
    for source, goal in zip(refs[:5], refs[5:]):
        goal[...] = source[...]


def leave_call(arrays):
    vmem = pl.BlockSpec(memory_space=pltpu.VMEM)
    return pl.pallas_call(
        leave_kernel,
        out_shape=tuple(jax.ShapeDtypeStruct(array.shape, array.dtype) for array in arrays),
        in_specs=[vmem] * 5,
        out_specs=(vmem,) * 5,
    )(*arrays)


def on_device_grouped(features, weights, gains, shifts, cotangent, size_group):
    count = lax.axis_size("crops")
    large = count // 4
    weight_rows = weights.shape[2] // LANES
    results = whole_call(
        group_rows(count),
        large,
        count - large,
        features[0],
        cotangent[0],
        weights[0]
        .reshape(MODULES, weight_rows, LANES)
        .transpose(1, 0, 2)
        .reshape(MODULES * weight_rows, LANES),
        gains[0],
        shifts[0],
        size_group,
    )
    out, grad, weight_grad, gain, shift = leave_call(results)
    share = weight_rows // count
    weight_grad = weight_grad.reshape(share, MODULES, LANES).transpose(1, 0, 2)
    weight_grad = with_layout_constraint(weight_grad, Layout((1, 0, 2)))
    return (
        out[None],
        grad[None],
        weight_grad.reshape(1, MODULES, share * LANES),
        gain[None],
        shift[None],
    )


def group_rows(count):
    large = count // 4
    rows = max(large * (LH // 8) * (LW // 8), (count - large) * (SH // 8) * (SW // 8))
    return -(-rows // 16) * 16


def fits(count):
    return count % 8 == 0 and group_rows(count) <= 96


def solution(mesh):
    placed = (
        P("branch", "crops", None),
        P("branch", None, None),
        P("branch", None, None, None),
        P("branch", None, None, None),
        P("branch", "crops", None),
        P(),
    )
    return jax.shard_map(
        on_device_grouped if fits(mesh.shape["crops"]) else on_device,
        mesh=mesh,
        in_specs=placed,
        out_specs=(
            P("branch", "crops", None),
            P("branch", "crops", None),
            P("branch", None, "crops"),
            P("branch", None, None, "crops"),
            P("branch", None, None, "crops"),
        ),
        check_vma=False,
    )
```

```python
from functools import partial
from types import SimpleNamespace
import math

import jax
import jax.numpy as jnp
import numpy as np
from jax import lax
from jax.experimental import pallas as pl
from jax.experimental.layout import Layout, with_layout_constraint
from jax.experimental.pallas import tpu as pltpu
from jax.sharding import PartitionSpec as P

C0 = 32
BLOCKS = 1
MODULES = 2
CROPS_DEV = 1
SH = 32
SW = 24
LH = 64
LW = 48
ROWS = 768
MSG_ROWS = 384


EPS = 1e-05


def as_sent(x):

    def short(part):
        return part.astype(jnp.bfloat16) if part.dtype == jnp.float32 else part

    return jax.tree.map(short, x)


def sender_plan(branch_index, top_channels, blocks):
    channels = top_channels << branch_index
    operations = []
    for block_index in range(blocks):
        operations.append(
            SimpleNamespace(
                phase=2 * block_index,
                source=("h", block_index),
                level=branch_index,
                cin=channels,
                cout=channels,
                stride=1,
                taps=3,
                act="silu",
                output=("u", block_index),
                skip=None,
                dest=-1,
            )
        )
        operations.append(
            SimpleNamespace(
                phase=2 * block_index + 1,
                source=("u", block_index),
                level=branch_index,
                cin=channels,
                cout=channels,
                stride=1,
                taps=3,
                act="res",
                output=("h", block_index + 1),
                skip=("h", block_index),
                dest=-1,
            )
        )
    top_name = ("h", blocks)
    for target in range(branch_index):
        operations.append(
            SimpleNamespace(
                phase=2 * blocks,
                source=top_name,
                level=branch_index,
                cin=channels,
                cout=top_channels << target,
                stride=1,
                taps=1,
                act="none",
                output=None,
                skip=None,
                dest=target,
            )
        )
    for target in range(branch_index + 1, 4):
        for depth_step in range(1, target - branch_index + 1):
            is_last = depth_step == target - branch_index
            operations.append(
                SimpleNamespace(
                    phase=2 * blocks + depth_step - 1,
                    source=top_name if depth_step == 1 else ("chain", target, depth_step - 1),
                    level=branch_index + depth_step,
                    cin=channels,
                    cout=top_channels << target if is_last else channels,
                    stride=2,
                    taps=3,
                    act="none" if is_last else "silu",
                    output=None if is_last else ("chain", target, depth_step),
                    skip=None,
                    dest=target if is_last else -1,
                )
            )
    for position, operation in enumerate(operations):
        operation.slot = position
        operation.size = (
            operation.taps * operation.taps * operation.cin * operation.cout
        )
        if operation.taps == 1:
            operation.kshape = (operation.cin, operation.cout)
        else:
            operation.kshape = (3, 3, operation.cin, operation.cout)
    return operations


def phase_lengths(top_channels, blocks):
    phase_count = 2 * blocks + 3
    lengths = [0] * phase_count
    for branch_index in range(4):
        per_phase = [0] * phase_count
        for operation in sender_plan(branch_index, top_channels, blocks):
            per_phase[operation.phase] += operation.size
        lengths = [max(current, candidate) for current, candidate in zip(lengths, per_phase)]
    return lengths


def weighted_plan(branch_index, top_channels, blocks):
    lengths = phase_lengths(top_channels, blocks)
    starts = [sum(lengths[:phase_index]) for phase_index in range(len(lengths))]
    running = [0] * len(lengths)
    operations = sender_plan(branch_index, top_channels, blocks)
    for operation in operations:
        phase_index = operation.phase
        operation.inner = running[phase_index]
        operation.offset = starts[phase_index] + running[phase_index]
        operation.position = sum(
            (1 for earlier in operations[: operation.slot] if earlier.phase == phase_index)
        )
        running[phase_index] += operation.size
    return operations


def phase_operations(branch_index, phase_index):
    return [
        operation
        for operation in weighted_plan(branch_index, C0, BLOCKS)
        if operation.phase == phase_index
    ]


def input_names(operations):
    source_names = []
    for operation in operations:
        if operation.source not in source_names:
            source_names.append(operation.source)
    return source_names


def silu_slope(value):
    sigmoid = jax.nn.sigmoid(value)
    return sigmoid * (1.0 + value * (1.0 - sigmoid))


def crop_cells(size_kind):
    return (LH, LW) if size_kind else (SH, SW)


def map_dims(size_kind, level, channels):
    height, breadth = crop_cells(size_kind)
    return (CROPS_DEV, height >> level, breadth >> level, channels)


def source_dims(branch_index, size_kind, map_name):
    level = branch_index + map_name[2] if map_name[0] == "chain" else branch_index
    return map_dims(size_kind, level, C0 << branch_index)


def preact_dims(size_kind, operation):
    return map_dims(size_kind, operation.level, operation.cout)


def to_canvas(arrays, value_type):
    if not arrays:
        return jnp.zeros((ROWS, 128), value_type)
    flattened = jnp.concatenate([array.reshape(-1).astype(value_type) for array in arrays])
    return jnp.pad(flattened, (0, ROWS * 128 - flattened.shape[0])).reshape(ROWS, 128)


def from_canvas(canvas, dims_list):
    flattened = canvas.reshape(-1)
    pieces = []
    offset = 0
    for dims_entry in dims_list:
        count_here = math.prod(dims_entry)
        pieces.append(flattened[offset : offset + count_here].reshape(dims_entry))
        offset += count_here
    return pieces


def to_slot(array):
    flattened = array.reshape(-1)
    return jnp.pad(flattened, (0, MSG_ROWS * 128 - flattened.shape[0])).reshape(MSG_ROWS, 128)


def from_slot(slot_rows, dims_entry):
    return slot_rows.reshape(-1)[: math.prod(dims_entry)].reshape(dims_entry)


def upsample(message, factor):
    crop_count, height, breadth, channels = message.shape
    widened = jnp.broadcast_to(
        message[:, :, None, :, None, :], (crop_count, height, factor, breadth, factor, channels)
    )
    return widened.reshape(crop_count, height * factor, breadth * factor, channels)


def block_pool(array, factor):
    crop_count, height, breadth, channels = array.shape
    return array.reshape(
        crop_count, height // factor, factor, breadth // factor, factor, channels
    ).sum(axis=(2, 4))


def kernel_piece(module_weights, operation):
    start = operation.offset
    return module_weights[start : start + operation.size].reshape(operation.kshape)


def conv_forward(operation, source, kernel):
    if operation.taps == 1:
        return jnp.einsum("nhwc,cd->nhwd", source, kernel, preferred_element_type=jnp.float32)
    stride = operation.stride
    return lax.conv_general_dilated(
        source,
        kernel,
        (stride, stride),
        ((1, 1), (1, 1)),
        dimension_numbers=("NHWC", "HWIO", "NHWC"),
        preferred_element_type=jnp.float32,
    )


def conv_backward(operation, source, kernel, upstream):
    if operation.taps == 1:
        source_grad = jnp.einsum(
            "nhwd,cd->nhwc", upstream, kernel, preferred_element_type=jnp.float32
        )
        kernel_grad = jnp.einsum(
            "nhwc,nhwd->cd", source, upstream, preferred_element_type=jnp.float32
        )
        return (source_grad, kernel_grad)
    stride = operation.stride
    flipped = jnp.transpose(kernel[::-1, ::-1], (0, 1, 3, 2))
    high_pad = 2 if stride == 2 else 1
    source_grad = lax.conv_general_dilated(
        upstream,
        flipped,
        (1, 1),
        ((1, high_pad), (1, high_pad)),
        lhs_dilation=(stride, stride),
        dimension_numbers=("NHWC", "HWIO", "NHWC"),
        preferred_element_type=jnp.float32,
    )
    kernel_grad = lax.conv_general_dilated(
        source,
        upstream,
        (1, 1),
        ((1, 2 - stride), (1, 2 - stride)),
        rhs_dilation=(stride, stride),
        dimension_numbers=("CHWN", "IHWO", "NHWC"),
        preferred_element_type=jnp.float32,
    )
    return (source_grad, jnp.transpose(kernel_grad, (1, 2, 0, 3)))


def cell_total(counts, size_kind, level):
    height, breadth = crop_cells(size_kind)
    return counts[size_kind] * float(CROPS_DEV * (height >> level) * (breadth >> level))


def norm_terms(totals, counts, size_kind, operation):
    cells_here = cell_total(counts, size_kind, operation.level)
    channels = operation.cout
    position = operation.position
    average = totals[size_kind, 0, position, :channels] / cells_here
    variance = totals[size_kind, 1, position, :channels] / cells_here - average * average
    return (average, lax.rsqrt(variance + EPS))


def forward_conv(branch_index, size_kind, phase_index, source_canvas, module_weights):
    operations = phase_operations(branch_index, phase_index)
    source_names = input_names(operations)
    pieces = from_canvas(
        source_canvas, [source_dims(branch_index, size_kind, map_name) for map_name in source_names]
    )
    sources = {
        map_name: piece.astype(jnp.bfloat16) for map_name, piece in zip(source_names, pieces)
    }
    preacts = []
    totals = jnp.zeros((2, 2, 3, 8 * C0), jnp.float32)
    for operation in operations:
        preact = conv_forward(
            operation, sources[operation.source], kernel_piece(module_weights, operation)
        )
        preacts.append(preact)
        channels = operation.cout
        position = operation.position
        totals = totals.at[size_kind, 0, position, :channels].set(jnp.sum(preact, axis=(0, 1, 2)))
        totals = totals.at[size_kind, 1, position, :channels].set(
            jnp.sum(preact * preact, axis=(0, 1, 2))
        )
    return (to_canvas(preacts, jnp.float32), totals)


def forward_norm(
    branch_index,
    size_kind,
    phase_index,
    preact_canvas,
    totals,
    counts,
    module_gains,
    module_shifts,
    skip_canvas,
    message_buffer,
):
    operations = phase_operations(branch_index, phase_index)
    preacts = from_canvas(
        preact_canvas, [preact_dims(size_kind, operation) for operation in operations]
    )
    skip_map = from_canvas(skip_canvas, [map_dims(size_kind, branch_index, C0 << branch_index)])[0]
    produced = []
    for operation, preact in zip(operations, preacts):
        average, inverse_std = norm_terms(totals, counts, size_kind, operation)
        norm_slot = operation.slot
        channels = operation.cout
        normed = (preact - average) * inverse_std * module_gains[
            norm_slot, :channels
        ] + module_shifts[norm_slot, :channels]
        if operation.act == "silu":
            produced.append(jax.nn.silu(normed))
        elif operation.act == "res":
            produced.append(jax.nn.silu(normed + skip_map))
        else:
            message_buffer = message_buffer.at[operation.dest].set(
                to_slot(normed.astype(jnp.bfloat16))
            )
    return (to_canvas(produced, jnp.float32), message_buffer)


def receive_forward(branch_index, size_kind, top_canvas, received):
    channels = C0 << branch_index
    summed = from_canvas(top_canvas, [map_dims(size_kind, branch_index, channels)])[0]
    for sender in range(4):
        if sender < branch_index:
            summed = summed + from_slot(
                received[sender], map_dims(size_kind, branch_index, channels)
            ).astype(jnp.float32)
        elif sender > branch_index:
            coarse = from_slot(received[sender], map_dims(size_kind, sender, channels))
            summed = summed + upsample(coarse, 2 ** (sender - branch_index)).astype(jnp.float32)
    return (to_canvas([jax.nn.silu(summed)], jnp.float32), to_canvas([summed], jnp.float32))


def receive_backward(branch_index, size_kind, grad_canvas, summed_canvas):
    dims_here = map_dims(size_kind, branch_index, C0 << branch_index)
    upstream = from_canvas(grad_canvas, [dims_here])[0]
    summed = from_canvas(summed_canvas, [dims_here])[0]
    summed_grad = upstream * silu_slope(summed)
    buffer = jnp.zeros((4, MSG_ROWS, 128), jnp.bfloat16)
    for sender in range(4):
        if sender < branch_index:
            buffer = buffer.at[sender].set(to_slot(summed_grad.astype(jnp.bfloat16)))
        elif sender > branch_index:
            pooled = block_pool(summed_grad, 2 ** (sender - branch_index))
            buffer = buffer.at[sender].set(to_slot(pooled.astype(jnp.bfloat16)))
    return (to_canvas([summed_grad], jnp.float32), buffer)


def backward_stats(
    branch_index,
    size_kind,
    phase_index,
    dout_canvas,
    message_grads,
    preact_canvas,
    totals,
    counts,
    module_gains,
    module_shifts,
    skip_canvas,
):
    operations = phase_operations(branch_index, phase_index)
    preacts = from_canvas(
        preact_canvas, [preact_dims(size_kind, operation) for operation in operations]
    )
    producing = [operation for operation in operations if operation.act != "none"]
    output_grads = from_canvas(
        dout_canvas, [preact_dims(size_kind, operation) for operation in producing]
    )
    grads_by_name = {
        operation.output: piece for operation, piece in zip(producing, output_grads)
    }
    skip_map = from_canvas(skip_canvas, [map_dims(size_kind, branch_index, C0 << branch_index)])[0]
    upstreams = []
    skip_grads = []
    sums_local = jnp.zeros((2, 2, 3, 8 * C0), jnp.float32)
    for operation, preact in zip(operations, preacts):
        average, inverse_std = norm_terms(totals, counts, size_kind, operation)
        norm_slot = operation.slot
        channels = operation.cout
        centered = (preact - average) * inverse_std
        normed = centered * module_gains[norm_slot, :channels] + module_shifts[norm_slot, :channels]
        if operation.act == "silu":
            upstream = grads_by_name[operation.output] * silu_slope(normed)
        elif operation.act == "res":
            upstream = grads_by_name[operation.output] * silu_slope(normed + skip_map)
            skip_grads.append(upstream)
        else:
            upstream = from_slot(
                message_grads[operation.dest], preact_dims(size_kind, operation)
            ).astype(jnp.float32)
        upstreams.append(upstream)
        position = operation.position
        sums_local = sums_local.at[size_kind, 0, position, :channels].set(
            jnp.sum(upstream, axis=(0, 1, 2))
        )
        sums_local = sums_local.at[size_kind, 1, position, :channels].set(
            jnp.sum(upstream * centered, axis=(0, 1, 2))
        )
    return (to_canvas(upstreams, jnp.float32), sums_local, to_canvas(skip_grads, jnp.float32))


def backward_apply(
    branch_index,
    size_kind,
    phase_index,
    upstream_canvas,
    preact_canvas,
    totals,
    grad_totals,
    counts,
    source_canvas,
    module_weights,
    module_gains,
):
    operations = phase_operations(branch_index, phase_index)
    preacts = from_canvas(
        preact_canvas, [preact_dims(size_kind, operation) for operation in operations]
    )
    upstreams = from_canvas(
        upstream_canvas, [preact_dims(size_kind, operation) for operation in operations]
    )
    source_names = input_names(operations)
    source_list = [source_dims(branch_index, size_kind, map_name) for map_name in source_names]
    pieces = from_canvas(source_canvas, source_list)
    sources = {
        map_name: piece.astype(jnp.bfloat16) for map_name, piece in zip(source_names, pieces)
    }
    source_grads = {
        map_name: jnp.zeros(dims_entry, jnp.float32)
        for map_name, dims_entry in zip(source_names, source_list)
    }
    kernel_grads = []
    slot_count = module_gains.shape[0]
    gain_part = jnp.zeros((slot_count, 8 * C0), jnp.float32)
    shift_part = jnp.zeros((slot_count, 8 * C0), jnp.float32)
    for operation, preact, upstream in zip(operations, preacts, upstreams):
        average, inverse_std = norm_terms(totals, counts, size_kind, operation)
        cells_here = cell_total(counts, size_kind, operation.level)
        norm_slot = operation.slot
        channels = operation.cout
        position = operation.position
        centered = (preact - average) * inverse_std
        mean_upstream = grad_totals[size_kind, 0, position, :channels] / cells_here
        mean_cross = grad_totals[size_kind, 1, position, :channels] / cells_here
        preact_grad = (
            module_gains[norm_slot, :channels]
            * inverse_std
            * (upstream - mean_upstream - centered * mean_cross)
        )
        source_grad, kernel_grad = conv_backward(
            operation,
            sources[operation.source],
            kernel_piece(module_weights, operation),
            preact_grad.astype(jnp.bfloat16),
        )
        source_grads[operation.source] = source_grads[operation.source] + source_grad
        kernel_grads.append(kernel_grad.reshape(-1))
        gain_part = gain_part.at[norm_slot, :channels].set(
            grad_totals[0, 1, position, :channels] + grad_totals[1, 1, position, :channels]
        )
        shift_part = shift_part.at[norm_slot, :channels].set(
            grad_totals[0, 0, position, :channels] + grad_totals[1, 0, position, :channels]
        )
    phase_length = phase_lengths(C0, BLOCKS)[phase_index]
    if kernel_grads:
        joined = jnp.concatenate(kernel_grads)
        weight_part = jnp.pad(joined, (0, phase_length - joined.shape[0]))
    else:
        weight_part = jnp.zeros((phase_length,), jnp.float32)
    return (
        to_canvas([source_grads[map_name] for map_name in source_names], jnp.float32),
        weight_part,
        gain_part,
        shift_part,
    )


def on_device(features, weights, gains, shifts, cotangent, size_group):
    crop_shard = lax.axis_index("crops")
    shard_count = lax.axis_size("crops")
    crop_kind = size_group[crop_shard]
    large_count = jnp.sum(size_group).astype(jnp.float32)
    counts = jnp.stack([shard_count - large_count, large_count])
    case_index = lax.axis_index("branch") * 2 + crop_kind
    phase_total = 2 * BLOCKS + 3
    zero_canvas = jnp.zeros((ROWS, 128), jnp.float32)
    empty_buffer = jnp.zeros((4, MSG_ROWS, 128), jnp.bfloat16)

    def run_phase(function, statics, operands):
        branches_list = [
            partial(function, branch_index, size_kind, *statics)
            for branch_index in range(4)
            for size_kind in range(2)
        ]
        return lax.switch(case_index, branches_list, *operands)

    def statistics(local_totals):
        return lax.psum(local_totals, "crops")

    def module_forward(module, start_canvas, kept):
        module_weights = weights[0, module]
        module_gains = gains[0, module]
        module_shifts = shifts[0, module]
        record = SimpleNamespace(sources=[], preacts=[], totals=[])
        h_canvas = start_canvas
        u_canvas = zero_canvas
        chain_canvas = zero_canvas
        buffer = empty_buffer
        for phase_index in range(phase_total):
            if phase_index < 2 * BLOCKS:
                source = h_canvas if phase_index % 2 == 0 else u_canvas
            elif phase_index == 2 * BLOCKS:
                source = h_canvas
            else:
                source = chain_canvas
            preact, local_totals = run_phase(forward_conv, (phase_index,), (source, module_weights))
            global_totals = kept.totals[phase_index] if kept else statistics(local_totals)
            produced, buffer = run_phase(
                forward_norm,
                (phase_index,),
                (preact, global_totals, counts, module_gains, module_shifts, h_canvas, buffer),
            )
            record.sources.append(source)
            record.preacts.append(preact)
            record.totals.append(global_totals)
            if phase_index < 2 * BLOCKS:
                if phase_index % 2 == 0:
                    u_canvas = produced
                else:
                    h_canvas = produced
            else:
                chain_canvas = produced
        received = (
            kept.received
            if kept
            else jax.tree.map(
                lambda part, own: part.astype(own.dtype),
                lax.all_to_all(as_sent(buffer), "branch", split_axis=0, concat_axis=0, tiled=True),
                buffer,
            )
        )
        result, summed = run_phase(receive_forward, (), (h_canvas, received))
        record.summed = summed
        record.received = received
        return (result, record)

    checkpoints = [features[0].astype(jnp.float32)]
    first_records = []
    for module in range(MODULES):
        result, record = module_forward(module, checkpoints[-1], None)
        checkpoints.append(result)
        first_records.append(record)
    outputs = checkpoints[-1].astype(jnp.bfloat16)
    grad_canvas = cotangent[0].astype(jnp.float32)
    module_grads = [None] * MODULES
    gain_grads = [None] * MODULES
    shift_grads = [None] * MODULES
    for module in reversed(range(MODULES)):
        kept = None
        unused_result, record = module_forward(module, checkpoints[module], kept)
        module_module_weights = weights[0, module]
        module_module_gains = gains[0, module]
        module_module_shifts = shifts[0, module]
        summed_grad, back_buffer = run_phase(receive_backward, (), (grad_canvas, record.summed))
        message_grads = jax.tree.map(
            lambda part, own: part.astype(own.dtype),
            lax.all_to_all(as_sent(back_buffer), "branch", split_axis=0, concat_axis=0, tiled=True),
            back_buffer,
        )
        top_grad = summed_grad
        chain_grad = zero_canvas
        u_grad = zero_canvas
        pending_skip = zero_canvas
        weight_parts = [None] * phase_total
        gain_total = jnp.zeros(gains.shape[2:], jnp.float32)
        shift_total = jnp.zeros(gains.shape[2:], jnp.float32)
        for module_phase_index in reversed(range(phase_total)):
            if module_phase_index >= 2 * BLOCKS:
                output_grad = chain_grad
                skip_canvas = zero_canvas
            elif module_phase_index % 2 == 1:
                output_grad = top_grad
                skip_canvas = record.sources[module_phase_index - 1]
            else:
                output_grad = u_grad
                skip_canvas = zero_canvas
            module_preact = record.preacts[module_phase_index]
            totals = record.totals[module_phase_index]
            upstream, module_local_totals, skip_grad = run_phase(
                backward_stats,
                (module_phase_index,),
                (
                    output_grad,
                    message_grads,
                    module_preact,
                    totals,
                    counts,
                    module_module_gains,
                    module_module_shifts,
                    skip_canvas,
                ),
            )
            grad_totals = lax.psum(module_local_totals, "crops")
            source_grad, weight_parts[module_phase_index], gain_part, shift_part = run_phase(
                backward_apply,
                (module_phase_index,),
                (
                    upstream,
                    module_preact,
                    totals,
                    grad_totals,
                    counts,
                    record.sources[module_phase_index],
                    module_module_weights,
                    module_module_gains,
                ),
            )
            gain_total = gain_total + gain_part
            shift_total = shift_total + shift_part
            if module_phase_index > 2 * BLOCKS:
                chain_grad = source_grad
            elif module_phase_index == 2 * BLOCKS:
                top_grad = top_grad + source_grad
            elif module_phase_index % 2 == 1:
                u_grad = source_grad
                pending_skip = skip_grad
            else:
                top_grad = source_grad + pending_skip
        joined = jnp.concatenate(weight_parts)
        weight_grad = jnp.pad(joined, (0, weights.shape[2] - joined.shape[0]))
        grad_canvas, weight_grad, gain_grads[module], shift_grads[module] = (
            top_grad,
            weight_grad,
            gain_total,
            shift_total,
        )
        module_grads[module] = weight_grad
    weight_out = lax.psum_scatter(jnp.stack(module_grads), "crops", scatter_dimension=1, tiled=True)
    share = gains.shape[3] // shard_count
    gain_out = lax.dynamic_slice_in_dim(jnp.stack(gain_grads), crop_shard * share, share, axis=2)
    shift_out = lax.dynamic_slice_in_dim(jnp.stack(shift_grads), crop_shard * share, share, axis=2)
    return (outputs[None], grad_canvas[None], weight_out[None], gain_out[None], shift_out[None])


LANES = 128
SLOTS = 8
MASKS = 7
DOWN = (((1,), (0,)), ((), ()))
ACROSS = (((1,), (1,)), ((), ()))
ALONG = (((0,), (0,)), ((), ()))


def unit_table(k):
    operations = weighted_plan(k, C0, BLOCKS)
    planes = 8 >> k
    channels = C0 << k
    units = {}
    stat = 0

    def add(name, kind, source, lanes_in, planes_in, planes_out, members):
        nonlocal stat
        segs = []
        tile = 0
        for operation, lanes, chain in members:
            cout = operation.cout
            level = operation.level if operation.taps == 3 else operation.dest
            segs.append(
                SimpleNamespace(
                    slot=operation.slot,
                    off=operation.offset // LANES,
                    cin=operation.cin,
                    cout=cout,
                    taps=operation.taps,
                    tile=tile,
                    tiles=lanes // LANES,
                    blocks=max(1, (8 >> level)),
                    dest=operation.dest,
                    act=operation.act,
                    chain=chain,
                    up=k - operation.dest if operation.taps == 1 else 0,
                )
            )
            tile += lanes // LANES
        rows = {"s1": (384, 384, 512, 768)[k], "s2": lanes_in + LANES, "p1": 256}[kind]
        units[name] = SimpleNamespace(
            name=name,
            kind=kind,
            source=source,
            lanes_in=lanes_in,
            blocks_in=planes_in,
            planes_in=planes_in,
            planes=planes_out,
            segs=segs,
            tiles=tile,
            rows=rows,
            stat=stat,
            depth=1 if kind == "p1" else 3,
        )
        stat += tile

    add("a", "s1", "h", 256, planes, planes, [(operations[0], 256, None)])
    add("b", "s1", "u", 256, planes, planes, [(operations[1], 256, None)])
    ups = [operation for operation in operations if operation.taps == 1]
    if ups:
        add("u", "p1", "t", 256, planes, planes, [(operation, 256, None) for operation in ups])
    firsts, chains = [], {}
    for target in range(k + 1, 4):
        steps = [
            operation
            for operation in operations
            if operation.taps == 3 and operation.stride == 2
        ]
        start = sum(i - k for i in range(k + 1, target))
        chains[target] = steps[start : start + target - k]
        if target == k + 1:
            firsts.append((chains[target][0], 256, None))
        else:
            firsts.append((chains[target][0], LANES, "c1" if target == k + 2 else "c2"))
    if firsts:
        add("d", "s2", "t", 256, planes, planes // 2, firsts)
    if k <= 1:
        add("e", "s2", "c1", LANES, planes // 2, planes // 4, [(chains[k + 2][1], 256, None)])
    if k == 0:
        add("f", "s2", "c2", LANES, planes // 2, planes // 4, [(chains[3][1], LANES, "c3")])
        add("g", "s2", "c3", LANES, planes // 4, planes // 8, [(chains[3][2], 256, None)])
    return units


def links(k, unit, seg):
    cin = seg.cin
    count_in, count_out = unit.blocks_in, seg.blocks
    found = []
    if unit.kind == "p1":
        for plane in range(count_in):
            wide = 1 << seg.up
            found.append((plane * cin, 0, set(range(plane * wide, plane * wide + wide))))
        return found
    if unit.kind == "s1" and k == 3:
        return [(256 * tap, tap, {0}) for tap in range(3)]
    stride = 1 if unit.kind == "s1" else 2
    for plane in range(count_in):
        for tap in range(3):
            at = plane - tap + 1
            if at % stride == 0 and 0 <= at // stride < count_out:
                found.append((plane * cin, tap, {at // stride}))
    if stride == 1:
        found.append((256, 2, {count_out - 1}))
        found.append((unit.rows - cin, 0, {0}))
    else:
        lanes_in = unit.lanes_in
        found.append((lanes_in + (count_in - 1) * cin - (lanes_in - LANES), 0, {0}))
    return found


def message_slot(k, other):
    return sum(2 * (8 >> max(k, before)) for before in range(other) if before != k)


def log2(value):
    return value.bit_length() - 1


def sigmoid_of(value):
    return 0.5 * jnp.tanh(0.5 * value) + 0.5


def silu_of(value):
    return value * sigmoid_of(value)


def slope_of(value):
    sigmoid = sigmoid_of(value)
    return sigmoid * (1.0 + value * (1.0 - sigmoid))


def planes_loop(count, body, turns=1):
    def step(index, carry):
        for turn in range(turns):
            body(index * turns + turn)
        return carry

    turns = min(turns, count)
    if count == turns:
        for index in range(count):
            body(index)
    else:
        lax.fori_loop(0, count // turns, step, 0)


def planes_sum(count, body, initial, turns=1):
    def step(index, carry):
        for turn in range(turns):
            carry = body(index * turns + turn, carry)
        return carry

    turns = min(turns, count)
    if count == turns:
        return step(0, initial)
    return lax.fori_loop(0, count // turns, step, initial)


def partial_sum(value):
    rows = value.shape[0]
    return jnp.sum(value.reshape(rows // 8, 8, value.shape[1]), axis=0)


class Planes:
    def __init__(self, mode, tiles, planes, masks, rows, main, edge=None, right=None, narrow=False):
        self.narrow, self.pending = narrow, None
        self.mode, self.tiles, self.planes = mode, tiles, planes
        self.masks, self.rows = masks, rows
        self.main, self.edge, self.right = main, edge, right
        self.base = 1 if mode in ("s1", "wide", "s2") else 0
        extra = {"s1": 2, "wide": 2, "s2": 1, "dz2": 1, "p": 0}[mode]
        self.span = planes + extra
        self.unit = tiles * self.span

    def at(self, m, tile, plane):
        return m * self.unit + tile * self.span + plane + self.base

    def edge_at(self, m, tile, plane):
        if self.mode == "s2" or self.narrow:
            return m * self.span + plane + self.base
        return self.at(m, tile, plane)

    def from_left(self, value):
        return pltpu.roll(value, 1, 0) * self.masks[1]

    def from_right(self, value):
        return pltpu.roll(value, self.rows - 1, 0) * self.masks[2]

    def store(self, m, tile, plane, value):
        self.put(m, tile, plane, value)

    def put(self, m, tile, plane, value):
        where = self.at(m, tile, plane)
        self.main[where] = value.astype(jnp.bfloat16)
        if self.mode == "s1":
            side = self.from_right(value) if tile == 0 else self.from_left(value)
            if not self.narrow:
                self.edge[where] = side.astype(jnp.bfloat16)
            elif tile == 0:
                self.pending = side
            else:
                lane = lax.broadcasted_iota(jnp.int32, side.shape, 1)
                side = jnp.where(lane < LANES // 2, self.pending, side)
                self.edge[self.edge_at(m, tile, plane)] = side.astype(jnp.bfloat16)
        elif self.mode == "wide":
            self.edge[where] = self.from_left(value).astype(jnp.bfloat16)
            self.right[where] = self.from_right(value).astype(jnp.bfloat16)
        elif self.mode == "s2":
            if tile == self.tiles - 1:
                self.edge[self.edge_at(m, tile, plane)] = self.from_left(value).astype(jnp.bfloat16)
        elif self.mode == "dz2":
            self.edge[where] = self.from_right(value).astype(jnp.bfloat16)

    def put_above(self, m, tile, last):
        if self.mode in ("s1", "wide", "s2"):
            above = pltpu.roll(last, 6, 0) * self.masks[3] + pltpu.roll(last, 3, 0) * self.masks[4]
            self.put(m, tile, -1, above)

    def put_below(self, m, tile, first):
        if self.mode in ("s1", "wide", "dz2"):
            rows = self.rows
            below = (
                pltpu.roll(first, rows - 6, 0) * self.masks[5]
                + pltpu.roll(first, rows - 3, 0) * self.masks[6]
            )
            self.put(m, tile, self.planes, below)

    def close(self, m):
        for tile in range(self.tiles):
            last = self.main[self.at(m, tile, self.planes - 1)].astype(jnp.float32)
            self.put_above(m, tile, last)
        for tile in range(self.tiles):
            first = self.main[self.at(m, tile, 0)].astype(jnp.float32)
            self.put_below(m, tile, first)


class Branch:
    def __init__(self, k, rows, large, small, share, refs, masks, core):
        self.k, self.rows, self.refs, self.masks = k, rows, refs, masks
        self.units = unit_table(k)
        self.planes = 8 >> k
        self.core = core
        self.large, self.small, self.count = large, small, large + small
        self.cells = (small * (SH // 8) * (SW // 8), large * (LH // 8) * (LW // 8))
        self.quarter = lax.axis_index("crops") // 2
        self.share = share
        r = refs
        make = partial(Planes, masks=masks, rows=rows)
        make_one = partial(make, narrow=k <= 1)
        one = "wide" if k == 3 else "s1"
        self.maps = dict(
            h=make_one(one, 2, self.planes, main=r.hC, edge=r.hE, right=r.hR),
            u=make_one(one, 2, self.planes, main=r.uC, edge=r.uE, right=r.uR),
            t=make("p" if k == 3 else "s2", 2, self.planes, main=r.tC, edge=r.tE),
        )
        if k <= 1:
            self.maps["c1"] = make("s2", 1, self.planes // 2, main=r.c1C, edge=r.c1E)
        if k == 0:
            self.maps["c2"] = make("s2", 1, 4, main=r.c2C, edge=r.c2E)
            self.maps["c3"] = make("s2", 1, 2, main=r.c3C, edge=r.c3E)
        self.grads = dict(t=r.gt, u=r.gu, c1=r.gc1, c2=r.gc2, c3=r.gc3)

    def lane_block(self, shape, cout):
        lanes = lax.broadcasted_iota(jnp.int32, shape, 1)
        return lanes >> log2(cout)

    def keep(self, value, cout, which):
        count = LANES // cout
        if len(which) == count:
            return value
        block = self.lane_block(value.shape, cout)
        mask = block == which[0]
        for entry in which[1:]:
            mask = mask | (block == entry)
        return jnp.where(mask, value, 0.0)

    def spread(self, value, cout):
        shift = LANES // 2
        while shift >= cout:
            value = value + pltpu.roll(value, shift, 1)
            shift //= 2
        return value

    def local_blocks(self, seg, tile, wanted):
        count = LANES // seg.cout
        return [q for q in range(count) if (tile * count + q) % seg.blocks in wanted]


    def segments(self):
        return [(unit, seg) for unit in self.units.values() for seg in unit.segs]

    def pieces(self):
        found, place = [], 0
        for index, (unit, seg) in enumerate(self.segments()):
            count = 2 * seg.taps**2 * seg.cin * seg.cout // LANES
            if self.k < 3:
                found.append((index, 0, count, place, index))
                place += count
            else:
                for d in range(unit.depth):
                    slot = len(found) % 3
                    found.append((index, d, count // unit.depth, slot * 3072, slot))
        return found

    def fetch(self, at):
        r = self.refs
        index, d, count, place, sem = self.pieces()[at]
        _, seg = self.segments()[index]
        return pltpu.make_async_copy(
            r.w.at[pl.ds(2 * seg.off + d * count, count)],
            r.raw.at[pl.ds(place, count)],
            r.wsem.at[sem],
        )

    def fetch_first(self):
        for at in range(len(self.pieces()) if self.k < 3 else 3):
            self.fetch(at).start()

    def expand(self, index):
        unit, seg = self.segments()[index]
        pieces = self.pieces()
        mine = [at for at, piece in enumerate(pieces) if piece[0] == index]
        if self.k < 3:
            (at,) = mine
            self.fetch(at).wait()
            count = pieces[at][2] // unit.depth
            planes_loop(
                unit.depth,
                lambda d: self.expand_row(unit, seg, d, count, pieces[at][3] + d * count),
            )
        else:
            for d, at in enumerate(mine):
                self.fetch(at).wait()
                self.expand_row(unit, seg, d, pieces[at][2], pieces[at][3])
                if at + 3 < len(pieces):
                    self.fetch(at + 3).start()
        for m in range(MODULES):
            self.spread_tables(m, unit, seg)

    def expand_row(self, unit, seg, d, count, place):
        r = self.refs
        chunk = math.gcd(count, 384)
        wf, rep = r.work, r.rep

        def widen(step):
            at = pl.multiple_of(step * chunk, 16)
            value = r.raw[pl.ds(pl.multiple_of(place + at, 16), chunk)].astype(jnp.float32)
            wf[pl.ds(at, chunk)] = value

        planes_loop(count // chunk, widen)
        count = count // MODULES
        depth, cin, cout = unit.depth, seg.cin, seg.cout
        target = getattr(r, "T" + unit.name)
        twice = unit.kind == "s1" and self.k < 3
        across = getattr(r, "T" + unit.name + unit.name) if twice else None
        by_row = {}
        for row, tap, wanted in links(self.k, unit, seg):
            by_row.setdefault(row, []).append((tap, wanted))

        def module(m):
            if cout < LANES:
                ratio = LANES // cout
                flat = wf[pl.ds(m, count, stride=2)]
                for part in range(ratio):
                    rep[pl.ds(part, count, stride=ratio)] = self.spread(
                        self.keep(flat, cout, [part]), cout
                    )

            def tap_rows(tap, tile):
                if cout < LANES:
                    return rep[tap * cin : (tap + 1) * cin]
                if cout == LANES:
                    return wf[pl.ds(m + tap * (2 * cin), cin, stride=2)]
                return wf[pl.ds(m + tap * (4 * cin) + 2 * tile, cin, stride=4)]

            for tile in range(seg.tiles):
                column = (seg.tile + tile) * LANES
                for row in range(0, unit.rows, cin):
                    total = None
                    for tap, wanted in by_row.get(row, []):
                        if cout <= LANES:
                            local = self.local_blocks(seg, tile, wanted)
                            if not local:
                                continue
                            piece = self.keep(tap_rows(tap, 0), cout, local)
                        else:
                            piece = tap_rows(tap, tile)
                        total = piece if total is None else total + piece
                    if total is None:
                        total = jnp.zeros((cin, LANES), jnp.float32)
                    block = total.astype(jnp.bfloat16)
                    target[m * depth + d, row : row + cin, column : column + LANES] = block

            if not twice:
                return
            turned = []
            if cin == LANES:
                turned = [jnp.transpose(tap_rows(tap, 0)) for tap in range(3)]
            else:
                both = jnp.transpose(rep[0 : -(-3 * cin // LANES) * LANES])
                for tap in range(3):
                    first = tap * cin // LANES * LANES
                    value = both[0:cin, first : first + LANES]
                    value = self.keep(value, cin, [tap * cin % LANES // cin])
                    turned.append(self.spread(value, cin))
            for tile in range(2):
                for row in range(0, unit.rows, cin):
                    total = None
                    for tap, wanted in by_row.get(row, []):
                        local = self.local_blocks(seg, tile, wanted)
                        if local:
                            piece = self.keep(turned[2 - tap], cin, local)
                            total = piece if total is None else total + piece
                    if total is None:
                        total = jnp.zeros((cin, LANES), jnp.float32)
                    column = tile * LANES
                    across[m * depth + d, row : row + cin, column : column + LANES] = total.astype(
                        jnp.bfloat16
                    )

        planes_loop(MODULES, module)


    def parts(self, unit, source):
        if unit.kind == "p1":
            return [(source.main, range(2), source.at)]
        if source.mode == "wide":
            return [
                (source.edge, range(2), source.at),
                (source.main, range(2), source.at),
                (source.right, range(2), source.at),
            ]
        if unit.kind == "s1":
            tiles = [0] if source.narrow else range(2)
            return [(source.main, range(2), source.at), (source.edge, tiles, source.edge_at)]
        last = source.tiles - 1
        return [
            (source.main, range(source.tiles), source.at),
            (source.edge, [last], source.edge_at),
        ]

    def rows_of(self, unit, part, m, d, first, count):
        ref, tiles, at = part
        pieces = []
        for tile in tiles:
            if unit.kind == "s2":
                rows = [ref[at(m, tile, 2 * (first + q) + d - 1)] for q in range(count)]
                pieces.append(rows[0] if count == 1 else jnp.concatenate(rows, axis=0))
            else:
                shift = d - 1 if unit.kind == "s1" else 0
                pieces.append(
                    ref[pl.ds(at(m, tile, first + shift), count)].reshape(count * self.rows, LANES)
                )
        return pieces

    def conv(self, m, unit):
        r = self.refs
        source = self.maps[unit.source]
        target = getattr(r, "T" + unit.name)
        z = getattr(r, "z" + unit.name)
        planes, tiles, depth = unit.planes, unit.tiles, unit.depth
        chunk = min(planes, 4 if tiles <= 2 else 2)
        lanes = tiles * LANES

        def body(step, sums):
            first = step * chunk
            pieces = []
            for d in range(depth):
                for part in self.parts(unit, source):
                    pieces += self.rows_of(unit, part, m, d, first, chunk)
            left = jnp.concatenate(pieces, axis=1)
            right = target[pl.ds(m * depth, depth), 0 : unit.rows, 0:lanes]
            right = right.reshape(depth * unit.rows, lanes)
            result = lax.dot_general(left, right, DOWN, preferred_element_type=jnp.float32)
            for tile in range(tiles):
                block = result[:, tile * LANES : (tile + 1) * LANES]
                z[pl.ds(m * tiles * planes + tile * planes + first, chunk)] = block.reshape(
                    chunk, self.rows, LANES
                )
            return (sums[0] + partial_sum(result), sums[1] + partial_sum(result * result))

        zero = jnp.zeros((8, lanes), jnp.float32)
        sums = planes_sum(planes // chunk, body, (zero, zero))
        for seg in unit.segs:
            scale = self.per_cell(unit, seg)
            totals = self.fold(seg, sums)
            self.norm_rows(m, unit, seg, totals, scale)

    def per_cell(self, unit, seg):
        blocks = seg.tiles * LANES // seg.cout
        small, large = self.cells
        count = unit.planes * blocks
        return jnp.where(self.core == 0, 1.0 / (large * count), 1.0 / (small * count)).astype(
            jnp.float32
        )

    def fold(self, seg, sums):
        first = seg.tile
        found = []
        for value in sums:
            tiles = [
                value[:, (first + t) * LANES : (first + t + 1) * LANES] for t in range(seg.tiles)
            ]
            if seg.cout <= LANES:
                total = tiles[0]
                for tile in tiles[1:]:
                    total = total + tile
                total = jnp.sum(self.spread(total, seg.cout), axis=0, keepdims=True)
                found.append([total] * seg.tiles)
            else:
                found.append([jnp.sum(tile, axis=0, keepdims=True) for tile in tiles])
        return found

    def table_row(self, ref, m, seg, tile):
        slot = seg.slot
        if seg.cout > LANES:
            return ref[m, slot : slot + 1, tile * LANES : (tile + 1) * LANES]
        row = jnp.broadcast_to(ref[m, slot : slot + 1, 0:LANES], (8, LANES))
        if seg.cout < LANES:
            row = self.spread(self.keep(row, seg.cout, [0]), seg.cout)
        return row[0:1]

    def norm_rows(self, m, unit, seg, totals, scale):
        st = self.refs.st
        for tile in range(seg.tiles):
            average = totals[0][tile] * scale
            variance = totals[1][tile] * scale - average * average
            inverse = lax.rsqrt(variance + EPS)
            where = m * STATS + unit.stat + seg.tile + tile
            factor = st[where, 4:5] * inverse
            st[where, 0:1] = average
            st[where, 1:2] = inverse
            st[where, 2:3] = factor
            st[where, 3:4] = st[where, 5:6] - average * factor

    def spread_tables(self, m, unit, seg):
        st = self.refs.st
        for tile in range(seg.tiles):
            where = m * STATS + unit.stat + seg.tile + tile
            st[where, 4:5] = self.table_row(self.refs.gains, m, seg, tile)
            st[where, 5:6] = self.table_row(self.refs.shifts, m, seg, tile)

    def normed(self, m, unit, tile, plane):
        st = self.refs.st
        z = getattr(self.refs, "z" + unit.name)
        where = m * STATS + unit.stat + tile
        value = z[m * unit.tiles * unit.planes + tile * unit.planes + plane]
        return value * st[where, 2:3] + st[where, 3:4]

    def apply_a(self, m):
        unit, u = self.units["a"], self.maps["u"]

        def body(plane):
            for tile in range(2):
                value = silu_of(self.normed(m, unit, tile, plane)) * self.masks[0]
                u.store(m, tile, plane, value)

        planes_loop(self.planes, body, TURNS)
        u.close(m)

    def apply_b(self, m):
        unit, top = self.units["b"], self.maps["t"]
        hf, s = self.refs.hf, self.refs.s

        def body(plane):
            for tile in range(2):
                where = m * 2 * self.planes + tile * self.planes + plane
                value = silu_of(self.normed(m, unit, tile, plane) + hf[where]) * self.masks[0]
                s[where] = value
                top.store(m, tile, plane, value)

        planes_loop(self.planes, body, TURNS)
        top.close(m)

    def apply_rest(self, m, unit):
        sb = self.refs.sb
        for seg in unit.segs:
            chain = self.maps[seg.chain] if seg.chain else None

            def body(plane):
                for tile in range(seg.tiles):
                    value = self.normed(m, unit, seg.tile + tile, plane)
                    if chain is not None:
                        chain.store(m, tile, plane, silu_of(value) * self.masks[0])
                    else:
                        at = message_slot(self.k, seg.dest) + tile * unit.planes + plane
                        sb[at] = value.astype(jnp.bfloat16)

            planes_loop(unit.planes, body, TURNS)
            if chain is not None:
                chain.close(m)
            else:
                self.message(m, seg.dest).start()

    def message(self, e, other):
        count = 2 * (8 >> max(self.k, other))
        r = self.refs
        return pltpu.make_async_remote_copy(
            src_ref=r.sb.at[pl.ds(message_slot(self.k, other), count)],
            dst_ref=r.rb.at[pl.ds(e * 16 + message_slot(other, self.k), count)],
            send_sem=r.ssem.at[e * 4 + other],
            recv_sem=r.rsem.at[e * 4 + self.k],
            device_id=dict(branch=other),
            device_id_type=pl.DeviceIdType.MESH,
        )

    def arrived(self, e, other):
        count = 2 * (8 >> max(self.k, other))
        r = self.refs
        at = message_slot(self.k, other)
        return pltpu.make_async_remote_copy(
            src_ref=r.sb.at[pl.ds(at, count)],
            dst_ref=r.rb.at[pl.ds(e * 16 + at, count)],
            send_sem=r.ssem.at[e * 4 + other],
            recv_sem=r.rsem.at[e * 4 + other],
            device_id=dict(branch=other),
            device_id_type=pl.DeviceIdType.MESH,
        )

    def others(self):
        return [other for other in range(4) if other != self.k]

    def sent(self, e):
        for other in self.others():
            self.message(e, other).wait_send()

    def receive(self, m):
        r = self.refs
        s, rb, hf, out = r.s, r.rb, r.hf, r.outs
        h = self.maps["h"]

        def total_at(tile, plane):
            where = m * 2 * self.planes + tile * self.planes + plane
            total = s[where]
            for other in self.others():
                count = 8 >> max(self.k, other)
                at = plane >> max(0, other - self.k)
                slot = m * 16 + message_slot(self.k, other) + tile * count + at
                total = total + rb[slot].astype(jnp.float32)
            s[where] = total
            return silu_of(total) * self.masks[0]

        def onward(plane):
            for tile in range(2):
                value = total_at(tile, plane)
                hf[(2 + tile) * self.planes + plane] = value
                h.store(1, tile, plane, value)

        def finish(plane):
            for tile in range(2):
                out[tile * self.planes + plane] = total_at(tile, plane).astype(jnp.bfloat16)

        @pl.when(m + 1 < MODULES)
        def _():
            planes_loop(self.planes, onward, TURNS)
            h.close(1)

        @pl.when(m + 1 == MODULES)
        def _():
            planes_loop(self.planes, finish, TURNS)

    def take_feature(self, tile, plane, value):
        self.refs.hf[tile * self.planes + plane] = value
        self.maps["h"].store(0, tile, plane, value)

    def take_cotangent(self, tile, plane, value):
        self.refs.gin[tile * self.planes + plane] = value

    def member(self, kind, order):
        kinds = self.refs.kinds
        found, before = jnp.int32(0), jnp.int32(0)
        for at in range(self.count):
            same = kinds[at] == kind
            found = jnp.where(same & (before == order), at, found)
            before = before + same.astype(jnp.int32)
        return found

    def order(self, device):
        kinds = self.refs.kinds
        kind = kinds[device]
        before = jnp.int32(0)
        for at in range(self.count):
            before = before + ((kinds[at] == kind) & (at < device)).astype(jnp.int32)
        return before

    def unpack(self, t, consume):
        r = self.refs
        work, rows, planes = r.work, self.rows, self.planes
        full = SH * SW * C0 // LANES
        gath = r.gathc if t else r.gathx

        @pl.when(self.core == 0)
        def _():
            for at in range(self.large):
                block = gath[self.member(1, at)]
                work[at * ROWS : (at + 1) * ROWS] = block.astype(jnp.float32)

        @pl.when(self.core == 1)
        def _():
            for at in range(self.small):
                block = gath[self.member(0, at), 0:full]
                work[at * full : (at + 1) * full] = block.astype(jnp.float32)
            work[self.small * full : self.large * ROWS] = jnp.zeros(
                (self.large * ROWS - self.small * full, LANES), jnp.float32
            )

        deep = self.large * ROWS // 2
        right = jnp.concatenate([work[pl.ds(j, deep, stride=2)] for j in range(2)], axis=1)
        right = right.astype(jnp.bfloat16)
        cells = Cells(self.core, (rows, LANES), self.small, self.large)
        base = cells.crop * cells.pick(ROWS // 2, full // 2)
        base = base + cells.along * (planes * cells.wide) + cells.across
        base = jnp.where(cells.valid, base, -(1 << 20))
        lane = lax.broadcasted_iota(jnp.int32, (rows, LANES), 1)
        chunk = min(planes, 4)

        def body(step):
            pieces = []
            for q in range(chunk):
                goal = base + (step * chunk + q) * cells.wide
                pieces.append(one_hot(goal, lane, deep))
            left = pieces[0] if chunk == 1 else jnp.concatenate(pieces, axis=0)
            result = lax.dot_general(left, right, DOWN, preferred_element_type=jnp.float32)
            for q in range(chunk):
                for tile in range(2):
                    value = result[q * rows : (q + 1) * rows, tile * LANES : (tile + 1) * LANES]
                    consume(tile, step * chunk + q, value)

        planes_loop(planes // chunk, body)

    def pack_size(self):
        return 48 * self.planes, -(-self.planes * self.rows // LANES) * LANES

    def plan_pack(self):
        r = self.refs
        high, deep = self.pack_size()
        planes = self.planes
        q = lax.broadcasted_iota(jnp.int32, (high, LANES), 0)
        lane = lax.broadcasted_iota(jnp.int32, (high, LANES), 1)
        wide, tall = jnp.where(self.core == 0, 6, 3), jnp.where(self.core == 0, 8, 4)
        cell = jnp.where(self.core == 0, (q * 43691) >> 18, (q * 43691) >> 17)
        across = q - cell * wide
        plane = cell & (planes - 1)
        along = cell >> log2(planes)
        base = plane * self.rows + along * wide + across
        base = jnp.where(along < tall, base, -(1 << 20))
        shard = lax.axis_index("crops")
        for at, device in enumerate((shard, shard + 1 - 2 * self.core)):
            goal = base + self.order(device) * (wide * tall)
            r.hot[at, 0:high, 0:deep] = one_hot(goal, lane, deep)

    def pack(self, units, put):
        high, deep = self.pack_size()
        right = jnp.concatenate([units(tile) for tile in range(2)], axis=1)
        short = deep - right.shape[0]
        parts = [right.astype(jnp.bfloat16)]
        if right.dtype == jnp.float32:
            parts.append((right - parts[0].astype(jnp.float32)).astype(jnp.bfloat16))
        if short:
            empty = jnp.zeros((short, 2 * LANES), jnp.bfloat16)
            parts = [jnp.concatenate([part, empty], axis=0) for part in parts]
        for at in range(2):
            total = None
            for part in parts:
                piece = lax.dot_general(
                    self.refs.hot[at, 0:high, 0:deep],
                    part,
                    DOWN,
                    preferred_element_type=jnp.float32,
                )
                total = piece if total is None else total + piece
            for tile in range(2):
                put(at, pl.ds(tile, high, stride=2), total[:, tile * LANES : (tile + 1) * LANES])

    def pack_outputs(self):
        r = self.refs
        high = 2 * self.pack_size()[0]

        def put(at, where, value):
            r.work[pl.ds(at * ROWS + where.start, where.size, stride=2)] = value

        def units(tile):
            block = r.outs[tile * self.planes : (tile + 1) * self.planes]
            return block.reshape(self.planes * self.rows, LANES)

        self.pack(units, put)
        for at in range(2):
            r.blocks[at, 0:high] = r.work[at * ROWS : at * ROWS + high].astype(jnp.bfloat16)
            if high < ROWS:
                r.blocks[at, high:ROWS] = jnp.zeros((ROWS - high, LANES), jnp.bfloat16)

    def pack_gradient(self):
        r = self.refs
        high = 2 * self.pack_size()[0]

        def put(at, where, value):
            r.slopes[at, where] = value

        def units(tile):
            block = r.gin[tile * self.planes : (tile + 1) * self.planes]
            return block.reshape(self.planes * self.rows, LANES)

        self.pack(units, put)
        if high < ROWS:
            for at in range(2):
                r.slopes[at, high:ROWS] = jnp.zeros((ROWS - high, LANES), jnp.float32)

    def forward(self, m, gather):
        def also(module, step):
            pl.when(m == module)(lambda: gather.step(1, step))

        self.conv(m, self.units["a"])
        self.apply_a(m)
        self.conv(m, self.units["b"])
        self.apply_b(m)
        also(0, 1)
        also(1, 3)

        @pl.when(m > 0)
        def _():
            self.sent(m - 1)

        for name in ("d", "u", "e", "f", "g"):
            if name in self.units:
                self.conv(m, self.units[name])
                self.apply_rest(m, self.units[name])
        also(0, 2)

        @pl.when(m == MODULES - 1)
        def _():
            gather.collect(1)
            self.unpack(1, self.take_cotangent)

        for other in self.others():
            self.arrived(m, other).wait_recv()
        self.receive(m)


    def send_back(self, m):
        r = self.refs
        s, gin, gt, sb = r.s, r.gin, r.gt, r.sb
        e = MODULES + m

        def body(plane):
            for tile in range(2):
                at = tile * self.planes + plane
                value = gin[at] * slope_of(s[m * 2 * self.planes + at])
                gt[at] = value
                for other in range(self.k):
                    sb[message_slot(self.k, other) + at] = value.astype(jnp.bfloat16)

        planes_loop(self.planes, body, TURNS)
        for other in reversed(self.others()):
            if other > self.k:
                count = 8 >> other
                wide = 1 << (other - self.k)

                def pool(plane):
                    for tile in range(2):
                        total = gt[tile * self.planes + plane * wide]
                        for step in range(1, wide):
                            total = total + gt[tile * self.planes + plane * wide + step]
                        slot = message_slot(self.k, other) + tile * count + plane
                        sb[slot] = total.astype(jnp.bfloat16)

                planes_loop(count, pool, TURNS)
            self.message(e, other).start()

    def back_unit(self, m, unit):
        r = self.refs
        st, dyb, z = r.st, r.dyb, getattr(r, "z" + unit.name)
        name, planes, tiles = unit.name, unit.planes, unit.tiles
        e = MODULES + m
        sums = {}

        def upstream(seg, tile, plane, normed):
            at = tile * planes + plane
            if name == "b":
                hf = r.hf[m * 2 * planes + at]
                value = r.gt[at] * slope_of(normed + hf)
                r.gin[at] = value
                return value
            if name == "a":
                return r.gu[at] * slope_of(normed)
            if seg.chain:
                return self.grads[seg.chain][at] * slope_of(normed)
            return r.rb[e * 16 + message_slot(self.k, seg.dest) + at].astype(jnp.float32)

        for seg in unit.segs:

            def body(plane, carry):
                result = []
                for tile in range(seg.tiles):
                    at = (seg.tile + tile) * planes + plane
                    where = m * STATS + unit.stat + seg.tile + tile
                    value = z[m * tiles * planes + at]
                    normed = value * st[where, 2:3] + st[where, 3:4]
                    dy = upstream(seg, tile, plane, normed)
                    dyb[at] = dy
                    zhat = (value - st[where, 0:1]) * st[where, 1:2]
                    result.append(carry[2 * tile] + partial_sum(dy))
                    result.append(carry[2 * tile + 1] + partial_sum(dy * zhat))
                return tuple(result)

            zero = jnp.zeros((8, LANES), jnp.float32)
            found = planes_sum(planes, body, (zero,) * (2 * seg.tiles), TURNS)
            pair = [
                jnp.concatenate([found[2 * tile + which] for tile in range(seg.tiles)], axis=1)
                for which in range(2)
            ]
            plain = SimpleNamespace(**vars(seg))
            plain.tile = 0
            totals = self.fold(plain, pair)
            self.table_grads(m, seg, totals)
            sums[seg.slot] = totals
        dz = self.dz_planes(unit)
        for seg in unit.segs:
            scale = self.per_cell(unit, seg)
            totals = sums[seg.slot]

            def apply(plane):
                for tile in range(seg.tiles):
                    at = (seg.tile + tile) * planes + plane
                    where = m * STATS + unit.stat + seg.tile + tile
                    zhat = (z[m * tiles * planes + at] - st[where, 0:1]) * st[where, 1:2]
                    inner = dyb[at] - totals[0][tile] * scale - zhat * (totals[1][tile] * scale)
                    dz.store(0, seg.tile + tile, plane, inner * st[where, 2:3] * self.masks[0])

            planes_loop(planes, apply, TURNS)
        dz.close(0)
        self.back_data(m, unit, dz)
        first = min(seg.off for seg in unit.segs)
        last = max(seg.off + seg.taps**2 * seg.cin * seg.cout // LANES for seg in unit.segs)
        wanted = (self.quarter * self.share < last) & ((self.quarter + 1) * self.share > first)

        @pl.when(wanted)
        def _():
            self.back_kernel(m, unit, dz)

    def dz_planes(self, unit):
        r = self.refs
        mode = {"p1": "p", "s2": "dz2", "s1": "wide" if self.k == 3 else "s1"}[unit.kind]
        return Planes(
            mode,
            unit.tiles,
            unit.planes,
            self.masks,
            self.rows,
            r.dC,
            r.dE,
            r.dR,
            self.k <= 1 and unit.kind == "s1",
        )

    def table_grads(self, m, seg, totals):
        gg = self.refs.gg
        slot = seg.slot
        for which, found in ((0, totals[1]), (1, totals[0])):
            if seg.cout > LANES:
                for tile in range(2):
                    gg[m, which, slot : slot + 1, tile * LANES : (tile + 1) * LANES] = found[tile]
            else:
                row = jnp.broadcast_to(found[0], (8, LANES))
                if seg.cout < LANES:
                    row = self.keep(row, seg.cout, [0])
                gg[m, which, slot : slot + 1, 0:LANES] = row[0:1]

    def wide_rows(self, ref, at, tiles, plane, count):
        pieces = [
            ref[pl.ds(at(0, tile, plane), count)].reshape(count * self.rows, LANES)
            for tile in range(tiles)
        ]
        return pieces[0] if tiles == 1 else jnp.concatenate(pieces, axis=1)

    def back_data(self, m, unit, dz):
        r = self.refs
        kind, tiles = unit.kind, unit.tiles
        target = getattr(r, "T" + unit.name)
        lanes = tiles * LANES
        rows = self.rows

        def kernel_rows(d, first, count):
            return target[m * unit.depth + d, first : first + count, 0:lanes]

        def product(left, right):
            return lax.dot_general(left, right, ACROSS, preferred_element_type=jnp.float32)

        def put(ref, tile, planes, first, count, value, step=1, add=False):
            block = value.reshape(count, rows, LANES)
            for q in range(count):
                at = tile * planes + first + q * step
                ref[at] = ref[at] + block[q] if add else block[q]

        planes = unit.planes
        if kind == "s1":
            goal = r.gu if unit.name == "b" else r.gin
            add = unit.name == "a"
            chunk = min(planes, 4)
            across = getattr(r, "T" + unit.name + unit.name)

            def body(step):
                first = step * chunk
                if self.k == 3:
                    total = None
                    for d in range(3):
                        for ref, at in ((dz.right, 0), (dz.main, 256), (dz.edge, 512)):
                            left = self.wide_rows(ref, dz.at, 2, first + 1 - d, chunk)
                            piece = product(left, kernel_rows(d, at, 256))
                            total = piece if total is None else total + piece
                else:
                    narrow = 1 if dz.narrow else 2
                    left = []
                    for d in range(3):
                        at = first + 1 - d
                        left.append(self.wide_rows(dz.main, dz.at, 2, at, chunk))
                        left.append(self.wide_rows(dz.edge, dz.edge_at, narrow, at, chunk))
                    right = across[pl.ds(m * 3, 3), 0 : unit.rows].reshape(3 * unit.rows, 256)
                    total = lax.dot_general(
                        jnp.concatenate(left, axis=1),
                        right,
                        DOWN,
                        preferred_element_type=jnp.float32,
                    )
                for tile in range(2):
                    put(
                        goal,
                        tile,
                        planes,
                        first,
                        chunk,
                        total[:, tile * LANES : (tile + 1) * LANES],
                        add=add,
                    )

            planes_loop(planes // chunk, body)
            return
        if kind == "p1":
            left = self.wide_rows(dz.main, dz.at, tiles, 0, planes)
            total = product(left, kernel_rows(0, 0, 256))
            for tile in range(2):
                put(
                    r.gt,
                    tile,
                    planes,
                    0,
                    planes,
                    total[:, tile * LANES : (tile + 1) * LANES],
                    add=True,
                )
            return
        goal = self.grads[unit.source]
        add = unit.source == "t"
        lanes_in = unit.lanes_in
        count_in = unit.planes_in
        for parity, terms in ((0, [(1, 0)]), (1, [(2, 0), (0, 1)])):
            total, side = None, None
            for d, offset in terms:
                left = self.wide_rows(dz.main, dz.at, tiles, offset, planes)
                piece = product(left, kernel_rows(d, 0, lanes_in))
                total = piece if total is None else total + piece
                left = self.wide_rows(dz.edge, dz.at, tiles, offset, planes)
                piece = product(left, kernel_rows(d, lanes_in, LANES))
                side = piece if side is None else side + piece
            for tile in range(lanes_in // LANES):
                value = total[:, tile * LANES : (tile + 1) * LANES]
                if tile == lanes_in // LANES - 1:
                    value = value + side
                put(goal, tile, count_in, parity, planes, value, step=2, add=add)

    def back_kernel(self, m, unit, dz):
        r = self.refs
        G, rep, wgv = r.work, r.rep, r.wgv
        tiles, planes = unit.tiles, unit.planes
        source = self.maps[unit.source]
        right = self.wide_rows(dz.main, dz.at, tiles, 0, planes)

        def gather(d):
            at = 0
            for part in self.parts(unit, source):
                pieces = self.rows_of(unit, part, m, d, 0, planes)
                left = pieces[0] if len(pieces) == 1 else jnp.concatenate(pieces, axis=1)
                count = left.shape[1]
                result = lax.dot_general(left, right, ALONG, preferred_element_type=jnp.float32)
                for tile in range(tiles):
                    row = pl.multiple_of((d * tiles + tile) * unit.rows + at, 8)
                    G[pl.ds(row, count)] = result[:, tile * LANES : (tile + 1) * LANES]
                at += count

        planes_loop(unit.depth, gather)
        for seg in unit.segs:
            self.fold_kernel(m, unit, seg)

    def fold_kernel(self, m, unit, seg):
        r = self.refs
        G, rep, wgv = r.work, r.rep, r.wgv
        cin, cout, tiles = seg.cin, seg.cout, unit.tiles
        width = 3 if seg.taps == 3 else 1
        found = links(self.k, unit, seg)
        off = seg.off

        def fold(d):
            for column in range(width):
                tap = d * width + column
                totals = []
                for tile in range(seg.tiles):
                    total = None
                    for row, which, wanted in found:
                        if which != column:
                            continue
                        at = pl.multiple_of((d * tiles + seg.tile + tile) * unit.rows + row, 8)
                        piece = G[pl.ds(at, cin)]
                        if cout <= LANES:
                            local = self.local_blocks(seg, tile, wanted)
                            if not local:
                                continue
                            piece = self.keep(piece, cout, local)
                        total = piece if total is None else total + piece
                    totals.append(total)
                if cout > LANES:
                    for tile in range(2):
                        wgv[pl.ds(off + tap * (2 * cin) + tile, cin, stride=2)] = totals[tile]
                    continue
                total = None
                for piece in totals:
                    if piece is not None:
                        total = piece if total is None else total + piece
                if cout == LANES:
                    wgv[pl.ds(pl.multiple_of(off + tap * cin, 8), cin)] = total
                else:
                    rep[pl.ds(pl.multiple_of(tap * cin, cin), cin)] = self.spread(total, cout)

        planes_loop(unit.depth, fold)
        if cout < LANES:
            ratio = LANES // cout
            count = width * width * cin // ratio
            total = None
            for part in range(ratio):
                piece = self.keep(rep[pl.ds(part, count, stride=ratio)], cout, [part])
                total = piece if total is None else total + piece
            wgv[off : off + count] = total

    def backward(self, m, meanwhile):
        e = MODULES + m
        last = m == MODULES - 1
        self.sent(jnp.where(last, m, e + 1))
        self.send_back(m)
        pl.when(last)(meanwhile)
        for name in ("g", "f", "e", "d", "u"):
            if name in self.units:
                for seg in self.units[name].segs:
                    if seg.dest >= 0:
                        self.arrived(e, seg.dest).wait_recv()
                self.back_unit(m, self.units[name])
        self.back_unit(m, self.units["b"])
        self.back_unit(m, self.units["a"])


STATS = 20
TURNS = 4
NAMES = list(
    dict(x=0, cot=0, w=0, gains=0, shifts=0, kinds=0, out=0, grad=0, wg=0, gain=0, shift=0)
)


def one_hot(goal, lane, deep):
    pieces = [
        jnp.where(goal == lane + first, 1.0, 0.0).astype(jnp.bfloat16)
        for first in range(0, deep, LANES)
    ]
    return jnp.concatenate(pieces, axis=1)


class Cells:
    def __init__(self, core, shape, small, large):
        self.core = core
        row = lax.broadcasted_iota(jnp.int32, shape, 0)
        self.wide = self.pick(LW // 8, SW // 8)
        tall = self.pick(LH // 8, SH // 8)
        self.crop = self.pick((row * 43691) >> 21, (row * 43691) >> 19)
        inner = row - self.crop * (self.wide * tall)
        self.along = self.pick((inner * 43691) >> 18, (inner * 43691) >> 17)
        self.across = inner - self.along * self.wide
        self.valid = self.crop < self.pick(large, small)
        self.last = tall - 1

    def pick(self, large, small):
        return jnp.where(self.core == 0, large, small)


def fill_masks(refs, rows, core, small, large):
    cells = Cells(core, (rows, LANES), small, large)
    valid = cells.valid
    six = cells.wide == 6
    up, down = valid & (cells.along > 0), valid & (cells.along < cells.last)
    tables = (
        valid,
        valid & (cells.across > 0),
        valid & (cells.across < cells.wide - 1),
        up & six,
        up & jnp.logical_not(six),
        down & six,
        down & jnp.logical_not(six),
    )
    for at, table in enumerate(tables):
        refs.masks[at] = jnp.where(table, 1.0, 0.0)


class Gather:
    def __init__(self, refs, core, count):
        self.refs, self.core, self.count = refs, core, count
        self.z = lax.axis_index("crops") // 2
        self.last = count // 2 - 1

    def hop(self, t, source, right):
        r = self.refs
        at = source * 2 + self.core
        gath = r.gathc if t else r.gathx
        to = self.z + 1 if right else self.z - 1
        return pltpu.make_async_remote_copy(
            src_ref=gath.at[at],
            dst_ref=gath.at[at],
            send_sem=r.hsem.at[(t * (self.last + 1) + source) * 3 + (0 if right else 1)],
            recv_sem=r.gsem.at[t * self.count + at],
            device_id=dict(crops=to * 2 + self.core),
            device_id_type=pl.DeviceIdType.MESH,
        )

    def across(self, t, source, core, rows):
        r = self.refs
        at = source * 2 + core
        gath = r.gathc if t else r.gathx
        return pltpu.make_async_remote_copy(
            src_ref=gath.at[at, pl.ds(0, rows)],
            dst_ref=gath.at[at, pl.ds(0, rows)],
            send_sem=r.hsem.at[(t * (self.last + 1) + source) * 3 + 2],
            recv_sem=r.gsem.at[t * self.count + at],
            device_id=dict(crops=self.z * 2 + 1 - self.core),
            device_id_type=pl.DeviceIdType.MESH,
        )

    def each_core(self, action):
        for core, rows in ((0, SH * SW * C0 // LANES), (1, ROWS)):

            @pl.when(self.core == core)
            def _():
                action(core, rows)

    def send(self, t, source, rightward, leftward):
        if rightward:

            @pl.when(self.z < self.last)
            def _():
                self.hop(t, source, True).start()

        if leftward:

            @pl.when(self.z > 0)
            def _():
                self.hop(t, source, False).start()

        self.each_core(lambda core, rows: self.across(t, source, core, rows).start())

    def step(self, t, s):
        r = self.refs
        if s == 0:
            at = self.z * 2 + self.core
            if t:
                r.gathc[at] = r.cot[...]
            else:
                r.gathx[at] = r.x[...]
            self.send(t, self.z, True, True)
            return

        @pl.when(self.z >= s)
        def _():
            self.hop(t, self.z - s, True).wait_recv()
            self.send(t, self.z - s, True, False)

        @pl.when(self.z + s <= self.last)
        def _():
            self.hop(t, self.z + s, True).wait_recv()
            self.send(t, self.z + s, False, True)

    def collect(self, t):
        for source in range(self.last + 1):
            for core, rows in ((0, ROWS), (1, SH * SW * C0 // LANES)):

                @pl.when(self.core == core)
                def _():
                    self.across(t, source, 1 - core, rows).wait_recv()

    def finish(self, t):
        def sent(source, rightward, leftward):
            if rightward:

                @pl.when(self.z < self.last)
                def _():
                    self.hop(t, source, True).wait_send()

            if leftward:

                @pl.when(self.z > 0)
                def _():
                    self.hop(t, source, False).wait_send()

            self.each_core(lambda core, rows: self.across(t, source, core, rows).wait_send())

        sent(self.z, True, True)
        for s in range(1, self.last + 1):

            @pl.when(self.z >= s)
            def _():
                sent(self.z - s, True, False)

            @pl.when(self.z + s <= self.last)
            def _():
                sent(self.z + s, False, True)


def scratch_table(rows, weight_rows, count):
    def half(many):
        return pltpu.VMEM((many, rows, LANES), jnp.bfloat16)

    def full(many):
        return pltpu.VMEM((many, rows, LANES), jnp.float32)

    def expanded(depth, deep, wide):
        return pltpu.VMEM((MODULES * depth, deep, wide), jnp.bfloat16)

    _, span, _ = pair_rows(weight_rows, count)
    return dict(
        masks=full(MASKS),
        hC=half(2 * 20),
        hE=half(2 * 10),
        hR=half(2 * 6),
        uC=half(2 * 20),
        uE=half(2 * 10),
        uR=half(2 * 6),
        tC=half(2 * 18),
        tE=half(2 * 9),
        c1C=half(2 * 5),
        c1E=half(2 * 5),
        c2C=half(2 * 5),
        c2E=half(2 * 5),
        c3C=half(2 * 3),
        c3E=half(2 * 3),
        dC=half(20),
        dE=half(20),
        dR=half(6),
        outs=half(16),
        hf=full(2 * 16),
        s=full(2 * 16),
        za=full(2 * 16),
        zb=full(2 * 16),
        zd=full(2 * 16),
        zu=full(2 * 8),
        ze=full(2 * 4),
        zf=full(2 * 2),
        zg=full(2 * 2),
        gt=full(16),
        gu=full(16),
        gin=full(16),
        gc1=full(4),
        gc2=full(4),
        gc3=full(2),
        dyb=full(16),
        sb=half(16),
        rb=half(4 * 16),
        st=pltpu.VMEM((MODULES * STATS, 8, LANES), jnp.float32),
        Ta=expanded(3, 768, 256),
        Tb=expanded(3, 768, 256),
        Taa=expanded(3, 512, 256),
        Tbb=expanded(3, 512, 256),
        Td=expanded(3, 384, 512),
        Tu=expanded(1, 256, 768),
        Te=expanded(3, 256, 256),
        Tf=expanded(3, 256, 128),
        Tg=expanded(3, 256, 256),
        raw=pltpu.VMEM((9408, LANES), jnp.bfloat16),
        work=pltpu.VMEM((4608, LANES), jnp.float32),
        rep=pltpu.VMEM((640, LANES), jnp.float32),
        wgv=pltpu.VMEM((weight_rows, LANES), jnp.float32),
        wq=pltpu.VMEM((MODULES, 2 * weight_rows // count, LANES), jnp.float32),
        wr=pltpu.VMEM((MODULES, span, LANES), jnp.float32),
        gathx=pltpu.VMEM((count, ROWS, LANES), jnp.bfloat16),
        gathc=pltpu.VMEM((count, ROWS, LANES), jnp.bfloat16),
        hot=pltpu.VMEM((2, 384, 768), jnp.bfloat16),
        blocks=pltpu.VMEM((2, ROWS, LANES), jnp.bfloat16),
        slopes=pltpu.VMEM((2, ROWS, LANES), jnp.float32),
        blockr=pltpu.VMEM((ROWS, LANES), jnp.bfloat16),
        sloper=pltpu.VMEM((ROWS, LANES), jnp.float32),
        gg=pltpu.VMEM((MODULES, 2, SLOTS, 256), jnp.float32),
        ggr=pltpu.VMEM((MODULES, 2, SLOTS, 256), jnp.float32),
        wsem=pltpu.SemaphoreType.DMA((8,)),
        ssem=pltpu.SemaphoreType.DMA((16,)),
        rsem=pltpu.SemaphoreType.DMA((16,)),
        hsem=pltpu.SemaphoreType.DMA((3 * count,)),
        gsem=pltpu.SemaphoreType.DMA((2 * count,)),
        psem=pltpu.SemaphoreType.DMA((5,)),
        qsem=pltpu.SemaphoreType.DMA((5,)),
        osem=pltpu.SemaphoreType.DMA((1,)),
    )


def pair_rows(weight_rows, count):
    share = weight_rows // count
    low = share // 8 * 8
    return share, 2 * share - low, low


def greet(core, count):
    barrier = pltpu.get_barrier_semaphore()
    me, shard = lax.axis_index("branch"), lax.axis_index("crops")
    z = shard // 2

    def signal(**where):
        pl.semaphore_signal(barrier, inc=1, device_id=where, device_id_type=pl.DeviceIdType.MESH)

    for step in range(1, 4):
        signal(branch=lax.rem(me + step, 4))
    signal(crops=shard + 1 - 2 * core)

    @pl.when(z > 0)
    def _():
        signal(crops=shard - 2)

    @pl.when(z < count // 2 - 1)
    def _():
        signal(crops=shard + 2)

    ends = (z == 0).astype(jnp.int32) + (z == count // 2 - 1).astype(jnp.int32)
    pl.semaphore_wait(barrier, 6 - ends)


def whole_kernel(names, rows, large, small, *args):
    refs = SimpleNamespace(**dict(zip(names, args)))
    count = large + small
    me, shard = lax.axis_index("branch"), lax.axis_index("crops")
    core = shard % 2
    weight_rows = refs.wgv.shape[0]
    share, span, low = pair_rows(weight_rows, count)
    quarter = pl.multiple_of(shard // 2 * (2 * share), 8)

    class Lazy:
        def __getitem__(self, index):
            return refs.masks[index]

    def across(source, goal, index):
        return pltpu.make_async_remote_copy(
            src_ref=source,
            dst_ref=goal,
            send_sem=refs.psem.at[index],
            recv_sem=refs.qsem.at[index],
            device_id=dict(crops=shard + 1 - 2 * core),
            device_id_type=pl.DeviceIdType.MESH,
        )

    def kernel_pair(m):
        at = pl.multiple_of(low * (1 - core), 8)
        return across(refs.wq.at[m, pl.ds(at, span)], refs.wr.at[m], m)

    outputs_pair = across(refs.blocks.at[1], refs.blockr, 2)
    gradient_pair = across(refs.slopes.at[1], refs.sloper, 3)
    table_pair = across(refs.gg, refs.ggr, 4)
    gather = Gather(refs, core, count)

    def every(action):
        for k in range(4):

            @pl.when(me == k)
            def _():
                action(Branch(k, rows, large, small, 2 * share, refs, Lazy(), core))

    def begin(branch):
        branch.fetch_first()

    def prepare(branch):
        found = branch.segments()
        stops = {0: 1, min(2, len(found) - 2): 2, len(found) - 1: 3}
        for index, (unit, seg) in enumerate(found):
            branch.expand(index)
            if index in stops:
                gather.step(0, stops[index])

    def main(branch):
        branch.unpack(0, branch.take_feature)
        branch.maps["h"].close(0)
        gather.step(1, 0)

        def ahead(m, carry):
            branch.forward(m, gather)
            return carry

        def meanwhile():
            branch.plan_pack()
            branch.pack_outputs()
            outputs_pair.start()

        def back(step, carry):
            m = MODULES - 1 - step
            branch.backward(m, meanwhile)
            refs.wq[m] = refs.wgv[pl.ds(quarter, 2 * share)]
            kernel_pair(m).start()
            return carry

        lax.fori_loop(0, MODULES, ahead, 0)
        lax.fori_loop(0, MODULES, back, 0)
        branch.sent(MODULES)
        branch.pack_gradient()
        gradient_pair.start()
        table_pair.start()

    every(begin)
    greet(core, count)
    gather.step(0, 0)
    fill_masks(refs, rows, core, small, large)
    refs.wgv[pl.ds(quarter, 2 * share)] = jnp.zeros((2 * share, LANES), jnp.float32)
    refs.gg[...] = jnp.zeros(refs.gg.shape, jnp.float32)
    every(prepare)
    gather.collect(0)
    every(main)

    for step in range(MODULES):
        m = MODULES - 1 - step
        kernel_pair(m).wait()
        mine = refs.wq[m, pl.ds(pl.multiple_of(low * core, 8), span)]
        refs.work[pl.ds(m, span, stride=MODULES)] = mine + refs.wr[m]
    skip = pl.multiple_of(core * (MODULES * (share - low)), 8)
    leave = pltpu.make_async_copy(
        refs.work.at[pl.ds(skip, MODULES * share)], refs.wg, refs.osem.at[0]
    )
    leave.start()
    outputs_pair.wait()
    gradient_pair.wait()
    table_pair.wait()
    own = refs.kinds[shard] != core
    refs.out[...] = jnp.where(own, refs.blocks[0].astype(jnp.float32), refs.blockr[...].astype(jnp.float32)).astype(jnp.bfloat16)
    refs.grad[...] = jnp.where(own, refs.slopes[0], refs.sloper[...])
    width = 256 // count
    for which, goal in ((0, refs.gain), (1, refs.shift)):
        for m in range(MODULES):
            total = refs.gg[m, which] + refs.ggr[m, which]
            found = None
            for at in range(count):
                piece = jnp.where(shard == at, total[:, at * width : (at + 1) * width], 0.0)
                found = piece if found is None else found + piece
            goal[m] = found
    gather.finish(0)
    gather.finish(1)
    leave.wait()


def whole_call(rows, large, small, x, cot, w, gains, shifts, kinds):
    count = large + small
    weight_rows = w.shape[0] // MODULES
    table = scratch_table(rows, weight_rows, count)
    vmem = pl.BlockSpec(memory_space=pltpu.VMEM)
    hbm = pl.BlockSpec(memory_space=pl.ANY)
    smem = pl.BlockSpec(memory_space=pltpu.SMEM)
    tables = jax.ShapeDtypeStruct((MODULES, SLOTS, 256 // count), jnp.float32)
    return pl.pallas_call(
        partial(whole_kernel, NAMES + list(table), rows, large, small),
        out_shape=(
            jax.ShapeDtypeStruct((ROWS, LANES), jnp.bfloat16),
            jax.ShapeDtypeStruct((ROWS, LANES), jnp.float32),
            jax.ShapeDtypeStruct((MODULES * weight_rows // count, LANES), jnp.float32),
            tables,
            tables,
        ),
        in_specs=[vmem, vmem, hbm, vmem, vmem, smem],
        out_specs=(vmem, vmem, hbm, vmem, vmem),
        scratch_shapes=list(table.values()),
        compiler_params=pltpu.CompilerParams(
            collective_id=0, has_side_effects=True, vmem_limit_bytes=62 * 1024 * 1024
        ),
    )(x, cot, w, gains, shifts, kinds)


def leave_kernel(*refs):
    for source, goal in zip(refs[:5], refs[5:]):
        goal[...] = source[...]


def leave_call(arrays):
    vmem = pl.BlockSpec(memory_space=pltpu.VMEM)
    return pl.pallas_call(
        leave_kernel,
        out_shape=tuple(jax.ShapeDtypeStruct(array.shape, array.dtype) for array in arrays),
        in_specs=[vmem] * 5,
        out_specs=(vmem,) * 5,
    )(*arrays)


def on_device_grouped(features, weights, gains, shifts, cotangent, size_group):
    count = lax.axis_size("crops")
    large = count // 4
    weight_rows = weights.shape[2] // LANES
    results = whole_call(
        group_rows(count),
        large,
        count - large,
        features[0],
        cotangent[0],
        weights[0]
        .reshape(MODULES, weight_rows, LANES)
        .transpose(1, 0, 2)
        .reshape(MODULES * weight_rows, LANES),
        gains[0],
        shifts[0],
        size_group,
    )
    out, grad, weight_grad, gain, shift = leave_call(results)
    share = weight_rows // count
    weight_grad = weight_grad.reshape(share, MODULES, LANES).transpose(1, 0, 2)
    weight_grad = with_layout_constraint(weight_grad, Layout((1, 0, 2)))
    return (
        out[None],
        grad[None],
        weight_grad.reshape(1, MODULES, share * LANES),
        gain[None],
        shift[None],
    )


def group_rows(count):
    large = count // 4
    rows = max(large * (LH // 8) * (LW // 8), (count - large) * (SH // 8) * (SW // 8))
    return -(-rows // 16) * 16


def fits(count):
    return count % 8 == 0 and group_rows(count) <= 96


def solution(mesh):
    placed = (
        P("branch", "crops", None),
        P("branch", None, None),
        P("branch", None, None, None),
        P("branch", None, None, None),
        P("branch", "crops", None),
        P(),
    )
    return jax.shard_map(
        on_device_grouped if fits(mesh.shape["crops"]) else on_device,
        mesh=mesh,
        in_specs=placed,
        out_specs=(
            P("branch", "crops", None),
            P("branch", "crops", None),
            P("branch", None, "crops"),
            P("branch", None, None, "crops"),
            P("branch", None, None, "crops"),
        ),
        check_vma=False,
    )
```

```python
from functools import partial
from types import SimpleNamespace
import math

import jax
import jax.numpy as jnp
import numpy as np
from jax import lax
from jax.experimental import pallas as pl
from jax.experimental.layout import Layout, with_layout_constraint
from jax.experimental.pallas import tpu as pltpu
from jax.sharding import PartitionSpec as P

C0 = 32
BLOCKS = 1
MODULES = 2
CROPS_DEV = 1
SH = 32
SW = 24
LH = 64
LW = 48
ROWS = 768
MSG_ROWS = 384


EPS = 1e-05


def as_sent(x):

    def short(part):
        return part.astype(jnp.bfloat16) if part.dtype == jnp.float32 else part

    return jax.tree.map(short, x)


def sender_plan(branch_index, top_channels, blocks):
    channels = top_channels << branch_index
    operations = []
    for block_index in range(blocks):
        operations.append(
            SimpleNamespace(
                phase=2 * block_index,
                source=("h", block_index),
                level=branch_index,
                cin=channels,
                cout=channels,
                stride=1,
                taps=3,
                act="silu",
                output=("u", block_index),
                skip=None,
                dest=-1,
            )
        )
        operations.append(
            SimpleNamespace(
                phase=2 * block_index + 1,
                source=("u", block_index),
                level=branch_index,
                cin=channels,
                cout=channels,
                stride=1,
                taps=3,
                act="res",
                output=("h", block_index + 1),
                skip=("h", block_index),
                dest=-1,
            )
        )
    top_name = ("h", blocks)
    for target in range(branch_index):
        operations.append(
            SimpleNamespace(
                phase=2 * blocks,
                source=top_name,
                level=branch_index,
                cin=channels,
                cout=top_channels << target,
                stride=1,
                taps=1,
                act="none",
                output=None,
                skip=None,
                dest=target,
            )
        )
    for target in range(branch_index + 1, 4):
        for depth_step in range(1, target - branch_index + 1):
            is_last = depth_step == target - branch_index
            operations.append(
                SimpleNamespace(
                    phase=2 * blocks + depth_step - 1,
                    source=top_name if depth_step == 1 else ("chain", target, depth_step - 1),
                    level=branch_index + depth_step,
                    cin=channels,
                    cout=top_channels << target if is_last else channels,
                    stride=2,
                    taps=3,
                    act="none" if is_last else "silu",
                    output=None if is_last else ("chain", target, depth_step),
                    skip=None,
                    dest=target if is_last else -1,
                )
            )
    for position, operation in enumerate(operations):
        operation.slot = position
        operation.size = (
            operation.taps * operation.taps * operation.cin * operation.cout
        )
        if operation.taps == 1:
            operation.kshape = (operation.cin, operation.cout)
        else:
            operation.kshape = (3, 3, operation.cin, operation.cout)
    return operations


def phase_lengths(top_channels, blocks):
    phase_count = 2 * blocks + 3
    lengths = [0] * phase_count
    for branch_index in range(4):
        per_phase = [0] * phase_count
        for operation in sender_plan(branch_index, top_channels, blocks):
            per_phase[operation.phase] += operation.size
        lengths = [max(current, candidate) for current, candidate in zip(lengths, per_phase)]
    return lengths


def weighted_plan(branch_index, top_channels, blocks):
    lengths = phase_lengths(top_channels, blocks)
    starts = [sum(lengths[:phase_index]) for phase_index in range(len(lengths))]
    running = [0] * len(lengths)
    operations = sender_plan(branch_index, top_channels, blocks)
    for operation in operations:
        phase_index = operation.phase
        operation.inner = running[phase_index]
        operation.offset = starts[phase_index] + running[phase_index]
        operation.position = sum(
            (1 for earlier in operations[: operation.slot] if earlier.phase == phase_index)
        )
        running[phase_index] += operation.size
    return operations


def phase_operations(branch_index, phase_index):
    return [
        operation
        for operation in weighted_plan(branch_index, C0, BLOCKS)
        if operation.phase == phase_index
    ]


def input_names(operations):
    source_names = []
    for operation in operations:
        if operation.source not in source_names:
            source_names.append(operation.source)
    return source_names


def silu_slope(value):
    sigmoid = jax.nn.sigmoid(value)
    return sigmoid * (1.0 + value * (1.0 - sigmoid))


def crop_cells(size_kind):
    return (LH, LW) if size_kind else (SH, SW)


def map_dims(size_kind, level, channels):
    height, breadth = crop_cells(size_kind)
    return (CROPS_DEV, height >> level, breadth >> level, channels)


def source_dims(branch_index, size_kind, map_name):
    level = branch_index + map_name[2] if map_name[0] == "chain" else branch_index
    return map_dims(size_kind, level, C0 << branch_index)


def preact_dims(size_kind, operation):
    return map_dims(size_kind, operation.level, operation.cout)


def to_canvas(arrays, value_type):
    if not arrays:
        return jnp.zeros((ROWS, 128), value_type)
    flattened = jnp.concatenate([array.reshape(-1).astype(value_type) for array in arrays])
    return jnp.pad(flattened, (0, ROWS * 128 - flattened.shape[0])).reshape(ROWS, 128)


def from_canvas(canvas, dims_list):
    flattened = canvas.reshape(-1)
    pieces = []
    offset = 0
    for dims_entry in dims_list:
        count_here = math.prod(dims_entry)
        pieces.append(flattened[offset : offset + count_here].reshape(dims_entry))
        offset += count_here
    return pieces


def to_slot(array):
    flattened = array.reshape(-1)
    return jnp.pad(flattened, (0, MSG_ROWS * 128 - flattened.shape[0])).reshape(MSG_ROWS, 128)


def from_slot(slot_rows, dims_entry):
    return slot_rows.reshape(-1)[: math.prod(dims_entry)].reshape(dims_entry)


def upsample(message, factor):
    crop_count, height, breadth, channels = message.shape
    widened = jnp.broadcast_to(
        message[:, :, None, :, None, :], (crop_count, height, factor, breadth, factor, channels)
    )
    return widened.reshape(crop_count, height * factor, breadth * factor, channels)


def block_pool(array, factor):
    crop_count, height, breadth, channels = array.shape
    return array.reshape(
        crop_count, height // factor, factor, breadth // factor, factor, channels
    ).sum(axis=(2, 4))


def kernel_piece(module_weights, operation):
    start = operation.offset
    return module_weights[start : start + operation.size].reshape(operation.kshape)


def conv_forward(operation, source, kernel):
    if operation.taps == 1:
        return jnp.einsum("nhwc,cd->nhwd", source, kernel, preferred_element_type=jnp.float32)
    stride = operation.stride
    return lax.conv_general_dilated(
        source,
        kernel,
        (stride, stride),
        ((1, 1), (1, 1)),
        dimension_numbers=("NHWC", "HWIO", "NHWC"),
        preferred_element_type=jnp.float32,
    )


def conv_backward(operation, source, kernel, upstream):
    if operation.taps == 1:
        source_grad = jnp.einsum(
            "nhwd,cd->nhwc", upstream, kernel, preferred_element_type=jnp.float32
        )
        kernel_grad = jnp.einsum(
            "nhwc,nhwd->cd", source, upstream, preferred_element_type=jnp.float32
        )
        return (source_grad, kernel_grad)
    stride = operation.stride
    flipped = jnp.transpose(kernel[::-1, ::-1], (0, 1, 3, 2))
    high_pad = 2 if stride == 2 else 1
    source_grad = lax.conv_general_dilated(
        upstream,
        flipped,
        (1, 1),
        ((1, high_pad), (1, high_pad)),
        lhs_dilation=(stride, stride),
        dimension_numbers=("NHWC", "HWIO", "NHWC"),
        preferred_element_type=jnp.float32,
    )
    kernel_grad = lax.conv_general_dilated(
        source,
        upstream,
        (1, 1),
        ((1, 2 - stride), (1, 2 - stride)),
        rhs_dilation=(stride, stride),
        dimension_numbers=("CHWN", "IHWO", "NHWC"),
        preferred_element_type=jnp.float32,
    )
    return (source_grad, jnp.transpose(kernel_grad, (1, 2, 0, 3)))


def cell_total(counts, size_kind, level):
    height, breadth = crop_cells(size_kind)
    return counts[size_kind] * float(CROPS_DEV * (height >> level) * (breadth >> level))


def norm_terms(totals, counts, size_kind, operation):
    cells_here = cell_total(counts, size_kind, operation.level)
    channels = operation.cout
    position = operation.position
    average = totals[size_kind, 0, position, :channels] / cells_here
    variance = totals[size_kind, 1, position, :channels] / cells_here - average * average
    return (average, lax.rsqrt(variance + EPS))


def forward_conv(branch_index, size_kind, phase_index, source_canvas, module_weights):
    operations = phase_operations(branch_index, phase_index)
    source_names = input_names(operations)
    pieces = from_canvas(
        source_canvas, [source_dims(branch_index, size_kind, map_name) for map_name in source_names]
    )
    sources = {
        map_name: piece.astype(jnp.bfloat16) for map_name, piece in zip(source_names, pieces)
    }
    preacts = []
    totals = jnp.zeros((2, 2, 3, 8 * C0), jnp.float32)
    for operation in operations:
        preact = conv_forward(
            operation, sources[operation.source], kernel_piece(module_weights, operation)
        )
        preacts.append(preact)
        channels = operation.cout
        position = operation.position
        totals = totals.at[size_kind, 0, position, :channels].set(jnp.sum(preact, axis=(0, 1, 2)))
        totals = totals.at[size_kind, 1, position, :channels].set(
            jnp.sum(preact * preact, axis=(0, 1, 2))
        )
    return (to_canvas(preacts, jnp.float32), totals)


def forward_norm(
    branch_index,
    size_kind,
    phase_index,
    preact_canvas,
    totals,
    counts,
    module_gains,
    module_shifts,
    skip_canvas,
    message_buffer,
):
    operations = phase_operations(branch_index, phase_index)
    preacts = from_canvas(
        preact_canvas, [preact_dims(size_kind, operation) for operation in operations]
    )
    skip_map = from_canvas(skip_canvas, [map_dims(size_kind, branch_index, C0 << branch_index)])[0]
    produced = []
    for operation, preact in zip(operations, preacts):
        average, inverse_std = norm_terms(totals, counts, size_kind, operation)
        norm_slot = operation.slot
        channels = operation.cout
        normed = (preact - average) * inverse_std * module_gains[
            norm_slot, :channels
        ] + module_shifts[norm_slot, :channels]
        if operation.act == "silu":
            produced.append(jax.nn.silu(normed))
        elif operation.act == "res":
            produced.append(jax.nn.silu(normed + skip_map))
        else:
            message_buffer = message_buffer.at[operation.dest].set(
                to_slot(normed.astype(jnp.bfloat16))
            )
    return (to_canvas(produced, jnp.float32), message_buffer)


def receive_forward(branch_index, size_kind, top_canvas, received):
    channels = C0 << branch_index
    summed = from_canvas(top_canvas, [map_dims(size_kind, branch_index, channels)])[0]
    for sender in range(4):
        if sender < branch_index:
            summed = summed + from_slot(
                received[sender], map_dims(size_kind, branch_index, channels)
            ).astype(jnp.float32)
        elif sender > branch_index:
            coarse = from_slot(received[sender], map_dims(size_kind, sender, channels))
            summed = summed + upsample(coarse, 2 ** (sender - branch_index)).astype(jnp.float32)
    return (to_canvas([jax.nn.silu(summed)], jnp.float32), to_canvas([summed], jnp.float32))


def receive_backward(branch_index, size_kind, grad_canvas, summed_canvas):
    dims_here = map_dims(size_kind, branch_index, C0 << branch_index)
    upstream = from_canvas(grad_canvas, [dims_here])[0]
    summed = from_canvas(summed_canvas, [dims_here])[0]
    summed_grad = upstream * silu_slope(summed)
    buffer = jnp.zeros((4, MSG_ROWS, 128), jnp.bfloat16)
    for sender in range(4):
        if sender < branch_index:
            buffer = buffer.at[sender].set(to_slot(summed_grad.astype(jnp.bfloat16)))
        elif sender > branch_index:
            pooled = block_pool(summed_grad, 2 ** (sender - branch_index))
            buffer = buffer.at[sender].set(to_slot(pooled.astype(jnp.bfloat16)))
    return (to_canvas([summed_grad], jnp.float32), buffer)


def backward_stats(
    branch_index,
    size_kind,
    phase_index,
    dout_canvas,
    message_grads,
    preact_canvas,
    totals,
    counts,
    module_gains,
    module_shifts,
    skip_canvas,
):
    operations = phase_operations(branch_index, phase_index)
    preacts = from_canvas(
        preact_canvas, [preact_dims(size_kind, operation) for operation in operations]
    )
    producing = [operation for operation in operations if operation.act != "none"]
    output_grads = from_canvas(
        dout_canvas, [preact_dims(size_kind, operation) for operation in producing]
    )
    grads_by_name = {
        operation.output: piece for operation, piece in zip(producing, output_grads)
    }
    skip_map = from_canvas(skip_canvas, [map_dims(size_kind, branch_index, C0 << branch_index)])[0]
    upstreams = []
    skip_grads = []
    sums_local = jnp.zeros((2, 2, 3, 8 * C0), jnp.float32)
    for operation, preact in zip(operations, preacts):
        average, inverse_std = norm_terms(totals, counts, size_kind, operation)
        norm_slot = operation.slot
        channels = operation.cout
        centered = (preact - average) * inverse_std
        normed = centered * module_gains[norm_slot, :channels] + module_shifts[norm_slot, :channels]
        if operation.act == "silu":
            upstream = grads_by_name[operation.output] * silu_slope(normed)
        elif operation.act == "res":
            upstream = grads_by_name[operation.output] * silu_slope(normed + skip_map)
            skip_grads.append(upstream)
        else:
            upstream = from_slot(
                message_grads[operation.dest], preact_dims(size_kind, operation)
            ).astype(jnp.float32)
        upstreams.append(upstream)
        position = operation.position
        sums_local = sums_local.at[size_kind, 0, position, :channels].set(
            jnp.sum(upstream, axis=(0, 1, 2))
        )
        sums_local = sums_local.at[size_kind, 1, position, :channels].set(
            jnp.sum(upstream * centered, axis=(0, 1, 2))
        )
    return (to_canvas(upstreams, jnp.float32), sums_local, to_canvas(skip_grads, jnp.float32))


def backward_apply(
    branch_index,
    size_kind,
    phase_index,
    upstream_canvas,
    preact_canvas,
    totals,
    grad_totals,
    counts,
    source_canvas,
    module_weights,
    module_gains,
):
    operations = phase_operations(branch_index, phase_index)
    preacts = from_canvas(
        preact_canvas, [preact_dims(size_kind, operation) for operation in operations]
    )
    upstreams = from_canvas(
        upstream_canvas, [preact_dims(size_kind, operation) for operation in operations]
    )
    source_names = input_names(operations)
    source_list = [source_dims(branch_index, size_kind, map_name) for map_name in source_names]
    pieces = from_canvas(source_canvas, source_list)
    sources = {
        map_name: piece.astype(jnp.bfloat16) for map_name, piece in zip(source_names, pieces)
    }
    source_grads = {
        map_name: jnp.zeros(dims_entry, jnp.float32)
        for map_name, dims_entry in zip(source_names, source_list)
    }
    kernel_grads = []
    slot_count = module_gains.shape[0]
    gain_part = jnp.zeros((slot_count, 8 * C0), jnp.float32)
    shift_part = jnp.zeros((slot_count, 8 * C0), jnp.float32)
    for operation, preact, upstream in zip(operations, preacts, upstreams):
        average, inverse_std = norm_terms(totals, counts, size_kind, operation)
        cells_here = cell_total(counts, size_kind, operation.level)
        norm_slot = operation.slot
        channels = operation.cout
        position = operation.position
        centered = (preact - average) * inverse_std
        mean_upstream = grad_totals[size_kind, 0, position, :channels] / cells_here
        mean_cross = grad_totals[size_kind, 1, position, :channels] / cells_here
        preact_grad = (
            module_gains[norm_slot, :channels]
            * inverse_std
            * (upstream - mean_upstream - centered * mean_cross)
        )
        source_grad, kernel_grad = conv_backward(
            operation,
            sources[operation.source],
            kernel_piece(module_weights, operation),
            preact_grad.astype(jnp.bfloat16),
        )
        source_grads[operation.source] = source_grads[operation.source] + source_grad
        kernel_grads.append(kernel_grad.reshape(-1))
        gain_part = gain_part.at[norm_slot, :channels].set(
            grad_totals[0, 1, position, :channels] + grad_totals[1, 1, position, :channels]
        )
        shift_part = shift_part.at[norm_slot, :channels].set(
            grad_totals[0, 0, position, :channels] + grad_totals[1, 0, position, :channels]
        )
    phase_length = phase_lengths(C0, BLOCKS)[phase_index]
    if kernel_grads:
        joined = jnp.concatenate(kernel_grads)
        weight_part = jnp.pad(joined, (0, phase_length - joined.shape[0]))
    else:
        weight_part = jnp.zeros((phase_length,), jnp.float32)
    return (
        to_canvas([source_grads[map_name] for map_name in source_names], jnp.float32),
        weight_part,
        gain_part,
        shift_part,
    )


def on_device(features, weights, gains, shifts, cotangent, size_group):
    crop_shard = lax.axis_index("crops")
    shard_count = lax.axis_size("crops")
    crop_kind = size_group[crop_shard]
    large_count = jnp.sum(size_group).astype(jnp.float32)
    counts = jnp.stack([shard_count - large_count, large_count])
    case_index = lax.axis_index("branch") * 2 + crop_kind
    phase_total = 2 * BLOCKS + 3
    zero_canvas = jnp.zeros((ROWS, 128), jnp.float32)
    empty_buffer = jnp.zeros((4, MSG_ROWS, 128), jnp.bfloat16)

    def run_phase(function, statics, operands):
        branches_list = [
            partial(function, branch_index, size_kind, *statics)
            for branch_index in range(4)
            for size_kind in range(2)
        ]
        return lax.switch(case_index, branches_list, *operands)

    def statistics(local_totals):
        return lax.psum(local_totals, "crops")

    def module_forward(module, start_canvas, kept):
        module_weights = weights[0, module]
        module_gains = gains[0, module]
        module_shifts = shifts[0, module]
        record = SimpleNamespace(sources=[], preacts=[], totals=[])
        h_canvas = start_canvas
        u_canvas = zero_canvas
        chain_canvas = zero_canvas
        buffer = empty_buffer
        for phase_index in range(phase_total):
            if phase_index < 2 * BLOCKS:
                source = h_canvas if phase_index % 2 == 0 else u_canvas
            elif phase_index == 2 * BLOCKS:
                source = h_canvas
            else:
                source = chain_canvas
            preact, local_totals = run_phase(forward_conv, (phase_index,), (source, module_weights))
            global_totals = kept.totals[phase_index] if kept else statistics(local_totals)
            produced, buffer = run_phase(
                forward_norm,
                (phase_index,),
                (preact, global_totals, counts, module_gains, module_shifts, h_canvas, buffer),
            )
            record.sources.append(source)
            record.preacts.append(preact)
            record.totals.append(global_totals)
            if phase_index < 2 * BLOCKS:
                if phase_index % 2 == 0:
                    u_canvas = produced
                else:
                    h_canvas = produced
            else:
                chain_canvas = produced
        received = (
            kept.received
            if kept
            else jax.tree.map(
                lambda part, own: part.astype(own.dtype),
                lax.all_to_all(as_sent(buffer), "branch", split_axis=0, concat_axis=0, tiled=True),
                buffer,
            )
        )
        result, summed = run_phase(receive_forward, (), (h_canvas, received))
        record.summed = summed
        record.received = received
        return (result, record)

    checkpoints = [features[0].astype(jnp.float32)]
    first_records = []
    for module in range(MODULES):
        result, record = module_forward(module, checkpoints[-1], None)
        checkpoints.append(result)
        first_records.append(record)
    outputs = checkpoints[-1].astype(jnp.bfloat16)
    grad_canvas = cotangent[0].astype(jnp.float32)
    module_grads = [None] * MODULES
    gain_grads = [None] * MODULES
    shift_grads = [None] * MODULES
    for module in reversed(range(MODULES)):
        kept = None
        unused_result, record = module_forward(module, checkpoints[module], kept)
        module_module_weights = weights[0, module]
        module_module_gains = gains[0, module]
        module_module_shifts = shifts[0, module]
        summed_grad, back_buffer = run_phase(receive_backward, (), (grad_canvas, record.summed))
        message_grads = jax.tree.map(
            lambda part, own: part.astype(own.dtype),
            lax.all_to_all(as_sent(back_buffer), "branch", split_axis=0, concat_axis=0, tiled=True),
            back_buffer,
        )
        top_grad = summed_grad
        chain_grad = zero_canvas
        u_grad = zero_canvas
        pending_skip = zero_canvas
        weight_parts = [None] * phase_total
        gain_total = jnp.zeros(gains.shape[2:], jnp.float32)
        shift_total = jnp.zeros(gains.shape[2:], jnp.float32)
        for module_phase_index in reversed(range(phase_total)):
            if module_phase_index >= 2 * BLOCKS:
                output_grad = chain_grad
                skip_canvas = zero_canvas
            elif module_phase_index % 2 == 1:
                output_grad = top_grad
                skip_canvas = record.sources[module_phase_index - 1]
            else:
                output_grad = u_grad
                skip_canvas = zero_canvas
            module_preact = record.preacts[module_phase_index]
            totals = record.totals[module_phase_index]
            upstream, module_local_totals, skip_grad = run_phase(
                backward_stats,
                (module_phase_index,),
                (
                    output_grad,
                    message_grads,
                    module_preact,
                    totals,
                    counts,
                    module_module_gains,
                    module_module_shifts,
                    skip_canvas,
                ),
            )
            grad_totals = lax.psum(module_local_totals, "crops")
            source_grad, weight_parts[module_phase_index], gain_part, shift_part = run_phase(
                backward_apply,
                (module_phase_index,),
                (
                    upstream,
                    module_preact,
                    totals,
                    grad_totals,
                    counts,
                    record.sources[module_phase_index],
                    module_module_weights,
                    module_module_gains,
                ),
            )
            gain_total = gain_total + gain_part
            shift_total = shift_total + shift_part
            if module_phase_index > 2 * BLOCKS:
                chain_grad = source_grad
            elif module_phase_index == 2 * BLOCKS:
                top_grad = top_grad + source_grad
            elif module_phase_index % 2 == 1:
                u_grad = source_grad
                pending_skip = skip_grad
            else:
                top_grad = source_grad + pending_skip
        joined = jnp.concatenate(weight_parts)
        weight_grad = jnp.pad(joined, (0, weights.shape[2] - joined.shape[0]))
        grad_canvas, weight_grad, gain_grads[module], shift_grads[module] = (
            top_grad,
            weight_grad,
            gain_total,
            shift_total,
        )
        module_grads[module] = weight_grad
    weight_out = lax.psum_scatter(jnp.stack(module_grads), "crops", scatter_dimension=1, tiled=True)
    share = gains.shape[3] // shard_count
    gain_out = lax.dynamic_slice_in_dim(jnp.stack(gain_grads), crop_shard * share, share, axis=2)
    shift_out = lax.dynamic_slice_in_dim(jnp.stack(shift_grads), crop_shard * share, share, axis=2)
    return (outputs[None], grad_canvas[None], weight_out[None], gain_out[None], shift_out[None])


LANES = 128
SLOTS = 8
MASKS = 7
DOWN = (((1,), (0,)), ((), ()))
ACROSS = (((1,), (1,)), ((), ()))
ALONG = (((0,), (0,)), ((), ()))


def unit_table(k):
    operations = weighted_plan(k, C0, BLOCKS)
    planes = 8 >> k
    channels = C0 << k
    units = {}
    stat = 0

    def add(name, kind, source, lanes_in, planes_in, planes_out, members):
        nonlocal stat
        segs = []
        tile = 0
        for operation, lanes, chain in members:
            cout = operation.cout
            level = operation.level if operation.taps == 3 else operation.dest
            segs.append(
                SimpleNamespace(
                    slot=operation.slot,
                    off=operation.offset // LANES,
                    cin=operation.cin,
                    cout=cout,
                    taps=operation.taps,
                    tile=tile,
                    tiles=lanes // LANES,
                    blocks=max(1, (8 >> level)),
                    dest=operation.dest,
                    act=operation.act,
                    chain=chain,
                    up=k - operation.dest if operation.taps == 1 else 0,
                )
            )
            tile += lanes // LANES
        rows = {"s1": (384, 384, 512, 768)[k], "s2": lanes_in + LANES, "p1": 256}[kind]
        units[name] = SimpleNamespace(
            name=name,
            kind=kind,
            source=source,
            lanes_in=lanes_in,
            blocks_in=planes_in,
            planes_in=planes_in,
            planes=planes_out,
            segs=segs,
            tiles=tile,
            rows=rows,
            stat=stat,
            depth=1 if kind == "p1" else 3,
        )
        stat += tile

    add("a", "s1", "h", 256, planes, planes, [(operations[0], 256, None)])
    add("b", "s1", "u", 256, planes, planes, [(operations[1], 256, None)])
    ups = [operation for operation in operations if operation.taps == 1]
    if ups:
        add("u", "p1", "t", 256, planes, planes, [(operation, 256, None) for operation in ups])
    firsts, chains = [], {}
    for target in range(k + 1, 4):
        steps = [
            operation
            for operation in operations
            if operation.taps == 3 and operation.stride == 2
        ]
        start = sum(i - k for i in range(k + 1, target))
        chains[target] = steps[start : start + target - k]
        if target == k + 1:
            firsts.append((chains[target][0], 256, None))
        else:
            firsts.append((chains[target][0], LANES, "c1" if target == k + 2 else "c2"))
    if firsts:
        add("d", "s2", "t", 256, planes, planes // 2, firsts)
    if k <= 1:
        add("e", "s2", "c1", LANES, planes // 2, planes // 4, [(chains[k + 2][1], 256, None)])
    if k == 0:
        add("f", "s2", "c2", LANES, planes // 2, planes // 4, [(chains[3][1], LANES, "c3")])
        add("g", "s2", "c3", LANES, planes // 4, planes // 8, [(chains[3][2], 256, None)])
    return units


def links(k, unit, seg):
    cin = seg.cin
    count_in, count_out = unit.blocks_in, seg.blocks
    found = []
    if unit.kind == "p1":
        for plane in range(count_in):
            wide = 1 << seg.up
            found.append((plane * cin, 0, set(range(plane * wide, plane * wide + wide))))
        return found
    if unit.kind == "s1" and k == 3:
        return [(256 * tap, tap, {0}) for tap in range(3)]
    stride = 1 if unit.kind == "s1" else 2
    for plane in range(count_in):
        for tap in range(3):
            at = plane - tap + 1
            if at % stride == 0 and 0 <= at // stride < count_out:
                found.append((plane * cin, tap, {at // stride}))
    if stride == 1:
        found.append((256, 2, {count_out - 1}))
        found.append((unit.rows - cin, 0, {0}))
    else:
        lanes_in = unit.lanes_in
        found.append((lanes_in + (count_in - 1) * cin - (lanes_in - LANES), 0, {0}))
    return found


def message_slot(k, other):
    return sum(2 * (8 >> max(k, before)) for before in range(other) if before != k)


def log2(value):
    return value.bit_length() - 1


def sigmoid_of(value):
    return 0.5 * jnp.tanh(0.5 * value) + 0.5


def silu_of(value):
    return value * sigmoid_of(value)


def slope_of(value):
    sigmoid = sigmoid_of(value)
    return sigmoid * (1.0 + value * (1.0 - sigmoid))


def planes_loop(count, body, turns=1):
    def step(index, carry):
        for turn in range(turns):
            body(index * turns + turn)
        return carry

    turns = min(turns, count)
    if count == turns:
        for index in range(count):
            body(index)
    else:
        lax.fori_loop(0, count // turns, step, 0)


def planes_sum(count, body, initial, turns=1):
    def step(index, carry):
        for turn in range(turns):
            carry = body(index * turns + turn, carry)
        return carry

    turns = min(turns, count)
    if count == turns:
        return step(0, initial)
    return lax.fori_loop(0, count // turns, step, initial)


def partial_sum(value):
    rows = value.shape[0]
    return jnp.sum(value.reshape(rows // 8, 8, value.shape[1]), axis=0)


class Planes:
    def __init__(self, mode, tiles, planes, masks, rows, main, edge=None, right=None, narrow=False):
        self.narrow, self.pending = narrow, None
        self.mode, self.tiles, self.planes = mode, tiles, planes
        self.masks, self.rows = masks, rows
        self.main, self.edge, self.right = main, edge, right
        self.base = 1 if mode in ("s1", "wide", "s2") else 0
        extra = {"s1": 2, "wide": 2, "s2": 1, "dz2": 1, "p": 0}[mode]
        self.span = planes + extra
        self.unit = tiles * self.span

    def at(self, m, tile, plane):
        return m * self.unit + tile * self.span + plane + self.base

    def edge_at(self, m, tile, plane):
        if self.mode == "s2" or self.narrow:
            return m * self.span + plane + self.base
        return self.at(m, tile, plane)

    def from_left(self, value):
        return pltpu.roll(value, 1, 0) * self.masks[1]

    def from_right(self, value):
        return pltpu.roll(value, self.rows - 1, 0) * self.masks[2]

    def store(self, m, tile, plane, value):
        self.put(m, tile, plane, value)

    def put(self, m, tile, plane, value):
        where = self.at(m, tile, plane)
        self.main[where] = value.astype(jnp.bfloat16)
        if self.mode == "s1":
            side = self.from_right(value) if tile == 0 else self.from_left(value)
            if not self.narrow:
                self.edge[where] = side.astype(jnp.bfloat16)
            elif tile == 0:
                self.pending = side
            else:
                lane = lax.broadcasted_iota(jnp.int32, side.shape, 1)
                side = jnp.where(lane < LANES // 2, self.pending, side)
                self.edge[self.edge_at(m, tile, plane)] = side.astype(jnp.bfloat16)
        elif self.mode == "wide":
            self.edge[where] = self.from_left(value).astype(jnp.bfloat16)
            self.right[where] = self.from_right(value).astype(jnp.bfloat16)
        elif self.mode == "s2":
            if tile == self.tiles - 1:
                self.edge[self.edge_at(m, tile, plane)] = self.from_left(value).astype(jnp.bfloat16)
        elif self.mode == "dz2":
            self.edge[where] = self.from_right(value).astype(jnp.bfloat16)

    def put_above(self, m, tile, last):
        if self.mode in ("s1", "wide", "s2"):
            above = pltpu.roll(last, 6, 0) * self.masks[3] + pltpu.roll(last, 3, 0) * self.masks[4]
            self.put(m, tile, -1, above)

    def put_below(self, m, tile, first):
        if self.mode in ("s1", "wide", "dz2"):
            rows = self.rows
            below = (
                pltpu.roll(first, rows - 6, 0) * self.masks[5]
                + pltpu.roll(first, rows - 3, 0) * self.masks[6]
            )
            self.put(m, tile, self.planes, below)

    def close(self, m):
        for tile in range(self.tiles):
            last = self.main[self.at(m, tile, self.planes - 1)].astype(jnp.float32)
            self.put_above(m, tile, last)
        for tile in range(self.tiles):
            first = self.main[self.at(m, tile, 0)].astype(jnp.float32)
            self.put_below(m, tile, first)


class Branch:
    def __init__(self, k, rows, large, small, share, refs, masks, core):
        self.k, self.rows, self.refs, self.masks = k, rows, refs, masks
        self.units = unit_table(k)
        self.planes = 8 >> k
        self.core = core
        self.large, self.small, self.count = large, small, large + small
        self.cells = (small * (SH // 8) * (SW // 8), large * (LH // 8) * (LW // 8))
        self.quarter = lax.axis_index("crops") // 2
        self.share = share
        r = refs
        make = partial(Planes, masks=masks, rows=rows)
        make_one = partial(make, narrow=k <= 1)
        one = "wide" if k == 3 else "s1"
        self.maps = dict(
            h=make_one(one, 2, self.planes, main=r.hC, edge=r.hE, right=r.hR),
            u=make_one(one, 2, self.planes, main=r.uC, edge=r.uE, right=r.uR),
            t=make("p" if k == 3 else "s2", 2, self.planes, main=r.tC, edge=r.tE),
        )
        if k <= 1:
            self.maps["c1"] = make("s2", 1, self.planes // 2, main=r.c1C, edge=r.c1E)
        if k == 0:
            self.maps["c2"] = make("s2", 1, 4, main=r.c2C, edge=r.c2E)
            self.maps["c3"] = make("s2", 1, 2, main=r.c3C, edge=r.c3E)
        self.grads = dict(t=r.gt, u=r.gu, c1=r.gc1, c2=r.gc2, c3=r.gc3)

    def lane_block(self, shape, cout):
        lanes = lax.broadcasted_iota(jnp.int32, shape, 1)
        return lanes >> log2(cout)

    def keep(self, value, cout, which):
        count = LANES // cout
        if len(which) == count:
            return value
        block = self.lane_block(value.shape, cout)
        mask = block == which[0]
        for entry in which[1:]:
            mask = mask | (block == entry)
        return jnp.where(mask, value, 0.0)

    def spread(self, value, cout):
        shift = LANES // 2
        while shift >= cout:
            value = value + pltpu.roll(value, shift, 1)
            shift //= 2
        return value

    def local_blocks(self, seg, tile, wanted):
        count = LANES // seg.cout
        return [q for q in range(count) if (tile * count + q) % seg.blocks in wanted]


    def segments(self):
        return [(unit, seg) for unit in self.units.values() for seg in unit.segs]

    def pieces(self):
        found, place = [], 0
        for index, (unit, seg) in enumerate(self.segments()):
            count = 2 * seg.taps**2 * seg.cin * seg.cout // LANES
            if self.k < 3:
                found.append((index, 0, count, place, index))
                place += count
            else:
                for d in range(unit.depth):
                    slot = len(found) % 3
                    found.append((index, d, count // unit.depth, slot * 3072, slot))
        return found

    def fetch(self, at):
        r = self.refs
        index, d, count, place, sem = self.pieces()[at]
        _, seg = self.segments()[index]
        return pltpu.make_async_copy(
            r.w.at[pl.ds(2 * seg.off + d * count, count)],
            r.raw.at[pl.ds(place, count)],
            r.wsem.at[sem],
        )

    def fetch_first(self):
        for at in range(len(self.pieces()) if self.k < 3 else 3):
            self.fetch(at).start()

    def expand(self, index):
        unit, seg = self.segments()[index]
        pieces = self.pieces()
        mine = [at for at, piece in enumerate(pieces) if piece[0] == index]
        if self.k < 3:
            (at,) = mine
            self.fetch(at).wait()
            count = pieces[at][2] // unit.depth
            planes_loop(
                unit.depth,
                lambda d: self.expand_row(unit, seg, d, count, pieces[at][3] + d * count),
            )
        else:
            for d, at in enumerate(mine):
                self.fetch(at).wait()
                self.expand_row(unit, seg, d, pieces[at][2], pieces[at][3])
                if at + 3 < len(pieces):
                    self.fetch(at + 3).start()
        for m in range(MODULES):
            self.spread_tables(m, unit, seg)

    def expand_row(self, unit, seg, d, count, place):
        r = self.refs
        chunk = math.gcd(count, 384)
        wf, rep = r.work, r.rep

        def widen(step):
            at = pl.multiple_of(step * chunk, 16)
            value = r.raw[pl.ds(pl.multiple_of(place + at, 16), chunk)].astype(jnp.float32)
            wf[pl.ds(at, chunk)] = value

        planes_loop(count // chunk, widen)
        count = count // MODULES
        depth, cin, cout = unit.depth, seg.cin, seg.cout
        target = getattr(r, "T" + unit.name)
        twice = unit.kind == "s1" and self.k < 3
        across = getattr(r, "T" + unit.name + unit.name) if twice else None
        by_row = {}
        for row, tap, wanted in links(self.k, unit, seg):
            by_row.setdefault(row, []).append((tap, wanted))

        def module(m):
            if cout < LANES:
                ratio = LANES // cout
                flat = wf[pl.ds(m, count, stride=2)]
                for part in range(ratio):
                    rep[pl.ds(part, count, stride=ratio)] = self.spread(
                        self.keep(flat, cout, [part]), cout
                    )

            def tap_rows(tap, tile):
                if cout < LANES:
                    return rep[tap * cin : (tap + 1) * cin]
                if cout == LANES:
                    return wf[pl.ds(m + tap * (2 * cin), cin, stride=2)]
                return wf[pl.ds(m + tap * (4 * cin) + 2 * tile, cin, stride=4)]

            for tile in range(seg.tiles):
                column = (seg.tile + tile) * LANES
                for row in range(0, unit.rows, cin):
                    total = None
                    for tap, wanted in by_row.get(row, []):
                        if cout <= LANES:
                            local = self.local_blocks(seg, tile, wanted)
                            if not local:
                                continue
                            piece = self.keep(tap_rows(tap, 0), cout, local)
                        else:
                            piece = tap_rows(tap, tile)
                        total = piece if total is None else total + piece
                    if total is None:
                        total = jnp.zeros((cin, LANES), jnp.float32)
                    block = total.astype(jnp.bfloat16)
                    target[m * depth + d, row : row + cin, column : column + LANES] = block

            if not twice:
                return
            turned = []
            if cin == LANES:
                turned = [jnp.transpose(tap_rows(tap, 0)) for tap in range(3)]
            else:
                both = jnp.transpose(rep[0 : -(-3 * cin // LANES) * LANES])
                for tap in range(3):
                    first = tap * cin // LANES * LANES
                    value = both[0:cin, first : first + LANES]
                    value = self.keep(value, cin, [tap * cin % LANES // cin])
                    turned.append(self.spread(value, cin))
            for tile in range(2):
                for row in range(0, unit.rows, cin):
                    total = None
                    for tap, wanted in by_row.get(row, []):
                        local = self.local_blocks(seg, tile, wanted)
                        if local:
                            piece = self.keep(turned[2 - tap], cin, local)
                            total = piece if total is None else total + piece
                    if total is None:
                        total = jnp.zeros((cin, LANES), jnp.float32)
                    column = tile * LANES
                    across[m * depth + d, row : row + cin, column : column + LANES] = total.astype(
                        jnp.bfloat16
                    )

        planes_loop(MODULES, module)


    def parts(self, unit, source):
        if unit.kind == "p1":
            return [(source.main, range(2), source.at)]
        if source.mode == "wide":
            return [
                (source.edge, range(2), source.at),
                (source.main, range(2), source.at),
                (source.right, range(2), source.at),
            ]
        if unit.kind == "s1":
            tiles = [0] if source.narrow else range(2)
            return [(source.main, range(2), source.at), (source.edge, tiles, source.edge_at)]
        last = source.tiles - 1
        return [
            (source.main, range(source.tiles), source.at),
            (source.edge, [last], source.edge_at),
        ]

    def rows_of(self, unit, part, m, d, first, count):
        ref, tiles, at = part
        pieces = []
        for tile in tiles:
            if unit.kind == "s2":
                rows = [ref[at(m, tile, 2 * (first + q) + d - 1)] for q in range(count)]
                pieces.append(rows[0] if count == 1 else jnp.concatenate(rows, axis=0))
            else:
                shift = d - 1 if unit.kind == "s1" else 0
                pieces.append(
                    ref[pl.ds(at(m, tile, first + shift), count)].reshape(count * self.rows, LANES)
                )
        return pieces

    def conv(self, m, unit):
        r = self.refs
        source = self.maps[unit.source]
        target = getattr(r, "T" + unit.name)
        z = getattr(r, "z" + unit.name)
        planes, tiles, depth = unit.planes, unit.tiles, unit.depth
        chunk = min(planes, 4 if tiles <= 2 else 2)
        lanes = tiles * LANES

        def body(step, sums):
            first = step * chunk
            pieces = []
            for d in range(depth):
                for part in self.parts(unit, source):
                    pieces += self.rows_of(unit, part, m, d, first, chunk)
            left = jnp.concatenate(pieces, axis=1)
            right = target[pl.ds(m * depth, depth), 0 : unit.rows, 0:lanes]
            right = right.reshape(depth * unit.rows, lanes)
            result = lax.dot_general(left, right, DOWN, preferred_element_type=jnp.float32)
            for tile in range(tiles):
                block = result[:, tile * LANES : (tile + 1) * LANES]
                z[pl.ds(m * tiles * planes + tile * planes + first, chunk)] = block.reshape(
                    chunk, self.rows, LANES
                )
            return (sums[0] + partial_sum(result), sums[1] + partial_sum(result * result))

        zero = jnp.zeros((8, lanes), jnp.float32)
        sums = planes_sum(planes // chunk, body, (zero, zero), 2)
        for seg in unit.segs:
            scale = self.per_cell(unit, seg)
            totals = self.fold(seg, sums)
            self.norm_rows(m, unit, seg, totals, scale)

    def per_cell(self, unit, seg):
        blocks = seg.tiles * LANES // seg.cout
        small, large = self.cells
        count = unit.planes * blocks
        return jnp.where(self.core == 0, 1.0 / (large * count), 1.0 / (small * count)).astype(
            jnp.float32
        )

    def fold(self, seg, sums):
        first = seg.tile
        found = []
        for value in sums:
            tiles = [
                value[:, (first + t) * LANES : (first + t + 1) * LANES] for t in range(seg.tiles)
            ]
            if seg.cout <= LANES:
                total = tiles[0]
                for tile in tiles[1:]:
                    total = total + tile
                total = jnp.sum(self.spread(total, seg.cout), axis=0, keepdims=True)
                found.append([total] * seg.tiles)
            else:
                found.append([jnp.sum(tile, axis=0, keepdims=True) for tile in tiles])
        return found

    def table_row(self, ref, m, seg, tile):
        slot = seg.slot
        if seg.cout > LANES:
            return ref[m, slot : slot + 1, tile * LANES : (tile + 1) * LANES]
        row = jnp.broadcast_to(ref[m, slot : slot + 1, 0:LANES], (8, LANES))
        if seg.cout < LANES:
            row = self.spread(self.keep(row, seg.cout, [0]), seg.cout)
        return row[0:1]

    def norm_rows(self, m, unit, seg, totals, scale):
        st = self.refs.st
        for tile in range(seg.tiles):
            average = totals[0][tile] * scale
            variance = totals[1][tile] * scale - average * average
            inverse = lax.rsqrt(variance + EPS)
            where = m * STATS + unit.stat + seg.tile + tile
            factor = st[where, 4:5] * inverse
            st[where, 0:1] = average
            st[where, 1:2] = inverse
            st[where, 2:3] = factor
            st[where, 3:4] = st[where, 5:6] - average * factor

    def spread_tables(self, m, unit, seg):
        st = self.refs.st
        for tile in range(seg.tiles):
            where = m * STATS + unit.stat + seg.tile + tile
            st[where, 4:5] = self.table_row(self.refs.gains, m, seg, tile)
            st[where, 5:6] = self.table_row(self.refs.shifts, m, seg, tile)

    def normed(self, m, unit, tile, plane):
        st = self.refs.st
        z = getattr(self.refs, "z" + unit.name)
        where = m * STATS + unit.stat + tile
        value = z[m * unit.tiles * unit.planes + tile * unit.planes + plane]
        return value * st[where, 2:3] + st[where, 3:4]

    def apply_a(self, m):
        unit, u = self.units["a"], self.maps["u"]

        def body(plane):
            for tile in range(2):
                value = silu_of(self.normed(m, unit, tile, plane)) * self.masks[0]
                u.store(m, tile, plane, value)

        planes_loop(self.planes, body, TURNS)
        u.close(m)

    def apply_b(self, m):
        unit, top = self.units["b"], self.maps["t"]
        hf, s = self.refs.hf, self.refs.s

        def body(plane):
            for tile in range(2):
                where = m * 2 * self.planes + tile * self.planes + plane
                value = silu_of(self.normed(m, unit, tile, plane) + hf[where]) * self.masks[0]
                s[where] = value
                top.store(m, tile, plane, value)

        planes_loop(self.planes, body, TURNS)
        top.close(m)

    def apply_rest(self, m, unit):
        sb = self.refs.sb
        for seg in unit.segs:
            chain = self.maps[seg.chain] if seg.chain else None

            def body(plane):
                for tile in range(seg.tiles):
                    value = self.normed(m, unit, seg.tile + tile, plane)
                    if chain is not None:
                        chain.store(m, tile, plane, silu_of(value) * self.masks[0])
                    else:
                        at = message_slot(self.k, seg.dest) + tile * unit.planes + plane
                        sb[at] = value.astype(jnp.bfloat16)

            planes_loop(unit.planes, body, TURNS)
            if chain is not None:
                chain.close(m)
            else:
                self.message(m, seg.dest).start()

    def message(self, e, other):
        count = 2 * (8 >> max(self.k, other))
        r = self.refs
        return pltpu.make_async_remote_copy(
            src_ref=r.sb.at[pl.ds(message_slot(self.k, other), count)],
            dst_ref=r.rb.at[pl.ds(e * 16 + message_slot(other, self.k), count)],
            send_sem=r.ssem.at[e * 4 + other],
            recv_sem=r.rsem.at[e * 4 + self.k],
            device_id=dict(branch=other),
            device_id_type=pl.DeviceIdType.MESH,
        )

    def arrived(self, e, other):
        count = 2 * (8 >> max(self.k, other))
        r = self.refs
        at = message_slot(self.k, other)
        return pltpu.make_async_remote_copy(
            src_ref=r.sb.at[pl.ds(at, count)],
            dst_ref=r.rb.at[pl.ds(e * 16 + at, count)],
            send_sem=r.ssem.at[e * 4 + other],
            recv_sem=r.rsem.at[e * 4 + other],
            device_id=dict(branch=other),
            device_id_type=pl.DeviceIdType.MESH,
        )

    def others(self):
        return [other for other in range(4) if other != self.k]

    def sent(self, e):
        for other in self.others():
            self.message(e, other).wait_send()

    def receive(self, m):
        r = self.refs
        s, rb, hf, out = r.s, r.rb, r.hf, r.outs
        h = self.maps["h"]

        def total_at(tile, plane):
            where = m * 2 * self.planes + tile * self.planes + plane
            total = s[where]
            for other in self.others():
                count = 8 >> max(self.k, other)
                at = plane >> max(0, other - self.k)
                slot = m * 16 + message_slot(self.k, other) + tile * count + at
                total = total + rb[slot].astype(jnp.float32)
            s[where] = total
            return silu_of(total) * self.masks[0]

        def onward(plane):
            for tile in range(2):
                value = total_at(tile, plane)
                hf[(2 + tile) * self.planes + plane] = value
                h.store(1, tile, plane, value)

        def finish(plane):
            for tile in range(2):
                out[tile * self.planes + plane] = total_at(tile, plane).astype(jnp.bfloat16)

        @pl.when(m + 1 < MODULES)
        def _():
            planes_loop(self.planes, onward, TURNS)
            h.close(1)

        @pl.when(m + 1 == MODULES)
        def _():
            planes_loop(self.planes, finish, TURNS)

    def take_feature(self, tile, plane, value):
        self.refs.hf[tile * self.planes + plane] = value
        self.maps["h"].store(0, tile, plane, value)

    def take_cotangent(self, tile, plane, value):
        self.refs.gin[tile * self.planes + plane] = value

    def member(self, kind, order):
        kinds = self.refs.kinds
        found, before = jnp.int32(0), jnp.int32(0)
        for at in range(self.count):
            same = kinds[at] == kind
            found = jnp.where(same & (before == order), at, found)
            before = before + same.astype(jnp.int32)
        return found

    def order(self, device):
        kinds = self.refs.kinds
        kind = kinds[device]
        before = jnp.int32(0)
        for at in range(self.count):
            before = before + ((kinds[at] == kind) & (at < device)).astype(jnp.int32)
        return before

    def unpack(self, t, consume):
        r = self.refs
        work, rows, planes = r.work, self.rows, self.planes
        full = SH * SW * C0 // LANES
        gath = r.gathc if t else r.gathx

        @pl.when(self.core == 0)
        def _():
            for at in range(self.large):
                block = gath[self.member(1, at)]
                work[at * ROWS : (at + 1) * ROWS] = block.astype(jnp.float32)

        @pl.when(self.core == 1)
        def _():
            for at in range(self.small):
                block = gath[self.member(0, at), 0:full]
                work[at * full : (at + 1) * full] = block.astype(jnp.float32)
            work[self.small * full : self.large * ROWS] = jnp.zeros(
                (self.large * ROWS - self.small * full, LANES), jnp.float32
            )

        deep = self.large * ROWS // 2
        right = jnp.concatenate([work[pl.ds(j, deep, stride=2)] for j in range(2)], axis=1)
        right = right.astype(jnp.bfloat16)
        cells = Cells(self.core, (rows, LANES), self.small, self.large)
        base = cells.crop * cells.pick(ROWS // 2, full // 2)
        base = base + cells.along * (planes * cells.wide) + cells.across
        base = jnp.where(cells.valid, base, -(1 << 20))
        lane = lax.broadcasted_iota(jnp.int32, (rows, LANES), 1)
        chunk = min(planes, 4)

        def body(step):
            pieces = []
            for q in range(chunk):
                goal = base + (step * chunk + q) * cells.wide
                pieces.append(one_hot(goal, lane, deep))
            left = pieces[0] if chunk == 1 else jnp.concatenate(pieces, axis=0)
            result = lax.dot_general(left, right, DOWN, preferred_element_type=jnp.float32)
            for q in range(chunk):
                for tile in range(2):
                    value = result[q * rows : (q + 1) * rows, tile * LANES : (tile + 1) * LANES]
                    consume(tile, step * chunk + q, value)

        planes_loop(planes // chunk, body)

    def pack_size(self):
        return 48 * self.planes, -(-self.planes * self.rows // LANES) * LANES

    def plan_pack(self):
        r = self.refs
        high, deep = self.pack_size()
        planes = self.planes
        q = lax.broadcasted_iota(jnp.int32, (high, LANES), 0)
        lane = lax.broadcasted_iota(jnp.int32, (high, LANES), 1)
        wide, tall = jnp.where(self.core == 0, 6, 3), jnp.where(self.core == 0, 8, 4)
        cell = jnp.where(self.core == 0, (q * 43691) >> 18, (q * 43691) >> 17)
        across = q - cell * wide
        plane = cell & (planes - 1)
        along = cell >> log2(planes)
        base = plane * self.rows + along * wide + across
        base = jnp.where(along < tall, base, -(1 << 20))
        shard = lax.axis_index("crops")
        for at, device in enumerate((shard, shard + 1 - 2 * self.core)):
            goal = base + self.order(device) * (wide * tall)
            r.hot[at, 0:high, 0:deep] = one_hot(goal, lane, deep)

    def pack(self, units, put):
        high, deep = self.pack_size()
        right = jnp.concatenate([units(tile) for tile in range(2)], axis=1)
        short = deep - right.shape[0]
        parts = [right.astype(jnp.bfloat16)]
        if right.dtype == jnp.float32:
            parts.append((right - parts[0].astype(jnp.float32)).astype(jnp.bfloat16))
        if short:
            empty = jnp.zeros((short, 2 * LANES), jnp.bfloat16)
            parts = [jnp.concatenate([part, empty], axis=0) for part in parts]
        for at in range(2):
            total = None
            for part in parts:
                piece = lax.dot_general(
                    self.refs.hot[at, 0:high, 0:deep],
                    part,
                    DOWN,
                    preferred_element_type=jnp.float32,
                )
                total = piece if total is None else total + piece
            for tile in range(2):
                put(at, pl.ds(tile, high, stride=2), total[:, tile * LANES : (tile + 1) * LANES])

    def pack_outputs(self):
        r = self.refs
        high = 2 * self.pack_size()[0]

        def put(at, where, value):
            r.work[pl.ds(at * ROWS + where.start, where.size, stride=2)] = value

        def units(tile):
            block = r.outs[tile * self.planes : (tile + 1) * self.planes]
            return block.reshape(self.planes * self.rows, LANES)

        self.pack(units, put)
        for at in range(2):
            r.blocks[at, 0:high] = r.work[at * ROWS : at * ROWS + high].astype(jnp.bfloat16)
            if high < ROWS:
                r.blocks[at, high:ROWS] = jnp.zeros((ROWS - high, LANES), jnp.bfloat16)

    def pack_gradient(self):
        r = self.refs
        high = 2 * self.pack_size()[0]

        def put(at, where, value):
            r.slopes[at, where] = value

        def units(tile):
            block = r.gin[tile * self.planes : (tile + 1) * self.planes]
            return block.reshape(self.planes * self.rows, LANES)

        self.pack(units, put)
        if high < ROWS:
            for at in range(2):
                r.slopes[at, high:ROWS] = jnp.zeros((ROWS - high, LANES), jnp.float32)

    def forward(self, m, gather):
        def also(module, step):
            pl.when(m == module)(lambda: gather.step(1, step))

        self.conv(m, self.units["a"])
        self.apply_a(m)
        self.conv(m, self.units["b"])
        self.apply_b(m)
        also(0, 1)
        also(1, 3)

        @pl.when(m > 0)
        def _():
            self.sent(m - 1)

        for name in ("d", "u", "e", "f", "g"):
            if name in self.units:
                self.conv(m, self.units[name])
                self.apply_rest(m, self.units[name])
        also(0, 2)

        @pl.when(m == MODULES - 1)
        def _():
            gather.collect(1)
            self.unpack(1, self.take_cotangent)

        for other in self.others():
            self.arrived(m, other).wait_recv()
        self.receive(m)


    def send_back(self, m):
        r = self.refs
        s, gin, gt, sb = r.s, r.gin, r.gt, r.sb
        e = MODULES + m

        def body(plane):
            for tile in range(2):
                at = tile * self.planes + plane
                value = gin[at] * slope_of(s[m * 2 * self.planes + at])
                gt[at] = value
                for other in range(self.k):
                    sb[message_slot(self.k, other) + at] = value.astype(jnp.bfloat16)

        planes_loop(self.planes, body, TURNS)
        for other in reversed(self.others()):
            if other > self.k:
                count = 8 >> other
                wide = 1 << (other - self.k)

                def pool(plane):
                    for tile in range(2):
                        total = gt[tile * self.planes + plane * wide]
                        for step in range(1, wide):
                            total = total + gt[tile * self.planes + plane * wide + step]
                        slot = message_slot(self.k, other) + tile * count + plane
                        sb[slot] = total.astype(jnp.bfloat16)

                planes_loop(count, pool, TURNS)
            self.message(e, other).start()

    def back_unit(self, m, unit):
        r = self.refs
        st, dyb, z = r.st, r.dyb, getattr(r, "z" + unit.name)
        name, planes, tiles = unit.name, unit.planes, unit.tiles
        e = MODULES + m
        sums = {}

        def upstream(seg, tile, plane, normed):
            at = tile * planes + plane
            if name == "b":
                hf = r.hf[m * 2 * planes + at]
                value = r.gt[at] * slope_of(normed + hf)
                r.gin[at] = value
                return value
            if name == "a":
                return r.gu[at] * slope_of(normed)
            if seg.chain:
                return self.grads[seg.chain][at] * slope_of(normed)
            return r.rb[e * 16 + message_slot(self.k, seg.dest) + at].astype(jnp.float32)

        for seg in unit.segs:

            def body(plane, carry):
                result = []
                for tile in range(seg.tiles):
                    at = (seg.tile + tile) * planes + plane
                    where = m * STATS + unit.stat + seg.tile + tile
                    value = z[m * tiles * planes + at]
                    normed = value * st[where, 2:3] + st[where, 3:4]
                    dy = upstream(seg, tile, plane, normed)
                    dyb[at] = dy
                    zhat = (value - st[where, 0:1]) * st[where, 1:2]
                    result.append(carry[2 * tile] + partial_sum(dy))
                    result.append(carry[2 * tile + 1] + partial_sum(dy * zhat))
                return tuple(result)

            zero = jnp.zeros((8, LANES), jnp.float32)
            found = planes_sum(planes, body, (zero,) * (2 * seg.tiles), TURNS)
            pair = [
                jnp.concatenate([found[2 * tile + which] for tile in range(seg.tiles)], axis=1)
                for which in range(2)
            ]
            plain = SimpleNamespace(**vars(seg))
            plain.tile = 0
            totals = self.fold(plain, pair)
            self.table_grads(m, seg, totals)
            sums[seg.slot] = totals
        dz = self.dz_planes(unit)
        for seg in unit.segs:
            scale = self.per_cell(unit, seg)
            totals = sums[seg.slot]

            def apply(plane):
                for tile in range(seg.tiles):
                    at = (seg.tile + tile) * planes + plane
                    where = m * STATS + unit.stat + seg.tile + tile
                    zhat = (z[m * tiles * planes + at] - st[where, 0:1]) * st[where, 1:2]
                    inner = dyb[at] - totals[0][tile] * scale - zhat * (totals[1][tile] * scale)
                    dz.store(0, seg.tile + tile, plane, inner * st[where, 2:3] * self.masks[0])

            planes_loop(planes, apply, TURNS)
        dz.close(0)
        self.back_data(m, unit, dz)
        first = min(seg.off for seg in unit.segs)
        last = max(seg.off + seg.taps**2 * seg.cin * seg.cout // LANES for seg in unit.segs)
        wanted = (self.quarter * self.share < last) & ((self.quarter + 1) * self.share > first)

        @pl.when(wanted)
        def _():
            self.back_kernel(m, unit, dz)

    def dz_planes(self, unit):
        r = self.refs
        mode = {"p1": "p", "s2": "dz2", "s1": "wide" if self.k == 3 else "s1"}[unit.kind]
        return Planes(
            mode,
            unit.tiles,
            unit.planes,
            self.masks,
            self.rows,
            r.dC,
            r.dE,
            r.dR,
            self.k <= 1 and unit.kind == "s1",
        )

    def table_grads(self, m, seg, totals):
        gg = self.refs.gg
        slot = seg.slot
        for which, found in ((0, totals[1]), (1, totals[0])):
            if seg.cout > LANES:
                for tile in range(2):
                    gg[m, which, slot : slot + 1, tile * LANES : (tile + 1) * LANES] = found[tile]
            else:
                row = jnp.broadcast_to(found[0], (8, LANES))
                if seg.cout < LANES:
                    row = self.keep(row, seg.cout, [0])
                gg[m, which, slot : slot + 1, 0:LANES] = row[0:1]

    def wide_rows(self, ref, at, tiles, plane, count):
        pieces = [
            ref[pl.ds(at(0, tile, plane), count)].reshape(count * self.rows, LANES)
            for tile in range(tiles)
        ]
        return pieces[0] if tiles == 1 else jnp.concatenate(pieces, axis=1)

    def back_data(self, m, unit, dz):
        r = self.refs
        kind, tiles = unit.kind, unit.tiles
        target = getattr(r, "T" + unit.name)
        lanes = tiles * LANES
        rows = self.rows

        def kernel_rows(d, first, count):
            return target[m * unit.depth + d, first : first + count, 0:lanes]

        def product(left, right):
            return lax.dot_general(left, right, ACROSS, preferred_element_type=jnp.float32)

        def put(ref, tile, planes, first, count, value, step=1, add=False):
            block = value.reshape(count, rows, LANES)
            for q in range(count):
                at = tile * planes + first + q * step
                ref[at] = ref[at] + block[q] if add else block[q]

        planes = unit.planes
        if kind == "s1":
            goal = r.gu if unit.name == "b" else r.gin
            add = unit.name == "a"
            chunk = min(planes, 4)
            across = getattr(r, "T" + unit.name + unit.name)

            def body(step):
                first = step * chunk
                if self.k == 3:
                    total = None
                    for d in range(3):
                        for ref, at in ((dz.right, 0), (dz.main, 256), (dz.edge, 512)):
                            left = self.wide_rows(ref, dz.at, 2, first + 1 - d, chunk)
                            piece = product(left, kernel_rows(d, at, 256))
                            total = piece if total is None else total + piece
                else:
                    narrow = 1 if dz.narrow else 2
                    left = []
                    for d in range(3):
                        at = first + 1 - d
                        left.append(self.wide_rows(dz.main, dz.at, 2, at, chunk))
                        left.append(self.wide_rows(dz.edge, dz.edge_at, narrow, at, chunk))
                    right = across[pl.ds(m * 3, 3), 0 : unit.rows].reshape(3 * unit.rows, 256)
                    total = lax.dot_general(
                        jnp.concatenate(left, axis=1),
                        right,
                        DOWN,
                        preferred_element_type=jnp.float32,
                    )
                for tile in range(2):
                    put(
                        goal,
                        tile,
                        planes,
                        first,
                        chunk,
                        total[:, tile * LANES : (tile + 1) * LANES],
                        add=add,
                    )

            planes_loop(planes // chunk, body, 2)
            return
        if kind == "p1":
            left = self.wide_rows(dz.main, dz.at, tiles, 0, planes)
            total = product(left, kernel_rows(0, 0, 256))
            for tile in range(2):
                put(
                    r.gt,
                    tile,
                    planes,
                    0,
                    planes,
                    total[:, tile * LANES : (tile + 1) * LANES],
                    add=True,
                )
            return
        goal = self.grads[unit.source]
        add = unit.source == "t"
        lanes_in = unit.lanes_in
        count_in = unit.planes_in
        for parity, terms in ((0, [(1, 0)]), (1, [(2, 0), (0, 1)])):
            total, side = None, None
            for d, offset in terms:
                left = self.wide_rows(dz.main, dz.at, tiles, offset, planes)
                piece = product(left, kernel_rows(d, 0, lanes_in))
                total = piece if total is None else total + piece
                left = self.wide_rows(dz.edge, dz.at, tiles, offset, planes)
                piece = product(left, kernel_rows(d, lanes_in, LANES))
                side = piece if side is None else side + piece
            for tile in range(lanes_in // LANES):
                value = total[:, tile * LANES : (tile + 1) * LANES]
                if tile == lanes_in // LANES - 1:
                    value = value + side
                put(goal, tile, count_in, parity, planes, value, step=2, add=add)

    def back_kernel(self, m, unit, dz):
        r = self.refs
        G, rep, wgv = r.work, r.rep, r.wgv
        tiles, planes = unit.tiles, unit.planes
        source = self.maps[unit.source]
        right = self.wide_rows(dz.main, dz.at, tiles, 0, planes)

        def gather(d):
            at = 0
            for part in self.parts(unit, source):
                pieces = self.rows_of(unit, part, m, d, 0, planes)
                left = pieces[0] if len(pieces) == 1 else jnp.concatenate(pieces, axis=1)
                count = left.shape[1]
                result = lax.dot_general(left, right, ALONG, preferred_element_type=jnp.float32)
                for tile in range(tiles):
                    row = pl.multiple_of((d * tiles + tile) * unit.rows + at, 8)
                    G[pl.ds(row, count)] = result[:, tile * LANES : (tile + 1) * LANES]
                at += count

        if self.k == 3 and unit.kind == "s1":
            self.direct_kernel(m, unit, right)
            return
        planes_loop(unit.depth, gather)
        for seg in unit.segs:
            self.fold_kernel(m, unit, seg)

    def direct_kernel(self, m, unit, right):
        wgv, (seg,) = self.refs.wgv, unit.segs
        source = self.maps[unit.source]
        span = 2 * seg.cin
        low, high = self.quarter * self.share, (self.quarter + 1) * self.share

        def tap_row(d):
            first = seg.off + d * (3 * span)

            @pl.when((first < high) & (first + 3 * span > low))
            def _():
                for column, part in enumerate(self.parts(unit, source)):
                    pieces = self.rows_of(unit, part, m, d, 0, unit.planes)
                    left = jnp.concatenate(pieces, axis=1)
                    result = lax.dot_general(left, right, ALONG, preferred_element_type=jnp.float32)
                    for tile in range(2):
                        rows = pl.ds(first + column * span + tile, seg.cin, stride=2)
                        wgv[rows] = result[:, tile * LANES : (tile + 1) * LANES]

        planes_loop(unit.depth, tap_row)

    def fold_kernel(self, m, unit, seg):
        r = self.refs
        G, rep, wgv = r.work, r.rep, r.wgv
        cin, cout, tiles = seg.cin, seg.cout, unit.tiles
        width = 3 if seg.taps == 3 else 1
        found = links(self.k, unit, seg)
        off = seg.off

        def fold(d):
            for column in range(width):
                tap = d * width + column
                totals = []
                for tile in range(seg.tiles):
                    total = None
                    for row, which, wanted in found:
                        if which != column:
                            continue
                        at = pl.multiple_of((d * tiles + seg.tile + tile) * unit.rows + row, 8)
                        piece = G[pl.ds(at, cin)]
                        if cout <= LANES:
                            local = self.local_blocks(seg, tile, wanted)
                            if not local:
                                continue
                            piece = self.keep(piece, cout, local)
                        total = piece if total is None else total + piece
                    totals.append(total)
                if cout > LANES:
                    for tile in range(2):
                        wgv[pl.ds(off + tap * (2 * cin) + tile, cin, stride=2)] = totals[tile]
                    continue
                total = None
                for piece in totals:
                    if piece is not None:
                        total = piece if total is None else total + piece
                if cout == LANES:
                    wgv[pl.ds(pl.multiple_of(off + tap * cin, 8), cin)] = total
                else:
                    rep[pl.ds(pl.multiple_of(tap * cin, cin), cin)] = self.spread(total, cout)

        planes_loop(unit.depth, fold)
        if cout < LANES:
            ratio = LANES // cout
            count = width * width * cin // ratio
            total = None
            for part in range(ratio):
                piece = self.keep(rep[pl.ds(part, count, stride=ratio)], cout, [part])
                total = piece if total is None else total + piece
            wgv[off : off + count] = total

    def backward(self, m, meanwhile):
        e = MODULES + m
        last = m == MODULES - 1
        self.sent(jnp.where(last, m, e + 1))
        self.send_back(m)
        pl.when(last)(meanwhile)
        for name in ("g", "f", "e", "d", "u"):
            if name in self.units:
                for seg in self.units[name].segs:
                    if seg.dest >= 0:
                        self.arrived(e, seg.dest).wait_recv()
                self.back_unit(m, self.units[name])
        self.back_unit(m, self.units["b"])
        self.back_unit(m, self.units["a"])


STATS = 20
TURNS = 8
NAMES = list(
    dict(x=0, cot=0, w=0, gains=0, shifts=0, kinds=0, out=0, grad=0, wg=0, gain=0, shift=0)
)


def one_hot(goal, lane, deep):
    pieces = [
        jnp.where(goal == lane + first, 1.0, 0.0).astype(jnp.bfloat16)
        for first in range(0, deep, LANES)
    ]
    return jnp.concatenate(pieces, axis=1)


class Cells:
    def __init__(self, core, shape, small, large):
        self.core = core
        row = lax.broadcasted_iota(jnp.int32, shape, 0)
        self.wide = self.pick(LW // 8, SW // 8)
        tall = self.pick(LH // 8, SH // 8)
        self.crop = self.pick((row * 43691) >> 21, (row * 43691) >> 19)
        inner = row - self.crop * (self.wide * tall)
        self.along = self.pick((inner * 43691) >> 18, (inner * 43691) >> 17)
        self.across = inner - self.along * self.wide
        self.valid = self.crop < self.pick(large, small)
        self.last = tall - 1

    def pick(self, large, small):
        return jnp.where(self.core == 0, large, small)


def fill_masks(refs, rows, core, small, large):
    cells = Cells(core, (rows, LANES), small, large)
    valid = cells.valid
    six = cells.wide == 6
    up, down = valid & (cells.along > 0), valid & (cells.along < cells.last)
    tables = (
        valid,
        valid & (cells.across > 0),
        valid & (cells.across < cells.wide - 1),
        up & six,
        up & jnp.logical_not(six),
        down & six,
        down & jnp.logical_not(six),
    )
    for at, table in enumerate(tables):
        refs.masks[at] = jnp.where(table, 1.0, 0.0)


class Gather:
    def __init__(self, refs, core, count):
        self.refs, self.core, self.count = refs, core, count
        self.z = lax.axis_index("crops") // 2
        self.last = count // 2 - 1

    def hop(self, t, source, right):
        r = self.refs
        at = source * 2 + self.core
        gath = r.gathc if t else r.gathx
        to = self.z + 1 if right else self.z - 1
        return pltpu.make_async_remote_copy(
            src_ref=gath.at[at],
            dst_ref=gath.at[at],
            send_sem=r.hsem.at[(t * (self.last + 1) + source) * 3 + (0 if right else 1)],
            recv_sem=r.gsem.at[t * self.count + at],
            device_id=dict(crops=to * 2 + self.core),
            device_id_type=pl.DeviceIdType.MESH,
        )

    def across(self, t, source, core, rows):
        r = self.refs
        at = source * 2 + core
        gath = r.gathc if t else r.gathx
        return pltpu.make_async_remote_copy(
            src_ref=gath.at[at, pl.ds(0, rows)],
            dst_ref=gath.at[at, pl.ds(0, rows)],
            send_sem=r.hsem.at[(t * (self.last + 1) + source) * 3 + 2],
            recv_sem=r.gsem.at[t * self.count + at],
            device_id=dict(crops=self.z * 2 + 1 - self.core),
            device_id_type=pl.DeviceIdType.MESH,
        )

    def each_core(self, action):
        for core, rows in ((0, SH * SW * C0 // LANES), (1, ROWS)):

            @pl.when(self.core == core)
            def _():
                action(core, rows)

    def send(self, t, source, rightward, leftward):
        if rightward:

            @pl.when(self.z < self.last)
            def _():
                self.hop(t, source, True).start()

        if leftward:

            @pl.when(self.z > 0)
            def _():
                self.hop(t, source, False).start()

        self.each_core(lambda core, rows: self.across(t, source, core, rows).start())

    def step(self, t, s):
        r = self.refs
        if s == 0:
            at = self.z * 2 + self.core
            if t:
                r.gathc[at] = r.cot[...]
            else:
                r.gathx[at] = r.x[...]
            self.send(t, self.z, True, True)
            return

        @pl.when(self.z >= s)
        def _():
            self.hop(t, self.z - s, True).wait_recv()
            self.send(t, self.z - s, True, False)

        @pl.when(self.z + s <= self.last)
        def _():
            self.hop(t, self.z + s, True).wait_recv()
            self.send(t, self.z + s, False, True)

    def collect(self, t):
        for source in range(self.last + 1):
            for core, rows in ((0, ROWS), (1, SH * SW * C0 // LANES)):

                @pl.when(self.core == core)
                def _():
                    self.across(t, source, 1 - core, rows).wait_recv()

    def finish(self, t):
        def sent(source, rightward, leftward):
            if rightward:

                @pl.when(self.z < self.last)
                def _():
                    self.hop(t, source, True).wait_send()

            if leftward:

                @pl.when(self.z > 0)
                def _():
                    self.hop(t, source, False).wait_send()

            self.each_core(lambda core, rows: self.across(t, source, core, rows).wait_send())

        sent(self.z, True, True)
        for s in range(1, self.last + 1):

            @pl.when(self.z >= s)
            def _():
                sent(self.z - s, True, False)

            @pl.when(self.z + s <= self.last)
            def _():
                sent(self.z + s, False, True)


def scratch_table(rows, weight_rows, count):
    def half(many):
        return pltpu.VMEM((many, rows, LANES), jnp.bfloat16)

    def full(many):
        return pltpu.VMEM((many, rows, LANES), jnp.float32)

    def expanded(depth, deep, wide):
        return pltpu.VMEM((MODULES * depth, deep, wide), jnp.bfloat16)

    _, span, _ = pair_rows(weight_rows, count)
    return dict(
        masks=full(MASKS),
        hC=half(2 * 20),
        hE=half(2 * 10),
        hR=half(2 * 6),
        uC=half(2 * 20),
        uE=half(2 * 10),
        uR=half(2 * 6),
        tC=half(2 * 18),
        tE=half(2 * 9),
        c1C=half(2 * 5),
        c1E=half(2 * 5),
        c2C=half(2 * 5),
        c2E=half(2 * 5),
        c3C=half(2 * 3),
        c3E=half(2 * 3),
        dC=half(20),
        dE=half(20),
        dR=half(6),
        outs=half(16),
        hf=full(2 * 16),
        s=full(2 * 16),
        za=full(2 * 16),
        zb=full(2 * 16),
        zd=full(2 * 16),
        zu=full(2 * 8),
        ze=full(2 * 4),
        zf=full(2 * 2),
        zg=full(2 * 2),
        gt=full(16),
        gu=full(16),
        gin=full(16),
        gc1=full(4),
        gc2=full(4),
        gc3=full(2),
        dyb=full(16),
        sb=half(16),
        rb=half(4 * 16),
        st=pltpu.VMEM((MODULES * STATS, 8, LANES), jnp.float32),
        Ta=expanded(3, 768, 256),
        Tb=expanded(3, 768, 256),
        Taa=expanded(3, 512, 256),
        Tbb=expanded(3, 512, 256),
        Td=expanded(3, 384, 512),
        Tu=expanded(1, 256, 768),
        Te=expanded(3, 256, 256),
        Tf=expanded(3, 256, 128),
        Tg=expanded(3, 256, 256),
        raw=pltpu.VMEM((9408, LANES), jnp.bfloat16),
        work=pltpu.VMEM((4608, LANES), jnp.float32),
        rep=pltpu.VMEM((640, LANES), jnp.float32),
        wgv=pltpu.VMEM((weight_rows, LANES), jnp.float32),
        wq=pltpu.VMEM((MODULES, 2 * weight_rows // count, LANES), jnp.float32),
        wr=pltpu.VMEM((MODULES, span, LANES), jnp.float32),
        gathx=pltpu.VMEM((count, ROWS, LANES), jnp.bfloat16),
        gathc=pltpu.VMEM((count, ROWS, LANES), jnp.bfloat16),
        hot=pltpu.VMEM((2, 384, 768), jnp.bfloat16),
        blocks=pltpu.VMEM((2, ROWS, LANES), jnp.bfloat16),
        slopes=pltpu.VMEM((2, ROWS, LANES), jnp.float32),
        blockr=pltpu.VMEM((ROWS, LANES), jnp.bfloat16),
        sloper=pltpu.VMEM((ROWS, LANES), jnp.float32),
        gg=pltpu.VMEM((MODULES, 2, SLOTS, 256), jnp.float32),
        ggr=pltpu.VMEM((MODULES, 2, SLOTS, 256), jnp.float32),
        wsem=pltpu.SemaphoreType.DMA((8,)),
        ssem=pltpu.SemaphoreType.DMA((16,)),
        rsem=pltpu.SemaphoreType.DMA((16,)),
        hsem=pltpu.SemaphoreType.DMA((3 * count,)),
        gsem=pltpu.SemaphoreType.DMA((2 * count,)),
        psem=pltpu.SemaphoreType.DMA((5,)),
        qsem=pltpu.SemaphoreType.DMA((5,)),
        osem=pltpu.SemaphoreType.DMA((1,)),
    )


def pair_rows(weight_rows, count):
    share = weight_rows // count
    low = share // 8 * 8
    return share, 2 * share - low, low


def greet(core, count):
    barrier = pltpu.get_barrier_semaphore()
    me, shard = lax.axis_index("branch"), lax.axis_index("crops")
    z = shard // 2

    def signal(**where):
        pl.semaphore_signal(barrier, inc=1, device_id=where, device_id_type=pl.DeviceIdType.MESH)

    for step in range(1, 4):
        signal(branch=lax.rem(me + step, 4))
    signal(crops=shard + 1 - 2 * core)

    @pl.when(z > 0)
    def _():
        signal(crops=shard - 2)

    @pl.when(z < count // 2 - 1)
    def _():
        signal(crops=shard + 2)

    ends = (z == 0).astype(jnp.int32) + (z == count // 2 - 1).astype(jnp.int32)
    pl.semaphore_wait(barrier, 6 - ends)


def whole_kernel(names, rows, large, small, *args):
    refs = SimpleNamespace(**dict(zip(names, args)))
    count = large + small
    me, shard = lax.axis_index("branch"), lax.axis_index("crops")
    core = shard % 2
    weight_rows = refs.wgv.shape[0]
    share, span, low = pair_rows(weight_rows, count)
    quarter = pl.multiple_of(shard // 2 * (2 * share), 8)

    class Lazy:
        def __getitem__(self, index):
            return refs.masks[index]

    def across(source, goal, index):
        return pltpu.make_async_remote_copy(
            src_ref=source,
            dst_ref=goal,
            send_sem=refs.psem.at[index],
            recv_sem=refs.qsem.at[index],
            device_id=dict(crops=shard + 1 - 2 * core),
            device_id_type=pl.DeviceIdType.MESH,
        )

    def kernel_pair(m):
        at = pl.multiple_of(low * (1 - core), 8)
        return across(refs.wq.at[m, pl.ds(at, span)], refs.wr.at[m], m)

    outputs_pair = across(refs.blocks.at[1], refs.blockr, 2)
    gradient_pair = across(refs.slopes.at[1], refs.sloper, 3)
    table_pair = across(refs.gg, refs.ggr, 4)
    gather = Gather(refs, core, count)

    def every(action):
        for k in range(4):

            @pl.when(me == k)
            def _():
                action(Branch(k, rows, large, small, 2 * share, refs, Lazy(), core))

    def begin(branch):
        branch.fetch_first()

    def prepare(branch):
        found = branch.segments()
        stops = {0: 1, min(2, len(found) - 2): 2, len(found) - 1: 3}
        for index, (unit, seg) in enumerate(found):
            branch.expand(index)
            if index in stops:
                gather.step(0, stops[index])

    def main(branch):
        branch.unpack(0, branch.take_feature)
        branch.maps["h"].close(0)
        gather.step(1, 0)

        def ahead(m, carry):
            branch.forward(m, gather)
            return carry

        def meanwhile():
            branch.plan_pack()
            branch.pack_outputs()
            outputs_pair.start()

        def back(step, carry):
            m = MODULES - 1 - step
            branch.backward(m, meanwhile)
            refs.wq[m] = refs.wgv[pl.ds(quarter, 2 * share)]
            kernel_pair(m).start()
            return carry

        lax.fori_loop(0, MODULES, ahead, 0)
        lax.fori_loop(0, MODULES, back, 0)
        branch.sent(MODULES)
        branch.pack_gradient()
        gradient_pair.start()
        table_pair.start()

    every(begin)
    greet(core, count)
    gather.step(0, 0)
    fill_masks(refs, rows, core, small, large)
    refs.wgv[pl.ds(quarter, 2 * share)] = jnp.zeros((2 * share, LANES), jnp.float32)
    refs.gg[...] = jnp.zeros(refs.gg.shape, jnp.float32)
    every(prepare)
    gather.collect(0)
    every(main)

    for step in range(MODULES):
        m = MODULES - 1 - step
        kernel_pair(m).wait()
        mine = refs.wq[m, pl.ds(pl.multiple_of(low * core, 8), span)]
        refs.work[pl.ds(m, span, stride=MODULES)] = mine + refs.wr[m]
    skip = pl.multiple_of(core * (MODULES * (share - low)), 8)
    leave = pltpu.make_async_copy(
        refs.work.at[pl.ds(skip, MODULES * share)], refs.wg, refs.osem.at[0]
    )
    leave.start()
    outputs_pair.wait()
    gradient_pair.wait()
    table_pair.wait()
    own = refs.kinds[shard] != core
    refs.out[...] = jnp.where(own, refs.blocks[0].astype(jnp.float32), refs.blockr[...].astype(jnp.float32)).astype(jnp.bfloat16)
    refs.grad[...] = jnp.where(own, refs.slopes[0], refs.sloper[...])
    width = 256 // count
    for which, goal in ((0, refs.gain), (1, refs.shift)):
        for m in range(MODULES):
            total = refs.gg[m, which] + refs.ggr[m, which]
            found = None
            for at in range(count):
                piece = jnp.where(shard == at, total[:, at * width : (at + 1) * width], 0.0)
                found = piece if found is None else found + piece
            goal[m] = found
    gather.finish(0)
    gather.finish(1)
    leave.wait()


def whole_call(rows, large, small, x, cot, w, gains, shifts, kinds):
    count = large + small
    weight_rows = w.shape[0] // MODULES
    table = scratch_table(rows, weight_rows, count)
    vmem = pl.BlockSpec(memory_space=pltpu.VMEM)
    hbm = pl.BlockSpec(memory_space=pl.ANY)
    smem = pl.BlockSpec(memory_space=pltpu.SMEM)
    tables = jax.ShapeDtypeStruct((MODULES, SLOTS, 256 // count), jnp.float32)
    return pl.pallas_call(
        partial(whole_kernel, NAMES + list(table), rows, large, small),
        out_shape=(
            jax.ShapeDtypeStruct((ROWS, LANES), jnp.bfloat16),
            jax.ShapeDtypeStruct((ROWS, LANES), jnp.float32),
            jax.ShapeDtypeStruct((MODULES * weight_rows // count, LANES), jnp.float32),
            tables,
            tables,
        ),
        in_specs=[vmem, vmem, hbm, vmem, vmem, smem],
        out_specs=(vmem, vmem, hbm, vmem, vmem),
        scratch_shapes=list(table.values()),
        compiler_params=pltpu.CompilerParams(
            collective_id=0, has_side_effects=True, vmem_limit_bytes=62 * 1024 * 1024
        ),
    )(x, cot, w, gains, shifts, kinds)


def leave_kernel(*args):
    sems = args[10]
    copies = [
        pltpu.make_async_copy(source, goal, sems.at[at])
        for at, (source, goal) in enumerate(zip(args[:5], args[5:10]))
    ]
    for copy in copies:
        copy.start()
    for copy in copies:
        copy.wait()


def leave_call(arrays):
    vmem = pl.BlockSpec(memory_space=pltpu.VMEM)
    hbm = pl.BlockSpec(memory_space=pl.ANY)
    return pl.pallas_call(
        leave_kernel,
        out_shape=tuple(jax.ShapeDtypeStruct(array.shape, array.dtype) for array in arrays),
        in_specs=[vmem] * 5,
        out_specs=(hbm,) * 5,
        scratch_shapes=[pltpu.SemaphoreType.DMA((5,))],
    )(*arrays)


def on_device_grouped(features, weights, gains, shifts, cotangent, size_group):
    count = lax.axis_size("crops")
    large = count // 4
    weight_rows = weights.shape[2] // LANES
    results = whole_call(
        group_rows(count),
        large,
        count - large,
        features[0],
        cotangent[0],
        weights[0]
        .reshape(MODULES, weight_rows, LANES)
        .transpose(1, 0, 2)
        .reshape(MODULES * weight_rows, LANES),
        gains[0],
        shifts[0],
        size_group,
    )
    out, grad, weight_grad, gain, shift = leave_call(results)
    share = weight_rows // count
    weight_grad = weight_grad.reshape(share, MODULES, LANES).transpose(1, 0, 2)
    weight_grad = with_layout_constraint(weight_grad, Layout((1, 0, 2)))
    return (
        out[None],
        grad[None],
        weight_grad.reshape(1, MODULES, share * LANES),
        gain[None],
        shift[None],
    )


def group_rows(count):
    large = count // 4
    rows = max(large * (LH // 8) * (LW // 8), (count - large) * (SH // 8) * (SW // 8))
    return -(-rows // 16) * 16


def fits(count):
    return count % 8 == 0 and group_rows(count) <= 96


def solution(mesh):
    placed = (
        P("branch", "crops", None),
        P("branch", None, None),
        P("branch", None, None, None),
        P("branch", None, None, None),
        P("branch", "crops", None),
        P(),
    )
    return jax.shard_map(
        on_device_grouped if fits(mesh.shape["crops"]) else on_device,
        mesh=mesh,
        in_specs=placed,
        out_specs=(
            P("branch", "crops", None),
            P("branch", "crops", None),
            P("branch", None, "crops"),
            P("branch", None, None, "crops"),
            P("branch", None, None, "crops"),
        ),
        check_vma=False,
    )
```

```python
from functools import partial
from types import SimpleNamespace
import math

import jax
import jax.numpy as jnp
import numpy as np
from jax import lax
from jax.experimental import pallas as pl
from jax.experimental.layout import Layout, with_layout_constraint
from jax.experimental.pallas import tpu as pltpu
from jax.sharding import PartitionSpec as P

C0 = 32
BLOCKS = 1
MODULES = 2
CROPS_DEV = 1
SH = 32
SW = 24
LH = 64
LW = 48
ROWS = 768
MSG_ROWS = 384


EPS = 1e-05


def as_sent(x):

    def short(part):
        return part.astype(jnp.bfloat16) if part.dtype == jnp.float32 else part

    return jax.tree.map(short, x)


def sender_plan(branch_index, top_channels, blocks):
    channels = top_channels << branch_index
    operations = []
    for block_index in range(blocks):
        operations.append(
            SimpleNamespace(
                phase=2 * block_index,
                source=("h", block_index),
                level=branch_index,
                cin=channels,
                cout=channels,
                stride=1,
                taps=3,
                act="silu",
                output=("u", block_index),
                skip=None,
                dest=-1,
            )
        )
        operations.append(
            SimpleNamespace(
                phase=2 * block_index + 1,
                source=("u", block_index),
                level=branch_index,
                cin=channels,
                cout=channels,
                stride=1,
                taps=3,
                act="res",
                output=("h", block_index + 1),
                skip=("h", block_index),
                dest=-1,
            )
        )
    top_name = ("h", blocks)
    for target in range(branch_index):
        operations.append(
            SimpleNamespace(
                phase=2 * blocks,
                source=top_name,
                level=branch_index,
                cin=channels,
                cout=top_channels << target,
                stride=1,
                taps=1,
                act="none",
                output=None,
                skip=None,
                dest=target,
            )
        )
    for target in range(branch_index + 1, 4):
        for depth_step in range(1, target - branch_index + 1):
            is_last = depth_step == target - branch_index
            operations.append(
                SimpleNamespace(
                    phase=2 * blocks + depth_step - 1,
                    source=top_name if depth_step == 1 else ("chain", target, depth_step - 1),
                    level=branch_index + depth_step,
                    cin=channels,
                    cout=top_channels << target if is_last else channels,
                    stride=2,
                    taps=3,
                    act="none" if is_last else "silu",
                    output=None if is_last else ("chain", target, depth_step),
                    skip=None,
                    dest=target if is_last else -1,
                )
            )
    for position, operation in enumerate(operations):
        operation.slot = position
        operation.size = (
            operation.taps * operation.taps * operation.cin * operation.cout
        )
        if operation.taps == 1:
            operation.kshape = (operation.cin, operation.cout)
        else:
            operation.kshape = (3, 3, operation.cin, operation.cout)
    return operations


def phase_lengths(top_channels, blocks):
    phase_count = 2 * blocks + 3
    lengths = [0] * phase_count
    for branch_index in range(4):
        per_phase = [0] * phase_count
        for operation in sender_plan(branch_index, top_channels, blocks):
            per_phase[operation.phase] += operation.size
        lengths = [max(current, candidate) for current, candidate in zip(lengths, per_phase)]
    return lengths


def weighted_plan(branch_index, top_channels, blocks):
    lengths = phase_lengths(top_channels, blocks)
    starts = [sum(lengths[:phase_index]) for phase_index in range(len(lengths))]
    running = [0] * len(lengths)
    operations = sender_plan(branch_index, top_channels, blocks)
    for operation in operations:
        phase_index = operation.phase
        operation.inner = running[phase_index]
        operation.offset = starts[phase_index] + running[phase_index]
        operation.position = sum(
            (1 for earlier in operations[: operation.slot] if earlier.phase == phase_index)
        )
        running[phase_index] += operation.size
    return operations


def phase_operations(branch_index, phase_index):
    return [
        operation
        for operation in weighted_plan(branch_index, C0, BLOCKS)
        if operation.phase == phase_index
    ]


def input_names(operations):
    source_names = []
    for operation in operations:
        if operation.source not in source_names:
            source_names.append(operation.source)
    return source_names


def silu_slope(value):
    sigmoid = jax.nn.sigmoid(value)
    return sigmoid * (1.0 + value * (1.0 - sigmoid))


def crop_cells(size_kind):
    return (LH, LW) if size_kind else (SH, SW)


def map_dims(size_kind, level, channels):
    height, breadth = crop_cells(size_kind)
    return (CROPS_DEV, height >> level, breadth >> level, channels)


def source_dims(branch_index, size_kind, map_name):
    level = branch_index + map_name[2] if map_name[0] == "chain" else branch_index
    return map_dims(size_kind, level, C0 << branch_index)


def preact_dims(size_kind, operation):
    return map_dims(size_kind, operation.level, operation.cout)


def to_canvas(arrays, value_type):
    if not arrays:
        return jnp.zeros((ROWS, 128), value_type)
    flattened = jnp.concatenate([array.reshape(-1).astype(value_type) for array in arrays])
    return jnp.pad(flattened, (0, ROWS * 128 - flattened.shape[0])).reshape(ROWS, 128)


def from_canvas(canvas, dims_list):
    flattened = canvas.reshape(-1)
    pieces = []
    offset = 0
    for dims_entry in dims_list:
        count_here = math.prod(dims_entry)
        pieces.append(flattened[offset : offset + count_here].reshape(dims_entry))
        offset += count_here
    return pieces


def to_slot(array):
    flattened = array.reshape(-1)
    return jnp.pad(flattened, (0, MSG_ROWS * 128 - flattened.shape[0])).reshape(MSG_ROWS, 128)


def from_slot(slot_rows, dims_entry):
    return slot_rows.reshape(-1)[: math.prod(dims_entry)].reshape(dims_entry)


def upsample(message, factor):
    crop_count, height, breadth, channels = message.shape
    widened = jnp.broadcast_to(
        message[:, :, None, :, None, :], (crop_count, height, factor, breadth, factor, channels)
    )
    return widened.reshape(crop_count, height * factor, breadth * factor, channels)


def block_pool(array, factor):
    crop_count, height, breadth, channels = array.shape
    return array.reshape(
        crop_count, height // factor, factor, breadth // factor, factor, channels
    ).sum(axis=(2, 4))


def kernel_piece(module_weights, operation):
    start = operation.offset
    return module_weights[start : start + operation.size].reshape(operation.kshape)


def conv_forward(operation, source, kernel):
    if operation.taps == 1:
        return jnp.einsum("nhwc,cd->nhwd", source, kernel, preferred_element_type=jnp.float32)
    stride = operation.stride
    return lax.conv_general_dilated(
        source,
        kernel,
        (stride, stride),
        ((1, 1), (1, 1)),
        dimension_numbers=("NHWC", "HWIO", "NHWC"),
        preferred_element_type=jnp.float32,
    )


def conv_backward(operation, source, kernel, upstream):
    if operation.taps == 1:
        source_grad = jnp.einsum(
            "nhwd,cd->nhwc", upstream, kernel, preferred_element_type=jnp.float32
        )
        kernel_grad = jnp.einsum(
            "nhwc,nhwd->cd", source, upstream, preferred_element_type=jnp.float32
        )
        return (source_grad, kernel_grad)
    stride = operation.stride
    flipped = jnp.transpose(kernel[::-1, ::-1], (0, 1, 3, 2))
    high_pad = 2 if stride == 2 else 1
    source_grad = lax.conv_general_dilated(
        upstream,
        flipped,
        (1, 1),
        ((1, high_pad), (1, high_pad)),
        lhs_dilation=(stride, stride),
        dimension_numbers=("NHWC", "HWIO", "NHWC"),
        preferred_element_type=jnp.float32,
    )
    kernel_grad = lax.conv_general_dilated(
        source,
        upstream,
        (1, 1),
        ((1, 2 - stride), (1, 2 - stride)),
        rhs_dilation=(stride, stride),
        dimension_numbers=("CHWN", "IHWO", "NHWC"),
        preferred_element_type=jnp.float32,
    )
    return (source_grad, jnp.transpose(kernel_grad, (1, 2, 0, 3)))


def cell_total(counts, size_kind, level):
    height, breadth = crop_cells(size_kind)
    return counts[size_kind] * float(CROPS_DEV * (height >> level) * (breadth >> level))


def norm_terms(totals, counts, size_kind, operation):
    cells_here = cell_total(counts, size_kind, operation.level)
    channels = operation.cout
    position = operation.position
    average = totals[size_kind, 0, position, :channels] / cells_here
    variance = totals[size_kind, 1, position, :channels] / cells_here - average * average
    return (average, lax.rsqrt(variance + EPS))


def forward_conv(branch_index, size_kind, phase_index, source_canvas, module_weights):
    operations = phase_operations(branch_index, phase_index)
    source_names = input_names(operations)
    pieces = from_canvas(
        source_canvas, [source_dims(branch_index, size_kind, map_name) for map_name in source_names]
    )
    sources = {
        map_name: piece.astype(jnp.bfloat16) for map_name, piece in zip(source_names, pieces)
    }
    preacts = []
    totals = jnp.zeros((2, 2, 3, 8 * C0), jnp.float32)
    for operation in operations:
        preact = conv_forward(
            operation, sources[operation.source], kernel_piece(module_weights, operation)
        )
        preacts.append(preact)
        channels = operation.cout
        position = operation.position
        totals = totals.at[size_kind, 0, position, :channels].set(jnp.sum(preact, axis=(0, 1, 2)))
        totals = totals.at[size_kind, 1, position, :channels].set(
            jnp.sum(preact * preact, axis=(0, 1, 2))
        )
    return (to_canvas(preacts, jnp.float32), totals)


def forward_norm(
    branch_index,
    size_kind,
    phase_index,
    preact_canvas,
    totals,
    counts,
    module_gains,
    module_shifts,
    skip_canvas,
    message_buffer,
):
    operations = phase_operations(branch_index, phase_index)
    preacts = from_canvas(
        preact_canvas, [preact_dims(size_kind, operation) for operation in operations]
    )
    skip_map = from_canvas(skip_canvas, [map_dims(size_kind, branch_index, C0 << branch_index)])[0]
    produced = []
    for operation, preact in zip(operations, preacts):
        average, inverse_std = norm_terms(totals, counts, size_kind, operation)
        norm_slot = operation.slot
        channels = operation.cout
        normed = (preact - average) * inverse_std * module_gains[
            norm_slot, :channels
        ] + module_shifts[norm_slot, :channels]
        if operation.act == "silu":
            produced.append(jax.nn.silu(normed))
        elif operation.act == "res":
            produced.append(jax.nn.silu(normed + skip_map))
        else:
            message_buffer = message_buffer.at[operation.dest].set(
                to_slot(normed.astype(jnp.bfloat16))
            )
    return (to_canvas(produced, jnp.float32), message_buffer)


def receive_forward(branch_index, size_kind, top_canvas, received):
    channels = C0 << branch_index
    summed = from_canvas(top_canvas, [map_dims(size_kind, branch_index, channels)])[0]
    for sender in range(4):
        if sender < branch_index:
            summed = summed + from_slot(
                received[sender], map_dims(size_kind, branch_index, channels)
            ).astype(jnp.float32)
        elif sender > branch_index:
            coarse = from_slot(received[sender], map_dims(size_kind, sender, channels))
            summed = summed + upsample(coarse, 2 ** (sender - branch_index)).astype(jnp.float32)
    return (to_canvas([jax.nn.silu(summed)], jnp.float32), to_canvas([summed], jnp.float32))


def receive_backward(branch_index, size_kind, grad_canvas, summed_canvas):
    dims_here = map_dims(size_kind, branch_index, C0 << branch_index)
    upstream = from_canvas(grad_canvas, [dims_here])[0]
    summed = from_canvas(summed_canvas, [dims_here])[0]
    summed_grad = upstream * silu_slope(summed)
    buffer = jnp.zeros((4, MSG_ROWS, 128), jnp.bfloat16)
    for sender in range(4):
        if sender < branch_index:
            buffer = buffer.at[sender].set(to_slot(summed_grad.astype(jnp.bfloat16)))
        elif sender > branch_index:
            pooled = block_pool(summed_grad, 2 ** (sender - branch_index))
            buffer = buffer.at[sender].set(to_slot(pooled.astype(jnp.bfloat16)))
    return (to_canvas([summed_grad], jnp.float32), buffer)


def backward_stats(
    branch_index,
    size_kind,
    phase_index,
    dout_canvas,
    message_grads,
    preact_canvas,
    totals,
    counts,
    module_gains,
    module_shifts,
    skip_canvas,
):
    operations = phase_operations(branch_index, phase_index)
    preacts = from_canvas(
        preact_canvas, [preact_dims(size_kind, operation) for operation in operations]
    )
    producing = [operation for operation in operations if operation.act != "none"]
    output_grads = from_canvas(
        dout_canvas, [preact_dims(size_kind, operation) for operation in producing]
    )
    grads_by_name = {
        operation.output: piece for operation, piece in zip(producing, output_grads)
    }
    skip_map = from_canvas(skip_canvas, [map_dims(size_kind, branch_index, C0 << branch_index)])[0]
    upstreams = []
    skip_grads = []
    sums_local = jnp.zeros((2, 2, 3, 8 * C0), jnp.float32)
    for operation, preact in zip(operations, preacts):
        average, inverse_std = norm_terms(totals, counts, size_kind, operation)
        norm_slot = operation.slot
        channels = operation.cout
        centered = (preact - average) * inverse_std
        normed = centered * module_gains[norm_slot, :channels] + module_shifts[norm_slot, :channels]
        if operation.act == "silu":
            upstream = grads_by_name[operation.output] * silu_slope(normed)
        elif operation.act == "res":
            upstream = grads_by_name[operation.output] * silu_slope(normed + skip_map)
            skip_grads.append(upstream)
        else:
            upstream = from_slot(
                message_grads[operation.dest], preact_dims(size_kind, operation)
            ).astype(jnp.float32)
        upstreams.append(upstream)
        position = operation.position
        sums_local = sums_local.at[size_kind, 0, position, :channels].set(
            jnp.sum(upstream, axis=(0, 1, 2))
        )
        sums_local = sums_local.at[size_kind, 1, position, :channels].set(
            jnp.sum(upstream * centered, axis=(0, 1, 2))
        )
    return (to_canvas(upstreams, jnp.float32), sums_local, to_canvas(skip_grads, jnp.float32))


def backward_apply(
    branch_index,
    size_kind,
    phase_index,
    upstream_canvas,
    preact_canvas,
    totals,
    grad_totals,
    counts,
    source_canvas,
    module_weights,
    module_gains,
):
    operations = phase_operations(branch_index, phase_index)
    preacts = from_canvas(
        preact_canvas, [preact_dims(size_kind, operation) for operation in operations]
    )
    upstreams = from_canvas(
        upstream_canvas, [preact_dims(size_kind, operation) for operation in operations]
    )
    source_names = input_names(operations)
    source_list = [source_dims(branch_index, size_kind, map_name) for map_name in source_names]
    pieces = from_canvas(source_canvas, source_list)
    sources = {
        map_name: piece.astype(jnp.bfloat16) for map_name, piece in zip(source_names, pieces)
    }
    source_grads = {
        map_name: jnp.zeros(dims_entry, jnp.float32)
        for map_name, dims_entry in zip(source_names, source_list)
    }
    kernel_grads = []
    slot_count = module_gains.shape[0]
    gain_part = jnp.zeros((slot_count, 8 * C0), jnp.float32)
    shift_part = jnp.zeros((slot_count, 8 * C0), jnp.float32)
    for operation, preact, upstream in zip(operations, preacts, upstreams):
        average, inverse_std = norm_terms(totals, counts, size_kind, operation)
        cells_here = cell_total(counts, size_kind, operation.level)
        norm_slot = operation.slot
        channels = operation.cout
        position = operation.position
        centered = (preact - average) * inverse_std
        mean_upstream = grad_totals[size_kind, 0, position, :channels] / cells_here
        mean_cross = grad_totals[size_kind, 1, position, :channels] / cells_here
        preact_grad = (
            module_gains[norm_slot, :channels]
            * inverse_std
            * (upstream - mean_upstream - centered * mean_cross)
        )
        source_grad, kernel_grad = conv_backward(
            operation,
            sources[operation.source],
            kernel_piece(module_weights, operation),
            preact_grad.astype(jnp.bfloat16),
        )
        source_grads[operation.source] = source_grads[operation.source] + source_grad
        kernel_grads.append(kernel_grad.reshape(-1))
        gain_part = gain_part.at[norm_slot, :channels].set(
            grad_totals[0, 1, position, :channels] + grad_totals[1, 1, position, :channels]
        )
        shift_part = shift_part.at[norm_slot, :channels].set(
            grad_totals[0, 0, position, :channels] + grad_totals[1, 0, position, :channels]
        )
    phase_length = phase_lengths(C0, BLOCKS)[phase_index]
    if kernel_grads:
        joined = jnp.concatenate(kernel_grads)
        weight_part = jnp.pad(joined, (0, phase_length - joined.shape[0]))
    else:
        weight_part = jnp.zeros((phase_length,), jnp.float32)
    return (
        to_canvas([source_grads[map_name] for map_name in source_names], jnp.float32),
        weight_part,
        gain_part,
        shift_part,
    )


def on_device(features, weights, gains, shifts, cotangent, size_group):
    crop_shard = lax.axis_index("crops")
    shard_count = lax.axis_size("crops")
    crop_kind = size_group[crop_shard]
    large_count = jnp.sum(size_group).astype(jnp.float32)
    counts = jnp.stack([shard_count - large_count, large_count])
    case_index = lax.axis_index("branch") * 2 + crop_kind
    phase_total = 2 * BLOCKS + 3
    zero_canvas = jnp.zeros((ROWS, 128), jnp.float32)
    empty_buffer = jnp.zeros((4, MSG_ROWS, 128), jnp.bfloat16)

    def run_phase(function, statics, operands):
        branches_list = [
            partial(function, branch_index, size_kind, *statics)
            for branch_index in range(4)
            for size_kind in range(2)
        ]
        return lax.switch(case_index, branches_list, *operands)

    def statistics(local_totals):
        return lax.psum(local_totals, "crops")

    def module_forward(module, start_canvas, kept):
        module_weights = weights[0, module]
        module_gains = gains[0, module]
        module_shifts = shifts[0, module]
        record = SimpleNamespace(sources=[], preacts=[], totals=[])
        h_canvas = start_canvas
        u_canvas = zero_canvas
        chain_canvas = zero_canvas
        buffer = empty_buffer
        for phase_index in range(phase_total):
            if phase_index < 2 * BLOCKS:
                source = h_canvas if phase_index % 2 == 0 else u_canvas
            elif phase_index == 2 * BLOCKS:
                source = h_canvas
            else:
                source = chain_canvas
            preact, local_totals = run_phase(forward_conv, (phase_index,), (source, module_weights))
            global_totals = kept.totals[phase_index] if kept else statistics(local_totals)
            produced, buffer = run_phase(
                forward_norm,
                (phase_index,),
                (preact, global_totals, counts, module_gains, module_shifts, h_canvas, buffer),
            )
            record.sources.append(source)
            record.preacts.append(preact)
            record.totals.append(global_totals)
            if phase_index < 2 * BLOCKS:
                if phase_index % 2 == 0:
                    u_canvas = produced
                else:
                    h_canvas = produced
            else:
                chain_canvas = produced
        received = (
            kept.received
            if kept
            else jax.tree.map(
                lambda part, own: part.astype(own.dtype),
                lax.all_to_all(as_sent(buffer), "branch", split_axis=0, concat_axis=0, tiled=True),
                buffer,
            )
        )
        result, summed = run_phase(receive_forward, (), (h_canvas, received))
        record.summed = summed
        record.received = received
        return (result, record)

    checkpoints = [features[0].astype(jnp.float32)]
    first_records = []
    for module in range(MODULES):
        result, record = module_forward(module, checkpoints[-1], None)
        checkpoints.append(result)
        first_records.append(record)
    outputs = checkpoints[-1].astype(jnp.bfloat16)
    grad_canvas = cotangent[0].astype(jnp.float32)
    module_grads = [None] * MODULES
    gain_grads = [None] * MODULES
    shift_grads = [None] * MODULES
    for module in reversed(range(MODULES)):
        kept = None
        unused_result, record = module_forward(module, checkpoints[module], kept)
        module_module_weights = weights[0, module]
        module_module_gains = gains[0, module]
        module_module_shifts = shifts[0, module]
        summed_grad, back_buffer = run_phase(receive_backward, (), (grad_canvas, record.summed))
        message_grads = jax.tree.map(
            lambda part, own: part.astype(own.dtype),
            lax.all_to_all(as_sent(back_buffer), "branch", split_axis=0, concat_axis=0, tiled=True),
            back_buffer,
        )
        top_grad = summed_grad
        chain_grad = zero_canvas
        u_grad = zero_canvas
        pending_skip = zero_canvas
        weight_parts = [None] * phase_total
        gain_total = jnp.zeros(gains.shape[2:], jnp.float32)
        shift_total = jnp.zeros(gains.shape[2:], jnp.float32)
        for module_phase_index in reversed(range(phase_total)):
            if module_phase_index >= 2 * BLOCKS:
                output_grad = chain_grad
                skip_canvas = zero_canvas
            elif module_phase_index % 2 == 1:
                output_grad = top_grad
                skip_canvas = record.sources[module_phase_index - 1]
            else:
                output_grad = u_grad
                skip_canvas = zero_canvas
            module_preact = record.preacts[module_phase_index]
            totals = record.totals[module_phase_index]
            upstream, module_local_totals, skip_grad = run_phase(
                backward_stats,
                (module_phase_index,),
                (
                    output_grad,
                    message_grads,
                    module_preact,
                    totals,
                    counts,
                    module_module_gains,
                    module_module_shifts,
                    skip_canvas,
                ),
            )
            grad_totals = lax.psum(module_local_totals, "crops")
            source_grad, weight_parts[module_phase_index], gain_part, shift_part = run_phase(
                backward_apply,
                (module_phase_index,),
                (
                    upstream,
                    module_preact,
                    totals,
                    grad_totals,
                    counts,
                    record.sources[module_phase_index],
                    module_module_weights,
                    module_module_gains,
                ),
            )
            gain_total = gain_total + gain_part
            shift_total = shift_total + shift_part
            if module_phase_index > 2 * BLOCKS:
                chain_grad = source_grad
            elif module_phase_index == 2 * BLOCKS:
                top_grad = top_grad + source_grad
            elif module_phase_index % 2 == 1:
                u_grad = source_grad
                pending_skip = skip_grad
            else:
                top_grad = source_grad + pending_skip
        joined = jnp.concatenate(weight_parts)
        weight_grad = jnp.pad(joined, (0, weights.shape[2] - joined.shape[0]))
        grad_canvas, weight_grad, gain_grads[module], shift_grads[module] = (
            top_grad,
            weight_grad,
            gain_total,
            shift_total,
        )
        module_grads[module] = weight_grad
    weight_out = lax.psum_scatter(jnp.stack(module_grads), "crops", scatter_dimension=1, tiled=True)
    share = gains.shape[3] // shard_count
    gain_out = lax.dynamic_slice_in_dim(jnp.stack(gain_grads), crop_shard * share, share, axis=2)
    shift_out = lax.dynamic_slice_in_dim(jnp.stack(shift_grads), crop_shard * share, share, axis=2)
    return (outputs[None], grad_canvas[None], weight_out[None], gain_out[None], shift_out[None])


LANES = 128
SLOTS = 8
MASKS = 7
DOWN = (((1,), (0,)), ((), ()))
ACROSS = (((1,), (1,)), ((), ()))
ALONG = (((0,), (0,)), ((), ()))


def unit_table(k):
    operations = weighted_plan(k, C0, BLOCKS)
    planes = 8 >> k
    channels = C0 << k
    units = {}
    stat = 0

    def add(name, kind, source, lanes_in, planes_in, planes_out, members):
        nonlocal stat
        segs = []
        tile = 0
        for operation, lanes, chain in members:
            cout = operation.cout
            level = operation.level if operation.taps == 3 else operation.dest
            segs.append(
                SimpleNamespace(
                    slot=operation.slot,
                    off=operation.offset // LANES,
                    cin=operation.cin,
                    cout=cout,
                    taps=operation.taps,
                    tile=tile,
                    tiles=lanes // LANES,
                    blocks=max(1, (8 >> level)),
                    dest=operation.dest,
                    act=operation.act,
                    chain=chain,
                    up=k - operation.dest if operation.taps == 1 else 0,
                )
            )
            tile += lanes // LANES
        rows = {"s1": (384, 384, 512, 768)[k], "s2": lanes_in + LANES, "p1": 256}[kind]
        units[name] = SimpleNamespace(
            name=name,
            kind=kind,
            source=source,
            lanes_in=lanes_in,
            blocks_in=planes_in,
            planes_in=planes_in,
            planes=planes_out,
            segs=segs,
            tiles=tile,
            rows=rows,
            stat=stat,
            depth=1 if kind == "p1" else 3,
        )
        stat += tile

    add("a", "s1", "h", 256, planes, planes, [(operations[0], 256, None)])
    add("b", "s1", "u", 256, planes, planes, [(operations[1], 256, None)])
    ups = [operation for operation in operations if operation.taps == 1]
    if ups:
        add("u", "p1", "t", 256, planes, planes, [(operation, 256, None) for operation in ups])
    firsts, chains = [], {}
    for target in range(k + 1, 4):
        steps = [
            operation
            for operation in operations
            if operation.taps == 3 and operation.stride == 2
        ]
        start = sum(i - k for i in range(k + 1, target))
        chains[target] = steps[start : start + target - k]
        if target == k + 1:
            firsts.append((chains[target][0], 256, None))
        else:
            firsts.append((chains[target][0], LANES, "c1" if target == k + 2 else "c2"))
    if firsts:
        add("d", "s2", "t", 256, planes, planes // 2, firsts)
    if k <= 1:
        add("e", "s2", "c1", LANES, planes // 2, planes // 4, [(chains[k + 2][1], 256, None)])
    if k == 0:
        add("f", "s2", "c2", LANES, planes // 2, planes // 4, [(chains[3][1], LANES, "c3")])
        add("g", "s2", "c3", LANES, planes // 4, planes // 8, [(chains[3][2], 256, None)])
    return units


def links(k, unit, seg):
    cin = seg.cin
    count_in, count_out = unit.blocks_in, seg.blocks
    found = []
    if unit.kind == "p1":
        for plane in range(count_in):
            wide = 1 << seg.up
            found.append((plane * cin, 0, set(range(plane * wide, plane * wide + wide))))
        return found
    if unit.kind == "s1" and k == 3:
        return [(256 * tap, tap, {0}) for tap in range(3)]
    stride = 1 if unit.kind == "s1" else 2
    for plane in range(count_in):
        for tap in range(3):
            at = plane - tap + 1
            if at % stride == 0 and 0 <= at // stride < count_out:
                found.append((plane * cin, tap, {at // stride}))
    if stride == 1:
        found.append((256, 2, {count_out - 1}))
        found.append((unit.rows - cin, 0, {0}))
    else:
        lanes_in = unit.lanes_in
        found.append((lanes_in + (count_in - 1) * cin - (lanes_in - LANES), 0, {0}))
    return found


def message_slot(k, other):
    return sum(2 * (8 >> max(k, before)) for before in range(other) if before != k)


def log2(value):
    return value.bit_length() - 1


def sigmoid_of(value):
    return 0.5 * jnp.tanh(0.5 * value) + 0.5


def silu_of(value):
    return value * sigmoid_of(value)


def slope_of(value):
    sigmoid = sigmoid_of(value)
    return sigmoid * (1.0 + value * (1.0 - sigmoid))


def planes_loop(count, body, turns=1):
    def step(index, carry):
        for turn in range(turns):
            body(index * turns + turn)
        return carry

    turns = min(turns, count)
    if count == turns:
        for index in range(count):
            body(index)
    else:
        lax.fori_loop(0, count // turns, step, 0)


def planes_sum(count, body, initial, turns=1):
    def step(index, carry):
        for turn in range(turns):
            carry = body(index * turns + turn, carry)
        return carry

    turns = min(turns, count)
    if count == turns:
        return step(0, initial)
    return lax.fori_loop(0, count // turns, step, initial)


def partial_sum(value):
    rows = value.shape[0]
    return jnp.sum(value.reshape(rows // 8, 8, value.shape[1]), axis=0)


class Planes:
    def __init__(self, mode, tiles, planes, masks, rows, main, edge=None, right=None, narrow=False):
        self.narrow, self.pending = narrow, {}
        self.mode, self.tiles, self.planes = mode, tiles, planes
        self.masks, self.rows = masks, rows
        self.main, self.edge, self.right = main, edge, right
        self.base = 1 if mode in ("s1", "wide", "s2") else 0
        extra = {"s1": 2, "wide": 2, "s2": 1, "dz2": 1, "p": 0}[mode]
        self.span = planes + extra
        self.unit = tiles * self.span

    def at(self, m, tile, plane):
        return m * self.unit + tile * self.span + plane + self.base

    def edge_at(self, m, tile, plane):
        if self.mode == "s2" or self.narrow:
            return m * self.span + plane + self.base
        return self.at(m, tile, plane)

    def from_left(self, value):
        return pltpu.roll(value, 1, 0) * self.masks[1]

    def from_right(self, value):
        return pltpu.roll(value, self.rows - 1, 0) * self.masks[2]

    def store(self, m, tile, plane, value):
        self.put(m, tile, plane, value)
        if isinstance(plane, int):
            if plane == self.planes - 1:
                self.put_above(m, tile, value)
            if plane == 0:
                self.put_below(m, tile, value)

    def put(self, m, tile, plane, value):
        where = self.at(m, tile, plane)
        self.main[where] = value.astype(jnp.bfloat16)
        if self.mode == "s1":
            side = self.from_right(value) if tile == 0 else self.from_left(value)
            if not self.narrow:
                self.edge[where] = side.astype(jnp.bfloat16)
            elif tile == 0:
                self.pending[plane if isinstance(plane, int) else self.span] = side
            else:
                lane = lax.broadcasted_iota(jnp.int32, side.shape, 1)
                other = self.pending.pop(plane if isinstance(plane, int) else self.span)
                side = jnp.where(lane < LANES // 2, other, side)
                self.edge[self.edge_at(m, tile, plane)] = side.astype(jnp.bfloat16)
        elif self.mode == "wide":
            self.edge[where] = self.from_left(value).astype(jnp.bfloat16)
            self.right[where] = self.from_right(value).astype(jnp.bfloat16)
        elif self.mode == "s2":
            if tile == self.tiles - 1:
                self.edge[self.edge_at(m, tile, plane)] = self.from_left(value).astype(jnp.bfloat16)
        elif self.mode == "dz2":
            self.edge[where] = self.from_right(value).astype(jnp.bfloat16)

    def put_above(self, m, tile, last):
        if self.mode in ("s1", "wide", "s2"):
            above = pltpu.roll(last, 6, 0) * self.masks[3] + pltpu.roll(last, 3, 0) * self.masks[4]
            self.put(m, tile, -1, above)

    def put_below(self, m, tile, first):
        if self.mode in ("s1", "wide", "dz2"):
            rows = self.rows
            below = (
                pltpu.roll(first, rows - 6, 0) * self.masks[5]
                + pltpu.roll(first, rows - 3, 0) * self.masks[6]
            )
            self.put(m, tile, self.planes, below)

    def close(self, m):
        for tile in range(self.tiles):
            last = self.main[self.at(m, tile, self.planes - 1)].astype(jnp.float32)
            self.put_above(m, tile, last)
        for tile in range(self.tiles):
            first = self.main[self.at(m, tile, 0)].astype(jnp.float32)
            self.put_below(m, tile, first)


class Branch:
    def __init__(self, k, rows, large, small, share, refs, masks, core):
        self.k, self.rows, self.refs, self.masks = k, rows, refs, masks
        self.units = unit_table(k)
        self.planes = 8 >> k
        self.core = core
        self.large, self.small, self.count = large, small, large + small
        self.cells = (small * (SH // 8) * (SW // 8), large * (LH // 8) * (LW // 8))
        self.quarter = lax.axis_index("crops") // 2
        self.share = share
        r = refs
        make = partial(Planes, masks=masks, rows=rows)
        make_one = partial(make, narrow=k <= 1)
        one = "wide" if k == 3 else "s1"
        self.maps = dict(
            h=make_one(one, 2, self.planes, main=r.hC, edge=r.hE, right=r.hR),
            u=make_one(one, 2, self.planes, main=r.uC, edge=r.uE, right=r.uR),
            t=make("p" if k == 3 else "s2", 2, self.planes, main=r.tC, edge=r.tE),
        )
        if k <= 1:
            self.maps["c1"] = make("s2", 1, self.planes // 2, main=r.c1C, edge=r.c1E)
        if k == 0:
            self.maps["c2"] = make("s2", 1, 4, main=r.c2C, edge=r.c2E)
            self.maps["c3"] = make("s2", 1, 2, main=r.c3C, edge=r.c3E)
        self.grads = dict(t=r.gt, u=r.gu, c1=r.gc1, c2=r.gc2, c3=r.gc3)

    def lane_block(self, shape, cout):
        lanes = lax.broadcasted_iota(jnp.int32, shape, 1)
        return lanes >> log2(cout)

    def keep(self, value, cout, which):
        count = LANES // cout
        if len(which) == count:
            return value
        block = self.lane_block(value.shape, cout)
        mask = block == which[0]
        for entry in which[1:]:
            mask = mask | (block == entry)
        return jnp.where(mask, value, 0.0)

    def spread(self, value, cout):
        shift = LANES // 2
        while shift >= cout:
            value = value + pltpu.roll(value, shift, 1)
            shift //= 2
        return value

    def local_blocks(self, seg, tile, wanted):
        count = LANES // seg.cout
        return [q for q in range(count) if (tile * count + q) % seg.blocks in wanted]


    def segments(self):
        return [(unit, seg) for unit in self.units.values() for seg in unit.segs]

    def pieces(self):
        found, place = [], 0
        for index, (unit, seg) in enumerate(self.segments()):
            count = 2 * seg.taps**2 * seg.cin * seg.cout // LANES
            if self.k < 3:
                found.append((index, 0, count, place, index))
                place += count
            else:
                for d in range(unit.depth):
                    slot = len(found) % 3
                    found.append((index, d, count // unit.depth, slot * 3072, slot))
        return found

    def fetch(self, at):
        r = self.refs
        index, d, count, place, sem = self.pieces()[at]
        _, seg = self.segments()[index]
        return pltpu.make_async_copy(
            r.w.at[pl.ds(2 * seg.off + d * count, count)],
            r.raw.at[pl.ds(place, count)],
            r.wsem.at[sem],
        )

    def fetch_first(self):
        for at in range(len(self.pieces()) if self.k < 3 else 3):
            self.fetch(at).start()

    def expand(self, index):
        unit, seg = self.segments()[index]
        pieces = self.pieces()
        mine = [at for at, piece in enumerate(pieces) if piece[0] == index]
        if self.k < 3:
            (at,) = mine
            self.fetch(at).wait()
            count = pieces[at][2] // unit.depth
            planes_loop(
                unit.depth,
                lambda d: self.expand_row(unit, seg, d, count, pieces[at][3] + d * count),
            )
        else:
            for d, at in enumerate(mine):
                self.fetch(at).wait()
                self.expand_row(unit, seg, d, pieces[at][2], pieces[at][3])
                if at + 3 < len(pieces):
                    self.fetch(at + 3).start()
        for m in range(MODULES):
            self.spread_tables(m, unit, seg)

    def expand_row(self, unit, seg, d, count, place):
        r = self.refs
        chunk = math.gcd(count, 384)
        wf, rep = r.work, r.rep

        def widen(step):
            at = pl.multiple_of(step * chunk, 16)
            value = r.raw[pl.ds(pl.multiple_of(place + at, 16), chunk)].astype(jnp.float32)
            wf[pl.ds(at, chunk)] = value

        planes_loop(count // chunk, widen)
        count = count // MODULES
        depth, cin, cout = unit.depth, seg.cin, seg.cout
        target = getattr(r, "T" + unit.name)
        twice = unit.kind == "s1" and self.k < 3
        across = getattr(r, "T" + unit.name + unit.name) if twice else None
        by_row = {}
        for row, tap, wanted in links(self.k, unit, seg):
            by_row.setdefault(row, []).append((tap, wanted))

        def module(m):
            if cout < LANES:
                ratio = LANES // cout
                flat = wf[pl.ds(m, count, stride=2)]
                for part in range(ratio):
                    rep[pl.ds(part, count, stride=ratio)] = self.spread(
                        self.keep(flat, cout, [part]), cout
                    )

            def tap_rows(tap, tile):
                if cout < LANES:
                    return rep[tap * cin : (tap + 1) * cin]
                if cout == LANES:
                    return wf[pl.ds(m + tap * (2 * cin), cin, stride=2)]
                return wf[pl.ds(m + tap * (4 * cin) + 2 * tile, cin, stride=4)]

            def place(goal, taps_at, width, column, tile):
                made = {}
                for row in range(0, unit.rows, cin):
                    key = []
                    for tap, wanted in by_row.get(row, []):
                        local = self.local_blocks(seg, tile, wanted) if width <= LANES else [0]
                        if local:
                            key.append((tap, tuple(local)))
                    key = tuple(key)
                    if key not in made:
                        total = None
                        for tap, local in key:
                            piece = taps_at[tap]
                            if width <= LANES:
                                piece = self.keep(piece, width, local)
                            total = piece if total is None else total + piece
                        if total is None:
                            total = jnp.zeros((cin, LANES), jnp.float32)
                        made[key] = total.astype(jnp.bfloat16)
                    goal[m * depth + d, row : row + cin, column : column + LANES] = made[key]

            width = 3 if seg.taps == 3 else 1
            for tile in range(seg.tiles):
                if tile == 0 or cout > LANES:
                    taps_at = [tap_rows(tap, tile) for tap in range(width)]
                place(target, taps_at, cout, (seg.tile + tile) * LANES, tile)
            if not twice:
                return
            turned = []
            if cin == LANES:
                turned = [jnp.transpose(tap_rows(tap, 0)) for tap in range(3)]
            else:
                both = jnp.transpose(rep[0 : -(-3 * cin // LANES) * LANES])
                for tap in range(3):
                    first = tap * cin // LANES * LANES
                    value = both[0:cin, first : first + LANES]
                    value = self.keep(value, cin, [tap * cin % LANES // cin])
                    turned.append(self.spread(value, cin))
            for tile in range(2):
                place(across, turned[::-1], cin, tile * LANES, tile)

        planes_loop(MODULES, module)


    def parts(self, unit, source):
        if unit.kind == "p1":
            return [(source.main, range(2), source.at)]
        if source.mode == "wide":
            return [
                (source.edge, range(2), source.at),
                (source.main, range(2), source.at),
                (source.right, range(2), source.at),
            ]
        if unit.kind == "s1":
            tiles = [0] if source.narrow else range(2)
            return [(source.main, range(2), source.at), (source.edge, tiles, source.edge_at)]
        last = source.tiles - 1
        return [
            (source.main, range(source.tiles), source.at),
            (source.edge, [last], source.edge_at),
        ]

    def rows_of(self, unit, part, m, d, first, count):
        ref, tiles, at = part
        pieces = []
        for tile in tiles:
            if unit.kind == "s2":
                rows = [ref[at(m, tile, 2 * (first + q) + d - 1)] for q in range(count)]
                pieces.append(rows[0] if count == 1 else jnp.concatenate(rows, axis=0))
            else:
                shift = d - 1 if unit.kind == "s1" else 0
                pieces.append(
                    ref[pl.ds(at(m, tile, first + shift), count)].reshape(count * self.rows, LANES)
                )
        return pieces

    def conv(self, m, unit):
        r = self.refs
        source = self.maps[unit.source]
        target = getattr(r, "T" + unit.name)
        z = getattr(r, "z" + unit.name)
        planes, tiles, depth = unit.planes, unit.tiles, unit.depth
        chunk = min(planes, 4 if tiles <= 2 else 2)
        lanes = tiles * LANES

        def body(step, sums):
            first = step * chunk
            pieces = []
            for d in range(depth):
                for part in self.parts(unit, source):
                    pieces += self.rows_of(unit, part, m, d, first, chunk)
            left = jnp.concatenate(pieces, axis=1)
            right = target[pl.ds(m * depth, depth), 0 : unit.rows, 0:lanes]
            right = right.reshape(depth * unit.rows, lanes)
            result = lax.dot_general(left, right, DOWN, preferred_element_type=jnp.float32)
            for tile in range(tiles):
                block = result[:, tile * LANES : (tile + 1) * LANES]
                z[pl.ds(m * tiles * planes + tile * planes + first, chunk)] = block.reshape(
                    chunk, self.rows, LANES
                )
            return (sums[0] + partial_sum(result), sums[1] + partial_sum(result * result))

        zero = jnp.zeros((8, lanes), jnp.float32)
        sums = planes_sum(planes // chunk, body, (zero, zero), 2)
        for seg in unit.segs:
            scale = self.per_cell(unit, seg)
            totals = self.fold(seg, sums)
            self.norm_rows(m, unit, seg, totals, scale)

    def per_cell(self, unit, seg):
        blocks = seg.tiles * LANES // seg.cout
        small, large = self.cells
        count = unit.planes * blocks
        return jnp.where(self.core == 0, 1.0 / (large * count), 1.0 / (small * count)).astype(
            jnp.float32
        )

    def fold(self, seg, sums):
        first = seg.tile
        found = []
        for value in sums:
            tiles = [
                value[:, (first + t) * LANES : (first + t + 1) * LANES] for t in range(seg.tiles)
            ]
            if seg.cout <= LANES:
                total = tiles[0]
                for tile in tiles[1:]:
                    total = total + tile
                total = jnp.sum(self.spread(total, seg.cout), axis=0, keepdims=True)
                found.append([total] * seg.tiles)
            else:
                found.append([jnp.sum(tile, axis=0, keepdims=True) for tile in tiles])
        return found

    def table_row(self, ref, m, seg, tile):
        slot = seg.slot
        if seg.cout > LANES:
            return ref[m, slot : slot + 1, tile * LANES : (tile + 1) * LANES]
        row = jnp.broadcast_to(ref[m, slot : slot + 1, 0:LANES], (8, LANES))
        if seg.cout < LANES:
            row = self.spread(self.keep(row, seg.cout, [0]), seg.cout)
        return row[0:1]

    def norm_rows(self, m, unit, seg, totals, scale):
        st = self.refs.st
        for tile in range(seg.tiles):
            average = totals[0][tile] * scale
            variance = totals[1][tile] * scale - average * average
            inverse = lax.rsqrt(variance + EPS)
            where = m * STATS + unit.stat + seg.tile + tile
            factor = st[where, 4:5] * inverse
            st[where, 0:1] = average
            st[where, 1:2] = inverse
            st[where, 2:3] = factor
            st[where, 3:4] = st[where, 5:6] - average * factor

    def spread_tables(self, m, unit, seg):
        st = self.refs.st
        for tile in range(seg.tiles):
            where = m * STATS + unit.stat + seg.tile + tile
            st[where, 4:5] = self.table_row(self.refs.gains, m, seg, tile)
            st[where, 5:6] = self.table_row(self.refs.shifts, m, seg, tile)

    def normed(self, m, unit, tile, plane):
        st = self.refs.st
        z = getattr(self.refs, "z" + unit.name)
        where = m * STATS + unit.stat + tile
        value = z[m * unit.tiles * unit.planes + tile * unit.planes + plane]
        return value * st[where, 2:3] + st[where, 3:4]

    def apply_a(self, m):
        unit, u = self.units["a"], self.maps["u"]

        def body(plane):
            for tile in range(2):
                value = silu_of(self.normed(m, unit, tile, plane)) * self.masks[0]
                u.store(m, tile, plane, value)

        planes_loop(self.planes, body, TURNS)

    def apply_b(self, m):
        unit, top = self.units["b"], self.maps["t"]
        hf, s = self.refs.hf, self.refs.s

        def body(plane):
            for tile in range(2):
                where = m * 2 * self.planes + tile * self.planes + plane
                value = silu_of(self.normed(m, unit, tile, plane) + hf[where]) * self.masks[0]
                s[where] = value
                top.store(m, tile, plane, value)

        planes_loop(self.planes, body, TURNS)

    def apply_rest(self, m, unit):
        sb = self.refs.sb
        for seg in unit.segs:
            chain = self.maps[seg.chain] if seg.chain else None

            def body(plane):
                for tile in range(seg.tiles):
                    value = self.normed(m, unit, seg.tile + tile, plane)
                    if chain is not None:
                        chain.store(m, tile, plane, silu_of(value) * self.masks[0])
                    else:
                        at = message_slot(self.k, seg.dest) + tile * unit.planes + plane
                        sb[at] = value.astype(jnp.bfloat16)

            planes_loop(unit.planes, body, TURNS)
            if chain is None:
                self.message(m, seg.dest).start()

    def message(self, e, other):
        count = 2 * (8 >> max(self.k, other))
        r = self.refs
        return pltpu.make_async_remote_copy(
            src_ref=r.sb.at[pl.ds(message_slot(self.k, other), count)],
            dst_ref=r.rb.at[pl.ds(e * 16 + message_slot(other, self.k), count)],
            send_sem=r.ssem.at[e * 4 + other],
            recv_sem=r.rsem.at[e * 4 + self.k],
            device_id=dict(branch=other),
            device_id_type=pl.DeviceIdType.MESH,
        )

    def arrived(self, e, other):
        count = 2 * (8 >> max(self.k, other))
        r = self.refs
        at = message_slot(self.k, other)
        return pltpu.make_async_remote_copy(
            src_ref=r.sb.at[pl.ds(at, count)],
            dst_ref=r.rb.at[pl.ds(e * 16 + at, count)],
            send_sem=r.ssem.at[e * 4 + other],
            recv_sem=r.rsem.at[e * 4 + other],
            device_id=dict(branch=other),
            device_id_type=pl.DeviceIdType.MESH,
        )

    def others(self):
        return [other for other in range(4) if other != self.k]

    def sent(self, e):
        for other in self.others():
            self.message(e, other).wait_send()

    def receive(self, m):
        r = self.refs
        s, rb, hf, out = r.s, r.rb, r.hf, r.outs
        h = self.maps["h"]

        def total_at(tile, plane):
            where = m * 2 * self.planes + tile * self.planes + plane
            total = s[where]
            for other in self.others():
                count = 8 >> max(self.k, other)
                at = plane >> max(0, other - self.k)
                slot = m * 16 + message_slot(self.k, other) + tile * count + at
                total = total + rb[slot].astype(jnp.float32)
            s[where] = total
            return silu_of(total) * self.masks[0]

        def onward(plane):
            for tile in range(2):
                value = total_at(tile, plane)
                hf[(2 + tile) * self.planes + plane] = value
                h.store(1, tile, plane, value)

        def finish(plane):
            for tile in range(2):
                out[tile * self.planes + plane] = total_at(tile, plane).astype(jnp.bfloat16)

        @pl.when(m + 1 < MODULES)
        def _():
            planes_loop(self.planes, onward, TURNS)

        @pl.when(m + 1 == MODULES)
        def _():
            planes_loop(self.planes, finish, TURNS)

    def take_feature(self, tile, plane, value):
        self.refs.hf[tile * self.planes + plane] = value
        self.maps["h"].store(0, tile, plane, value)

    def take_cotangent(self, tile, plane, value):
        self.refs.gin[tile * self.planes + plane] = value

    def member(self, kind, order):
        kinds = self.refs.kinds
        found, before = jnp.int32(0), jnp.int32(0)
        for at in range(self.count):
            same = kinds[at] == kind
            found = jnp.where(same & (before == order), at, found)
            before = before + same.astype(jnp.int32)
        return found

    def order(self, device):
        kinds = self.refs.kinds
        kind = kinds[device]
        before = jnp.int32(0)
        for at in range(self.count):
            before = before + ((kinds[at] == kind) & (at < device)).astype(jnp.int32)
        return before

    def unpack(self, t, consume):
        r = self.refs
        work, rows, planes = r.work, self.rows, self.planes
        full = SH * SW * C0 // LANES
        gath = r.gathc if t else r.gathx

        @pl.when(self.core == 0)
        def _():
            for at in range(self.large):
                block = gath[self.member(1, at)]
                work[at * ROWS : (at + 1) * ROWS] = block.astype(jnp.float32)

        @pl.when(self.core == 1)
        def _():
            for at in range(self.small):
                block = gath[self.member(0, at), 0:full]
                work[at * full : (at + 1) * full] = block.astype(jnp.float32)
            work[self.small * full : self.large * ROWS] = jnp.zeros(
                (self.large * ROWS - self.small * full, LANES), jnp.float32
            )

        deep = self.large * ROWS // 2
        right = jnp.concatenate([work[pl.ds(j, deep, stride=2)] for j in range(2)], axis=1)
        right = right.astype(jnp.bfloat16)
        cells = Cells(self.core, (rows, LANES), self.small, self.large)
        base = cells.crop * cells.pick(ROWS // 2, full // 2)
        base = base + cells.along * (planes * cells.wide) + cells.across
        base = jnp.where(cells.valid, base, -(1 << 20))
        lane = lax.broadcasted_iota(jnp.int32, (rows, LANES), 1)
        chunk = min(planes, 4)

        def body(step):
            pieces = []
            for q in range(chunk):
                goal = base + (step * chunk + q) * cells.wide
                pieces.append(one_hot(goal, lane, deep))
            left = pieces[0] if chunk == 1 else jnp.concatenate(pieces, axis=0)
            result = lax.dot_general(left, right, DOWN, preferred_element_type=jnp.float32)
            for q in range(chunk):
                for tile in range(2):
                    value = result[q * rows : (q + 1) * rows, tile * LANES : (tile + 1) * LANES]
                    consume(tile, step * chunk + q, value)

        planes_loop(planes // chunk, body)

    def pack_size(self):
        return 48 * self.planes, -(-self.planes * self.rows // LANES) * LANES

    def plan_pack(self):
        r = self.refs
        high, deep = self.pack_size()
        planes = self.planes
        q = lax.broadcasted_iota(jnp.int32, (high, LANES), 0)
        lane = lax.broadcasted_iota(jnp.int32, (high, LANES), 1)
        wide, tall = jnp.where(self.core == 0, 6, 3), jnp.where(self.core == 0, 8, 4)
        cell = jnp.where(self.core == 0, (q * 43691) >> 18, (q * 43691) >> 17)
        across = q - cell * wide
        plane = cell & (planes - 1)
        along = cell >> log2(planes)
        base = plane * self.rows + along * wide + across
        base = jnp.where(along < tall, base, -(1 << 20))
        shard = lax.axis_index("crops")
        for at, device in enumerate((shard, shard + 1 - 2 * self.core)):
            goal = base + self.order(device) * (wide * tall)
            r.hot[at, 0:high, 0:deep] = one_hot(goal, lane, deep)

    def pack(self, units, put):
        high, deep = self.pack_size()
        right = jnp.concatenate([units(tile) for tile in range(2)], axis=1)
        short = deep - right.shape[0]
        parts = [right.astype(jnp.bfloat16)]
        if right.dtype == jnp.float32:
            parts.append((right - parts[0].astype(jnp.float32)).astype(jnp.bfloat16))
        if short:
            empty = jnp.zeros((short, 2 * LANES), jnp.bfloat16)
            parts = [jnp.concatenate([part, empty], axis=0) for part in parts]
        for at in range(2):
            total = None
            for part in parts:
                piece = lax.dot_general(
                    self.refs.hot[at, 0:high, 0:deep],
                    part,
                    DOWN,
                    preferred_element_type=jnp.float32,
                )
                total = piece if total is None else total + piece
            for tile in range(2):
                put(at, pl.ds(tile, high, stride=2), total[:, tile * LANES : (tile + 1) * LANES])

    def pack_outputs(self):
        r = self.refs
        high = 2 * self.pack_size()[0]

        def put(at, where, value):
            r.work[pl.ds(at * ROWS + where.start, where.size, stride=2)] = value

        def units(tile):
            block = r.outs[tile * self.planes : (tile + 1) * self.planes]
            return block.reshape(self.planes * self.rows, LANES)

        self.pack(units, put)
        for at in range(2):
            r.blocks[at, 0:high] = r.work[at * ROWS : at * ROWS + high].astype(jnp.bfloat16)
            if high < ROWS:
                r.blocks[at, high:ROWS] = jnp.zeros((ROWS - high, LANES), jnp.bfloat16)

    def pack_gradient(self):
        r = self.refs
        high = 2 * self.pack_size()[0]

        def put(at, where, value):
            r.slopes[at, where] = value

        def units(tile):
            block = r.gin[tile * self.planes : (tile + 1) * self.planes]
            return block.reshape(self.planes * self.rows, LANES)

        self.pack(units, put)
        if high < ROWS:
            for at in range(2):
                r.slopes[at, high:ROWS] = jnp.zeros((ROWS - high, LANES), jnp.float32)

    def forward(self, m, gather):
        def also(module, step):
            pl.when(m == module)(lambda: gather.step(1, step))

        self.conv(m, self.units["a"])
        self.apply_a(m)
        self.conv(m, self.units["b"])
        self.apply_b(m)
        also(0, 1)
        also(1, 3)

        @pl.when(m > 0)
        def _():
            self.sent(m - 1)

        for name in ("d", "u", "e", "f", "g"):
            if name in self.units:
                self.conv(m, self.units[name])
                self.apply_rest(m, self.units[name])
        also(0, 2)

        @pl.when(m == MODULES - 1)
        def _():
            gather.collect(1)
            self.unpack(1, self.take_cotangent)

        for other in self.others():
            self.arrived(m, other).wait_recv()
        self.receive(m)


    def send_back(self, m):
        r = self.refs
        s, gin, gt, sb = r.s, r.gin, r.gt, r.sb
        e = MODULES + m

        def body(plane):
            for tile in range(2):
                at = tile * self.planes + plane
                value = gin[at] * slope_of(s[m * 2 * self.planes + at])
                gt[at] = value
                for other in range(self.k):
                    sb[message_slot(self.k, other) + at] = value.astype(jnp.bfloat16)

        planes_loop(self.planes, body, TURNS)
        for other in reversed(self.others()):
            if other > self.k:
                count = 8 >> other
                wide = 1 << (other - self.k)

                def pool(plane):
                    for tile in range(2):
                        total = gt[tile * self.planes + plane * wide]
                        for step in range(1, wide):
                            total = total + gt[tile * self.planes + plane * wide + step]
                        slot = message_slot(self.k, other) + tile * count + plane
                        sb[slot] = total.astype(jnp.bfloat16)

                planes_loop(count, pool, TURNS)
            self.message(e, other).start()

    def back_unit(self, m, unit):
        r = self.refs
        st, dyb, z = r.st, r.dyb, getattr(r, "z" + unit.name)
        name, planes, tiles = unit.name, unit.planes, unit.tiles
        e = MODULES + m
        sums = {}

        def upstream(seg, tile, plane, normed):
            at = tile * planes + plane
            if name == "b":
                hf = r.hf[m * 2 * planes + at]
                value = r.gt[at] * slope_of(normed + hf)
                r.gin[at] = value
                return value
            if name == "a":
                return r.gu[at] * slope_of(normed)
            if seg.chain:
                return self.grads[seg.chain][at] * slope_of(normed)
            return r.rb[e * 16 + message_slot(self.k, seg.dest) + at].astype(jnp.float32)

        for seg in unit.segs:

            def body(plane, carry):
                result = []
                for tile in range(seg.tiles):
                    at = (seg.tile + tile) * planes + plane
                    where = m * STATS + unit.stat + seg.tile + tile
                    value = z[m * tiles * planes + at]
                    normed = value * st[where, 2:3] + st[where, 3:4]
                    dy = upstream(seg, tile, plane, normed)
                    dyb[at] = dy
                    zhat = (value - st[where, 0:1]) * st[where, 1:2]
                    result.append(carry[2 * tile] + partial_sum(dy))
                    result.append(carry[2 * tile + 1] + partial_sum(dy * zhat))
                return tuple(result)

            zero = jnp.zeros((8, LANES), jnp.float32)
            found = planes_sum(planes, body, (zero,) * (2 * seg.tiles), TURNS)
            pair = [
                jnp.concatenate([found[2 * tile + which] for tile in range(seg.tiles)], axis=1)
                for which in range(2)
            ]
            plain = SimpleNamespace(**vars(seg))
            plain.tile = 0
            totals = self.fold(plain, pair)
            self.table_grads(m, seg, totals)
            sums[seg.slot] = totals
        dz = self.dz_planes(unit)
        for seg in unit.segs:
            scale = self.per_cell(unit, seg)
            totals = sums[seg.slot]

            def apply(plane):
                for tile in range(seg.tiles):
                    at = (seg.tile + tile) * planes + plane
                    where = m * STATS + unit.stat + seg.tile + tile
                    zhat = (z[m * tiles * planes + at] - st[where, 0:1]) * st[where, 1:2]
                    inner = dyb[at] - totals[0][tile] * scale - zhat * (totals[1][tile] * scale)
                    dz.store(0, seg.tile + tile, plane, inner * st[where, 2:3] * self.masks[0])

            planes_loop(planes, apply, TURNS)
        self.back_data(m, unit, dz)
        first = min(seg.off for seg in unit.segs)
        last = max(seg.off + seg.taps**2 * seg.cin * seg.cout // LANES for seg in unit.segs)
        wanted = (self.quarter * self.share < last) & ((self.quarter + 1) * self.share > first)

        @pl.when(wanted)
        def _():
            self.back_kernel(m, unit, dz)

    def dz_planes(self, unit):
        r = self.refs
        mode = {"p1": "p", "s2": "dz2", "s1": "wide" if self.k == 3 else "s1"}[unit.kind]
        return Planes(
            mode,
            unit.tiles,
            unit.planes,
            self.masks,
            self.rows,
            r.dC,
            r.dE,
            r.dR,
            self.k <= 1 and unit.kind == "s1",
        )

    def table_grads(self, m, seg, totals):
        gg = self.refs.gg
        slot = seg.slot
        for which, found in ((0, totals[1]), (1, totals[0])):
            if seg.cout > LANES:
                for tile in range(2):
                    gg[m, which, slot : slot + 1, tile * LANES : (tile + 1) * LANES] = found[tile]
            else:
                row = jnp.broadcast_to(found[0], (8, LANES))
                if seg.cout < LANES:
                    row = self.keep(row, seg.cout, [0])
                gg[m, which, slot : slot + 1, 0:LANES] = row[0:1]

    def wide_rows(self, ref, at, tiles, plane, count):
        pieces = [
            ref[pl.ds(at(0, tile, plane), count)].reshape(count * self.rows, LANES)
            for tile in range(tiles)
        ]
        return pieces[0] if tiles == 1 else jnp.concatenate(pieces, axis=1)

    def back_data(self, m, unit, dz):
        r = self.refs
        kind, tiles = unit.kind, unit.tiles
        target = getattr(r, "T" + unit.name)
        lanes = tiles * LANES
        rows = self.rows

        def kernel_rows(d, first, count):
            return target[m * unit.depth + d, first : first + count, 0:lanes]

        def product(left, right):
            return lax.dot_general(left, right, ACROSS, preferred_element_type=jnp.float32)

        def put(ref, tile, planes, first, count, value, step=1, add=False):
            block = value.reshape(count, rows, LANES)
            for q in range(count):
                at = tile * planes + first + q * step
                ref[at] = ref[at] + block[q] if add else block[q]

        planes = unit.planes
        if kind == "s1":
            goal = r.gu if unit.name == "b" else r.gin
            add = unit.name == "a"
            chunk = min(planes, 4)
            across = getattr(r, "T" + unit.name + unit.name)

            def body(step):
                first = step * chunk
                if self.k == 3:
                    total = None
                    for d in range(3):
                        for ref, at in ((dz.right, 0), (dz.main, 256), (dz.edge, 512)):
                            left = self.wide_rows(ref, dz.at, 2, first + 1 - d, chunk)
                            piece = product(left, kernel_rows(d, at, 256))
                            total = piece if total is None else total + piece
                else:
                    narrow = 1 if dz.narrow else 2
                    left = []
                    for d in range(3):
                        at = first + 1 - d
                        left.append(self.wide_rows(dz.main, dz.at, 2, at, chunk))
                        left.append(self.wide_rows(dz.edge, dz.edge_at, narrow, at, chunk))
                    right = across[pl.ds(m * 3, 3), 0 : unit.rows].reshape(3 * unit.rows, 256)
                    total = lax.dot_general(
                        jnp.concatenate(left, axis=1),
                        right,
                        DOWN,
                        preferred_element_type=jnp.float32,
                    )
                for tile in range(2):
                    put(
                        goal,
                        tile,
                        planes,
                        first,
                        chunk,
                        total[:, tile * LANES : (tile + 1) * LANES],
                        add=add,
                    )

            planes_loop(planes // chunk, body, 2)
            return
        if kind == "p1":
            left = self.wide_rows(dz.main, dz.at, tiles, 0, planes)
            total = product(left, kernel_rows(0, 0, 256))
            for tile in range(2):
                put(
                    r.gt,
                    tile,
                    planes,
                    0,
                    planes,
                    total[:, tile * LANES : (tile + 1) * LANES],
                    add=True,
                )
            return
        goal = self.grads[unit.source]
        add = unit.source == "t"
        lanes_in = unit.lanes_in
        count_in = unit.planes_in
        for parity, terms in ((0, [(1, 0)]), (1, [(2, 0), (0, 1)])):
            total, side = None, None
            for d, offset in terms:
                left = self.wide_rows(dz.main, dz.at, tiles, offset, planes)
                piece = product(left, kernel_rows(d, 0, lanes_in))
                total = piece if total is None else total + piece
                left = self.wide_rows(dz.edge, dz.at, tiles, offset, planes)
                piece = product(left, kernel_rows(d, lanes_in, LANES))
                side = piece if side is None else side + piece
            for tile in range(lanes_in // LANES):
                value = total[:, tile * LANES : (tile + 1) * LANES]
                if tile == lanes_in // LANES - 1:
                    value = value + side
                put(goal, tile, count_in, parity, planes, value, step=2, add=add)

    def back_kernel(self, m, unit, dz):
        r = self.refs
        G, rep, wgv = r.work, r.rep, r.wgv
        tiles, planes = unit.tiles, unit.planes
        source = self.maps[unit.source]
        right = self.wide_rows(dz.main, dz.at, tiles, 0, planes)

        def gather(d):
            at = 0
            for part in self.parts(unit, source):
                pieces = self.rows_of(unit, part, m, d, 0, planes)
                left = pieces[0] if len(pieces) == 1 else jnp.concatenate(pieces, axis=1)
                count = left.shape[1]
                result = lax.dot_general(left, right, ALONG, preferred_element_type=jnp.float32)
                for tile in range(tiles):
                    row = pl.multiple_of((d * tiles + tile) * unit.rows + at, 8)
                    G[pl.ds(row, count)] = result[:, tile * LANES : (tile + 1) * LANES]
                at += count

        if self.k == 3 and unit.kind == "s1":
            self.direct_kernel(m, unit, right)
            return
        planes_loop(unit.depth, gather)
        for seg in unit.segs:
            self.fold_kernel(m, unit, seg)

    def direct_kernel(self, m, unit, right):
        wgv, (seg,) = self.refs.wgv, unit.segs
        source = self.maps[unit.source]
        span = 2 * seg.cin
        low, high = self.quarter * self.share, (self.quarter + 1) * self.share

        def tap_row(d):
            first = seg.off + d * (3 * span)

            @pl.when((first < high) & (first + 3 * span > low))
            def _():
                for column, part in enumerate(self.parts(unit, source)):
                    pieces = self.rows_of(unit, part, m, d, 0, unit.planes)
                    left = jnp.concatenate(pieces, axis=1)
                    result = lax.dot_general(left, right, ALONG, preferred_element_type=jnp.float32)
                    for tile in range(2):
                        rows = pl.ds(first + column * span + tile, seg.cin, stride=2)
                        wgv[rows] = result[:, tile * LANES : (tile + 1) * LANES]

        planes_loop(unit.depth, tap_row)

    def fold_kernel(self, m, unit, seg):
        r = self.refs
        G, rep, wgv = r.work, r.rep, r.wgv
        cin, cout, tiles = seg.cin, seg.cout, unit.tiles
        width = 3 if seg.taps == 3 else 1
        found = links(self.k, unit, seg)
        off = seg.off

        def fold(d):
            for column in range(width):
                tap = d * width + column
                totals = []
                for tile in range(seg.tiles):
                    total = None
                    for row, which, wanted in found:
                        if which != column:
                            continue
                        at = pl.multiple_of((d * tiles + seg.tile + tile) * unit.rows + row, 8)
                        piece = G[pl.ds(at, cin)]
                        if cout <= LANES:
                            local = self.local_blocks(seg, tile, wanted)
                            if not local:
                                continue
                            piece = self.keep(piece, cout, local)
                        total = piece if total is None else total + piece
                    totals.append(total)
                if cout > LANES:
                    for tile in range(2):
                        wgv[pl.ds(off + tap * (2 * cin) + tile, cin, stride=2)] = totals[tile]
                    continue
                total = None
                for piece in totals:
                    if piece is not None:
                        total = piece if total is None else total + piece
                if cout == LANES:
                    wgv[pl.ds(pl.multiple_of(off + tap * cin, 8), cin)] = total
                else:
                    rep[pl.ds(pl.multiple_of(tap * cin, cin), cin)] = self.spread(total, cout)

        planes_loop(unit.depth, fold)
        if cout < LANES:
            ratio = LANES // cout
            count = width * width * cin // ratio
            total = None
            for part in range(ratio):
                piece = self.keep(rep[pl.ds(part, count, stride=ratio)], cout, [part])
                total = piece if total is None else total + piece
            wgv[off : off + count] = total

    def backward(self, m, meanwhile):
        e = MODULES + m
        last = m == MODULES - 1
        self.sent(jnp.where(last, m, e + 1))
        self.send_back(m)
        pl.when(last)(meanwhile)
        for name in ("g", "f", "e", "d", "u"):
            if name in self.units:
                for seg in self.units[name].segs:
                    if seg.dest >= 0:
                        self.arrived(e, seg.dest).wait_recv()
                self.back_unit(m, self.units[name])
        self.back_unit(m, self.units["b"])
        self.back_unit(m, self.units["a"])


STATS = 20
TURNS = 8
NAMES = list(
    dict(x=0, cot=0, w=0, gains=0, shifts=0, kinds=0, out=0, grad=0, wg=0, gain=0, shift=0)
)


def one_hot(goal, lane, deep):
    pieces = [
        jnp.where(goal == lane + first, 1.0, 0.0).astype(jnp.bfloat16)
        for first in range(0, deep, LANES)
    ]
    return jnp.concatenate(pieces, axis=1)


class Cells:
    def __init__(self, core, shape, small, large):
        self.core = core
        row = lax.broadcasted_iota(jnp.int32, shape, 0)
        self.wide = self.pick(LW // 8, SW // 8)
        tall = self.pick(LH // 8, SH // 8)
        self.crop = self.pick((row * 43691) >> 21, (row * 43691) >> 19)
        inner = row - self.crop * (self.wide * tall)
        self.along = self.pick((inner * 43691) >> 18, (inner * 43691) >> 17)
        self.across = inner - self.along * self.wide
        self.valid = self.crop < self.pick(large, small)
        self.last = tall - 1

    def pick(self, large, small):
        return jnp.where(self.core == 0, large, small)


def fill_masks(refs, rows, core, small, large):
    cells = Cells(core, (rows, LANES), small, large)
    valid = cells.valid
    six = cells.wide == 6
    up, down = valid & (cells.along > 0), valid & (cells.along < cells.last)
    tables = (
        valid,
        valid & (cells.across > 0),
        valid & (cells.across < cells.wide - 1),
        up & six,
        up & jnp.logical_not(six),
        down & six,
        down & jnp.logical_not(six),
    )
    for at, table in enumerate(tables):
        refs.masks[at] = jnp.where(table, 1.0, 0.0)


class Gather:
    def __init__(self, refs, core, count):
        self.refs, self.core, self.count = refs, core, count
        self.z = lax.axis_index("crops") // 2
        self.last = count // 2 - 1

    def hop(self, t, source, right):
        r = self.refs
        at = source * 2 + self.core
        gath = r.gathc if t else r.gathx
        to = self.z + 1 if right else self.z - 1
        return pltpu.make_async_remote_copy(
            src_ref=gath.at[at],
            dst_ref=gath.at[at],
            send_sem=r.hsem.at[(t * (self.last + 1) + source) * 3 + (0 if right else 1)],
            recv_sem=r.gsem.at[t * self.count + at],
            device_id=dict(crops=to * 2 + self.core),
            device_id_type=pl.DeviceIdType.MESH,
        )

    def across(self, t, source, core, rows):
        r = self.refs
        at = source * 2 + core
        gath = r.gathc if t else r.gathx
        return pltpu.make_async_remote_copy(
            src_ref=gath.at[at, pl.ds(0, rows)],
            dst_ref=gath.at[at, pl.ds(0, rows)],
            send_sem=r.hsem.at[(t * (self.last + 1) + source) * 3 + 2],
            recv_sem=r.gsem.at[t * self.count + at],
            device_id=dict(crops=self.z * 2 + 1 - self.core),
            device_id_type=pl.DeviceIdType.MESH,
        )

    def each_core(self, action):
        for core, rows in ((0, SH * SW * C0 // LANES), (1, ROWS)):

            @pl.when(self.core == core)
            def _():
                action(core, rows)

    def send(self, t, source, rightward, leftward):
        if rightward:

            @pl.when(self.z < self.last)
            def _():
                self.hop(t, source, True).start()

        if leftward:

            @pl.when(self.z > 0)
            def _():
                self.hop(t, source, False).start()

        self.each_core(lambda core, rows: self.across(t, source, core, rows).start())

    def step(self, t, s):
        r = self.refs
        if s == 0:
            at = self.z * 2 + self.core
            if t:
                r.gathc[at] = r.cot[...]
            else:
                r.gathx[at] = r.x[...]
            self.send(t, self.z, True, True)
            return

        @pl.when(self.z >= s)
        def _():
            self.hop(t, self.z - s, True).wait_recv()
            self.send(t, self.z - s, True, False)

        @pl.when(self.z + s <= self.last)
        def _():
            self.hop(t, self.z + s, True).wait_recv()
            self.send(t, self.z + s, False, True)

    def collect(self, t):
        for source in range(self.last + 1):
            for core, rows in ((0, ROWS), (1, SH * SW * C0 // LANES)):

                @pl.when(self.core == core)
                def _():
                    self.across(t, source, 1 - core, rows).wait_recv()

    def finish(self, t):
        def sent(source, rightward, leftward):
            if rightward:

                @pl.when(self.z < self.last)
                def _():
                    self.hop(t, source, True).wait_send()

            if leftward:

                @pl.when(self.z > 0)
                def _():
                    self.hop(t, source, False).wait_send()

            self.each_core(lambda core, rows: self.across(t, source, core, rows).wait_send())

        sent(self.z, True, True)
        for s in range(1, self.last + 1):

            @pl.when(self.z >= s)
            def _():
                sent(self.z - s, True, False)

            @pl.when(self.z + s <= self.last)
            def _():
                sent(self.z + s, False, True)


def scratch_table(rows, weight_rows, count):
    def half(many):
        return pltpu.VMEM((many, rows, LANES), jnp.bfloat16)

    def full(many):
        return pltpu.VMEM((many, rows, LANES), jnp.float32)

    def expanded(depth, deep, wide):
        return pltpu.VMEM((MODULES * depth, deep, wide), jnp.bfloat16)

    _, span, _ = pair_rows(weight_rows, count)
    return dict(
        masks=full(MASKS),
        hC=half(2 * 20),
        hE=half(2 * 10),
        hR=half(2 * 6),
        uC=half(2 * 20),
        uE=half(2 * 10),
        uR=half(2 * 6),
        tC=half(2 * 18),
        tE=half(2 * 9),
        c1C=half(2 * 5),
        c1E=half(2 * 5),
        c2C=half(2 * 5),
        c2E=half(2 * 5),
        c3C=half(2 * 3),
        c3E=half(2 * 3),
        dC=half(20),
        dE=half(20),
        dR=half(6),
        outs=half(16),
        hf=full(2 * 16),
        s=full(2 * 16),
        za=full(2 * 16),
        zb=full(2 * 16),
        zd=full(2 * 16),
        zu=full(2 * 8),
        ze=full(2 * 4),
        zf=full(2 * 2),
        zg=full(2 * 2),
        gt=full(16),
        gu=full(16),
        gin=full(16),
        gc1=full(4),
        gc2=full(4),
        gc3=full(2),
        dyb=full(16),
        sb=half(16),
        rb=half(4 * 16),
        st=pltpu.VMEM((MODULES * STATS, 8, LANES), jnp.float32),
        Ta=expanded(3, 768, 256),
        Tb=expanded(3, 768, 256),
        Taa=expanded(3, 512, 256),
        Tbb=expanded(3, 512, 256),
        Td=expanded(3, 384, 512),
        Tu=expanded(1, 256, 768),
        Te=expanded(3, 256, 256),
        Tf=expanded(3, 256, 128),
        Tg=expanded(3, 256, 256),
        raw=pltpu.VMEM((9408, LANES), jnp.bfloat16),
        work=pltpu.VMEM((4608, LANES), jnp.float32),
        rep=pltpu.VMEM((640, LANES), jnp.float32),
        wgv=pltpu.VMEM((weight_rows, LANES), jnp.float32),
        wq=pltpu.VMEM((MODULES, 2 * weight_rows // count, LANES), jnp.float32),
        wr=pltpu.VMEM((MODULES, span, LANES), jnp.float32),
        gathx=pltpu.VMEM((count, ROWS, LANES), jnp.bfloat16),
        gathc=pltpu.VMEM((count, ROWS, LANES), jnp.bfloat16),
        hot=pltpu.VMEM((2, 384, 768), jnp.bfloat16),
        blocks=pltpu.VMEM((2, ROWS, LANES), jnp.bfloat16),
        slopes=pltpu.VMEM((2, ROWS, LANES), jnp.float32),
        blockr=pltpu.VMEM((ROWS, LANES), jnp.bfloat16),
        sloper=pltpu.VMEM((ROWS, LANES), jnp.float32),
        gg=pltpu.VMEM((MODULES, 2, SLOTS, 256), jnp.float32),
        ggr=pltpu.VMEM((MODULES, 2, SLOTS, 256), jnp.float32),
        wsem=pltpu.SemaphoreType.DMA((8,)),
        ssem=pltpu.SemaphoreType.DMA((16,)),
        rsem=pltpu.SemaphoreType.DMA((16,)),
        hsem=pltpu.SemaphoreType.DMA((3 * count,)),
        gsem=pltpu.SemaphoreType.DMA((2 * count,)),
        psem=pltpu.SemaphoreType.DMA((5,)),
        qsem=pltpu.SemaphoreType.DMA((5,)),
        osem=pltpu.SemaphoreType.DMA((1,)),
    )


def pair_rows(weight_rows, count):
    share = weight_rows // count
    low = share // 8 * 8
    return share, 2 * share - low, low


def greet(core, count):
    barrier = pltpu.get_barrier_semaphore()
    me, shard = lax.axis_index("branch"), lax.axis_index("crops")
    z = shard // 2

    def signal(**where):
        pl.semaphore_signal(barrier, inc=1, device_id=where, device_id_type=pl.DeviceIdType.MESH)

    for step in range(1, 4):
        signal(branch=lax.rem(me + step, 4))
    signal(crops=shard + 1 - 2 * core)

    @pl.when(z > 0)
    def _():
        signal(crops=shard - 2)

    @pl.when(z < count // 2 - 1)
    def _():
        signal(crops=shard + 2)

    ends = (z == 0).astype(jnp.int32) + (z == count // 2 - 1).astype(jnp.int32)
    pl.semaphore_wait(barrier, 6 - ends)


def whole_kernel(names, rows, large, small, *args):
    refs = SimpleNamespace(**dict(zip(names, args)))
    count = large + small
    me, shard = lax.axis_index("branch"), lax.axis_index("crops")
    core = shard % 2
    weight_rows = refs.wgv.shape[0]
    share, span, low = pair_rows(weight_rows, count)
    quarter = pl.multiple_of(shard // 2 * (2 * share), 8)

    class Lazy:
        def __getitem__(self, index):
            return refs.masks[index]

    def across(source, goal, index):
        return pltpu.make_async_remote_copy(
            src_ref=source,
            dst_ref=goal,
            send_sem=refs.psem.at[index],
            recv_sem=refs.qsem.at[index],
            device_id=dict(crops=shard + 1 - 2 * core),
            device_id_type=pl.DeviceIdType.MESH,
        )

    def kernel_pair(m):
        at = pl.multiple_of(low * (1 - core), 8)
        return across(refs.wq.at[m, pl.ds(at, span)], refs.wr.at[m], m)

    outputs_pair = across(refs.blocks.at[1], refs.blockr, 2)
    gradient_pair = across(refs.slopes.at[1], refs.sloper, 3)
    table_pair = across(refs.gg, refs.ggr, 4)
    gather = Gather(refs, core, count)

    def every(action):
        for k in range(4):

            @pl.when(me == k)
            def _():
                action(Branch(k, rows, large, small, 2 * share, refs, Lazy(), core))

    def begin(branch):
        branch.fetch_first()

    def prepare(branch):
        found = branch.segments()
        stops = {0: 1, min(2, len(found) - 2): 2, len(found) - 1: 3}
        for index, (unit, seg) in enumerate(found):
            branch.expand(index)
            if index in stops:
                gather.step(0, stops[index])

    def main(branch):
        branch.unpack(0, branch.take_feature)
        branch.maps["h"].close(0)
        gather.step(1, 0)

        def ahead(m, carry):
            branch.forward(m, gather)
            return carry

        def meanwhile():
            branch.plan_pack()
            branch.pack_outputs()
            outputs_pair.start()

        def back(step, carry):
            m = MODULES - 1 - step
            branch.backward(m, meanwhile)
            refs.wq[m] = refs.wgv[pl.ds(quarter, 2 * share)]
            kernel_pair(m).start()
            return carry

        lax.fori_loop(0, MODULES, ahead, 0)
        lax.fori_loop(0, MODULES, back, 0)
        branch.sent(MODULES)
        branch.pack_gradient()
        gradient_pair.start()
        table_pair.start()

    every(begin)
    greet(core, count)
    gather.step(0, 0)
    fill_masks(refs, rows, core, small, large)
    refs.wgv[pl.ds(quarter, 2 * share)] = jnp.zeros((2 * share, LANES), jnp.float32)
    refs.gg[...] = jnp.zeros(refs.gg.shape, jnp.float32)
    every(prepare)
    gather.collect(0)
    every(main)

    for step in range(MODULES):
        m = MODULES - 1 - step
        kernel_pair(m).wait()
        mine = refs.wq[m, pl.ds(pl.multiple_of(low * core, 8), span)]
        refs.work[pl.ds(m, span, stride=MODULES)] = mine + refs.wr[m]
    skip = pl.multiple_of(core * (MODULES * (share - low)), 8)
    leave = pltpu.make_async_copy(
        refs.work.at[pl.ds(skip, MODULES * share)], refs.wg, refs.osem.at[0]
    )
    leave.start()
    outputs_pair.wait()
    gradient_pair.wait()
    table_pair.wait()
    own = refs.kinds[shard] != core
    refs.out[...] = jnp.where(own, refs.blocks[0].astype(jnp.float32), refs.blockr[...].astype(jnp.float32)).astype(jnp.bfloat16)
    refs.grad[...] = jnp.where(own, refs.slopes[0], refs.sloper[...])
    width = 256 // count
    for which, goal in ((0, refs.gain), (1, refs.shift)):
        for m in range(MODULES):
            total = refs.gg[m, which] + refs.ggr[m, which]
            found = None
            for at in range(count):
                piece = jnp.where(shard == at, total[:, at * width : (at + 1) * width], 0.0)
                found = piece if found is None else found + piece
            goal[m] = found
    gather.finish(0)
    gather.finish(1)
    leave.wait()


def whole_call(rows, large, small, x, cot, w, gains, shifts, kinds):
    count = large + small
    weight_rows = w.shape[0] // MODULES
    table = scratch_table(rows, weight_rows, count)
    vmem = pl.BlockSpec(memory_space=pltpu.VMEM)
    hbm = pl.BlockSpec(memory_space=pl.ANY)
    smem = pl.BlockSpec(memory_space=pltpu.SMEM)
    tables = jax.ShapeDtypeStruct((MODULES, SLOTS, 256 // count), jnp.float32)
    return pl.pallas_call(
        partial(whole_kernel, NAMES + list(table), rows, large, small),
        out_shape=(
            jax.ShapeDtypeStruct((ROWS, LANES), jnp.bfloat16),
            jax.ShapeDtypeStruct((ROWS, LANES), jnp.float32),
            jax.ShapeDtypeStruct((MODULES * weight_rows // count, LANES), jnp.float32),
            tables,
            tables,
        ),
        in_specs=[vmem, vmem, hbm, vmem, vmem, smem],
        out_specs=(vmem, vmem, hbm, vmem, vmem),
        scratch_shapes=list(table.values()),
        compiler_params=pltpu.CompilerParams(
            collective_id=0, has_side_effects=True, vmem_limit_bytes=62 * 1024 * 1024
        ),
    )(x, cot, w, gains, shifts, kinds)


def leave_kernel(*args):
    sources, goals, rooms, arrive, depart = args[:5], args[5:10], args[10:15], args[15], args[16]
    pieces = []
    for source, goal, room in zip(sources, goals, rooms):
        high = source.shape[0]
        parts = 3 if high % 24 == 0 else 1
        for part in range(parts):
            rows = pl.ds(part * (high // parts), high // parts)
            at = len(pieces)
            pieces.append(
                (
                    pltpu.make_async_copy(source.at[rows], room.at[rows], arrive.at[at]),
                    pltpu.make_async_copy(room.at[rows], goal.at[rows], depart.at[at]),
                )
            )
    for come, _ in pieces:
        come.start()
    for come, go in pieces:
        come.wait()
        go.start()
    for _, go in pieces:
        go.wait()


def leave_call(arrays):
    hbm = pl.BlockSpec(memory_space=pl.ANY)
    return pl.pallas_call(
        leave_kernel,
        out_shape=tuple(jax.ShapeDtypeStruct(array.shape, array.dtype) for array in arrays),
        in_specs=[hbm] * 5,
        out_specs=(hbm,) * 5,
        scratch_shapes=[pltpu.VMEM(array.shape, array.dtype) for array in arrays]
        + [pltpu.SemaphoreType.DMA((16,)), pltpu.SemaphoreType.DMA((16,))],
    )(*arrays)


def on_device_grouped(features, weights, gains, shifts, cotangent, size_group):
    count = lax.axis_size("crops")
    large = count // 4
    weight_rows = weights.shape[2] // LANES
    results = whole_call(
        group_rows(count),
        large,
        count - large,
        features[0],
        cotangent[0],
        weights[0]
        .reshape(MODULES, weight_rows, LANES)
        .transpose(1, 0, 2)
        .reshape(MODULES * weight_rows, LANES),
        gains[0],
        shifts[0],
        size_group,
    )
    out, grad, weight_grad, gain, shift = leave_call(results)
    share = weight_rows // count
    weight_grad = weight_grad.reshape(share, MODULES, LANES).transpose(1, 0, 2)
    weight_grad = with_layout_constraint(weight_grad, Layout((1, 0, 2)))
    return (
        out[None],
        grad[None],
        weight_grad.reshape(1, MODULES, share * LANES),
        gain[None],
        shift[None],
    )


def group_rows(count):
    large = count // 4
    rows = max(large * (LH // 8) * (LW // 8), (count - large) * (SH // 8) * (SW // 8))
    return -(-rows // 16) * 16


def fits(count):
    return count % 8 == 0 and group_rows(count) <= 96


def solution(mesh):
    placed = (
        P("branch", "crops", None),
        P("branch", None, None),
        P("branch", None, None, None),
        P("branch", None, None, None),
        P("branch", "crops", None),
        P(),
    )
    return jax.shard_map(
        on_device_grouped if fits(mesh.shape["crops"]) else on_device,
        mesh=mesh,
        in_specs=placed,
        out_specs=(
            P("branch", "crops", None),
            P("branch", "crops", None),
            P("branch", None, "crops"),
            P("branch", None, None, "crops"),
            P("branch", None, None, "crops"),
        ),
        check_vma=False,
    )
```

```python
from functools import partial
from types import SimpleNamespace
import math

import jax
import jax.numpy as jnp
import numpy as np
from jax import lax
from jax.experimental import pallas as pl
from jax.experimental.layout import Layout, with_layout_constraint
from jax.experimental.pallas import tpu as pltpu
from jax.sharding import PartitionSpec as P

C0 = 32
BLOCKS = 1
MODULES = 2
CROPS_DEV = 1
SH = 32
SW = 24
LH = 64
LW = 48
ROWS = 768
MSG_ROWS = 384


EPS = 1e-05


def as_sent(x):

    def short(part):
        return part.astype(jnp.bfloat16) if part.dtype == jnp.float32 else part

    return jax.tree.map(short, x)


def sender_plan(branch_index, top_channels, blocks):
    channels = top_channels << branch_index
    operations = []
    for block_index in range(blocks):
        operations.append(
            SimpleNamespace(
                phase=2 * block_index,
                source=("h", block_index),
                level=branch_index,
                cin=channels,
                cout=channels,
                stride=1,
                taps=3,
                act="silu",
                output=("u", block_index),
                skip=None,
                dest=-1,
            )
        )
        operations.append(
            SimpleNamespace(
                phase=2 * block_index + 1,
                source=("u", block_index),
                level=branch_index,
                cin=channels,
                cout=channels,
                stride=1,
                taps=3,
                act="res",
                output=("h", block_index + 1),
                skip=("h", block_index),
                dest=-1,
            )
        )
    top_name = ("h", blocks)
    for target in range(branch_index):
        operations.append(
            SimpleNamespace(
                phase=2 * blocks,
                source=top_name,
                level=branch_index,
                cin=channels,
                cout=top_channels << target,
                stride=1,
                taps=1,
                act="none",
                output=None,
                skip=None,
                dest=target,
            )
        )
    for target in range(branch_index + 1, 4):
        for depth_step in range(1, target - branch_index + 1):
            is_last = depth_step == target - branch_index
            operations.append(
                SimpleNamespace(
                    phase=2 * blocks + depth_step - 1,
                    source=top_name if depth_step == 1 else ("chain", target, depth_step - 1),
                    level=branch_index + depth_step,
                    cin=channels,
                    cout=top_channels << target if is_last else channels,
                    stride=2,
                    taps=3,
                    act="none" if is_last else "silu",
                    output=None if is_last else ("chain", target, depth_step),
                    skip=None,
                    dest=target if is_last else -1,
                )
            )
    for position, operation in enumerate(operations):
        operation.slot = position
        operation.size = (
            operation.taps * operation.taps * operation.cin * operation.cout
        )
        if operation.taps == 1:
            operation.kshape = (operation.cin, operation.cout)
        else:
            operation.kshape = (3, 3, operation.cin, operation.cout)
    return operations


def phase_lengths(top_channels, blocks):
    phase_count = 2 * blocks + 3
    lengths = [0] * phase_count
    for branch_index in range(4):
        per_phase = [0] * phase_count
        for operation in sender_plan(branch_index, top_channels, blocks):
            per_phase[operation.phase] += operation.size
        lengths = [max(current, candidate) for current, candidate in zip(lengths, per_phase)]
    return lengths


def weighted_plan(branch_index, top_channels, blocks):
    lengths = phase_lengths(top_channels, blocks)
    starts = [sum(lengths[:phase_index]) for phase_index in range(len(lengths))]
    running = [0] * len(lengths)
    operations = sender_plan(branch_index, top_channels, blocks)
    for operation in operations:
        phase_index = operation.phase
        operation.inner = running[phase_index]
        operation.offset = starts[phase_index] + running[phase_index]
        operation.position = sum(
            (1 for earlier in operations[: operation.slot] if earlier.phase == phase_index)
        )
        running[phase_index] += operation.size
    return operations


def phase_operations(branch_index, phase_index):
    return [
        operation
        for operation in weighted_plan(branch_index, C0, BLOCKS)
        if operation.phase == phase_index
    ]


def input_names(operations):
    source_names = []
    for operation in operations:
        if operation.source not in source_names:
            source_names.append(operation.source)
    return source_names


def silu_slope(value):
    sigmoid = jax.nn.sigmoid(value)
    return sigmoid * (1.0 + value * (1.0 - sigmoid))


def crop_cells(size_kind):
    return (LH, LW) if size_kind else (SH, SW)


def map_dims(size_kind, level, channels):
    height, breadth = crop_cells(size_kind)
    return (CROPS_DEV, height >> level, breadth >> level, channels)


def source_dims(branch_index, size_kind, map_name):
    level = branch_index + map_name[2] if map_name[0] == "chain" else branch_index
    return map_dims(size_kind, level, C0 << branch_index)


def preact_dims(size_kind, operation):
    return map_dims(size_kind, operation.level, operation.cout)


def to_canvas(arrays, value_type):
    if not arrays:
        return jnp.zeros((ROWS, 128), value_type)
    flattened = jnp.concatenate([array.reshape(-1).astype(value_type) for array in arrays])
    return jnp.pad(flattened, (0, ROWS * 128 - flattened.shape[0])).reshape(ROWS, 128)


def from_canvas(canvas, dims_list):
    flattened = canvas.reshape(-1)
    pieces = []
    offset = 0
    for dims_entry in dims_list:
        count_here = math.prod(dims_entry)
        pieces.append(flattened[offset : offset + count_here].reshape(dims_entry))
        offset += count_here
    return pieces


def to_slot(array):
    flattened = array.reshape(-1)
    return jnp.pad(flattened, (0, MSG_ROWS * 128 - flattened.shape[0])).reshape(MSG_ROWS, 128)


def from_slot(slot_rows, dims_entry):
    return slot_rows.reshape(-1)[: math.prod(dims_entry)].reshape(dims_entry)


def upsample(message, factor):
    crop_count, height, breadth, channels = message.shape
    widened = jnp.broadcast_to(
        message[:, :, None, :, None, :], (crop_count, height, factor, breadth, factor, channels)
    )
    return widened.reshape(crop_count, height * factor, breadth * factor, channels)


def block_pool(array, factor):
    crop_count, height, breadth, channels = array.shape
    return array.reshape(
        crop_count, height // factor, factor, breadth // factor, factor, channels
    ).sum(axis=(2, 4))


def kernel_piece(module_weights, operation):
    start = operation.offset
    return module_weights[start : start + operation.size].reshape(operation.kshape)


def conv_forward(operation, source, kernel):
    if operation.taps == 1:
        return jnp.einsum("nhwc,cd->nhwd", source, kernel, preferred_element_type=jnp.float32)
    stride = operation.stride
    return lax.conv_general_dilated(
        source,
        kernel,
        (stride, stride),
        ((1, 1), (1, 1)),
        dimension_numbers=("NHWC", "HWIO", "NHWC"),
        preferred_element_type=jnp.float32,
    )


def conv_backward(operation, source, kernel, upstream):
    if operation.taps == 1:
        source_grad = jnp.einsum(
            "nhwd,cd->nhwc", upstream, kernel, preferred_element_type=jnp.float32
        )
        kernel_grad = jnp.einsum(
            "nhwc,nhwd->cd", source, upstream, preferred_element_type=jnp.float32
        )
        return (source_grad, kernel_grad)
    stride = operation.stride
    flipped = jnp.transpose(kernel[::-1, ::-1], (0, 1, 3, 2))
    high_pad = 2 if stride == 2 else 1
    source_grad = lax.conv_general_dilated(
        upstream,
        flipped,
        (1, 1),
        ((1, high_pad), (1, high_pad)),
        lhs_dilation=(stride, stride),
        dimension_numbers=("NHWC", "HWIO", "NHWC"),
        preferred_element_type=jnp.float32,
    )
    kernel_grad = lax.conv_general_dilated(
        source,
        upstream,
        (1, 1),
        ((1, 2 - stride), (1, 2 - stride)),
        rhs_dilation=(stride, stride),
        dimension_numbers=("CHWN", "IHWO", "NHWC"),
        preferred_element_type=jnp.float32,
    )
    return (source_grad, jnp.transpose(kernel_grad, (1, 2, 0, 3)))


def cell_total(counts, size_kind, level):
    height, breadth = crop_cells(size_kind)
    return counts[size_kind] * float(CROPS_DEV * (height >> level) * (breadth >> level))


def norm_terms(totals, counts, size_kind, operation):
    cells_here = cell_total(counts, size_kind, operation.level)
    channels = operation.cout
    position = operation.position
    average = totals[size_kind, 0, position, :channels] / cells_here
    variance = totals[size_kind, 1, position, :channels] / cells_here - average * average
    return (average, lax.rsqrt(variance + EPS))


def forward_conv(branch_index, size_kind, phase_index, source_canvas, module_weights):
    operations = phase_operations(branch_index, phase_index)
    source_names = input_names(operations)
    pieces = from_canvas(
        source_canvas, [source_dims(branch_index, size_kind, map_name) for map_name in source_names]
    )
    sources = {
        map_name: piece.astype(jnp.bfloat16) for map_name, piece in zip(source_names, pieces)
    }
    preacts = []
    totals = jnp.zeros((2, 2, 3, 8 * C0), jnp.float32)
    for operation in operations:
        preact = conv_forward(
            operation, sources[operation.source], kernel_piece(module_weights, operation)
        )
        preacts.append(preact)
        channels = operation.cout
        position = operation.position
        totals = totals.at[size_kind, 0, position, :channels].set(jnp.sum(preact, axis=(0, 1, 2)))
        totals = totals.at[size_kind, 1, position, :channels].set(
            jnp.sum(preact * preact, axis=(0, 1, 2))
        )
    return (to_canvas(preacts, jnp.float32), totals)


def forward_norm(
    branch_index,
    size_kind,
    phase_index,
    preact_canvas,
    totals,
    counts,
    module_gains,
    module_shifts,
    skip_canvas,
    message_buffer,
):
    operations = phase_operations(branch_index, phase_index)
    preacts = from_canvas(
        preact_canvas, [preact_dims(size_kind, operation) for operation in operations]
    )
    skip_map = from_canvas(skip_canvas, [map_dims(size_kind, branch_index, C0 << branch_index)])[0]
    produced = []
    for operation, preact in zip(operations, preacts):
        average, inverse_std = norm_terms(totals, counts, size_kind, operation)
        norm_slot = operation.slot
        channels = operation.cout
        normed = (preact - average) * inverse_std * module_gains[
            norm_slot, :channels
        ] + module_shifts[norm_slot, :channels]
        if operation.act == "silu":
            produced.append(jax.nn.silu(normed))
        elif operation.act == "res":
            produced.append(jax.nn.silu(normed + skip_map))
        else:
            message_buffer = message_buffer.at[operation.dest].set(
                to_slot(normed.astype(jnp.bfloat16))
            )
    return (to_canvas(produced, jnp.float32), message_buffer)


def receive_forward(branch_index, size_kind, top_canvas, received):
    channels = C0 << branch_index
    summed = from_canvas(top_canvas, [map_dims(size_kind, branch_index, channels)])[0]
    for sender in range(4):
        if sender < branch_index:
            summed = summed + from_slot(
                received[sender], map_dims(size_kind, branch_index, channels)
            ).astype(jnp.float32)
        elif sender > branch_index:
            coarse = from_slot(received[sender], map_dims(size_kind, sender, channels))
            summed = summed + upsample(coarse, 2 ** (sender - branch_index)).astype(jnp.float32)
    return (to_canvas([jax.nn.silu(summed)], jnp.float32), to_canvas([summed], jnp.float32))


def receive_backward(branch_index, size_kind, grad_canvas, summed_canvas):
    dims_here = map_dims(size_kind, branch_index, C0 << branch_index)
    upstream = from_canvas(grad_canvas, [dims_here])[0]
    summed = from_canvas(summed_canvas, [dims_here])[0]
    summed_grad = upstream * silu_slope(summed)
    buffer = jnp.zeros((4, MSG_ROWS, 128), jnp.bfloat16)
    for sender in range(4):
        if sender < branch_index:
            buffer = buffer.at[sender].set(to_slot(summed_grad.astype(jnp.bfloat16)))
        elif sender > branch_index:
            pooled = block_pool(summed_grad, 2 ** (sender - branch_index))
            buffer = buffer.at[sender].set(to_slot(pooled.astype(jnp.bfloat16)))
    return (to_canvas([summed_grad], jnp.float32), buffer)


def backward_stats(
    branch_index,
    size_kind,
    phase_index,
    dout_canvas,
    message_grads,
    preact_canvas,
    totals,
    counts,
    module_gains,
    module_shifts,
    skip_canvas,
):
    operations = phase_operations(branch_index, phase_index)
    preacts = from_canvas(
        preact_canvas, [preact_dims(size_kind, operation) for operation in operations]
    )
    producing = [operation for operation in operations if operation.act != "none"]
    output_grads = from_canvas(
        dout_canvas, [preact_dims(size_kind, operation) for operation in producing]
    )
    grads_by_name = {
        operation.output: piece for operation, piece in zip(producing, output_grads)
    }
    skip_map = from_canvas(skip_canvas, [map_dims(size_kind, branch_index, C0 << branch_index)])[0]
    upstreams = []
    skip_grads = []
    sums_local = jnp.zeros((2, 2, 3, 8 * C0), jnp.float32)
    for operation, preact in zip(operations, preacts):
        average, inverse_std = norm_terms(totals, counts, size_kind, operation)
        norm_slot = operation.slot
        channels = operation.cout
        centered = (preact - average) * inverse_std
        normed = centered * module_gains[norm_slot, :channels] + module_shifts[norm_slot, :channels]
        if operation.act == "silu":
            upstream = grads_by_name[operation.output] * silu_slope(normed)
        elif operation.act == "res":
            upstream = grads_by_name[operation.output] * silu_slope(normed + skip_map)
            skip_grads.append(upstream)
        else:
            upstream = from_slot(
                message_grads[operation.dest], preact_dims(size_kind, operation)
            ).astype(jnp.float32)
        upstreams.append(upstream)
        position = operation.position
        sums_local = sums_local.at[size_kind, 0, position, :channels].set(
            jnp.sum(upstream, axis=(0, 1, 2))
        )
        sums_local = sums_local.at[size_kind, 1, position, :channels].set(
            jnp.sum(upstream * centered, axis=(0, 1, 2))
        )
    return (to_canvas(upstreams, jnp.float32), sums_local, to_canvas(skip_grads, jnp.float32))


def backward_apply(
    branch_index,
    size_kind,
    phase_index,
    upstream_canvas,
    preact_canvas,
    totals,
    grad_totals,
    counts,
    source_canvas,
    module_weights,
    module_gains,
):
    operations = phase_operations(branch_index, phase_index)
    preacts = from_canvas(
        preact_canvas, [preact_dims(size_kind, operation) for operation in operations]
    )
    upstreams = from_canvas(
        upstream_canvas, [preact_dims(size_kind, operation) for operation in operations]
    )
    source_names = input_names(operations)
    source_list = [source_dims(branch_index, size_kind, map_name) for map_name in source_names]
    pieces = from_canvas(source_canvas, source_list)
    sources = {
        map_name: piece.astype(jnp.bfloat16) for map_name, piece in zip(source_names, pieces)
    }
    source_grads = {
        map_name: jnp.zeros(dims_entry, jnp.float32)
        for map_name, dims_entry in zip(source_names, source_list)
    }
    kernel_grads = []
    slot_count = module_gains.shape[0]
    gain_part = jnp.zeros((slot_count, 8 * C0), jnp.float32)
    shift_part = jnp.zeros((slot_count, 8 * C0), jnp.float32)
    for operation, preact, upstream in zip(operations, preacts, upstreams):
        average, inverse_std = norm_terms(totals, counts, size_kind, operation)
        cells_here = cell_total(counts, size_kind, operation.level)
        norm_slot = operation.slot
        channels = operation.cout
        position = operation.position
        centered = (preact - average) * inverse_std
        mean_upstream = grad_totals[size_kind, 0, position, :channels] / cells_here
        mean_cross = grad_totals[size_kind, 1, position, :channels] / cells_here
        preact_grad = (
            module_gains[norm_slot, :channels]
            * inverse_std
            * (upstream - mean_upstream - centered * mean_cross)
        )
        source_grad, kernel_grad = conv_backward(
            operation,
            sources[operation.source],
            kernel_piece(module_weights, operation),
            preact_grad.astype(jnp.bfloat16),
        )
        source_grads[operation.source] = source_grads[operation.source] + source_grad
        kernel_grads.append(kernel_grad.reshape(-1))
        gain_part = gain_part.at[norm_slot, :channels].set(
            grad_totals[0, 1, position, :channels] + grad_totals[1, 1, position, :channels]
        )
        shift_part = shift_part.at[norm_slot, :channels].set(
            grad_totals[0, 0, position, :channels] + grad_totals[1, 0, position, :channels]
        )
    phase_length = phase_lengths(C0, BLOCKS)[phase_index]
    if kernel_grads:
        joined = jnp.concatenate(kernel_grads)
        weight_part = jnp.pad(joined, (0, phase_length - joined.shape[0]))
    else:
        weight_part = jnp.zeros((phase_length,), jnp.float32)
    return (
        to_canvas([source_grads[map_name] for map_name in source_names], jnp.float32),
        weight_part,
        gain_part,
        shift_part,
    )


def on_device(features, weights, gains, shifts, cotangent, size_group):
    crop_shard = lax.axis_index("crops")
    shard_count = lax.axis_size("crops")
    crop_kind = size_group[crop_shard]
    large_count = jnp.sum(size_group).astype(jnp.float32)
    counts = jnp.stack([shard_count - large_count, large_count])
    case_index = lax.axis_index("branch") * 2 + crop_kind
    phase_total = 2 * BLOCKS + 3
    zero_canvas = jnp.zeros((ROWS, 128), jnp.float32)
    empty_buffer = jnp.zeros((4, MSG_ROWS, 128), jnp.bfloat16)

    def run_phase(function, statics, operands):
        branches_list = [
            partial(function, branch_index, size_kind, *statics)
            for branch_index in range(4)
            for size_kind in range(2)
        ]
        return lax.switch(case_index, branches_list, *operands)

    def statistics(local_totals):
        return lax.psum(local_totals, "crops")

    def module_forward(module, start_canvas, kept):
        module_weights = weights[0, module]
        module_gains = gains[0, module]
        module_shifts = shifts[0, module]
        record = SimpleNamespace(sources=[], preacts=[], totals=[])
        h_canvas = start_canvas
        u_canvas = zero_canvas
        chain_canvas = zero_canvas
        buffer = empty_buffer
        for phase_index in range(phase_total):
            if phase_index < 2 * BLOCKS:
                source = h_canvas if phase_index % 2 == 0 else u_canvas
            elif phase_index == 2 * BLOCKS:
                source = h_canvas
            else:
                source = chain_canvas
            preact, local_totals = run_phase(forward_conv, (phase_index,), (source, module_weights))
            global_totals = kept.totals[phase_index] if kept else statistics(local_totals)
            produced, buffer = run_phase(
                forward_norm,
                (phase_index,),
                (preact, global_totals, counts, module_gains, module_shifts, h_canvas, buffer),
            )
            record.sources.append(source)
            record.preacts.append(preact)
            record.totals.append(global_totals)
            if phase_index < 2 * BLOCKS:
                if phase_index % 2 == 0:
                    u_canvas = produced
                else:
                    h_canvas = produced
            else:
                chain_canvas = produced
        received = (
            kept.received
            if kept
            else jax.tree.map(
                lambda part, own: part.astype(own.dtype),
                lax.all_to_all(as_sent(buffer), "branch", split_axis=0, concat_axis=0, tiled=True),
                buffer,
            )
        )
        result, summed = run_phase(receive_forward, (), (h_canvas, received))
        record.summed = summed
        record.received = received
        return (result, record)

    checkpoints = [features[0].astype(jnp.float32)]
    first_records = []
    for module in range(MODULES):
        result, record = module_forward(module, checkpoints[-1], None)
        checkpoints.append(result)
        first_records.append(record)
    outputs = checkpoints[-1].astype(jnp.bfloat16)
    grad_canvas = cotangent[0].astype(jnp.float32)
    module_grads = [None] * MODULES
    gain_grads = [None] * MODULES
    shift_grads = [None] * MODULES
    for module in reversed(range(MODULES)):
        kept = None
        unused_result, record = module_forward(module, checkpoints[module], kept)
        module_module_weights = weights[0, module]
        module_module_gains = gains[0, module]
        module_module_shifts = shifts[0, module]
        summed_grad, back_buffer = run_phase(receive_backward, (), (grad_canvas, record.summed))
        message_grads = jax.tree.map(
            lambda part, own: part.astype(own.dtype),
            lax.all_to_all(as_sent(back_buffer), "branch", split_axis=0, concat_axis=0, tiled=True),
            back_buffer,
        )
        top_grad = summed_grad
        chain_grad = zero_canvas
        u_grad = zero_canvas
        pending_skip = zero_canvas
        weight_parts = [None] * phase_total
        gain_total = jnp.zeros(gains.shape[2:], jnp.float32)
        shift_total = jnp.zeros(gains.shape[2:], jnp.float32)
        for module_phase_index in reversed(range(phase_total)):
            if module_phase_index >= 2 * BLOCKS:
                output_grad = chain_grad
                skip_canvas = zero_canvas
            elif module_phase_index % 2 == 1:
                output_grad = top_grad
                skip_canvas = record.sources[module_phase_index - 1]
            else:
                output_grad = u_grad
                skip_canvas = zero_canvas
            module_preact = record.preacts[module_phase_index]
            totals = record.totals[module_phase_index]
            upstream, module_local_totals, skip_grad = run_phase(
                backward_stats,
                (module_phase_index,),
                (
                    output_grad,
                    message_grads,
                    module_preact,
                    totals,
                    counts,
                    module_module_gains,
                    module_module_shifts,
                    skip_canvas,
                ),
            )
            grad_totals = lax.psum(module_local_totals, "crops")
            source_grad, weight_parts[module_phase_index], gain_part, shift_part = run_phase(
                backward_apply,
                (module_phase_index,),
                (
                    upstream,
                    module_preact,
                    totals,
                    grad_totals,
                    counts,
                    record.sources[module_phase_index],
                    module_module_weights,
                    module_module_gains,
                ),
            )
            gain_total = gain_total + gain_part
            shift_total = shift_total + shift_part
            if module_phase_index > 2 * BLOCKS:
                chain_grad = source_grad
            elif module_phase_index == 2 * BLOCKS:
                top_grad = top_grad + source_grad
            elif module_phase_index % 2 == 1:
                u_grad = source_grad
                pending_skip = skip_grad
            else:
                top_grad = source_grad + pending_skip
        joined = jnp.concatenate(weight_parts)
        weight_grad = jnp.pad(joined, (0, weights.shape[2] - joined.shape[0]))
        grad_canvas, weight_grad, gain_grads[module], shift_grads[module] = (
            top_grad,
            weight_grad,
            gain_total,
            shift_total,
        )
        module_grads[module] = weight_grad
    weight_out = lax.psum_scatter(jnp.stack(module_grads), "crops", scatter_dimension=1, tiled=True)
    share = gains.shape[3] // shard_count
    gain_out = lax.dynamic_slice_in_dim(jnp.stack(gain_grads), crop_shard * share, share, axis=2)
    shift_out = lax.dynamic_slice_in_dim(jnp.stack(shift_grads), crop_shard * share, share, axis=2)
    return (outputs[None], grad_canvas[None], weight_out[None], gain_out[None], shift_out[None])


LANES = 128
SLOTS = 8
MASKS = 7
DOWN = (((1,), (0,)), ((), ()))
ACROSS = (((1,), (1,)), ((), ()))
ALONG = (((0,), (0,)), ((), ()))


def unit_table(k):
    operations = weighted_plan(k, C0, BLOCKS)
    planes = 8 >> k
    channels = C0 << k
    units = {}
    stat = 0

    def add(name, kind, source, lanes_in, planes_in, planes_out, members):
        nonlocal stat
        segs = []
        tile = 0
        for operation, lanes, chain in members:
            cout = operation.cout
            level = operation.level if operation.taps == 3 else operation.dest
            segs.append(
                SimpleNamespace(
                    slot=operation.slot,
                    off=operation.offset // LANES,
                    cin=operation.cin,
                    cout=cout,
                    taps=operation.taps,
                    tile=tile,
                    tiles=lanes // LANES,
                    blocks=max(1, (8 >> level)),
                    dest=operation.dest,
                    act=operation.act,
                    chain=chain,
                    up=k - operation.dest if operation.taps == 1 else 0,
                )
            )
            tile += lanes // LANES
        rows = {"s1": (384, 384, 512, 768)[k], "s2": lanes_in + LANES, "p1": 256}[kind]
        units[name] = SimpleNamespace(
            name=name,
            kind=kind,
            source=source,
            lanes_in=lanes_in,
            blocks_in=planes_in,
            planes_in=planes_in,
            planes=planes_out,
            segs=segs,
            tiles=tile,
            rows=rows,
            stat=stat,
            depth=1 if kind == "p1" else 3,
        )
        stat += tile

    add("a", "s1", "h", 256, planes, planes, [(operations[0], 256, None)])
    add("b", "s1", "u", 256, planes, planes, [(operations[1], 256, None)])
    ups = [operation for operation in operations if operation.taps == 1]
    if ups:
        add("u", "p1", "t", 256, planes, planes, [(operation, 256, None) for operation in ups])
    firsts, chains = [], {}
    for target in range(k + 1, 4):
        steps = [
            operation
            for operation in operations
            if operation.taps == 3 and operation.stride == 2
        ]
        start = sum(i - k for i in range(k + 1, target))
        chains[target] = steps[start : start + target - k]
        if target == k + 1:
            firsts.append((chains[target][0], 256, None))
        else:
            firsts.append((chains[target][0], LANES, "c1" if target == k + 2 else "c2"))
    if firsts:
        add("d", "s2", "t", 256, planes, planes // 2, firsts)
    if k <= 1:
        add("e", "s2", "c1", LANES, planes // 2, planes // 4, [(chains[k + 2][1], 256, None)])
    if k == 0:
        add("f", "s2", "c2", LANES, planes // 2, planes // 4, [(chains[3][1], LANES, "c3")])
        add("g", "s2", "c3", LANES, planes // 4, planes // 8, [(chains[3][2], 256, None)])
    return units


def links(k, unit, seg):
    cin = seg.cin
    count_in, count_out = unit.blocks_in, seg.blocks
    found = []
    if unit.kind == "p1":
        for plane in range(count_in):
            wide = 1 << seg.up
            found.append((plane * cin, 0, set(range(plane * wide, plane * wide + wide))))
        return found
    if unit.kind == "s1" and k == 3:
        return [(256 * tap, tap, {0}) for tap in range(3)]
    stride = 1 if unit.kind == "s1" else 2
    for plane in range(count_in):
        for tap in range(3):
            at = plane - tap + 1
            if at % stride == 0 and 0 <= at // stride < count_out:
                found.append((plane * cin, tap, {at // stride}))
    if stride == 1:
        found.append((256, 2, {count_out - 1}))
        found.append((unit.rows - cin, 0, {0}))
    else:
        lanes_in = unit.lanes_in
        found.append((lanes_in + (count_in - 1) * cin - (lanes_in - LANES), 0, {0}))
    return found


def message_slot(k, other):
    return sum(2 * (8 >> max(k, before)) for before in range(other) if before != k)


def log2(value):
    return value.bit_length() - 1


def sigmoid_of(value):
    return 0.5 * jnp.tanh(0.5 * value) + 0.5


def silu_of(value):
    return value * sigmoid_of(value)


def slope_of(value):
    sigmoid = sigmoid_of(value)
    return sigmoid * (1.0 + value * (1.0 - sigmoid))


def planes_loop(count, body, turns=1):
    def step(index, carry):
        for turn in range(turns):
            body(index * turns + turn)
        return carry

    turns = min(turns, count)
    if count == turns:
        for index in range(count):
            body(index)
    else:
        lax.fori_loop(0, count // turns, step, 0)


def planes_sum(count, body, initial, turns=1):
    def step(index, carry):
        for turn in range(turns):
            carry = body(index * turns + turn, carry)
        return carry

    turns = min(turns, count)
    if count == turns:
        return step(0, initial)
    return lax.fori_loop(0, count // turns, step, initial)


def partial_sum(value):
    rows = value.shape[0]
    return jnp.sum(value.reshape(rows // 8, 8, value.shape[1]), axis=0)


class Planes:
    def __init__(self, mode, tiles, planes, masks, rows, main, edge=None, right=None, narrow=False):
        self.narrow, self.pending = narrow, {}
        self.mode, self.tiles, self.planes = mode, tiles, planes
        self.masks, self.rows = masks, rows
        self.main, self.edge, self.right = main, edge, right
        self.base = 1 if mode in ("s1", "wide", "s2") else 0
        extra = {"s1": 2, "wide": 2, "s2": 1, "dz2": 1, "p": 0}[mode]
        self.span = planes + extra
        self.unit = tiles * self.span

    def at(self, m, tile, plane):
        return m * self.unit + tile * self.span + plane + self.base

    def edge_at(self, m, tile, plane):
        if self.mode == "s2" or self.narrow:
            return m * self.span + plane + self.base
        return self.at(m, tile, plane)

    def from_left(self, value):
        return pltpu.roll(value, 1, 0) * self.masks[1]

    def from_right(self, value):
        return pltpu.roll(value, self.rows - 1, 0) * self.masks[2]

    def store(self, m, tile, plane, value):
        self.put(m, tile, plane, value)
        if isinstance(plane, int):
            if plane == self.planes - 1:
                self.put_above(m, tile, value)
            if plane == 0:
                self.put_below(m, tile, value)

    def put(self, m, tile, plane, value):
        where = self.at(m, tile, plane)
        self.main[where] = value.astype(jnp.bfloat16)
        if self.mode == "s1":
            side = self.from_right(value) if tile == 0 else self.from_left(value)
            if not self.narrow:
                self.edge[where] = side.astype(jnp.bfloat16)
            elif tile == 0:
                self.pending[plane if isinstance(plane, int) else self.span] = side
            else:
                lane = lax.broadcasted_iota(jnp.int32, side.shape, 1)
                other = self.pending.pop(plane if isinstance(plane, int) else self.span)
                side = jnp.where(lane < LANES // 2, other, side)
                self.edge[self.edge_at(m, tile, plane)] = side.astype(jnp.bfloat16)
        elif self.mode == "wide":
            self.edge[where] = self.from_left(value).astype(jnp.bfloat16)
            self.right[where] = self.from_right(value).astype(jnp.bfloat16)
        elif self.mode == "s2":
            if tile == self.tiles - 1:
                self.edge[self.edge_at(m, tile, plane)] = self.from_left(value).astype(jnp.bfloat16)
        elif self.mode == "dz2":
            self.edge[where] = self.from_right(value).astype(jnp.bfloat16)

    def put_above(self, m, tile, last):
        if self.mode in ("s1", "wide", "s2"):
            above = pltpu.roll(last, 6, 0) * self.masks[3] + pltpu.roll(last, 3, 0) * self.masks[4]
            self.put(m, tile, -1, above)

    def put_below(self, m, tile, first):
        if self.mode in ("s1", "wide", "dz2"):
            rows = self.rows
            below = (
                pltpu.roll(first, rows - 6, 0) * self.masks[5]
                + pltpu.roll(first, rows - 3, 0) * self.masks[6]
            )
            self.put(m, tile, self.planes, below)

    def close(self, m):
        for tile in range(self.tiles):
            last = self.main[self.at(m, tile, self.planes - 1)].astype(jnp.float32)
            self.put_above(m, tile, last)
        for tile in range(self.tiles):
            first = self.main[self.at(m, tile, 0)].astype(jnp.float32)
            self.put_below(m, tile, first)


class Branch:
    def __init__(self, k, rows, large, small, share, refs, masks, core):
        self.k, self.rows, self.refs, self.masks = k, rows, refs, masks
        self.units = unit_table(k)
        self.planes = 8 >> k
        self.core = core
        self.large, self.small, self.count = large, small, large + small
        self.cells = (small * (SH // 8) * (SW // 8), large * (LH // 8) * (LW // 8))
        self.quarter = lax.axis_index("crops") // 2
        self.share = share
        r = refs
        make = partial(Planes, masks=masks, rows=rows)
        make_one = partial(make, narrow=k <= 1)
        one = "wide" if k == 3 else "s1"
        self.maps = dict(
            h=make_one(one, 2, self.planes, main=r.hC, edge=r.hE, right=r.hR),
            u=make_one(one, 2, self.planes, main=r.uC, edge=r.uE, right=r.uR),
            t=make("p" if k == 3 else "s2", 2, self.planes, main=r.tC, edge=r.tE),
        )
        if k <= 1:
            self.maps["c1"] = make("s2", 1, self.planes // 2, main=r.c1C, edge=r.c1E)
        if k == 0:
            self.maps["c2"] = make("s2", 1, 4, main=r.c2C, edge=r.c2E)
            self.maps["c3"] = make("s2", 1, 2, main=r.c3C, edge=r.c3E)
        self.grads = dict(t=r.gt, u=r.gu, c1=r.gc1, c2=r.gc2, c3=r.gc3)

    def lane_block(self, shape, cout):
        lanes = lax.broadcasted_iota(jnp.int32, shape, 1)
        return lanes >> log2(cout)

    def keep(self, value, cout, which):
        count = LANES // cout
        if len(which) == count:
            return value
        block = self.lane_block(value.shape, cout)
        mask = block == which[0]
        for entry in which[1:]:
            mask = mask | (block == entry)
        return jnp.where(mask, value, 0.0)

    def spread(self, value, cout):
        shift = LANES // 2
        while shift >= cout:
            value = value + pltpu.roll(value, shift, 1)
            shift //= 2
        return value

    def local_blocks(self, seg, tile, wanted):
        count = LANES // seg.cout
        return [q for q in range(count) if (tile * count + q) % seg.blocks in wanted]


    def segments(self):
        return [(unit, seg) for unit in self.units.values() for seg in unit.segs]

    def pieces(self):
        found, place = [], 0
        for index, (unit, seg) in enumerate(self.segments()):
            count = 2 * seg.taps**2 * seg.cin * seg.cout // LANES
            if self.k < 3:
                found.append((index, 0, count, place, index))
                place += count
            else:
                for d in range(unit.depth):
                    slot = len(found) % 3
                    found.append((index, d, count // unit.depth, slot * 3072, slot))
        return found

    def fetch(self, at):
        r = self.refs
        index, d, count, place, sem = self.pieces()[at]
        _, seg = self.segments()[index]
        return pltpu.make_async_copy(
            r.w.at[pl.ds(2 * seg.off + d * count, count)],
            r.raw.at[pl.ds(place, count)],
            r.wsem.at[sem],
        )

    def fetch_first(self):
        for at in range(len(self.pieces()) if self.k < 3 else 3):
            self.fetch(at).start()

    def expand(self, index):
        unit, seg = self.segments()[index]
        pieces = self.pieces()
        mine = [at for at, piece in enumerate(pieces) if piece[0] == index]
        if self.k < 3:
            (at,) = mine
            self.fetch(at).wait()
            count = pieces[at][2] // unit.depth
            planes_loop(
                unit.depth,
                lambda d: self.expand_row(unit, seg, d, count, pieces[at][3] + d * count),
            )
        else:
            for d, at in enumerate(mine):
                self.fetch(at).wait()
                self.expand_row(unit, seg, d, pieces[at][2], pieces[at][3])
                if at + 3 < len(pieces):
                    self.fetch(at + 3).start()
        for m in range(MODULES):
            self.spread_tables(m, unit, seg)

    def expand_row(self, unit, seg, d, count, place):
        r = self.refs
        chunk = math.gcd(count, 384)
        wf, rep = r.work, r.rep

        def widen(step):
            at = pl.multiple_of(step * chunk, 16)
            value = r.raw[pl.ds(pl.multiple_of(place + at, 16), chunk)].astype(jnp.float32)
            wf[pl.ds(at, chunk)] = value

        planes_loop(count // chunk, widen)
        count = count // MODULES
        depth, cin, cout = unit.depth, seg.cin, seg.cout
        target = getattr(r, "T" + unit.name)
        twice = unit.kind == "s1" and self.k < 3
        across = getattr(r, "T" + unit.name + unit.name) if twice else None
        by_row = {}
        for row, tap, wanted in links(self.k, unit, seg):
            by_row.setdefault(row, []).append((tap, wanted))

        def module(m):
            if cout < LANES:
                ratio = LANES // cout
                flat = wf[pl.ds(m, count, stride=2)]
                for part in range(ratio):
                    rep[pl.ds(part, count, stride=ratio)] = self.spread(
                        self.keep(flat, cout, [part]), cout
                    )

            def tap_rows(tap, tile):
                if cout < LANES:
                    return rep[tap * cin : (tap + 1) * cin]
                if cout == LANES:
                    return wf[pl.ds(m + tap * (2 * cin), cin, stride=2)]
                return wf[pl.ds(m + tap * (4 * cin) + 2 * tile, cin, stride=4)]

            def place(goal, taps_at, width, column, tile):
                made = {}
                for row in range(0, unit.rows, cin):
                    key = []
                    for tap, wanted in by_row.get(row, []):
                        local = self.local_blocks(seg, tile, wanted) if width <= LANES else [0]
                        if local:
                            key.append((tap, tuple(local)))
                    key = tuple(key)
                    if key not in made:
                        total = None
                        for tap, local in key:
                            piece = taps_at[tap]
                            if width <= LANES:
                                piece = self.keep(piece, width, local)
                            total = piece if total is None else total + piece
                        if total is None:
                            total = jnp.zeros((cin, LANES), jnp.float32)
                        made[key] = total.astype(jnp.bfloat16)
                    goal[m * depth + d, row : row + cin, column : column + LANES] = made[key]

            width = 3 if seg.taps == 3 else 1
            for tile in range(seg.tiles):
                if tile == 0 or cout > LANES:
                    taps_at = [tap_rows(tap, tile) for tap in range(width)]
                place(target, taps_at, cout, (seg.tile + tile) * LANES, tile)
            if not twice:
                return
            turned = []
            if cin == LANES:
                turned = [jnp.transpose(tap_rows(tap, 0)) for tap in range(3)]
            else:
                both = jnp.transpose(rep[0 : -(-3 * cin // LANES) * LANES])
                for tap in range(3):
                    first = tap * cin // LANES * LANES
                    value = both[0:cin, first : first + LANES]
                    value = self.keep(value, cin, [tap * cin % LANES // cin])
                    turned.append(self.spread(value, cin))
            for tile in range(2):
                place(across, turned[::-1], cin, tile * LANES, tile)

        planes_loop(MODULES, module)


    def parts(self, unit, source):
        if unit.kind == "p1":
            return [(source.main, range(2), source.at)]
        if source.mode == "wide":
            return [
                (source.edge, range(2), source.at),
                (source.main, range(2), source.at),
                (source.right, range(2), source.at),
            ]
        if unit.kind == "s1":
            tiles = [0] if source.narrow else range(2)
            return [(source.main, range(2), source.at), (source.edge, tiles, source.edge_at)]
        last = source.tiles - 1
        return [
            (source.main, range(source.tiles), source.at),
            (source.edge, [last], source.edge_at),
        ]

    def rows_of(self, unit, part, m, d, first, count):
        ref, tiles, at = part
        pieces = []
        for tile in tiles:
            if unit.kind == "s2":
                rows = [ref[at(m, tile, 2 * (first + q) + d - 1)] for q in range(count)]
                pieces.append(rows[0] if count == 1 else jnp.concatenate(rows, axis=0))
            else:
                shift = d - 1 if unit.kind == "s1" else 0
                pieces.append(
                    ref[pl.ds(at(m, tile, first + shift), count)].reshape(count * self.rows, LANES)
                )
        return pieces

    def conv(self, m, unit):
        r = self.refs
        source = self.maps[unit.source]
        target = getattr(r, "T" + unit.name)
        z = getattr(r, "z" + unit.name)
        planes, tiles, depth = unit.planes, unit.tiles, unit.depth
        chunk = min(planes, 4 if tiles <= 2 else 2)
        lanes = tiles * LANES

        def body(step, sums):
            first = step * chunk
            pieces = []
            for d in range(depth):
                for part in self.parts(unit, source):
                    pieces += self.rows_of(unit, part, m, d, first, chunk)
            left = jnp.concatenate(pieces, axis=1)
            right = target[pl.ds(m * depth, depth), 0 : unit.rows, 0:lanes]
            right = right.reshape(depth * unit.rows, lanes)
            result = lax.dot_general(left, right, DOWN, preferred_element_type=jnp.float32)
            for tile in range(tiles):
                block = result[:, tile * LANES : (tile + 1) * LANES]
                z[pl.ds(m * tiles * planes + tile * planes + first, chunk)] = block.reshape(
                    chunk, self.rows, LANES
                )
            return (sums[0] + partial_sum(result), sums[1] + partial_sum(result * result))

        zero = jnp.zeros((8, lanes), jnp.float32)
        sums = planes_sum(planes // chunk, body, (zero, zero), 2)
        for seg in unit.segs:
            scale = self.per_cell(unit, seg)
            totals = self.fold(seg, sums)
            self.norm_rows(m, unit, seg, totals, scale)

    def per_cell(self, unit, seg):
        blocks = seg.tiles * LANES // seg.cout
        small, large = self.cells
        count = unit.planes * blocks
        return jnp.where(self.core == 0, 1.0 / (large * count), 1.0 / (small * count)).astype(
            jnp.float32
        )

    def fold(self, seg, sums):
        first = seg.tile
        found = []
        for value in sums:
            tiles = [
                value[:, (first + t) * LANES : (first + t + 1) * LANES] for t in range(seg.tiles)
            ]
            if seg.cout <= LANES:
                total = tiles[0]
                for tile in tiles[1:]:
                    total = total + tile
                total = jnp.sum(self.spread(total, seg.cout), axis=0, keepdims=True)
                found.append([total] * seg.tiles)
            else:
                found.append([jnp.sum(tile, axis=0, keepdims=True) for tile in tiles])
        return found

    def table_row(self, ref, m, seg, tile):
        slot = seg.slot
        if seg.cout > LANES:
            return ref[m, slot : slot + 1, tile * LANES : (tile + 1) * LANES]
        row = jnp.broadcast_to(ref[m, slot : slot + 1, 0:LANES], (8, LANES))
        if seg.cout < LANES:
            row = self.spread(self.keep(row, seg.cout, [0]), seg.cout)
        return row[0:1]

    def norm_rows(self, m, unit, seg, totals, scale):
        st = self.refs.st
        for tile in range(seg.tiles):
            average = totals[0][tile] * scale
            variance = totals[1][tile] * scale - average * average
            inverse = lax.rsqrt(variance + EPS)
            where = m * STATS + unit.stat + seg.tile + tile
            factor = st[where, 4:5] * inverse
            st[where, 0:1] = average
            st[where, 1:2] = inverse
            st[where, 2:3] = factor
            st[where, 3:4] = st[where, 5:6] - average * factor

    def spread_tables(self, m, unit, seg):
        st = self.refs.st
        for tile in range(seg.tiles):
            where = m * STATS + unit.stat + seg.tile + tile
            st[where, 4:5] = self.table_row(self.refs.gains, m, seg, tile)
            st[where, 5:6] = self.table_row(self.refs.shifts, m, seg, tile)

    def normed(self, m, unit, tile, plane):
        st = self.refs.st
        z = getattr(self.refs, "z" + unit.name)
        where = m * STATS + unit.stat + tile
        value = z[m * unit.tiles * unit.planes + tile * unit.planes + plane]
        return value * st[where, 2:3] + st[where, 3:4]

    def apply_a(self, m):
        unit, u = self.units["a"], self.maps["u"]

        def body(plane):
            for tile in range(2):
                value = silu_of(self.normed(m, unit, tile, plane)) * self.masks[0]
                u.store(m, tile, plane, value)

        planes_loop(self.planes, body, TURNS)

    def apply_b(self, m):
        unit, top = self.units["b"], self.maps["t"]
        hf, s = self.refs.hf, self.refs.s

        def body(plane):
            for tile in range(2):
                where = m * 2 * self.planes + tile * self.planes + plane
                value = silu_of(self.normed(m, unit, tile, plane) + hf[where]) * self.masks[0]
                s[where] = value
                top.store(m, tile, plane, value)

        planes_loop(self.planes, body, TURNS)

    def apply_rest(self, m, unit):
        sb = self.refs.sb
        for seg in unit.segs:
            chain = self.maps[seg.chain] if seg.chain else None

            def body(plane):
                for tile in range(seg.tiles):
                    value = self.normed(m, unit, seg.tile + tile, plane)
                    if chain is not None:
                        chain.store(m, tile, plane, silu_of(value) * self.masks[0])
                    else:
                        at = message_slot(self.k, seg.dest) + tile * unit.planes + plane
                        sb[at] = value.astype(jnp.bfloat16)

            planes_loop(unit.planes, body, TURNS)
            if chain is None:
                self.message(m, seg.dest).start()

    def message(self, e, other):
        count = 2 * (8 >> max(self.k, other))
        r = self.refs
        return pltpu.make_async_remote_copy(
            src_ref=r.sb.at[pl.ds(message_slot(self.k, other), count)],
            dst_ref=r.rb.at[pl.ds(e * 16 + message_slot(other, self.k), count)],
            send_sem=r.ssem.at[e * 4 + other],
            recv_sem=r.rsem.at[e * 4 + self.k],
            device_id=dict(branch=other),
            device_id_type=pl.DeviceIdType.MESH,
        )

    def arrived(self, e, other):
        count = 2 * (8 >> max(self.k, other))
        r = self.refs
        at = message_slot(self.k, other)
        return pltpu.make_async_remote_copy(
            src_ref=r.sb.at[pl.ds(at, count)],
            dst_ref=r.rb.at[pl.ds(e * 16 + at, count)],
            send_sem=r.ssem.at[e * 4 + other],
            recv_sem=r.rsem.at[e * 4 + other],
            device_id=dict(branch=other),
            device_id_type=pl.DeviceIdType.MESH,
        )

    def others(self):
        return [other for other in range(4) if other != self.k]

    def sent(self, e):
        for other in self.others():
            self.message(e, other).wait_send()

    def receive(self, m):
        r = self.refs
        s, rb, hf, out = r.s, r.rb, r.hf, r.outs
        h = self.maps["h"]

        def total_at(tile, plane):
            where = m * 2 * self.planes + tile * self.planes + plane
            total = s[where]
            for other in self.others():
                count = 8 >> max(self.k, other)
                at = plane >> max(0, other - self.k)
                slot = m * 16 + message_slot(self.k, other) + tile * count + at
                total = total + rb[slot].astype(jnp.float32)
            s[where] = total
            return silu_of(total) * self.masks[0]

        def onward(plane):
            for tile in range(2):
                value = total_at(tile, plane)
                hf[(2 + tile) * self.planes + plane] = value
                h.store(1, tile, plane, value)

        def finish(plane):
            for tile in range(2):
                out[tile * self.planes + plane] = total_at(tile, plane).astype(jnp.bfloat16)

        @pl.when(m + 1 < MODULES)
        def _():
            planes_loop(self.planes, onward, TURNS)

        @pl.when(m + 1 == MODULES)
        def _():
            planes_loop(self.planes, finish, TURNS)

    def take_feature(self, tile, plane, value):
        self.refs.hf[tile * self.planes + plane] = value
        self.maps["h"].store(0, tile, plane, value)

    def take_cotangent(self, tile, plane, value):
        self.refs.gin[tile * self.planes + plane] = value

    def member(self, kind, order):
        kinds = self.refs.kinds
        found, before = jnp.int32(0), jnp.int32(0)
        for at in range(self.count):
            same = kinds[at] == kind
            found = jnp.where(same & (before == order), at, found)
            before = before + same.astype(jnp.int32)
        return found

    def order(self, device):
        kinds = self.refs.kinds
        kind = kinds[device]
        before = jnp.int32(0)
        for at in range(self.count):
            before = before + ((kinds[at] == kind) & (at < device)).astype(jnp.int32)
        return before

    def unpack(self, t, consume):
        r = self.refs
        work, rows, planes = r.work, self.rows, self.planes
        full = SH * SW * C0 // LANES
        gath = r.gathc if t else r.gathx

        @pl.when(self.core == 0)
        def _():
            for at in range(self.large):
                block = gath[self.member(1, at)]
                work[at * ROWS : (at + 1) * ROWS] = block.astype(jnp.float32)

        @pl.when(self.core == 1)
        def _():
            for at in range(self.small):
                block = gath[self.member(0, at), 0:full]
                work[at * full : (at + 1) * full] = block.astype(jnp.float32)
            work[self.small * full : self.large * ROWS] = jnp.zeros(
                (self.large * ROWS - self.small * full, LANES), jnp.float32
            )

        deep = self.large * ROWS // 2
        right = jnp.concatenate([work[pl.ds(j, deep, stride=2)] for j in range(2)], axis=1)
        right = right.astype(jnp.bfloat16)
        cells = Cells(self.core, (rows, LANES), self.small, self.large)
        base = cells.crop * cells.pick(ROWS // 2, full // 2)
        base = base + cells.along * (planes * cells.wide) + cells.across
        base = jnp.where(cells.valid, base, -(1 << 20))
        lane = lax.broadcasted_iota(jnp.int32, (rows, LANES), 1)
        chunk = min(planes, 4)

        def body(step):
            pieces = []
            for q in range(chunk):
                goal = base + (step * chunk + q) * cells.wide
                pieces.append(one_hot(goal, lane, deep))
            left = pieces[0] if chunk == 1 else jnp.concatenate(pieces, axis=0)
            result = lax.dot_general(left, right, DOWN, preferred_element_type=jnp.float32)
            for q in range(chunk):
                for tile in range(2):
                    value = result[q * rows : (q + 1) * rows, tile * LANES : (tile + 1) * LANES]
                    consume(tile, step * chunk + q, value)

        planes_loop(planes // chunk, body)

    def pack_size(self):
        return 48 * self.planes, -(-self.planes * self.rows // LANES) * LANES

    def plan_pack(self):
        r = self.refs
        high, deep = self.pack_size()
        planes = self.planes
        q = lax.broadcasted_iota(jnp.int32, (high, LANES), 0)
        lane = lax.broadcasted_iota(jnp.int32, (high, LANES), 1)
        wide, tall = jnp.where(self.core == 0, 6, 3), jnp.where(self.core == 0, 8, 4)
        cell = jnp.where(self.core == 0, (q * 43691) >> 18, (q * 43691) >> 17)
        across = q - cell * wide
        plane = cell & (planes - 1)
        along = cell >> log2(planes)
        base = plane * self.rows + along * wide + across
        base = jnp.where(along < tall, base, -(1 << 20))
        shard = lax.axis_index("crops")
        for at, device in enumerate((shard, shard + 1 - 2 * self.core)):
            goal = base + self.order(device) * (wide * tall)
            r.hot[at, 0:high, 0:deep] = one_hot(goal, lane, deep)

    def pack(self, units, put):
        high, deep = self.pack_size()
        right = jnp.concatenate([units(tile) for tile in range(2)], axis=1)
        short = deep - right.shape[0]
        parts = [right.astype(jnp.bfloat16)]
        if right.dtype == jnp.float32:
            parts.append((right - parts[0].astype(jnp.float32)).astype(jnp.bfloat16))
        if short:
            empty = jnp.zeros((short, 2 * LANES), jnp.bfloat16)
            parts = [jnp.concatenate([part, empty], axis=0) for part in parts]
        for at in range(2):
            total = None
            for part in parts:
                piece = lax.dot_general(
                    self.refs.hot[at, 0:high, 0:deep],
                    part,
                    DOWN,
                    preferred_element_type=jnp.float32,
                )
                total = piece if total is None else total + piece
            for tile in range(2):
                put(at, pl.ds(tile, high, stride=2), total[:, tile * LANES : (tile + 1) * LANES])

    def pack_outputs(self):
        r = self.refs
        high = 2 * self.pack_size()[0]

        def put(at, where, value):
            r.work[pl.ds(at * ROWS + where.start, where.size, stride=2)] = value

        def units(tile):
            block = r.outs[tile * self.planes : (tile + 1) * self.planes]
            return block.reshape(self.planes * self.rows, LANES)

        self.pack(units, put)
        for at in range(2):
            r.blocks[at, 0:high] = r.work[at * ROWS : at * ROWS + high].astype(jnp.bfloat16)
            if high < ROWS:
                r.blocks[at, high:ROWS] = jnp.zeros((ROWS - high, LANES), jnp.bfloat16)

    def pack_gradient(self):
        r = self.refs
        high = 2 * self.pack_size()[0]

        def put(at, where, value):
            r.slopes[at, where] = value

        def units(tile):
            block = r.gin[tile * self.planes : (tile + 1) * self.planes]
            return block.reshape(self.planes * self.rows, LANES)

        self.pack(units, put)
        if high < ROWS:
            for at in range(2):
                r.slopes[at, high:ROWS] = jnp.zeros((ROWS - high, LANES), jnp.float32)

    def forward(self, m, gather):
        def also(module, step):
            pl.when(m == module)(lambda: gather.step(1, step))

        self.conv(m, self.units["a"])
        self.apply_a(m)
        self.conv(m, self.units["b"])
        self.apply_b(m)
        also(1, 2)

        @pl.when(m > 0)
        def _():
            self.sent(m - 1)

        for name in ("d", "u", "e", "f", "g"):
            if name in self.units:
                self.conv(m, self.units[name])
                self.apply_rest(m, self.units[name])
        also(0, 1)
        also(1, 3)

        @pl.when(m == MODULES - 1)
        def _():
            gather.collect(1)
            self.unpack(1, self.take_cotangent)

        for other in self.others():
            self.arrived(m, other).wait_recv()
        self.receive(m)


    def send_back(self, m):
        r = self.refs
        s, gin, gt, sb = r.s, r.gin, r.gt, r.sb
        e = MODULES + m

        def body(plane):
            for tile in range(2):
                at = tile * self.planes + plane
                value = gin[at] * slope_of(s[m * 2 * self.planes + at])
                gt[at] = value
                for other in range(self.k):
                    sb[message_slot(self.k, other) + at] = value.astype(jnp.bfloat16)

        planes_loop(self.planes, body, TURNS)
        for other in reversed(self.others()):
            if other > self.k:
                count = 8 >> other
                wide = 1 << (other - self.k)

                def pool(plane):
                    for tile in range(2):
                        total = gt[tile * self.planes + plane * wide]
                        for step in range(1, wide):
                            total = total + gt[tile * self.planes + plane * wide + step]
                        slot = message_slot(self.k, other) + tile * count + plane
                        sb[slot] = total.astype(jnp.bfloat16)

                planes_loop(count, pool, TURNS)
            self.message(e, other).start()

    def back_unit(self, m, unit):
        r = self.refs
        st, dyb, z = r.st, r.dyb, getattr(r, "z" + unit.name)
        name, planes, tiles = unit.name, unit.planes, unit.tiles
        e = MODULES + m
        sums = {}

        def upstream(seg, tile, plane, normed):
            at = tile * planes + plane
            if name == "b":
                hf = r.hf[m * 2 * planes + at]
                value = r.gt[at] * slope_of(normed + hf)
                r.gin[at] = value
                return value
            if name == "a":
                return r.gu[at] * slope_of(normed)
            if seg.chain:
                return self.grads[seg.chain][at] * slope_of(normed)
            return r.rb[e * 16 + message_slot(self.k, seg.dest) + at].astype(jnp.float32)

        for seg in unit.segs:

            def body(plane, carry):
                result = []
                for tile in range(seg.tiles):
                    at = (seg.tile + tile) * planes + plane
                    where = m * STATS + unit.stat + seg.tile + tile
                    value = z[m * tiles * planes + at]
                    normed = value * st[where, 2:3] + st[where, 3:4]
                    dy = upstream(seg, tile, plane, normed)
                    dyb[at] = dy
                    zhat = (value - st[where, 0:1]) * st[where, 1:2]
                    result.append(carry[2 * tile] + partial_sum(dy))
                    result.append(carry[2 * tile + 1] + partial_sum(dy * zhat))
                return tuple(result)

            zero = jnp.zeros((8, LANES), jnp.float32)
            found = planes_sum(planes, body, (zero,) * (2 * seg.tiles), TURNS)
            pair = [
                jnp.concatenate([found[2 * tile + which] for tile in range(seg.tiles)], axis=1)
                for which in range(2)
            ]
            plain = SimpleNamespace(**vars(seg))
            plain.tile = 0
            totals = self.fold(plain, pair)
            self.table_grads(m, seg, totals)
            sums[seg.slot] = totals
        dz = self.dz_planes(unit)
        for seg in unit.segs:
            scale = self.per_cell(unit, seg)
            totals = sums[seg.slot]

            def apply(plane):
                for tile in range(seg.tiles):
                    at = (seg.tile + tile) * planes + plane
                    where = m * STATS + unit.stat + seg.tile + tile
                    zhat = (z[m * tiles * planes + at] - st[where, 0:1]) * st[where, 1:2]
                    inner = dyb[at] - totals[0][tile] * scale - zhat * (totals[1][tile] * scale)
                    dz.store(0, seg.tile + tile, plane, inner * st[where, 2:3] * self.masks[0])

            planes_loop(planes, apply, TURNS)
        self.back_data(m, unit, dz)
        first = min(seg.off for seg in unit.segs)
        last = max(seg.off + seg.taps**2 * seg.cin * seg.cout // LANES for seg in unit.segs)
        wanted = (self.quarter * self.share < last) & ((self.quarter + 1) * self.share > first)

        @pl.when(wanted)
        def _():
            self.back_kernel(m, unit, dz)

    def dz_planes(self, unit):
        r = self.refs
        mode = {"p1": "p", "s2": "dz2", "s1": "wide" if self.k == 3 else "s1"}[unit.kind]
        return Planes(
            mode,
            unit.tiles,
            unit.planes,
            self.masks,
            self.rows,
            r.dC,
            r.dE,
            r.dR,
            self.k <= 1 and unit.kind == "s1",
        )

    def table_grads(self, m, seg, totals):
        gg = self.refs.gg
        slot = seg.slot
        for which, found in ((0, totals[1]), (1, totals[0])):
            if seg.cout > LANES:
                for tile in range(2):
                    gg[m, which, slot : slot + 1, tile * LANES : (tile + 1) * LANES] = found[tile]
            else:
                row = jnp.broadcast_to(found[0], (8, LANES))
                if seg.cout < LANES:
                    row = self.keep(row, seg.cout, [0])
                gg[m, which, slot : slot + 1, 0:LANES] = row[0:1]

    def wide_rows(self, ref, at, tiles, plane, count):
        pieces = [
            ref[pl.ds(at(0, tile, plane), count)].reshape(count * self.rows, LANES)
            for tile in range(tiles)
        ]
        return pieces[0] if tiles == 1 else jnp.concatenate(pieces, axis=1)

    def back_data(self, m, unit, dz):
        r = self.refs
        kind, tiles = unit.kind, unit.tiles
        target = getattr(r, "T" + unit.name)
        lanes = tiles * LANES
        rows = self.rows

        def kernel_rows(d, first, count):
            return target[m * unit.depth + d, first : first + count, 0:lanes]

        def product(left, right):
            return lax.dot_general(left, right, ACROSS, preferred_element_type=jnp.float32)

        def put(ref, tile, planes, first, count, value, step=1, add=False):
            block = value.reshape(count, rows, LANES)
            for q in range(count):
                at = tile * planes + first + q * step
                ref[at] = ref[at] + block[q] if add else block[q]

        planes = unit.planes
        if kind == "s1":
            goal = r.gu if unit.name == "b" else r.gin
            add = unit.name == "a"
            chunk = min(planes, 4)
            across = getattr(r, "T" + unit.name + unit.name)

            def body(step):
                first = step * chunk
                if self.k == 3:
                    total = None
                    for d in range(3):
                        for ref, at in ((dz.right, 0), (dz.main, 256), (dz.edge, 512)):
                            left = self.wide_rows(ref, dz.at, 2, first + 1 - d, chunk)
                            piece = product(left, kernel_rows(d, at, 256))
                            total = piece if total is None else total + piece
                else:
                    narrow = 1 if dz.narrow else 2
                    left = []
                    for d in range(3):
                        at = first + 1 - d
                        left.append(self.wide_rows(dz.main, dz.at, 2, at, chunk))
                        left.append(self.wide_rows(dz.edge, dz.edge_at, narrow, at, chunk))
                    right = across[pl.ds(m * 3, 3), 0 : unit.rows].reshape(3 * unit.rows, 256)
                    total = lax.dot_general(
                        jnp.concatenate(left, axis=1),
                        right,
                        DOWN,
                        preferred_element_type=jnp.float32,
                    )
                for tile in range(2):
                    put(
                        goal,
                        tile,
                        planes,
                        first,
                        chunk,
                        total[:, tile * LANES : (tile + 1) * LANES],
                        add=add,
                    )

            planes_loop(planes // chunk, body, 2)
            return
        if kind == "p1":
            left = self.wide_rows(dz.main, dz.at, tiles, 0, planes)
            total = product(left, kernel_rows(0, 0, 256))
            for tile in range(2):
                put(
                    r.gt,
                    tile,
                    planes,
                    0,
                    planes,
                    total[:, tile * LANES : (tile + 1) * LANES],
                    add=True,
                )
            return
        goal = self.grads[unit.source]
        add = unit.source == "t"
        lanes_in = unit.lanes_in
        count_in = unit.planes_in
        for parity, terms in ((0, [(1, 0)]), (1, [(2, 0), (0, 1)])):
            total, side = None, None
            for d, offset in terms:
                left = self.wide_rows(dz.main, dz.at, tiles, offset, planes)
                piece = product(left, kernel_rows(d, 0, lanes_in))
                total = piece if total is None else total + piece
                left = self.wide_rows(dz.edge, dz.at, tiles, offset, planes)
                piece = product(left, kernel_rows(d, lanes_in, LANES))
                side = piece if side is None else side + piece
            for tile in range(lanes_in // LANES):
                value = total[:, tile * LANES : (tile + 1) * LANES]
                if tile == lanes_in // LANES - 1:
                    value = value + side
                put(goal, tile, count_in, parity, planes, value, step=2, add=add)

    def back_kernel(self, m, unit, dz):
        r = self.refs
        G, rep, wgv = r.work, r.rep, r.wgv
        tiles, planes = unit.tiles, unit.planes
        source = self.maps[unit.source]
        right = self.wide_rows(dz.main, dz.at, tiles, 0, planes)

        def gather(d):
            at = 0
            for part in self.parts(unit, source):
                pieces = self.rows_of(unit, part, m, d, 0, planes)
                left = pieces[0] if len(pieces) == 1 else jnp.concatenate(pieces, axis=1)
                count = left.shape[1]
                result = lax.dot_general(left, right, ALONG, preferred_element_type=jnp.float32)
                for tile in range(tiles):
                    row = pl.multiple_of((d * tiles + tile) * unit.rows + at, 8)
                    G[pl.ds(row, count)] = result[:, tile * LANES : (tile + 1) * LANES]
                at += count

        if self.k == 3 and unit.kind == "s1":
            self.direct_kernel(m, unit, right)
            return
        planes_loop(unit.depth, gather)
        for seg in unit.segs:
            self.fold_kernel(m, unit, seg)

    def direct_kernel(self, m, unit, right):
        wgv, (seg,) = self.refs.wgv, unit.segs
        source = self.maps[unit.source]
        span = 2 * seg.cin
        low, high = self.quarter * self.share, (self.quarter + 1) * self.share

        def tap_row(d):
            first = seg.off + d * (3 * span)

            @pl.when((first < high) & (first + 3 * span > low))
            def _():
                for column, part in enumerate(self.parts(unit, source)):
                    pieces = self.rows_of(unit, part, m, d, 0, unit.planes)
                    left = jnp.concatenate(pieces, axis=1)
                    result = lax.dot_general(left, right, ALONG, preferred_element_type=jnp.float32)
                    for tile in range(2):
                        rows = pl.ds(first + column * span + tile, seg.cin, stride=2)
                        wgv[rows] = result[:, tile * LANES : (tile + 1) * LANES]

        planes_loop(unit.depth, tap_row)

    def fold_kernel(self, m, unit, seg):
        r = self.refs
        G, rep, wgv = r.work, r.rep, r.wgv
        cin, cout, tiles = seg.cin, seg.cout, unit.tiles
        width = 3 if seg.taps == 3 else 1
        found = links(self.k, unit, seg)
        off = seg.off

        def fold(d):
            for column in range(width):
                tap = d * width + column
                totals = []
                for tile in range(seg.tiles):
                    total = None
                    for row, which, wanted in found:
                        if which != column:
                            continue
                        at = pl.multiple_of((d * tiles + seg.tile + tile) * unit.rows + row, 8)
                        piece = G[pl.ds(at, cin)]
                        if cout <= LANES:
                            local = self.local_blocks(seg, tile, wanted)
                            if not local:
                                continue
                            piece = self.keep(piece, cout, local)
                        total = piece if total is None else total + piece
                    totals.append(total)
                if cout > LANES:
                    for tile in range(2):
                        wgv[pl.ds(off + tap * (2 * cin) + tile, cin, stride=2)] = totals[tile]
                    continue
                total = None
                for piece in totals:
                    if piece is not None:
                        total = piece if total is None else total + piece
                if cout == LANES:
                    wgv[pl.ds(pl.multiple_of(off + tap * cin, 8), cin)] = total
                else:
                    rep[pl.ds(pl.multiple_of(tap * cin, cin), cin)] = self.spread(total, cout)

        planes_loop(unit.depth, fold)
        if cout < LANES:
            ratio = LANES // cout
            count = width * width * cin // ratio
            total = None
            for part in range(ratio):
                piece = self.keep(rep[pl.ds(part, count, stride=ratio)], cout, [part])
                total = piece if total is None else total + piece
            wgv[off : off + count] = total

    def backward(self, m, meanwhile):
        e = MODULES + m
        last = m == MODULES - 1
        self.sent(jnp.where(last, m, e + 1))
        self.send_back(m)
        pl.when(last)(meanwhile)
        for name in ("g", "f", "e", "d", "u"):
            if name in self.units:
                for seg in self.units[name].segs:
                    if seg.dest >= 0:
                        self.arrived(e, seg.dest).wait_recv()
                self.back_unit(m, self.units[name])
        self.back_unit(m, self.units["b"])
        self.back_unit(m, self.units["a"])


STATS = 20
TURNS = 8
NAMES = list(
    dict(x=0, cot=0, w=0, gains=0, shifts=0, kinds=0, out=0, grad=0, wg=0, gain=0, shift=0)
)


def one_hot(goal, lane, deep):
    pieces = [
        jnp.where(goal == lane + first, 1.0, 0.0).astype(jnp.bfloat16)
        for first in range(0, deep, LANES)
    ]
    return jnp.concatenate(pieces, axis=1)


class Cells:
    def __init__(self, core, shape, small, large):
        self.core = core
        row = lax.broadcasted_iota(jnp.int32, shape, 0)
        self.wide = self.pick(LW // 8, SW // 8)
        tall = self.pick(LH // 8, SH // 8)
        self.crop = self.pick((row * 43691) >> 21, (row * 43691) >> 19)
        inner = row - self.crop * (self.wide * tall)
        self.along = self.pick((inner * 43691) >> 18, (inner * 43691) >> 17)
        self.across = inner - self.along * self.wide
        self.valid = self.crop < self.pick(large, small)
        self.last = tall - 1

    def pick(self, large, small):
        return jnp.where(self.core == 0, large, small)


def fill_masks(refs, rows, core, small, large):
    cells = Cells(core, (rows, LANES), small, large)
    valid = cells.valid
    six = cells.wide == 6
    up, down = valid & (cells.along > 0), valid & (cells.along < cells.last)
    tables = (
        valid,
        valid & (cells.across > 0),
        valid & (cells.across < cells.wide - 1),
        up & six,
        up & jnp.logical_not(six),
        down & six,
        down & jnp.logical_not(six),
    )
    for at, table in enumerate(tables):
        refs.masks[at] = jnp.where(table, 1.0, 0.0)


class Gather:
    def __init__(self, refs, core, count):
        self.refs, self.core, self.count = refs, core, count
        self.z = lax.axis_index("crops") // 2
        self.last = count // 2 - 1

    def hop(self, t, source, right):
        r = self.refs
        at = source * 2 + self.core
        gath = r.gathc if t else r.gathx
        to = self.z + 1 if right else self.z - 1
        return pltpu.make_async_remote_copy(
            src_ref=gath.at[at],
            dst_ref=gath.at[at],
            send_sem=r.hsem.at[(t * (self.last + 1) + source) * 3 + (0 if right else 1)],
            recv_sem=r.gsem.at[t * self.count + at],
            device_id=dict(crops=to * 2 + self.core),
            device_id_type=pl.DeviceIdType.MESH,
        )

    def across(self, t, source, core, rows):
        r = self.refs
        at = source * 2 + core
        gath = r.gathc if t else r.gathx
        return pltpu.make_async_remote_copy(
            src_ref=gath.at[at, pl.ds(0, rows)],
            dst_ref=gath.at[at, pl.ds(0, rows)],
            send_sem=r.hsem.at[(t * (self.last + 1) + source) * 3 + 2],
            recv_sem=r.gsem.at[t * self.count + at],
            device_id=dict(crops=self.z * 2 + 1 - self.core),
            device_id_type=pl.DeviceIdType.MESH,
        )

    def each_core(self, action):
        for core, rows in ((0, SH * SW * C0 // LANES), (1, ROWS)):

            @pl.when(self.core == core)
            def _():
                action(core, rows)

    def send(self, t, source, rightward, leftward):
        if rightward:

            @pl.when(self.z < self.last)
            def _():
                self.hop(t, source, True).start()

        if leftward:

            @pl.when(self.z > 0)
            def _():
                self.hop(t, source, False).start()

        self.each_core(lambda core, rows: self.across(t, source, core, rows).start())

    def step(self, t, s):
        r = self.refs
        if s == 0:
            at = self.z * 2 + self.core
            if t:
                r.gathc[at] = r.cot[...]
            else:
                r.gathx[at] = r.x[...]
            self.send(t, self.z, True, True)
            return

        @pl.when(self.z >= s)
        def _():
            self.hop(t, self.z - s, True).wait_recv()
            self.send(t, self.z - s, True, False)

        @pl.when(self.z + s <= self.last)
        def _():
            self.hop(t, self.z + s, True).wait_recv()
            self.send(t, self.z + s, False, True)

    def collect(self, t):
        for source in range(self.last + 1):
            for core, rows in ((0, ROWS), (1, SH * SW * C0 // LANES)):

                @pl.when(self.core == core)
                def _():
                    self.across(t, source, 1 - core, rows).wait_recv()

    def finish(self, t):
        def sent(source, rightward, leftward):
            if rightward:

                @pl.when(self.z < self.last)
                def _():
                    self.hop(t, source, True).wait_send()

            if leftward:

                @pl.when(self.z > 0)
                def _():
                    self.hop(t, source, False).wait_send()

            self.each_core(lambda core, rows: self.across(t, source, core, rows).wait_send())

        sent(self.z, True, True)
        for s in range(1, self.last + 1):

            @pl.when(self.z >= s)
            def _():
                sent(self.z - s, True, False)

            @pl.when(self.z + s <= self.last)
            def _():
                sent(self.z + s, False, True)


def scratch_table(rows, weight_rows, count):
    def half(many):
        return pltpu.VMEM((many, rows, LANES), jnp.bfloat16)

    def full(many):
        return pltpu.VMEM((many, rows, LANES), jnp.float32)

    def expanded(depth, deep, wide):
        return pltpu.VMEM((MODULES * depth, deep, wide), jnp.bfloat16)

    _, span, low = pair_rows(weight_rows, count)
    return dict(
        masks=full(MASKS),
        hC=half(2 * 20),
        hE=half(2 * 10),
        hR=half(2 * 6),
        uC=half(2 * 20),
        uE=half(2 * 10),
        uR=half(2 * 6),
        tC=half(2 * 18),
        tE=half(2 * 9),
        c1C=half(2 * 5),
        c1E=half(2 * 5),
        c2C=half(2 * 5),
        c2E=half(2 * 5),
        c3C=half(2 * 3),
        c3E=half(2 * 3),
        dC=half(20),
        dE=half(20),
        dR=half(6),
        outs=half(16),
        hf=full(2 * 16),
        s=full(2 * 16),
        za=full(2 * 16),
        zb=full(2 * 16),
        zd=full(2 * 16),
        zu=full(2 * 8),
        ze=full(2 * 4),
        zf=full(2 * 2),
        zg=full(2 * 2),
        gt=full(16),
        gu=full(16),
        gin=full(16),
        gc1=full(4),
        gc2=full(4),
        gc3=full(2),
        dyb=full(16),
        sb=half(16),
        rb=half(4 * 16),
        st=pltpu.VMEM((MODULES * STATS, 8, LANES), jnp.float32),
        Ta=expanded(3, 768, 256),
        Tb=expanded(3, 768, 256),
        Taa=expanded(3, 512, 256),
        Tbb=expanded(3, 512, 256),
        Td=expanded(3, 384, 512),
        Tu=expanded(1, 256, 768),
        Te=expanded(3, 256, 256),
        Tf=expanded(3, 256, 128),
        Tg=expanded(3, 256, 256),
        raw=pltpu.VMEM((9408, LANES), jnp.bfloat16),
        work=pltpu.VMEM((4608, LANES), jnp.float32),
        rep=pltpu.VMEM((640, LANES), jnp.float32),
        wgv=pltpu.VMEM((weight_rows, LANES), jnp.float32),
        wq=pltpu.VMEM((MODULES, low + span, LANES), jnp.float32),
        wh=pltpu.VMEM((MODULES, low + span, LANES), jnp.bfloat16),
        wr=pltpu.VMEM((MODULES, span, LANES), jnp.bfloat16),
        gathx=pltpu.VMEM((count, ROWS, LANES), jnp.bfloat16),
        gathc=pltpu.VMEM((count, ROWS, LANES), jnp.bfloat16),
        hot=pltpu.VMEM((2, 384, 768), jnp.bfloat16),
        blocks=pltpu.VMEM((2, ROWS, LANES), jnp.bfloat16),
        slopes=pltpu.VMEM((2, ROWS, LANES), jnp.float32),
        blockr=pltpu.VMEM((ROWS, LANES), jnp.bfloat16),
        slopeh=pltpu.VMEM((ROWS, LANES), jnp.bfloat16),
        sloper=pltpu.VMEM((ROWS, LANES), jnp.bfloat16),
        gg=pltpu.VMEM((MODULES, 2, SLOTS, 256), jnp.float32),
        ggr=pltpu.VMEM((MODULES, 2, SLOTS, 256), jnp.float32),
        wsem=pltpu.SemaphoreType.DMA((8,)),
        ssem=pltpu.SemaphoreType.DMA((16,)),
        rsem=pltpu.SemaphoreType.DMA((16,)),
        hsem=pltpu.SemaphoreType.DMA((3 * count,)),
        gsem=pltpu.SemaphoreType.DMA((2 * count,)),
        psem=pltpu.SemaphoreType.DMA((5,)),
        qsem=pltpu.SemaphoreType.DMA((5,)),
        osem=pltpu.SemaphoreType.DMA((1,)),
    )


def pair_rows(weight_rows, count):
    share = weight_rows // count
    low = share // 16 * 16
    return share, -(-(2 * share - low) // 16) * 16, low


def greet(core, count):
    barrier = pltpu.get_barrier_semaphore()
    me, shard = lax.axis_index("branch"), lax.axis_index("crops")
    z = shard // 2

    def signal(**where):
        pl.semaphore_signal(barrier, inc=1, device_id=where, device_id_type=pl.DeviceIdType.MESH)

    for step in range(1, 4):
        signal(branch=lax.rem(me + step, 4))
    signal(crops=shard + 1 - 2 * core)

    @pl.when(z > 0)
    def _():
        signal(crops=shard - 2)

    @pl.when(z < count // 2 - 1)
    def _():
        signal(crops=shard + 2)

    ends = (z == 0).astype(jnp.int32) + (z == count // 2 - 1).astype(jnp.int32)
    pl.semaphore_wait(barrier, 6 - ends)


def whole_kernel(names, rows, large, small, *args):
    refs = SimpleNamespace(**dict(zip(names, args)))
    count = large + small
    me, shard = lax.axis_index("branch"), lax.axis_index("crops")
    core = shard % 2
    weight_rows = refs.wgv.shape[0]
    share, span, low = pair_rows(weight_rows, count)
    quarter = pl.multiple_of(shard // 2 * (2 * share), 8)

    class Lazy:
        def __getitem__(self, index):
            return refs.masks[index]

    def across(source, goal, index):
        return pltpu.make_async_remote_copy(
            src_ref=source,
            dst_ref=goal,
            send_sem=refs.psem.at[index],
            recv_sem=refs.qsem.at[index],
            device_id=dict(crops=shard + 1 - 2 * core),
            device_id_type=pl.DeviceIdType.MESH,
        )

    def kernel_pair(m):
        at = pl.multiple_of(low * (1 - core), 16)
        return across(refs.wh.at[m, pl.ds(at, span)], refs.wr.at[m], m)

    outputs_pair = across(refs.blocks.at[1], refs.blockr, 2)
    gradient_pair = across(refs.slopeh, refs.sloper, 3)
    table_pair = across(refs.gg, refs.ggr, 4)
    gather = Gather(refs, core, count)

    def every(action):
        for k in range(4):

            @pl.when(me == k)
            def _():
                action(Branch(k, rows, large, small, 2 * share, refs, Lazy(), core))

    def begin(branch):
        branch.fetch_first()

    def prepare(branch):
        found = branch.segments()
        stops = {0: 1, min(2, len(found) - 2): 2, len(found) - 1: 3}
        for index, (unit, seg) in enumerate(found):
            branch.expand(index)
            if index in stops:
                gather.step(0, stops[index])

    def main(branch):
        branch.unpack(0, branch.take_feature)
        branch.maps["h"].close(0)
        gather.step(1, 0)

        def ahead(m, carry):
            branch.forward(m, gather)
            return carry

        def meanwhile():
            branch.plan_pack()
            branch.pack_outputs()
            outputs_pair.start()

        def back(step, carry):
            m = MODULES - 1 - step
            branch.backward(m, meanwhile)
            found = refs.wgv[pl.ds(quarter, 2 * share)]
            refs.wq[m, 0 : 2 * share] = found
            spare = jnp.zeros((low + span - 2 * share, LANES), jnp.float32)
            refs.wh[m] = jnp.concatenate([found, spare], axis=0).astype(jnp.bfloat16)
            kernel_pair(m).start()
            return carry

        lax.fori_loop(0, MODULES, ahead, 0)
        lax.fori_loop(0, MODULES, back, 0)
        branch.sent(MODULES)
        branch.pack_gradient()
        refs.slopeh[...] = refs.slopes[1].astype(jnp.bfloat16)
        gradient_pair.start()
        table_pair.start()

    every(begin)
    greet(core, count)
    gather.step(0, 0)
    fill_masks(refs, rows, core, small, large)
    refs.wgv[pl.ds(quarter, 2 * share)] = jnp.zeros((2 * share, LANES), jnp.float32)
    refs.gg[...] = jnp.zeros(refs.gg.shape, jnp.float32)
    every(prepare)
    gather.collect(0)
    every(main)

    for step in range(MODULES):
        m = MODULES - 1 - step
        kernel_pair(m).wait()
        mine = refs.wq[m, pl.ds(pl.multiple_of(low * core, 8), span)]
        refs.work[pl.ds(m, span, stride=MODULES)] = mine + refs.wr[m].astype(jnp.float32)
    skip = pl.multiple_of(core * (MODULES * (share - low)), 8)
    leave = pltpu.make_async_copy(
        refs.work.at[pl.ds(skip, MODULES * share)], refs.wg, refs.osem.at[0]
    )
    leave.start()
    outputs_pair.wait()
    gradient_pair.wait()
    table_pair.wait()
    own = refs.kinds[shard] != core
    refs.out[...] = jnp.where(own, refs.blocks[0].astype(jnp.float32), refs.blockr[...].astype(jnp.float32)).astype(jnp.bfloat16)
    refs.grad[...] = jnp.where(own, refs.slopes[0], refs.sloper[...].astype(jnp.float32))
    width = 256 // count
    for which, goal in ((0, refs.gain), (1, refs.shift)):
        for m in range(MODULES):
            total = refs.gg[m, which] + refs.ggr[m, which]
            found = None
            for at in range(count):
                piece = jnp.where(shard == at, total[:, at * width : (at + 1) * width], 0.0)
                found = piece if found is None else found + piece
            goal[m] = found
    gather.finish(0)
    gather.finish(1)
    leave.wait()


def whole_call(rows, large, small, x, cot, w, gains, shifts, kinds):
    count = large + small
    weight_rows = w.shape[0] // MODULES
    table = scratch_table(rows, weight_rows, count)
    vmem = pl.BlockSpec(memory_space=pltpu.VMEM)
    hbm = pl.BlockSpec(memory_space=pl.ANY)
    smem = pl.BlockSpec(memory_space=pltpu.SMEM)
    tables = jax.ShapeDtypeStruct((MODULES, SLOTS, 256 // count), jnp.float32)
    return pl.pallas_call(
        partial(whole_kernel, NAMES + list(table), rows, large, small),
        out_shape=(
            jax.ShapeDtypeStruct((ROWS, LANES), jnp.bfloat16),
            jax.ShapeDtypeStruct((ROWS, LANES), jnp.float32),
            jax.ShapeDtypeStruct((MODULES * weight_rows // count, LANES), jnp.float32),
            tables,
            tables,
        ),
        in_specs=[vmem, vmem, hbm, vmem, vmem, smem],
        out_specs=(vmem, vmem, hbm, vmem, vmem),
        scratch_shapes=list(table.values()),
        compiler_params=pltpu.CompilerParams(
            collective_id=0, has_side_effects=True, vmem_limit_bytes=62 * 1024 * 1024
        ),
    )(x, cot, w, gains, shifts, kinds)


def leave_kernel(*args):
    sources, goals, rooms, arrive, depart = args[:5], args[5:10], args[10:15], args[15], args[16]
    pieces = []
    for source, goal, room in zip(sources, goals, rooms):
        high = source.shape[0]
        parts = 3 if high % 24 == 0 else 1
        for part in range(parts):
            rows = pl.ds(part * (high // parts), high // parts)
            at = len(pieces)
            pieces.append(
                (
                    pltpu.make_async_copy(source.at[rows], room.at[rows], arrive.at[at]),
                    pltpu.make_async_copy(room.at[rows], goal.at[rows], depart.at[at]),
                )
            )
    for come, _ in pieces:
        come.start()
    for come, go in pieces:
        come.wait()
        go.start()
    for _, go in pieces:
        go.wait()


def leave_call(arrays):
    hbm = pl.BlockSpec(memory_space=pl.ANY)
    return pl.pallas_call(
        leave_kernel,
        out_shape=tuple(jax.ShapeDtypeStruct(array.shape, array.dtype) for array in arrays),
        in_specs=[hbm] * 5,
        out_specs=(hbm,) * 5,
        scratch_shapes=[pltpu.VMEM(array.shape, array.dtype) for array in arrays]
        + [pltpu.SemaphoreType.DMA((16,)), pltpu.SemaphoreType.DMA((16,))],
    )(*arrays)


def on_device_grouped(features, weights, gains, shifts, cotangent, size_group):
    count = lax.axis_size("crops")
    large = count // 4
    weight_rows = weights.shape[2] // LANES
    results = whole_call(
        group_rows(count),
        large,
        count - large,
        features[0],
        cotangent[0],
        weights[0]
        .reshape(MODULES, weight_rows, LANES)
        .transpose(1, 0, 2)
        .reshape(MODULES * weight_rows, LANES),
        gains[0],
        shifts[0],
        size_group,
    )
    out, grad, weight_grad, gain, shift = leave_call(results)
    share = weight_rows // count
    weight_grad = weight_grad.reshape(share, MODULES, LANES).transpose(1, 0, 2)
    weight_grad = with_layout_constraint(weight_grad, Layout((1, 0, 2)))
    return (
        out[None],
        grad[None],
        weight_grad.reshape(1, MODULES, share * LANES),
        gain[None],
        shift[None],
    )


def group_rows(count):
    large = count // 4
    rows = max(large * (LH // 8) * (LW // 8), (count - large) * (SH // 8) * (SW // 8))
    return -(-rows // 16) * 16


def fits(count):
    return count % 8 == 0 and group_rows(count) <= 96


def solution(mesh):
    placed = (
        P("branch", "crops", None),
        P("branch", None, None),
        P("branch", None, None, None),
        P("branch", None, None, None),
        P("branch", "crops", None),
        P(),
    )
    return jax.shard_map(
        on_device_grouped if fits(mesh.shape["crops"]) else on_device,
        mesh=mesh,
        in_specs=placed,
        out_specs=(
            P("branch", "crops", None),
            P("branch", "crops", None),
            P("branch", None, "crops"),
            P("branch", None, None, "crops"),
            P("branch", None, None, "crops"),
        ),
        check_vma=False,
    )
```

```python
from functools import partial
from types import SimpleNamespace
import math

import jax
import jax.numpy as jnp
import numpy as np
from jax import lax
from jax.experimental import pallas as pl
from jax.experimental.layout import Layout, with_layout_constraint
from jax.experimental.pallas import tpu as pltpu
from jax.sharding import PartitionSpec as P

C0 = 32
BLOCKS = 1
MODULES = 2
CROPS_DEV = 1
SH = 32
SW = 24
LH = 64
LW = 48
ROWS = 768
MSG_ROWS = 384


EPS = 1e-05


def as_sent(x):

    def short(part):
        return part.astype(jnp.bfloat16) if part.dtype == jnp.float32 else part

    return jax.tree.map(short, x)


def sender_plan(branch_index, top_channels, blocks):
    channels = top_channels << branch_index
    operations = []
    for block_index in range(blocks):
        operations.append(
            SimpleNamespace(
                phase=2 * block_index,
                source=("h", block_index),
                level=branch_index,
                cin=channels,
                cout=channels,
                stride=1,
                taps=3,
                act="silu",
                output=("u", block_index),
                skip=None,
                dest=-1,
            )
        )
        operations.append(
            SimpleNamespace(
                phase=2 * block_index + 1,
                source=("u", block_index),
                level=branch_index,
                cin=channels,
                cout=channels,
                stride=1,
                taps=3,
                act="res",
                output=("h", block_index + 1),
                skip=("h", block_index),
                dest=-1,
            )
        )
    top_name = ("h", blocks)
    for target in range(branch_index):
        operations.append(
            SimpleNamespace(
                phase=2 * blocks,
                source=top_name,
                level=branch_index,
                cin=channels,
                cout=top_channels << target,
                stride=1,
                taps=1,
                act="none",
                output=None,
                skip=None,
                dest=target,
            )
        )
    for target in range(branch_index + 1, 4):
        for depth_step in range(1, target - branch_index + 1):
            is_last = depth_step == target - branch_index
            operations.append(
                SimpleNamespace(
                    phase=2 * blocks + depth_step - 1,
                    source=top_name if depth_step == 1 else ("chain", target, depth_step - 1),
                    level=branch_index + depth_step,
                    cin=channels,
                    cout=top_channels << target if is_last else channels,
                    stride=2,
                    taps=3,
                    act="none" if is_last else "silu",
                    output=None if is_last else ("chain", target, depth_step),
                    skip=None,
                    dest=target if is_last else -1,
                )
            )
    for position, operation in enumerate(operations):
        operation.slot = position
        operation.size = (
            operation.taps * operation.taps * operation.cin * operation.cout
        )
        if operation.taps == 1:
            operation.kshape = (operation.cin, operation.cout)
        else:
            operation.kshape = (3, 3, operation.cin, operation.cout)
    return operations


def phase_lengths(top_channels, blocks):
    phase_count = 2 * blocks + 3
    lengths = [0] * phase_count
    for branch_index in range(4):
        per_phase = [0] * phase_count
        for operation in sender_plan(branch_index, top_channels, blocks):
            per_phase[operation.phase] += operation.size
        lengths = [max(current, candidate) for current, candidate in zip(lengths, per_phase)]
    return lengths


def weighted_plan(branch_index, top_channels, blocks):
    lengths = phase_lengths(top_channels, blocks)
    starts = [sum(lengths[:phase_index]) for phase_index in range(len(lengths))]
    running = [0] * len(lengths)
    operations = sender_plan(branch_index, top_channels, blocks)
    for operation in operations:
        phase_index = operation.phase
        operation.inner = running[phase_index]
        operation.offset = starts[phase_index] + running[phase_index]
        operation.position = sum(
            (1 for earlier in operations[: operation.slot] if earlier.phase == phase_index)
        )
        running[phase_index] += operation.size
    return operations


def phase_operations(branch_index, phase_index):
    return [
        operation
        for operation in weighted_plan(branch_index, C0, BLOCKS)
        if operation.phase == phase_index
    ]


def input_names(operations):
    source_names = []
    for operation in operations:
        if operation.source not in source_names:
            source_names.append(operation.source)
    return source_names


def silu_slope(value):
    sigmoid = jax.nn.sigmoid(value)
    return sigmoid * (1.0 + value * (1.0 - sigmoid))


def crop_cells(size_kind):
    return (LH, LW) if size_kind else (SH, SW)


def map_dims(size_kind, level, channels):
    height, breadth = crop_cells(size_kind)
    return (CROPS_DEV, height >> level, breadth >> level, channels)


def source_dims(branch_index, size_kind, map_name):
    level = branch_index + map_name[2] if map_name[0] == "chain" else branch_index
    return map_dims(size_kind, level, C0 << branch_index)


def preact_dims(size_kind, operation):
    return map_dims(size_kind, operation.level, operation.cout)


def to_canvas(arrays, value_type):
    if not arrays:
        return jnp.zeros((ROWS, 128), value_type)
    flattened = jnp.concatenate([array.reshape(-1).astype(value_type) for array in arrays])
    return jnp.pad(flattened, (0, ROWS * 128 - flattened.shape[0])).reshape(ROWS, 128)


def from_canvas(canvas, dims_list):
    flattened = canvas.reshape(-1)
    pieces = []
    offset = 0
    for dims_entry in dims_list:
        count_here = math.prod(dims_entry)
        pieces.append(flattened[offset : offset + count_here].reshape(dims_entry))
        offset += count_here
    return pieces


def to_slot(array):
    flattened = array.reshape(-1)
    return jnp.pad(flattened, (0, MSG_ROWS * 128 - flattened.shape[0])).reshape(MSG_ROWS, 128)


def from_slot(slot_rows, dims_entry):
    return slot_rows.reshape(-1)[: math.prod(dims_entry)].reshape(dims_entry)


def upsample(message, factor):
    crop_count, height, breadth, channels = message.shape
    widened = jnp.broadcast_to(
        message[:, :, None, :, None, :], (crop_count, height, factor, breadth, factor, channels)
    )
    return widened.reshape(crop_count, height * factor, breadth * factor, channels)


def block_pool(array, factor):
    crop_count, height, breadth, channels = array.shape
    return array.reshape(
        crop_count, height // factor, factor, breadth // factor, factor, channels
    ).sum(axis=(2, 4))


def kernel_piece(module_weights, operation):
    start = operation.offset
    return module_weights[start : start + operation.size].reshape(operation.kshape)


def conv_forward(operation, source, kernel):
    if operation.taps == 1:
        return jnp.einsum("nhwc,cd->nhwd", source, kernel, preferred_element_type=jnp.float32)
    stride = operation.stride
    return lax.conv_general_dilated(
        source,
        kernel,
        (stride, stride),
        ((1, 1), (1, 1)),
        dimension_numbers=("NHWC", "HWIO", "NHWC"),
        preferred_element_type=jnp.float32,
    )


def conv_backward(operation, source, kernel, upstream):
    if operation.taps == 1:
        source_grad = jnp.einsum(
            "nhwd,cd->nhwc", upstream, kernel, preferred_element_type=jnp.float32
        )
        kernel_grad = jnp.einsum(
            "nhwc,nhwd->cd", source, upstream, preferred_element_type=jnp.float32
        )
        return (source_grad, kernel_grad)
    stride = operation.stride
    flipped = jnp.transpose(kernel[::-1, ::-1], (0, 1, 3, 2))
    high_pad = 2 if stride == 2 else 1
    source_grad = lax.conv_general_dilated(
        upstream,
        flipped,
        (1, 1),
        ((1, high_pad), (1, high_pad)),
        lhs_dilation=(stride, stride),
        dimension_numbers=("NHWC", "HWIO", "NHWC"),
        preferred_element_type=jnp.float32,
    )
    kernel_grad = lax.conv_general_dilated(
        source,
        upstream,
        (1, 1),
        ((1, 2 - stride), (1, 2 - stride)),
        rhs_dilation=(stride, stride),
        dimension_numbers=("CHWN", "IHWO", "NHWC"),
        preferred_element_type=jnp.float32,
    )
    return (source_grad, jnp.transpose(kernel_grad, (1, 2, 0, 3)))


def cell_total(counts, size_kind, level):
    height, breadth = crop_cells(size_kind)
    return counts[size_kind] * float(CROPS_DEV * (height >> level) * (breadth >> level))


def norm_terms(totals, counts, size_kind, operation):
    cells_here = cell_total(counts, size_kind, operation.level)
    channels = operation.cout
    position = operation.position
    average = totals[size_kind, 0, position, :channels] / cells_here
    variance = totals[size_kind, 1, position, :channels] / cells_here - average * average
    return (average, lax.rsqrt(variance + EPS))


def forward_conv(branch_index, size_kind, phase_index, source_canvas, module_weights):
    operations = phase_operations(branch_index, phase_index)
    source_names = input_names(operations)
    pieces = from_canvas(
        source_canvas, [source_dims(branch_index, size_kind, map_name) for map_name in source_names]
    )
    sources = {
        map_name: piece.astype(jnp.bfloat16) for map_name, piece in zip(source_names, pieces)
    }
    preacts = []
    totals = jnp.zeros((2, 2, 3, 8 * C0), jnp.float32)
    for operation in operations:
        preact = conv_forward(
            operation, sources[operation.source], kernel_piece(module_weights, operation)
        )
        preacts.append(preact)
        channels = operation.cout
        position = operation.position
        totals = totals.at[size_kind, 0, position, :channels].set(jnp.sum(preact, axis=(0, 1, 2)))
        totals = totals.at[size_kind, 1, position, :channels].set(
            jnp.sum(preact * preact, axis=(0, 1, 2))
        )
    return (to_canvas(preacts, jnp.float32), totals)


def forward_norm(
    branch_index,
    size_kind,
    phase_index,
    preact_canvas,
    totals,
    counts,
    module_gains,
    module_shifts,
    skip_canvas,
    message_buffer,
):
    operations = phase_operations(branch_index, phase_index)
    preacts = from_canvas(
        preact_canvas, [preact_dims(size_kind, operation) for operation in operations]
    )
    skip_map = from_canvas(skip_canvas, [map_dims(size_kind, branch_index, C0 << branch_index)])[0]
    produced = []
    for operation, preact in zip(operations, preacts):
        average, inverse_std = norm_terms(totals, counts, size_kind, operation)
        norm_slot = operation.slot
        channels = operation.cout
        normed = (preact - average) * inverse_std * module_gains[
            norm_slot, :channels
        ] + module_shifts[norm_slot, :channels]
        if operation.act == "silu":
            produced.append(jax.nn.silu(normed))
        elif operation.act == "res":
            produced.append(jax.nn.silu(normed + skip_map))
        else:
            message_buffer = message_buffer.at[operation.dest].set(
                to_slot(normed.astype(jnp.bfloat16))
            )
    return (to_canvas(produced, jnp.float32), message_buffer)


def receive_forward(branch_index, size_kind, top_canvas, received):
    channels = C0 << branch_index
    summed = from_canvas(top_canvas, [map_dims(size_kind, branch_index, channels)])[0]
    for sender in range(4):
        if sender < branch_index:
            summed = summed + from_slot(
                received[sender], map_dims(size_kind, branch_index, channels)
            ).astype(jnp.float32)
        elif sender > branch_index:
            coarse = from_slot(received[sender], map_dims(size_kind, sender, channels))
            summed = summed + upsample(coarse, 2 ** (sender - branch_index)).astype(jnp.float32)
    return (to_canvas([jax.nn.silu(summed)], jnp.float32), to_canvas([summed], jnp.float32))


def receive_backward(branch_index, size_kind, grad_canvas, summed_canvas):
    dims_here = map_dims(size_kind, branch_index, C0 << branch_index)
    upstream = from_canvas(grad_canvas, [dims_here])[0]
    summed = from_canvas(summed_canvas, [dims_here])[0]
    summed_grad = upstream * silu_slope(summed)
    buffer = jnp.zeros((4, MSG_ROWS, 128), jnp.bfloat16)
    for sender in range(4):
        if sender < branch_index:
            buffer = buffer.at[sender].set(to_slot(summed_grad.astype(jnp.bfloat16)))
        elif sender > branch_index:
            pooled = block_pool(summed_grad, 2 ** (sender - branch_index))
            buffer = buffer.at[sender].set(to_slot(pooled.astype(jnp.bfloat16)))
    return (to_canvas([summed_grad], jnp.float32), buffer)


def backward_stats(
    branch_index,
    size_kind,
    phase_index,
    dout_canvas,
    message_grads,
    preact_canvas,
    totals,
    counts,
    module_gains,
    module_shifts,
    skip_canvas,
):
    operations = phase_operations(branch_index, phase_index)
    preacts = from_canvas(
        preact_canvas, [preact_dims(size_kind, operation) for operation in operations]
    )
    producing = [operation for operation in operations if operation.act != "none"]
    output_grads = from_canvas(
        dout_canvas, [preact_dims(size_kind, operation) for operation in producing]
    )
    grads_by_name = {
        operation.output: piece for operation, piece in zip(producing, output_grads)
    }
    skip_map = from_canvas(skip_canvas, [map_dims(size_kind, branch_index, C0 << branch_index)])[0]
    upstreams = []
    skip_grads = []
    sums_local = jnp.zeros((2, 2, 3, 8 * C0), jnp.float32)
    for operation, preact in zip(operations, preacts):
        average, inverse_std = norm_terms(totals, counts, size_kind, operation)
        norm_slot = operation.slot
        channels = operation.cout
        centered = (preact - average) * inverse_std
        normed = centered * module_gains[norm_slot, :channels] + module_shifts[norm_slot, :channels]
        if operation.act == "silu":
            upstream = grads_by_name[operation.output] * silu_slope(normed)
        elif operation.act == "res":
            upstream = grads_by_name[operation.output] * silu_slope(normed + skip_map)
            skip_grads.append(upstream)
        else:
            upstream = from_slot(
                message_grads[operation.dest], preact_dims(size_kind, operation)
            ).astype(jnp.float32)
        upstreams.append(upstream)
        position = operation.position
        sums_local = sums_local.at[size_kind, 0, position, :channels].set(
            jnp.sum(upstream, axis=(0, 1, 2))
        )
        sums_local = sums_local.at[size_kind, 1, position, :channels].set(
            jnp.sum(upstream * centered, axis=(0, 1, 2))
        )
    return (to_canvas(upstreams, jnp.float32), sums_local, to_canvas(skip_grads, jnp.float32))


def backward_apply(
    branch_index,
    size_kind,
    phase_index,
    upstream_canvas,
    preact_canvas,
    totals,
    grad_totals,
    counts,
    source_canvas,
    module_weights,
    module_gains,
):
    operations = phase_operations(branch_index, phase_index)
    preacts = from_canvas(
        preact_canvas, [preact_dims(size_kind, operation) for operation in operations]
    )
    upstreams = from_canvas(
        upstream_canvas, [preact_dims(size_kind, operation) for operation in operations]
    )
    source_names = input_names(operations)
    source_list = [source_dims(branch_index, size_kind, map_name) for map_name in source_names]
    pieces = from_canvas(source_canvas, source_list)
    sources = {
        map_name: piece.astype(jnp.bfloat16) for map_name, piece in zip(source_names, pieces)
    }
    source_grads = {
        map_name: jnp.zeros(dims_entry, jnp.float32)
        for map_name, dims_entry in zip(source_names, source_list)
    }
    kernel_grads = []
    slot_count = module_gains.shape[0]
    gain_part = jnp.zeros((slot_count, 8 * C0), jnp.float32)
    shift_part = jnp.zeros((slot_count, 8 * C0), jnp.float32)
    for operation, preact, upstream in zip(operations, preacts, upstreams):
        average, inverse_std = norm_terms(totals, counts, size_kind, operation)
        cells_here = cell_total(counts, size_kind, operation.level)
        norm_slot = operation.slot
        channels = operation.cout
        position = operation.position
        centered = (preact - average) * inverse_std
        mean_upstream = grad_totals[size_kind, 0, position, :channels] / cells_here
        mean_cross = grad_totals[size_kind, 1, position, :channels] / cells_here
        preact_grad = (
            module_gains[norm_slot, :channels]
            * inverse_std
            * (upstream - mean_upstream - centered * mean_cross)
        )
        source_grad, kernel_grad = conv_backward(
            operation,
            sources[operation.source],
            kernel_piece(module_weights, operation),
            preact_grad.astype(jnp.bfloat16),
        )
        source_grads[operation.source] = source_grads[operation.source] + source_grad
        kernel_grads.append(kernel_grad.reshape(-1))
        gain_part = gain_part.at[norm_slot, :channels].set(
            grad_totals[0, 1, position, :channels] + grad_totals[1, 1, position, :channels]
        )
        shift_part = shift_part.at[norm_slot, :channels].set(
            grad_totals[0, 0, position, :channels] + grad_totals[1, 0, position, :channels]
        )
    phase_length = phase_lengths(C0, BLOCKS)[phase_index]
    if kernel_grads:
        joined = jnp.concatenate(kernel_grads)
        weight_part = jnp.pad(joined, (0, phase_length - joined.shape[0]))
    else:
        weight_part = jnp.zeros((phase_length,), jnp.float32)
    return (
        to_canvas([source_grads[map_name] for map_name in source_names], jnp.float32),
        weight_part,
        gain_part,
        shift_part,
    )


def on_device(features, weights, gains, shifts, cotangent, size_group):
    crop_shard = lax.axis_index("crops")
    shard_count = lax.axis_size("crops")
    crop_kind = size_group[crop_shard]
    large_count = jnp.sum(size_group).astype(jnp.float32)
    counts = jnp.stack([shard_count - large_count, large_count])
    case_index = lax.axis_index("branch") * 2 + crop_kind
    phase_total = 2 * BLOCKS + 3
    zero_canvas = jnp.zeros((ROWS, 128), jnp.float32)
    empty_buffer = jnp.zeros((4, MSG_ROWS, 128), jnp.bfloat16)

    def run_phase(function, statics, operands):
        branches_list = [
            partial(function, branch_index, size_kind, *statics)
            for branch_index in range(4)
            for size_kind in range(2)
        ]
        return lax.switch(case_index, branches_list, *operands)

    def statistics(local_totals):
        return lax.psum(local_totals, "crops")

    def module_forward(module, start_canvas, kept):
        module_weights = weights[0, module]
        module_gains = gains[0, module]
        module_shifts = shifts[0, module]
        record = SimpleNamespace(sources=[], preacts=[], totals=[])
        h_canvas = start_canvas
        u_canvas = zero_canvas
        chain_canvas = zero_canvas
        buffer = empty_buffer
        for phase_index in range(phase_total):
            if phase_index < 2 * BLOCKS:
                source = h_canvas if phase_index % 2 == 0 else u_canvas
            elif phase_index == 2 * BLOCKS:
                source = h_canvas
            else:
                source = chain_canvas
            preact, local_totals = run_phase(forward_conv, (phase_index,), (source, module_weights))
            global_totals = kept.totals[phase_index] if kept else statistics(local_totals)
            produced, buffer = run_phase(
                forward_norm,
                (phase_index,),
                (preact, global_totals, counts, module_gains, module_shifts, h_canvas, buffer),
            )
            record.sources.append(source)
            record.preacts.append(preact)
            record.totals.append(global_totals)
            if phase_index < 2 * BLOCKS:
                if phase_index % 2 == 0:
                    u_canvas = produced
                else:
                    h_canvas = produced
            else:
                chain_canvas = produced
        received = (
            kept.received
            if kept
            else jax.tree.map(
                lambda part, own: part.astype(own.dtype),
                lax.all_to_all(as_sent(buffer), "branch", split_axis=0, concat_axis=0, tiled=True),
                buffer,
            )
        )
        result, summed = run_phase(receive_forward, (), (h_canvas, received))
        record.summed = summed
        record.received = received
        return (result, record)

    checkpoints = [features[0].astype(jnp.float32)]
    first_records = []
    for module in range(MODULES):
        result, record = module_forward(module, checkpoints[-1], None)
        checkpoints.append(result)
        first_records.append(record)
    outputs = checkpoints[-1].astype(jnp.bfloat16)
    grad_canvas = cotangent[0].astype(jnp.float32)
    module_grads = [None] * MODULES
    gain_grads = [None] * MODULES
    shift_grads = [None] * MODULES
    for module in reversed(range(MODULES)):
        kept = None
        unused_result, record = module_forward(module, checkpoints[module], kept)
        module_module_weights = weights[0, module]
        module_module_gains = gains[0, module]
        module_module_shifts = shifts[0, module]
        summed_grad, back_buffer = run_phase(receive_backward, (), (grad_canvas, record.summed))
        message_grads = jax.tree.map(
            lambda part, own: part.astype(own.dtype),
            lax.all_to_all(as_sent(back_buffer), "branch", split_axis=0, concat_axis=0, tiled=True),
            back_buffer,
        )
        top_grad = summed_grad
        chain_grad = zero_canvas
        u_grad = zero_canvas
        pending_skip = zero_canvas
        weight_parts = [None] * phase_total
        gain_total = jnp.zeros(gains.shape[2:], jnp.float32)
        shift_total = jnp.zeros(gains.shape[2:], jnp.float32)
        for module_phase_index in reversed(range(phase_total)):
            if module_phase_index >= 2 * BLOCKS:
                output_grad = chain_grad
                skip_canvas = zero_canvas
            elif module_phase_index % 2 == 1:
                output_grad = top_grad
                skip_canvas = record.sources[module_phase_index - 1]
            else:
                output_grad = u_grad
                skip_canvas = zero_canvas
            module_preact = record.preacts[module_phase_index]
            totals = record.totals[module_phase_index]
            upstream, module_local_totals, skip_grad = run_phase(
                backward_stats,
                (module_phase_index,),
                (
                    output_grad,
                    message_grads,
                    module_preact,
                    totals,
                    counts,
                    module_module_gains,
                    module_module_shifts,
                    skip_canvas,
                ),
            )
            grad_totals = lax.psum(module_local_totals, "crops")
            source_grad, weight_parts[module_phase_index], gain_part, shift_part = run_phase(
                backward_apply,
                (module_phase_index,),
                (
                    upstream,
                    module_preact,
                    totals,
                    grad_totals,
                    counts,
                    record.sources[module_phase_index],
                    module_module_weights,
                    module_module_gains,
                ),
            )
            gain_total = gain_total + gain_part
            shift_total = shift_total + shift_part
            if module_phase_index > 2 * BLOCKS:
                chain_grad = source_grad
            elif module_phase_index == 2 * BLOCKS:
                top_grad = top_grad + source_grad
            elif module_phase_index % 2 == 1:
                u_grad = source_grad
                pending_skip = skip_grad
            else:
                top_grad = source_grad + pending_skip
        joined = jnp.concatenate(weight_parts)
        weight_grad = jnp.pad(joined, (0, weights.shape[2] - joined.shape[0]))
        grad_canvas, weight_grad, gain_grads[module], shift_grads[module] = (
            top_grad,
            weight_grad,
            gain_total,
            shift_total,
        )
        module_grads[module] = weight_grad
    weight_out = lax.psum_scatter(jnp.stack(module_grads), "crops", scatter_dimension=1, tiled=True)
    share = gains.shape[3] // shard_count
    gain_out = lax.dynamic_slice_in_dim(jnp.stack(gain_grads), crop_shard * share, share, axis=2)
    shift_out = lax.dynamic_slice_in_dim(jnp.stack(shift_grads), crop_shard * share, share, axis=2)
    return (outputs[None], grad_canvas[None], weight_out[None], gain_out[None], shift_out[None])


LANES = 128
SLOTS = 8
MASKS = 7
DOWN = (((1,), (0,)), ((), ()))
ACROSS = (((1,), (1,)), ((), ()))
ALONG = (((0,), (0,)), ((), ()))


def unit_table(k):
    operations = weighted_plan(k, C0, BLOCKS)
    planes = 8 >> k
    channels = C0 << k
    units = {}
    stat = 0

    def add(name, kind, source, lanes_in, planes_in, planes_out, members):
        nonlocal stat
        segs = []
        tile = 0
        for operation, lanes, chain in members:
            cout = operation.cout
            level = operation.level if operation.taps == 3 else operation.dest
            segs.append(
                SimpleNamespace(
                    slot=operation.slot,
                    off=operation.offset // LANES,
                    cin=operation.cin,
                    cout=cout,
                    taps=operation.taps,
                    tile=tile,
                    tiles=lanes // LANES,
                    blocks=max(1, (8 >> level)),
                    dest=operation.dest,
                    act=operation.act,
                    chain=chain,
                    up=k - operation.dest if operation.taps == 1 else 0,
                )
            )
            tile += lanes // LANES
        rows = {"s1": (384, 384, 512, 768)[k], "s2": lanes_in + LANES, "p1": 256}[kind]
        units[name] = SimpleNamespace(
            name=name,
            kind=kind,
            source=source,
            lanes_in=lanes_in,
            blocks_in=planes_in,
            planes_in=planes_in,
            planes=planes_out,
            segs=segs,
            tiles=tile,
            rows=rows,
            stat=stat,
            depth=1 if kind == "p1" else 3,
        )
        stat += tile

    add("a", "s1", "h", 256, planes, planes, [(operations[0], 256, None)])
    add("b", "s1", "u", 256, planes, planes, [(operations[1], 256, None)])
    ups = [operation for operation in operations if operation.taps == 1]
    if ups:
        add("u", "p1", "t", 256, planes, planes, [(operation, 256, None) for operation in ups])
    firsts, chains = [], {}
    for target in range(k + 1, 4):
        steps = [
            operation
            for operation in operations
            if operation.taps == 3 and operation.stride == 2
        ]
        start = sum(i - k for i in range(k + 1, target))
        chains[target] = steps[start : start + target - k]
        if target == k + 1:
            firsts.append((chains[target][0], 256, None))
        else:
            firsts.append((chains[target][0], LANES, "c1" if target == k + 2 else "c2"))
    if firsts:
        add("d", "s2", "t", 256, planes, planes // 2, firsts)
    if k <= 1:
        add("e", "s2", "c1", LANES, planes // 2, planes // 4, [(chains[k + 2][1], 256, None)])
    if k == 0:
        add("f", "s2", "c2", LANES, planes // 2, planes // 4, [(chains[3][1], LANES, "c3")])
        add("g", "s2", "c3", LANES, planes // 4, planes // 8, [(chains[3][2], 256, None)])
    return units


def links(k, unit, seg):
    cin = seg.cin
    count_in, count_out = unit.blocks_in, seg.blocks
    found = []
    if unit.kind == "p1":
        for plane in range(count_in):
            wide = 1 << seg.up
            found.append((plane * cin, 0, set(range(plane * wide, plane * wide + wide))))
        return found
    if unit.kind == "s1" and k == 3:
        return [(256 * tap, tap, {0}) for tap in range(3)]
    stride = 1 if unit.kind == "s1" else 2
    for plane in range(count_in):
        for tap in range(3):
            at = plane - tap + 1
            if at % stride == 0 and 0 <= at // stride < count_out:
                found.append((plane * cin, tap, {at // stride}))
    if stride == 1:
        found.append((256, 2, {count_out - 1}))
        found.append((unit.rows - cin, 0, {0}))
    else:
        lanes_in = unit.lanes_in
        found.append((lanes_in + (count_in - 1) * cin - (lanes_in - LANES), 0, {0}))
    return found


def message_slot(k, other):
    return sum(2 * (8 >> max(k, before)) for before in range(other) if before != k)


def log2(value):
    return value.bit_length() - 1


def sigmoid_of(value):
    return 0.5 * jnp.tanh(0.5 * value) + 0.5


def silu_of(value):
    return value * sigmoid_of(value)


def slope_of(value):
    sigmoid = sigmoid_of(value)
    return sigmoid * (1.0 + value * (1.0 - sigmoid))


def planes_loop(count, body, turns=1):
    def step(index, carry):
        for turn in range(turns):
            body(index * turns + turn)
        return carry

    turns = min(turns, count)
    if count == turns:
        for index in range(count):
            body(index)
    else:
        lax.fori_loop(0, count // turns, step, 0)


def planes_sum(count, body, initial, turns=1):
    def step(index, carry):
        for turn in range(turns):
            carry = body(index * turns + turn, carry)
        return carry

    turns = min(turns, count)
    if count == turns:
        return step(0, initial)
    return lax.fori_loop(0, count // turns, step, initial)


def partial_sum(value):
    rows = value.shape[0]
    return jnp.sum(value.reshape(rows // 8, 8, value.shape[1]), axis=0)


class Planes:
    def __init__(self, mode, tiles, planes, masks, rows, main, edge=None, right=None, narrow=False):
        self.narrow, self.pending = narrow, {}
        self.mode, self.tiles, self.planes = mode, tiles, planes
        self.masks, self.rows = masks, rows
        self.main, self.edge, self.right = main, edge, right
        self.base = 1 if mode in ("s1", "wide", "s2") else 0
        extra = {"s1": 2, "wide": 2, "s2": 1, "dz2": 1, "p": 0}[mode]
        self.span = planes + extra
        self.unit = tiles * self.span

    def at(self, m, tile, plane):
        return m * self.unit + tile * self.span + plane + self.base

    def edge_at(self, m, tile, plane):
        if self.mode == "s2" or self.narrow:
            return m * self.span + plane + self.base
        return self.at(m, tile, plane)

    def from_left(self, value):
        return pltpu.roll(value, 1, 0) * self.masks[1]

    def from_right(self, value):
        return pltpu.roll(value, self.rows - 1, 0) * self.masks[2]

    def store(self, m, tile, plane, value):
        self.put(m, tile, plane, value)
        if isinstance(plane, int):
            if plane == self.planes - 1:
                self.put_above(m, tile, value)
            if plane == 0:
                self.put_below(m, tile, value)

    def put(self, m, tile, plane, value):
        where = self.at(m, tile, plane)
        self.main[where] = value.astype(jnp.bfloat16)
        if self.mode == "s1":
            side = self.from_right(value) if tile == 0 else self.from_left(value)
            if not self.narrow:
                self.edge[where] = side.astype(jnp.bfloat16)
            elif tile == 0:
                self.pending[plane if isinstance(plane, int) else self.span] = side
            else:
                lane = lax.broadcasted_iota(jnp.int32, side.shape, 1)
                other = self.pending.pop(plane if isinstance(plane, int) else self.span)
                side = jnp.where(lane < LANES // 2, other, side)
                self.edge[self.edge_at(m, tile, plane)] = side.astype(jnp.bfloat16)
        elif self.mode == "wide":
            self.edge[where] = self.from_left(value).astype(jnp.bfloat16)
            self.right[where] = self.from_right(value).astype(jnp.bfloat16)
        elif self.mode == "s2":
            if tile == self.tiles - 1:
                self.edge[self.edge_at(m, tile, plane)] = self.from_left(value).astype(jnp.bfloat16)
        elif self.mode == "dz2":
            self.edge[where] = self.from_right(value).astype(jnp.bfloat16)

    def put_above(self, m, tile, last):
        if self.mode in ("s1", "wide", "s2"):
            above = pltpu.roll(last, 6, 0) * self.masks[3] + pltpu.roll(last, 3, 0) * self.masks[4]
            self.put(m, tile, -1, above)

    def put_below(self, m, tile, first):
        if self.mode in ("s1", "wide", "dz2"):
            rows = self.rows
            below = (
                pltpu.roll(first, rows - 6, 0) * self.masks[5]
                + pltpu.roll(first, rows - 3, 0) * self.masks[6]
            )
            self.put(m, tile, self.planes, below)

    def close(self, m):
        for tile in range(self.tiles):
            last = self.main[self.at(m, tile, self.planes - 1)].astype(jnp.float32)
            self.put_above(m, tile, last)
        for tile in range(self.tiles):
            first = self.main[self.at(m, tile, 0)].astype(jnp.float32)
            self.put_below(m, tile, first)


class Branch:
    def __init__(self, k, rows, large, small, share, refs, masks, core):
        self.k, self.rows, self.refs, self.masks = k, rows, refs, masks
        self.units = unit_table(k)
        self.planes = 8 >> k
        self.core = core
        self.large, self.small, self.count = large, small, large + small
        self.cells = (small * (SH // 8) * (SW // 8), large * (LH // 8) * (LW // 8))
        self.quarter = lax.axis_index("crops") // 2
        self.share = share
        r = refs
        make = partial(Planes, masks=masks, rows=rows)
        make_one = partial(make, narrow=k <= 1)
        one = "wide" if k == 3 else "s1"
        self.maps = dict(
            h=make_one(one, 2, self.planes, main=r.hC, edge=r.hE, right=r.hR),
            u=make_one(one, 2, self.planes, main=r.uC, edge=r.uE, right=r.uR),
            t=make("p" if k == 3 else "s2", 2, self.planes, main=r.tC, edge=r.tE),
        )
        if k <= 1:
            self.maps["c1"] = make("s2", 1, self.planes // 2, main=r.c1C, edge=r.c1E)
        if k == 0:
            self.maps["c2"] = make("s2", 1, 4, main=r.c2C, edge=r.c2E)
            self.maps["c3"] = make("s2", 1, 2, main=r.c3C, edge=r.c3E)
        self.grads = dict(t=r.gt, u=r.gu, c1=r.gc1, c2=r.gc2, c3=r.gc3)

    def lane_block(self, shape, cout):
        lanes = lax.broadcasted_iota(jnp.int32, shape, 1)
        return lanes >> log2(cout)

    def keep(self, value, cout, which):
        count = LANES // cout
        if len(which) == count:
            return value
        block = self.lane_block(value.shape, cout)
        mask = block == which[0]
        for entry in which[1:]:
            mask = mask | (block == entry)
        return jnp.where(mask, value, 0.0)

    def spread(self, value, cout):
        shift = LANES // 2
        while shift >= cout:
            value = value + pltpu.roll(value, shift, 1)
            shift //= 2
        return value

    def local_blocks(self, seg, tile, wanted):
        count = LANES // seg.cout
        return [q for q in range(count) if (tile * count + q) % seg.blocks in wanted]


    def segments(self):
        return [(unit, seg) for unit in self.units.values() for seg in unit.segs]

    def pieces(self):
        found, place = [], 0
        for index, (unit, seg) in enumerate(self.segments()):
            count = 2 * seg.taps**2 * seg.cin * seg.cout // LANES
            if self.k < 3:
                found.append((index, 0, count, place, index))
                place += count
            else:
                for d in range(unit.depth):
                    slot = len(found) % 3
                    found.append((index, d, count // unit.depth, slot * 3072, slot))
        return found

    def fetch(self, at):
        r = self.refs
        index, d, count, place, sem = self.pieces()[at]
        _, seg = self.segments()[index]
        return pltpu.make_async_copy(
            r.w.at[pl.ds(2 * seg.off + d * count, count)],
            r.raw.at[pl.ds(place, count)],
            r.wsem.at[sem],
        )

    def fetch_first(self):
        for at in range(len(self.pieces()) if self.k < 3 else 3):
            self.fetch(at).start()

    def expand(self, index):
        unit, seg = self.segments()[index]
        pieces = self.pieces()
        mine = [at for at, piece in enumerate(pieces) if piece[0] == index]
        if self.k < 3:
            (at,) = mine
            self.fetch(at).wait()
            count = pieces[at][2] // unit.depth
            planes_loop(
                unit.depth,
                lambda d: self.expand_row(unit, seg, d, count, pieces[at][3] + d * count),
            )
        else:
            for d, at in enumerate(mine):
                self.fetch(at).wait()
                self.expand_row(unit, seg, d, pieces[at][2], pieces[at][3])
                if at + 3 < len(pieces):
                    self.fetch(at + 3).start()
        for m in range(MODULES):
            self.spread_tables(m, unit, seg)

    def expand_row(self, unit, seg, d, count, place):
        r = self.refs
        chunk = math.gcd(count, 384)
        wf, rep = r.work, r.rep

        def widen(step):
            at = pl.multiple_of(step * chunk, 16)
            value = r.raw[pl.ds(pl.multiple_of(place + at, 16), chunk)].astype(jnp.float32)
            wf[pl.ds(at, chunk)] = value

        planes_loop(count // chunk, widen)
        count = count // MODULES
        depth, cin, cout = unit.depth, seg.cin, seg.cout
        target = getattr(r, "T" + unit.name)
        twice = unit.kind == "s1" and self.k < 3
        across = getattr(r, "T" + unit.name + unit.name) if twice else None
        by_row = {}
        for row, tap, wanted in links(self.k, unit, seg):
            by_row.setdefault(row, []).append((tap, wanted))

        def module(m):
            if cout < LANES:
                ratio = LANES // cout
                flat = wf[pl.ds(m, count, stride=2)]
                for part in range(ratio):
                    rep[pl.ds(part, count, stride=ratio)] = self.spread(
                        self.keep(flat, cout, [part]), cout
                    )

            def tap_rows(tap, tile):
                if cout < LANES:
                    return rep[tap * cin : (tap + 1) * cin]
                if cout == LANES:
                    return wf[pl.ds(m + tap * (2 * cin), cin, stride=2)]
                return wf[pl.ds(m + tap * (4 * cin) + 2 * tile, cin, stride=4)]

            def place(goal, taps_at, width, column, tile):
                made = {}
                for row in range(0, unit.rows, cin):
                    key = []
                    for tap, wanted in by_row.get(row, []):
                        local = self.local_blocks(seg, tile, wanted) if width <= LANES else [0]
                        if local:
                            key.append((tap, tuple(local)))
                    key = tuple(key)
                    if key not in made:
                        total = None
                        for tap, local in key:
                            piece = taps_at[tap]
                            if width <= LANES:
                                piece = self.keep(piece, width, local)
                            total = piece if total is None else total + piece
                        if total is None:
                            total = jnp.zeros((cin, LANES), jnp.float32)
                        made[key] = total.astype(jnp.bfloat16)
                    goal[m * depth + d, row : row + cin, column : column + LANES] = made[key]

            width = 3 if seg.taps == 3 else 1
            for tile in range(seg.tiles):
                if tile == 0 or cout > LANES:
                    taps_at = [tap_rows(tap, tile) for tap in range(width)]
                place(target, taps_at, cout, (seg.tile + tile) * LANES, tile)
            if not twice:
                return
            turned = []
            if cin == LANES:
                turned = [jnp.transpose(tap_rows(tap, 0)) for tap in range(3)]
            else:
                both = jnp.transpose(rep[0 : -(-3 * cin // LANES) * LANES])
                for tap in range(3):
                    first = tap * cin // LANES * LANES
                    value = both[0:cin, first : first + LANES]
                    value = self.keep(value, cin, [tap * cin % LANES // cin])
                    turned.append(self.spread(value, cin))
            for tile in range(2):
                place(across, turned[::-1], cin, tile * LANES, tile)

        planes_loop(MODULES, module)


    def parts(self, unit, source):
        if unit.kind == "p1":
            return [(source.main, range(2), source.at)]
        if source.mode == "wide":
            return [
                (source.edge, range(2), source.at),
                (source.main, range(2), source.at),
                (source.right, range(2), source.at),
            ]
        if unit.kind == "s1":
            tiles = [0] if source.narrow else range(2)
            return [(source.main, range(2), source.at), (source.edge, tiles, source.edge_at)]
        last = source.tiles - 1
        return [
            (source.main, range(source.tiles), source.at),
            (source.edge, [last], source.edge_at),
        ]

    def rows_of(self, unit, part, m, d, first, count):
        ref, tiles, at = part
        pieces = []
        for tile in tiles:
            if unit.kind == "s2":
                rows = [ref[at(m, tile, 2 * (first + q) + d - 1)] for q in range(count)]
                pieces.append(rows[0] if count == 1 else jnp.concatenate(rows, axis=0))
            else:
                shift = d - 1 if unit.kind == "s1" else 0
                pieces.append(
                    ref[pl.ds(at(m, tile, first + shift), count)].reshape(count * self.rows, LANES)
                )
        return pieces

    def conv(self, m, unit):
        r = self.refs
        source = self.maps[unit.source]
        target = getattr(r, "T" + unit.name)
        z = getattr(r, "z" + unit.name)
        planes, tiles, depth = unit.planes, unit.tiles, unit.depth
        chunk = min(planes, 4 if tiles <= 2 else 2)
        lanes = tiles * LANES

        def body(step, sums):
            first = step * chunk
            pieces = []
            for d in range(depth):
                for part in self.parts(unit, source):
                    pieces += self.rows_of(unit, part, m, d, first, chunk)
            left = jnp.concatenate(pieces, axis=1)
            right = target[pl.ds(m * depth, depth), 0 : unit.rows, 0:lanes]
            right = right.reshape(depth * unit.rows, lanes)
            result = lax.dot_general(left, right, DOWN, preferred_element_type=jnp.float32)
            for tile in range(tiles):
                block = result[:, tile * LANES : (tile + 1) * LANES]
                z[pl.ds(m * tiles * planes + tile * planes + first, chunk)] = block.reshape(
                    chunk, self.rows, LANES
                )
            return (sums[0] + partial_sum(result), sums[1] + partial_sum(result * result))

        zero = jnp.zeros((8, lanes), jnp.float32)
        sums = planes_sum(planes // chunk, body, (zero, zero), 2)
        for seg in unit.segs:
            scale = self.per_cell(unit, seg)
            totals = self.fold(seg, sums)
            self.norm_rows(m, unit, seg, totals, scale)

    def per_cell(self, unit, seg):
        blocks = seg.tiles * LANES // seg.cout
        small, large = self.cells
        count = unit.planes * blocks
        return jnp.where(self.core == 0, 1.0 / (large * count), 1.0 / (small * count)).astype(
            jnp.float32
        )

    def fold(self, seg, sums):
        first = seg.tile
        found = []
        for value in sums:
            tiles = [
                value[:, (first + t) * LANES : (first + t + 1) * LANES] for t in range(seg.tiles)
            ]
            if seg.cout <= LANES:
                total = tiles[0]
                for tile in tiles[1:]:
                    total = total + tile
                total = jnp.sum(self.spread(total, seg.cout), axis=0, keepdims=True)
                found.append([total] * seg.tiles)
            else:
                found.append([jnp.sum(tile, axis=0, keepdims=True) for tile in tiles])
        return found

    def table_row(self, ref, m, seg, tile):
        slot = seg.slot
        if seg.cout > LANES:
            return ref[m, slot : slot + 1, tile * LANES : (tile + 1) * LANES]
        row = jnp.broadcast_to(ref[m, slot : slot + 1, 0:LANES], (8, LANES))
        if seg.cout < LANES:
            row = self.spread(self.keep(row, seg.cout, [0]), seg.cout)
        return row[0:1]

    def norm_rows(self, m, unit, seg, totals, scale):
        st = self.refs.st
        for tile in range(seg.tiles):
            average = totals[0][tile] * scale
            variance = totals[1][tile] * scale - average * average
            inverse = lax.rsqrt(variance + EPS)
            where = m * STATS + unit.stat + seg.tile + tile
            factor = st[where, 4:5] * inverse
            st[where, 0:1] = average
            st[where, 1:2] = inverse
            st[where, 2:3] = factor
            st[where, 3:4] = st[where, 5:6] - average * factor

    def spread_tables(self, m, unit, seg):
        st = self.refs.st
        for tile in range(seg.tiles):
            where = m * STATS + unit.stat + seg.tile + tile
            st[where, 4:5] = self.table_row(self.refs.gains, m, seg, tile)
            st[where, 5:6] = self.table_row(self.refs.shifts, m, seg, tile)

    def normed(self, m, unit, tile, plane):
        st = self.refs.st
        z = getattr(self.refs, "z" + unit.name)
        where = m * STATS + unit.stat + tile
        value = z[m * unit.tiles * unit.planes + tile * unit.planes + plane]
        return value * st[where, 2:3] + st[where, 3:4]

    def apply_a(self, m):
        unit, u = self.units["a"], self.maps["u"]

        def body(plane):
            for tile in range(2):
                value = silu_of(self.normed(m, unit, tile, plane)) * self.masks[0]
                u.store(m, tile, plane, value)

        planes_loop(self.planes, body, TURNS)

    def apply_b(self, m):
        unit, top = self.units["b"], self.maps["t"]
        hf, s = self.refs.hf, self.refs.s

        def body(plane):
            for tile in range(2):
                where = m * 2 * self.planes + tile * self.planes + plane
                value = silu_of(self.normed(m, unit, tile, plane) + hf[where]) * self.masks[0]
                s[where] = value
                top.store(m, tile, plane, value)

        planes_loop(self.planes, body, TURNS)

    def apply_rest(self, m, unit):
        sb = self.refs.sb
        for seg in unit.segs:
            chain = self.maps[seg.chain] if seg.chain else None

            def body(plane):
                for tile in range(seg.tiles):
                    value = self.normed(m, unit, seg.tile + tile, plane)
                    if chain is not None:
                        chain.store(m, tile, plane, silu_of(value) * self.masks[0])
                    else:
                        at = message_slot(self.k, seg.dest) + tile * unit.planes + plane
                        sb[at] = value.astype(jnp.bfloat16)

            planes_loop(unit.planes, body, TURNS)
            if chain is None:
                self.message(m, seg.dest).start()

    def message(self, e, other):
        count = 2 * (8 >> max(self.k, other))
        r = self.refs
        return pltpu.make_async_remote_copy(
            src_ref=r.sb.at[pl.ds(message_slot(self.k, other), count)],
            dst_ref=r.rb.at[pl.ds(e * 16 + message_slot(other, self.k), count)],
            send_sem=r.ssem.at[e * 4 + other],
            recv_sem=r.rsem.at[e * 4 + self.k],
            device_id=dict(branch=other),
            device_id_type=pl.DeviceIdType.MESH,
        )

    def arrived(self, e, other):
        count = 2 * (8 >> max(self.k, other))
        r = self.refs
        at = message_slot(self.k, other)
        return pltpu.make_async_remote_copy(
            src_ref=r.sb.at[pl.ds(at, count)],
            dst_ref=r.rb.at[pl.ds(e * 16 + at, count)],
            send_sem=r.ssem.at[e * 4 + other],
            recv_sem=r.rsem.at[e * 4 + other],
            device_id=dict(branch=other),
            device_id_type=pl.DeviceIdType.MESH,
        )

    def others(self):
        return [other for other in range(4) if other != self.k]

    def sent(self, e):
        for other in self.others():
            self.message(e, other).wait_send()

    def receive(self, m):
        r = self.refs
        s, rb, hf, out = r.s, r.rb, r.hf, r.outs
        h = self.maps["h"]

        def total_at(tile, plane):
            where = m * 2 * self.planes + tile * self.planes + plane
            total = s[where]
            for other in self.others():
                count = 8 >> max(self.k, other)
                at = plane >> max(0, other - self.k)
                slot = m * 16 + message_slot(self.k, other) + tile * count + at
                total = total + rb[slot].astype(jnp.float32)
            s[where] = total
            return silu_of(total) * self.masks[0]

        def onward(plane):
            for tile in range(2):
                value = total_at(tile, plane)
                hf[(2 + tile) * self.planes + plane] = value
                h.store(1, tile, plane, value)

        def finish(plane):
            for tile in range(2):
                out[tile * self.planes + plane] = total_at(tile, plane).astype(jnp.bfloat16)

        @pl.when(m + 1 < MODULES)
        def _():
            planes_loop(self.planes, onward, TURNS)

        @pl.when(m + 1 == MODULES)
        def _():
            planes_loop(self.planes, finish, TURNS)

    def take_feature(self, tile, plane, value):
        self.refs.hf[tile * self.planes + plane] = value
        self.maps["h"].store(0, tile, plane, value)

    def take_cotangent(self, tile, plane, value):
        self.refs.gin[tile * self.planes + plane] = value

    def member(self, kind, order):
        kinds = self.refs.kinds
        found, before = jnp.int32(0), jnp.int32(0)
        for at in range(self.count):
            same = kinds[at] == kind
            found = jnp.where(same & (before == order), at, found)
            before = before + same.astype(jnp.int32)
        return found

    def order(self, device):
        kinds = self.refs.kinds
        kind = kinds[device]
        before = jnp.int32(0)
        for at in range(self.count):
            before = before + ((kinds[at] == kind) & (at < device)).astype(jnp.int32)
        return before

    def unpack(self, t, consume):
        r = self.refs
        work, rows, planes = r.work, self.rows, self.planes
        full = SH * SW * C0 // LANES
        gath = r.gathc if t else r.gathx

        @pl.when(self.core == 0)
        def _():
            for at in range(self.large):
                block = gath[self.member(1, at)]
                work[at * ROWS : (at + 1) * ROWS] = block.astype(jnp.float32)

        @pl.when(self.core == 1)
        def _():
            for at in range(self.small):
                block = gath[self.member(0, at), 0:full]
                work[at * full : (at + 1) * full] = block.astype(jnp.float32)
            work[self.small * full : self.large * ROWS] = jnp.zeros(
                (self.large * ROWS - self.small * full, LANES), jnp.float32
            )

        deep = self.large * ROWS // 2
        right = jnp.concatenate([work[pl.ds(j, deep, stride=2)] for j in range(2)], axis=1)
        right = right.astype(jnp.bfloat16)
        cells = Cells(self.core, (rows, LANES), self.small, self.large)
        base = cells.crop * cells.pick(ROWS // 2, full // 2)
        base = base + cells.along * (planes * cells.wide) + cells.across
        base = jnp.where(cells.valid, base, -(1 << 20))
        lane = lax.broadcasted_iota(jnp.int32, (rows, LANES), 1)
        chunk = min(planes, 4)

        def body(step):
            pieces = []
            for q in range(chunk):
                goal = base + (step * chunk + q) * cells.wide
                pieces.append(one_hot(goal, lane, deep))
            left = pieces[0] if chunk == 1 else jnp.concatenate(pieces, axis=0)
            result = lax.dot_general(left, right, DOWN, preferred_element_type=jnp.float32)
            for q in range(chunk):
                for tile in range(2):
                    value = result[q * rows : (q + 1) * rows, tile * LANES : (tile + 1) * LANES]
                    consume(tile, step * chunk + q, value)

        planes_loop(planes // chunk, body)

    def pack_size(self):
        return 48 * self.planes, -(-self.planes * self.rows // LANES) * LANES

    def plan_pack(self):
        r = self.refs
        high, deep = self.pack_size()
        planes = self.planes
        q = lax.broadcasted_iota(jnp.int32, (high, LANES), 0)
        lane = lax.broadcasted_iota(jnp.int32, (high, LANES), 1)
        wide, tall = jnp.where(self.core == 0, 6, 3), jnp.where(self.core == 0, 8, 4)
        cell = jnp.where(self.core == 0, (q * 43691) >> 18, (q * 43691) >> 17)
        across = q - cell * wide
        plane = cell & (planes - 1)
        along = cell >> log2(planes)
        base = plane * self.rows + along * wide + across
        base = jnp.where(along < tall, base, -(1 << 20))
        shard = lax.axis_index("crops")
        for at, device in enumerate((shard, shard + 1 - 2 * self.core)):
            goal = base + self.order(device) * (wide * tall)
            r.hot[at, 0:high, 0:deep] = one_hot(goal, lane, deep)

    def pack(self, units, put, after=None):
        high, deep = self.pack_size()
        right = jnp.concatenate([units(tile) for tile in range(2)], axis=1)
        short = deep - right.shape[0]
        parts = [right.astype(jnp.bfloat16)]
        if right.dtype == jnp.float32:
            parts.append((right - parts[0].astype(jnp.float32)).astype(jnp.bfloat16))
        if short:
            empty = jnp.zeros((short, 2 * LANES), jnp.bfloat16)
            parts = [jnp.concatenate([part, empty], axis=0) for part in parts]
        for at in (1, 0):
            total = None
            for part in parts:
                piece = lax.dot_general(
                    self.refs.hot[at, 0:high, 0:deep],
                    part,
                    DOWN,
                    preferred_element_type=jnp.float32,
                )
                total = piece if total is None else total + piece
            for tile in range(2):
                put(at, pl.ds(tile, high, stride=2), total[:, tile * LANES : (tile + 1) * LANES])
            if at and after is not None:
                after()

    def pack_outputs(self):
        r = self.refs
        high = 2 * self.pack_size()[0]

        def put(at, where, value):
            r.work[pl.ds(at * ROWS + where.start, where.size, stride=2)] = value

        def units(tile):
            block = r.outs[tile * self.planes : (tile + 1) * self.planes]
            return block.reshape(self.planes * self.rows, LANES)

        self.pack(units, put)
        for at in range(2):
            r.blocks[at, 0:high] = r.work[at * ROWS : at * ROWS + high].astype(jnp.bfloat16)
            if high < ROWS:
                r.blocks[at, high:ROWS] = jnp.zeros((ROWS - high, LANES), jnp.bfloat16)

    def pack_gradient(self, after):
        r = self.refs
        high = 2 * self.pack_size()[0]

        def put(at, where, value):
            r.slopes[at, where] = value

        def units(tile):
            block = r.gin[tile * self.planes : (tile + 1) * self.planes]
            return block.reshape(self.planes * self.rows, LANES)

        if high < ROWS:
            for at in range(2):
                r.slopes[at, high:ROWS] = jnp.zeros((ROWS - high, LANES), jnp.float32)
        self.pack(units, put, after)

    def forward(self, m, gather):
        def also(module, step):
            pl.when(m == module)(lambda: gather.step(1, step))

        self.conv(m, self.units["a"])
        self.apply_a(m)
        self.conv(m, self.units["b"])
        self.apply_b(m)
        also(1, 2)

        @pl.when(m > 0)
        def _():
            self.sent(m - 1)

        for name in ("d", "u", "e", "f", "g"):
            if name in self.units:
                self.conv(m, self.units[name])
                self.apply_rest(m, self.units[name])
        also(0, 1)
        also(1, 3)

        @pl.when(m == MODULES - 1)
        def _():
            gather.collect(1)
            self.unpack(1, self.take_cotangent)

        for other in self.others():
            self.arrived(m, other).wait_recv()
        self.receive(m)


    def send_back(self, m):
        r = self.refs
        s, gin, gt, sb = r.s, r.gin, r.gt, r.sb
        e = MODULES + m

        def body(plane):
            for tile in range(2):
                at = tile * self.planes + plane
                value = gin[at] * slope_of(s[m * 2 * self.planes + at])
                gt[at] = value
                for other in range(self.k):
                    sb[message_slot(self.k, other) + at] = value.astype(jnp.bfloat16)

        planes_loop(self.planes, body, TURNS)
        for other in reversed(self.others()):
            if other > self.k:
                count = 8 >> other
                wide = 1 << (other - self.k)

                def pool(plane):
                    for tile in range(2):
                        total = gt[tile * self.planes + plane * wide]
                        for step in range(1, wide):
                            total = total + gt[tile * self.planes + plane * wide + step]
                        slot = message_slot(self.k, other) + tile * count + plane
                        sb[slot] = total.astype(jnp.bfloat16)

                planes_loop(count, pool, TURNS)
            self.message(e, other).start()

    def back_unit(self, m, unit):
        r = self.refs
        st, dyb, z = r.st, r.dyb, getattr(r, "z" + unit.name)
        name, planes, tiles = unit.name, unit.planes, unit.tiles
        e = MODULES + m
        sums = {}

        def upstream(seg, tile, plane, normed):
            at = tile * planes + plane
            if name == "b":
                hf = r.hf[m * 2 * planes + at]
                value = r.gt[at] * slope_of(normed + hf)
                r.gin[at] = value
                return value
            if name == "a":
                return r.gu[at] * slope_of(normed)
            if seg.chain:
                return self.grads[seg.chain][at] * slope_of(normed)
            return r.rb[e * 16 + message_slot(self.k, seg.dest) + at].astype(jnp.float32)

        for seg in unit.segs:

            def body(plane, carry):
                result = []
                for tile in range(seg.tiles):
                    at = (seg.tile + tile) * planes + plane
                    where = m * STATS + unit.stat + seg.tile + tile
                    value = z[m * tiles * planes + at]
                    normed = value * st[where, 2:3] + st[where, 3:4]
                    dy = upstream(seg, tile, plane, normed)
                    dyb[at] = dy
                    zhat = (value - st[where, 0:1]) * st[where, 1:2]
                    result.append(carry[2 * tile] + partial_sum(dy))
                    result.append(carry[2 * tile + 1] + partial_sum(dy * zhat))
                return tuple(result)

            zero = jnp.zeros((8, LANES), jnp.float32)
            found = planes_sum(planes, body, (zero,) * (2 * seg.tiles), TURNS)
            pair = [
                jnp.concatenate([found[2 * tile + which] for tile in range(seg.tiles)], axis=1)
                for which in range(2)
            ]
            plain = SimpleNamespace(**vars(seg))
            plain.tile = 0
            totals = self.fold(plain, pair)
            self.table_grads(m, seg, totals)
            sums[seg.slot] = totals
        dz = self.dz_planes(unit)
        for seg in unit.segs:
            scale = self.per_cell(unit, seg)
            totals = sums[seg.slot]

            def apply(plane):
                for tile in range(seg.tiles):
                    at = (seg.tile + tile) * planes + plane
                    where = m * STATS + unit.stat + seg.tile + tile
                    zhat = (z[m * tiles * planes + at] - st[where, 0:1]) * st[where, 1:2]
                    inner = dyb[at] - totals[0][tile] * scale - zhat * (totals[1][tile] * scale)
                    dz.store(0, seg.tile + tile, plane, inner * st[where, 2:3] * self.masks[0])

            planes_loop(planes, apply, TURNS)
        self.back_data(m, unit, dz)
        first = min(seg.off for seg in unit.segs)
        last = max(seg.off + seg.taps**2 * seg.cin * seg.cout // LANES for seg in unit.segs)
        wanted = (self.quarter * self.share < last) & ((self.quarter + 1) * self.share > first)

        @pl.when(wanted)
        def _():
            self.back_kernel(m, unit, dz)

    def dz_planes(self, unit):
        r = self.refs
        mode = {"p1": "p", "s2": "dz2", "s1": "wide" if self.k == 3 else "s1"}[unit.kind]
        return Planes(
            mode,
            unit.tiles,
            unit.planes,
            self.masks,
            self.rows,
            r.dC,
            r.dE,
            r.dR,
            self.k <= 1 and unit.kind == "s1",
        )

    def table_grads(self, m, seg, totals):
        gg = self.refs.gg
        slot = seg.slot
        for which, found in ((0, totals[1]), (1, totals[0])):
            if seg.cout > LANES:
                for tile in range(2):
                    gg[m, which, slot : slot + 1, tile * LANES : (tile + 1) * LANES] = found[tile]
            else:
                row = jnp.broadcast_to(found[0], (8, LANES))
                if seg.cout < LANES:
                    row = self.keep(row, seg.cout, [0])
                gg[m, which, slot : slot + 1, 0:LANES] = row[0:1]

    def wide_rows(self, ref, at, tiles, plane, count):
        pieces = [
            ref[pl.ds(at(0, tile, plane), count)].reshape(count * self.rows, LANES)
            for tile in range(tiles)
        ]
        return pieces[0] if tiles == 1 else jnp.concatenate(pieces, axis=1)

    def back_data(self, m, unit, dz):
        r = self.refs
        kind, tiles = unit.kind, unit.tiles
        target = getattr(r, "T" + unit.name)
        lanes = tiles * LANES
        rows = self.rows

        def kernel_rows(d, first, count):
            return target[m * unit.depth + d, first : first + count, 0:lanes]

        def product(left, right):
            return lax.dot_general(left, right, ACROSS, preferred_element_type=jnp.float32)

        def put(ref, tile, planes, first, count, value, step=1, add=False):
            block = value.reshape(count, rows, LANES)
            for q in range(count):
                at = tile * planes + first + q * step
                ref[at] = ref[at] + block[q] if add else block[q]

        planes = unit.planes
        if kind == "s1":
            goal = r.gu if unit.name == "b" else r.gin
            add = unit.name == "a"
            chunk = min(planes, 4)
            across = getattr(r, "T" + unit.name + unit.name)

            def body(step):
                first = step * chunk
                if self.k == 3:
                    total = None
                    for d in range(3):
                        for ref, at in ((dz.right, 0), (dz.main, 256), (dz.edge, 512)):
                            left = self.wide_rows(ref, dz.at, 2, first + 1 - d, chunk)
                            piece = product(left, kernel_rows(d, at, 256))
                            total = piece if total is None else total + piece
                else:
                    narrow = 1 if dz.narrow else 2
                    left = []
                    for d in range(3):
                        at = first + 1 - d
                        left.append(self.wide_rows(dz.main, dz.at, 2, at, chunk))
                        left.append(self.wide_rows(dz.edge, dz.edge_at, narrow, at, chunk))
                    right = across[pl.ds(m * 3, 3), 0 : unit.rows].reshape(3 * unit.rows, 256)
                    total = lax.dot_general(
                        jnp.concatenate(left, axis=1),
                        right,
                        DOWN,
                        preferred_element_type=jnp.float32,
                    )
                for tile in range(2):
                    put(
                        goal,
                        tile,
                        planes,
                        first,
                        chunk,
                        total[:, tile * LANES : (tile + 1) * LANES],
                        add=add,
                    )

            planes_loop(planes // chunk, body, 2)
            return
        if kind == "p1":
            left = self.wide_rows(dz.main, dz.at, tiles, 0, planes)
            total = product(left, kernel_rows(0, 0, 256))
            for tile in range(2):
                put(
                    r.gt,
                    tile,
                    planes,
                    0,
                    planes,
                    total[:, tile * LANES : (tile + 1) * LANES],
                    add=True,
                )
            return
        goal = self.grads[unit.source]
        add = unit.source == "t"
        lanes_in = unit.lanes_in
        count_in = unit.planes_in
        for parity, terms in ((0, [(1, 0)]), (1, [(2, 0), (0, 1)])):
            total, side = None, None
            for d, offset in terms:
                left = self.wide_rows(dz.main, dz.at, tiles, offset, planes)
                piece = product(left, kernel_rows(d, 0, lanes_in))
                total = piece if total is None else total + piece
                left = self.wide_rows(dz.edge, dz.at, tiles, offset, planes)
                piece = product(left, kernel_rows(d, lanes_in, LANES))
                side = piece if side is None else side + piece
            for tile in range(lanes_in // LANES):
                value = total[:, tile * LANES : (tile + 1) * LANES]
                if tile == lanes_in // LANES - 1:
                    value = value + side
                put(goal, tile, count_in, parity, planes, value, step=2, add=add)

    def back_kernel(self, m, unit, dz):
        r = self.refs
        G, rep, wgv = r.work, r.rep, r.wgv
        tiles, planes = unit.tiles, unit.planes
        source = self.maps[unit.source]
        right = self.wide_rows(dz.main, dz.at, tiles, 0, planes)

        def gather(d):
            at = 0
            for part in self.parts(unit, source):
                pieces = self.rows_of(unit, part, m, d, 0, planes)
                left = pieces[0] if len(pieces) == 1 else jnp.concatenate(pieces, axis=1)
                count = left.shape[1]
                result = lax.dot_general(left, right, ALONG, preferred_element_type=jnp.float32)
                for tile in range(tiles):
                    row = pl.multiple_of((d * tiles + tile) * unit.rows + at, 8)
                    G[pl.ds(row, count)] = result[:, tile * LANES : (tile + 1) * LANES]
                at += count

        if self.k == 3 and unit.kind == "s1":
            self.direct_kernel(m, unit, right)
            return
        planes_loop(unit.depth, gather)
        for seg in unit.segs:
            self.fold_kernel(m, unit, seg)

    def direct_kernel(self, m, unit, right):
        wgv, (seg,) = self.refs.wgv, unit.segs
        source = self.maps[unit.source]
        span = 2 * seg.cin
        low, high = self.quarter * self.share, (self.quarter + 1) * self.share

        def tap_row(d):
            first = seg.off + d * (3 * span)

            @pl.when((first < high) & (first + 3 * span > low))
            def _():
                for column, part in enumerate(self.parts(unit, source)):
                    pieces = self.rows_of(unit, part, m, d, 0, unit.planes)
                    left = jnp.concatenate(pieces, axis=1)
                    result = lax.dot_general(left, right, ALONG, preferred_element_type=jnp.float32)
                    for tile in range(2):
                        rows = pl.ds(first + column * span + tile, seg.cin, stride=2)
                        wgv[rows] = result[:, tile * LANES : (tile + 1) * LANES]

        planes_loop(unit.depth, tap_row)

    def fold_kernel(self, m, unit, seg):
        r = self.refs
        G, rep, wgv = r.work, r.rep, r.wgv
        cin, cout, tiles = seg.cin, seg.cout, unit.tiles
        width = 3 if seg.taps == 3 else 1
        found = links(self.k, unit, seg)
        off = seg.off

        def fold(d):
            for column in range(width):
                tap = d * width + column
                totals = []
                for tile in range(seg.tiles):
                    total = None
                    for row, which, wanted in found:
                        if which != column:
                            continue
                        at = pl.multiple_of((d * tiles + seg.tile + tile) * unit.rows + row, 8)
                        piece = G[pl.ds(at, cin)]
                        if cout <= LANES:
                            local = self.local_blocks(seg, tile, wanted)
                            if not local:
                                continue
                            piece = self.keep(piece, cout, local)
                        total = piece if total is None else total + piece
                    totals.append(total)
                if cout > LANES:
                    for tile in range(2):
                        wgv[pl.ds(off + tap * (2 * cin) + tile, cin, stride=2)] = totals[tile]
                    continue
                total = None
                for piece in totals:
                    if piece is not None:
                        total = piece if total is None else total + piece
                if cout == LANES:
                    wgv[pl.ds(pl.multiple_of(off + tap * cin, 8), cin)] = total
                else:
                    rep[pl.ds(pl.multiple_of(tap * cin, cin), cin)] = self.spread(total, cout)

        planes_loop(unit.depth, fold)
        if cout < LANES:
            ratio = LANES // cout
            count = width * width * cin // ratio
            total = None
            for part in range(ratio):
                piece = self.keep(rep[pl.ds(part, count, stride=ratio)], cout, [part])
                total = piece if total is None else total + piece
            wgv[off : off + count] = total

    def backward(self, m, meanwhile):
        e = MODULES + m
        last = m == MODULES - 1
        self.sent(jnp.where(last, m, e + 1))
        self.send_back(m)
        pl.when(last)(meanwhile)
        for name in ("g", "f", "e", "d", "u"):
            if name in self.units:
                for seg in self.units[name].segs:
                    if seg.dest >= 0:
                        self.arrived(e, seg.dest).wait_recv()
                self.back_unit(m, self.units[name])
        self.back_unit(m, self.units["b"])
        self.back_unit(m, self.units["a"])


STATS = 20
TURNS = 8
NAMES = list(
    dict(x=0, cot=0, w=0, gains=0, shifts=0, kinds=0, out=0, grad=0, wg=0, gain=0, shift=0)
)


def one_hot(goal, lane, deep):
    pieces = [
        jnp.where(goal == lane + first, 1.0, 0.0).astype(jnp.bfloat16)
        for first in range(0, deep, LANES)
    ]
    return jnp.concatenate(pieces, axis=1)


class Cells:
    def __init__(self, core, shape, small, large):
        self.core = core
        row = lax.broadcasted_iota(jnp.int32, shape, 0)
        self.wide = self.pick(LW // 8, SW // 8)
        tall = self.pick(LH // 8, SH // 8)
        self.crop = self.pick((row * 43691) >> 21, (row * 43691) >> 19)
        inner = row - self.crop * (self.wide * tall)
        self.along = self.pick((inner * 43691) >> 18, (inner * 43691) >> 17)
        self.across = inner - self.along * self.wide
        self.valid = self.crop < self.pick(large, small)
        self.last = tall - 1

    def pick(self, large, small):
        return jnp.where(self.core == 0, large, small)


def fill_masks(refs, rows, core, small, large):
    cells = Cells(core, (rows, LANES), small, large)
    valid = cells.valid
    six = cells.wide == 6
    up, down = valid & (cells.along > 0), valid & (cells.along < cells.last)
    tables = (
        valid,
        valid & (cells.across > 0),
        valid & (cells.across < cells.wide - 1),
        up & six,
        up & jnp.logical_not(six),
        down & six,
        down & jnp.logical_not(six),
    )
    for at, table in enumerate(tables):
        refs.masks[at] = jnp.where(table, 1.0, 0.0)


class Gather:
    def __init__(self, refs, core, count):
        self.refs, self.core, self.count = refs, core, count
        self.z = lax.axis_index("crops") // 2
        self.last = count // 2 - 1

    def hop(self, t, source, right):
        r = self.refs
        at = source * 2 + self.core
        gath = r.gathc if t else r.gathx
        to = self.z + 1 if right else self.z - 1
        return pltpu.make_async_remote_copy(
            src_ref=gath.at[at],
            dst_ref=gath.at[at],
            send_sem=r.hsem.at[(t * (self.last + 1) + source) * 3 + (0 if right else 1)],
            recv_sem=r.gsem.at[t * self.count + at],
            device_id=dict(crops=to * 2 + self.core),
            device_id_type=pl.DeviceIdType.MESH,
        )

    def across(self, t, source, core, rows):
        r = self.refs
        at = source * 2 + core
        gath = r.gathc if t else r.gathx
        return pltpu.make_async_remote_copy(
            src_ref=gath.at[at, pl.ds(0, rows)],
            dst_ref=gath.at[at, pl.ds(0, rows)],
            send_sem=r.hsem.at[(t * (self.last + 1) + source) * 3 + 2],
            recv_sem=r.gsem.at[t * self.count + at],
            device_id=dict(crops=self.z * 2 + 1 - self.core),
            device_id_type=pl.DeviceIdType.MESH,
        )

    def each_core(self, action):
        for core, rows in ((0, SH * SW * C0 // LANES), (1, ROWS)):

            @pl.when(self.core == core)
            def _():
                action(core, rows)

    def send(self, t, source, rightward, leftward):
        if rightward:

            @pl.when(self.z < self.last)
            def _():
                self.hop(t, source, True).start()

        if leftward:

            @pl.when(self.z > 0)
            def _():
                self.hop(t, source, False).start()

        self.each_core(lambda core, rows: self.across(t, source, core, rows).start())

    def step(self, t, s):
        r = self.refs
        if s == 0:
            at = self.z * 2 + self.core
            if t:
                r.gathc[at] = r.cot[...]
            else:
                r.gathx[at] = r.x[...]
            self.send(t, self.z, True, True)
            return

        @pl.when(self.z >= s)
        def _():
            self.hop(t, self.z - s, True).wait_recv()
            self.send(t, self.z - s, True, False)

        @pl.when(self.z + s <= self.last)
        def _():
            self.hop(t, self.z + s, True).wait_recv()
            self.send(t, self.z + s, False, True)

    def collect(self, t):
        for source in range(self.last + 1):
            for core, rows in ((0, ROWS), (1, SH * SW * C0 // LANES)):

                @pl.when(self.core == core)
                def _():
                    self.across(t, source, 1 - core, rows).wait_recv()

    def finish(self, t):
        def sent(source, rightward, leftward):
            if rightward:

                @pl.when(self.z < self.last)
                def _():
                    self.hop(t, source, True).wait_send()

            if leftward:

                @pl.when(self.z > 0)
                def _():
                    self.hop(t, source, False).wait_send()

            self.each_core(lambda core, rows: self.across(t, source, core, rows).wait_send())

        sent(self.z, True, True)
        for s in range(1, self.last + 1):

            @pl.when(self.z >= s)
            def _():
                sent(self.z - s, True, False)

            @pl.when(self.z + s <= self.last)
            def _():
                sent(self.z + s, False, True)


def scratch_table(rows, weight_rows, count):
    def half(many):
        return pltpu.VMEM((many, rows, LANES), jnp.bfloat16)

    def full(many):
        return pltpu.VMEM((many, rows, LANES), jnp.float32)

    def expanded(depth, deep, wide):
        return pltpu.VMEM((MODULES * depth, deep, wide), jnp.bfloat16)

    _, span, low = pair_rows(weight_rows, count)
    return dict(
        masks=full(MASKS),
        hC=half(2 * 20),
        hE=half(2 * 10),
        hR=half(2 * 6),
        uC=half(2 * 20),
        uE=half(2 * 10),
        uR=half(2 * 6),
        tC=half(2 * 18),
        tE=half(2 * 9),
        c1C=half(2 * 5),
        c1E=half(2 * 5),
        c2C=half(2 * 5),
        c2E=half(2 * 5),
        c3C=half(2 * 3),
        c3E=half(2 * 3),
        dC=half(20),
        dE=half(20),
        dR=half(6),
        outs=half(16),
        hf=full(2 * 16),
        s=full(2 * 16),
        za=full(2 * 16),
        zb=full(2 * 16),
        zd=full(2 * 16),
        zu=full(2 * 8),
        ze=full(2 * 4),
        zf=full(2 * 2),
        zg=full(2 * 2),
        gt=full(16),
        gu=full(16),
        gin=full(16),
        gc1=full(4),
        gc2=full(4),
        gc3=full(2),
        dyb=full(16),
        sb=half(16),
        rb=half(4 * 16),
        st=pltpu.VMEM((MODULES * STATS, 8, LANES), jnp.float32),
        Ta=expanded(3, 768, 256),
        Tb=expanded(3, 768, 256),
        Taa=expanded(3, 512, 256),
        Tbb=expanded(3, 512, 256),
        Td=expanded(3, 384, 512),
        Tu=expanded(1, 256, 768),
        Te=expanded(3, 256, 256),
        Tf=expanded(3, 256, 128),
        Tg=expanded(3, 256, 256),
        raw=pltpu.VMEM((9408, LANES), jnp.bfloat16),
        work=pltpu.VMEM((4608, LANES), jnp.float32),
        rep=pltpu.VMEM((640, LANES), jnp.float32),
        wgv=pltpu.VMEM((weight_rows, LANES), jnp.float32),
        wq=pltpu.VMEM((MODULES, low + span, LANES), jnp.float32),
        wh=pltpu.VMEM((MODULES, low + span, LANES), jnp.bfloat16),
        wr=pltpu.VMEM((MODULES, span, LANES), jnp.bfloat16),
        gathx=pltpu.VMEM((count, ROWS, LANES), jnp.bfloat16),
        gathc=pltpu.VMEM((count, ROWS, LANES), jnp.bfloat16),
        hot=pltpu.VMEM((2, 384, 768), jnp.bfloat16),
        blocks=pltpu.VMEM((2, ROWS, LANES), jnp.bfloat16),
        slopes=pltpu.VMEM((2, ROWS, LANES), jnp.float32),
        blockr=pltpu.VMEM((ROWS, LANES), jnp.bfloat16),
        slopeh=pltpu.VMEM((ROWS, LANES), jnp.bfloat16),
        sloper=pltpu.VMEM((ROWS, LANES), jnp.bfloat16),
        gg=pltpu.VMEM((MODULES, 2, SLOTS, 256), jnp.float32),
        ggr=pltpu.VMEM((MODULES, 2, SLOTS, 256), jnp.float32),
        wsem=pltpu.SemaphoreType.DMA((8,)),
        ssem=pltpu.SemaphoreType.DMA((16,)),
        rsem=pltpu.SemaphoreType.DMA((16,)),
        hsem=pltpu.SemaphoreType.DMA((3 * count,)),
        gsem=pltpu.SemaphoreType.DMA((2 * count,)),
        psem=pltpu.SemaphoreType.DMA((5,)),
        qsem=pltpu.SemaphoreType.DMA((5,)),
        osem=pltpu.SemaphoreType.DMA((1,)),
    )


def pair_rows(weight_rows, count):
    share = weight_rows // count
    low = share // 16 * 16
    return share, -(-(2 * share - low) // 16) * 16, low


def greet(core, count):
    barrier = pltpu.get_barrier_semaphore()
    me, shard = lax.axis_index("branch"), lax.axis_index("crops")
    z = shard // 2

    def signal(**where):
        pl.semaphore_signal(barrier, inc=1, device_id=where, device_id_type=pl.DeviceIdType.MESH)

    for step in range(1, 4):
        signal(branch=lax.rem(me + step, 4))
    signal(crops=shard + 1 - 2 * core)

    @pl.when(z > 0)
    def _():
        signal(crops=shard - 2)

    @pl.when(z < count // 2 - 1)
    def _():
        signal(crops=shard + 2)

    ends = (z == 0).astype(jnp.int32) + (z == count // 2 - 1).astype(jnp.int32)
    pl.semaphore_wait(barrier, 6 - ends)


def whole_kernel(names, rows, large, small, *args):
    refs = SimpleNamespace(**dict(zip(names, args)))
    count = large + small
    me, shard = lax.axis_index("branch"), lax.axis_index("crops")
    core = shard % 2
    weight_rows = refs.wgv.shape[0]
    share, span, low = pair_rows(weight_rows, count)
    quarter = pl.multiple_of(shard // 2 * (2 * share), 8)

    class Lazy:
        def __getitem__(self, index):
            return refs.masks[index]

    def across(source, goal, index):
        return pltpu.make_async_remote_copy(
            src_ref=source,
            dst_ref=goal,
            send_sem=refs.psem.at[index],
            recv_sem=refs.qsem.at[index],
            device_id=dict(crops=shard + 1 - 2 * core),
            device_id_type=pl.DeviceIdType.MESH,
        )

    def kernel_pair(m):
        at = pl.multiple_of(low * (1 - core), 16)
        return across(refs.wh.at[m, pl.ds(at, span)], refs.wr.at[m], m)

    outputs_pair = across(refs.blocks.at[1], refs.blockr, 2)
    gradient_pair = across(refs.slopeh, refs.sloper, 3)
    table_pair = across(refs.gg, refs.ggr, 4)
    gather = Gather(refs, core, count)

    def every(action):
        for k in range(4):

            @pl.when(me == k)
            def _():
                action(Branch(k, rows, large, small, 2 * share, refs, Lazy(), core))

    def begin(branch):
        branch.fetch_first()

    def prepare(branch):
        found = branch.segments()
        first, second = ((1, 4), (1, 3), (0, 2), (0, 1))[branch.k]
        stops = {first: 1, second: 2, len(found) - 1: 3}
        for index, (unit, seg) in enumerate(found):
            branch.expand(index)
            if index in stops:
                gather.step(0, stops[index])

    def main(branch):
        branch.unpack(0, branch.take_feature)
        branch.maps["h"].close(0)
        gather.step(1, 0)

        def ahead(m, carry):
            branch.forward(m, gather)
            return carry

        def meanwhile():
            branch.plan_pack()
            branch.pack_outputs()
            outputs_pair.start()

        def back(step, carry):
            m = MODULES - 1 - step
            branch.backward(m, meanwhile)
            found = refs.wgv[pl.ds(quarter, 2 * share)]
            refs.wq[m, 0 : 2 * share] = found
            spare = jnp.zeros((low + span - 2 * share, LANES), jnp.float32)
            refs.wh[m] = jnp.concatenate([found, spare], axis=0).astype(jnp.bfloat16)
            kernel_pair(m).start()
            return carry

        lax.fori_loop(0, MODULES, ahead, 0)
        lax.fori_loop(0, MODULES, back, 0)
        branch.sent(MODULES)
        table_pair.start()

        def share_gradient():
            refs.slopeh[...] = refs.slopes[1].astype(jnp.bfloat16)
            gradient_pair.start()

        branch.pack_gradient(share_gradient)

    every(begin)
    greet(core, count)
    gather.step(0, 0)
    fill_masks(refs, rows, core, small, large)
    refs.wgv[pl.ds(quarter, 2 * share)] = jnp.zeros((2 * share, LANES), jnp.float32)
    refs.gg[...] = jnp.zeros(refs.gg.shape, jnp.float32)
    every(prepare)
    gather.collect(0)
    every(main)

    for step in range(MODULES):
        m = MODULES - 1 - step
        kernel_pair(m).wait()
        mine = refs.wq[m, pl.ds(pl.multiple_of(low * core, 8), span)]
        refs.work[pl.ds(m, span, stride=MODULES)] = mine + refs.wr[m].astype(jnp.float32)
    skip = pl.multiple_of(core * (MODULES * (share - low)), 8)
    leave = pltpu.make_async_copy(
        refs.work.at[pl.ds(skip, MODULES * share)], refs.wg, refs.osem.at[0]
    )
    leave.start()
    outputs_pair.wait()
    gradient_pair.wait()
    table_pair.wait()
    own = refs.kinds[shard] != core
    refs.out[...] = jnp.where(own, refs.blocks[0].astype(jnp.float32), refs.blockr[...].astype(jnp.float32)).astype(jnp.bfloat16)
    refs.grad[...] = jnp.where(own, refs.slopes[0], refs.sloper[...].astype(jnp.float32))
    width = 256 // count
    for which, goal in ((0, refs.gain), (1, refs.shift)):
        for m in range(MODULES):
            total = refs.gg[m, which] + refs.ggr[m, which]
            found = None
            for at in range(count):
                piece = jnp.where(shard == at, total[:, at * width : (at + 1) * width], 0.0)
                found = piece if found is None else found + piece
            goal[m] = found
    gather.finish(0)
    gather.finish(1)
    leave.wait()


def whole_call(rows, large, small, x, cot, w, gains, shifts, kinds):
    count = large + small
    weight_rows = w.shape[0] // MODULES
    table = scratch_table(rows, weight_rows, count)
    vmem = pl.BlockSpec(memory_space=pltpu.VMEM)
    hbm = pl.BlockSpec(memory_space=pl.ANY)
    smem = pl.BlockSpec(memory_space=pltpu.SMEM)
    tables = jax.ShapeDtypeStruct((MODULES, SLOTS, 256 // count), jnp.float32)
    return pl.pallas_call(
        partial(whole_kernel, NAMES + list(table), rows, large, small),
        out_shape=(
            jax.ShapeDtypeStruct((ROWS, LANES), jnp.bfloat16),
            jax.ShapeDtypeStruct((ROWS, LANES), jnp.float32),
            jax.ShapeDtypeStruct((MODULES * weight_rows // count, LANES), jnp.float32),
            tables,
            tables,
        ),
        in_specs=[vmem, vmem, hbm, vmem, vmem, smem],
        out_specs=(vmem, vmem, hbm, vmem, vmem),
        scratch_shapes=list(table.values()),
        compiler_params=pltpu.CompilerParams(
            collective_id=0, has_side_effects=True, vmem_limit_bytes=62 * 1024 * 1024
        ),
    )(x, cot, w, gains, shifts, kinds)


def leave_kernel(*args):
    sources, goals, rooms, arrive, depart = args[:5], args[5:10], args[10:15], args[15], args[16]
    pieces = []
    for source, goal, room in zip(sources, goals, rooms):
        high = source.shape[0]
        parts = 3 if high % 24 == 0 else 1
        for part in range(parts):
            rows = pl.ds(part * (high // parts), high // parts)
            at = len(pieces)
            pieces.append(
                (
                    pltpu.make_async_copy(source.at[rows], room.at[rows], arrive.at[at]),
                    pltpu.make_async_copy(room.at[rows], goal.at[rows], depart.at[at]),
                )
            )
    for come, _ in pieces:
        come.start()
    for come, go in pieces:
        come.wait()
        go.start()
    for _, go in pieces:
        go.wait()


def leave_call(arrays):
    hbm = pl.BlockSpec(memory_space=pl.ANY)
    return pl.pallas_call(
        leave_kernel,
        out_shape=tuple(jax.ShapeDtypeStruct(array.shape, array.dtype) for array in arrays),
        in_specs=[hbm] * 5,
        out_specs=(hbm,) * 5,
        scratch_shapes=[pltpu.VMEM(array.shape, array.dtype) for array in arrays]
        + [pltpu.SemaphoreType.DMA((16,)), pltpu.SemaphoreType.DMA((16,))],
    )(*arrays)


def on_device_grouped(features, weights, gains, shifts, cotangent, size_group):
    count = lax.axis_size("crops")
    large = count // 4
    weight_rows = weights.shape[2] // LANES
    results = whole_call(
        group_rows(count),
        large,
        count - large,
        features[0],
        cotangent[0],
        weights[0]
        .reshape(MODULES, weight_rows, LANES)
        .transpose(1, 0, 2)
        .reshape(MODULES * weight_rows, LANES),
        gains[0],
        shifts[0],
        size_group,
    )
    out, grad, weight_grad, gain, shift = leave_call(results)
    share = weight_rows // count
    weight_grad = weight_grad.reshape(share, MODULES, LANES).transpose(1, 0, 2)
    weight_grad = with_layout_constraint(weight_grad, Layout((1, 0, 2)))
    return (
        out[None],
        grad[None],
        weight_grad.reshape(1, MODULES, share * LANES),
        gain[None],
        shift[None],
    )


def group_rows(count):
    large = count // 4
    rows = max(large * (LH // 8) * (LW // 8), (count - large) * (SH // 8) * (SW // 8))
    return -(-rows // 16) * 16


def fits(count):
    return count % 8 == 0 and group_rows(count) <= 96


def solution(mesh):
    placed = (
        P("branch", "crops", None),
        P("branch", None, None),
        P("branch", None, None, None),
        P("branch", None, None, None),
        P("branch", "crops", None),
        P(),
    )
    return jax.shard_map(
        on_device_grouped if fits(mesh.shape["crops"]) else on_device,
        mesh=mesh,
        in_specs=placed,
        out_specs=(
            P("branch", "crops", None),
            P("branch", "crops", None),
            P("branch", None, "crops"),
            P("branch", None, None, "crops"),
            P("branch", None, None, "crops"),
        ),
        check_vma=False,
    )
```

```python
from functools import partial
from types import SimpleNamespace
import math

import jax
import jax.numpy as jnp
import numpy as np
from jax import lax
from jax.experimental import pallas as pl
from jax.experimental.layout import Layout, with_layout_constraint
from jax.experimental.pallas import tpu as pltpu
from jax.sharding import PartitionSpec as P

C0 = 32
BLOCKS = 1
MODULES = 2
CROPS_DEV = 1
SH = 32
SW = 24
LH = 64
LW = 48
ROWS = 768
MSG_ROWS = 384


EPS = 1e-05


def as_sent(x):

    def short(part):
        return part.astype(jnp.bfloat16) if part.dtype == jnp.float32 else part

    return jax.tree.map(short, x)


def sender_plan(branch_index, top_channels, blocks):
    channels = top_channels << branch_index
    operations = []
    for block_index in range(blocks):
        operations.append(
            SimpleNamespace(
                phase=2 * block_index,
                source=("h", block_index),
                level=branch_index,
                cin=channels,
                cout=channels,
                stride=1,
                taps=3,
                act="silu",
                output=("u", block_index),
                skip=None,
                dest=-1,
            )
        )
        operations.append(
            SimpleNamespace(
                phase=2 * block_index + 1,
                source=("u", block_index),
                level=branch_index,
                cin=channels,
                cout=channels,
                stride=1,
                taps=3,
                act="res",
                output=("h", block_index + 1),
                skip=("h", block_index),
                dest=-1,
            )
        )
    top_name = ("h", blocks)
    for target in range(branch_index):
        operations.append(
            SimpleNamespace(
                phase=2 * blocks,
                source=top_name,
                level=branch_index,
                cin=channels,
                cout=top_channels << target,
                stride=1,
                taps=1,
                act="none",
                output=None,
                skip=None,
                dest=target,
            )
        )
    for target in range(branch_index + 1, 4):
        for depth_step in range(1, target - branch_index + 1):
            is_last = depth_step == target - branch_index
            operations.append(
                SimpleNamespace(
                    phase=2 * blocks + depth_step - 1,
                    source=top_name if depth_step == 1 else ("chain", target, depth_step - 1),
                    level=branch_index + depth_step,
                    cin=channels,
                    cout=top_channels << target if is_last else channels,
                    stride=2,
                    taps=3,
                    act="none" if is_last else "silu",
                    output=None if is_last else ("chain", target, depth_step),
                    skip=None,
                    dest=target if is_last else -1,
                )
            )
    for position, operation in enumerate(operations):
        operation.slot = position
        operation.size = (
            operation.taps * operation.taps * operation.cin * operation.cout
        )
        if operation.taps == 1:
            operation.kshape = (operation.cin, operation.cout)
        else:
            operation.kshape = (3, 3, operation.cin, operation.cout)
    return operations


def phase_lengths(top_channels, blocks):
    phase_count = 2 * blocks + 3
    lengths = [0] * phase_count
    for branch_index in range(4):
        per_phase = [0] * phase_count
        for operation in sender_plan(branch_index, top_channels, blocks):
            per_phase[operation.phase] += operation.size
        lengths = [max(current, candidate) for current, candidate in zip(lengths, per_phase)]
    return lengths


def weighted_plan(branch_index, top_channels, blocks):
    lengths = phase_lengths(top_channels, blocks)
    starts = [sum(lengths[:phase_index]) for phase_index in range(len(lengths))]
    running = [0] * len(lengths)
    operations = sender_plan(branch_index, top_channels, blocks)
    for operation in operations:
        phase_index = operation.phase
        operation.inner = running[phase_index]
        operation.offset = starts[phase_index] + running[phase_index]
        operation.position = sum(
            (1 for earlier in operations[: operation.slot] if earlier.phase == phase_index)
        )
        running[phase_index] += operation.size
    return operations


def phase_operations(branch_index, phase_index):
    return [
        operation
        for operation in weighted_plan(branch_index, C0, BLOCKS)
        if operation.phase == phase_index
    ]


def input_names(operations):
    source_names = []
    for operation in operations:
        if operation.source not in source_names:
            source_names.append(operation.source)
    return source_names


def silu_slope(value):
    sigmoid = jax.nn.sigmoid(value)
    return sigmoid * (1.0 + value * (1.0 - sigmoid))


def crop_cells(size_kind):
    return (LH, LW) if size_kind else (SH, SW)


def map_dims(size_kind, level, channels):
    height, breadth = crop_cells(size_kind)
    return (CROPS_DEV, height >> level, breadth >> level, channels)


def source_dims(branch_index, size_kind, map_name):
    level = branch_index + map_name[2] if map_name[0] == "chain" else branch_index
    return map_dims(size_kind, level, C0 << branch_index)


def preact_dims(size_kind, operation):
    return map_dims(size_kind, operation.level, operation.cout)


def to_canvas(arrays, value_type):
    if not arrays:
        return jnp.zeros((ROWS, 128), value_type)
    flattened = jnp.concatenate([array.reshape(-1).astype(value_type) for array in arrays])
    return jnp.pad(flattened, (0, ROWS * 128 - flattened.shape[0])).reshape(ROWS, 128)


def from_canvas(canvas, dims_list):
    flattened = canvas.reshape(-1)
    pieces = []
    offset = 0
    for dims_entry in dims_list:
        count_here = math.prod(dims_entry)
        pieces.append(flattened[offset : offset + count_here].reshape(dims_entry))
        offset += count_here
    return pieces


def to_slot(array):
    flattened = array.reshape(-1)
    return jnp.pad(flattened, (0, MSG_ROWS * 128 - flattened.shape[0])).reshape(MSG_ROWS, 128)


def from_slot(slot_rows, dims_entry):
    return slot_rows.reshape(-1)[: math.prod(dims_entry)].reshape(dims_entry)


def upsample(message, factor):
    crop_count, height, breadth, channels = message.shape
    widened = jnp.broadcast_to(
        message[:, :, None, :, None, :], (crop_count, height, factor, breadth, factor, channels)
    )
    return widened.reshape(crop_count, height * factor, breadth * factor, channels)


def block_pool(array, factor):
    crop_count, height, breadth, channels = array.shape
    return array.reshape(
        crop_count, height // factor, factor, breadth // factor, factor, channels
    ).sum(axis=(2, 4))


def kernel_piece(module_weights, operation):
    start = operation.offset
    return module_weights[start : start + operation.size].reshape(operation.kshape)


def conv_forward(operation, source, kernel):
    if operation.taps == 1:
        return jnp.einsum("nhwc,cd->nhwd", source, kernel, preferred_element_type=jnp.float32)
    stride = operation.stride
    return lax.conv_general_dilated(
        source,
        kernel,
        (stride, stride),
        ((1, 1), (1, 1)),
        dimension_numbers=("NHWC", "HWIO", "NHWC"),
        preferred_element_type=jnp.float32,
    )


def conv_backward(operation, source, kernel, upstream):
    if operation.taps == 1:
        source_grad = jnp.einsum(
            "nhwd,cd->nhwc", upstream, kernel, preferred_element_type=jnp.float32
        )
        kernel_grad = jnp.einsum(
            "nhwc,nhwd->cd", source, upstream, preferred_element_type=jnp.float32
        )
        return (source_grad, kernel_grad)
    stride = operation.stride
    flipped = jnp.transpose(kernel[::-1, ::-1], (0, 1, 3, 2))
    high_pad = 2 if stride == 2 else 1
    source_grad = lax.conv_general_dilated(
        upstream,
        flipped,
        (1, 1),
        ((1, high_pad), (1, high_pad)),
        lhs_dilation=(stride, stride),
        dimension_numbers=("NHWC", "HWIO", "NHWC"),
        preferred_element_type=jnp.float32,
    )
    kernel_grad = lax.conv_general_dilated(
        source,
        upstream,
        (1, 1),
        ((1, 2 - stride), (1, 2 - stride)),
        rhs_dilation=(stride, stride),
        dimension_numbers=("CHWN", "IHWO", "NHWC"),
        preferred_element_type=jnp.float32,
    )
    return (source_grad, jnp.transpose(kernel_grad, (1, 2, 0, 3)))


def cell_total(counts, size_kind, level):
    height, breadth = crop_cells(size_kind)
    return counts[size_kind] * float(CROPS_DEV * (height >> level) * (breadth >> level))


def norm_terms(totals, counts, size_kind, operation):
    cells_here = cell_total(counts, size_kind, operation.level)
    channels = operation.cout
    position = operation.position
    average = totals[size_kind, 0, position, :channels] / cells_here
    variance = totals[size_kind, 1, position, :channels] / cells_here - average * average
    return (average, lax.rsqrt(variance + EPS))


def forward_conv(branch_index, size_kind, phase_index, source_canvas, module_weights):
    operations = phase_operations(branch_index, phase_index)
    source_names = input_names(operations)
    pieces = from_canvas(
        source_canvas, [source_dims(branch_index, size_kind, map_name) for map_name in source_names]
    )
    sources = {
        map_name: piece.astype(jnp.bfloat16) for map_name, piece in zip(source_names, pieces)
    }
    preacts = []
    totals = jnp.zeros((2, 2, 3, 8 * C0), jnp.float32)
    for operation in operations:
        preact = conv_forward(
            operation, sources[operation.source], kernel_piece(module_weights, operation)
        )
        preacts.append(preact)
        channels = operation.cout
        position = operation.position
        totals = totals.at[size_kind, 0, position, :channels].set(jnp.sum(preact, axis=(0, 1, 2)))
        totals = totals.at[size_kind, 1, position, :channels].set(
            jnp.sum(preact * preact, axis=(0, 1, 2))
        )
    return (to_canvas(preacts, jnp.float32), totals)


def forward_norm(
    branch_index,
    size_kind,
    phase_index,
    preact_canvas,
    totals,
    counts,
    module_gains,
    module_shifts,
    skip_canvas,
    message_buffer,
):
    operations = phase_operations(branch_index, phase_index)
    preacts = from_canvas(
        preact_canvas, [preact_dims(size_kind, operation) for operation in operations]
    )
    skip_map = from_canvas(skip_canvas, [map_dims(size_kind, branch_index, C0 << branch_index)])[0]
    produced = []
    for operation, preact in zip(operations, preacts):
        average, inverse_std = norm_terms(totals, counts, size_kind, operation)
        norm_slot = operation.slot
        channels = operation.cout
        normed = (preact - average) * inverse_std * module_gains[
            norm_slot, :channels
        ] + module_shifts[norm_slot, :channels]
        if operation.act == "silu":
            produced.append(jax.nn.silu(normed))
        elif operation.act == "res":
            produced.append(jax.nn.silu(normed + skip_map))
        else:
            message_buffer = message_buffer.at[operation.dest].set(
                to_slot(normed.astype(jnp.bfloat16))
            )
    return (to_canvas(produced, jnp.float32), message_buffer)


def receive_forward(branch_index, size_kind, top_canvas, received):
    channels = C0 << branch_index
    summed = from_canvas(top_canvas, [map_dims(size_kind, branch_index, channels)])[0]
    for sender in range(4):
        if sender < branch_index:
            summed = summed + from_slot(
                received[sender], map_dims(size_kind, branch_index, channels)
            ).astype(jnp.float32)
        elif sender > branch_index:
            coarse = from_slot(received[sender], map_dims(size_kind, sender, channels))
            summed = summed + upsample(coarse, 2 ** (sender - branch_index)).astype(jnp.float32)
    return (to_canvas([jax.nn.silu(summed)], jnp.float32), to_canvas([summed], jnp.float32))


def receive_backward(branch_index, size_kind, grad_canvas, summed_canvas):
    dims_here = map_dims(size_kind, branch_index, C0 << branch_index)
    upstream = from_canvas(grad_canvas, [dims_here])[0]
    summed = from_canvas(summed_canvas, [dims_here])[0]
    summed_grad = upstream * silu_slope(summed)
    buffer = jnp.zeros((4, MSG_ROWS, 128), jnp.bfloat16)
    for sender in range(4):
        if sender < branch_index:
            buffer = buffer.at[sender].set(to_slot(summed_grad.astype(jnp.bfloat16)))
        elif sender > branch_index:
            pooled = block_pool(summed_grad, 2 ** (sender - branch_index))
            buffer = buffer.at[sender].set(to_slot(pooled.astype(jnp.bfloat16)))
    return (to_canvas([summed_grad], jnp.float32), buffer)


def backward_stats(
    branch_index,
    size_kind,
    phase_index,
    dout_canvas,
    message_grads,
    preact_canvas,
    totals,
    counts,
    module_gains,
    module_shifts,
    skip_canvas,
):
    operations = phase_operations(branch_index, phase_index)
    preacts = from_canvas(
        preact_canvas, [preact_dims(size_kind, operation) for operation in operations]
    )
    producing = [operation for operation in operations if operation.act != "none"]
    output_grads = from_canvas(
        dout_canvas, [preact_dims(size_kind, operation) for operation in producing]
    )
    grads_by_name = {
        operation.output: piece for operation, piece in zip(producing, output_grads)
    }
    skip_map = from_canvas(skip_canvas, [map_dims(size_kind, branch_index, C0 << branch_index)])[0]
    upstreams = []
    skip_grads = []
    sums_local = jnp.zeros((2, 2, 3, 8 * C0), jnp.float32)
    for operation, preact in zip(operations, preacts):
        average, inverse_std = norm_terms(totals, counts, size_kind, operation)
        norm_slot = operation.slot
        channels = operation.cout
        centered = (preact - average) * inverse_std
        normed = centered * module_gains[norm_slot, :channels] + module_shifts[norm_slot, :channels]
        if operation.act == "silu":
            upstream = grads_by_name[operation.output] * silu_slope(normed)
        elif operation.act == "res":
            upstream = grads_by_name[operation.output] * silu_slope(normed + skip_map)
            skip_grads.append(upstream)
        else:
            upstream = from_slot(
                message_grads[operation.dest], preact_dims(size_kind, operation)
            ).astype(jnp.float32)
        upstreams.append(upstream)
        position = operation.position
        sums_local = sums_local.at[size_kind, 0, position, :channels].set(
            jnp.sum(upstream, axis=(0, 1, 2))
        )
        sums_local = sums_local.at[size_kind, 1, position, :channels].set(
            jnp.sum(upstream * centered, axis=(0, 1, 2))
        )
    return (to_canvas(upstreams, jnp.float32), sums_local, to_canvas(skip_grads, jnp.float32))


def backward_apply(
    branch_index,
    size_kind,
    phase_index,
    upstream_canvas,
    preact_canvas,
    totals,
    grad_totals,
    counts,
    source_canvas,
    module_weights,
    module_gains,
):
    operations = phase_operations(branch_index, phase_index)
    preacts = from_canvas(
        preact_canvas, [preact_dims(size_kind, operation) for operation in operations]
    )
    upstreams = from_canvas(
        upstream_canvas, [preact_dims(size_kind, operation) for operation in operations]
    )
    source_names = input_names(operations)
    source_list = [source_dims(branch_index, size_kind, map_name) for map_name in source_names]
    pieces = from_canvas(source_canvas, source_list)
    sources = {
        map_name: piece.astype(jnp.bfloat16) for map_name, piece in zip(source_names, pieces)
    }
    source_grads = {
        map_name: jnp.zeros(dims_entry, jnp.float32)
        for map_name, dims_entry in zip(source_names, source_list)
    }
    kernel_grads = []
    slot_count = module_gains.shape[0]
    gain_part = jnp.zeros((slot_count, 8 * C0), jnp.float32)
    shift_part = jnp.zeros((slot_count, 8 * C0), jnp.float32)
    for operation, preact, upstream in zip(operations, preacts, upstreams):
        average, inverse_std = norm_terms(totals, counts, size_kind, operation)
        cells_here = cell_total(counts, size_kind, operation.level)
        norm_slot = operation.slot
        channels = operation.cout
        position = operation.position
        centered = (preact - average) * inverse_std
        mean_upstream = grad_totals[size_kind, 0, position, :channels] / cells_here
        mean_cross = grad_totals[size_kind, 1, position, :channels] / cells_here
        preact_grad = (
            module_gains[norm_slot, :channels]
            * inverse_std
            * (upstream - mean_upstream - centered * mean_cross)
        )
        source_grad, kernel_grad = conv_backward(
            operation,
            sources[operation.source],
            kernel_piece(module_weights, operation),
            preact_grad.astype(jnp.bfloat16),
        )
        source_grads[operation.source] = source_grads[operation.source] + source_grad
        kernel_grads.append(kernel_grad.reshape(-1))
        gain_part = gain_part.at[norm_slot, :channels].set(
            grad_totals[0, 1, position, :channels] + grad_totals[1, 1, position, :channels]
        )
        shift_part = shift_part.at[norm_slot, :channels].set(
            grad_totals[0, 0, position, :channels] + grad_totals[1, 0, position, :channels]
        )
    phase_length = phase_lengths(C0, BLOCKS)[phase_index]
    if kernel_grads:
        joined = jnp.concatenate(kernel_grads)
        weight_part = jnp.pad(joined, (0, phase_length - joined.shape[0]))
    else:
        weight_part = jnp.zeros((phase_length,), jnp.float32)
    return (
        to_canvas([source_grads[map_name] for map_name in source_names], jnp.float32),
        weight_part,
        gain_part,
        shift_part,
    )


def on_device(features, weights, gains, shifts, cotangent, size_group):
    crop_shard = lax.axis_index("crops")
    shard_count = lax.axis_size("crops")
    crop_kind = size_group[crop_shard]
    large_count = jnp.sum(size_group).astype(jnp.float32)
    counts = jnp.stack([shard_count - large_count, large_count])
    case_index = lax.axis_index("branch") * 2 + crop_kind
    phase_total = 2 * BLOCKS + 3
    zero_canvas = jnp.zeros((ROWS, 128), jnp.float32)
    empty_buffer = jnp.zeros((4, MSG_ROWS, 128), jnp.bfloat16)

    def run_phase(function, statics, operands):
        branches_list = [
            partial(function, branch_index, size_kind, *statics)
            for branch_index in range(4)
            for size_kind in range(2)
        ]
        return lax.switch(case_index, branches_list, *operands)

    def statistics(local_totals):
        return lax.psum(local_totals, "crops")

    def module_forward(module, start_canvas, kept):
        module_weights = weights[0, module]
        module_gains = gains[0, module]
        module_shifts = shifts[0, module]
        record = SimpleNamespace(sources=[], preacts=[], totals=[])
        h_canvas = start_canvas
        u_canvas = zero_canvas
        chain_canvas = zero_canvas
        buffer = empty_buffer
        for phase_index in range(phase_total):
            if phase_index < 2 * BLOCKS:
                source = h_canvas if phase_index % 2 == 0 else u_canvas
            elif phase_index == 2 * BLOCKS:
                source = h_canvas
            else:
                source = chain_canvas
            preact, local_totals = run_phase(forward_conv, (phase_index,), (source, module_weights))
            global_totals = kept.totals[phase_index] if kept else statistics(local_totals)
            produced, buffer = run_phase(
                forward_norm,
                (phase_index,),
                (preact, global_totals, counts, module_gains, module_shifts, h_canvas, buffer),
            )
            record.sources.append(source)
            record.preacts.append(preact)
            record.totals.append(global_totals)
            if phase_index < 2 * BLOCKS:
                if phase_index % 2 == 0:
                    u_canvas = produced
                else:
                    h_canvas = produced
            else:
                chain_canvas = produced
        received = (
            kept.received
            if kept
            else jax.tree.map(
                lambda part, own: part.astype(own.dtype),
                lax.all_to_all(as_sent(buffer), "branch", split_axis=0, concat_axis=0, tiled=True),
                buffer,
            )
        )
        result, summed = run_phase(receive_forward, (), (h_canvas, received))
        record.summed = summed
        record.received = received
        return (result, record)

    checkpoints = [features[0].astype(jnp.float32)]
    first_records = []
    for module in range(MODULES):
        result, record = module_forward(module, checkpoints[-1], None)
        checkpoints.append(result)
        first_records.append(record)
    outputs = checkpoints[-1].astype(jnp.bfloat16)
    grad_canvas = cotangent[0].astype(jnp.float32)
    module_grads = [None] * MODULES
    gain_grads = [None] * MODULES
    shift_grads = [None] * MODULES
    for module in reversed(range(MODULES)):
        kept = None
        unused_result, record = module_forward(module, checkpoints[module], kept)
        module_module_weights = weights[0, module]
        module_module_gains = gains[0, module]
        module_module_shifts = shifts[0, module]
        summed_grad, back_buffer = run_phase(receive_backward, (), (grad_canvas, record.summed))
        message_grads = jax.tree.map(
            lambda part, own: part.astype(own.dtype),
            lax.all_to_all(as_sent(back_buffer), "branch", split_axis=0, concat_axis=0, tiled=True),
            back_buffer,
        )
        top_grad = summed_grad
        chain_grad = zero_canvas
        u_grad = zero_canvas
        pending_skip = zero_canvas
        weight_parts = [None] * phase_total
        gain_total = jnp.zeros(gains.shape[2:], jnp.float32)
        shift_total = jnp.zeros(gains.shape[2:], jnp.float32)
        for module_phase_index in reversed(range(phase_total)):
            if module_phase_index >= 2 * BLOCKS:
                output_grad = chain_grad
                skip_canvas = zero_canvas
            elif module_phase_index % 2 == 1:
                output_grad = top_grad
                skip_canvas = record.sources[module_phase_index - 1]
            else:
                output_grad = u_grad
                skip_canvas = zero_canvas
            module_preact = record.preacts[module_phase_index]
            totals = record.totals[module_phase_index]
            upstream, module_local_totals, skip_grad = run_phase(
                backward_stats,
                (module_phase_index,),
                (
                    output_grad,
                    message_grads,
                    module_preact,
                    totals,
                    counts,
                    module_module_gains,
                    module_module_shifts,
                    skip_canvas,
                ),
            )
            grad_totals = lax.psum(module_local_totals, "crops")
            source_grad, weight_parts[module_phase_index], gain_part, shift_part = run_phase(
                backward_apply,
                (module_phase_index,),
                (
                    upstream,
                    module_preact,
                    totals,
                    grad_totals,
                    counts,
                    record.sources[module_phase_index],
                    module_module_weights,
                    module_module_gains,
                ),
            )
            gain_total = gain_total + gain_part
            shift_total = shift_total + shift_part
            if module_phase_index > 2 * BLOCKS:
                chain_grad = source_grad
            elif module_phase_index == 2 * BLOCKS:
                top_grad = top_grad + source_grad
            elif module_phase_index % 2 == 1:
                u_grad = source_grad
                pending_skip = skip_grad
            else:
                top_grad = source_grad + pending_skip
        joined = jnp.concatenate(weight_parts)
        weight_grad = jnp.pad(joined, (0, weights.shape[2] - joined.shape[0]))
        grad_canvas, weight_grad, gain_grads[module], shift_grads[module] = (
            top_grad,
            weight_grad,
            gain_total,
            shift_total,
        )
        module_grads[module] = weight_grad
    weight_out = lax.psum_scatter(jnp.stack(module_grads), "crops", scatter_dimension=1, tiled=True)
    share = gains.shape[3] // shard_count
    gain_out = lax.dynamic_slice_in_dim(jnp.stack(gain_grads), crop_shard * share, share, axis=2)
    shift_out = lax.dynamic_slice_in_dim(jnp.stack(shift_grads), crop_shard * share, share, axis=2)
    return (outputs[None], grad_canvas[None], weight_out[None], gain_out[None], shift_out[None])


LANES = 128
SLOTS = 8
MASKS = 7
DOWN = (((1,), (0,)), ((), ()))
ACROSS = (((1,), (1,)), ((), ()))
ALONG = (((0,), (0,)), ((), ()))


def unit_table(k):
    operations = weighted_plan(k, C0, BLOCKS)
    planes = 8 >> k
    channels = C0 << k
    units = {}
    stat = 0

    def add(name, kind, source, lanes_in, planes_in, planes_out, members):
        nonlocal stat
        segs = []
        tile = 0
        for operation, lanes, chain in members:
            cout = operation.cout
            level = operation.level if operation.taps == 3 else operation.dest
            segs.append(
                SimpleNamespace(
                    slot=operation.slot,
                    off=operation.offset // LANES,
                    cin=operation.cin,
                    cout=cout,
                    taps=operation.taps,
                    tile=tile,
                    tiles=lanes // LANES,
                    blocks=max(1, (8 >> level)),
                    dest=operation.dest,
                    act=operation.act,
                    chain=chain,
                    up=k - operation.dest if operation.taps == 1 else 0,
                )
            )
            tile += lanes // LANES
        rows = {"s1": (384, 384, 512, 768)[k], "s2": lanes_in + LANES, "p1": 256}[kind]
        units[name] = SimpleNamespace(
            name=name,
            kind=kind,
            source=source,
            lanes_in=lanes_in,
            blocks_in=planes_in,
            planes_in=planes_in,
            planes=planes_out,
            segs=segs,
            tiles=tile,
            rows=rows,
            stat=stat,
            depth=1 if kind == "p1" else 3,
        )
        stat += tile

    add("a", "s1", "h", 256, planes, planes, [(operations[0], 256, None)])
    add("b", "s1", "u", 256, planes, planes, [(operations[1], 256, None)])
    ups = [operation for operation in operations if operation.taps == 1]
    if ups:
        add("u", "p1", "t", 256, planes, planes, [(operation, 256, None) for operation in ups])
    firsts, chains = [], {}
    for target in range(k + 1, 4):
        steps = [
            operation
            for operation in operations
            if operation.taps == 3 and operation.stride == 2
        ]
        start = sum(i - k for i in range(k + 1, target))
        chains[target] = steps[start : start + target - k]
        if target == k + 1:
            firsts.append((chains[target][0], 256, None))
        else:
            firsts.append((chains[target][0], LANES, "c1" if target == k + 2 else "c2"))
    if firsts:
        add("d", "s2", "t", 256, planes, planes // 2, firsts)
    if k <= 1:
        add("e", "s2", "c1", LANES, planes // 2, planes // 4, [(chains[k + 2][1], 256, None)])
    if k == 0:
        add("f", "s2", "c2", LANES, planes // 2, planes // 4, [(chains[3][1], LANES, "c3")])
        add("g", "s2", "c3", LANES, planes // 4, planes // 8, [(chains[3][2], 256, None)])
    return units


def links(k, unit, seg):
    cin = seg.cin
    count_in, count_out = unit.blocks_in, seg.blocks
    found = []
    if unit.kind == "p1":
        for plane in range(count_in):
            wide = 1 << seg.up
            found.append((plane * cin, 0, set(range(plane * wide, plane * wide + wide))))
        return found
    if unit.kind == "s1" and k == 3:
        return [(256 * tap, tap, {0}) for tap in range(3)]
    stride = 1 if unit.kind == "s1" else 2
    for plane in range(count_in):
        for tap in range(3):
            at = plane - tap + 1
            if at % stride == 0 and 0 <= at // stride < count_out:
                found.append((plane * cin, tap, {at // stride}))
    if stride == 1:
        found.append((256, 2, {count_out - 1}))
        found.append((unit.rows - cin, 0, {0}))
    else:
        lanes_in = unit.lanes_in
        found.append((lanes_in + (count_in - 1) * cin - (lanes_in - LANES), 0, {0}))
    return found


def message_slot(k, other):
    return sum(2 * (8 >> max(k, before)) for before in range(other) if before != k)


def log2(value):
    return value.bit_length() - 1


def sigmoid_of(value):
    return 0.5 * jnp.tanh(0.5 * value) + 0.5


def silu_of(value):
    return value * sigmoid_of(value)


def slope_of(value):
    sigmoid = sigmoid_of(value)
    return sigmoid * (1.0 + value * (1.0 - sigmoid))


def planes_loop(count, body, turns=1):
    def step(index, carry):
        for turn in range(turns):
            body(index * turns + turn)
        return carry

    turns = min(turns, count)
    if count == turns:
        for index in range(count):
            body(index)
    else:
        lax.fori_loop(0, count // turns, step, 0)


def planes_sum(count, body, initial, turns=1):
    def step(index, carry):
        for turn in range(turns):
            carry = body(index * turns + turn, carry)
        return carry

    turns = min(turns, count)
    if count == turns:
        return step(0, initial)
    return lax.fori_loop(0, count // turns, step, initial)


def partial_sum(value):
    rows = value.shape[0]
    return jnp.sum(value.reshape(rows // 8, 8, value.shape[1]), axis=0)


class Planes:
    def __init__(self, mode, tiles, planes, masks, rows, main, edge=None, right=None, narrow=False):
        self.narrow, self.pending = narrow, {}
        self.mode, self.tiles, self.planes = mode, tiles, planes
        self.masks, self.rows = masks, rows
        self.main, self.edge, self.right = main, edge, right
        self.base = 1 if mode in ("s1", "wide", "s2") else 0
        extra = {"s1": 2, "wide": 2, "s2": 1, "dz2": 1, "p": 0}[mode]
        self.span = planes + extra
        self.unit = tiles * self.span

    def at(self, m, tile, plane):
        return m * self.unit + tile * self.span + plane + self.base

    def edge_at(self, m, tile, plane):
        if self.mode == "s2" or self.narrow:
            return m * self.span + plane + self.base
        return self.at(m, tile, plane)

    def from_left(self, value):
        return pltpu.roll(value, 1, 0) * self.masks[1]

    def from_right(self, value):
        return pltpu.roll(value, self.rows - 1, 0) * self.masks[2]

    def store(self, m, tile, plane, value):
        self.put(m, tile, plane, value)
        if isinstance(plane, int):
            if plane == self.planes - 1:
                self.put_above(m, tile, value)
            if plane == 0:
                self.put_below(m, tile, value)

    def put(self, m, tile, plane, value):
        where = self.at(m, tile, plane)
        self.main[where] = value.astype(jnp.bfloat16)
        if self.mode == "s1":
            side = self.from_right(value) if tile == 0 else self.from_left(value)
            if not self.narrow:
                self.edge[where] = side.astype(jnp.bfloat16)
            elif tile == 0:
                self.pending[plane if isinstance(plane, int) else self.span] = side
            else:
                lane = lax.broadcasted_iota(jnp.int32, side.shape, 1)
                other = self.pending.pop(plane if isinstance(plane, int) else self.span)
                side = jnp.where(lane < LANES // 2, other, side)
                self.edge[self.edge_at(m, tile, plane)] = side.astype(jnp.bfloat16)
        elif self.mode == "wide":
            self.edge[where] = self.from_left(value).astype(jnp.bfloat16)
            self.right[where] = self.from_right(value).astype(jnp.bfloat16)
        elif self.mode == "s2":
            if tile == self.tiles - 1:
                self.edge[self.edge_at(m, tile, plane)] = self.from_left(value).astype(jnp.bfloat16)
        elif self.mode == "dz2":
            self.edge[where] = self.from_right(value).astype(jnp.bfloat16)

    def put_above(self, m, tile, last):
        if self.mode in ("s1", "wide", "s2"):
            above = pltpu.roll(last, 6, 0) * self.masks[3] + pltpu.roll(last, 3, 0) * self.masks[4]
            self.put(m, tile, -1, above)

    def put_below(self, m, tile, first):
        if self.mode in ("s1", "wide", "dz2"):
            rows = self.rows
            below = (
                pltpu.roll(first, rows - 6, 0) * self.masks[5]
                + pltpu.roll(first, rows - 3, 0) * self.masks[6]
            )
            self.put(m, tile, self.planes, below)

    def close(self, m):
        for tile in range(self.tiles):
            last = self.main[self.at(m, tile, self.planes - 1)].astype(jnp.float32)
            self.put_above(m, tile, last)
        for tile in range(self.tiles):
            first = self.main[self.at(m, tile, 0)].astype(jnp.float32)
            self.put_below(m, tile, first)


class Branch:
    def __init__(self, k, rows, large, small, share, refs, masks, core):
        self.k, self.rows, self.refs, self.masks = k, rows, refs, masks
        self.units = unit_table(k)
        self.planes = 8 >> k
        self.core = core
        self.large, self.small, self.count = large, small, large + small
        self.cells = (small * (SH // 8) * (SW // 8), large * (LH // 8) * (LW // 8))
        self.quarter = lax.axis_index("crops") // 2
        self.share = share
        r = refs
        make = partial(Planes, masks=masks, rows=rows)
        make_one = partial(make, narrow=k <= 1)
        one = "wide" if k == 3 else "s1"
        self.maps = dict(
            h=make_one(one, 2, self.planes, main=r.hC, edge=r.hE, right=r.hR),
            u=make_one(one, 2, self.planes, main=r.uC, edge=r.uE, right=r.uR),
            t=make("p" if k == 3 else "s2", 2, self.planes, main=r.tC, edge=r.tE),
        )
        if k <= 1:
            self.maps["c1"] = make("s2", 1, self.planes // 2, main=r.c1C, edge=r.c1E)
        if k == 0:
            self.maps["c2"] = make("s2", 1, 4, main=r.c2C, edge=r.c2E)
            self.maps["c3"] = make("s2", 1, 2, main=r.c3C, edge=r.c3E)
        self.grads = dict(t=r.gt, u=r.gu, c1=r.gc1, c2=r.gc2, c3=r.gc3)

    def lane_block(self, shape, cout):
        lanes = lax.broadcasted_iota(jnp.int32, shape, 1)
        return lanes >> log2(cout)

    def keep(self, value, cout, which):
        count = LANES // cout
        if len(which) == count:
            return value
        block = self.lane_block(value.shape, cout)
        mask = block == which[0]
        for entry in which[1:]:
            mask = mask | (block == entry)
        return jnp.where(mask, value, 0.0)

    def spread(self, value, cout):
        shift = LANES // 2
        while shift >= cout:
            value = value + pltpu.roll(value, shift, 1)
            shift //= 2
        return value

    def local_blocks(self, seg, tile, wanted):
        count = LANES // seg.cout
        return [q for q in range(count) if (tile * count + q) % seg.blocks in wanted]


    def segments(self):
        return [(unit, seg) for unit in self.units.values() for seg in unit.segs]

    def pieces(self):
        found, place = [], 0
        for index, (unit, seg) in enumerate(self.segments()):
            count = 2 * seg.taps**2 * seg.cin * seg.cout // LANES
            if self.k < 3:
                found.append((index, 0, count, place, index))
                place += count
            else:
                for d in range(unit.depth):
                    slot = len(found) % 3
                    found.append((index, d, count // unit.depth, slot * 3072, slot))
        return found

    def fetch(self, at):
        r = self.refs
        index, d, count, place, sem = self.pieces()[at]
        _, seg = self.segments()[index]
        return pltpu.make_async_copy(
            r.w.at[pl.ds(2 * seg.off + d * count, count)],
            r.raw.at[pl.ds(place, count)],
            r.wsem.at[sem],
        )

    def fetch_first(self):
        for at in range(len(self.pieces()) if self.k < 3 else 3):
            self.fetch(at).start()

    def expand(self, index):
        unit, seg = self.segments()[index]
        pieces = self.pieces()
        mine = [at for at, piece in enumerate(pieces) if piece[0] == index]
        if self.k < 3:
            (at,) = mine
            self.fetch(at).wait()
            count = pieces[at][2] // unit.depth
            planes_loop(
                unit.depth,
                lambda d: self.expand_row(unit, seg, d, count, pieces[at][3] + d * count),
            )
        else:
            for d, at in enumerate(mine):
                self.fetch(at).wait()
                self.expand_row(unit, seg, d, pieces[at][2], pieces[at][3])
                if at + 3 < len(pieces):
                    self.fetch(at + 3).start()
        for m in range(MODULES):
            self.spread_tables(m, unit, seg)

    def expand_row(self, unit, seg, d, count, place):
        r = self.refs
        chunk = math.gcd(count, 384)
        wf, rep = r.work, r.rep

        def widen(step):
            at = pl.multiple_of(step * chunk, 16)
            value = r.raw[pl.ds(pl.multiple_of(place + at, 16), chunk)].astype(jnp.float32)
            wf[pl.ds(at, chunk)] = value

        planes_loop(count // chunk, widen)
        count = count // MODULES
        depth, cin, cout = unit.depth, seg.cin, seg.cout
        target = getattr(r, "T" + unit.name)
        twice = unit.kind == "s1" and self.k < 3
        across = getattr(r, "T" + unit.name + unit.name) if twice else None
        by_row = {}
        for row, tap, wanted in links(self.k, unit, seg):
            by_row.setdefault(row, []).append((tap, wanted))

        def module(m):
            if cout < LANES:
                ratio = LANES // cout
                flat = wf[pl.ds(m, count, stride=2)]
                for part in range(ratio):
                    rep[pl.ds(part, count, stride=ratio)] = self.spread(
                        self.keep(flat, cout, [part]), cout
                    )

            def tap_rows(tap, tile):
                if cout < LANES:
                    return rep[tap * cin : (tap + 1) * cin]
                if cout == LANES:
                    return wf[pl.ds(m + tap * (2 * cin), cin, stride=2)]
                return wf[pl.ds(m + tap * (4 * cin) + 2 * tile, cin, stride=4)]

            def place(goal, taps_at, width, column, tile):
                made = {}
                for row in range(0, unit.rows, cin):
                    key = []
                    for tap, wanted in by_row.get(row, []):
                        local = self.local_blocks(seg, tile, wanted) if width <= LANES else [0]
                        if local:
                            key.append((tap, tuple(local)))
                    key = tuple(key)
                    if key not in made:
                        total = None
                        for tap, local in key:
                            piece = taps_at[tap]
                            if width <= LANES:
                                piece = self.keep(piece, width, local)
                            total = piece if total is None else total + piece
                        if total is None:
                            total = jnp.zeros((cin, LANES), jnp.float32)
                        made[key] = total.astype(jnp.bfloat16)
                    goal[m * depth + d, row : row + cin, column : column + LANES] = made[key]

            width = 3 if seg.taps == 3 else 1
            for tile in range(seg.tiles):
                if tile == 0 or cout > LANES:
                    taps_at = [tap_rows(tap, tile) for tap in range(width)]
                place(target, taps_at, cout, (seg.tile + tile) * LANES, tile)
            if not twice:
                return
            turned = []
            if cin == LANES:
                turned = [jnp.transpose(tap_rows(tap, 0)) for tap in range(3)]
            else:
                both = jnp.transpose(rep[0 : -(-3 * cin // LANES) * LANES])
                for tap in range(3):
                    first = tap * cin // LANES * LANES
                    value = both[0:cin, first : first + LANES]
                    value = self.keep(value, cin, [tap * cin % LANES // cin])
                    turned.append(self.spread(value, cin))
            for tile in range(2):
                place(across, turned[::-1], cin, tile * LANES, tile)

        planes_loop(MODULES, module)


    def parts(self, unit, source):
        if unit.kind == "p1":
            return [(source.main, range(2), source.at)]
        if source.mode == "wide":
            return [
                (source.edge, range(2), source.at),
                (source.main, range(2), source.at),
                (source.right, range(2), source.at),
            ]
        if unit.kind == "s1":
            tiles = [0] if source.narrow else range(2)
            return [(source.main, range(2), source.at), (source.edge, tiles, source.edge_at)]
        last = source.tiles - 1
        return [
            (source.main, range(source.tiles), source.at),
            (source.edge, [last], source.edge_at),
        ]

    def rows_of(self, unit, part, m, d, first, count):
        ref, tiles, at = part
        pieces = []
        for tile in tiles:
            if unit.kind == "s2":
                rows = [ref[at(m, tile, 2 * (first + q) + d - 1)] for q in range(count)]
                pieces.append(rows[0] if count == 1 else jnp.concatenate(rows, axis=0))
            else:
                shift = d - 1 if unit.kind == "s1" else 0
                pieces.append(
                    ref[pl.ds(at(m, tile, first + shift), count)].reshape(count * self.rows, LANES)
                )
        return pieces

    def conv(self, m, unit):
        r = self.refs
        source = self.maps[unit.source]
        target = getattr(r, "T" + unit.name)
        z = getattr(r, "z" + unit.name)
        planes, tiles, depth = unit.planes, unit.tiles, unit.depth
        chunk = min(planes, 4 if tiles <= 2 else 2)
        lanes = tiles * LANES

        def body(step, sums):
            first = step * chunk
            pieces = []
            for d in range(depth):
                for part in self.parts(unit, source):
                    pieces += self.rows_of(unit, part, m, d, first, chunk)
            left = jnp.concatenate(pieces, axis=1)
            right = target[pl.ds(m * depth, depth), 0 : unit.rows, 0:lanes]
            right = right.reshape(depth * unit.rows, lanes)
            result = lax.dot_general(left, right, DOWN, preferred_element_type=jnp.float32)
            for tile in range(tiles):
                block = result[:, tile * LANES : (tile + 1) * LANES]
                z[pl.ds(m * tiles * planes + tile * planes + first, chunk)] = block.reshape(
                    chunk, self.rows, LANES
                )
            return (sums[0] + partial_sum(result), sums[1] + partial_sum(result * result))

        zero = jnp.zeros((8, lanes), jnp.float32)
        sums = planes_sum(planes // chunk, body, (zero, zero), 2)
        for seg in unit.segs:
            scale = self.per_cell(unit, seg)
            totals = self.fold(seg, sums)
            self.norm_rows(m, unit, seg, totals, scale)

    def per_cell(self, unit, seg):
        blocks = seg.tiles * LANES // seg.cout
        small, large = self.cells
        count = unit.planes * blocks
        return jnp.where(self.core == 0, 1.0 / (large * count), 1.0 / (small * count)).astype(
            jnp.float32
        )

    def fold(self, seg, sums):
        first = seg.tile
        found = []
        for value in sums:
            tiles = [
                value[:, (first + t) * LANES : (first + t + 1) * LANES] for t in range(seg.tiles)
            ]
            if seg.cout <= LANES:
                total = tiles[0]
                for tile in tiles[1:]:
                    total = total + tile
                total = jnp.sum(self.spread(total, seg.cout), axis=0, keepdims=True)
                found.append([total] * seg.tiles)
            else:
                found.append([jnp.sum(tile, axis=0, keepdims=True) for tile in tiles])
        return found

    def table_row(self, ref, m, seg, tile):
        slot = seg.slot
        if seg.cout > LANES:
            return ref[m, slot : slot + 1, tile * LANES : (tile + 1) * LANES]
        row = jnp.broadcast_to(ref[m, slot : slot + 1, 0:LANES], (8, LANES))
        if seg.cout < LANES:
            row = self.spread(self.keep(row, seg.cout, [0]), seg.cout)
        return row[0:1]

    def norm_rows(self, m, unit, seg, totals, scale):
        st = self.refs.st
        for tile in range(seg.tiles):
            average = totals[0][tile] * scale
            variance = totals[1][tile] * scale - average * average
            inverse = lax.rsqrt(variance + EPS)
            where = m * STATS + unit.stat + seg.tile + tile
            factor = st[where, 4:5] * inverse
            st[where, 0:1] = average
            st[where, 1:2] = inverse
            st[where, 2:3] = factor
            st[where, 3:4] = st[where, 5:6] - average * factor

    def spread_tables(self, m, unit, seg):
        st = self.refs.st
        for tile in range(seg.tiles):
            where = m * STATS + unit.stat + seg.tile + tile
            st[where, 4:5] = self.table_row(self.refs.gains, m, seg, tile)
            st[where, 5:6] = self.table_row(self.refs.shifts, m, seg, tile)

    def normed(self, m, unit, tile, plane):
        st = self.refs.st
        z = getattr(self.refs, "z" + unit.name)
        where = m * STATS + unit.stat + tile
        value = z[m * unit.tiles * unit.planes + tile * unit.planes + plane]
        return value * st[where, 2:3] + st[where, 3:4]

    def apply_a(self, m):
        unit, u = self.units["a"], self.maps["u"]

        def body(plane):
            for tile in range(2):
                value = silu_of(self.normed(m, unit, tile, plane)) * self.masks[0]
                u.store(m, tile, plane, value)

        planes_loop(self.planes, body, TURNS)

    def apply_b(self, m):
        unit, top = self.units["b"], self.maps["t"]
        hf, s = self.refs.hf, self.refs.s

        def body(plane):
            for tile in range(2):
                where = m * 2 * self.planes + tile * self.planes + plane
                value = silu_of(self.normed(m, unit, tile, plane) + hf[where]) * self.masks[0]
                s[where] = value
                top.store(m, tile, plane, value)

        planes_loop(self.planes, body, TURNS)

    def apply_rest(self, m, unit):
        sb = self.refs.sb
        for seg in unit.segs:
            chain = self.maps[seg.chain] if seg.chain else None

            def body(plane):
                for tile in range(seg.tiles):
                    value = self.normed(m, unit, seg.tile + tile, plane)
                    if chain is not None:
                        chain.store(m, tile, plane, silu_of(value) * self.masks[0])
                    else:
                        at = message_slot(self.k, seg.dest) + tile * unit.planes + plane
                        sb[at] = value.astype(jnp.bfloat16)

            planes_loop(unit.planes, body, TURNS)
            if chain is None:
                self.message(m, seg.dest).start()

    def message(self, e, other):
        count = 2 * (8 >> max(self.k, other))
        r = self.refs
        return pltpu.make_async_remote_copy(
            src_ref=r.sb.at[pl.ds(message_slot(self.k, other), count)],
            dst_ref=r.rb.at[pl.ds(e * 16 + message_slot(other, self.k), count)],
            send_sem=r.ssem.at[e * 4 + other],
            recv_sem=r.rsem.at[e * 4 + self.k],
            device_id=dict(branch=other),
            device_id_type=pl.DeviceIdType.MESH,
        )

    def arrived(self, e, other):
        count = 2 * (8 >> max(self.k, other))
        r = self.refs
        at = message_slot(self.k, other)
        return pltpu.make_async_remote_copy(
            src_ref=r.sb.at[pl.ds(at, count)],
            dst_ref=r.rb.at[pl.ds(e * 16 + at, count)],
            send_sem=r.ssem.at[e * 4 + other],
            recv_sem=r.rsem.at[e * 4 + other],
            device_id=dict(branch=other),
            device_id_type=pl.DeviceIdType.MESH,
        )

    def others(self):
        return [other for other in range(4) if other != self.k]

    def sent(self, e):
        for other in self.others():
            self.message(e, other).wait_send()

    def receive(self, m):
        r = self.refs
        s, rb, hf, out = r.s, r.rb, r.hf, r.outs
        h = self.maps["h"]

        def total_at(tile, plane):
            where = m * 2 * self.planes + tile * self.planes + plane
            total = s[where]
            for other in self.others():
                count = 8 >> max(self.k, other)
                at = plane >> max(0, other - self.k)
                slot = m * 16 + message_slot(self.k, other) + tile * count + at
                total = total + rb[slot].astype(jnp.float32)
            s[where] = total
            return silu_of(total) * self.masks[0]

        def onward(plane):
            for tile in range(2):
                value = total_at(tile, plane)
                hf[(2 + tile) * self.planes + plane] = value
                h.store(1, tile, plane, value)

        def finish(plane):
            for tile in range(2):
                out[tile * self.planes + plane] = total_at(tile, plane).astype(jnp.bfloat16)

        @pl.when(m + 1 < MODULES)
        def _():
            planes_loop(self.planes, onward, TURNS)

        @pl.when(m + 1 == MODULES)
        def _():
            planes_loop(self.planes, finish, TURNS)

    def take_feature(self, tile, plane, value):
        self.refs.hf[tile * self.planes + plane] = value
        self.maps["h"].store(0, tile, plane, value)

    def take_cotangent(self, tile, plane, value):
        self.refs.gin[tile * self.planes + plane] = value

    def member(self, kind, order):
        kinds = self.refs.kinds
        found, before = jnp.int32(0), jnp.int32(0)
        for at in range(self.count):
            same = kinds[at] == kind
            found = jnp.where(same & (before == order), at, found)
            before = before + same.astype(jnp.int32)
        return found

    def order(self, device):
        kinds = self.refs.kinds
        kind = kinds[device]
        before = jnp.int32(0)
        for at in range(self.count):
            before = before + ((kinds[at] == kind) & (at < device)).astype(jnp.int32)
        return before

    def unpack(self, t, consume):
        r = self.refs
        work, rows, planes = r.work, self.rows, self.planes
        full = SH * SW * C0 // LANES
        gath = r.gathc if t else r.gathx

        @pl.when(self.core == 0)
        def _():
            for at in range(self.large):
                block = gath[self.member(1, at)]
                work[at * ROWS : (at + 1) * ROWS] = block.astype(jnp.float32)

        @pl.when(self.core == 1)
        def _():
            for at in range(self.small):
                block = gath[self.member(0, at), 0:full]
                work[at * full : (at + 1) * full] = block.astype(jnp.float32)
            work[self.small * full : self.large * ROWS] = jnp.zeros(
                (self.large * ROWS - self.small * full, LANES), jnp.float32
            )

        deep = self.large * ROWS // 2
        right = jnp.concatenate([work[pl.ds(j, deep, stride=2)] for j in range(2)], axis=1)
        right = right.astype(jnp.bfloat16)
        cells = Cells(self.core, (rows, LANES), self.small, self.large)
        base = cells.crop * cells.pick(ROWS // 2, full // 2)
        base = base + cells.along * (planes * cells.wide) + cells.across
        base = jnp.where(cells.valid, base, -(1 << 20))
        lane = lax.broadcasted_iota(jnp.int32, (rows, LANES), 1)
        chunk = min(planes, 4)

        def body(step):
            pieces = []
            for q in range(chunk):
                goal = base + (step * chunk + q) * cells.wide
                pieces.append(one_hot(goal, lane, deep))
            left = pieces[0] if chunk == 1 else jnp.concatenate(pieces, axis=0)
            result = lax.dot_general(left, right, DOWN, preferred_element_type=jnp.float32)
            for q in range(chunk):
                for tile in range(2):
                    value = result[q * rows : (q + 1) * rows, tile * LANES : (tile + 1) * LANES]
                    consume(tile, step * chunk + q, value)

        planes_loop(planes // chunk, body)

    def pack_size(self):
        return 48 * self.planes, -(-self.planes * self.rows // LANES) * LANES

    def plan_pack(self):
        r = self.refs
        high, deep = self.pack_size()
        planes = self.planes
        q = lax.broadcasted_iota(jnp.int32, (high, LANES), 0)
        lane = lax.broadcasted_iota(jnp.int32, (high, LANES), 1)
        wide, tall = jnp.where(self.core == 0, 6, 3), jnp.where(self.core == 0, 8, 4)
        cell = jnp.where(self.core == 0, (q * 43691) >> 18, (q * 43691) >> 17)
        across = q - cell * wide
        plane = cell & (planes - 1)
        along = cell >> log2(planes)
        base = plane * self.rows + along * wide + across
        base = jnp.where(along < tall, base, -(1 << 20))
        shard = lax.axis_index("crops")
        for at, device in enumerate((shard, shard + 1 - 2 * self.core)):
            goal = base + self.order(device) * (wide * tall)
            r.hot[at, 0:high, 0:deep] = one_hot(goal, lane, deep)

    def pack(self, units, put, after=None):
        high, deep = self.pack_size()
        right = jnp.concatenate([units(tile) for tile in range(2)], axis=1)
        short = deep - right.shape[0]
        parts = [right.astype(jnp.bfloat16)]
        if right.dtype == jnp.float32:
            parts.append((right - parts[0].astype(jnp.float32)).astype(jnp.bfloat16))
        if short:
            empty = jnp.zeros((short, 2 * LANES), jnp.bfloat16)
            parts = [jnp.concatenate([part, empty], axis=0) for part in parts]
        for at in (1, 0):
            total = None
            for part in parts:
                piece = lax.dot_general(
                    self.refs.hot[at, 0:high, 0:deep],
                    part,
                    DOWN,
                    preferred_element_type=jnp.float32,
                )
                total = piece if total is None else total + piece
            for tile in range(2):
                put(at, pl.ds(tile, high, stride=2), total[:, tile * LANES : (tile + 1) * LANES])
            if at and after is not None:
                after()

    def pack_outputs(self):
        r = self.refs
        high = 2 * self.pack_size()[0]

        def put(at, where, value):
            r.work[pl.ds(at * ROWS + where.start, where.size, stride=2)] = value

        def units(tile):
            block = r.outs[tile * self.planes : (tile + 1) * self.planes]
            return block.reshape(self.planes * self.rows, LANES)

        self.pack(units, put)
        for at in range(2):
            r.blocks[at, 0:high] = r.work[at * ROWS : at * ROWS + high].astype(jnp.bfloat16)
            if high < ROWS:
                r.blocks[at, high:ROWS] = jnp.zeros((ROWS - high, LANES), jnp.bfloat16)

    def pack_gradient(self, after):
        r = self.refs
        high = 2 * self.pack_size()[0]

        def put(at, where, value):
            r.slopes[at, where] = value

        def units(tile):
            block = r.gin[tile * self.planes : (tile + 1) * self.planes]
            return block.reshape(self.planes * self.rows, LANES)

        if high < ROWS:
            for at in range(2):
                r.slopes[at, high:ROWS] = jnp.zeros((ROWS - high, LANES), jnp.float32)
        self.pack(units, put, after)

    def forward(self, m, gather):
        def also(module, step):
            pl.when(m == module)(lambda: gather.step(1, step))

        self.conv(m, self.units["a"])
        self.apply_a(m)
        self.conv(m, self.units["b"])
        self.apply_b(m)
        also(1, 2)

        @pl.when(m > 0)
        def _():
            self.sent(m - 1)

        for name in ("d", "u", "e", "f", "g"):
            if name in self.units:
                self.conv(m, self.units[name])
                self.apply_rest(m, self.units[name])
        also(0, 1)
        also(1, 3)

        @pl.when(m == MODULES - 1)
        def _():
            gather.collect(1)
            self.unpack(1, self.take_cotangent)

        for other in self.others():
            self.arrived(m, other).wait_recv()
        self.receive(m)


    def send_back(self, m):
        r = self.refs
        s, gin, gt, sb = r.s, r.gin, r.gt, r.sb
        e = MODULES + m

        def body(plane):
            for tile in range(2):
                at = tile * self.planes + plane
                value = gin[at] * slope_of(s[m * 2 * self.planes + at])
                gt[at] = value
                for other in range(self.k):
                    sb[message_slot(self.k, other) + at] = value.astype(jnp.bfloat16)

        planes_loop(self.planes, body, TURNS)
        for other in reversed(self.others()):
            if other > self.k:
                count = 8 >> other
                wide = 1 << (other - self.k)

                def pool(plane):
                    for tile in range(2):
                        total = gt[tile * self.planes + plane * wide]
                        for step in range(1, wide):
                            total = total + gt[tile * self.planes + plane * wide + step]
                        slot = message_slot(self.k, other) + tile * count + plane
                        sb[slot] = total.astype(jnp.bfloat16)

                planes_loop(count, pool, TURNS)
            self.message(e, other).start()

    def back_unit(self, m, unit):
        r = self.refs
        st, dyb, z = r.st, r.dyb, getattr(r, "z" + unit.name)
        name, planes, tiles = unit.name, unit.planes, unit.tiles
        e = MODULES + m
        sums = {}

        def upstream(seg, tile, plane, normed):
            at = tile * planes + plane
            if name == "b":
                hf = r.hf[m * 2 * planes + at]
                value = r.gt[at] * slope_of(normed + hf)
                r.gin[at] = value
                return value
            if name == "a":
                return r.gu[at] * slope_of(normed)
            if seg.chain:
                return self.grads[seg.chain][at] * slope_of(normed)
            return r.rb[e * 16 + message_slot(self.k, seg.dest) + at].astype(jnp.float32)

        for seg in unit.segs:

            def body(plane, carry):
                result = []
                for tile in range(seg.tiles):
                    at = (seg.tile + tile) * planes + plane
                    where = m * STATS + unit.stat + seg.tile + tile
                    value = z[m * tiles * planes + at]
                    normed = value * st[where, 2:3] + st[where, 3:4]
                    dy = upstream(seg, tile, plane, normed)
                    dyb[at] = dy
                    zhat = (value - st[where, 0:1]) * st[where, 1:2]
                    result.append(carry[2 * tile] + partial_sum(dy))
                    result.append(carry[2 * tile + 1] + partial_sum(dy * zhat))
                return tuple(result)

            zero = jnp.zeros((8, LANES), jnp.float32)
            found = planes_sum(planes, body, (zero,) * (2 * seg.tiles), TURNS)
            pair = [
                jnp.concatenate([found[2 * tile + which] for tile in range(seg.tiles)], axis=1)
                for which in range(2)
            ]
            plain = SimpleNamespace(**vars(seg))
            plain.tile = 0
            totals = self.fold(plain, pair)
            self.table_grads(m, seg, totals)
            sums[seg.slot] = totals
        dz = self.dz_planes(unit)
        for seg in unit.segs:
            scale = self.per_cell(unit, seg)
            totals = sums[seg.slot]

            def apply(plane):
                for tile in range(seg.tiles):
                    at = (seg.tile + tile) * planes + plane
                    where = m * STATS + unit.stat + seg.tile + tile
                    zhat = (z[m * tiles * planes + at] - st[where, 0:1]) * st[where, 1:2]
                    inner = dyb[at] - totals[0][tile] * scale - zhat * (totals[1][tile] * scale)
                    dz.store(0, seg.tile + tile, plane, inner * st[where, 2:3] * self.masks[0])

            planes_loop(planes, apply, TURNS)
        self.back_data(m, unit, dz)
        first = min(seg.off for seg in unit.segs)
        last = max(seg.off + seg.taps**2 * seg.cin * seg.cout // LANES for seg in unit.segs)
        wanted = (self.quarter * self.share < last) & ((self.quarter + 1) * self.share > first)

        @pl.when(wanted)
        def _():
            self.back_kernel(m, unit, dz)

    def dz_planes(self, unit):
        r = self.refs
        mode = {"p1": "p", "s2": "dz2", "s1": "wide" if self.k == 3 else "s1"}[unit.kind]
        return Planes(
            mode,
            unit.tiles,
            unit.planes,
            self.masks,
            self.rows,
            r.dC,
            r.dE,
            r.dR,
            self.k <= 1 and unit.kind == "s1",
        )

    def table_grads(self, m, seg, totals):
        gg = self.refs.gg
        slot = seg.slot
        for which, found in ((0, totals[1]), (1, totals[0])):
            if seg.cout > LANES:
                for tile in range(2):
                    gg[m, which, slot : slot + 1, tile * LANES : (tile + 1) * LANES] = found[tile]
            else:
                row = jnp.broadcast_to(found[0], (8, LANES))
                if seg.cout < LANES:
                    row = self.keep(row, seg.cout, [0])
                gg[m, which, slot : slot + 1, 0:LANES] = row[0:1]

    def wide_rows(self, ref, at, tiles, plane, count):
        pieces = [
            ref[pl.ds(at(0, tile, plane), count)].reshape(count * self.rows, LANES)
            for tile in range(tiles)
        ]
        return pieces[0] if tiles == 1 else jnp.concatenate(pieces, axis=1)

    def back_data(self, m, unit, dz):
        r = self.refs
        kind, tiles = unit.kind, unit.tiles
        target = getattr(r, "T" + unit.name)
        lanes = tiles * LANES
        rows = self.rows

        def kernel_rows(d, first, count):
            return target[m * unit.depth + d, first : first + count, 0:lanes]

        def product(left, right):
            return lax.dot_general(left, right, ACROSS, preferred_element_type=jnp.float32)

        def put(ref, tile, planes, first, count, value, step=1, add=False):
            block = value.reshape(count, rows, LANES)
            for q in range(count):
                at = tile * planes + first + q * step
                ref[at] = ref[at] + block[q] if add else block[q]

        planes = unit.planes
        if kind == "s1":
            goal = r.gu if unit.name == "b" else r.gin
            add = unit.name == "a"
            chunk = min(planes, 4)
            across = getattr(r, "T" + unit.name + unit.name)

            def body(step):
                first = step * chunk
                if self.k == 3:
                    total = None
                    for d in range(3):
                        for ref, at in ((dz.right, 0), (dz.main, 256), (dz.edge, 512)):
                            left = self.wide_rows(ref, dz.at, 2, first + 1 - d, chunk)
                            piece = product(left, kernel_rows(d, at, 256))
                            total = piece if total is None else total + piece
                else:
                    narrow = 1 if dz.narrow else 2
                    left = []
                    for d in range(3):
                        at = first + 1 - d
                        left.append(self.wide_rows(dz.main, dz.at, 2, at, chunk))
                        left.append(self.wide_rows(dz.edge, dz.edge_at, narrow, at, chunk))
                    right = across[pl.ds(m * 3, 3), 0 : unit.rows].reshape(3 * unit.rows, 256)
                    total = lax.dot_general(
                        jnp.concatenate(left, axis=1),
                        right,
                        DOWN,
                        preferred_element_type=jnp.float32,
                    )
                for tile in range(2):
                    put(
                        goal,
                        tile,
                        planes,
                        first,
                        chunk,
                        total[:, tile * LANES : (tile + 1) * LANES],
                        add=add,
                    )

            planes_loop(planes // chunk, body, 2)
            return
        if kind == "p1":
            left = self.wide_rows(dz.main, dz.at, tiles, 0, planes)
            total = product(left, kernel_rows(0, 0, 256))
            for tile in range(2):
                put(
                    r.gt,
                    tile,
                    planes,
                    0,
                    planes,
                    total[:, tile * LANES : (tile + 1) * LANES],
                    add=True,
                )
            return
        goal = self.grads[unit.source]
        add = unit.source == "t"
        lanes_in = unit.lanes_in
        count_in = unit.planes_in
        for parity, terms in ((0, [(1, 0)]), (1, [(2, 0), (0, 1)])):
            total, side = None, None
            for d, offset in terms:
                left = self.wide_rows(dz.main, dz.at, tiles, offset, planes)
                piece = product(left, kernel_rows(d, 0, lanes_in))
                total = piece if total is None else total + piece
                left = self.wide_rows(dz.edge, dz.at, tiles, offset, planes)
                piece = product(left, kernel_rows(d, lanes_in, LANES))
                side = piece if side is None else side + piece
            for tile in range(lanes_in // LANES):
                value = total[:, tile * LANES : (tile + 1) * LANES]
                if tile == lanes_in // LANES - 1:
                    value = value + side
                put(goal, tile, count_in, parity, planes, value, step=2, add=add)

    def back_kernel(self, m, unit, dz):
        r = self.refs
        G, rep, wgv = r.work, r.rep, r.wgv
        tiles, planes = unit.tiles, unit.planes
        source = self.maps[unit.source]
        right = self.wide_rows(dz.main, dz.at, tiles, 0, planes)

        def gather(d):
            at = 0
            for part in self.parts(unit, source):
                pieces = self.rows_of(unit, part, m, d, 0, planes)
                left = pieces[0] if len(pieces) == 1 else jnp.concatenate(pieces, axis=1)
                count = left.shape[1]
                result = lax.dot_general(left, right, ALONG, preferred_element_type=jnp.float32)
                for tile in range(tiles):
                    row = pl.multiple_of((d * tiles + tile) * unit.rows + at, 8)
                    G[pl.ds(row, count)] = result[:, tile * LANES : (tile + 1) * LANES]
                at += count

        if self.k == 3 and unit.kind == "s1":
            self.direct_kernel(m, unit, right)
            return
        planes_loop(unit.depth, gather)
        for seg in unit.segs:
            self.fold_kernel(m, unit, seg)

    def direct_kernel(self, m, unit, right):
        wgv, (seg,) = self.refs.wgv, unit.segs
        source = self.maps[unit.source]
        span = 2 * seg.cin
        low, high = self.quarter * self.share, (self.quarter + 1) * self.share

        def tap_row(d):
            first = seg.off + d * (3 * span)

            @pl.when((first < high) & (first + 3 * span > low))
            def _():
                for column, part in enumerate(self.parts(unit, source)):
                    pieces = self.rows_of(unit, part, m, d, 0, unit.planes)
                    left = jnp.concatenate(pieces, axis=1)
                    result = lax.dot_general(left, right, ALONG, preferred_element_type=jnp.float32)
                    for tile in range(2):
                        rows = pl.ds(first + column * span + tile, seg.cin, stride=2)
                        wgv[rows] = result[:, tile * LANES : (tile + 1) * LANES]

        planes_loop(unit.depth, tap_row)

    def fold_kernel(self, m, unit, seg):
        r = self.refs
        G, rep, wgv = r.work, r.rep, r.wgv
        cin, cout, tiles = seg.cin, seg.cout, unit.tiles
        width = 3 if seg.taps == 3 else 1
        found = links(self.k, unit, seg)
        off = seg.off

        def fold(d):
            for column in range(width):
                tap = d * width + column
                totals = []
                for tile in range(seg.tiles):
                    total = None
                    for row, which, wanted in found:
                        if which != column:
                            continue
                        at = pl.multiple_of((d * tiles + seg.tile + tile) * unit.rows + row, 8)
                        piece = G[pl.ds(at, cin)]
                        if cout <= LANES:
                            local = self.local_blocks(seg, tile, wanted)
                            if not local:
                                continue
                            piece = self.keep(piece, cout, local)
                        total = piece if total is None else total + piece
                    totals.append(total)
                if cout > LANES:
                    for tile in range(2):
                        wgv[pl.ds(off + tap * (2 * cin) + tile, cin, stride=2)] = totals[tile]
                    continue
                total = None
                for piece in totals:
                    if piece is not None:
                        total = piece if total is None else total + piece
                if cout == LANES:
                    wgv[pl.ds(pl.multiple_of(off + tap * cin, 8), cin)] = total
                else:
                    rep[pl.ds(pl.multiple_of(tap * cin, cin), cin)] = self.spread(total, cout)

        planes_loop(unit.depth, fold)
        if cout < LANES:
            ratio = LANES // cout
            count = width * width * cin // ratio
            total = None
            for part in range(ratio):
                piece = self.keep(rep[pl.ds(part, count, stride=ratio)], cout, [part])
                total = piece if total is None else total + piece
            wgv[off : off + count] = total

    def backward(self, m, meanwhile):
        e = MODULES + m
        last = m == MODULES - 1
        self.sent(jnp.where(last, m, e + 1))
        self.send_back(m)
        pl.when(last)(meanwhile)
        for name in ("g", "f", "e", "d", "u"):
            if name in self.units:
                for seg in self.units[name].segs:
                    if seg.dest >= 0:
                        self.arrived(e, seg.dest).wait_recv()
                self.back_unit(m, self.units[name])
        self.back_unit(m, self.units["b"])
        self.back_unit(m, self.units["a"])


STATS = 20
TURNS = 8
NAMES = list(
    dict(x=0, cot=0, w=0, gains=0, shifts=0, kinds=0, out=0, grad=0, wg=0, gain=0, shift=0)
)


def one_hot(goal, lane, deep):
    pieces = [
        jnp.where(goal == lane + first, 1.0, 0.0).astype(jnp.bfloat16)
        for first in range(0, deep, LANES)
    ]
    return jnp.concatenate(pieces, axis=1)


class Cells:
    def __init__(self, core, shape, small, large):
        self.core = core
        row = lax.broadcasted_iota(jnp.int32, shape, 0)
        self.wide = self.pick(LW // 8, SW // 8)
        tall = self.pick(LH // 8, SH // 8)
        self.crop = self.pick((row * 43691) >> 21, (row * 43691) >> 19)
        inner = row - self.crop * (self.wide * tall)
        self.along = self.pick((inner * 43691) >> 18, (inner * 43691) >> 17)
        self.across = inner - self.along * self.wide
        self.valid = self.crop < self.pick(large, small)
        self.last = tall - 1

    def pick(self, large, small):
        return jnp.where(self.core == 0, large, small)


def fill_masks(refs, rows, core, small, large):
    cells = Cells(core, (rows, LANES), small, large)
    valid = cells.valid
    six = cells.wide == 6
    up, down = valid & (cells.along > 0), valid & (cells.along < cells.last)
    tables = (
        valid,
        valid & (cells.across > 0),
        valid & (cells.across < cells.wide - 1),
        up & six,
        up & jnp.logical_not(six),
        down & six,
        down & jnp.logical_not(six),
    )
    for at, table in enumerate(tables):
        refs.masks[at] = jnp.where(table, 1.0, 0.0)


class Gather:
    def __init__(self, refs, core, count):
        self.refs, self.core, self.count = refs, core, count
        self.z = lax.axis_index("crops") // 2
        self.last = count // 2 - 1

    def hop(self, t, source, right):
        r = self.refs
        at = source * 2 + self.core
        gath = r.gathc if t else r.gathx
        to = self.z + 1 if right else self.z - 1
        return pltpu.make_async_remote_copy(
            src_ref=gath.at[at],
            dst_ref=gath.at[at],
            send_sem=r.hsem.at[(t * (self.last + 1) + source) * 3 + (0 if right else 1)],
            recv_sem=r.gsem.at[t * self.count + at],
            device_id=dict(crops=to * 2 + self.core),
            device_id_type=pl.DeviceIdType.MESH,
        )

    def across(self, t, source, core, rows):
        r = self.refs
        at = source * 2 + core
        gath = r.gathc if t else r.gathx
        return pltpu.make_async_remote_copy(
            src_ref=gath.at[at, pl.ds(0, rows)],
            dst_ref=gath.at[at, pl.ds(0, rows)],
            send_sem=r.hsem.at[(t * (self.last + 1) + source) * 3 + 2],
            recv_sem=r.gsem.at[t * self.count + at],
            device_id=dict(crops=self.z * 2 + 1 - self.core),
            device_id_type=pl.DeviceIdType.MESH,
        )

    def each_core(self, action):
        for core, rows in ((0, SH * SW * C0 // LANES), (1, ROWS)):

            @pl.when(self.core == core)
            def _():
                action(core, rows)

    def send(self, t, source, rightward, leftward):
        if rightward:

            @pl.when(self.z < self.last)
            def _():
                self.hop(t, source, True).start()

        if leftward:

            @pl.when(self.z > 0)
            def _():
                self.hop(t, source, False).start()

        self.each_core(lambda core, rows: self.across(t, source, core, rows).start())

    def step(self, t, s):
        r = self.refs
        if s == 0:
            at = self.z * 2 + self.core
            if t:
                r.gathc[at] = r.cot[...]
            else:
                r.gathx[at] = r.x[...]
            self.send(t, self.z, True, True)
            return

        @pl.when(self.z >= s)
        def _():
            self.hop(t, self.z - s, True).wait_recv()
            self.send(t, self.z - s, True, False)

        @pl.when(self.z + s <= self.last)
        def _():
            self.hop(t, self.z + s, True).wait_recv()
            self.send(t, self.z + s, False, True)

    def collect(self, t):
        for source in range(self.last + 1):
            for core, rows in ((0, ROWS), (1, SH * SW * C0 // LANES)):

                @pl.when(self.core == core)
                def _():
                    self.across(t, source, 1 - core, rows).wait_recv()

    def finish(self, t):
        def sent(source, rightward, leftward):
            if rightward:

                @pl.when(self.z < self.last)
                def _():
                    self.hop(t, source, True).wait_send()

            if leftward:

                @pl.when(self.z > 0)
                def _():
                    self.hop(t, source, False).wait_send()

            self.each_core(lambda core, rows: self.across(t, source, core, rows).wait_send())

        sent(self.z, True, True)
        for s in range(1, self.last + 1):

            @pl.when(self.z >= s)
            def _():
                sent(self.z - s, True, False)

            @pl.when(self.z + s <= self.last)
            def _():
                sent(self.z + s, False, True)


def scratch_table(rows, weight_rows, count):
    def half(many):
        return pltpu.VMEM((many, rows, LANES), jnp.bfloat16)

    def full(many):
        return pltpu.VMEM((many, rows, LANES), jnp.float32)

    def expanded(depth, deep, wide):
        return pltpu.VMEM((MODULES * depth, deep, wide), jnp.bfloat16)

    _, span, low = pair_rows(weight_rows, count)
    return dict(
        masks=full(MASKS),
        hC=half(2 * 20),
        hE=half(2 * 10),
        hR=half(2 * 6),
        uC=half(2 * 20),
        uE=half(2 * 10),
        uR=half(2 * 6),
        tC=half(2 * 18),
        tE=half(2 * 9),
        c1C=half(2 * 5),
        c1E=half(2 * 5),
        c2C=half(2 * 5),
        c2E=half(2 * 5),
        c3C=half(2 * 3),
        c3E=half(2 * 3),
        dC=half(20),
        dE=half(20),
        dR=half(6),
        outs=half(16),
        hf=full(2 * 16),
        s=full(2 * 16),
        za=full(2 * 16),
        zb=full(2 * 16),
        zd=full(2 * 16),
        zu=full(2 * 8),
        ze=full(2 * 4),
        zf=full(2 * 2),
        zg=full(2 * 2),
        gt=full(16),
        gu=full(16),
        gin=full(16),
        gc1=full(4),
        gc2=full(4),
        gc3=full(2),
        dyb=full(16),
        sb=half(16),
        rb=half(4 * 16),
        st=pltpu.VMEM((MODULES * STATS, 8, LANES), jnp.float32),
        Ta=expanded(3, 768, 256),
        Tb=expanded(3, 768, 256),
        Taa=expanded(3, 512, 256),
        Tbb=expanded(3, 512, 256),
        Td=expanded(3, 384, 512),
        Tu=expanded(1, 256, 768),
        Te=expanded(3, 256, 256),
        Tf=expanded(3, 256, 128),
        Tg=expanded(3, 256, 256),
        raw=pltpu.VMEM((9408, LANES), jnp.bfloat16),
        work=pltpu.VMEM((4608, LANES), jnp.float32),
        rep=pltpu.VMEM((640, LANES), jnp.float32),
        wgv=pltpu.VMEM((weight_rows, LANES), jnp.float32),
        wq=pltpu.VMEM((MODULES, low + span, LANES), jnp.float32),
        wh=pltpu.VMEM((MODULES, low + span, LANES), jnp.bfloat16),
        wr=pltpu.VMEM((MODULES, span, LANES), jnp.bfloat16),
        gathx=pltpu.VMEM((count, ROWS, LANES), jnp.bfloat16),
        gathc=pltpu.VMEM((count, ROWS, LANES), jnp.bfloat16),
        hot=pltpu.VMEM((2, 384, 768), jnp.bfloat16),
        blocks=pltpu.VMEM((2, ROWS, LANES), jnp.bfloat16),
        slopes=pltpu.VMEM((2, ROWS, LANES), jnp.float32),
        blockr=pltpu.VMEM((ROWS, LANES), jnp.bfloat16),
        slopeh=pltpu.VMEM((ROWS, LANES), jnp.bfloat16),
        sloper=pltpu.VMEM((ROWS, LANES), jnp.bfloat16),
        gg=pltpu.VMEM((MODULES, 2, SLOTS, 256), jnp.float32),
        ggr=pltpu.VMEM((MODULES, 2, SLOTS, 256), jnp.float32),
        wsem=pltpu.SemaphoreType.DMA((8,)),
        ssem=pltpu.SemaphoreType.DMA((16,)),
        rsem=pltpu.SemaphoreType.DMA((16,)),
        hsem=pltpu.SemaphoreType.DMA((3 * count,)),
        gsem=pltpu.SemaphoreType.DMA((2 * count,)),
        psem=pltpu.SemaphoreType.DMA((5,)),
        qsem=pltpu.SemaphoreType.DMA((5,)),
        osem=pltpu.SemaphoreType.DMA((1,)),
    )


def pair_rows(weight_rows, count):
    share = weight_rows // count
    low = share // 16 * 16
    return share, -(-(2 * share - low) // 16) * 16, low


def greet(core, count):
    barrier = pltpu.get_barrier_semaphore()
    me, shard = lax.axis_index("branch"), lax.axis_index("crops")
    z = shard // 2

    def signal(**where):
        pl.semaphore_signal(barrier, inc=1, device_id=where, device_id_type=pl.DeviceIdType.MESH)

    for step in range(1, 4):
        signal(branch=lax.rem(me + step, 4))
    signal(crops=shard + 1 - 2 * core)

    @pl.when(z > 0)
    def _():
        signal(crops=shard - 2)

    @pl.when(z < count // 2 - 1)
    def _():
        signal(crops=shard + 2)

    ends = (z == 0).astype(jnp.int32) + (z == count // 2 - 1).astype(jnp.int32)
    pl.semaphore_wait(barrier, 6 - ends)


def whole_kernel(names, rows, large, small, *args):
    refs = SimpleNamespace(**dict(zip(names, args)))
    count = large + small
    me, shard = lax.axis_index("branch"), lax.axis_index("crops")
    core = shard % 2
    weight_rows = refs.wgv.shape[0]
    share, span, low = pair_rows(weight_rows, count)
    quarter = pl.multiple_of(shard // 2 * (2 * share), 8)

    class Lazy:
        def __getitem__(self, index):
            return refs.masks[index]

    def across(source, goal, index):
        return pltpu.make_async_remote_copy(
            src_ref=source,
            dst_ref=goal,
            send_sem=refs.psem.at[index],
            recv_sem=refs.qsem.at[index],
            device_id=dict(crops=shard + 1 - 2 * core),
            device_id_type=pl.DeviceIdType.MESH,
        )

    def kernel_pair(m):
        at = pl.multiple_of(low * (1 - core), 16)
        return across(refs.wh.at[m, pl.ds(at, span)], refs.wr.at[m], m)

    outputs_pair = across(refs.blocks.at[1], refs.blockr, 2)
    gradient_pair = across(refs.slopeh, refs.sloper, 3)
    table_pair = across(refs.gg, refs.ggr, 4)
    gather = Gather(refs, core, count)

    def every(action):
        for k in range(4):

            @pl.when(me == k)
            def _():
                action(Branch(k, rows, large, small, 2 * share, refs, Lazy(), core))

    def begin(branch):
        branch.fetch_first()

    def prepare(branch):
        found = branch.segments()
        first, second = ((0, 2), (1, 3), (0, 2), (0, 1))[branch.k]
        stops = {first: 1, second: 2, len(found) - 1: 3}
        for index, (unit, seg) in enumerate(found):
            branch.expand(index)
            if index in stops:
                gather.step(0, stops[index])

    def main(branch):
        branch.unpack(0, branch.take_feature)
        branch.maps["h"].close(0)
        gather.step(1, 0)

        def ahead(m, carry):
            branch.forward(m, gather)
            return carry

        def meanwhile():
            branch.plan_pack()
            branch.pack_outputs()
            outputs_pair.start()

        def back(step, carry):
            m = MODULES - 1 - step
            branch.backward(m, meanwhile)
            found = refs.wgv[pl.ds(quarter, 2 * share)]
            refs.wq[m, 0 : 2 * share] = found
            spare = jnp.zeros((low + span - 2 * share, LANES), jnp.float32)
            refs.wh[m] = jnp.concatenate([found, spare], axis=0).astype(jnp.bfloat16)
            kernel_pair(m).start()
            return carry

        lax.fori_loop(0, MODULES, ahead, 0)
        lax.fori_loop(0, MODULES, back, 0)
        branch.sent(MODULES)
        table_pair.start()

        def share_gradient():
            refs.slopeh[...] = refs.slopes[1].astype(jnp.bfloat16)
            gradient_pair.start()

        branch.pack_gradient(share_gradient)

    every(begin)
    greet(core, count)
    gather.step(0, 0)
    fill_masks(refs, rows, core, small, large)
    refs.wgv[pl.ds(quarter, 2 * share)] = jnp.zeros((2 * share, LANES), jnp.float32)
    refs.gg[...] = jnp.zeros(refs.gg.shape, jnp.float32)
    every(prepare)
    gather.collect(0)
    every(main)

    for step in range(MODULES):
        m = MODULES - 1 - step
        kernel_pair(m).wait()
        mine = refs.wq[m, pl.ds(pl.multiple_of(low * core, 8), span)]
        refs.work[pl.ds(m, span, stride=MODULES)] = mine + refs.wr[m].astype(jnp.float32)
    skip = pl.multiple_of(core * (MODULES * (share - low)), 8)
    leave = pltpu.make_async_copy(
        refs.work.at[pl.ds(skip, MODULES * share)], refs.wg, refs.osem.at[0]
    )
    leave.start()
    outputs_pair.wait()
    gradient_pair.wait()
    table_pair.wait()
    own = refs.kinds[shard] != core
    refs.out[...] = jnp.where(own, refs.blocks[0].astype(jnp.float32), refs.blockr[...].astype(jnp.float32)).astype(jnp.bfloat16)
    refs.grad[...] = jnp.where(own, refs.slopes[0], refs.sloper[...].astype(jnp.float32))
    width = 256 // count
    for which, goal in ((0, refs.gain), (1, refs.shift)):
        for m in range(MODULES):
            total = refs.gg[m, which] + refs.ggr[m, which]
            found = None
            for at in range(count):
                piece = jnp.where(shard == at, total[:, at * width : (at + 1) * width], 0.0)
                found = piece if found is None else found + piece
            goal[m] = found
    gather.finish(0)
    gather.finish(1)
    leave.wait()


def whole_call(rows, large, small, x, cot, w, gains, shifts, kinds):
    count = large + small
    weight_rows = w.shape[0] // MODULES
    table = scratch_table(rows, weight_rows, count)
    vmem = pl.BlockSpec(memory_space=pltpu.VMEM)
    hbm = pl.BlockSpec(memory_space=pl.ANY)
    smem = pl.BlockSpec(memory_space=pltpu.SMEM)
    tables = jax.ShapeDtypeStruct((MODULES, SLOTS, 256 // count), jnp.float32)
    return pl.pallas_call(
        partial(whole_kernel, NAMES + list(table), rows, large, small),
        out_shape=(
            jax.ShapeDtypeStruct((ROWS, LANES), jnp.bfloat16),
            jax.ShapeDtypeStruct((ROWS, LANES), jnp.float32),
            jax.ShapeDtypeStruct((MODULES * weight_rows // count, LANES), jnp.float32),
            tables,
            tables,
        ),
        in_specs=[vmem, vmem, hbm, vmem, vmem, smem],
        out_specs=(vmem, vmem, hbm, vmem, vmem),
        scratch_shapes=list(table.values()),
        compiler_params=pltpu.CompilerParams(
            collective_id=0, has_side_effects=True, vmem_limit_bytes=62 * 1024 * 1024
        ),
    )(x, cot, w, gains, shifts, kinds)


def leave_kernel(*args):
    sources, goals, rooms, arrive, depart = args[:5], args[5:10], args[10:15], args[15], args[16]
    pieces = []
    for source, goal, room in zip(sources, goals, rooms):
        high = source.shape[0]
        parts = 3 if high % 24 == 0 else 1
        for part in range(parts):
            rows = pl.ds(part * (high // parts), high // parts)
            at = len(pieces)
            pieces.append(
                (
                    pltpu.make_async_copy(source.at[rows], room.at[rows], arrive.at[at]),
                    pltpu.make_async_copy(room.at[rows], goal.at[rows], depart.at[at]),
                )
            )
    for come, _ in pieces:
        come.start()
    for come, go in pieces:
        come.wait()
        go.start()
    for _, go in pieces:
        go.wait()


def leave_call(arrays):
    hbm = pl.BlockSpec(memory_space=pl.ANY)
    return pl.pallas_call(
        leave_kernel,
        out_shape=tuple(jax.ShapeDtypeStruct(array.shape, array.dtype) for array in arrays),
        in_specs=[hbm] * 5,
        out_specs=(hbm,) * 5,
        scratch_shapes=[pltpu.VMEM(array.shape, array.dtype) for array in arrays]
        + [pltpu.SemaphoreType.DMA((16,)), pltpu.SemaphoreType.DMA((16,))],
    )(*arrays)


def on_device_grouped(features, weights, gains, shifts, cotangent, size_group):
    count = lax.axis_size("crops")
    large = count // 4
    weight_rows = weights.shape[2] // LANES
    results = whole_call(
        group_rows(count),
        large,
        count - large,
        features[0],
        cotangent[0],
        weights[0]
        .reshape(MODULES, weight_rows, LANES)
        .transpose(1, 0, 2)
        .reshape(MODULES * weight_rows, LANES),
        gains[0],
        shifts[0],
        size_group,
    )
    out, grad, weight_grad, gain, shift = leave_call(results)
    share = weight_rows // count
    weight_grad = weight_grad.reshape(share, MODULES, LANES).transpose(1, 0, 2)
    weight_grad = with_layout_constraint(weight_grad, Layout((1, 0, 2)))
    return (
        out[None],
        grad[None],
        weight_grad.reshape(1, MODULES, share * LANES),
        gain[None],
        shift[None],
    )


def group_rows(count):
    large = count // 4
    rows = max(large * (LH // 8) * (LW // 8), (count - large) * (SH // 8) * (SW // 8))
    return -(-rows // 16) * 16


def fits(count):
    return count % 8 == 0 and group_rows(count) <= 96


def solution(mesh):
    placed = (
        P("branch", "crops", None),
        P("branch", None, None),
        P("branch", None, None, None),
        P("branch", None, None, None),
        P("branch", "crops", None),
        P(),
    )
    return jax.shard_map(
        on_device_grouped if fits(mesh.shape["crops"]) else on_device,
        mesh=mesh,
        in_specs=placed,
        out_specs=(
            P("branch", "crops", None),
            P("branch", "crops", None),
            P("branch", None, "crops"),
            P("branch", None, None, "crops"),
            P("branch", None, None, "crops"),
        ),
        check_vma=False,
    )
```
